32 devices in a mesh: blk: 2 (over core), dp: 16 (over z, y, x).
Axes of the slice: x: 2, y: 2, z: 4, core: 2. Of those that a mesh axis runs over, the one named last changes fastest.
Arguments:
- inputs: bfloat16 [64, 1024, 768], P('dp', 'blk'), may hold values from -6 to 6
- cotangent: bfloat16 [64, 1024, 768], P('dp', 'blk'), may hold values from -6 to 6
- doc_lengths: int32 [64, 2], P('dp'), may hold values from 0 to 1024, as said below
- owner_list: int32 [12], replicated, may hold values from 0 to 15, as said below
- master: float32 [48, 768, 768], P('dp', 'blk'), as said below
- first_moment: float32 [48, 768, 768], P('dp', 'blk'), as said below
- second_moment: float32 [48, 768, 768], P('dp', 'blk'), as said below
- vectors: float32 [12, 768], replicated
- vector_first: float32 [12, 768], P(None, 'blk')
- vector_second: float32 [12, 768], P(None, 'blk'), as said below
Outputs:
- block_out: float32 [64, 1024, 768], P('dp', 'blk')
- input_grad: float32 [64, 1024, 768], P('dp', 'blk')
- new_master: float32 [48, 768, 768], P('dp', 'blk')
- new_first: float32 [48, 768, 768], P('dp', 'blk')
- new_second: float32 [48, 768, 768], P('dp', 'blk')
- new_vectors: float32 [12, 768], P(None, 'blk')
- new_vector_first: float32 [12, 768], P(None, 'blk')
- new_vector_second: float32 [12, 768], P(None, 'blk')
The draws below stay inside these ranges and needn't reach their ends.
Inputs may be any that keep to these rules, and one draw needn't show every extreme that they name: `doc_lengths`: each row holds either one document (first entry 1024, second 0) or two of half of 1024 each; among the 4 rows of each aligned block both kinds occur. `owner_list`: one owner holds exactly 3 tiles and none holds more. `master`: slots that no tile names are not read. `first_moment`: slots that no tile names are not read. `second_moment`: entries are positive; slots that no tile names are not read. `vector_second`: entries are positive.
All inputs are finite; a program needn't handle non-finite values.
Results may differ from the reference program's by a relative error of at most 0.023.
Values may be sent and summed in bfloat16 or wider, within the bound.
A program may use at most 384 MiB of HBM per device.

```python
import math
import jax
import jax.numpy as jnp
from jax import lax

D = 768
FF = 3072
HEADS = 12
HEAD_DIM = 64
LEN = 1024
ROWS_DEV = 4
CAP = 3
STEP = 10
ROWS = 64
TOKENS = 65536
PIECES = 12
VROWS = 12
SLOTS = 48
N_DP = 16


def owner_table(key):
    base = jax.random.fold_in(key, 101)
    key_tiles, key_owners, key_count = jax.random.split(base, 3)
    tile_order = jax.random.permutation(key_tiles, PIECES)
    owner_order = jax.random.permutation(key_owners, N_DP)
    second = jax.random.randint(key_count, (), 1, CAP + 1)
    place = jnp.arange(PIECES)
    group = jnp.where(place < CAP, 0, jnp.where(place < CAP + second, 1, 2 + place - CAP - second))
    return jnp.zeros((PIECES,), jnp.int32).at[tile_order].set(owner_order[group].astype(jnp.int32))


def slot_tiles(owners):
    order = jnp.arange(PIECES)
    same = owners[:, None] == owners[None, :]
    ranks = jnp.sum(same & (order[None, :] < order[:, None]), axis=1)
    slot_of = owners * CAP + ranks
    hits = slot_of[None, :] == jnp.arange(SLOTS)[:, None]
    return jnp.sum(jnp.where(hits, order[None, :] + 1, 0), axis=1) - 1


def tile_values(tile, query_key, value, output, upper, lower, empty):
    fold = FF // D
    chosen = jnp.where(tile < 2, query_key, jnp.where(tile == 2, value, jnp.where(tile == 3, output, jnp.where(tile < 4 + fold, upper, lower))))
    return jnp.where(tile < 0, empty, chosen)


def grad_size(key):
    tile = slot_tiles(owner_table(key))
    return tile_values(tile, 0.7, 1.0, 0.25, 0.45, 0.6, 0.5) * math.sqrt(TOKENS)


def draw_owner_list(key, part):
    return owner_table(key)


def draw_doc_lengths(key, part):
    key = jax.random.fold_in(key, 5)
    key_kind, key_pick = jax.random.split(key)
    kinds = jax.random.randint(key_kind, (ROWS,), 0, 2)
    chosen = jax.random.randint(key_pick, (N_DP,), 0, ROWS_DEV)
    rows = jnp.arange(ROWS)
    within = rows % ROWS_DEV
    device_pick = chosen[rows // ROWS_DEV]
    kinds = jnp.where(within == device_pick, 0, jnp.where(within == (device_pick + 1) % ROWS_DEV, 1, kinds))
    first = jnp.where(kinds == 0, LEN, LEN // 2)
    second = jnp.where(kinds == 0, 0, LEN // 2)
    return jnp.stack([first, second], axis=1).astype(jnp.int32)


def draw_master(key, part):
    tile = slot_tiles(owner_table(key))
    key = jax.random.fold_in(key, 3)
    factor = tile_values(tile, 1.4, 1.0, 4.0, 1.0, 1.6 * math.sqrt(D / FF), 1.0) * D ** (-0.5)
    return jax.random.normal(key, (SLOTS, D, D), jnp.float32) * factor[:, None, None]


def draw_first_moment(key, part):
    size = grad_size(key)
    key = jax.random.fold_in(key, 13)
    return jax.random.normal(key, (SLOTS, D, D), jnp.float32) * (size / 9.0)[:, None, None]


def draw_second_moment(key, part):
    size = grad_size(key)
    key = jax.random.fold_in(key, 17)
    spread = jnp.exp(jax.random.uniform(key, (SLOTS, D, D), jnp.float32, 0.0, math.log(4.0)))
    return spread * (size * size * (0.001 / 0.999))[:, None, None]


def draw_vectors(key, part):
    key = jax.random.fold_in(key, 7)
    key_gain, key_shift = jax.random.split(key)
    gains = jax.random.uniform(key_gain, (VROWS, D), jnp.float32, 0.7, 1.3)
    shifts = 0.3 * jax.random.normal(key_shift, (VROWS, D), jnp.float32)
    row = jnp.arange(VROWS)[:, None]
    return jnp.where((row == 0) | (row == 2), gains, shifts)


def draw_vector_first(key, part):
    key = jax.random.fold_in(key, 9)
    return jax.random.normal(key, (VROWS, D), jnp.float32) * (math.sqrt(TOKENS) / 9.0)


def draw_vector_second(key, part):
    key = jax.random.fold_in(key, 11)
    spread = jnp.exp(jax.random.uniform(key, (VROWS, D), jnp.float32, 0.0, math.log(4.0)))
    return spread * (TOKENS * 0.001 / 0.999)


def level_of(rng, extent, cuts, low, high):
    def one(position, shards_of):
        heights = jax.random.uniform(jax.random.fold_in(jax.random.fold_in(rng, 6), position), (shards_of,), jnp.float32, low / len(cuts), high / len(cuts))
        return jnp.repeat(jnp.exp(heights), extent[position] // shards_of).reshape((-1,) + (1,) * (len(extent) - position - 1))

    level = one(*cuts[0])
    for cut in cuts[1:]:
        level = level * one(*cut)
    return level


def normal_values(key, dims, scale, limit, cuts=(), dtype=jnp.bfloat16):
    array = jax.random.normal(key, dims, jnp.float32) * scale
    if len(cuts) > 0:
        array = level_of(key, dims, cuts, -0.22, 0.18) * array
    return jnp.clip(array, min=-limit, max=limit).astype(dtype)


def setup_inputs(seed: int = 0) -> dict:
    key_list = jax.random.split(jax.random.key(seed), 11)
    return {
        "inputs": normal_values(key_list[0], (ROWS, LEN, D), 1.0, 6.0, ((0, 16), (1, 2))),
        "cotangent": normal_values(key_list[1], (ROWS, LEN, D), 1.0, 6.0, ((0, 16), (1, 2))),
        "doc_lengths": draw_doc_lengths(jax.random.fold_in(key_list[10], 71), 0),
        "owner_list": draw_owner_list(jax.random.fold_in(key_list[10], 71), 0),
        "master": draw_master(jax.random.fold_in(key_list[10], 71), 0),
        "first_moment": draw_first_moment(jax.random.fold_in(key_list[10], 71), 0),
        "second_moment": draw_second_moment(jax.random.fold_in(key_list[10], 71), 0),
        "vectors": draw_vectors(jax.random.fold_in(key_list[10], 71), 0),
        "vector_first": draw_vector_first(jax.random.fold_in(key_list[10], 71), 0),
        "vector_second": draw_vector_second(jax.random.fold_in(key_list[10], 71), 0),
    }


EPS_NORM = 1e-05
BETA_ONE = 0.9
BETA_TWO = 0.999
RATE = 0.04
VEC_RATE = 0.25
DECAY = 0.01
ADAM_EPS = 1e-08

@jax.custom_vjp
def low(v):
    return lax.optimization_barrier(v.astype(jnp.bfloat16)).astype(jnp.float32)

@jax.custom_vjp
def low_back(v):
    return v

def low_keep(v):
    return (low(v), None)

def low_pass(kept, grad):
    return (grad,)

def back_keep(v):
    return (v, None)

def back_low(kept, grad):
    return (low(grad),)
low.defvjp(low_keep, low_pass)
low_back.defvjp(back_keep, back_low)

def normalize(values_in, gain, shift):
    center = lax.optimization_barrier(jnp.mean(values_in, axis=-1, keepdims=True))
    offset = values_in - center
    spread = lax.optimization_barrier(jnp.mean(offset * offset, axis=-1, keepdims=True))
    return offset * lax.rsqrt(spread + EPS_NORM) * gain + shift

def matmul(left, right):
    return jnp.einsum('...i,ij->...j', left, right, precision=lax.Precision.HIGHEST)

def adam_step(weight, grad, first, second, rate):
    first_new = BETA_ONE * first + (1.0 - BETA_ONE) * grad
    second_new = BETA_TWO * second + (1.0 - BETA_TWO) * grad * grad
    corrected = first_new / (1.0 - BETA_ONE ** STEP) / (jnp.sqrt(second_new / (1.0 - BETA_TWO ** STEP)) + ADAM_EPS)
    return (weight - rate * (corrected + DECAY * weight), first_new, second_new)

def group_forward(rows_in, row_lengths, tiles, vectors):
    fold = FF // D
    count = rows_in.shape[0]
    up_weight = jnp.transpose(tiles[4:4 + fold], (1, 0, 2)).reshape(D, FF)
    down_weight = tiles[4 + fold:].reshape(FF, D)
    normed = low(normalize(rows_in, vectors[0], vectors[1]))
    queries = low_back(low(matmul(normed, tiles[0]) + vectors[4])).reshape(count, LEN, HEADS, HEAD_DIM)
    keys = low_back(low(matmul(normed, tiles[1]))).reshape(count, LEN, HEADS, HEAD_DIM)
    values = low_back(low(matmul(normed, tiles[2]) + vectors[5])).reshape(count, LEN, HEADS, HEAD_DIM)
    scores = low_back(jnp.einsum('gqhd,gkhd->ghqk', queries, keys, precision=lax.Precision.HIGHEST) * HEAD_DIM ** (-0.5))
    segment = jnp.arange(LEN)[None, :] >= row_lengths[:, 0:1]
    allowed = segment[:, None, :, None] == segment[:, None, None, :]
    weights = jax.nn.softmax(jnp.where(allowed, scores, -1e+30), axis=-1)
    context = jnp.einsum('ghqk,gkhd->gqhd', low(weights), values, precision=lax.Precision.HIGHEST)
    context = low_back(low(context)).reshape(count, LEN, D)
    attended = low_back(matmul(context, tiles[3]) + vectors[6])
    residual = rows_in + attended
    normed_two = low(normalize(residual, vectors[2], vectors[3]))
    hidden = low_back(matmul(normed_two, up_weight) + vectors[8:].reshape(FF))
    active = low(jax.nn.gelu(hidden, approximate=False))
    return residual + low_back(matmul(active, down_weight) + vectors[7])

def reference(inputs, cotangent, doc_lengths, owner_list, master, first_moment, second_moment, vectors, vector_first, vector_second):
    order = jnp.arange(PIECES)
    same = owner_list[:, None] == owner_list[None, :]
    ranks = lax.optimization_barrier(jnp.sum(same & (order[None, :] < order[:, None]), axis=1)).astype(jnp.int32)
    slot_of = (owner_list * CAP + ranks).astype(jnp.int32)
    tile_master = master[slot_of]
    group = 2

    def forward(rows_in, tiles, vec):
        low_tiles = low(tiles)
        stacked = rows_in.reshape(ROWS // group, group, LEN, D)
        lengths = doc_lengths.reshape(ROWS // group, group, 2)

        def one(item):
            return group_forward(item[0], item[1], low_tiles, vec)
        result = lax.map(jax.checkpoint(one), (stacked, lengths))
        return result.reshape(ROWS, LEN, D)
    block_out, pull = jax.vjp(forward, inputs.astype(jnp.float32), tile_master, vectors)
    input_grad, tile_grads, vector_grads = pull(cotangent.astype(jnp.float32))
    slot_grads = jnp.zeros((SLOTS, D, D), jnp.float32).at[slot_of].set(tile_grads)
    occupied = jnp.zeros((SLOTS,), jnp.float32).at[slot_of].set(1.0)[:, None, None]
    new_master, new_first, new_second = adam_step(master, slot_grads, first_moment, second_moment, RATE)
    new_vectors, new_vector_first, new_vector_second = adam_step(vectors, vector_grads, vector_first, vector_second, VEC_RATE)
    return (block_out, input_grad, new_master * occupied, new_first * occupied, new_second * occupied, new_vectors, new_vector_first, new_vector_second)
```

```python
from functools import partial

import jax
import jax.numpy as jnp
from jax import lax
from jax.experimental import pallas as pl
from jax.experimental.pallas import tpu as pltpu
from jax.sharding import PartitionSpec as P

D = 768
FF = 3072
HEADS = 12
HEAD_DIM = 64
LEN = 1024
CAP = 3
STEP = 10
PIECES = 12


EPS_NORM = 1e-05
BETA_ONE = 0.9
BETA_TWO = 0.999
RATE = 0.04
VEC_RATE = 0.25
DECAY = 0.01
ADAM_EPS = 1e-08


def normalize(values_in, gain, shift):
    center = jnp.mean(values_in, axis=-1, keepdims=True)
    offset = values_in - center
    spread = jnp.mean(offset * offset, axis=-1, keepdims=True)
    return offset * lax.rsqrt(spread + EPS_NORM) * gain + shift


def adam_step(weight, grad, first, second, rate):
    first_new = BETA_ONE * first + (1.0 - BETA_ONE) * grad
    second_new = BETA_TWO * second + (1.0 - BETA_TWO) * grad * grad
    corrected = (
        first_new
        / (1.0 - BETA_ONE**STEP)
        / (jnp.sqrt(second_new / (1.0 - BETA_TWO**STEP)) + ADAM_EPS)
    )
    return (weight - rate * (corrected + DECAY * weight), first_new, second_new)


def shards_any(
    inputs,
    cotangent,
    doc_lengths,
    owner_list,
    master,
    first_moment,
    second_moment,
    vectors,
    vector_first,
    vector_second,
):
    rows_here, span, width = inputs.shape
    tokens_here = rows_here * span
    fold = FF // D
    scale = HEAD_DIM ** (-0.5)
    place = lax.axis_index("blk")
    f32 = jnp.float32
    b16 = jnp.bfloat16
    order = jnp.arange(PIECES)
    same_owner = owner_list[:, None] == owner_list[None, :]
    ranks = jnp.sum(same_owner & (order[None, :] < order[:, None]), axis=1)
    slot_of = owner_list * CAP + ranks

    mine = (owner_list == lax.axis_index("dp"))[:, None, None]
    tile_rows = lax.psum(jnp.where(mine, master[ranks], 0.0).astype(b16), "dp")
    tiles = lax.all_gather(tile_rows, "blk", axis=1, tiled=True)
    query_weight = tiles[0]
    key_weight = tiles[1]
    value_weight = tiles[2]
    out_weight = tiles[3]
    up_weight = jnp.transpose(tiles[4 : 4 + fold], (1, 0, 2)).reshape(width, FF)
    down_weight = tiles[4 + fold :].reshape(FF, width)
    flat_in = inputs.reshape(tokens_here, width).astype(f32)
    normed_one = normalize(flat_in, vectors[0], vectors[1]).astype(b16)
    queries = (jnp.dot(normed_one, query_weight, preferred_element_type=f32) + vectors[4]).astype(
        b16
    )
    keys_here = jnp.dot(normed_one, key_weight, preferred_element_type=f32).astype(b16)
    values_here = (
        jnp.dot(normed_one, value_weight, preferred_element_type=f32) + vectors[5]
    ).astype(b16)
    query_heads = queries.reshape(rows_here, span, HEADS, HEAD_DIM)
    first_len = doc_lengths[:, 0]
    query_seg = (place * span + jnp.arange(span))[None, :] >= first_len[:, None]

    def block_scores(key_block, start):
        count = key_block.shape[1]
        key_heads = key_block.reshape(rows_here, count, HEADS, HEAD_DIM)
        raw = (
            jnp.einsum("rqhd,rkhd->rhqk", query_heads, key_heads, preferred_element_type=f32)
            * scale
        )
        key_seg = (start + jnp.arange(count))[None, :] >= first_len[:, None]
        allowed = query_seg[:, None, :, None] == key_seg[:, None, None, :]
        return (raw, allowed)

    key_rows = keys_here.reshape(rows_here, span, width)
    value_rows = values_here.reshape(rows_here, span, width)
    top = jnp.full((rows_here, HEADS, span), -1e30, f32)
    key_block = lax.all_gather(key_rows, "blk", axis=1, tiled=True)
    value_block = lax.all_gather(value_rows, "blk", axis=1, tiled=True)
    count = key_block.shape[1]
    raw, allowed = block_scores(key_block, jnp.int32(0))
    new_top = jnp.maximum(top, jnp.max(jnp.where(allowed, raw, -1e30), axis=-1))
    weights = jnp.where(allowed, jnp.exp(raw - new_top[..., None]), 0.0)
    value_heads = value_block.reshape(rows_here, count, HEADS, HEAD_DIM)
    update = jnp.einsum(
        "rhqk,rkhd->rhqd", weights.astype(b16), value_heads, preferred_element_type=f32
    )
    total = jnp.sum(weights, axis=-1)
    log_total = new_top + jnp.log(total)
    context_raw = update / total[..., None]
    context_low = jnp.transpose(context_raw, (0, 2, 1, 3)).reshape(tokens_here, width).astype(b16)
    residual = flat_in + (jnp.dot(context_low, out_weight, preferred_element_type=f32) + vectors[6])
    normed_two = normalize(residual, vectors[2], vectors[3]).astype(b16)
    hidden = jnp.dot(normed_two, up_weight, preferred_element_type=f32) + vectors[8:].reshape(FF)
    gelu_exact = partial(jax.nn.gelu, approximate=False)
    active, gelu_pull = jax.vjp(gelu_exact, hidden)
    active_low = active.astype(b16)
    block_out = (
        residual + (jnp.dot(active_low, down_weight, preferred_element_type=f32) + vectors[7])
    ).reshape(rows_here, span, width)
    grad_out = cotangent.reshape(tokens_here, width)
    down_grad = jnp.einsum("tf,td->fd", active_low, grad_out, preferred_element_type=f32)
    down_sum = jnp.sum(grad_out, axis=0, dtype=f32)
    grad_active = jnp.einsum("td,fd->tf", grad_out, down_weight, preferred_element_type=f32)
    grad_hidden = gelu_pull(grad_active)[0].astype(b16)
    up_grad = jnp.einsum("td,tf->df", normed_two, grad_hidden, preferred_element_type=f32)
    up_sum = jnp.sum(grad_hidden, axis=0, dtype=f32)
    ffn_tiles = jnp.concatenate(
        [
            jnp.transpose(up_grad.reshape(width, fold, width), (1, 0, 2)),
            down_grad.reshape(fold, width, width),
        ],
        axis=0,
    )
    grad_normed_two = jnp.einsum("tf,df->td", grad_hidden, up_weight, preferred_element_type=f32)
    unused, second_pull = jax.vjp(normalize, residual, vectors[2], vectors[3])
    residual_part, gain_two_grad, shift_two_grad = second_pull(grad_normed_two)
    grad_residual = grad_out.astype(f32) + residual_part
    grad_attended = grad_residual.astype(b16)
    out_grad = jnp.einsum("tm,td->md", context_low, grad_attended, preferred_element_type=f32)
    out_sum = jnp.sum(grad_attended, axis=0, dtype=f32)
    grad_context = jnp.einsum(
        "td,md->tm", grad_attended, out_weight, preferred_element_type=f32
    ).astype(b16)
    grad_heads = grad_context.reshape(rows_here, span, HEADS, HEAD_DIM)
    delta = jnp.einsum("rqhd,rhqd->rhq", grad_heads.astype(f32), context_raw)
    key_all, value_all = (
        lax.all_gather(key_rows, "blk", axis=1, tiled=True),
        lax.all_gather(value_rows, "blk", axis=1, tiled=True),
    )
    key_size = min(512, LEN)

    def back_block(index, carry):
        grad_query, key_total, value_total = carry
        start = index * key_size
        key_block = lax.dynamic_slice_in_dim(key_all, start, key_size, 1)
        value_block = lax.dynamic_slice_in_dim(value_all, start, key_size, 1)
        raw, allowed = block_scores(key_block, start)
        weights_back = jnp.where(allowed, jnp.exp(raw - log_total[..., None]), 0.0)
        key_heads = key_block.reshape(rows_here, key_size, HEADS, HEAD_DIM)
        value_heads = value_block.reshape(rows_here, key_size, HEADS, HEAD_DIM)
        value_grad = jnp.einsum(
            "rhqk,rqhd->rkhd", weights_back.astype(b16), grad_heads, preferred_element_type=f32
        )
        weight_grad = jnp.einsum(
            "rqhd,rkhd->rhqk", grad_heads, value_heads, preferred_element_type=f32
        )
        score_grad = (weights_back * (weight_grad - delta[..., None])).astype(b16)
        grad_query = (
            grad_query
            + jnp.einsum("rhqk,rkhd->rqhd", score_grad, key_heads, preferred_element_type=f32)
            * scale
        )
        key_grad = (
            jnp.einsum("rhqk,rqhd->rkhd", score_grad, query_heads, preferred_element_type=f32)
            * scale
        )
        key_total = lax.dynamic_update_slice_in_dim(
            key_total, key_grad.reshape(rows_here, key_size, width), start, 1
        )
        value_total = lax.dynamic_update_slice_in_dim(
            value_total, value_grad.reshape(rows_here, key_size, width), start, 1
        )
        return (grad_query, key_total, value_total)

    zero_rows = jnp.zeros((rows_here, LEN, width), f32)
    grad_query, key_total, value_total = lax.fori_loop(
        0,
        LEN // key_size,
        back_block,
        (jnp.zeros((rows_here, span, HEADS, HEAD_DIM), f32), zero_rows, zero_rows),
    )
    key_grad_here, value_grad_here = (
        lax.psum_scatter(
            key_total.astype(jnp.bfloat16), "blk", scatter_dimension=1, tiled=True
        ).astype(jnp.float32),
        lax.psum_scatter(
            value_total.astype(jnp.bfloat16), "blk", scatter_dimension=1, tiled=True
        ).astype(jnp.float32),
    )
    query_low = grad_query.reshape(tokens_here, width).astype(b16)
    key_low = key_grad_here.reshape(tokens_here, width).astype(b16)
    value_low = value_grad_here.reshape(tokens_here, width).astype(b16)
    query_tile = jnp.einsum("td,te->de", normed_one, query_low, preferred_element_type=f32)
    key_tile = jnp.einsum("td,te->de", normed_one, key_low, preferred_element_type=f32)
    value_tile = jnp.einsum("td,te->de", normed_one, value_low, preferred_element_type=f32)
    grad_normed_one = (
        jnp.einsum("te,de->td", query_low, query_weight, preferred_element_type=f32)
        + jnp.einsum("te,de->td", key_low, key_weight, preferred_element_type=f32)
        + jnp.einsum("te,de->td", value_low, value_weight, preferred_element_type=f32)
    )
    unused, first_pull = jax.vjp(normalize, flat_in, vectors[0], vectors[1])
    input_part, gain_one_grad, shift_one_grad = first_pull(grad_normed_one)
    input_grad = (grad_residual + input_part).reshape(rows_here, span, width)
    vector_grads = jnp.concatenate(
        [
            jnp.stack(
                [
                    gain_one_grad,
                    shift_one_grad,
                    gain_two_grad,
                    shift_two_grad,
                    jnp.sum(query_low, axis=0, dtype=f32),
                    jnp.sum(value_low, axis=0, dtype=f32),
                    out_sum,
                    down_sum,
                ]
            ),
            up_sum.reshape(fold, width),
        ],
        axis=0,
    )
    attn_tiles = jnp.stack([query_tile, key_tile, value_tile, out_grad])
    piece_share, vector_share = (
        lax.psum_scatter(
            jnp.concatenate([attn_tiles, ffn_tiles], axis=0).astype(jnp.bfloat16),
            "blk",
            scatter_dimension=1,
            tiled=True,
        ).astype(jnp.float32),
        lax.psum_scatter(
            vector_grads.astype(jnp.bfloat16), "blk", scatter_dimension=1, tiled=True
        ).astype(jnp.float32),
    )
    own_slots = lax.axis_index("dp") * CAP + jnp.arange(CAP)
    pick = (own_slots[:, None] == slot_of[None, :]).astype(f32)
    occupied = jnp.sum(pick, axis=1)[:, None, None]
    total_share, vector_total = (
        lax.psum(piece_share.astype(jnp.bfloat16), "dp").astype(jnp.float32),
        lax.psum(vector_share.astype(jnp.bfloat16), "dp").astype(jnp.float32),
    )
    slot_grads = jnp.einsum("cp,prd->crd", pick, total_share, precision=lax.Precision.HIGHEST)
    new_master, new_first, new_second = adam_step(
        master, slot_grads, first_moment, second_moment, RATE
    )
    columns = vector_first.shape[1]
    vector_cols = lax.dynamic_slice_in_dim(vectors, place * columns, columns, 1)
    new_vectors, new_vector_first, new_vector_second = adam_step(
        vector_cols, vector_total, vector_first, vector_second, VEC_RATE
    )
    return (
        block_out,
        input_grad,
        new_master * occupied,
        new_first * occupied,
        new_second * occupied,
        new_vectors,
        new_vector_first,
        new_vector_second,
    )


f32 = jnp.float32
b16 = jnp.bfloat16
LOG2E = 1.4426950408889634
MIB = 1024 * 1024
PAIRS = HEADS // 2
PAIR = 2 * HEAD_DIM


def dot_nn(left, right):
    return lax.dot_general(left, right, (((1,), (0,)), ((), ())), preferred_element_type=f32)


def dot_nt(left, right):
    return lax.dot_general(left, right, (((1,), (1,)), ((), ())), preferred_element_type=f32)


def dot_tn(left, right):
    return lax.dot_general(left, right, (((0,), (0,)), ((), ())), preferred_element_type=f32)


def norm_parts(values_in):
    center = jnp.mean(values_in, axis=-1, keepdims=True)
    offset = values_in - center
    spread = jnp.mean(offset * offset, axis=-1, keepdims=True)
    rstd = lax.rsqrt(spread + EPS_NORM)
    return offset * rstd, rstd


def norm_back(grad, unit, rstd, gain):
    scaled = grad * gain
    first = jnp.mean(scaled, axis=-1, keepdims=True)
    second = jnp.mean(scaled * unit, axis=-1, keepdims=True)
    return rstd * (scaled - first - unit * second)


def gelu_parts(value):
    bell = jnp.exp2(value * value * (-0.5 * LOG2E))
    ratio = pl.reciprocal(1.0 + (0.3275911 * 0.7071067811865476) * jnp.abs(value))
    poly = 0.5 * 1.061405429
    poly = poly * ratio + 0.5 * -1.453152027
    poly = poly * ratio + 0.5 * 1.421413741
    poly = poly * ratio + 0.5 * -0.284496736
    poly = poly * ratio + 0.5 * 0.254829592
    tail = poly * ratio * bell
    cdf = jnp.where(value >= 0.0, 1.0 - tail, tail)
    return value * cdf, cdf + value * (bell * 0.3989422804014327)


def project_kernel(x_ref, w_ref, vec_ref, k_ref, v_ref, t_ref, n_ref):
    unit, unused = norm_parts(x_ref[...].astype(f32))
    normed = (unit * vec_ref[0:1, :] + vec_ref[1:2, :]).astype(b16)
    n_ref[...] = normed.T
    queries = (dot_nn(normed, w_ref[0]) + vec_ref[4:5, :]) * (HEAD_DIM**-0.5 * LOG2E)
    t_ref[0] = queries.astype(b16).T
    keys = dot_nn(normed, w_ref[1]).astype(b16)
    k_ref[...] = keys
    t_ref[1] = keys.T
    values = (dot_nn(normed, w_ref[2]) + vec_ref[5:6, :]).astype(b16)
    v_ref[...] = values
    t_ref[2] = values.T


def project(x, weights, vectors):
    tokens = x.shape[0]
    size = 512
    return pl.pallas_call(
        project_kernel,
        grid=(tokens // size,),
        in_specs=[
            pl.BlockSpec((size, D), lambda i: (i, 0)),
            pl.BlockSpec((3, D, D), lambda i: (0, 0, 0), pipeline_mode=pl.Buffered(1)),
            pl.BlockSpec((PIECES, D), lambda i: (0, 0)),
        ],
        out_specs=[
            pl.BlockSpec((size, D), lambda i: (i, 0)),
            pl.BlockSpec((size, D), lambda i: (i, 0)),
            pl.BlockSpec((3, D, size), lambda i: (0, 0, i)),
            pl.BlockSpec((D, size), lambda i: (0, i)),
        ],
        out_shape=[
            jax.ShapeDtypeStruct((tokens, D), b16),
            jax.ShapeDtypeStruct((tokens, D), b16),
            jax.ShapeDtypeStruct((3, D, tokens), b16),
            jax.ShapeDtypeStruct((D, tokens), b16),
        ],
        compiler_params=pltpu.CompilerParams(vmem_limit_bytes=48 * MIB),
        cost_estimate=pl.CostEstimate(
            flops=6 * tokens * D * D, bytes_accessed=14 * tokens * D + 6 * D * D, transcendentals=0
        ),
        name="project",
    )(x, weights, vectors)


def head_only(block, head):
    lane = lax.broadcasted_iota(jnp.int32, block.shape, 1)
    keep = (lane >= head * HEAD_DIM) & (lane < (head + 1) * HEAD_DIM)
    return jnp.where(keep, block, jnp.zeros_like(block))


def attend_kernel(bias_ref, k_ref, q_ref, v_ref, p_ref, r_ref, o_ref, c_ref):
    half = LEN // 2
    bias = bias_ref[pl.program_id(0)]
    for head in range(2):
        part = slice(head * HEAD_DIM, (head + 1) * HEAD_DIM)
        keys = head_only(k_ref[...], head)
        for step in range(2):
            cols = slice(step * half, (step + 1) * half)
            rows = slice((1 - step) * half, (2 - step) * half)
            near = dot_nn(keys[cols], q_ref[0, :, cols])
            far = dot_nn(keys[rows], q_ref[0, :, cols]) + bias
            top = jnp.maximum(jnp.max(near, 0, keepdims=True), jnp.max(far, 0, keepdims=True))
            near = jnp.exp2(near - top)
            far = jnp.exp2(far - top)
            total = jnp.sum(near, 0, keepdims=True) + jnp.sum(far, 0, keepdims=True)
            recip = 1.0 / total
            p_ref[head, cols, cols] = near.astype(b16)
            p_ref[head, rows, cols] = far.astype(b16)
            r_ref[0, head : head + 1, cols] = recip
            out = dot_nn(v_ref[0, part, :], p_ref[head, :, cols]) * recip
            o_ref[part, cols] = out.astype(b16)
    c_ref[...] = o_ref[...].T


def attend(bias, keys, turned):
    tokens = keys.shape[0]
    rows = tokens // LEN
    return pl.pallas_call(
        attend_kernel,
        grid=(rows, PAIRS),
        in_specs=[
            pl.BlockSpec(memory_space=pltpu.SMEM),
            pl.BlockSpec((LEN, PAIR), lambda r, h: (r, h)),
            pl.BlockSpec((1, PAIR, LEN), lambda r, h: (0, h, r)),
            pl.BlockSpec((1, PAIR, LEN), lambda r, h: (2, h, r)),
        ],
        out_specs=[
            pl.BlockSpec((2, LEN, LEN), lambda r, h: (r * PAIRS + h, 0, 0)),
            pl.BlockSpec((1, 2, LEN), lambda r, h: (r * PAIRS + h, 0, 0)),
            pl.BlockSpec((PAIR, LEN), lambda r, h: (h, r)),
            pl.BlockSpec((LEN, PAIR), lambda r, h: (r, h)),
        ],
        out_shape=[
            jax.ShapeDtypeStruct((rows * HEADS, LEN, LEN), b16),
            jax.ShapeDtypeStruct((rows * PAIRS, 2, LEN), f32),
            jax.ShapeDtypeStruct((D, tokens), b16),
            jax.ShapeDtypeStruct((tokens, D), b16),
        ],
        compiler_params=pltpu.CompilerParams(vmem_limit_bytes=56 * MIB),
        cost_estimate=pl.CostEstimate(
            flops=16 * tokens * LEN * D,
            bytes_accessed=2 * rows * HEADS * LEN * LEN + 10 * tokens * D,
            transcendentals=rows * HEADS * LEN * LEN,
        ),
        name="attend",
    )(bias, keys, turned, turned)


def attend_back_kernel(p_ref, r_ref, v_ref, q_ref, k_ref, o_ref, g_ref, d_ref):
    half = LEN // 2
    for head in range(2):
        part = slice(head * HEAD_DIM, (head + 1) * HEAD_DIM)
        values = head_only(v_ref[...], head)
        recip = r_ref[0, head : head + 1, :]
        grad = g_ref[part, :].astype(f32) * recip
        delta = jnp.sum(grad * o_ref[part, :].astype(f32), 0, keepdims=True)
        grad = grad.astype(b16)
        wide = jnp.concatenate([grad, grad], axis=0)
        value_grad = jnp.zeros((HEAD_DIM, LEN), f32)
        key_grad = jnp.zeros((HEAD_DIM, LEN), f32)
        for step in range(2):
            cols = slice(step * half, (step + 1) * half)
            weights = p_ref[head, :, cols]
            slope = dot_nn(values, wide[:, cols]) - delta[:, cols]
            slope = (weights.astype(f32) * slope).astype(b16)
            value_grad = value_grad + dot_nt(grad[:, cols], weights)
            key_grad = key_grad + dot_nt(q_ref[0, part, cols], slope)
            query_grad = dot_nn(k_ref[0, part, :], slope) * (HEAD_DIM**-0.5)
            d_ref[0, part, cols] = query_grad.astype(b16)
        d_ref[1, part, :] = (key_grad * (1.0 / LOG2E)).astype(b16)
        d_ref[2, part, :] = value_grad.astype(b16)


def attend_back(weights, recips, values, turned, context, grad):
    tokens = values.shape[0]
    rows = tokens // LEN
    return pl.pallas_call(
        attend_back_kernel,
        grid=(rows, PAIRS),
        in_specs=[
            pl.BlockSpec((2, LEN, LEN), lambda r, h: (r * PAIRS + h, 0, 0)),
            pl.BlockSpec((1, 2, LEN), lambda r, h: (r * PAIRS + h, 0, 0)),
            pl.BlockSpec((LEN, PAIR), lambda r, h: (r, h)),
            pl.BlockSpec((1, PAIR, LEN), lambda r, h: (0, h, r)),
            pl.BlockSpec((1, PAIR, LEN), lambda r, h: (1, h, r)),
            pl.BlockSpec((PAIR, LEN), lambda r, h: (h, r)),
            pl.BlockSpec((PAIR, LEN), lambda r, h: (h, r)),
        ],
        out_specs=pl.BlockSpec((3, PAIR, LEN), lambda r, h: (0, h, r)),
        out_shape=jax.ShapeDtypeStruct((3, D, tokens), b16),
        compiler_params=pltpu.CompilerParams(vmem_limit_bytes=56 * MIB),
        cost_estimate=pl.CostEstimate(
            flops=32 * tokens * LEN * D,
            bytes_accessed=2 * rows * HEADS * LEN * LEN + 16 * tokens * D,
            transcendentals=0,
        ),
        name="attend_back",
    )(weights, recips, values, turned, turned, context, grad)


def feed_kernel(
    c_ref, o_ref, x_ref, g_ref, w_ref, vec_ref,
    y_ref, r_ref, d_ref, sums_ref, tiles_ref,
    acc_ref, stage_ref, sem_ref,
):
    fold = FF // D
    step = pl.program_id(0)

    @pl.when(step == 0)
    def clear():
        acc_ref[...] = jnp.zeros_like(acc_ref)
        sums_ref[...] = jnp.zeros_like(sums_ref)

    residual = x_ref[...].astype(f32) + (dot_nn(c_ref[...], w_ref[0]) + vec_ref[6:7, :])
    unit, rstd = norm_parts(residual)
    gain = vec_ref[2:3, :]
    normed = (unit * gain + vec_ref[3:4, :]).astype(b16)
    turned = normed.T
    cot = g_ref[...]
    out = residual + vec_ref[7:8, :]
    grad = jnp.zeros_like(out)
    for part in range(fold):
        hidden = dot_nn(normed, w_ref[1 + part]) + vec_ref[8 + part : 9 + part, :]
        pulled = dot_nt(cot, w_ref[1 + fold + part])
        active, slope = gelu_parts(hidden)
        active = active.astype(b16)
        pulled = (pulled * slope).astype(b16)
        out = out + dot_nn(active, w_ref[1 + fold + part])
        grad = grad + dot_nt(pulled, w_ref[1 + part])
        acc_ref[1 + part] += dot_nn(turned, pulled)
        acc_ref[1 + fold + part] += dot_tn(active, cot)
        sums_ref[4 + part : 5 + part, :] += jnp.sum(pulled.astype(f32), 0, keepdims=True)
    y_ref[...] = out
    wide = cot.astype(f32)
    sums_ref[0:1, :] += jnp.sum(grad * unit, 0, keepdims=True)
    sums_ref[1:2, :] += jnp.sum(grad, 0, keepdims=True)
    sums_ref[3:4, :] += jnp.sum(wide, 0, keepdims=True)
    back = wide + norm_back(grad, unit, rstd, gain)
    r_ref[...] = back
    low = back.astype(b16)
    sums_ref[2:3, :] += jnp.sum(low.astype(f32), 0, keepdims=True)
    d_ref[...] = dot_nt(w_ref[0], low).astype(b16)
    acc_ref[0] += dot_nn(o_ref[...], low)

    @pl.when(step == pl.num_programs(0) - 1)
    def send():
        count = 1 + 2 * fold
        copies = []
        for part in range(count):
            if part >= 2:
                copies[part - 2].wait()
            stage_ref[part % 2] = acc_ref[part].astype(b16)
            copy = pltpu.make_async_copy(stage_ref.at[part % 2], tiles_ref.at[part], sem_ref.at[part % 2])
            copy.start()
            copies.append(copy)
        copies[count - 2].wait()
        copies[count - 1].wait()


def feed(context, turned, x, cot, weights, vectors):
    tokens = x.shape[0]
    size = 256
    count = 1 + 2 * (FF // D)
    token_block = pl.BlockSpec((size, D), lambda i: (i, 0))
    turned_block = pl.BlockSpec((D, size), lambda i: (0, i))
    return pl.pallas_call(
        feed_kernel,
        grid=(tokens // size,),
        in_specs=[
            token_block,
            turned_block,
            token_block,
            token_block,
            pl.BlockSpec((count, D, D), lambda i: (0, 0, 0), pipeline_mode=pl.Buffered(1)),
            pl.BlockSpec((PIECES, D), lambda i: (0, 0)),
        ],
        out_specs=[
            token_block,
            token_block,
            turned_block,
            pl.BlockSpec((8, D), lambda i: (0, 0)),
            pl.BlockSpec(memory_space=pl.ANY),
        ],
        out_shape=[
            jax.ShapeDtypeStruct((tokens, D), f32),
            jax.ShapeDtypeStruct((tokens, D), f32),
            jax.ShapeDtypeStruct((D, tokens), b16),
            jax.ShapeDtypeStruct((8, D), f32),
            jax.ShapeDtypeStruct((count, D, D), b16),
        ],
        scratch_shapes=[
            pltpu.VMEM((count, D, D), f32),
            pltpu.VMEM((2, D, D), b16),
            pltpu.SemaphoreType.DMA((2,)),
        ],
        compiler_params=pltpu.CompilerParams(vmem_limit_bytes=60 * MIB),
        cost_estimate=pl.CostEstimate(
            flops=6 * count * tokens * D * D,
            bytes_accessed=18 * tokens * D + 4 * count * D * D,
            transcendentals=2 * tokens * FF,
        ),
        name="feed",
    )(context, turned, x, cot, weights, vectors)


def finish_kernel(d_ref, n_ref, x_ref, r_ref, w_ref, vec_ref, i_ref, sums_ref, tiles_ref, acc_ref):
    step = pl.program_id(0)

    @pl.when(step == 0)
    def clear():
        acc_ref[...] = jnp.zeros_like(acc_ref)
        sums_ref[...] = jnp.zeros_like(sums_ref)

    ones = jnp.ones((8, d_ref.shape[2]), b16)
    grad = None
    for part in range(3):
        acc_ref[part] += dot_nt(n_ref[...], d_ref[part])
        term = dot_nn(w_ref[part], d_ref[part])
        grad = term if part == 0 else grad + term
    sums_ref[2:3, :] += dot_nt(ones, d_ref[0])[0:1]
    sums_ref[3:4, :] += dot_nt(ones, d_ref[2])[0:1]
    grad = grad.T
    unit, rstd = norm_parts(x_ref[...].astype(f32))
    sums_ref[0:1, :] += jnp.sum(grad * unit, 0, keepdims=True)
    sums_ref[1:2, :] += jnp.sum(grad, 0, keepdims=True)
    i_ref[...] = r_ref[...] + norm_back(grad, unit, rstd, vec_ref[0:1, :])

    @pl.when(step == pl.num_programs(0) - 1)
    def send():
        tiles_ref[...] = acc_ref[...].astype(b16)


def finish(grads, normed, x, residual, weights, vectors):
    tokens = x.shape[0]
    size = 512
    token_block = pl.BlockSpec((size, D), lambda i: (i, 0))
    return pl.pallas_call(
        finish_kernel,
        grid=(tokens // size,),
        in_specs=[
            pl.BlockSpec((3, D, size), lambda i: (0, 0, i)),
            pl.BlockSpec((D, size), lambda i: (0, i)),
            token_block,
            token_block,
            pl.BlockSpec((3, D, D), lambda i: (0, 0, 0), pipeline_mode=pl.Buffered(1)),
            pl.BlockSpec((PIECES, D), lambda i: (0, 0)),
        ],
        out_specs=[
            token_block,
            pl.BlockSpec((8, D), lambda i: (0, 0)),
            pl.BlockSpec((3, D, D), lambda i: (0, 0, 0)),
        ],
        out_shape=[
            jax.ShapeDtypeStruct((tokens, D), f32),
            jax.ShapeDtypeStruct((8, D), f32),
            jax.ShapeDtypeStruct((3, D, D), b16),
        ],
        scratch_shapes=[pltpu.VMEM((3, D, D), f32)],
        compiler_params=pltpu.CompilerParams(vmem_limit_bytes=56 * MIB),
        cost_estimate=pl.CostEstimate(
            flops=12 * tokens * D * D, bytes_accessed=18 * tokens * D + 12 * D * D, transcendentals=0
        ),
        name="finish",
    )(grads, normed, x, residual, weights, vectors)


def to_rows(block):
    whole = lax.all_to_all(block, "blk", split_axis=0, concat_axis=1, tiled=True)
    return whole.reshape(-1, block.shape[-1])


def to_spans(block, rows, span):
    whole = block.astype(b16).reshape(rows, LEN, -1)
    return lax.all_to_all(whole, "blk", split_axis=1, concat_axis=0, tiled=True).astype(f32)


def shards_paired(
    inputs,
    cotangent,
    doc_lengths,
    owner_list,
    master,
    first_moment,
    second_moment,
    vectors,
    vector_first,
    vector_second,
):
    rows_here, span, width = inputs.shape
    place = lax.axis_index("blk")
    member = lax.axis_index("dp")
    rows_mine = rows_here // 2
    order = jnp.arange(PIECES)
    same_owner = owner_list[:, None] == owner_list[None, :]
    ranks = jnp.sum(same_owner & (order[None, :] < order[:, None]), axis=1)
    slot_of = owner_list * CAP + ranks
    low_master = master.astype(b16)

    def spread(first, last):
        mine = (owner_list[first:last] == member)[:, None, None]
        piece = jnp.where(mine, low_master[ranks[first:last]], jnp.zeros((), b16))
        return lax.all_gather(lax.psum(piece, "dp"), "blk", axis=1, tiled=True)

    weights_one = spread(0, 3)
    weights_two = spread(3, PIECES)
    x = to_rows(inputs)
    cot = to_rows(cotangent)
    lengths = lax.dynamic_slice_in_dim(doc_lengths[:, 0], place * rows_mine, rows_mine, 0)
    bias = jnp.where(lengths < LEN, -1e30, 0.0).astype(f32)
    keys, values, turned, normed = project(x, weights_one, vectors)
    weights, recips, context_turned, context = attend(bias, keys, turned)
    block_out, residual, grad_context, sums_two, tiles_two = feed(
        context, context_turned, x, cot, weights_two, vectors
    )
    block_out = to_spans(block_out, rows_mine, span)
    share_two = lax.psum_scatter(tiles_two, "blk", scatter_dimension=1, tiled=True)
    total_two = lax.psum(share_two, "dp")
    grads = attend_back(weights, recips, values, turned, context_turned, grad_context)
    input_grad, sums_one, tiles_one = finish(grads, normed, x, residual, weights_one, vectors)
    input_grad = to_spans(input_grad, rows_mine, span)
    vector_grads = jnp.concatenate(
        [sums_one[0:2], sums_two[0:2], sums_one[2:4], sums_two[2:4], sums_two[4:8]], axis=0
    )
    vector_share = lax.psum_scatter(
        vector_grads.astype(b16), "blk", scatter_dimension=1, tiled=True
    )
    share_one = lax.psum_scatter(tiles_one, "blk", scatter_dimension=1, tiled=True)
    total_one = lax.psum(share_one, "dp")
    vector_total = lax.psum(vector_share, "dp").astype(f32)
    own_slots = member * CAP + jnp.arange(CAP)
    pick = own_slots[:, None] == slot_of[None, :]
    occupied = jnp.any(pick, axis=1)[:, None, None]
    chosen = jnp.argmax(pick, axis=1)
    slot_grads = jnp.concatenate([total_one, total_two], axis=0)[chosen].astype(f32)
    updated = adam_step(master, slot_grads, first_moment, second_moment, RATE)
    updated = [jnp.where(occupied, part, 0.0) for part in updated]
    columns = vector_first.shape[1]
    vector_cols = lax.dynamic_slice_in_dim(vectors, place * columns, columns, 1)
    updated_vectors = adam_step(vector_cols, vector_total, vector_first, vector_second, VEC_RATE)
    return (block_out, input_grad, *updated, *updated_vectors)


def solution(mesh):
    in_specs = (
        P("dp", "blk", None),
        P("dp", "blk", None),
        P("dp", None),
        P(),
        P("dp", "blk", None),
        P("dp", "blk", None),
        P("dp", "blk", None),
        P(),
        P(None, "blk"),
        P(None, "blk"),
    )
    out_specs = (
        P("dp", "blk", None),
        P("dp", "blk", None),
        P("dp", "blk", None),
        P("dp", "blk", None),
        P("dp", "blk", None),
        P(None, "blk"),
        P(None, "blk"),
        P(None, "blk"),
    )
    paired = mesh.shape["blk"] == 2
    shards = shards_paired if paired else shards_any
    return jax.shard_map(shards, mesh=mesh, in_specs=in_specs, out_specs=out_specs, check_vma=False)
```

```python
from functools import partial

import jax
import jax.numpy as jnp
from jax import lax
from jax.experimental import pallas as pl
from jax.experimental.pallas import tpu as pltpu
from jax.sharding import PartitionSpec as P

D = 768
FF = 3072
HEADS = 12
HEAD_DIM = 64
LEN = 1024
CAP = 3
STEP = 10
PIECES = 12


EPS_NORM = 1e-05
BETA_ONE = 0.9
BETA_TWO = 0.999
RATE = 0.04
VEC_RATE = 0.25
DECAY = 0.01
ADAM_EPS = 1e-08


def normalize(values_in, gain, shift):
    center = jnp.mean(values_in, axis=-1, keepdims=True)
    offset = values_in - center
    spread = jnp.mean(offset * offset, axis=-1, keepdims=True)
    return offset * lax.rsqrt(spread + EPS_NORM) * gain + shift


def adam_step(weight, grad, first, second, rate):
    first_new = BETA_ONE * first + (1.0 - BETA_ONE) * grad
    second_new = BETA_TWO * second + (1.0 - BETA_TWO) * grad * grad
    corrected = (
        first_new
        / (1.0 - BETA_ONE**STEP)
        / (jnp.sqrt(second_new / (1.0 - BETA_TWO**STEP)) + ADAM_EPS)
    )
    return (weight - rate * (corrected + DECAY * weight), first_new, second_new)


def shards_any(
    inputs,
    cotangent,
    doc_lengths,
    owner_list,
    master,
    first_moment,
    second_moment,
    vectors,
    vector_first,
    vector_second,
):
    rows_here, span, width = inputs.shape
    tokens_here = rows_here * span
    fold = FF // D
    scale = HEAD_DIM ** (-0.5)
    place = lax.axis_index("blk")
    f32 = jnp.float32
    b16 = jnp.bfloat16
    order = jnp.arange(PIECES)
    same_owner = owner_list[:, None] == owner_list[None, :]
    ranks = jnp.sum(same_owner & (order[None, :] < order[:, None]), axis=1)
    slot_of = owner_list * CAP + ranks

    mine = (owner_list == lax.axis_index("dp"))[:, None, None]
    tile_rows = lax.psum(jnp.where(mine, master[ranks], 0.0).astype(b16), "dp")
    tiles = lax.all_gather(tile_rows, "blk", axis=1, tiled=True)
    query_weight = tiles[0]
    key_weight = tiles[1]
    value_weight = tiles[2]
    out_weight = tiles[3]
    up_weight = jnp.transpose(tiles[4 : 4 + fold], (1, 0, 2)).reshape(width, FF)
    down_weight = tiles[4 + fold :].reshape(FF, width)
    flat_in = inputs.reshape(tokens_here, width).astype(f32)
    normed_one = normalize(flat_in, vectors[0], vectors[1]).astype(b16)
    queries = (jnp.dot(normed_one, query_weight, preferred_element_type=f32) + vectors[4]).astype(
        b16
    )
    keys_here = jnp.dot(normed_one, key_weight, preferred_element_type=f32).astype(b16)
    values_here = (
        jnp.dot(normed_one, value_weight, preferred_element_type=f32) + vectors[5]
    ).astype(b16)
    query_heads = queries.reshape(rows_here, span, HEADS, HEAD_DIM)
    first_len = doc_lengths[:, 0]
    query_seg = (place * span + jnp.arange(span))[None, :] >= first_len[:, None]

    def block_scores(key_block, start):
        count = key_block.shape[1]
        key_heads = key_block.reshape(rows_here, count, HEADS, HEAD_DIM)
        raw = (
            jnp.einsum("rqhd,rkhd->rhqk", query_heads, key_heads, preferred_element_type=f32)
            * scale
        )
        key_seg = (start + jnp.arange(count))[None, :] >= first_len[:, None]
        allowed = query_seg[:, None, :, None] == key_seg[:, None, None, :]
        return (raw, allowed)

    key_rows = keys_here.reshape(rows_here, span, width)
    value_rows = values_here.reshape(rows_here, span, width)
    top = jnp.full((rows_here, HEADS, span), -1e30, f32)
    key_block = lax.all_gather(key_rows, "blk", axis=1, tiled=True)
    value_block = lax.all_gather(value_rows, "blk", axis=1, tiled=True)
    count = key_block.shape[1]
    raw, allowed = block_scores(key_block, jnp.int32(0))
    new_top = jnp.maximum(top, jnp.max(jnp.where(allowed, raw, -1e30), axis=-1))
    weights = jnp.where(allowed, jnp.exp(raw - new_top[..., None]), 0.0)
    value_heads = value_block.reshape(rows_here, count, HEADS, HEAD_DIM)
    update = jnp.einsum(
        "rhqk,rkhd->rhqd", weights.astype(b16), value_heads, preferred_element_type=f32
    )
    total = jnp.sum(weights, axis=-1)
    log_total = new_top + jnp.log(total)
    context_raw = update / total[..., None]
    context_low = jnp.transpose(context_raw, (0, 2, 1, 3)).reshape(tokens_here, width).astype(b16)
    residual = flat_in + (jnp.dot(context_low, out_weight, preferred_element_type=f32) + vectors[6])
    normed_two = normalize(residual, vectors[2], vectors[3]).astype(b16)
    hidden = jnp.dot(normed_two, up_weight, preferred_element_type=f32) + vectors[8:].reshape(FF)
    gelu_exact = partial(jax.nn.gelu, approximate=False)
    active, gelu_pull = jax.vjp(gelu_exact, hidden)
    active_low = active.astype(b16)
    block_out = (
        residual + (jnp.dot(active_low, down_weight, preferred_element_type=f32) + vectors[7])
    ).reshape(rows_here, span, width)
    grad_out = cotangent.reshape(tokens_here, width)
    down_grad = jnp.einsum("tf,td->fd", active_low, grad_out, preferred_element_type=f32)
    down_sum = jnp.sum(grad_out, axis=0, dtype=f32)
    grad_active = jnp.einsum("td,fd->tf", grad_out, down_weight, preferred_element_type=f32)
    grad_hidden = gelu_pull(grad_active)[0].astype(b16)
    up_grad = jnp.einsum("td,tf->df", normed_two, grad_hidden, preferred_element_type=f32)
    up_sum = jnp.sum(grad_hidden, axis=0, dtype=f32)
    ffn_tiles = jnp.concatenate(
        [
            jnp.transpose(up_grad.reshape(width, fold, width), (1, 0, 2)),
            down_grad.reshape(fold, width, width),
        ],
        axis=0,
    )
    grad_normed_two = jnp.einsum("tf,df->td", grad_hidden, up_weight, preferred_element_type=f32)
    unused, second_pull = jax.vjp(normalize, residual, vectors[2], vectors[3])
    residual_part, gain_two_grad, shift_two_grad = second_pull(grad_normed_two)
    grad_residual = grad_out.astype(f32) + residual_part
    grad_attended = grad_residual.astype(b16)
    out_grad = jnp.einsum("tm,td->md", context_low, grad_attended, preferred_element_type=f32)
    out_sum = jnp.sum(grad_attended, axis=0, dtype=f32)
    grad_context = jnp.einsum(
        "td,md->tm", grad_attended, out_weight, preferred_element_type=f32
    ).astype(b16)
    grad_heads = grad_context.reshape(rows_here, span, HEADS, HEAD_DIM)
    delta = jnp.einsum("rqhd,rhqd->rhq", grad_heads.astype(f32), context_raw)
    key_all, value_all = (
        lax.all_gather(key_rows, "blk", axis=1, tiled=True),
        lax.all_gather(value_rows, "blk", axis=1, tiled=True),
    )
    key_size = min(512, LEN)

    def back_block(index, carry):
        grad_query, key_total, value_total = carry
        start = index * key_size
        key_block = lax.dynamic_slice_in_dim(key_all, start, key_size, 1)
        value_block = lax.dynamic_slice_in_dim(value_all, start, key_size, 1)
        raw, allowed = block_scores(key_block, start)
        weights_back = jnp.where(allowed, jnp.exp(raw - log_total[..., None]), 0.0)
        key_heads = key_block.reshape(rows_here, key_size, HEADS, HEAD_DIM)
        value_heads = value_block.reshape(rows_here, key_size, HEADS, HEAD_DIM)
        value_grad = jnp.einsum(
            "rhqk,rqhd->rkhd", weights_back.astype(b16), grad_heads, preferred_element_type=f32
        )
        weight_grad = jnp.einsum(
            "rqhd,rkhd->rhqk", grad_heads, value_heads, preferred_element_type=f32
        )
        score_grad = (weights_back * (weight_grad - delta[..., None])).astype(b16)
        grad_query = (
            grad_query
            + jnp.einsum("rhqk,rkhd->rqhd", score_grad, key_heads, preferred_element_type=f32)
            * scale
        )
        key_grad = (
            jnp.einsum("rhqk,rqhd->rkhd", score_grad, query_heads, preferred_element_type=f32)
            * scale
        )
        key_total = lax.dynamic_update_slice_in_dim(
            key_total, key_grad.reshape(rows_here, key_size, width), start, 1
        )
        value_total = lax.dynamic_update_slice_in_dim(
            value_total, value_grad.reshape(rows_here, key_size, width), start, 1
        )
        return (grad_query, key_total, value_total)

    zero_rows = jnp.zeros((rows_here, LEN, width), f32)
    grad_query, key_total, value_total = lax.fori_loop(
        0,
        LEN // key_size,
        back_block,
        (jnp.zeros((rows_here, span, HEADS, HEAD_DIM), f32), zero_rows, zero_rows),
    )
    key_grad_here, value_grad_here = (
        lax.psum_scatter(
            key_total.astype(jnp.bfloat16), "blk", scatter_dimension=1, tiled=True
        ).astype(jnp.float32),
        lax.psum_scatter(
            value_total.astype(jnp.bfloat16), "blk", scatter_dimension=1, tiled=True
        ).astype(jnp.float32),
    )
    query_low = grad_query.reshape(tokens_here, width).astype(b16)
    key_low = key_grad_here.reshape(tokens_here, width).astype(b16)
    value_low = value_grad_here.reshape(tokens_here, width).astype(b16)
    query_tile = jnp.einsum("td,te->de", normed_one, query_low, preferred_element_type=f32)
    key_tile = jnp.einsum("td,te->de", normed_one, key_low, preferred_element_type=f32)
    value_tile = jnp.einsum("td,te->de", normed_one, value_low, preferred_element_type=f32)
    grad_normed_one = (
        jnp.einsum("te,de->td", query_low, query_weight, preferred_element_type=f32)
        + jnp.einsum("te,de->td", key_low, key_weight, preferred_element_type=f32)
        + jnp.einsum("te,de->td", value_low, value_weight, preferred_element_type=f32)
    )
    unused, first_pull = jax.vjp(normalize, flat_in, vectors[0], vectors[1])
    input_part, gain_one_grad, shift_one_grad = first_pull(grad_normed_one)
    input_grad = (grad_residual + input_part).reshape(rows_here, span, width)
    vector_grads = jnp.concatenate(
        [
            jnp.stack(
                [
                    gain_one_grad,
                    shift_one_grad,
                    gain_two_grad,
                    shift_two_grad,
                    jnp.sum(query_low, axis=0, dtype=f32),
                    jnp.sum(value_low, axis=0, dtype=f32),
                    out_sum,
                    down_sum,
                ]
            ),
            up_sum.reshape(fold, width),
        ],
        axis=0,
    )
    attn_tiles = jnp.stack([query_tile, key_tile, value_tile, out_grad])
    piece_share, vector_share = (
        lax.psum_scatter(
            jnp.concatenate([attn_tiles, ffn_tiles], axis=0).astype(jnp.bfloat16),
            "blk",
            scatter_dimension=1,
            tiled=True,
        ).astype(jnp.float32),
        lax.psum_scatter(
            vector_grads.astype(jnp.bfloat16), "blk", scatter_dimension=1, tiled=True
        ).astype(jnp.float32),
    )
    own_slots = lax.axis_index("dp") * CAP + jnp.arange(CAP)
    pick = (own_slots[:, None] == slot_of[None, :]).astype(f32)
    occupied = jnp.sum(pick, axis=1)[:, None, None]
    total_share, vector_total = (
        lax.psum(piece_share.astype(jnp.bfloat16), "dp").astype(jnp.float32),
        lax.psum(vector_share.astype(jnp.bfloat16), "dp").astype(jnp.float32),
    )
    slot_grads = jnp.einsum("cp,prd->crd", pick, total_share, precision=lax.Precision.HIGHEST)
    new_master, new_first, new_second = adam_step(
        master, slot_grads, first_moment, second_moment, RATE
    )
    columns = vector_first.shape[1]
    vector_cols = lax.dynamic_slice_in_dim(vectors, place * columns, columns, 1)
    new_vectors, new_vector_first, new_vector_second = adam_step(
        vector_cols, vector_total, vector_first, vector_second, VEC_RATE
    )
    return (
        block_out,
        input_grad,
        new_master * occupied,
        new_first * occupied,
        new_second * occupied,
        new_vectors,
        new_vector_first,
        new_vector_second,
    )


f32 = jnp.float32
b16 = jnp.bfloat16
LOG2E = 1.4426950408889634
MIB = 1024 * 1024
PAIRS = HEADS // 2
PAIR = 2 * HEAD_DIM


def dot_nn(left, right):
    return lax.dot_general(left, right, (((1,), (0,)), ((), ())), preferred_element_type=f32)


def dot_nt(left, right):
    return lax.dot_general(left, right, (((1,), (1,)), ((), ())), preferred_element_type=f32)


def dot_tn(left, right):
    return lax.dot_general(left, right, (((0,), (0,)), ((), ())), preferred_element_type=f32)


def norm_parts(values_in):
    center = jnp.mean(values_in, axis=-1, keepdims=True)
    offset = values_in - center
    spread = jnp.mean(offset * offset, axis=-1, keepdims=True)
    rstd = lax.rsqrt(spread + EPS_NORM)
    return offset * rstd, rstd


def norm_back(grad, unit, rstd, gain):
    scaled = grad * gain
    first = jnp.mean(scaled, axis=-1, keepdims=True)
    second = jnp.mean(scaled * unit, axis=-1, keepdims=True)
    return rstd * (scaled - first - unit * second)


def gelu_parts(value):
    bell = jnp.exp2(value * value * (-0.5 * LOG2E))
    ratio = pl.reciprocal(1.0 + (0.3275911 * 0.7071067811865476) * jnp.abs(value))
    poly = 0.5 * 1.061405429
    poly = poly * ratio + 0.5 * -1.453152027
    poly = poly * ratio + 0.5 * 1.421413741
    poly = poly * ratio + 0.5 * -0.284496736
    poly = poly * ratio + 0.5 * 0.254829592
    tail = poly * ratio * bell
    cdf = jnp.where(value >= 0.0, 1.0 - tail, tail)
    return value * cdf, cdf + value * (bell * 0.3989422804014327)


def project_kernel(x_ref, w_ref, vec_ref, k_ref, v_ref, t_ref, n_ref):
    unit, unused = norm_parts(x_ref[...].astype(f32))
    normed = (unit * vec_ref[0:1, :] + vec_ref[1:2, :]).astype(b16)
    n_ref[...] = normed.T
    queries = (dot_nn(normed, w_ref[0]) + vec_ref[4:5, :]) * (HEAD_DIM**-0.5 * LOG2E)
    t_ref[0] = queries.astype(b16).T
    keys = dot_nn(normed, w_ref[1]).astype(b16)
    k_ref[...] = keys
    t_ref[1] = keys.T
    values = (dot_nn(normed, w_ref[2]) + vec_ref[5:6, :]).astype(b16)
    v_ref[...] = values
    t_ref[2] = values.T


def project(x, weights, vectors):
    tokens = x.shape[0]
    size = 512
    return pl.pallas_call(
        project_kernel,
        grid=(tokens // size,),
        in_specs=[
            pl.BlockSpec((size, D), lambda i: (i, 0)),
            pl.BlockSpec((3, D, D), lambda i: (0, 0, 0), pipeline_mode=pl.Buffered(1)),
            pl.BlockSpec((PIECES, D), lambda i: (0, 0)),
        ],
        out_specs=[
            pl.BlockSpec((size, D), lambda i: (i, 0)),
            pl.BlockSpec((size, D), lambda i: (i, 0)),
            pl.BlockSpec((3, D, size), lambda i: (0, 0, i)),
            pl.BlockSpec((D, size), lambda i: (0, i)),
        ],
        out_shape=[
            jax.ShapeDtypeStruct((tokens, D), b16),
            jax.ShapeDtypeStruct((tokens, D), b16),
            jax.ShapeDtypeStruct((3, D, tokens), b16),
            jax.ShapeDtypeStruct((D, tokens), b16),
        ],
        compiler_params=pltpu.CompilerParams(vmem_limit_bytes=48 * MIB),
        cost_estimate=pl.CostEstimate(
            flops=6 * tokens * D * D, bytes_accessed=14 * tokens * D + 6 * D * D, transcendentals=0
        ),
        name="project",
    )(x, weights, vectors)


def head_only(block, head):
    lane = lax.broadcasted_iota(jnp.int32, block.shape, 1)
    keep = (lane >= head * HEAD_DIM) & (lane < (head + 1) * HEAD_DIM)
    return jnp.where(keep, block, jnp.zeros_like(block))


def attend_kernel(bias_ref, k_ref, q_ref, v_ref, p_ref, r_ref, o_ref, c_ref):
    half = LEN // 2
    bias = bias_ref[pl.program_id(0)]
    for head in range(2):
        part = slice(head * HEAD_DIM, (head + 1) * HEAD_DIM)
        keys = head_only(k_ref[...], head)
        for step in range(2):
            cols = slice(step * half, (step + 1) * half)
            rows = slice((1 - step) * half, (2 - step) * half)
            near = dot_nn(keys[cols], q_ref[0, :, cols])
            far = dot_nn(keys[rows], q_ref[0, :, cols]) + bias
            top = jnp.maximum(jnp.max(near, 0, keepdims=True), jnp.max(far, 0, keepdims=True))
            near = jnp.exp2(near - top)
            far = jnp.exp2(far - top)
            total = jnp.sum(near, 0, keepdims=True) + jnp.sum(far, 0, keepdims=True)
            recip = 1.0 / total
            p_ref[head, cols, cols] = near.astype(b16)
            p_ref[head, rows, cols] = far.astype(b16)
            r_ref[0, head : head + 1, cols] = recip
            out = dot_nn(v_ref[0, part, :], p_ref[head, :, cols]) * recip
            o_ref[part, cols] = out.astype(b16)
    c_ref[...] = o_ref[...].T


def attend(bias, keys, turned):
    tokens = keys.shape[0]
    rows = tokens // LEN
    return pl.pallas_call(
        attend_kernel,
        grid=(rows, PAIRS),
        in_specs=[
            pl.BlockSpec(memory_space=pltpu.SMEM),
            pl.BlockSpec((LEN, PAIR), lambda r, h: (r, h)),
            pl.BlockSpec((1, PAIR, LEN), lambda r, h: (0, h, r)),
            pl.BlockSpec((1, PAIR, LEN), lambda r, h: (2, h, r)),
        ],
        out_specs=[
            pl.BlockSpec((2, LEN, LEN), lambda r, h: (r * PAIRS + h, 0, 0)),
            pl.BlockSpec((1, 2, LEN), lambda r, h: (r * PAIRS + h, 0, 0)),
            pl.BlockSpec((PAIR, LEN), lambda r, h: (h, r)),
            pl.BlockSpec((LEN, PAIR), lambda r, h: (r, h)),
        ],
        out_shape=[
            jax.ShapeDtypeStruct((rows * HEADS, LEN, LEN), b16),
            jax.ShapeDtypeStruct((rows * PAIRS, 2, LEN), f32),
            jax.ShapeDtypeStruct((D, tokens), b16),
            jax.ShapeDtypeStruct((tokens, D), b16),
        ],
        compiler_params=pltpu.CompilerParams(vmem_limit_bytes=56 * MIB),
        cost_estimate=pl.CostEstimate(
            flops=16 * tokens * LEN * D,
            bytes_accessed=2 * rows * HEADS * LEN * LEN + 10 * tokens * D,
            transcendentals=rows * HEADS * LEN * LEN,
        ),
        name="attend",
    )(bias, keys, turned, turned)


def attend_back_kernel(p_ref, r_ref, v_ref, q_ref, k_ref, o_ref, g_ref, d_ref):
    half = LEN // 2
    for head in range(2):
        part = slice(head * HEAD_DIM, (head + 1) * HEAD_DIM)
        values = head_only(v_ref[...], head)
        recip = r_ref[0, head : head + 1, :]
        grad = g_ref[part, :].astype(f32) * recip
        delta = jnp.sum(grad * o_ref[part, :].astype(f32), 0, keepdims=True)
        grad = grad.astype(b16)
        wide = jnp.concatenate([grad, grad], axis=0)
        value_grad = jnp.zeros((HEAD_DIM, LEN), f32)
        key_grad = jnp.zeros((HEAD_DIM, LEN), f32)
        for step in range(2):
            cols = slice(step * half, (step + 1) * half)
            weights = p_ref[head, :, cols]
            slope = dot_nn(values, wide[:, cols]) - delta[:, cols]
            slope = (weights.astype(f32) * slope).astype(b16)
            value_grad = value_grad + dot_nt(grad[:, cols], weights)
            key_grad = key_grad + dot_nt(q_ref[0, part, cols], slope)
            query_grad = dot_nn(k_ref[0, part, :], slope) * (HEAD_DIM**-0.5)
            d_ref[0, part, cols] = query_grad.astype(b16)
        d_ref[1, part, :] = (key_grad * (1.0 / LOG2E)).astype(b16)
        d_ref[2, part, :] = value_grad.astype(b16)


def attend_back(weights, recips, values, turned, context, grad):
    tokens = values.shape[0]
    rows = tokens // LEN
    return pl.pallas_call(
        attend_back_kernel,
        grid=(rows, PAIRS),
        in_specs=[
            pl.BlockSpec((2, LEN, LEN), lambda r, h: (r * PAIRS + h, 0, 0)),
            pl.BlockSpec((1, 2, LEN), lambda r, h: (r * PAIRS + h, 0, 0)),
            pl.BlockSpec((LEN, PAIR), lambda r, h: (r, h)),
            pl.BlockSpec((1, PAIR, LEN), lambda r, h: (0, h, r)),
            pl.BlockSpec((1, PAIR, LEN), lambda r, h: (1, h, r)),
            pl.BlockSpec((PAIR, LEN), lambda r, h: (h, r)),
            pl.BlockSpec((PAIR, LEN), lambda r, h: (h, r)),
        ],
        out_specs=pl.BlockSpec((3, PAIR, LEN), lambda r, h: (0, h, r)),
        out_shape=jax.ShapeDtypeStruct((3, D, tokens), b16),
        compiler_params=pltpu.CompilerParams(vmem_limit_bytes=56 * MIB),
        cost_estimate=pl.CostEstimate(
            flops=32 * tokens * LEN * D,
            bytes_accessed=2 * rows * HEADS * LEN * LEN + 16 * tokens * D,
            transcendentals=0,
        ),
        name="attend_back",
    )(weights, recips, values, turned, turned, context, grad)


def feed_kernel(
    c_ref, o_ref, x_ref, g_ref, w_ref, vec_ref,
    y_ref, r_ref, d_ref, sums_ref, tiles_ref,
    acc_ref, stage_ref, sem_ref,
):
    fold = FF // D
    step = pl.program_id(0)

    @pl.when(step == 0)
    def clear():
        acc_ref[...] = jnp.zeros_like(acc_ref)
        sums_ref[...] = jnp.zeros_like(sums_ref)

    residual = x_ref[...].astype(f32) + (dot_nn(c_ref[...], w_ref[0]) + vec_ref[6:7, :])
    unit, rstd = norm_parts(residual)
    gain = vec_ref[2:3, :]
    normed = (unit * gain + vec_ref[3:4, :]).astype(b16)
    turned = normed.T
    cot = g_ref[...]
    out = residual + vec_ref[7:8, :]
    grad = jnp.zeros_like(out)
    for part in range(fold):
        hidden = dot_nn(normed, w_ref[1 + part]) + vec_ref[8 + part : 9 + part, :]
        pulled = dot_nt(cot, w_ref[1 + fold + part])
        active, slope = gelu_parts(hidden)
        active = active.astype(b16)
        pulled = (pulled * slope).astype(b16)
        out = out + dot_nn(active, w_ref[1 + fold + part])
        grad = grad + dot_nt(pulled, w_ref[1 + part])
        acc_ref[1 + part] += dot_nn(turned, pulled)
        acc_ref[1 + fold + part] += dot_tn(active, cot)
        sums_ref[4 + part : 5 + part, :] += jnp.sum(pulled.astype(f32), 0, keepdims=True)
    y_ref[...] = out.astype(b16)
    wide = cot.astype(f32)
    sums_ref[0:1, :] += jnp.sum(grad * unit, 0, keepdims=True)
    sums_ref[1:2, :] += jnp.sum(grad, 0, keepdims=True)
    sums_ref[3:4, :] += jnp.sum(wide, 0, keepdims=True)
    back = wide + norm_back(grad, unit, rstd, gain)
    r_ref[...] = back
    low = back.astype(b16)
    sums_ref[2:3, :] += jnp.sum(low.astype(f32), 0, keepdims=True)
    d_ref[...] = dot_nt(w_ref[0], low).astype(b16)
    acc_ref[0] += dot_nn(o_ref[...], low)

    @pl.when(step == pl.num_programs(0) - 1)
    def send():
        count = 1 + 2 * fold
        copies = []
        for part in range(count):
            if part >= 2:
                copies[part - 2].wait()
            stage_ref[part % 2] = acc_ref[part].astype(b16)
            copy = pltpu.make_async_copy(stage_ref.at[part % 2], tiles_ref.at[part], sem_ref.at[part % 2])
            copy.start()
            copies.append(copy)
        copies[count - 2].wait()
        copies[count - 1].wait()


def feed(context, turned, x, cot, weights, vectors):
    tokens = x.shape[0]
    size = 256
    count = 1 + 2 * (FF // D)
    token_block = pl.BlockSpec((size, D), lambda i: (i, 0))
    turned_block = pl.BlockSpec((D, size), lambda i: (0, i))
    return pl.pallas_call(
        feed_kernel,
        grid=(tokens // size,),
        in_specs=[
            token_block,
            turned_block,
            token_block,
            token_block,
            pl.BlockSpec((count, D, D), lambda i: (0, 0, 0), pipeline_mode=pl.Buffered(1)),
            pl.BlockSpec((PIECES, D), lambda i: (0, 0)),
        ],
        out_specs=[
            token_block,
            token_block,
            turned_block,
            pl.BlockSpec((8, D), lambda i: (0, 0)),
            pl.BlockSpec(memory_space=pl.ANY),
        ],
        out_shape=[
            jax.ShapeDtypeStruct((tokens, D), b16),
            jax.ShapeDtypeStruct((tokens, D), f32),
            jax.ShapeDtypeStruct((D, tokens), b16),
            jax.ShapeDtypeStruct((8, D), f32),
            jax.ShapeDtypeStruct((count, D, D), b16),
        ],
        scratch_shapes=[
            pltpu.VMEM((count, D, D), f32),
            pltpu.VMEM((2, D, D), b16),
            pltpu.SemaphoreType.DMA((2,)),
        ],
        compiler_params=pltpu.CompilerParams(vmem_limit_bytes=60 * MIB),
        cost_estimate=pl.CostEstimate(
            flops=6 * count * tokens * D * D,
            bytes_accessed=18 * tokens * D + 4 * count * D * D,
            transcendentals=2 * tokens * FF,
        ),
        name="feed",
    )(context, turned, x, cot, weights, vectors)


def finish_kernel(d_ref, n_ref, x_ref, r_ref, w_ref, vec_ref, i_ref, sums_ref, tiles_ref, acc_ref):
    step = pl.program_id(0)

    @pl.when(step == 0)
    def clear():
        acc_ref[...] = jnp.zeros_like(acc_ref)
        sums_ref[...] = jnp.zeros_like(sums_ref)

    ones = jnp.ones((8, d_ref.shape[2]), b16)
    grad = None
    for part in range(3):
        acc_ref[part] += dot_nt(n_ref[...], d_ref[part])
        term = dot_nn(w_ref[part], d_ref[part])
        grad = term if part == 0 else grad + term
    sums_ref[2:3, :] += dot_nt(ones, d_ref[0])[0:1]
    sums_ref[3:4, :] += dot_nt(ones, d_ref[2])[0:1]
    grad = grad.T
    unit, rstd = norm_parts(x_ref[...].astype(f32))
    sums_ref[0:1, :] += jnp.sum(grad * unit, 0, keepdims=True)
    sums_ref[1:2, :] += jnp.sum(grad, 0, keepdims=True)
    total = r_ref[...] + norm_back(grad, unit, rstd, vec_ref[0:1, :])
    i_ref[...] = total.astype(b16)

    @pl.when(step == pl.num_programs(0) - 1)
    def send():
        tiles_ref[...] = acc_ref[...].astype(b16)


def finish(grads, normed, x, residual, weights, vectors):
    tokens = x.shape[0]
    size = 512
    token_block = pl.BlockSpec((size, D), lambda i: (i, 0))
    return pl.pallas_call(
        finish_kernel,
        grid=(tokens // size,),
        in_specs=[
            pl.BlockSpec((3, D, size), lambda i: (0, 0, i)),
            pl.BlockSpec((D, size), lambda i: (0, i)),
            token_block,
            token_block,
            pl.BlockSpec((3, D, D), lambda i: (0, 0, 0), pipeline_mode=pl.Buffered(1)),
            pl.BlockSpec((PIECES, D), lambda i: (0, 0)),
        ],
        out_specs=[
            token_block,
            pl.BlockSpec((8, D), lambda i: (0, 0)),
            pl.BlockSpec((3, D, D), lambda i: (0, 0, 0)),
        ],
        out_shape=[
            jax.ShapeDtypeStruct((tokens, D), b16),
            jax.ShapeDtypeStruct((8, D), f32),
            jax.ShapeDtypeStruct((3, D, D), b16),
        ],
        scratch_shapes=[pltpu.VMEM((3, D, D), f32)],
        compiler_params=pltpu.CompilerParams(vmem_limit_bytes=56 * MIB),
        cost_estimate=pl.CostEstimate(
            flops=12 * tokens * D * D, bytes_accessed=18 * tokens * D + 12 * D * D, transcendentals=0
        ),
        name="finish",
    )(grads, normed, x, residual, weights, vectors)


MESH = pl.DeviceIdType.MESH
HALF = D // 2
UNIT = 128
UNITS = HALF // UNIT
STEPS = 6


class Place:
    def __init__(self):
        me = lax.axis_index("dp")
        self.core = lax.axis_index("blk")
        self.bits = [lax.rem(me // weight, 2) for weight in (1, 2, 4, 8)]
        self.partners = [
            me + weight - 2 * weight * bit for weight, bit in zip((1, 2, 4, 8), self.bits)
        ]
        self.other = 1 - self.core

    def greet(self):
        barrier = pltpu.get_barrier_semaphore()
        for partner in self.partners:
            pl.semaphore_signal(barrier, 1, device_id={"dp": partner}, device_id_type=MESH)
        pl.semaphore_signal(barrier, 1, device_id={"blk": self.other}, device_id_type=MESH)
        pl.semaphore_wait(barrier, 5)


def remote(source, target, sems, index, device):
    return pltpu.make_async_remote_copy(
        src_ref=source,
        dst_ref=target,
        send_sem=sems[0].at[index],
        recv_sem=sems[1].at[index],
        device_id=device,
        device_id_type=MESH,
    )


def rows_at(start, count):
    return pl.ds(pl.multiple_of(start, 16), count)


class Mover:
    def __init__(self, place, work, wide, narrow, sems):
        self.place, self.work, self.wide, self.narrow, self.sems = place, work, wide, narrow, sems

    def copies(self, tile, part):
        place = self.place
        unit = tile * UNITS + part
        first, second = (0, 1) if unit % 2 == 0 else (1, 0)
        base = place.core * HALF + part * UNIT
        quarter, eighth = UNIT // 2, UNIT // 4
        near = base + place.bits[first] * quarter
        far = base + quarter - place.bits[first] * quarter
        keep = near + place.bits[second] * eighth
        give = near + eighth - place.bits[second] * eighth
        tile_ref = self.work.at[tile]
        near_rows, keep_rows = rows_at(near, quarter), rows_at(keep, eighth)
        partner = [{"dp": p} for p in self.place.partners]
        plan = [
            (tile_ref.at[rows_at(far, quarter)], self.wide.at[unit], partner[first]),
            (tile_ref.at[rows_at(give, eighth)], self.narrow.at[unit, 0], partner[second]),
            (tile_ref.at[keep_rows], self.narrow.at[unit, 1], partner[2]),
            (tile_ref.at[keep_rows], self.narrow.at[unit, 2], partner[3]),
            (tile_ref.at[keep_rows], tile_ref.at[keep_rows], partner[second]),
            (tile_ref.at[near_rows], tile_ref.at[near_rows], partner[first]),
        ]

        def made(index):
            source, target, device = plan[index]
            return remote(source, target, self.sems, (unit, index), device)

        landed = [
            (near_rows, self.wide.at[unit]),
            (keep_rows, self.narrow.at[unit, 0]),
            (keep_rows, self.narrow.at[unit, 1]),
            (keep_rows, self.narrow.at[unit, 2]),
        ]
        return made, landed

    def step(self, tile, part, index):
        made, landed = self.copies(tile, part)
        if index > 0:
            made(index - 1).wait()
            if index <= 4:
                rows, source = landed[index - 1]
                total = self.work[tile, rows].astype(f32) + source[...].astype(f32)
                self.work[tile, rows] = total.astype(b16)
        if index < STEPS:
            made(index).start()


def mover_scratch(tiles):
    units = tiles * UNITS
    return [
        pltpu.VMEM((tiles, D, D), b16),
        pltpu.VMEM((units, UNIT // 2, D), b16),
        pltpu.VMEM((units, 3, UNIT // 4, D), b16),
        pltpu.SemaphoreType.DMA((units, STEPS)),
        pltpu.SemaphoreType.DMA((units, STEPS)),
        pltpu.SemaphoreType.DMA((tiles,)),
        pltpu.SemaphoreType.DMA((tiles,)),
    ]


class Spread:
    def __init__(self, place, count, first, own, rank, master, scratch):
        work, wide, narrow, send, receive, pair_send, pair_receive = scratch
        self.place, self.count, self.first, self.work = place, count, first, work
        self.own, self.rank, self.master = own, rank, master
        self.pair_sems = (pair_send, pair_receive)
        self.mover = Mover(place, work, wide, narrow, (send, receive))

    def pair(self, tile):
        rows = self.work.at[tile, rows_at(self.place.core * HALF, HALF)]
        return remote(rows, rows, self.pair_sems, tile, {"blk": self.place.other})

    def load(self, tile):
        piece = self.master[self.rank[self.first + tile]]
        piece = jnp.where(self.own[self.first + tile] == 1, piece, jnp.zeros_like(piece))
        self.work[tile, rows_at(self.place.core * HALF, HALF)] = piece.astype(b16)

    def step(self, tile, index):
        if index == 0:
            self.load(tile)
        if index <= STEPS:
            for part in range(UNITS):
                self.mover.step(tile, part, index)
        if index == STEPS:
            self.pair(tile).start()
        if index == STEPS + 1:
            self.pair(tile).wait()

    steps = STEPS + 2


class Reduce:
    def __init__(self, place, count, scratch):
        work, wide, narrow, send, receive, pair_send, pair_receive, land = scratch
        self.place, self.count, self.work, self.land = place, count, work, land
        self.pair_sems = (pair_send, pair_receive)
        self.mover = Mover(place, work, wide, narrow, (send, receive))

    def pair(self, tile):
        rows = self.work.at[tile, rows_at(self.place.other * HALF, HALF)]
        return remote(rows, self.land.at[tile], self.pair_sems, tile, {"blk": self.place.other})

    def step(self, tile, index):
        if index == 0:
            self.pair(tile).start()
        if index == 1:
            self.pair(tile).wait()
            rows = rows_at(self.place.core * HALF, HALF)
            total = self.work[tile, rows].astype(f32) + self.land[tile].astype(f32)
            self.work[tile, rows] = total.astype(b16)
        if index >= 1:
            for part in range(UNITS):
                self.mover.step(tile, part, index - 1)

    steps = STEPS + 2


def run_all(stream):
    for tick in range(stream.count + stream.steps - 1):
        for tile in range(stream.count):
            if 0 <= tick - tile < stream.steps:
                stream.step(tile, tick - tile)


def own_part(refs, sems, place, rows, span):
    made = []
    for index, (source, target) in enumerate(refs):
        here = pl.ds(place.core * span, span)
        made.append(
            pltpu.make_async_copy(
                source.at[pl.ds(place.core * rows, rows)], target.at[:, here], sems[2].at[index]
            )
        )
        made.append(
            remote(
                source.at[pl.ds(place.other * rows, rows)],
                target.at[:, here],
                sems,
                index,
                {"blk": place.other},
            )
        )
    return made


def back_part(refs, sems, place, rows, span):
    made = []
    for index, (source, target) in enumerate(refs):
        there = pl.ds(place.core * rows, rows)
        made.append(
            pltpu.make_async_copy(
                source.at[:, pl.ds(place.core * span, span)], target.at[there], sems[2].at[index]
            )
        )
        made.append(
            remote(
                source.at[:, pl.ds(place.other * span, span)],
                target.at[there],
                sems,
                index,
                {"blk": place.other},
            )
        )
    return made


def part_sems(count):
    return [pltpu.SemaphoreType.DMA((count,)) for unused in range(3)]


def spread_kernel(
    own, rank, master, x_in, c_in, x_out, c_out, one_out, two_out, *scratch
):
    place = Place()
    place.greet()
    rows, span = x_in.shape[0] // 2, x_in.shape[1]
    moved = own_part([(x_in, x_out), (c_in, c_out)], scratch[:3], place, rows, span)
    for copy in moved:
        copy.start()
    stream = Spread(place, PIECES, 0, own, rank, master, scratch[4:])
    run_all(stream)
    copies = [
        pltpu.make_async_copy(stream.work.at[pl.ds(0, 3)], one_out, scratch[3].at[0]),
        pltpu.make_async_copy(stream.work.at[pl.ds(3, PIECES - 3)], two_out, scratch[3].at[1]),
    ]
    for copy in copies:
        copy.start()
    for copy in copies + moved:
        copy.wait()


def spread(own, rank, master, inputs, cotangent):
    rows, span = inputs.shape[0] // 2, inputs.shape[1]
    any_spec = pl.BlockSpec(memory_space=pl.ANY)
    smem = pl.BlockSpec(memory_space=pltpu.SMEM)
    whole = jax.ShapeDtypeStruct((rows, 2 * span, D), b16)
    return pl.pallas_call(
        spread_kernel,
        in_specs=[smem, smem, pl.BlockSpec(memory_space=pltpu.VMEM), any_spec, any_spec],
        out_specs=[any_spec] * 4,
        out_shape=[
            whole,
            whole,
            jax.ShapeDtypeStruct((3, D, D), b16),
            jax.ShapeDtypeStruct((PIECES - 3, D, D), b16),
        ],
        scratch_shapes=part_sems(2) + [pltpu.SemaphoreType.DMA((2,))] + mover_scratch(PIECES),
        compiler_params=pltpu.CompilerParams(
            collective_id=0, has_side_effects=True, vmem_limit_bytes=56 * MIB
        ),
        name="spread",
    )(own, rank, master, inputs, cotangent)


def reduce_kernel(tiles_in, y_in, y_out, total_out, *scratch):
    place = Place()
    place.greet()
    rows, span = y_in.shape[0], y_in.shape[1] // 2
    moved = back_part([(y_in, y_out)], scratch[:3], place, rows, span)
    for copy in moved:
        copy.start()
    stream = Reduce(place, tiles_in.shape[0], scratch[4:])
    load = pltpu.make_async_copy(tiles_in, stream.work, scratch[3].at[0])
    load.start()
    load.wait()
    run_all(stream)
    store = pltpu.make_async_copy(
        stream.work.at[:, rows_at(place.core * HALF, HALF)], total_out, scratch[3].at[1]
    )
    store.start()
    store.wait()
    for copy in moved:
        copy.wait()


def reduce_tiles(tiles, outputs, number):
    count = tiles.shape[0]
    rows, length = outputs.shape[:2]
    any_spec = pl.BlockSpec(memory_space=pl.ANY)
    return pl.pallas_call(
        reduce_kernel,
        in_specs=[any_spec] * 2,
        out_specs=[any_spec] * 2,
        out_shape=[
            jax.ShapeDtypeStruct((2 * rows, length // 2, D), b16),
            jax.ShapeDtypeStruct((count, HALF, D), b16),
        ],
        scratch_shapes=part_sems(1)
        + [pltpu.SemaphoreType.DMA((2,))]
        + mover_scratch(count)
        + [pltpu.VMEM((count, HALF, D), b16)],
        compiler_params=pltpu.CompilerParams(
            collective_id=number, has_side_effects=True, vmem_limit_bytes=56 * MIB
        ),
        name="reduce_tiles",
    )(tiles, outputs)


def reduce_last_kernel(tiles_in, vec_in, y_in, y_out, total_out, vec_out, *scratch):
    place = Place()
    place.greet()
    vec_land, vec_send, vec_receive = scratch[:3]
    devices = [{"blk": place.other}] + [{"dp": p} for p in place.partners]

    def vector_step(index):
        copy = remote(
            vec_out.at[...],
            vec_land.at[index],
            (vec_send, vec_receive),
            index,
            devices[index],
        )
        return copy

    vec_out[...] = vec_in[...]
    vector_step(0).start()
    rest = scratch[3:]
    rows, span = y_in.shape[0], y_in.shape[1] // 2
    moved = back_part([(y_in, y_out)], rest[:3], place, rows, span)
    for copy in moved:
        copy.start()
    stream = Reduce(place, tiles_in.shape[0], rest[4:])
    load = pltpu.make_async_copy(tiles_in, stream.work, rest[3].at[0])
    load.start()
    load.wait()
    for tick in range(stream.count + stream.steps - 1):
        for tile in range(stream.count):
            if 0 <= tick - tile < stream.steps:
                stream.step(tile, tick - tile)
        if tick < 5:
            vector_step(tick).wait()
            vec_out[...] += vec_land[tick]
            if tick < 4:
                vector_step(tick + 1).start()
    store = pltpu.make_async_copy(
        stream.work.at[:, rows_at(place.core * HALF, HALF)], total_out, rest[3].at[1]
    )
    store.start()
    store.wait()
    for copy in moved:
        copy.wait()


def reduce_last(tiles, vectors, outputs, number):
    count = tiles.shape[0]
    rows, length = outputs.shape[:2]
    any_spec = pl.BlockSpec(memory_space=pl.ANY)
    vmem = pl.BlockSpec(memory_space=pltpu.VMEM)
    return pl.pallas_call(
        reduce_last_kernel,
        in_specs=[any_spec, vmem, any_spec],
        out_specs=[any_spec, any_spec, vmem],
        out_shape=[
            jax.ShapeDtypeStruct((2 * rows, length // 2, D), b16),
            jax.ShapeDtypeStruct((count, HALF, D), b16),
            jax.ShapeDtypeStruct(vectors.shape, f32),
        ],
        scratch_shapes=[
            pltpu.VMEM((5,) + vectors.shape, f32),
            pltpu.SemaphoreType.DMA((5,)),
            pltpu.SemaphoreType.DMA((5,)),
        ]
        + part_sems(1)
        + [pltpu.SemaphoreType.DMA((2,))]
        + mover_scratch(count)
        + [pltpu.VMEM((count, HALF, D), b16)],
        compiler_params=pltpu.CompilerParams(
            collective_id=number, has_side_effects=True, vmem_limit_bytes=56 * MIB
        ),
        name="reduce_last",
    )(tiles, vectors, outputs)


def update_kernel(chosen, used, one, two, w_ref, m_ref, s_ref, w_out, m_out, s_out):
    slot = pl.program_id(0)
    grad = jnp.where(chosen[slot] < 3, one[0], two[0]).astype(f32)
    keep = used[slot] == 1
    parts = adam_step(w_ref[0], grad, m_ref[0], s_ref[0], RATE)
    for target, part in zip((w_out, m_out, s_out), parts):
        target[0] = jnp.where(keep, part, jnp.zeros_like(part))


def update(chosen, used, one, two, master, first, second):
    slots = master.shape[0]
    size = HALF // 2
    state = pl.BlockSpec((1, size, D), lambda s, b, chosen, used: (s, b, 0))
    return pl.pallas_call(
        update_kernel,
        grid_spec=pltpu.PrefetchScalarGridSpec(
            num_scalar_prefetch=2,
            grid=(slots, HALF // size),
            in_specs=[
                pl.BlockSpec(
                    (1, size, D), lambda s, b, chosen, used: (jnp.minimum(chosen[s], 2), b, 0)
                ),
                pl.BlockSpec(
                    (1, size, D), lambda s, b, chosen, used: (jnp.maximum(chosen[s] - 3, 0), b, 0)
                ),
                state,
                state,
                state,
            ],
            out_specs=[state] * 3,
        ),
        out_shape=[jax.ShapeDtypeStruct(master.shape, f32)] * 3,
        compiler_params=pltpu.CompilerParams(vmem_limit_bytes=32 * MIB),
        name="update",
    )(chosen, used, one, two, master, first, second)


def shards_paired(
    inputs,
    cotangent,
    doc_lengths,
    owner_list,
    master,
    first_moment,
    second_moment,
    vectors,
    vector_first,
    vector_second,
):
    rows_here, span, width = inputs.shape
    place = lax.axis_index("blk")
    member = lax.axis_index("dp")
    rows_mine = rows_here // 2
    order = jnp.arange(PIECES)
    same_owner = owner_list[:, None] == owner_list[None, :]
    ranks = jnp.sum(same_owner & (order[None, :] < order[:, None]), axis=1).astype(jnp.int32)
    slot_of = owner_list * CAP + ranks
    own = (owner_list == member).astype(jnp.int32)
    x, cot, weights_one, weights_two = spread(own, ranks, master, inputs, cotangent)
    x = x.reshape(-1, width)
    cot = cot.reshape(-1, width)
    lengths = lax.dynamic_slice_in_dim(doc_lengths[:, 0], place * rows_mine, rows_mine, 0)
    bias = jnp.where(lengths < LEN, -1e30, 0.0).astype(f32)
    keys, values, turned, normed = project(x, weights_one, vectors)
    weights, recips, context_turned, context = attend(bias, keys, turned)
    block_out, residual, grad_context, sums_two, tiles_two = feed(
        context, context_turned, x, cot, weights_two, vectors
    )
    block_out, total_two = reduce_tiles(tiles_two, block_out.reshape(rows_mine, LEN, width), 1)
    grads = attend_back(weights, recips, values, turned, context_turned, grad_context)
    input_grad, sums_one, tiles_one = finish(grads, normed, x, residual, weights_one, vectors)
    vector_grads = jnp.concatenate(
        [sums_one[0:2], sums_two[0:2], sums_one[2:4], sums_two[2:4], sums_two[4:8]], axis=0
    )
    input_grad, total_one, vector_total = reduce_last(
        tiles_one,
        jnp.pad(vector_grads, ((0, 4), (0, 0))),
        input_grad.reshape(rows_mine, LEN, width),
        2,
    )
    own_slots = member * CAP + jnp.arange(CAP)
    pick = own_slots[:, None] == slot_of[None, :]
    used = jnp.any(pick, axis=1).astype(jnp.int32)
    chosen = jnp.argmax(pick, axis=1).astype(jnp.int32)
    updated = update(chosen, used, total_one, total_two, master, first_moment, second_moment)
    columns = vector_first.shape[1]
    vector_cols = lax.dynamic_slice_in_dim(vectors, place * columns, columns, 1)
    vector_total = lax.dynamic_slice(vector_total, (0, place * columns), (PIECES, columns))
    updated_vectors = adam_step(vector_cols, vector_total, vector_first, vector_second, VEC_RATE)
    return (
        block_out.astype(f32),
        input_grad.astype(f32),
        *updated,
        *updated_vectors,
    )


def solution(mesh):
    in_specs = (
        P("dp", "blk", None),
        P("dp", "blk", None),
        P("dp", None),
        P(),
        P("dp", "blk", None),
        P("dp", "blk", None),
        P("dp", "blk", None),
        P(),
        P(None, "blk"),
        P(None, "blk"),
    )
    out_specs = (
        P("dp", "blk", None),
        P("dp", "blk", None),
        P("dp", "blk", None),
        P("dp", "blk", None),
        P("dp", "blk", None),
        P(None, "blk"),
        P(None, "blk"),
        P(None, "blk"),
    )
    paired = mesh.shape["blk"] == 2 and mesh.shape["dp"] == 16
    shards = shards_paired if paired else shards_any
    return jax.shard_map(shards, mesh=mesh, in_specs=in_specs, out_specs=out_specs, check_vma=False)
```

```python
from functools import partial

import jax
import jax.numpy as jnp
from jax import lax
from jax.experimental import pallas as pl
from jax.experimental.pallas import tpu as pltpu
from jax.sharding import PartitionSpec as P

D = 768
FF = 3072
HEADS = 12
HEAD_DIM = 64
LEN = 1024
CAP = 3
STEP = 10
PIECES = 12


EPS_NORM = 1e-05
BETA_ONE = 0.9
BETA_TWO = 0.999
RATE = 0.04
VEC_RATE = 0.25
DECAY = 0.01
ADAM_EPS = 1e-08


def normalize(values_in, gain, shift):
    center = jnp.mean(values_in, axis=-1, keepdims=True)
    offset = values_in - center
    spread = jnp.mean(offset * offset, axis=-1, keepdims=True)
    return offset * lax.rsqrt(spread + EPS_NORM) * gain + shift


def adam_step(weight, grad, first, second, rate):
    first_new = BETA_ONE * first + (1.0 - BETA_ONE) * grad
    second_new = BETA_TWO * second + (1.0 - BETA_TWO) * grad * grad
    corrected = (
        first_new
        / (1.0 - BETA_ONE**STEP)
        / (jnp.sqrt(second_new / (1.0 - BETA_TWO**STEP)) + ADAM_EPS)
    )
    return (weight - rate * (corrected + DECAY * weight), first_new, second_new)


def shards_any(
    inputs,
    cotangent,
    doc_lengths,
    owner_list,
    master,
    first_moment,
    second_moment,
    vectors,
    vector_first,
    vector_second,
):
    rows_here, span, width = inputs.shape
    tokens_here = rows_here * span
    fold = FF // D
    scale = HEAD_DIM ** (-0.5)
    place = lax.axis_index("blk")
    f32 = jnp.float32
    b16 = jnp.bfloat16
    order = jnp.arange(PIECES)
    same_owner = owner_list[:, None] == owner_list[None, :]
    ranks = jnp.sum(same_owner & (order[None, :] < order[:, None]), axis=1)
    slot_of = owner_list * CAP + ranks

    mine = (owner_list == lax.axis_index("dp"))[:, None, None]
    tile_rows = lax.psum(jnp.where(mine, master[ranks], 0.0).astype(b16), "dp")
    tiles = lax.all_gather(tile_rows, "blk", axis=1, tiled=True)
    query_weight = tiles[0]
    key_weight = tiles[1]
    value_weight = tiles[2]
    out_weight = tiles[3]
    up_weight = jnp.transpose(tiles[4 : 4 + fold], (1, 0, 2)).reshape(width, FF)
    down_weight = tiles[4 + fold :].reshape(FF, width)
    flat_in = inputs.reshape(tokens_here, width).astype(f32)
    normed_one = normalize(flat_in, vectors[0], vectors[1]).astype(b16)
    queries = (jnp.dot(normed_one, query_weight, preferred_element_type=f32) + vectors[4]).astype(
        b16
    )
    keys_here = jnp.dot(normed_one, key_weight, preferred_element_type=f32).astype(b16)
    values_here = (
        jnp.dot(normed_one, value_weight, preferred_element_type=f32) + vectors[5]
    ).astype(b16)
    query_heads = queries.reshape(rows_here, span, HEADS, HEAD_DIM)
    first_len = doc_lengths[:, 0]
    query_seg = (place * span + jnp.arange(span))[None, :] >= first_len[:, None]

    def block_scores(key_block, start):
        count = key_block.shape[1]
        key_heads = key_block.reshape(rows_here, count, HEADS, HEAD_DIM)
        raw = (
            jnp.einsum("rqhd,rkhd->rhqk", query_heads, key_heads, preferred_element_type=f32)
            * scale
        )
        key_seg = (start + jnp.arange(count))[None, :] >= first_len[:, None]
        allowed = query_seg[:, None, :, None] == key_seg[:, None, None, :]
        return (raw, allowed)

    key_rows = keys_here.reshape(rows_here, span, width)
    value_rows = values_here.reshape(rows_here, span, width)
    top = jnp.full((rows_here, HEADS, span), -1e30, f32)
    key_block = lax.all_gather(key_rows, "blk", axis=1, tiled=True)
    value_block = lax.all_gather(value_rows, "blk", axis=1, tiled=True)
    count = key_block.shape[1]
    raw, allowed = block_scores(key_block, jnp.int32(0))
    new_top = jnp.maximum(top, jnp.max(jnp.where(allowed, raw, -1e30), axis=-1))
    weights = jnp.where(allowed, jnp.exp(raw - new_top[..., None]), 0.0)
    value_heads = value_block.reshape(rows_here, count, HEADS, HEAD_DIM)
    update = jnp.einsum(
        "rhqk,rkhd->rhqd", weights.astype(b16), value_heads, preferred_element_type=f32
    )
    total = jnp.sum(weights, axis=-1)
    log_total = new_top + jnp.log(total)
    context_raw = update / total[..., None]
    context_low = jnp.transpose(context_raw, (0, 2, 1, 3)).reshape(tokens_here, width).astype(b16)
    residual = flat_in + (jnp.dot(context_low, out_weight, preferred_element_type=f32) + vectors[6])
    normed_two = normalize(residual, vectors[2], vectors[3]).astype(b16)
    hidden = jnp.dot(normed_two, up_weight, preferred_element_type=f32) + vectors[8:].reshape(FF)
    gelu_exact = partial(jax.nn.gelu, approximate=False)
    active, gelu_pull = jax.vjp(gelu_exact, hidden)
    active_low = active.astype(b16)
    block_out = (
        residual + (jnp.dot(active_low, down_weight, preferred_element_type=f32) + vectors[7])
    ).reshape(rows_here, span, width)
    grad_out = cotangent.reshape(tokens_here, width)
    down_grad = jnp.einsum("tf,td->fd", active_low, grad_out, preferred_element_type=f32)
    down_sum = jnp.sum(grad_out, axis=0, dtype=f32)
    grad_active = jnp.einsum("td,fd->tf", grad_out, down_weight, preferred_element_type=f32)
    grad_hidden = gelu_pull(grad_active)[0].astype(b16)
    up_grad = jnp.einsum("td,tf->df", normed_two, grad_hidden, preferred_element_type=f32)
    up_sum = jnp.sum(grad_hidden, axis=0, dtype=f32)
    ffn_tiles = jnp.concatenate(
        [
            jnp.transpose(up_grad.reshape(width, fold, width), (1, 0, 2)),
            down_grad.reshape(fold, width, width),
        ],
        axis=0,
    )
    grad_normed_two = jnp.einsum("tf,df->td", grad_hidden, up_weight, preferred_element_type=f32)
    unused, second_pull = jax.vjp(normalize, residual, vectors[2], vectors[3])
    residual_part, gain_two_grad, shift_two_grad = second_pull(grad_normed_two)
    grad_residual = grad_out.astype(f32) + residual_part
    grad_attended = grad_residual.astype(b16)
    out_grad = jnp.einsum("tm,td->md", context_low, grad_attended, preferred_element_type=f32)
    out_sum = jnp.sum(grad_attended, axis=0, dtype=f32)
    grad_context = jnp.einsum(
        "td,md->tm", grad_attended, out_weight, preferred_element_type=f32
    ).astype(b16)
    grad_heads = grad_context.reshape(rows_here, span, HEADS, HEAD_DIM)
    delta = jnp.einsum("rqhd,rhqd->rhq", grad_heads.astype(f32), context_raw)
    key_all, value_all = (
        lax.all_gather(key_rows, "blk", axis=1, tiled=True),
        lax.all_gather(value_rows, "blk", axis=1, tiled=True),
    )
    key_size = min(512, LEN)

    def back_block(index, carry):
        grad_query, key_total, value_total = carry
        start = index * key_size
        key_block = lax.dynamic_slice_in_dim(key_all, start, key_size, 1)
        value_block = lax.dynamic_slice_in_dim(value_all, start, key_size, 1)
        raw, allowed = block_scores(key_block, start)
        weights_back = jnp.where(allowed, jnp.exp(raw - log_total[..., None]), 0.0)
        key_heads = key_block.reshape(rows_here, key_size, HEADS, HEAD_DIM)
        value_heads = value_block.reshape(rows_here, key_size, HEADS, HEAD_DIM)
        value_grad = jnp.einsum(
            "rhqk,rqhd->rkhd", weights_back.astype(b16), grad_heads, preferred_element_type=f32
        )
        weight_grad = jnp.einsum(
            "rqhd,rkhd->rhqk", grad_heads, value_heads, preferred_element_type=f32
        )
        score_grad = (weights_back * (weight_grad - delta[..., None])).astype(b16)
        grad_query = (
            grad_query
            + jnp.einsum("rhqk,rkhd->rqhd", score_grad, key_heads, preferred_element_type=f32)
            * scale
        )
        key_grad = (
            jnp.einsum("rhqk,rqhd->rkhd", score_grad, query_heads, preferred_element_type=f32)
            * scale
        )
        key_total = lax.dynamic_update_slice_in_dim(
            key_total, key_grad.reshape(rows_here, key_size, width), start, 1
        )
        value_total = lax.dynamic_update_slice_in_dim(
            value_total, value_grad.reshape(rows_here, key_size, width), start, 1
        )
        return (grad_query, key_total, value_total)

    zero_rows = jnp.zeros((rows_here, LEN, width), f32)
    grad_query, key_total, value_total = lax.fori_loop(
        0,
        LEN // key_size,
        back_block,
        (jnp.zeros((rows_here, span, HEADS, HEAD_DIM), f32), zero_rows, zero_rows),
    )
    key_grad_here, value_grad_here = (
        lax.psum_scatter(
            key_total.astype(jnp.bfloat16), "blk", scatter_dimension=1, tiled=True
        ).astype(jnp.float32),
        lax.psum_scatter(
            value_total.astype(jnp.bfloat16), "blk", scatter_dimension=1, tiled=True
        ).astype(jnp.float32),
    )
    query_low = grad_query.reshape(tokens_here, width).astype(b16)
    key_low = key_grad_here.reshape(tokens_here, width).astype(b16)
    value_low = value_grad_here.reshape(tokens_here, width).astype(b16)
    query_tile = jnp.einsum("td,te->de", normed_one, query_low, preferred_element_type=f32)
    key_tile = jnp.einsum("td,te->de", normed_one, key_low, preferred_element_type=f32)
    value_tile = jnp.einsum("td,te->de", normed_one, value_low, preferred_element_type=f32)
    grad_normed_one = (
        jnp.einsum("te,de->td", query_low, query_weight, preferred_element_type=f32)
        + jnp.einsum("te,de->td", key_low, key_weight, preferred_element_type=f32)
        + jnp.einsum("te,de->td", value_low, value_weight, preferred_element_type=f32)
    )
    unused, first_pull = jax.vjp(normalize, flat_in, vectors[0], vectors[1])
    input_part, gain_one_grad, shift_one_grad = first_pull(grad_normed_one)
    input_grad = (grad_residual + input_part).reshape(rows_here, span, width)
    vector_grads = jnp.concatenate(
        [
            jnp.stack(
                [
                    gain_one_grad,
                    shift_one_grad,
                    gain_two_grad,
                    shift_two_grad,
                    jnp.sum(query_low, axis=0, dtype=f32),
                    jnp.sum(value_low, axis=0, dtype=f32),
                    out_sum,
                    down_sum,
                ]
            ),
            up_sum.reshape(fold, width),
        ],
        axis=0,
    )
    attn_tiles = jnp.stack([query_tile, key_tile, value_tile, out_grad])
    piece_share, vector_share = (
        lax.psum_scatter(
            jnp.concatenate([attn_tiles, ffn_tiles], axis=0).astype(jnp.bfloat16),
            "blk",
            scatter_dimension=1,
            tiled=True,
        ).astype(jnp.float32),
        lax.psum_scatter(
            vector_grads.astype(jnp.bfloat16), "blk", scatter_dimension=1, tiled=True
        ).astype(jnp.float32),
    )
    own_slots = lax.axis_index("dp") * CAP + jnp.arange(CAP)
    pick = (own_slots[:, None] == slot_of[None, :]).astype(f32)
    occupied = jnp.sum(pick, axis=1)[:, None, None]
    total_share, vector_total = (
        lax.psum(piece_share.astype(jnp.bfloat16), "dp").astype(jnp.float32),
        lax.psum(vector_share.astype(jnp.bfloat16), "dp").astype(jnp.float32),
    )
    slot_grads = jnp.einsum("cp,prd->crd", pick, total_share, precision=lax.Precision.HIGHEST)
    new_master, new_first, new_second = adam_step(
        master, slot_grads, first_moment, second_moment, RATE
    )
    columns = vector_first.shape[1]
    vector_cols = lax.dynamic_slice_in_dim(vectors, place * columns, columns, 1)
    new_vectors, new_vector_first, new_vector_second = adam_step(
        vector_cols, vector_total, vector_first, vector_second, VEC_RATE
    )
    return (
        block_out,
        input_grad,
        new_master * occupied,
        new_first * occupied,
        new_second * occupied,
        new_vectors,
        new_vector_first,
        new_vector_second,
    )


f32 = jnp.float32
b16 = jnp.bfloat16
LOG2E = 1.4426950408889634
MIB = 1024 * 1024
PAIRS = HEADS // 2
PAIR = 2 * HEAD_DIM


def dot_nn(left, right):
    return lax.dot_general(left, right, (((1,), (0,)), ((), ())), preferred_element_type=f32)


def dot_nt(left, right):
    return lax.dot_general(left, right, (((1,), (1,)), ((), ())), preferred_element_type=f32)


def dot_tn(left, right):
    return lax.dot_general(left, right, (((0,), (0,)), ((), ())), preferred_element_type=f32)


def norm_parts(values_in):
    center = jnp.mean(values_in, axis=-1, keepdims=True)
    offset = values_in - center
    spread = jnp.mean(offset * offset, axis=-1, keepdims=True)
    rstd = lax.rsqrt(spread + EPS_NORM)
    return offset * rstd, rstd


def norm_back(grad, unit, rstd, gain):
    scaled = grad * gain
    first = jnp.mean(scaled, axis=-1, keepdims=True)
    second = jnp.mean(scaled * unit, axis=-1, keepdims=True)
    return rstd * (scaled - first - unit * second)


def gelu_parts(value):
    bell = jnp.exp2(value * value * (-0.5 * LOG2E))
    ratio = pl.reciprocal(1.0 + (0.3275911 * 0.7071067811865476) * jnp.abs(value))
    poly = 0.5 * 1.061405429
    poly = poly * ratio + 0.5 * -1.453152027
    poly = poly * ratio + 0.5 * 1.421413741
    poly = poly * ratio + 0.5 * -0.284496736
    poly = poly * ratio + 0.5 * 0.254829592
    tail = poly * ratio * bell
    cdf = jnp.where(value >= 0.0, 1.0 - tail, tail)
    return value * cdf, cdf + value * (bell * 0.3989422804014327)


def head_only(block, head):
    lane = lax.broadcasted_iota(jnp.int32, block.shape, 1)
    keep = (lane >= head * HEAD_DIM) & (lane < (head + 1) * HEAD_DIM)
    return jnp.where(keep, block, jnp.zeros_like(block))


def attend_back_kernel(p_ref, r_ref, v_ref, q_ref, k_ref, o_ref, g_ref, d_ref):
    half = LEN // 2
    for head in range(2):
        part = slice(head * HEAD_DIM, (head + 1) * HEAD_DIM)
        values = head_only(v_ref[...], head)
        recip = r_ref[0, head : head + 1, :]
        grad = g_ref[part, :].astype(f32) * recip
        delta = jnp.sum(grad * o_ref[part, :].astype(f32), 0, keepdims=True)
        grad = grad.astype(b16)
        wide = jnp.concatenate([grad, grad], axis=0)
        value_grad = jnp.zeros((HEAD_DIM, LEN), f32)
        key_grad = jnp.zeros((HEAD_DIM, LEN), f32)
        for step in range(2):
            cols = slice(step * half, (step + 1) * half)
            weights = p_ref[head, :, cols]
            slope = dot_nn(values, wide[:, cols]) - delta[:, cols]
            slope = (weights.astype(f32) * slope).astype(b16)
            value_grad = value_grad + dot_nt(grad[:, cols], weights)
            key_grad = key_grad + dot_nt(q_ref[part, cols], slope)
            query_grad = dot_nn(k_ref[part, :], slope) * (HEAD_DIM**-0.5)
            d_ref[0, part, cols] = query_grad.astype(b16)
        d_ref[1, part, :] = (key_grad * (1.0 / LOG2E)).astype(b16)
        d_ref[2, part, :] = value_grad.astype(b16)


def attend_back(weights, recips, values, queries, keys, context, grad):
    tokens = values.shape[0]
    rows = tokens // LEN
    return pl.pallas_call(
        attend_back_kernel,
        grid=(rows, PAIRS),
        in_specs=[
            pl.BlockSpec((2, LEN, LEN), lambda r, h: (h * 2 + r, 0, 0)),
            pl.BlockSpec((1, 2, LEN), lambda r, h: (h * 2 + r, 0, 0)),
            pl.BlockSpec((LEN, PAIR), lambda r, h: (r, h)),
            pl.BlockSpec((PAIR, LEN), lambda r, h: (h, r)),
            pl.BlockSpec((PAIR, LEN), lambda r, h: (h, r)),
            pl.BlockSpec((PAIR, LEN), lambda r, h: (h, r)),
            pl.BlockSpec((PAIR, LEN), lambda r, h: (h, r)),
        ],
        out_specs=pl.BlockSpec((3, PAIR, LEN), lambda r, h: (0, h, r)),
        out_shape=jax.ShapeDtypeStruct((3, D, tokens), b16),
        compiler_params=pltpu.CompilerParams(vmem_limit_bytes=56 * MIB),
        cost_estimate=pl.CostEstimate(
            flops=32 * tokens * LEN * D,
            bytes_accessed=2 * rows * HEADS * LEN * LEN + 16 * tokens * D,
            transcendentals=0,
        ),
        name="attend_back",
    )(weights, recips, values, queries, keys, context, grad)


def feed_kernel(
    c_ref, o_ref, x_ref, g_ref, w_ref, vec_ref,
    y_ref, r_ref, d_ref, sums_ref, tiles_ref,
    acc_ref, stage_ref, sem_ref,
):
    fold = FF // D
    step = pl.program_id(0)

    @pl.when(step == 0)
    def clear():
        acc_ref[...] = jnp.zeros_like(acc_ref)
        sums_ref[...] = jnp.zeros_like(sums_ref)

    residual = x_ref[...].astype(f32) + (dot_nn(c_ref[...], w_ref[0]) + vec_ref[6:7, :])
    unit, rstd = norm_parts(residual)
    gain = vec_ref[2:3, :]
    normed = (unit * gain + vec_ref[3:4, :]).astype(b16)
    turned = normed.T
    cot = g_ref[...]
    out = residual + vec_ref[7:8, :]
    grad = jnp.zeros_like(out)
    for part in range(fold):
        hidden = dot_nn(normed, w_ref[1 + part]) + vec_ref[8 + part : 9 + part, :]
        pulled = dot_nt(cot, w_ref[1 + fold + part])
        active, slope = gelu_parts(hidden)
        active = active.astype(b16)
        pulled = (pulled * slope).astype(b16)
        out = out + dot_nn(active, w_ref[1 + fold + part])
        grad = grad + dot_nt(pulled, w_ref[1 + part])
        acc_ref[1 + part] += dot_nn(turned, pulled)
        acc_ref[1 + fold + part] += dot_tn(active, cot)
        sums_ref[4 + part : 5 + part, :] += jnp.sum(pulled.astype(f32), 0, keepdims=True)
    y_ref[...] = out.astype(b16)
    wide = cot.astype(f32)
    sums_ref[0:1, :] += jnp.sum(grad * unit, 0, keepdims=True)
    sums_ref[1:2, :] += jnp.sum(grad, 0, keepdims=True)
    sums_ref[3:4, :] += jnp.sum(wide, 0, keepdims=True)
    back = wide + norm_back(grad, unit, rstd, gain)
    r_ref[...] = back
    low = back.astype(b16)
    sums_ref[2:3, :] += jnp.sum(low.astype(f32), 0, keepdims=True)
    d_ref[...] = dot_nt(w_ref[0], low).astype(b16)
    acc_ref[0] += dot_nn(o_ref[...], low)

    @pl.when(step == pl.num_programs(0) - 1)
    def send():
        count = 1 + 2 * fold
        copies = []
        for part in range(count):
            if part >= 2:
                copies[part - 2].wait()
            stage_ref[part % 2] = acc_ref[part].astype(b16)
            copy = pltpu.make_async_copy(stage_ref.at[part % 2], tiles_ref.at[part], sem_ref.at[part % 2])
            copy.start()
            copies.append(copy)
        copies[count - 2].wait()
        copies[count - 1].wait()


def feed(context, turned, x, cot, weights, vectors):
    tokens = x.shape[0]
    size = 256
    count = 1 + 2 * (FF // D)
    token_block = pl.BlockSpec((size, D), lambda i: (i, 0))
    turned_block = pl.BlockSpec((D, size), lambda i: (0, i))
    return pl.pallas_call(
        feed_kernel,
        grid=(tokens // size,),
        in_specs=[
            token_block,
            turned_block,
            token_block,
            token_block,
            pl.BlockSpec((count, D, D), lambda i: (0, 0, 0), pipeline_mode=pl.Buffered(1)),
            pl.BlockSpec((PIECES, D), lambda i: (0, 0)),
        ],
        out_specs=[
            token_block,
            token_block,
            turned_block,
            pl.BlockSpec((8, D), lambda i: (0, 0)),
            pl.BlockSpec(memory_space=pl.ANY),
        ],
        out_shape=[
            jax.ShapeDtypeStruct((tokens, D), b16),
            jax.ShapeDtypeStruct((tokens, D), f32),
            jax.ShapeDtypeStruct((D, tokens), b16),
            jax.ShapeDtypeStruct((8, D), f32),
            jax.ShapeDtypeStruct((count, D, D), b16),
        ],
        scratch_shapes=[
            pltpu.VMEM((count, D, D), f32),
            pltpu.VMEM((2, D, D), b16),
            pltpu.SemaphoreType.DMA((2,)),
        ],
        compiler_params=pltpu.CompilerParams(vmem_limit_bytes=60 * MIB),
        cost_estimate=pl.CostEstimate(
            flops=6 * count * tokens * D * D,
            bytes_accessed=18 * tokens * D + 4 * count * D * D,
            transcendentals=2 * tokens * FF,
        ),
        name="feed",
    )(context, turned, x, cot, weights, vectors)


def finish_kernel(d_ref, n_ref, x_ref, r_ref, w_ref, vec_ref, i_ref, sums_ref, tiles_ref, acc_ref):
    step = pl.program_id(0)

    @pl.when(step == 0)
    def clear():
        acc_ref[...] = jnp.zeros_like(acc_ref)
        sums_ref[...] = jnp.zeros_like(sums_ref)

    ones = jnp.ones((8, d_ref.shape[2]), b16)
    turned = n_ref[...].T
    grad = None
    for part in range(3):
        acc_ref[part] += dot_nt(turned, d_ref[part])
        term = dot_nn(w_ref[part], d_ref[part])
        grad = term if part == 0 else grad + term
    sums_ref[2:3, :] += dot_nt(ones, d_ref[0])[0:1]
    sums_ref[3:4, :] += dot_nt(ones, d_ref[2])[0:1]
    grad = grad.T
    unit, rstd = norm_parts(x_ref[...].astype(f32))
    sums_ref[0:1, :] += jnp.sum(grad * unit, 0, keepdims=True)
    sums_ref[1:2, :] += jnp.sum(grad, 0, keepdims=True)
    total = r_ref[...] + norm_back(grad, unit, rstd, vec_ref[0:1, :])
    i_ref[...] = total.astype(b16)

    @pl.when(step == pl.num_programs(0) - 1)
    def send():
        tiles_ref[...] = acc_ref[...].astype(b16)


def finish(grads, normed, x, residual, weights, vectors):
    tokens = x.shape[0]
    size = 512
    token_block = pl.BlockSpec((size, D), lambda i: (i, 0))
    return pl.pallas_call(
        finish_kernel,
        grid=(tokens // size,),
        in_specs=[
            pl.BlockSpec((3, D, size), lambda i: (0, 0, i)),
            token_block,
            token_block,
            token_block,
            pl.BlockSpec((3, D, D), lambda i: (0, 0, 0), pipeline_mode=pl.Buffered(1)),
            pl.BlockSpec((PIECES, D), lambda i: (0, 0)),
        ],
        out_specs=[
            token_block,
            pl.BlockSpec((8, D), lambda i: (0, 0)),
            pl.BlockSpec((3, D, D), lambda i: (0, 0, 0)),
        ],
        out_shape=[
            jax.ShapeDtypeStruct((tokens, D), b16),
            jax.ShapeDtypeStruct((8, D), f32),
            jax.ShapeDtypeStruct((3, D, D), b16),
        ],
        scratch_shapes=[pltpu.VMEM((3, D, D), f32)],
        compiler_params=pltpu.CompilerParams(vmem_limit_bytes=56 * MIB),
        cost_estimate=pl.CostEstimate(
            flops=12 * tokens * D * D, bytes_accessed=18 * tokens * D + 12 * D * D, transcendentals=0
        ),
        name="finish",
    )(grads, normed, x, residual, weights, vectors)


MESH = pl.DeviceIdType.MESH
HALF = D // 2
FLOWS = 2
FLOW = HALF // FLOWS
NEAR = FLOW // 2
KEEP = NEAR // 2
WIDE = 3 * PAIR
REST = PIECES - 3
CHUNKS = 3
CHUNK = D // CHUNKS


class Place:
    def __init__(self):
        self.me = lax.axis_index("dp")
        self.core = lax.axis_index("blk")
        self.bits = [lax.rem(self.me // weight, 2) for weight in (1, 2, 4, 8)]
        self.chips = [
            self.me + weight - 2 * weight * bit for weight, bit in zip((1, 2, 4, 8), self.bits)
        ]
        self.partners = [{"dp": chip} for chip in self.chips]
        self.other = 1 - self.core
        self.twin = {"blk": self.other}

    def greet(self):
        barrier = pltpu.get_barrier_semaphore()
        for device in self.partners + [self.twin]:
            pl.semaphore_signal(barrier, 1, device_id=device, device_id_type=MESH)
        pl.semaphore_wait(barrier, 5)

    def flow(self, index):
        first, second = (0, 1) if index == 0 else (1, 0)
        base = index * FLOW
        near = base + self.bits[first] * NEAR
        far = base + NEAR - self.bits[first] * NEAR
        keep = near + self.bits[second] * KEEP
        give = near + KEEP - self.bits[second] * KEEP
        return first, second, near, far, keep, give


def remote(source, target, send, receive, device):
    return pltpu.make_async_remote_copy(
        src_ref=source,
        dst_ref=target,
        send_sem=send,
        recv_sem=receive,
        device_id=device,
        device_id_type=MESH,
    )


def rows_at(start, count):
    return pl.ds(pl.multiple_of(start, 16), count)


class Spread:
    def __init__(self, place, owner, rank, slots, land, gift, sems):
        self.place, self.owner, self.rank = place, owner, rank
        self.slots, self.land, self.gift, self.sems = slots, land, gift, sems

    def first_copy(self, chunk, index):
        first, second, near, far, keep, give = self.place.flow(index)
        cols = pl.ds(chunk * CHUNK, CHUNK)
        return remote(
            self.slots.at[:, rows_at(far, NEAR), cols],
            self.land[chunk].at[index],
            self.sems[0].at[chunk, index, 0],
            self.sems[1].at[chunk, index, 0],
            self.place.partners[first],
        )

    def second_copy(self, chunk, index, which):
        first, second, near, far, keep, give = self.place.flow(index)
        if which == 0:
            source = self.slots.at[:, rows_at(give, KEEP), pl.ds(chunk * CHUNK, CHUNK)]
        else:
            source = self.land[chunk].at[index, :, rows_at(give - near, KEEP)]
        return remote(
            source,
            self.gift[chunk].at[index, pl.ds(which * CAP, CAP)],
            self.sems[0].at[chunk, index, 1 + which],
            self.sems[1].at[chunk, index, 1 + which],
            self.place.partners[second],
        )

    def step(self, chunk, index):
        for flow in range(FLOWS):
            if index == 0:
                self.first_copy(chunk, flow).start()
                self.second_copy(chunk, flow, 0).start()
            if index == 1:
                self.first_copy(chunk, flow).wait()
                self.second_copy(chunk, flow, 1).start()
            if index == 2:
                self.second_copy(chunk, flow, 0).wait()
                self.second_copy(chunk, flow, 1).wait()

    def piece(self, tile, index, chunk, start, count):
        first, second, near, far, keep, give = self.place.flow(index)
        owner, rank = self.owner[tile], self.rank[tile]
        bits = [lax.rem(owner, 2), lax.rem(owner // 2, 2)]
        apart = [bit != mine for bit, mine in zip(bits, self.place.bits)]
        cols = pl.ds(start, count)
        mine = self.slots[rank, rows_at(keep, KEEP), pl.ds(chunk * CHUNK + start, count)]
        firsts = self.land[chunk][index, rank, rows_at(keep - near, KEEP), cols]
        gifts = self.gift[chunk][index, jnp.where(apart[first], CAP, 0) + rank, :, cols]
        value = jnp.where(apart[second], gifts, jnp.where(apart[first], firsts, mine))
        layer = owner // 4 == self.place.me // 4
        return jnp.where(layer, value, jnp.zeros_like(value))


class Item:
    steps = 6

    def __init__(self, place, work, land, sems, load, store=None):
        self.place, self.work, self.land, self.sems = place, work, land, sems
        self.load, self.store = load, store
        self.base = place.core * HALF

    def copy(self, flow, index):
        first, second, near, far, keep, give = self.place.flow(flow)
        kept = self.work.at[rows_at(self.base + keep, KEEP)]
        half = self.work.at[rows_at(self.base + near, NEAR)]
        source, target, device = [
            (kept, self.land.at[flow, 0], self.place.partners[2]),
            (kept, self.land.at[flow, 1], self.place.partners[3]),
            (kept, kept, self.place.partners[second]),
            (half, half, self.place.partners[first]),
        ][index]
        return remote(
            source, target, self.sems[0].at[flow, index], self.sems[1].at[flow, index], device
        )

    def pair(self):
        rows = self.work.at[rows_at(self.base, HALF)]
        return remote(rows, rows, self.sems[0].at[0, 4], self.sems[1].at[0, 4], self.place.twin)

    def step(self, index):
        for flow in range(FLOWS):
            keep = self.place.flow(flow)[4]
            rows = rows_at(self.base + keep, KEEP)
            if index == 0:
                self.load(self.work, rows, flow)
            if 1 <= index <= 4:
                self.copy(flow, index - 1).wait()
            if 1 <= index <= 2:
                total = self.work[rows].astype(f32) + self.land[flow, index - 1].astype(f32)
                self.work[rows] = total.astype(b16)
            if index <= 3:
                self.copy(flow, index).start()
        if index == 4:
            self.pair().start()
        if index == 5:
            self.pair().wait()
            self.store().start()


FRONT_FIRST = 2
FRONT_REST = 6
FRONT_LEAD = 8


def front_kernel(
    owner, rank, bias, master, vec_ref, x_in, c_in,
    x_out, c_out, n_out, one_out, two_out, q_ref, k_ref, v_ref, p_ref, r_ref, o_ref, ctx_ref,
    rows_ref, normed, keys, turned_values, slots,
    land_one, land_two, land_three, gift_one, gift_two, gift_three,
    one, one_land, two, two_land,
    spread_send, spread_recv, one_send, one_recv, two_send, two_recv,
    swap_send, swap_recv, swap_local, store_sem,
):
    pair = pl.program_id(0)
    row = pl.program_id(1)
    grid_step = pair * 2 + row
    place = Place()
    rows, span = x_in.shape[0] // 2, x_in.shape[1]
    land = (land_one, land_two, land_three)
    gift = (gift_one, gift_two, gift_three)
    spread = Spread(place, owner, rank, slots, land, gift, (spread_send, spread_recv))

    def swaps(index):
        source, target = [(x_in, rows_ref), (c_in, c_out)][index]
        here = pl.ds(place.core * span, span)
        near = pltpu.make_async_copy(
            source.at[pl.ds(place.core * rows, rows)], target.at[:, here], swap_local.at[index]
        )
        far = remote(
            source.at[pl.ds(place.other * rows, rows)],
            target.at[:, here],
            swap_send.at[index],
            swap_recv.at[index],
            place.twin,
        )
        return near, far

    def row_store():
        return pltpu.make_async_copy(rows_ref, x_out, store_sem.at[PAIRS + REST])

    def normed_store():
        return pltpu.make_async_copy(normed, n_out, store_sem.at[PAIRS + REST + 1])

    def pair_item(index):
        def load(work, where, flow):
            for tile in range(3):
                part = spread.piece(tile, flow, index // 2, index % 2 * PAIR, PAIR)
                work[where, pl.ds(tile * PAIR, PAIR)] = part

        def store():
            return pltpu.make_async_copy(one.at[index], one_out.at[index], store_sem.at[index])

        sems = (one_send.at[index], one_recv.at[index])
        return Item(place, one.at[index], one_land.at[index], sems, load, store)

    def rest_item(index):
        def load(work, where, flow):
            for chunk in range(CHUNKS):
                part = spread.piece(3 + index, flow, chunk, 0, CHUNK)
                work[where, pl.ds(chunk * CHUNK, CHUNK)] = part

        def store():
            return pltpu.make_async_copy(
                two.at[index], two_out.at[index], store_sem.at[PAIRS + index]
            )

        sems = (two_send.at[index], two_recv.at[index])
        return Item(place, two.at[index], two_land.at[index], sems, load, store)

    def tick(number):
        if number == 0:
            for chunk in range(CHUNKS):
                spread.step(chunk, 0)
        for chunk in range(CHUNKS):
            if number >= 1 and number - 1 - chunk in (0, 1):
                spread.step(chunk, number - chunk)
        starts = [(pair_item, index, FRONT_FIRST + index) for index in range(PAIRS)]
        starts += [(rest_item, index, FRONT_REST + index) for index in range(REST)]
        for make, index, start in starts:
            if 0 <= number - start < Item.steps:
                make(index).step(number - start)

    @pl.when(grid_step == 0)
    def lead():
        place.greet()
        for index in range(2):
            for copy in swaps(index):
                copy.start()
        slots[...] = master[...].astype(b16)
        tick(0)
        for copy in swaps(0):
            copy.wait()
        row_store().start()

        def norm_rows(index, carry):
            where = pl.ds(index * 256, 256)
            for part in range(rows):
                unit, unused = norm_parts(rows_ref[part, where].astype(f32))
                low = (unit * vec_ref[0:1, :] + vec_ref[1:2, :]).astype(b16)
                normed[pl.ds(part * LEN + index * 256, 256)] = low
            return carry

        lax.fori_loop(0, LEN // 256, norm_rows, 0)
        normed_store().start()
        for number in range(1, FRONT_LEAD):
            tick(number)

    for number in range(2 * PAIRS):
        pl.when(grid_step == number)(partial(tick, FRONT_LEAD + number))

    @pl.when(row == 0)
    def project():
        lanes = pl.ds(pl.multiple_of(pair * PAIR, PAIR), PAIR)
        weight = one[pair]

        def part(index, carry):
            where = pl.ds(pl.multiple_of(index * 512, 512), 512)
            both = dot_nn(normed[where], weight)
            queries = both[:, :PAIR] + vec_ref[4:5, lanes]
            queries = (queries * (HEAD_DIM**-0.5 * LOG2E)).astype(b16)
            q_ref[:, where] = queries.T
            low = both[:, PAIR : 2 * PAIR].astype(b16)
            keys[where] = low
            k_ref[:, where] = low.T
            values = (both[:, 2 * PAIR :] + vec_ref[5:6, lanes]).astype(b16)
            v_ref[where] = values
            turned_values[:, where] = values.T
            return carry

        lax.fori_loop(0, normed.shape[0] // 512, part, 0)

    half = LEN // 2
    start = pl.multiple_of(row * LEN, LEN)
    shift = bias[row]
    for head in range(2):
        part = slice(head * HEAD_DIM, (head + 1) * HEAD_DIM)
        for step in range(2):
            cols = pl.ds(pl.multiple_of(start + step * half, half), half)
            others = pl.ds(pl.multiple_of(start + (1 - step) * half, half), half)
            queries = q_ref[:, cols]
            near = dot_nn(head_only(keys[cols], head), queries)
            far = dot_nn(head_only(keys[others], head), queries) + shift
            top = jnp.maximum(jnp.max(near, 0, keepdims=True), jnp.max(far, 0, keepdims=True))
            near = jnp.exp2(near - top)
            far = jnp.exp2(far - top)
            total = jnp.sum(near, 0, keepdims=True) + jnp.sum(far, 0, keepdims=True)
            recip = 1.0 / total
            here = slice(step * half, (step + 1) * half)
            there = slice((1 - step) * half, (2 - step) * half)
            p_ref[head, here, here] = near.astype(b16)
            p_ref[head, there, here] = far.astype(b16)
            r_ref[0, head : head + 1, here] = recip
            values = turned_values[part, pl.ds(start, LEN)]
            out = dot_nn(values, p_ref[head, :, here]) * recip
            o_ref[part, here] = out.astype(b16)
    ctx_ref[...] = o_ref[...].T

    @pl.when(grid_step == 2 * PAIRS - 1)
    def finish_copies():
        for copy in swaps(1):
            copy.wait()
        row_store().wait()
        normed_store().wait()
        for index in range(PAIRS):
            pair_item(index).store().wait()
        for index in range(REST):
            rest_item(index).store().wait()


def front(owner, rank, bias, master, vectors, inputs, cotangent):
    rows, span = inputs.shape[0] // 2, inputs.shape[1]
    tokens = rows * LEN
    any_spec = pl.BlockSpec(memory_space=pl.ANY)
    smem = pl.BlockSpec(memory_space=pltpu.SMEM)
    whole = jax.ShapeDtypeStruct((rows, LEN, D), b16)
    dma = pltpu.SemaphoreType.DMA
    return pl.pallas_call(
        front_kernel,
        grid=(PAIRS, rows),
        in_specs=[
            smem,
            smem,
            smem,
            pl.BlockSpec((CAP, HALF, D), lambda h, r: (0, 0, 0), pipeline_mode=pl.Buffered(1)),
            pl.BlockSpec((PIECES, D), lambda h, r: (0, 0)),
            any_spec,
            any_spec,
        ],
        out_specs=[any_spec] * 5
        + [
            pl.BlockSpec((PAIR, tokens), lambda h, r: (h, 0)),
            pl.BlockSpec((PAIR, tokens), lambda h, r: (h, 0)),
            pl.BlockSpec((tokens, PAIR), lambda h, r: (0, h)),
            pl.BlockSpec((2, LEN, LEN), lambda h, r: (h * 2 + r, 0, 0)),
            pl.BlockSpec((1, 2, LEN), lambda h, r: (h * 2 + r, 0, 0)),
            pl.BlockSpec((PAIR, LEN), lambda h, r: (h, r)),
            pl.BlockSpec((LEN, PAIR), lambda h, r: (r, h)),
        ],
        out_shape=[
            whole,
            whole,
            jax.ShapeDtypeStruct((tokens, D), b16),
            jax.ShapeDtypeStruct((PAIRS, D, WIDE), b16),
            jax.ShapeDtypeStruct((REST, D, D), b16),
            jax.ShapeDtypeStruct((D, tokens), b16),
            jax.ShapeDtypeStruct((D, tokens), b16),
            jax.ShapeDtypeStruct((tokens, D), b16),
            jax.ShapeDtypeStruct((rows * HEADS, LEN, LEN), b16),
            jax.ShapeDtypeStruct((rows * PAIRS, 2, LEN), f32),
            jax.ShapeDtypeStruct((D, tokens), b16),
            jax.ShapeDtypeStruct((tokens, D), b16),
        ],
        scratch_shapes=[
            pltpu.VMEM((rows, LEN, D), b16),
            pltpu.VMEM((tokens, D), b16),
            pltpu.VMEM((tokens, PAIR), b16),
            pltpu.VMEM((PAIR, tokens), b16),
            pltpu.VMEM((CAP, HALF, D), b16),
        ]
        + [pltpu.VMEM((FLOWS, CAP, NEAR, CHUNK), b16)] * CHUNKS
        + [pltpu.VMEM((FLOWS, 2 * CAP, KEEP, CHUNK), b16)] * CHUNKS
        + [
            pltpu.VMEM((PAIRS, D, WIDE), b16),
            pltpu.VMEM((PAIRS, FLOWS, 2, KEEP, WIDE), b16),
            pltpu.VMEM((REST, D, D), b16),
            pltpu.VMEM((REST, FLOWS, 2, KEEP, D), b16),
            dma((CHUNKS, FLOWS, 3)),
            dma((CHUNKS, FLOWS, 3)),
            dma((PAIRS, FLOWS, 5)),
            dma((PAIRS, FLOWS, 5)),
            dma((REST, FLOWS, 5)),
            dma((REST, FLOWS, 5)),
            dma((2,)),
            dma((2,)),
            dma((2,)),
            dma((PAIRS + REST + 2,)),
        ],
        compiler_params=pltpu.CompilerParams(
            collective_id=0, has_side_effects=True, vmem_limit_bytes=60 * MIB
        ),
        name="front",
    )(owner, rank, bias, master, vectors, inputs, cotangent)


UNIT = 128
UNITS = HALF // UNIT
STEPS = 6


class Mover:
    def __init__(self, place, work, wide, narrow, sems):
        self.place, self.work, self.wide, self.narrow, self.sems = place, work, wide, narrow, sems

    def copies(self, tile, part):
        place = self.place
        unit = tile * UNITS + part
        first, second = (0, 1) if unit % 2 == 0 else (1, 0)
        base = place.core * HALF + part * UNIT
        quarter, eighth = UNIT // 2, UNIT // 4
        near = base + place.bits[first] * quarter
        far = base + quarter - place.bits[first] * quarter
        keep = near + place.bits[second] * eighth
        give = near + eighth - place.bits[second] * eighth
        tile_ref = self.work.at[tile]
        near_rows, keep_rows = rows_at(near, quarter), rows_at(keep, eighth)
        partner = [p for p in self.place.partners]
        plan = [
            (tile_ref.at[rows_at(far, quarter)], self.wide.at[unit], partner[first]),
            (tile_ref.at[rows_at(give, eighth)], self.narrow.at[unit, 0], partner[second]),
            (tile_ref.at[keep_rows], self.narrow.at[unit, 1], partner[2]),
            (tile_ref.at[keep_rows], self.narrow.at[unit, 2], partner[3]),
            (tile_ref.at[keep_rows], tile_ref.at[keep_rows], partner[second]),
            (tile_ref.at[near_rows], tile_ref.at[near_rows], partner[first]),
        ]

        def made(index):
            source, target, device = plan[index]
            return remote(source, target, self.sems[0].at[unit, index], self.sems[1].at[unit, index], device)

        landed = [
            (near_rows, self.wide.at[unit]),
            (keep_rows, self.narrow.at[unit, 0]),
            (keep_rows, self.narrow.at[unit, 1]),
            (keep_rows, self.narrow.at[unit, 2]),
        ]
        return made, landed

    def step(self, tile, part, index):
        made, landed = self.copies(tile, part)
        if index > 0:
            made(index - 1).wait()
            if index <= 4:
                rows, source = landed[index - 1]
                total = self.work[tile, rows].astype(f32) + source[...].astype(f32)
                self.work[tile, rows] = total.astype(b16)
        if index < STEPS:
            made(index).start()


def mover_scratch(tiles):
    units = tiles * UNITS
    return [
        pltpu.VMEM((tiles, D, D), b16),
        pltpu.VMEM((units, UNIT // 2, D), b16),
        pltpu.VMEM((units, 3, UNIT // 4, D), b16),
        pltpu.SemaphoreType.DMA((units, STEPS)),
        pltpu.SemaphoreType.DMA((units, STEPS)),
        pltpu.SemaphoreType.DMA((tiles,)),
        pltpu.SemaphoreType.DMA((tiles,)),
    ]


class Reduce:
    def __init__(self, place, count, scratch):
        work, wide, narrow, send, receive, pair_send, pair_receive, land = scratch
        self.place, self.count, self.work, self.land = place, count, work, land
        self.pair_sems = (pair_send, pair_receive)
        self.mover = Mover(place, work, wide, narrow, (send, receive))

    def pair(self, tile):
        rows = self.work.at[tile, rows_at(self.place.other * HALF, HALF)]
        return remote(rows, self.land.at[tile], self.pair_sems[0].at[tile], self.pair_sems[1].at[tile], self.place.twin)

    def step(self, tile, index):
        if index == 0:
            self.pair(tile).start()
        if index == 1:
            self.pair(tile).wait()
            rows = rows_at(self.place.core * HALF, HALF)
            total = self.work[tile, rows].astype(f32) + self.land[tile].astype(f32)
            self.work[tile, rows] = total.astype(b16)
        if index >= 1:
            for part in range(UNITS):
                self.mover.step(tile, part, index - 1)

    steps = STEPS + 2


def run_all(stream):
    for tick in range(stream.count + stream.steps - 1):
        for tile in range(stream.count):
            if 0 <= tick - tile < stream.steps:
                stream.step(tile, tick - tile)


def back_part(refs, sems, place, rows, span):
    made = []
    for index, (source, target) in enumerate(refs):
        there = pl.ds(place.core * rows, rows)
        made.append(
            pltpu.make_async_copy(
                source.at[:, pl.ds(place.core * span, span)], target.at[there], sems[2].at[index]
            )
        )
        made.append(
            remote(
                source.at[:, pl.ds(place.other * span, span)],
                target.at[there],
                sems[0].at[index],
                sems[1].at[index],
                place.twin,
            )
        )
    return made


def part_sems(count):
    return [pltpu.SemaphoreType.DMA((count,)) for unused in range(3)]


def reduce_kernel(tiles_in, y_in, y_out, total_out, *scratch):
    place = Place()
    place.greet()
    rows, span = y_in.shape[0], y_in.shape[1] // 2
    moved = back_part([(y_in, y_out)], scratch[:3], place, rows, span)
    for copy in moved:
        copy.start()
    stream = Reduce(place, tiles_in.shape[0], scratch[4:])
    load = pltpu.make_async_copy(tiles_in, stream.work, scratch[3].at[0])
    load.start()
    load.wait()
    run_all(stream)
    store = pltpu.make_async_copy(
        stream.work.at[:, rows_at(place.core * HALF, HALF)], total_out, scratch[3].at[1]
    )
    store.start()
    store.wait()
    for copy in moved:
        copy.wait()


def reduce_tiles(tiles, outputs, number):
    count = tiles.shape[0]
    rows, length = outputs.shape[:2]
    any_spec = pl.BlockSpec(memory_space=pl.ANY)
    return pl.pallas_call(
        reduce_kernel,
        in_specs=[any_spec] * 2,
        out_specs=[any_spec] * 2,
        out_shape=[
            jax.ShapeDtypeStruct((2 * rows, length // 2, D), b16),
            jax.ShapeDtypeStruct((count, HALF, D), b16),
        ],
        scratch_shapes=part_sems(1)
        + [pltpu.SemaphoreType.DMA((2,))]
        + mover_scratch(count)
        + [pltpu.VMEM((count, HALF, D), b16)],
        compiler_params=pltpu.CompilerParams(
            collective_id=number, has_side_effects=True, vmem_limit_bytes=56 * MIB
        ),
        name="reduce_tiles",
    )(tiles, outputs)


def reduce_last_kernel(tiles_in, vec_in, y_in, y_out, total_out, vec_out, *scratch):
    place = Place()
    place.greet()
    vec_land, vec_send, vec_receive = scratch[:3]
    devices = [{"blk": place.other}] + list(place.partners)

    def vector_step(index):
        copy = remote(
            vec_out.at[...],
            vec_land.at[index],
            vec_send.at[index],
            vec_receive.at[index],
            devices[index],
        )
        return copy

    vec_out[...] = vec_in[...]
    vector_step(0).start()
    rest = scratch[3:]
    rows, span = y_in.shape[0], y_in.shape[1] // 2
    moved = back_part([(y_in, y_out)], rest[:3], place, rows, span)
    for copy in moved:
        copy.start()
    stream = Reduce(place, tiles_in.shape[0], rest[4:])
    load = pltpu.make_async_copy(tiles_in, stream.work, rest[3].at[0])
    load.start()
    load.wait()
    for tick in range(stream.count + stream.steps - 1):
        for tile in range(stream.count):
            if 0 <= tick - tile < stream.steps:
                stream.step(tile, tick - tile)
        if tick < 5:
            vector_step(tick).wait()
            vec_out[...] += vec_land[tick]
            if tick < 4:
                vector_step(tick + 1).start()
    store = pltpu.make_async_copy(
        stream.work.at[:, rows_at(place.core * HALF, HALF)], total_out, rest[3].at[1]
    )
    store.start()
    store.wait()
    for copy in moved:
        copy.wait()


def reduce_last(tiles, vectors, outputs, number):
    count = tiles.shape[0]
    rows, length = outputs.shape[:2]
    any_spec = pl.BlockSpec(memory_space=pl.ANY)
    vmem = pl.BlockSpec(memory_space=pltpu.VMEM)
    return pl.pallas_call(
        reduce_last_kernel,
        in_specs=[any_spec, vmem, any_spec],
        out_specs=[any_spec, any_spec, vmem],
        out_shape=[
            jax.ShapeDtypeStruct((2 * rows, length // 2, D), b16),
            jax.ShapeDtypeStruct((count, HALF, D), b16),
            jax.ShapeDtypeStruct(vectors.shape, f32),
        ],
        scratch_shapes=[
            pltpu.VMEM((5,) + vectors.shape, f32),
            pltpu.SemaphoreType.DMA((5,)),
            pltpu.SemaphoreType.DMA((5,)),
        ]
        + part_sems(1)
        + [pltpu.SemaphoreType.DMA((2,))]
        + mover_scratch(count)
        + [pltpu.VMEM((count, HALF, D), b16)],
        compiler_params=pltpu.CompilerParams(
            collective_id=number, has_side_effects=True, vmem_limit_bytes=56 * MIB
        ),
        name="reduce_last",
    )(tiles, vectors, outputs)


def update_kernel(chosen, used, one, two, w_ref, m_ref, s_ref, w_out, m_out, s_out):
    slot = pl.program_id(0)
    grad = jnp.where(chosen[slot] < 3, one[0], two[0]).astype(f32)
    keep = used[slot] == 1
    parts = adam_step(w_ref[0], grad, m_ref[0], s_ref[0], RATE)
    for target, part in zip((w_out, m_out, s_out), parts):
        target[0] = jnp.where(keep, part, jnp.zeros_like(part))


def update(chosen, used, one, two, master, first, second):
    slots = master.shape[0]
    size = HALF // 2
    state = pl.BlockSpec((1, size, D), lambda s, b, chosen, used: (s, b, 0))
    return pl.pallas_call(
        update_kernel,
        grid_spec=pltpu.PrefetchScalarGridSpec(
            num_scalar_prefetch=2,
            grid=(slots, HALF // size),
            in_specs=[
                pl.BlockSpec(
                    (1, size, D), lambda s, b, chosen, used: (jnp.minimum(chosen[s], 2), b, 0)
                ),
                pl.BlockSpec(
                    (1, size, D), lambda s, b, chosen, used: (jnp.maximum(chosen[s] - 3, 0), b, 0)
                ),
                state,
                state,
                state,
            ],
            out_specs=[state] * 3,
        ),
        out_shape=[jax.ShapeDtypeStruct(master.shape, f32)] * 3,
        compiler_params=pltpu.CompilerParams(vmem_limit_bytes=32 * MIB),
        name="update",
    )(chosen, used, one, two, master, first, second)


def shards_paired(
    inputs,
    cotangent,
    doc_lengths,
    owner_list,
    master,
    first_moment,
    second_moment,
    vectors,
    vector_first,
    vector_second,
):
    rows_here, span, width = inputs.shape
    place = lax.axis_index("blk")
    member = lax.axis_index("dp")
    rows_mine = rows_here // 2
    order = jnp.arange(PIECES)
    same_owner = owner_list[:, None] == owner_list[None, :]
    ranks = jnp.sum(same_owner & (order[None, :] < order[:, None]), axis=1).astype(jnp.int32)
    slot_of = owner_list * CAP + ranks
    lengths = lax.dynamic_slice_in_dim(doc_lengths[:, 0], place * rows_mine, rows_mine, 0)
    bias = jnp.where(lengths < LEN, -1e30, 0.0).astype(f32)
    front_outs = front(owner_list, ranks, bias, master, vectors, inputs, cotangent)
    x, cot, normed, weights_one, weights_two, queries, keys, values = front_outs[:8]
    weights, recips, context_turned, context = front_outs[8:]
    x = x.reshape(-1, width)
    cot = cot.reshape(-1, width)
    block_out, residual, grad_context, sums_two, tiles_two = feed(
        context, context_turned, x, cot, weights_two, vectors
    )
    block_out, total_two = reduce_tiles(tiles_two, block_out.reshape(rows_mine, LEN, width), 1)
    grads = attend_back(weights, recips, values, queries, keys, context_turned, grad_context)
    weights_one = jnp.transpose(weights_one.reshape(PAIRS, D, 3, PAIR), (2, 1, 0, 3)).reshape(3, D, D)
    input_grad, sums_one, tiles_one = finish(grads, normed, x, residual, weights_one, vectors)
    vector_grads = jnp.concatenate(
        [sums_one[0:2], sums_two[0:2], sums_one[2:4], sums_two[2:4], sums_two[4:8]], axis=0
    )
    input_grad, total_one, vector_total = reduce_last(
        tiles_one,
        jnp.pad(vector_grads, ((0, 4), (0, 0))),
        input_grad.reshape(rows_mine, LEN, width),
        2,
    )
    own_slots = member * CAP + jnp.arange(CAP)
    pick = own_slots[:, None] == slot_of[None, :]
    used = jnp.any(pick, axis=1).astype(jnp.int32)
    chosen = jnp.argmax(pick, axis=1).astype(jnp.int32)
    updated = update(chosen, used, total_one, total_two, master, first_moment, second_moment)
    columns = vector_first.shape[1]
    vector_cols = lax.dynamic_slice_in_dim(vectors, place * columns, columns, 1)
    vector_total = lax.dynamic_slice(vector_total, (0, place * columns), (PIECES, columns))
    updated_vectors = adam_step(vector_cols, vector_total, vector_first, vector_second, VEC_RATE)
    return (
        block_out.astype(f32),
        input_grad.astype(f32),
        *updated,
        *updated_vectors,
    )


def solution(mesh):
    in_specs = (
        P("dp", "blk", None),
        P("dp", "blk", None),
        P("dp", None),
        P(),
        P("dp", "blk", None),
        P("dp", "blk", None),
        P("dp", "blk", None),
        P(),
        P(None, "blk"),
        P(None, "blk"),
    )
    out_specs = (
        P("dp", "blk", None),
        P("dp", "blk", None),
        P("dp", "blk", None),
        P("dp", "blk", None),
        P("dp", "blk", None),
        P(None, "blk"),
        P(None, "blk"),
        P(None, "blk"),
    )
    paired = mesh.shape["blk"] == 2 and mesh.shape["dp"] == 16
    shards = shards_paired if paired else shards_any
    return jax.shard_map(shards, mesh=mesh, in_specs=in_specs, out_specs=out_specs, check_vma=False)
```

```python
from functools import partial

import jax
import jax.numpy as jnp
from jax import lax
from jax.experimental import pallas as pl
from jax.experimental.pallas import tpu as pltpu
from jax.sharding import PartitionSpec as P

D = 768
FF = 3072
HEADS = 12
HEAD_DIM = 64
LEN = 1024
CAP = 3
STEP = 10
PIECES = 12


EPS_NORM = 1e-05
BETA_ONE = 0.9
BETA_TWO = 0.999
RATE = 0.04
VEC_RATE = 0.25
DECAY = 0.01
ADAM_EPS = 1e-08


def normalize(values_in, gain, shift):
    center = jnp.mean(values_in, axis=-1, keepdims=True)
    offset = values_in - center
    spread = jnp.mean(offset * offset, axis=-1, keepdims=True)
    return offset * lax.rsqrt(spread + EPS_NORM) * gain + shift


def adam_step(weight, grad, first, second, rate):
    first_new = BETA_ONE * first + (1.0 - BETA_ONE) * grad
    second_new = BETA_TWO * second + (1.0 - BETA_TWO) * grad * grad
    corrected = (
        first_new
        / (1.0 - BETA_ONE**STEP)
        / (jnp.sqrt(second_new / (1.0 - BETA_TWO**STEP)) + ADAM_EPS)
    )
    return (weight - rate * (corrected + DECAY * weight), first_new, second_new)


def shards_any(
    inputs,
    cotangent,
    doc_lengths,
    owner_list,
    master,
    first_moment,
    second_moment,
    vectors,
    vector_first,
    vector_second,
):
    rows_here, span, width = inputs.shape
    tokens_here = rows_here * span
    fold = FF // D
    scale = HEAD_DIM ** (-0.5)
    place = lax.axis_index("blk")
    f32 = jnp.float32
    b16 = jnp.bfloat16
    order = jnp.arange(PIECES)
    same_owner = owner_list[:, None] == owner_list[None, :]
    ranks = jnp.sum(same_owner & (order[None, :] < order[:, None]), axis=1)
    slot_of = owner_list * CAP + ranks

    mine = (owner_list == lax.axis_index("dp"))[:, None, None]
    tile_rows = lax.psum(jnp.where(mine, master[ranks], 0.0).astype(b16), "dp")
    tiles = lax.all_gather(tile_rows, "blk", axis=1, tiled=True)
    query_weight = tiles[0]
    key_weight = tiles[1]
    value_weight = tiles[2]
    out_weight = tiles[3]
    up_weight = jnp.transpose(tiles[4 : 4 + fold], (1, 0, 2)).reshape(width, FF)
    down_weight = tiles[4 + fold :].reshape(FF, width)
    flat_in = inputs.reshape(tokens_here, width).astype(f32)
    normed_one = normalize(flat_in, vectors[0], vectors[1]).astype(b16)
    queries = (jnp.dot(normed_one, query_weight, preferred_element_type=f32) + vectors[4]).astype(
        b16
    )
    keys_here = jnp.dot(normed_one, key_weight, preferred_element_type=f32).astype(b16)
    values_here = (
        jnp.dot(normed_one, value_weight, preferred_element_type=f32) + vectors[5]
    ).astype(b16)
    query_heads = queries.reshape(rows_here, span, HEADS, HEAD_DIM)
    first_len = doc_lengths[:, 0]
    query_seg = (place * span + jnp.arange(span))[None, :] >= first_len[:, None]

    def block_scores(key_block, start):
        count = key_block.shape[1]
        key_heads = key_block.reshape(rows_here, count, HEADS, HEAD_DIM)
        raw = (
            jnp.einsum("rqhd,rkhd->rhqk", query_heads, key_heads, preferred_element_type=f32)
            * scale
        )
        key_seg = (start + jnp.arange(count))[None, :] >= first_len[:, None]
        allowed = query_seg[:, None, :, None] == key_seg[:, None, None, :]
        return (raw, allowed)

    key_rows = keys_here.reshape(rows_here, span, width)
    value_rows = values_here.reshape(rows_here, span, width)
    top = jnp.full((rows_here, HEADS, span), -1e30, f32)
    key_block = lax.all_gather(key_rows, "blk", axis=1, tiled=True)
    value_block = lax.all_gather(value_rows, "blk", axis=1, tiled=True)
    count = key_block.shape[1]
    raw, allowed = block_scores(key_block, jnp.int32(0))
    new_top = jnp.maximum(top, jnp.max(jnp.where(allowed, raw, -1e30), axis=-1))
    weights = jnp.where(allowed, jnp.exp(raw - new_top[..., None]), 0.0)
    value_heads = value_block.reshape(rows_here, count, HEADS, HEAD_DIM)
    update = jnp.einsum(
        "rhqk,rkhd->rhqd", weights.astype(b16), value_heads, preferred_element_type=f32
    )
    total = jnp.sum(weights, axis=-1)
    log_total = new_top + jnp.log(total)
    context_raw = update / total[..., None]
    context_low = jnp.transpose(context_raw, (0, 2, 1, 3)).reshape(tokens_here, width).astype(b16)
    residual = flat_in + (jnp.dot(context_low, out_weight, preferred_element_type=f32) + vectors[6])
    normed_two = normalize(residual, vectors[2], vectors[3]).astype(b16)
    hidden = jnp.dot(normed_two, up_weight, preferred_element_type=f32) + vectors[8:].reshape(FF)
    gelu_exact = partial(jax.nn.gelu, approximate=False)
    active, gelu_pull = jax.vjp(gelu_exact, hidden)
    active_low = active.astype(b16)
    block_out = (
        residual + (jnp.dot(active_low, down_weight, preferred_element_type=f32) + vectors[7])
    ).reshape(rows_here, span, width)
    grad_out = cotangent.reshape(tokens_here, width)
    down_grad = jnp.einsum("tf,td->fd", active_low, grad_out, preferred_element_type=f32)
    down_sum = jnp.sum(grad_out, axis=0, dtype=f32)
    grad_active = jnp.einsum("td,fd->tf", grad_out, down_weight, preferred_element_type=f32)
    grad_hidden = gelu_pull(grad_active)[0].astype(b16)
    up_grad = jnp.einsum("td,tf->df", normed_two, grad_hidden, preferred_element_type=f32)
    up_sum = jnp.sum(grad_hidden, axis=0, dtype=f32)
    ffn_tiles = jnp.concatenate(
        [
            jnp.transpose(up_grad.reshape(width, fold, width), (1, 0, 2)),
            down_grad.reshape(fold, width, width),
        ],
        axis=0,
    )
    grad_normed_two = jnp.einsum("tf,df->td", grad_hidden, up_weight, preferred_element_type=f32)
    unused, second_pull = jax.vjp(normalize, residual, vectors[2], vectors[3])
    residual_part, gain_two_grad, shift_two_grad = second_pull(grad_normed_two)
    grad_residual = grad_out.astype(f32) + residual_part
    grad_attended = grad_residual.astype(b16)
    out_grad = jnp.einsum("tm,td->md", context_low, grad_attended, preferred_element_type=f32)
    out_sum = jnp.sum(grad_attended, axis=0, dtype=f32)
    grad_context = jnp.einsum(
        "td,md->tm", grad_attended, out_weight, preferred_element_type=f32
    ).astype(b16)
    grad_heads = grad_context.reshape(rows_here, span, HEADS, HEAD_DIM)
    delta = jnp.einsum("rqhd,rhqd->rhq", grad_heads.astype(f32), context_raw)
    key_all, value_all = (
        lax.all_gather(key_rows, "blk", axis=1, tiled=True),
        lax.all_gather(value_rows, "blk", axis=1, tiled=True),
    )
    key_size = min(512, LEN)

    def back_block(index, carry):
        grad_query, key_total, value_total = carry
        start = index * key_size
        key_block = lax.dynamic_slice_in_dim(key_all, start, key_size, 1)
        value_block = lax.dynamic_slice_in_dim(value_all, start, key_size, 1)
        raw, allowed = block_scores(key_block, start)
        weights_back = jnp.where(allowed, jnp.exp(raw - log_total[..., None]), 0.0)
        key_heads = key_block.reshape(rows_here, key_size, HEADS, HEAD_DIM)
        value_heads = value_block.reshape(rows_here, key_size, HEADS, HEAD_DIM)
        value_grad = jnp.einsum(
            "rhqk,rqhd->rkhd", weights_back.astype(b16), grad_heads, preferred_element_type=f32
        )
        weight_grad = jnp.einsum(
            "rqhd,rkhd->rhqk", grad_heads, value_heads, preferred_element_type=f32
        )
        score_grad = (weights_back * (weight_grad - delta[..., None])).astype(b16)
        grad_query = (
            grad_query
            + jnp.einsum("rhqk,rkhd->rqhd", score_grad, key_heads, preferred_element_type=f32)
            * scale
        )
        key_grad = (
            jnp.einsum("rhqk,rqhd->rkhd", score_grad, query_heads, preferred_element_type=f32)
            * scale
        )
        key_total = lax.dynamic_update_slice_in_dim(
            key_total, key_grad.reshape(rows_here, key_size, width), start, 1
        )
        value_total = lax.dynamic_update_slice_in_dim(
            value_total, value_grad.reshape(rows_here, key_size, width), start, 1
        )
        return (grad_query, key_total, value_total)

    zero_rows = jnp.zeros((rows_here, LEN, width), f32)
    grad_query, key_total, value_total = lax.fori_loop(
        0,
        LEN // key_size,
        back_block,
        (jnp.zeros((rows_here, span, HEADS, HEAD_DIM), f32), zero_rows, zero_rows),
    )
    key_grad_here, value_grad_here = (
        lax.psum_scatter(
            key_total.astype(jnp.bfloat16), "blk", scatter_dimension=1, tiled=True
        ).astype(jnp.float32),
        lax.psum_scatter(
            value_total.astype(jnp.bfloat16), "blk", scatter_dimension=1, tiled=True
        ).astype(jnp.float32),
    )
    query_low = grad_query.reshape(tokens_here, width).astype(b16)
    key_low = key_grad_here.reshape(tokens_here, width).astype(b16)
    value_low = value_grad_here.reshape(tokens_here, width).astype(b16)
    query_tile = jnp.einsum("td,te->de", normed_one, query_low, preferred_element_type=f32)
    key_tile = jnp.einsum("td,te->de", normed_one, key_low, preferred_element_type=f32)
    value_tile = jnp.einsum("td,te->de", normed_one, value_low, preferred_element_type=f32)
    grad_normed_one = (
        jnp.einsum("te,de->td", query_low, query_weight, preferred_element_type=f32)
        + jnp.einsum("te,de->td", key_low, key_weight, preferred_element_type=f32)
        + jnp.einsum("te,de->td", value_low, value_weight, preferred_element_type=f32)
    )
    unused, first_pull = jax.vjp(normalize, flat_in, vectors[0], vectors[1])
    input_part, gain_one_grad, shift_one_grad = first_pull(grad_normed_one)
    input_grad = (grad_residual + input_part).reshape(rows_here, span, width)
    vector_grads = jnp.concatenate(
        [
            jnp.stack(
                [
                    gain_one_grad,
                    shift_one_grad,
                    gain_two_grad,
                    shift_two_grad,
                    jnp.sum(query_low, axis=0, dtype=f32),
                    jnp.sum(value_low, axis=0, dtype=f32),
                    out_sum,
                    down_sum,
                ]
            ),
            up_sum.reshape(fold, width),
        ],
        axis=0,
    )
    attn_tiles = jnp.stack([query_tile, key_tile, value_tile, out_grad])
    piece_share, vector_share = (
        lax.psum_scatter(
            jnp.concatenate([attn_tiles, ffn_tiles], axis=0).astype(jnp.bfloat16),
            "blk",
            scatter_dimension=1,
            tiled=True,
        ).astype(jnp.float32),
        lax.psum_scatter(
            vector_grads.astype(jnp.bfloat16), "blk", scatter_dimension=1, tiled=True
        ).astype(jnp.float32),
    )
    own_slots = lax.axis_index("dp") * CAP + jnp.arange(CAP)
    pick = (own_slots[:, None] == slot_of[None, :]).astype(f32)
    occupied = jnp.sum(pick, axis=1)[:, None, None]
    total_share, vector_total = (
        lax.psum(piece_share.astype(jnp.bfloat16), "dp").astype(jnp.float32),
        lax.psum(vector_share.astype(jnp.bfloat16), "dp").astype(jnp.float32),
    )
    slot_grads = jnp.einsum("cp,prd->crd", pick, total_share, precision=lax.Precision.HIGHEST)
    new_master, new_first, new_second = adam_step(
        master, slot_grads, first_moment, second_moment, RATE
    )
    columns = vector_first.shape[1]
    vector_cols = lax.dynamic_slice_in_dim(vectors, place * columns, columns, 1)
    new_vectors, new_vector_first, new_vector_second = adam_step(
        vector_cols, vector_total, vector_first, vector_second, VEC_RATE
    )
    return (
        block_out,
        input_grad,
        new_master * occupied,
        new_first * occupied,
        new_second * occupied,
        new_vectors,
        new_vector_first,
        new_vector_second,
    )


f32 = jnp.float32
b16 = jnp.bfloat16
LOG2E = 1.4426950408889634
MIB = 1024 * 1024
PAIRS = HEADS // 2
PAIR = 2 * HEAD_DIM


def dot_nn(left, right):
    return lax.dot_general(left, right, (((1,), (0,)), ((), ())), preferred_element_type=f32)


def dot_nt(left, right):
    return lax.dot_general(left, right, (((1,), (1,)), ((), ())), preferred_element_type=f32)


def dot_tn(left, right):
    return lax.dot_general(left, right, (((0,), (0,)), ((), ())), preferred_element_type=f32)


def norm_parts(values_in):
    center = jnp.mean(values_in, axis=-1, keepdims=True)
    offset = values_in - center
    spread = jnp.mean(offset * offset, axis=-1, keepdims=True)
    rstd = lax.rsqrt(spread + EPS_NORM)
    return offset * rstd, rstd


def norm_back(grad, unit, rstd, gain):
    scaled = grad * gain
    first = jnp.mean(scaled, axis=-1, keepdims=True)
    second = jnp.mean(scaled * unit, axis=-1, keepdims=True)
    return rstd * (scaled - first - unit * second)


def gelu_parts(value):
    bell = jnp.exp2(value * value * (-0.5 * LOG2E))
    ratio = pl.reciprocal(1.0 + (0.3275911 * 0.7071067811865476) * jnp.abs(value))
    poly = 0.5 * 1.061405429
    poly = poly * ratio + 0.5 * -1.453152027
    poly = poly * ratio + 0.5 * 1.421413741
    poly = poly * ratio + 0.5 * -0.284496736
    poly = poly * ratio + 0.5 * 0.254829592
    tail = poly * ratio * bell
    cdf = jnp.where(value >= 0.0, 1.0 - tail, tail)
    return value * cdf, cdf + value * (bell * 0.3989422804014327)


def head_only(block, head):
    lane = lax.broadcasted_iota(jnp.int32, block.shape, 1)
    keep = (lane >= head * HEAD_DIM) & (lane < (head + 1) * HEAD_DIM)
    return jnp.where(keep, block, jnp.zeros_like(block))


def feed_kernel(
    c_ref, o_ref, x_ref, g_ref, w_ref, vec_ref,
    y_ref, r_ref, d_ref, sums_ref, tiles_ref,
    acc_ref, stage_ref, sem_ref,
):
    fold = FF // D
    step = pl.program_id(0)

    @pl.when(step == 0)
    def clear():
        acc_ref[...] = jnp.zeros_like(acc_ref)
        sums_ref[...] = jnp.zeros_like(sums_ref)

    residual = x_ref[...].astype(f32) + (dot_nn(c_ref[...], w_ref[0]) + vec_ref[6:7, :])
    unit, rstd = norm_parts(residual)
    gain = vec_ref[2:3, :]
    normed = (unit * gain + vec_ref[3:4, :]).astype(b16)
    turned = normed.T
    cot = g_ref[...]
    out = residual + vec_ref[7:8, :]
    grad = jnp.zeros_like(out)

    def begin(part):
        hidden = dot_nn(normed, w_ref[1 + part])
        return hidden, dot_nt(cot, w_ref[1 + fold + part])

    ready = begin(0)
    for part in range(fold):
        hidden, pulled = ready
        if part + 1 < fold:
            ready = begin(part + 1)
        active, slope = gelu_parts(hidden + vec_ref[8 + part : 9 + part, :])
        active = active.astype(b16)
        pulled = (pulled * slope).astype(b16)
        out = out + dot_nn(active, w_ref[1 + fold + part])
        grad = grad + dot_nt(pulled, w_ref[1 + part])
        acc_ref[1 + part] += dot_nn(turned, pulled)
        acc_ref[1 + fold + part] += dot_tn(active, cot)
        sums_ref[8 + part : 9 + part, :] += jnp.sum(pulled.astype(f32), 0, keepdims=True)
    y_ref[...] = out.astype(b16)
    wide = cot.astype(f32)
    sums_ref[2:3, :] += jnp.sum(grad * unit, 0, keepdims=True)
    sums_ref[3:4, :] += jnp.sum(grad, 0, keepdims=True)
    sums_ref[7:8, :] += jnp.sum(wide, 0, keepdims=True)
    back = wide + norm_back(grad, unit, rstd, gain)
    r_ref[...] = back.astype(b16)
    low = back.astype(b16)
    sums_ref[6:7, :] += jnp.sum(low.astype(f32), 0, keepdims=True)
    d_ref[...] = dot_nt(w_ref[0], low).astype(b16)
    acc_ref[0] += dot_nn(o_ref[...], low)

    @pl.when(step == pl.num_programs(0) - 1)
    def send():
        count = 1 + 2 * fold
        copies = []
        for part in range(count):
            if part >= 2:
                copies[part - 2].wait()
            stage_ref[part % 2] = acc_ref[part].astype(b16)
            copy = pltpu.make_async_copy(stage_ref.at[part % 2], tiles_ref.at[part], sem_ref.at[part % 2])
            copy.start()
            copies.append(copy)
        copies[count - 2].wait()
        copies[count - 1].wait()


def feed(context, turned, x, cot, weights, vectors):
    tokens = x.shape[0]
    size = 256
    count = 1 + 2 * (FF // D)
    token_block = pl.BlockSpec((size, D), lambda i: (i, 0))
    turned_block = pl.BlockSpec((D, size), lambda i: (0, i))
    return pl.pallas_call(
        feed_kernel,
        grid=(tokens // size,),
        in_specs=[
            token_block,
            turned_block,
            token_block,
            token_block,
            pl.BlockSpec((count, D, D), lambda i: (0, 0, 0), pipeline_mode=pl.Buffered(1)),
            pl.BlockSpec((PIECES, D), lambda i: (0, 0)),
        ],
        out_specs=[
            token_block,
            token_block,
            turned_block,
            pl.BlockSpec((16, D), lambda i: (0, 0)),
            pl.BlockSpec(memory_space=pl.ANY),
        ],
        out_shape=[
            jax.ShapeDtypeStruct((tokens, D), b16),
            jax.ShapeDtypeStruct((tokens, D), b16),
            jax.ShapeDtypeStruct((D, tokens), b16),
            jax.ShapeDtypeStruct((16, D), f32),
            jax.ShapeDtypeStruct((count, D, D), b16),
        ],
        scratch_shapes=[
            pltpu.VMEM((count, D, D), f32),
            pltpu.VMEM((2, D, D), b16),
            pltpu.SemaphoreType.DMA((2,)),
        ],
        compiler_params=pltpu.CompilerParams(vmem_limit_bytes=60 * MIB),
        cost_estimate=pl.CostEstimate(
            flops=6 * count * tokens * D * D,
            bytes_accessed=18 * tokens * D + 4 * count * D * D,
            transcendentals=2 * tokens * FF,
        ),
        name="feed",
    )(context, turned, x, cot, weights, vectors)


MESH = pl.DeviceIdType.MESH
HALF = D // 2
FLOWS = 2
FLOW = HALF // FLOWS
NEAR = FLOW // 2
KEEP = NEAR // 2
WIDE = 3 * PAIR
REST = PIECES - 3
GROUPS = ((0, 1), (1, 2), (3, 3))
CHUNKS = len(GROUPS)


class Place:
    def __init__(self):
        self.me = lax.axis_index("dp")
        self.core = lax.axis_index("blk")
        self.bits = [lax.rem(self.me // weight, 2) for weight in (1, 2, 4, 8)]
        self.chips = [
            self.me + weight - 2 * weight * bit for weight, bit in zip((1, 2, 4, 8), self.bits)
        ]
        self.partners = [{"dp": chip} for chip in self.chips]
        low, high = self.bits[2:]
        self.inner = low != high
        self.across = {"dp": self.me + 4 - 8 * low + 8 - 16 * high}
        self.other = 1 - self.core
        self.twin = {"blk": self.other}

    def greet(self):
        barrier = pltpu.get_barrier_semaphore()
        for device in self.partners + [self.across, self.twin]:
            pl.semaphore_signal(barrier, 1, device_id=device, device_id_type=MESH)
        pl.semaphore_wait(barrier, 6)

    def flow(self, index):
        first, second = (0, 1) if index == 0 else (1, 0)
        base = index * FLOW
        near = base + self.bits[first] * NEAR
        far = base + NEAR - self.bits[first] * NEAR
        keep = near + self.bits[second] * KEEP
        give = near + KEEP - self.bits[second] * KEEP
        return first, second, near, far, keep, give


def remote(source, target, send, receive, device):
    return pltpu.make_async_remote_copy(
        src_ref=source,
        dst_ref=target,
        send_sem=send,
        recv_sem=receive,
        device_id=device,
        device_id_type=MESH,
    )


def rows_at(start, count):
    return pl.ds(pl.multiple_of(start, 16), count)


class Spread:
    def __init__(self, place, owner, rank, slots, land, gift, sems):
        self.place, self.owner, self.rank = place, owner, rank
        self.slots, self.land, self.gift, self.sems = slots, land, gift, sems

    def cols(self, chunk):
        return pl.ds(GROUPS[chunk][0] * PAIR, GROUPS[chunk][1] * PAIR)

    def first_copy(self, chunk, index):
        first, second, near, far, keep, give = self.place.flow(index)
        return remote(
            self.slots.at[:, rows_at(far, NEAR), self.cols(chunk)],
            self.land[chunk].at[index],
            self.sems[0].at[chunk, index, 0],
            self.sems[1].at[chunk, index, 0],
            self.place.partners[first],
        )

    def second_copy(self, chunk, index, which):
        first, second, near, far, keep, give = self.place.flow(index)
        if which == 0:
            source = self.slots.at[:, rows_at(give, KEEP), self.cols(chunk)]
        else:
            source = self.land[chunk].at[index, :, rows_at(give - near, KEEP)]
        return remote(
            source,
            self.gift[chunk].at[index, pl.ds(which * CAP, CAP)],
            self.sems[0].at[chunk, index, 1 + which],
            self.sems[1].at[chunk, index, 1 + which],
            self.place.partners[second],
        )

    def step(self, chunk, index):
        for flow in range(FLOWS):
            if index == 0:
                self.first_copy(chunk, flow).start()
                self.second_copy(chunk, flow, 0).start()
            if index == 1:
                self.first_copy(chunk, flow).wait()
                self.second_copy(chunk, flow, 1).start()
            if index == 2:
                self.second_copy(chunk, flow, 0).wait()
                self.second_copy(chunk, flow, 1).wait()

    def piece(self, tile, index, chunk, start, count):
        first, second, near, far, keep, give = self.place.flow(index)
        owner, rank = self.owner[tile], self.rank[tile]
        bits = [lax.rem(owner, 2), lax.rem(owner // 2, 2)]
        apart = [bit != mine for bit, mine in zip(bits, self.place.bits)]
        cols = pl.ds(start, count)
        mine = self.slots[rank, rows_at(keep, KEEP), pl.ds(GROUPS[chunk][0] * PAIR + start, count)]
        firsts = self.land[chunk][index, rank, rows_at(keep - near, KEEP), cols]
        gifts = self.gift[chunk][index, jnp.where(apart[first], CAP, 0) + rank, :, cols]
        value = jnp.where(apart[second], gifts, jnp.where(apart[first], firsts, mine))
        layer = owner // 4 == self.place.me // 4
        return jnp.where(layer, value, jnp.zeros_like(value))


class Column:
    steps = 4

    def __init__(self, place, kept, read, write, land, sems):
        self.place, self.kept, self.read, self.write = place, kept, read, write
        self.land, self.sems = land, sems

    def copy(self, index):
        target = self.land.at[index % 2]
        device = self.place.across if index == 1 else self.place.partners[2]
        return remote(
            self.kept, target, self.sems[0].at[index], self.sems[1].at[index], device
        )

    def add(self, index):
        self.write((self.read().astype(f32) + self.land[index].astype(f32)).astype(b16))


def column_step(place, columns, index):
    @pl.when(place.inner)
    def inner():
        for column in columns:
            if index == 1:
                column.copy(0).wait_recv()
                column.add(0)
                column.copy(1).start()
            if index == 2:
                column.copy(1).wait()
                column.add(1)
                column.copy(2).start()
            if index == 3:
                column.copy(2).wait_send()

    @pl.when(jnp.logical_not(place.inner))
    def outer():
        for column in columns:
            if index == 0:
                column.copy(0).start()
            if index == 1:
                column.copy(0).wait_send()
            if index == 3:
                column.copy(2).wait_recv()
                column.write(column.land[0])


class Item:
    steps = 7

    def __init__(self, place, work, land, sems, load, store=None):
        self.place, self.work, self.land, self.sems = place, work, land, sems
        self.load, self.store = load, store
        self.base = place.core * HALF

    def column(self, flow):
        rows = rows_at(self.base + self.place.flow(flow)[4], KEEP)

        def read():
            return self.work[:, rows]

        def write(value):
            self.work[:, rows] = value

        sems = (self.sems[0].at[flow], self.sems[1].at[flow])
        return Column(self.place, self.work.at[:, rows], read, write, self.land.at[flow], sems)

    def copy(self, flow, index):
        first, second, near, far, keep, give = self.place.flow(flow)
        kept = self.work.at[:, rows_at(self.base + keep, KEEP)]
        half = self.work.at[:, rows_at(self.base + near, NEAR)]
        source, device = [
            (kept, self.place.partners[second]),
            (half, self.place.partners[first]),
        ][index]
        return remote(
            source, source, self.sems[0].at[flow, 3 + index], self.sems[1].at[flow, 3 + index], device
        )

    def pair(self):
        rows = self.work.at[:, rows_at(self.base, HALF)]
        return remote(rows, rows, self.sems[0].at[0, 5], self.sems[1].at[0, 5], self.place.twin)

    def step(self, index):
        for flow in range(FLOWS):
            if index == 0:
                self.load(self.work, rows_at(self.base + self.place.flow(flow)[4], KEEP), flow)
        if index <= 3:
            column_step(self.place, [self.column(flow) for flow in range(FLOWS)], index)
        for flow in range(FLOWS):
            if 4 <= index <= 5:
                self.copy(flow, index - 4).wait()
            if 3 <= index <= 4:
                self.copy(flow, index - 3).start()
        if index == 5:
            self.pair().start()
        if index == 6:
            self.pair().wait()
            self.store().start()


REST_GROUPS = ((0, 3), (3, 3), (6, 3))
FRONT_PAIRS = (2, 4, 6)
FRONT_REST = (8, 11, 14)
FRONT_LEAD = 9


def front_kernel(
    owner, lengths, master, vec_ref, x_in, c_in,
    x_out, c_out, n_out, one_out, two_out, q_ref, k_ref, v_ref, p_ref, r_ref, o_ref, ctx_ref,
    rank, rows_ref, normed, keys, turned_values, slots,
    land_one, land_two, land_three, gift_one, gift_two, gift_three,
    one, one_land, two, two_land,
    spread_send, spread_recv, one_send, one_recv, two_send, two_recv,
    swap_send, swap_recv, swap_local, store_sem,
):
    pair = pl.program_id(0)
    row = pl.program_id(1)
    grid_step = pair * 2 + row
    place = Place()
    rows, span = x_in.shape[0] // 2, x_in.shape[1]
    land = (land_one, land_two, land_three)
    gift = (gift_one, gift_two, gift_three)
    spread = Spread(place, owner, rank, slots, land, gift, (spread_send, spread_recv))

    def swaps(index):
        source, target = [(x_in, rows_ref), (c_in, c_out)][index]
        here = pl.ds(place.core * span, span)
        near = pltpu.make_async_copy(
            source.at[pl.ds(place.core * rows, rows)], target.at[:, here], swap_local.at[index]
        )
        far = remote(
            source.at[pl.ds(place.other * rows, rows)],
            target.at[:, here],
            swap_send.at[index],
            swap_recv.at[index],
            place.twin,
        )
        return near, far

    def row_store():
        return pltpu.make_async_copy(rows_ref, x_out, store_sem.at[6])

    def normed_store():
        return pltpu.make_async_copy(normed, n_out, store_sem.at[7])

    def pair_item(group):
        first, count = GROUPS[group]
        span_of = pl.ds(first, count)

        def load(work, where, flow):
            for index in range(count):
                for tile in range(3):
                    part = spread.piece(tile, flow, group, index * PAIR, PAIR)
                    work[index, where, pl.ds(tile * PAIR, PAIR)] = part

        def store():
            return pltpu.make_async_copy(one.at[span_of], one_out.at[span_of], store_sem.at[group])

        sems = (one_send.at[group], one_recv.at[group])
        return Item(place, one.at[span_of], one_land.at[:, :, span_of], sems, load, store)

    def rest_item(group):
        first, count = REST_GROUPS[group]
        span_of = pl.ds(first, count)

        def load(work, where, flow):
            for index in range(count):
                for chunk, (start, wide) in enumerate(GROUPS):
                    part = spread.piece(3 + first + index, flow, chunk, 0, wide * PAIR)
                    work[index, where, pl.ds(start * PAIR, wide * PAIR)] = part

        def store():
            return pltpu.make_async_copy(
                two.at[span_of], two_out.at[span_of], store_sem.at[3 + group]
            )

        sems = (two_send.at[group], two_recv.at[group])
        return Item(place, two.at[span_of], two_land.at[:, :, span_of], sems, load, store)

    def tick(number):
        for chunk in range(CHUNKS):
            if 0 <= number - chunk <= 2:
                spread.step(chunk, number - chunk)
        starts = [(pair_item, group, start) for group, start in enumerate(FRONT_PAIRS)]
        starts += [(rest_item, group, start) for group, start in enumerate(FRONT_REST)]
        for make, group, start in starts:
            if 0 <= number - start < Item.steps:
                make(group).step(number - start)

    @pl.when(grid_step == 0)
    def lead():
        slots[...] = master[...].astype(b16)
        for tile in range(PIECES):
            count = jnp.int32(0)
            for before in range(tile):
                count = count + (owner[before] == owner[tile]).astype(jnp.int32)
            rank[tile] = jnp.minimum(count, CAP - 1)
        place.greet()
        for copy in swaps(0):
            copy.start()
        tick(0)
        for copy in swaps(1):
            copy.start()
        for copy in swaps(0):
            copy.wait()
        row_store().start()

        def norm_rows(index, carry):
            where = pl.ds(index * 256, 256)
            for part in range(rows):
                unit, unused = norm_parts(rows_ref[part, where].astype(f32))
                low = (unit * vec_ref[0:1, :] + vec_ref[1:2, :]).astype(b16)
                normed[pl.ds(part * LEN + index * 256, 256)] = low
            return carry

        tick(1)
        lax.fori_loop(0, LEN // 256, norm_rows, 0)
        normed_store().start()
        for number in range(2, FRONT_LEAD):
            tick(number)

    for number in range(2 * PAIRS):
        pl.when(grid_step == number)(partial(tick, FRONT_LEAD + number))

    @pl.when(row == 0)
    def project():
        lanes = pl.ds(pl.multiple_of(pair * PAIR, PAIR), PAIR)
        weight = one[pair]

        def part(index, carry):
            where = pl.ds(pl.multiple_of(index * 512, 512), 512)
            both = dot_nn(normed[where], weight)
            queries = both[:, :PAIR] + vec_ref[4:5, lanes]
            queries = (queries * (HEAD_DIM**-0.5 * LOG2E)).astype(b16)
            q_ref[:, where] = queries.T
            low = both[:, PAIR : 2 * PAIR].astype(b16)
            keys[where] = low
            k_ref[:, where] = low.T
            values = (both[:, 2 * PAIR :] + vec_ref[5:6, lanes]).astype(b16)
            v_ref[where] = values
            turned_values[:, where] = values.T
            return carry

        lax.fori_loop(0, normed.shape[0] // 512, part, 0)

    half = LEN // 2
    start = pl.multiple_of(row * LEN, LEN)
    split = lengths[place.core * rows + row, 0] < LEN
    shift = jnp.where(split, jnp.float32(-1e30), jnp.float32(0.0))

    def scores(head, step):
        cols = pl.ds(pl.multiple_of(start + step * half, half), half)
        others = pl.ds(pl.multiple_of(start + (1 - step) * half, half), half)
        queries = q_ref[:, cols]
        near = dot_nn(head_only(keys[cols], head), queries)
        far = dot_nn(head_only(keys[others], head), queries) + shift
        return near, far

    units = [(head, step) for head in range(2) for step in range(2)]
    ready = scores(*units[0])
    for index, (head, step) in enumerate(units):
        near, far = ready
        if index + 1 < len(units):
            ready = scores(*units[index + 1])
        part = slice(head * HEAD_DIM, (head + 1) * HEAD_DIM)
        top = jnp.maximum(jnp.max(near, 0, keepdims=True), jnp.max(far, 0, keepdims=True))
        near = jnp.exp2(near - top)
        far = jnp.exp2(far - top)
        total = jnp.sum(near, 0, keepdims=True) + jnp.sum(far, 0, keepdims=True)
        recip = 1.0 / total
        here = slice(step * half, (step + 1) * half)
        there = slice((1 - step) * half, (2 - step) * half)
        near, far = near.astype(b16), far.astype(b16)
        p_ref[head, here, here] = near
        p_ref[head, there, here] = far
        r_ref[0, head : head + 1, here] = recip
        cols = pl.ds(pl.multiple_of(start + step * half, half), half)
        others = pl.ds(pl.multiple_of(start + (1 - step) * half, half), half)
        out = dot_nn(turned_values[part, cols], near) + dot_nn(turned_values[part, others], far)
        o_ref[part, here] = (out * recip).astype(b16)
    ctx_ref[...] = o_ref[...].T

    @pl.when(grid_step == 2 * PAIRS - 1)
    def finish_copies():
        for copy in swaps(1):
            copy.wait()
        row_store().wait()
        normed_store().wait()
        for group in range(3):
            pair_item(group).store().wait()
            rest_item(group).store().wait()


def front(owner, lengths, master, vectors, inputs, cotangent):
    rows, span = inputs.shape[0] // 2, inputs.shape[1]
    tokens = rows * LEN
    any_spec = pl.BlockSpec(memory_space=pl.ANY)
    smem = pl.BlockSpec(memory_space=pltpu.SMEM)
    whole = jax.ShapeDtypeStruct((rows, LEN, D), b16)
    dma = pltpu.SemaphoreType.DMA
    return pl.pallas_call(
        front_kernel,
        grid=(PAIRS, rows),
        in_specs=[
            smem,
            smem,
            pl.BlockSpec((CAP, HALF, D), lambda h, r: (0, 0, 0), pipeline_mode=pl.Buffered(1)),
            pl.BlockSpec((PIECES, D), lambda h, r: (0, 0)),
            any_spec,
            any_spec,
        ],
        out_specs=[any_spec] * 5
        + [
            pl.BlockSpec((PAIR, tokens), lambda h, r: (h, 0)),
            pl.BlockSpec((PAIR, tokens), lambda h, r: (h, 0)),
            pl.BlockSpec((tokens, PAIR), lambda h, r: (0, h)),
            pl.BlockSpec((2, LEN, LEN), lambda h, r: (h * 2 + r, 0, 0)),
            pl.BlockSpec((1, 2, LEN), lambda h, r: (h * 2 + r, 0, 0)),
            pl.BlockSpec((PAIR, LEN), lambda h, r: (h, r)),
            pl.BlockSpec((LEN, PAIR), lambda h, r: (r, h)),
        ],
        out_shape=[
            whole,
            whole,
            jax.ShapeDtypeStruct((tokens, D), b16),
            jax.ShapeDtypeStruct((PAIRS, D, WIDE), b16),
            jax.ShapeDtypeStruct((REST, D, D), b16),
            jax.ShapeDtypeStruct((D, tokens), b16),
            jax.ShapeDtypeStruct((D, tokens), b16),
            jax.ShapeDtypeStruct((tokens, D), b16),
            jax.ShapeDtypeStruct((rows * HEADS, LEN, LEN), b16),
            jax.ShapeDtypeStruct((rows * PAIRS, 2, LEN), f32),
            jax.ShapeDtypeStruct((D, tokens), b16),
            jax.ShapeDtypeStruct((tokens, D), b16),
        ],
        scratch_shapes=[
            pltpu.SMEM((PIECES,), jnp.int32),
            pltpu.VMEM((rows, LEN, D), b16),
            pltpu.VMEM((tokens, D), b16),
            pltpu.VMEM((tokens, PAIR), b16),
            pltpu.VMEM((PAIR, tokens), b16),
            pltpu.VMEM((CAP, HALF, D), b16),
        ]
        + [pltpu.VMEM((FLOWS, CAP, NEAR, wide * PAIR), b16) for unused, wide in GROUPS]
        + [pltpu.VMEM((FLOWS, 2 * CAP, KEEP, wide * PAIR), b16) for unused, wide in GROUPS]
        + [
            pltpu.VMEM((PAIRS, D, WIDE), b16),
            pltpu.VMEM((FLOWS, 2, PAIRS, KEEP, WIDE), b16),
            pltpu.VMEM((REST, D, D), b16),
            pltpu.VMEM((FLOWS, 2, REST, KEEP, D), b16),
            dma((CHUNKS, FLOWS, 3)),
            dma((CHUNKS, FLOWS, 3)),
            dma((3, FLOWS, 6)),
            dma((3, FLOWS, 6)),
            dma((3, FLOWS, 6)),
            dma((3, FLOWS, 6)),
            dma((2,)),
            dma((2,)),
            dma((2,)),
            dma((8,)),
        ],
        compiler_params=pltpu.CompilerParams(
            collective_id=0, has_side_effects=True, vmem_limit_bytes=60 * MIB
        ),
        name="front",
    )(owner, lengths, master, vectors, inputs, cotangent)


class Sum:
    steps = 7

    def __init__(self, place, work, wide, narrow, sems, send_pair, add_own):
        self.place, self.work, self.wide, self.narrow, self.sems = place, work, wide, narrow, sems
        self.send_pair, self.add_own = send_pair, add_own

    def column(self, flow):
        rows = rows_at(self.place.flow(flow)[4], KEEP)

        def read():
            return self.work[:, rows]

        def write(value):
            self.work[:, rows] = value

        sems = (self.sems[0].at[flow, pl.ds(2, 3)], self.sems[1].at[flow, pl.ds(2, 3)])
        land = self.narrow.at[flow, pl.ds(1, 2)]
        return Column(self.place, self.work.at[:, rows], read, write, land, sems)

    def copy(self, flow, index):
        first, second, near, far, keep, give = self.place.flow(flow)
        source, target, device = [
            (self.work.at[:, rows_at(far, NEAR)], self.wide.at[flow], first),
            (self.work.at[:, rows_at(give, KEEP)], self.narrow.at[flow, 0], second),
        ][index]
        return remote(
            source,
            target,
            self.sems[0].at[flow, index],
            self.sems[1].at[flow, index],
            self.place.partners[device],
        )

    def add(self, rows, value):
        self.work[:, rows] = (self.work[:, rows].astype(f32) + value.astype(f32)).astype(b16)

    def step(self, index):
        if index == 0:
            self.send_pair().start()
        if index == 1:
            self.send_pair().wait()
            self.add_own()
        for flow in range(FLOWS):
            first, second, near, far, keep, give = self.place.flow(flow)
            if index == 1:
                self.copy(flow, 0).start()
            if index == 2:
                self.copy(flow, 0).wait()
                self.add(rows_at(near, NEAR), self.wide[flow])
                self.copy(flow, 1).start()
            if index == 3:
                self.copy(flow, 1).wait()
                self.add(rows_at(keep, KEEP), self.narrow[flow, 0])
        if index >= 3:
            columns = [self.column(flow) for flow in range(FLOWS)]
            column_step(self.place, columns, index - 3)


class Gather:
    steps = 3

    def __init__(self, place, work, narrow, wide, sems):
        self.place, self.work, self.narrow, self.wide = place, work, narrow, wide
        self.sems = sems

    def copy(self, flow, index):
        first, second, near, far, keep, give = self.place.flow(flow)
        rows, target, device = [
            (rows_at(keep, KEEP), self.narrow, second),
            (rows_at(near, NEAR), self.wide, first),
        ][index]
        return remote(
            self.work.at[:, rows],
            target.at[flow],
            self.sems[0].at[flow, 5 + index],
            self.sems[1].at[flow, 5 + index],
            self.place.partners[device],
        )

    def step(self, index):
        for flow in range(FLOWS):
            first, second, near, far, keep, give = self.place.flow(flow)
            if index > 0:
                self.copy(flow, index - 1).wait()
            if index == 1:
                self.work[:, rows_at(give, KEEP)] = self.narrow[flow]
            if index == 2:
                self.work[:, rows_at(far, NEAR)] = self.wide[flow]
            if index < 2:
                self.copy(flow, index).start()


class Hand:
    steps = 3

    def __init__(self, place, table, work, bag, gift, pack, last, own, out, sems, store_sems):
        self.place, self.table, self.work = place, table, work
        self.bag, self.gift, self.pack, self.last, self.own = bag, gift, pack, last, own
        self.out, self.sems, self.store_sems = out, sems, store_sems

    def tile(self, chip, rank, rows):
        return self.work[self.table[chip * CAP + rank], rows]

    def copy(self, flow, index):
        first, second = self.place.flow(flow)[:2]
        source, target, device = [
            (self.bag.at[flow], self.gift.at[flow], second),
            (self.pack.at[flow], self.last.at[flow], first),
        ][index]
        return remote(
            source,
            target,
            self.sems[0].at[flow, index],
            self.sems[1].at[flow, index],
            self.place.partners[device],
        )

    def stores(self, flow):
        first, second, near, far, keep, give = self.place.flow(flow)
        parts = [
            (self.own.at[flow], rows_at(keep, KEEP)),
            (self.gift.at[flow, pl.ds(0, CAP)], rows_at(give, KEEP)),
            (self.last.at[flow], rows_at(far, NEAR)),
        ]
        return [
            pltpu.make_async_copy(source, self.out.at[:, rows], self.store_sems.at[flow, index])
            for index, (source, rows) in enumerate(parts)
        ]

    def step(self, index):
        for flow in range(FLOWS):
            first, second, near, far, keep, give = self.place.flow(flow)
            rows = rows_at(keep, KEEP)
            if index == 0:
                beside = self.place.chips[second]
                across = beside + self.place.chips[first] - self.place.me
                for rank in range(CAP):
                    self.bag[flow, rank] = self.tile(beside, rank, rows)
                    self.bag[flow, CAP + rank] = self.tile(across, rank, rows)
                    self.own[flow, rank] = self.tile(self.place.me, rank, rows)
                self.copy(flow, 0).start()
            if index == 1:
                self.copy(flow, 0).wait()
                for rank in range(CAP):
                    mine = self.tile(self.place.chips[first], rank, rows)
                    self.pack[flow, rank, rows_at(keep - near, KEEP)] = mine
                    self.pack[flow, rank, rows_at(give - near, KEEP)] = self.gift[flow, CAP + rank]
                self.copy(flow, 1).start()
            if index == 2:
                self.copy(flow, 1).wait()
                for copy in self.stores(flow):
                    copy.start()


BACK_STEPS = 2 * PAIRS
BACK_TAIL = 4
BACK_PAIRS = ((0, 3), (3, 2), (5, 1))
BACK_REST = (0, 2, 4)
BACK_HAND = 11


def back_kernel(
    table, p_ref, r_ref, v_ref, q_ref, k_ref, o_ref, g_ref, w_ref, n_ref, x_ref, z_ref, vec_ref,
    tiles_in, sums_in, y_in,
    y_out, i_out, pairs_out, slots_out, sums_ref,
    grad_sum, wide_sum, turned, block_out,
    two, two_wide, two_narrow, two_stage, one, one_wide, one_narrow, one_send_stage, one_stage,
    gather_narrow, gather_wide,
    bag, gift, pack, last, own, vec_land,
    two_send, two_recv, one_send, one_recv, hand_send, hand_recv, hand_store,
    pair_two_send, pair_two_recv, pair_one_send, pair_one_recv, load_sem, store_sem,
    swap_send, swap_recv, swap_local, vec_send, vec_recv,
):
    step = pl.program_id(0)
    place = Place()
    rows, span = y_in.shape[0], y_in.shape[1] // 2
    near_half = rows_at(place.core * HALF, HALF)
    far_half = rows_at(place.other * HALF, HALF)

    def load_two(group):
        first, count = REST_GROUPS[group]
        return pltpu.make_async_copy(
            tiles_in.at[pl.ds(first, count), near_half], two_stage, load_sem.at[0]
        )

    def rest_sum(group):
        first, count = REST_GROUPS[group]
        span_of = pl.ds(first, count)
        work = two.at[span_of]

        def send_pair():
            return remote(
                tiles_in.at[span_of, far_half],
                work,
                pair_two_send.at[group],
                pair_two_recv.at[group],
                place.twin,
            )

        def add_own():
            load_two(group).wait()
            work[...] = (work[...].astype(f32) + two_stage[...].astype(f32)).astype(b16)

        sems = (two_send.at[group], two_recv.at[group])
        wide, narrow = two_wide.at[:, span_of], two_narrow.at[:, :, span_of]
        return Sum(place, work, wide, narrow, sems, send_pair, add_own)

    def pair_sum(group):
        first, count = BACK_PAIRS[group]
        span_of = pl.ds(first, count)
        work = one.at[span_of]

        def send_pair():
            return remote(
                one_send_stage.at[span_of],
                work,
                pair_one_send.at[group],
                pair_one_recv.at[group],
                place.twin,
            )

        def add_own():
            own = one_stage[span_of].astype(f32)
            work[...] = (work[...].astype(f32) + own).astype(b16)

        sems = (one_send.at[group], one_recv.at[group])
        wide, narrow = one_wide.at[:, span_of], one_narrow.at[:, :, span_of]
        return Sum(place, work, wide, narrow, sems, send_pair, add_own)

    def pair_gather(group):
        first, count = BACK_PAIRS[group]
        span_of = pl.ds(first, count)
        sems = (one_send.at[group], one_recv.at[group])
        narrow, wide = gather_narrow.at[:, span_of], gather_wide.at[:, span_of]
        return Gather(place, one.at[span_of], narrow, wide, sems)

    hand = Hand(
        place, table, two, bag, gift, pack, last, own, slots_out, (hand_send, hand_recv), hand_store
    )

    def pair_store(index, tile):
        return pltpu.make_async_copy(
            one.at[index, :, pl.ds(tile * PAIR, PAIR)],
            pairs_out.at[tile, :, pl.ds(index * PAIR, PAIR)],
            store_sem.at[index, tile],
        )

    def tick(number):
        for group, start in enumerate(BACK_REST):
            if 0 <= number - start < Sum.steps:
                rest_sum(group).step(number - start)
        for group, (first, count) in enumerate(BACK_PAIRS):
            start = 2 * (first + count)
            if 0 <= number - start < Sum.steps:
                pair_sum(group).step(number - start)
            if 0 <= number - start - Sum.steps + 1 < Gather.steps:
                pair_gather(group).step(number - start - Sum.steps + 1)
            if number == start + Sum.steps + 1:
                for index in range(first, first + count):
                    for tile in range(3):
                        pair_store(index, tile).start()
        if 0 <= number - BACK_HAND < Hand.steps:
            hand.step(number - BACK_HAND)
        for group, start in enumerate(BACK_REST):
            if number == max(start - 1, 0):
                load_two(group).start()

    def swap_y(index):
        there = pl.ds(place.core * rows, rows)
        if index == 0:
            return pltpu.make_async_copy(
                y_in.at[:, pl.ds(place.core * span, span)], y_out.at[there], swap_local.at[0]
            )
        return remote(
            y_in.at[:, pl.ds(place.other * span, span)],
            y_out.at[there],
            swap_send.at[0],
            swap_recv.at[0],
            place.twin,
        )

    @pl.when(step == 0)
    def lead():
        place.greet()
        for index in range(2):
            swap_y(index).start()
        sums_ref[...] = sums_in[...]

    for number in range(BACK_STEPS + BACK_TAIL):
        pl.when(step == number)(partial(tick, number))

    @pl.when(step < BACK_STEPS)
    def attention():
        pair, row = step // 2, lax.rem(step, 2)
        half = LEN // 2
        heads = []
        for head in range(2):
            part = slice(head * HEAD_DIM, (head + 1) * HEAD_DIM)
            values = head_only(v_ref[...], head)
            recip = r_ref[0, head : head + 1, :]
            grad = g_ref[part, :].astype(f32) * recip
            delta = jnp.sum(grad * o_ref[part, :].astype(f32), 0, keepdims=True)
            grad = grad.astype(b16)
            heads.append((values, grad, delta, jnp.concatenate([grad, grad], axis=0)))

        def raw(head, which):
            values, grad, delta, doubled = heads[head]
            return dot_nn(values, doubled[:, which * half : (which + 1) * half])

        units = [(head, which) for head in range(2) for which in range(2)]
        ready = raw(*units[0])
        for index, (head, which) in enumerate(units):
            slope = ready
            if index + 1 < len(units):
                ready = raw(*units[index + 1])
            values, grad, delta, doubled = heads[head]
            part = slice(head * HEAD_DIM, (head + 1) * HEAD_DIM)
            cols = slice(which * half, (which + 1) * half)
            weights = p_ref[head, :, cols]
            slope = (weights.astype(f32) * (slope - delta[:, cols])).astype(b16)
            value_grad = dot_nt(grad[:, cols], weights)
            key_grad = dot_nt(q_ref[part, cols], slope)
            query_grad = dot_nn(k_ref[part, :], slope) * (HEAD_DIM**-0.5)
            turned[part, cols] = query_grad.astype(b16)
            if which == 0:
                value_first, key_first = value_grad, key_grad
            else:
                value_grad, key_grad = value_first + value_grad, key_first + key_grad
                lower = slice(PAIR + head * HEAD_DIM, PAIR + (head + 1) * HEAD_DIM)
                turned[lower, :] = (key_grad * (1.0 / LOG2E)).astype(b16)
                lower = slice(2 * PAIR + head * HEAD_DIM, 2 * PAIR + (head + 1) * HEAD_DIM)
                turned[lower, :] = value_grad.astype(b16)
        where = pl.ds(pl.multiple_of(row * LEN, LEN), LEN)
        block = dot_nn(turned[...], n_ref[where])
        back = turned[...].T
        lanes = pl.ds(pl.multiple_of(pair * PAIR, PAIR), PAIR)
        ones = jnp.sum(back.astype(f32), 0, keepdims=True)
        sums_ref[4:5, lanes] += ones[:, :PAIR]
        sums_ref[5:6, lanes] += ones[:, 2 * PAIR :]
        term = dot_nt(back, w_ref[0])

        @pl.when(pair == 0)
        def begin():
            grad_sum[where] = term

        @pl.when(pair > 0)
        def add():
            grad_sum[where] += term

        @pl.when(row == 0)
        def keep():
            wide_sum[...] = block

        @pl.when(row == 1)
        def hand_on():
            whole = (wide_sum[...] + block).T
            low = whole.astype(b16)
            for core in range(2):

                @pl.when(place.core == core)
                def split():
                    one_stage[pair] = low[core * HALF : (core + 1) * HALF]
                    one_send_stage[pair] = low[(1 - core) * HALF : (2 - core) * HALF]

    def store_block(index):
        row, half = index // 2, index % 2
        target = i_out.at[place.core * rows + row]
        local = pltpu.make_async_copy(block_out.at[index], target, swap_local.at[1 + row])
        far = remote(
            block_out.at[index], target, swap_send.at[1 + row], swap_recv.at[1 + row], place.twin
        )
        return local, far, half

    for index in range(BACK_TAIL):

        @pl.when(step == BACK_STEPS + index)
        def close():
            size = LEN // 2
            grad = grad_sum[index * size : (index + 1) * size]
            unit, rstd = norm_parts(x_ref[...].astype(f32))
            sums_ref[0:1, :] += jnp.sum(grad * unit, 0, keepdims=True)
            sums_ref[1:2, :] += jnp.sum(grad, 0, keepdims=True)
            total = z_ref[...].astype(f32) + norm_back(grad, unit, rstd, vec_ref[0:1, :])
            block_out[index] = total.astype(b16)
            local, far, half = store_block(index)

            @pl.when(place.core == half)
            def keep():
                local.start()

            @pl.when(place.core != half)
            def give():
                far.start()

    @pl.when(step == BACK_STEPS + BACK_TAIL - 1)
    def drain():
        devices = [place.twin] + place.partners

        def vector(index):
            return remote(
                sums_ref, vec_land.at[index], vec_send.at[index], vec_recv.at[index], devices[index]
            )

        vector(0).start()
        for number in range(BACK_STEPS + BACK_TAIL, BACK_STEPS + Sum.steps + Gather.steps):
            tick(number)
            index = number - BACK_STEPS - BACK_TAIL
            if index < 5:
                vector(index).wait()
                sums_ref[...] += vec_land[index]
                if index < 4:
                    vector(index + 1).start()
        for index in range(2):
            swap_y(index).wait()
        for index in range(BACK_TAIL):
            local, far, half = store_block(index)

            @pl.when(place.core == half)
            def keep():
                local.wait()

            @pl.when(place.core != half)
            def give():
                far.wait()

        for index in range(PAIRS):
            for tile in range(3):
                pair_store(index, tile).wait()
        for flow in range(FLOWS):
            for copy in hand.stores(flow):
                copy.wait()


def back(table, attention, weights, normed, x, residual, vectors, tiles, sums, y):
    rows, length = y.shape[:2]
    tokens = rows * length
    any_spec = pl.BlockSpec(memory_space=pl.ANY)
    smem = pl.BlockSpec(memory_space=pltpu.SMEM)
    dma = pltpu.SemaphoreType.DMA

    def now(step):
        return jnp.minimum(step, BACK_STEPS - 1)

    def tail(step):
        return jnp.maximum(step - BACK_STEPS, 0)

    head_block = pl.BlockSpec((PAIR, LEN), lambda s: (now(s) // 2, lax.rem(now(s), 2)))
    tail_block = pl.BlockSpec((LEN // 2, D), lambda s: (tail(s), 0))
    whole = pl.BlockSpec((PIECES, D), lambda s: (0, 0))
    sums_block = pl.BlockSpec((16, D), lambda s: (0, 0))
    return pl.pallas_call(
        back_kernel,
        grid=(BACK_STEPS + BACK_TAIL,),
        in_specs=[
            smem,
            pl.BlockSpec((2, LEN, LEN), lambda s: (now(s), 0, 0)),
            pl.BlockSpec((1, 2, LEN), lambda s: (now(s), 0, 0)),
            pl.BlockSpec((LEN, PAIR), lambda s: (lax.rem(now(s), 2), now(s) // 2)),
            head_block,
            head_block,
            head_block,
            head_block,
            pl.BlockSpec((1, D, WIDE), lambda s: (now(s) // 2, 0, 0)),
            pl.BlockSpec((tokens, D), lambda s: (0, 0), pipeline_mode=pl.Buffered(1)),
            tail_block,
            tail_block,
            whole,
            any_spec,
            sums_block,
            any_spec,
        ],
        out_specs=[any_spec] * 4 + [sums_block],
        out_shape=[
            jax.ShapeDtypeStruct((2 * rows, length // 2, D), b16),
            jax.ShapeDtypeStruct((2 * rows, length // 2, D), b16),
            jax.ShapeDtypeStruct((3, HALF, D), b16),
            jax.ShapeDtypeStruct((CAP, HALF, D), b16),
            jax.ShapeDtypeStruct((16, D), f32),
        ],
        scratch_shapes=[
            pltpu.VMEM((tokens, D), f32),
            pltpu.VMEM((WIDE, D), f32),
            pltpu.VMEM((WIDE, LEN), b16),
            pltpu.VMEM((BACK_TAIL, LEN // 2, D), b16),
            pltpu.VMEM((REST, HALF, D), b16),
            pltpu.VMEM((FLOWS, REST, NEAR, D), b16),
            pltpu.VMEM((FLOWS, 3, REST, KEEP, D), b16),
            pltpu.VMEM((3, HALF, D), b16),
            pltpu.VMEM((PAIRS, HALF, WIDE), b16),
            pltpu.VMEM((FLOWS, PAIRS, NEAR, WIDE), b16),
            pltpu.VMEM((FLOWS, 3, PAIRS, KEEP, WIDE), b16),
            pltpu.VMEM((PAIRS, HALF, WIDE), b16),
            pltpu.VMEM((PAIRS, HALF, WIDE), b16),
            pltpu.VMEM((FLOWS, PAIRS, KEEP, WIDE), b16),
            pltpu.VMEM((FLOWS, PAIRS, NEAR, WIDE), b16),
            pltpu.VMEM((FLOWS, 2 * CAP, KEEP, D), b16),
            pltpu.VMEM((FLOWS, 2 * CAP, KEEP, D), b16),
            pltpu.VMEM((FLOWS, CAP, NEAR, D), b16),
            pltpu.VMEM((FLOWS, CAP, NEAR, D), b16),
            pltpu.VMEM((FLOWS, CAP, KEEP, D), b16),
            pltpu.VMEM((5, 16, D), f32),
            dma((3, FLOWS, 5)),
            dma((3, FLOWS, 5)),
            dma((3, FLOWS, 7)),
            dma((3, FLOWS, 7)),
            dma((FLOWS, 2)),
            dma((FLOWS, 2)),
            dma((FLOWS, 3)),
            dma((3,)),
            dma((3,)),
            dma((3,)),
            dma((3,)),
            dma((1,)),
            dma((PAIRS, 3)),
            dma((3,)),
            dma((3,)),
            dma((3,)),
            dma((5,)),
            dma((5,)),
        ],
        compiler_params=pltpu.CompilerParams(
            collective_id=1, has_side_effects=True, vmem_limit_bytes=62 * MIB
        ),
        name="back",
    )(table, *attention, weights, normed, x, residual, vectors, tiles, sums, y)


def update_kernel(tile_at, one, two, w_ref, m_ref, s_ref, y_in, i_in, w_out, m_out, s_out, y_out, i_out):
    step = pl.program_id(0)
    tile = tile_at[step // 4]
    grad = jnp.where(tile < 3, one[0], two[0]).astype(f32)
    parts = adam_step(w_ref[0], grad, m_ref[0], s_ref[0], RATE)
    for target, part in zip((w_out, m_out, s_out), parts):
        target[0] = jnp.where(tile >= 0, part, jnp.zeros_like(part))

    @pl.when(step < 8)
    def widen():
        y_out[...] = y_in[...].astype(f32)
        i_out[...] = i_in[...].astype(f32)


def update(tile_at, one, two, master, first, second, y, grad):
    tokens = y.shape[0]
    size = HALF // 4
    state = pl.BlockSpec((1, size, D), lambda s, tile_at: (s // 4, lax.rem(s, 4), 0))
    wide = pl.BlockSpec((tokens // 8, D), lambda s, tile_at: (jnp.minimum(s, 7), 0))
    return pl.pallas_call(
        update_kernel,
        grid_spec=pltpu.PrefetchScalarGridSpec(
            num_scalar_prefetch=1,
            grid=(CAP * 4,),
            in_specs=[
                pl.BlockSpec(
                    (1, size, D),
                    lambda s, tile_at: (jnp.clip(tile_at[s // 4], 0, 2), lax.rem(s, 4), 0),
                ),
                state,
                state,
                state,
                state,
                wide,
                wide,
            ],
            out_specs=[state] * 3 + [wide] * 2,
        ),
        out_shape=[jax.ShapeDtypeStruct(master.shape, f32)] * 3
        + [jax.ShapeDtypeStruct((tokens, D), f32)] * 2,
        compiler_params=pltpu.CompilerParams(vmem_limit_bytes=60 * MIB),
        name="update",
    )(tile_at, one, two, master, first, second, y, grad)


def shards_paired(
    inputs,
    cotangent,
    doc_lengths,
    owner_list,
    master,
    first_moment,
    second_moment,
    vectors,
    vector_first,
    vector_second,
):
    rows_here, span, width = inputs.shape
    place = lax.axis_index("blk")
    member = lax.axis_index("dp")
    rows_mine = rows_here // 2
    order = jnp.arange(PIECES)
    same_owner = owner_list[:, None] == owner_list[None, :]
    ranks = jnp.sum(same_owner & (order[None, :] < order[:, None]), axis=1).astype(jnp.int32)
    slot_of = owner_list * CAP + ranks
    front_outs = front(owner_list, doc_lengths, master, vectors, inputs, cotangent)
    x, cot, normed, weights_one, weights_two, queries, keys, values = front_outs[:8]
    weights, recips, context_turned, context = front_outs[8:]
    x = x.reshape(-1, width)
    cot = cot.reshape(-1, width)
    block_out, residual, grad_context, sums, tiles_two = feed(
        context, context_turned, x, cot, weights_two, vectors
    )
    hits = jnp.arange(16 * CAP)[:, None] == slot_of[None, :]
    tile_at = jnp.sum(jnp.where(hits, order[None, :] + 1, 0), axis=1).astype(jnp.int32) - 1
    table = jnp.maximum(tile_at - 3, 0)
    block_out, input_grad, total_one, total_two, vector_total = back(
        table,
        (weights, recips, values, queries, keys, context_turned, grad_context),
        weights_one,
        normed,
        x,
        residual,
        vectors,
        tiles_two,
        sums,
        block_out.reshape(rows_mine, LEN, width),
    )
    mine = lax.dynamic_slice_in_dim(tile_at, member * CAP, CAP, 0)
    *updated, block_out, input_grad = update(
        mine,
        total_one,
        total_two,
        master,
        first_moment,
        second_moment,
        block_out.reshape(-1, width),
        input_grad.reshape(-1, width),
    )
    columns = vector_first.shape[1]
    vector_cols = lax.dynamic_slice_in_dim(vectors, place * columns, columns, 1)
    vector_total = lax.dynamic_slice(vector_total, (0, place * columns), (PIECES, columns))
    updated_vectors = adam_step(vector_cols, vector_total, vector_first, vector_second, VEC_RATE)
    return (
        block_out.reshape(inputs.shape),
        input_grad.reshape(inputs.shape),
        *updated,
        *updated_vectors,
    )


def solution(mesh):
    in_specs = (
        P("dp", "blk", None),
        P("dp", "blk", None),
        P("dp", None),
        P(),
        P("dp", "blk", None),
        P("dp", "blk", None),
        P("dp", "blk", None),
        P(),
        P(None, "blk"),
        P(None, "blk"),
    )
    out_specs = (
        P("dp", "blk", None),
        P("dp", "blk", None),
        P("dp", "blk", None),
        P("dp", "blk", None),
        P("dp", "blk", None),
        P(None, "blk"),
        P(None, "blk"),
        P(None, "blk"),
    )
    paired = mesh.shape["blk"] == 2 and mesh.shape["dp"] == 16
    shards = shards_paired if paired else shards_any
    return jax.shard_map(shards, mesh=mesh, in_specs=in_specs, out_specs=out_specs, check_vma=False)
```

```python
from functools import partial

import jax
import jax.numpy as jnp
from jax import lax
from jax.experimental import pallas as pl
from jax.experimental.pallas import tpu as pltpu
from jax.sharding import PartitionSpec as P

D = 768
FF = 3072
HEADS = 12
HEAD_DIM = 64
LEN = 1024
CAP = 3
STEP = 10
PIECES = 12


EPS_NORM = 1e-05
BETA_ONE = 0.9
BETA_TWO = 0.999
RATE = 0.04
VEC_RATE = 0.25
DECAY = 0.01
ADAM_EPS = 1e-08


def normalize(values_in, gain, shift):
    center = jnp.mean(values_in, axis=-1, keepdims=True)
    offset = values_in - center
    spread = jnp.mean(offset * offset, axis=-1, keepdims=True)
    return offset * lax.rsqrt(spread + EPS_NORM) * gain + shift


def adam_step(weight, grad, first, second, rate):
    first_new = BETA_ONE * first + (1.0 - BETA_ONE) * grad
    second_new = BETA_TWO * second + (1.0 - BETA_TWO) * grad * grad
    corrected = (
        first_new
        / (1.0 - BETA_ONE**STEP)
        / (jnp.sqrt(second_new / (1.0 - BETA_TWO**STEP)) + ADAM_EPS)
    )
    return (weight - rate * (corrected + DECAY * weight), first_new, second_new)


def shards_any(
    inputs,
    cotangent,
    doc_lengths,
    owner_list,
    master,
    first_moment,
    second_moment,
    vectors,
    vector_first,
    vector_second,
):
    rows_here, span, width = inputs.shape
    tokens_here = rows_here * span
    fold = FF // D
    scale = HEAD_DIM ** (-0.5)
    place = lax.axis_index("blk")
    f32 = jnp.float32
    b16 = jnp.bfloat16
    order = jnp.arange(PIECES)
    same_owner = owner_list[:, None] == owner_list[None, :]
    ranks = jnp.sum(same_owner & (order[None, :] < order[:, None]), axis=1)
    slot_of = owner_list * CAP + ranks

    mine = (owner_list == lax.axis_index("dp"))[:, None, None]
    tile_rows = lax.psum(jnp.where(mine, master[ranks], 0.0).astype(b16), "dp")
    tiles = lax.all_gather(tile_rows, "blk", axis=1, tiled=True)
    query_weight = tiles[0]
    key_weight = tiles[1]
    value_weight = tiles[2]
    out_weight = tiles[3]
    up_weight = jnp.transpose(tiles[4 : 4 + fold], (1, 0, 2)).reshape(width, FF)
    down_weight = tiles[4 + fold :].reshape(FF, width)
    flat_in = inputs.reshape(tokens_here, width).astype(f32)
    normed_one = normalize(flat_in, vectors[0], vectors[1]).astype(b16)
    queries = (jnp.dot(normed_one, query_weight, preferred_element_type=f32) + vectors[4]).astype(
        b16
    )
    keys_here = jnp.dot(normed_one, key_weight, preferred_element_type=f32).astype(b16)
    values_here = (
        jnp.dot(normed_one, value_weight, preferred_element_type=f32) + vectors[5]
    ).astype(b16)
    query_heads = queries.reshape(rows_here, span, HEADS, HEAD_DIM)
    first_len = doc_lengths[:, 0]
    query_seg = (place * span + jnp.arange(span))[None, :] >= first_len[:, None]

    def block_scores(key_block, start):
        count = key_block.shape[1]
        key_heads = key_block.reshape(rows_here, count, HEADS, HEAD_DIM)
        raw = (
            jnp.einsum("rqhd,rkhd->rhqk", query_heads, key_heads, preferred_element_type=f32)
            * scale
        )
        key_seg = (start + jnp.arange(count))[None, :] >= first_len[:, None]
        allowed = query_seg[:, None, :, None] == key_seg[:, None, None, :]
        return (raw, allowed)

    key_rows = keys_here.reshape(rows_here, span, width)
    value_rows = values_here.reshape(rows_here, span, width)
    top = jnp.full((rows_here, HEADS, span), -1e30, f32)
    key_block = lax.all_gather(key_rows, "blk", axis=1, tiled=True)
    value_block = lax.all_gather(value_rows, "blk", axis=1, tiled=True)
    count = key_block.shape[1]
    raw, allowed = block_scores(key_block, jnp.int32(0))
    new_top = jnp.maximum(top, jnp.max(jnp.where(allowed, raw, -1e30), axis=-1))
    weights = jnp.where(allowed, jnp.exp(raw - new_top[..., None]), 0.0)
    value_heads = value_block.reshape(rows_here, count, HEADS, HEAD_DIM)
    update = jnp.einsum(
        "rhqk,rkhd->rhqd", weights.astype(b16), value_heads, preferred_element_type=f32
    )
    total = jnp.sum(weights, axis=-1)
    log_total = new_top + jnp.log(total)
    context_raw = update / total[..., None]
    context_low = jnp.transpose(context_raw, (0, 2, 1, 3)).reshape(tokens_here, width).astype(b16)
    residual = flat_in + (jnp.dot(context_low, out_weight, preferred_element_type=f32) + vectors[6])
    normed_two = normalize(residual, vectors[2], vectors[3]).astype(b16)
    hidden = jnp.dot(normed_two, up_weight, preferred_element_type=f32) + vectors[8:].reshape(FF)
    gelu_exact = partial(jax.nn.gelu, approximate=False)
    active, gelu_pull = jax.vjp(gelu_exact, hidden)
    active_low = active.astype(b16)
    block_out = (
        residual + (jnp.dot(active_low, down_weight, preferred_element_type=f32) + vectors[7])
    ).reshape(rows_here, span, width)
    grad_out = cotangent.reshape(tokens_here, width)
    down_grad = jnp.einsum("tf,td->fd", active_low, grad_out, preferred_element_type=f32)
    down_sum = jnp.sum(grad_out, axis=0, dtype=f32)
    grad_active = jnp.einsum("td,fd->tf", grad_out, down_weight, preferred_element_type=f32)
    grad_hidden = gelu_pull(grad_active)[0].astype(b16)
    up_grad = jnp.einsum("td,tf->df", normed_two, grad_hidden, preferred_element_type=f32)
    up_sum = jnp.sum(grad_hidden, axis=0, dtype=f32)
    ffn_tiles = jnp.concatenate(
        [
            jnp.transpose(up_grad.reshape(width, fold, width), (1, 0, 2)),
            down_grad.reshape(fold, width, width),
        ],
        axis=0,
    )
    grad_normed_two = jnp.einsum("tf,df->td", grad_hidden, up_weight, preferred_element_type=f32)
    unused, second_pull = jax.vjp(normalize, residual, vectors[2], vectors[3])
    residual_part, gain_two_grad, shift_two_grad = second_pull(grad_normed_two)
    grad_residual = grad_out.astype(f32) + residual_part
    grad_attended = grad_residual.astype(b16)
    out_grad = jnp.einsum("tm,td->md", context_low, grad_attended, preferred_element_type=f32)
    out_sum = jnp.sum(grad_attended, axis=0, dtype=f32)
    grad_context = jnp.einsum(
        "td,md->tm", grad_attended, out_weight, preferred_element_type=f32
    ).astype(b16)
    grad_heads = grad_context.reshape(rows_here, span, HEADS, HEAD_DIM)
    delta = jnp.einsum("rqhd,rhqd->rhq", grad_heads.astype(f32), context_raw)
    key_all, value_all = (
        lax.all_gather(key_rows, "blk", axis=1, tiled=True),
        lax.all_gather(value_rows, "blk", axis=1, tiled=True),
    )
    key_size = min(512, LEN)

    def back_block(index, carry):
        grad_query, key_total, value_total = carry
        start = index * key_size
        key_block = lax.dynamic_slice_in_dim(key_all, start, key_size, 1)
        value_block = lax.dynamic_slice_in_dim(value_all, start, key_size, 1)
        raw, allowed = block_scores(key_block, start)
        weights_back = jnp.where(allowed, jnp.exp(raw - log_total[..., None]), 0.0)
        key_heads = key_block.reshape(rows_here, key_size, HEADS, HEAD_DIM)
        value_heads = value_block.reshape(rows_here, key_size, HEADS, HEAD_DIM)
        value_grad = jnp.einsum(
            "rhqk,rqhd->rkhd", weights_back.astype(b16), grad_heads, preferred_element_type=f32
        )
        weight_grad = jnp.einsum(
            "rqhd,rkhd->rhqk", grad_heads, value_heads, preferred_element_type=f32
        )
        score_grad = (weights_back * (weight_grad - delta[..., None])).astype(b16)
        grad_query = (
            grad_query
            + jnp.einsum("rhqk,rkhd->rqhd", score_grad, key_heads, preferred_element_type=f32)
            * scale
        )
        key_grad = (
            jnp.einsum("rhqk,rqhd->rkhd", score_grad, query_heads, preferred_element_type=f32)
            * scale
        )
        key_total = lax.dynamic_update_slice_in_dim(
            key_total, key_grad.reshape(rows_here, key_size, width), start, 1
        )
        value_total = lax.dynamic_update_slice_in_dim(
            value_total, value_grad.reshape(rows_here, key_size, width), start, 1
        )
        return (grad_query, key_total, value_total)

    zero_rows = jnp.zeros((rows_here, LEN, width), f32)
    grad_query, key_total, value_total = lax.fori_loop(
        0,
        LEN // key_size,
        back_block,
        (jnp.zeros((rows_here, span, HEADS, HEAD_DIM), f32), zero_rows, zero_rows),
    )
    key_grad_here, value_grad_here = (
        lax.psum_scatter(
            key_total.astype(jnp.bfloat16), "blk", scatter_dimension=1, tiled=True
        ).astype(jnp.float32),
        lax.psum_scatter(
            value_total.astype(jnp.bfloat16), "blk", scatter_dimension=1, tiled=True
        ).astype(jnp.float32),
    )
    query_low = grad_query.reshape(tokens_here, width).astype(b16)
    key_low = key_grad_here.reshape(tokens_here, width).astype(b16)
    value_low = value_grad_here.reshape(tokens_here, width).astype(b16)
    query_tile = jnp.einsum("td,te->de", normed_one, query_low, preferred_element_type=f32)
    key_tile = jnp.einsum("td,te->de", normed_one, key_low, preferred_element_type=f32)
    value_tile = jnp.einsum("td,te->de", normed_one, value_low, preferred_element_type=f32)
    grad_normed_one = (
        jnp.einsum("te,de->td", query_low, query_weight, preferred_element_type=f32)
        + jnp.einsum("te,de->td", key_low, key_weight, preferred_element_type=f32)
        + jnp.einsum("te,de->td", value_low, value_weight, preferred_element_type=f32)
    )
    unused, first_pull = jax.vjp(normalize, flat_in, vectors[0], vectors[1])
    input_part, gain_one_grad, shift_one_grad = first_pull(grad_normed_one)
    input_grad = (grad_residual + input_part).reshape(rows_here, span, width)
    vector_grads = jnp.concatenate(
        [
            jnp.stack(
                [
                    gain_one_grad,
                    shift_one_grad,
                    gain_two_grad,
                    shift_two_grad,
                    jnp.sum(query_low, axis=0, dtype=f32),
                    jnp.sum(value_low, axis=0, dtype=f32),
                    out_sum,
                    down_sum,
                ]
            ),
            up_sum.reshape(fold, width),
        ],
        axis=0,
    )
    attn_tiles = jnp.stack([query_tile, key_tile, value_tile, out_grad])
    piece_share, vector_share = (
        lax.psum_scatter(
            jnp.concatenate([attn_tiles, ffn_tiles], axis=0).astype(jnp.bfloat16),
            "blk",
            scatter_dimension=1,
            tiled=True,
        ).astype(jnp.float32),
        lax.psum_scatter(
            vector_grads.astype(jnp.bfloat16), "blk", scatter_dimension=1, tiled=True
        ).astype(jnp.float32),
    )
    own_slots = lax.axis_index("dp") * CAP + jnp.arange(CAP)
    pick = (own_slots[:, None] == slot_of[None, :]).astype(f32)
    occupied = jnp.sum(pick, axis=1)[:, None, None]
    total_share, vector_total = (
        lax.psum(piece_share.astype(jnp.bfloat16), "dp").astype(jnp.float32),
        lax.psum(vector_share.astype(jnp.bfloat16), "dp").astype(jnp.float32),
    )
    slot_grads = jnp.einsum("cp,prd->crd", pick, total_share, precision=lax.Precision.HIGHEST)
    new_master, new_first, new_second = adam_step(
        master, slot_grads, first_moment, second_moment, RATE
    )
    columns = vector_first.shape[1]
    vector_cols = lax.dynamic_slice_in_dim(vectors, place * columns, columns, 1)
    new_vectors, new_vector_first, new_vector_second = adam_step(
        vector_cols, vector_total, vector_first, vector_second, VEC_RATE
    )
    return (
        block_out,
        input_grad,
        new_master * occupied,
        new_first * occupied,
        new_second * occupied,
        new_vectors,
        new_vector_first,
        new_vector_second,
    )


f32 = jnp.float32
b16 = jnp.bfloat16
LOG2E = 1.4426950408889634
MIB = 1024 * 1024
PAIRS = HEADS // 2
PAIR = 2 * HEAD_DIM


def dot_nn(left, right):
    return lax.dot_general(left, right, (((1,), (0,)), ((), ())), preferred_element_type=f32)


def dot_nt(left, right):
    return lax.dot_general(left, right, (((1,), (1,)), ((), ())), preferred_element_type=f32)


def dot_tn(left, right):
    return lax.dot_general(left, right, (((0,), (0,)), ((), ())), preferred_element_type=f32)


def norm_parts(values_in):
    center = jnp.mean(values_in, axis=-1, keepdims=True)
    offset = values_in - center
    spread = jnp.mean(offset * offset, axis=-1, keepdims=True)
    rstd = lax.rsqrt(spread + EPS_NORM)
    return offset * rstd, rstd


def norm_back(grad, unit, rstd, gain):
    scaled = grad * gain
    first = jnp.mean(scaled, axis=-1, keepdims=True)
    second = jnp.mean(scaled * unit, axis=-1, keepdims=True)
    return rstd * (scaled - first - unit * second)


def gelu_parts(value):
    bell = jnp.exp2(value * value * (-0.5 * LOG2E))
    ratio = pl.reciprocal(1.0 + (0.3275911 * 0.7071067811865476) * jnp.abs(value))
    poly = 0.5 * 1.061405429
    poly = poly * ratio + 0.5 * -1.453152027
    poly = poly * ratio + 0.5 * 1.421413741
    poly = poly * ratio + 0.5 * -0.284496736
    poly = poly * ratio + 0.5 * 0.254829592
    tail = poly * ratio * bell
    cdf = jnp.where(value >= 0.0, 1.0 - tail, tail)
    return value * cdf, cdf + value * (bell * 0.3989422804014327)


def head_only(block, head):
    lane = lax.broadcasted_iota(jnp.int32, block.shape, 1)
    keep = (lane >= head * HEAD_DIM) & (lane < (head + 1) * HEAD_DIM)
    return jnp.where(keep, block, jnp.zeros_like(block))


def feed_kernel(
    c_ref, o_ref, x_ref, g_ref, w_ref, vec_ref,
    y_ref, r_ref, d_ref, sums_ref, tiles_ref,
    acc_ref, stage_ref, sem_ref,
):
    fold = FF // D
    step = pl.program_id(0)

    @pl.when(step == 0)
    def clear():
        acc_ref[...] = jnp.zeros_like(acc_ref)
        sums_ref[...] = jnp.zeros_like(sums_ref)

    residual = x_ref[...].astype(f32) + (dot_nn(c_ref[...], w_ref[0]) + vec_ref[6:7, :])
    unit, rstd = norm_parts(residual)
    gain = vec_ref[2:3, :]
    normed = (unit * gain + vec_ref[3:4, :]).astype(b16)
    turned = normed.T
    cot = g_ref[...]
    out = residual + vec_ref[7:8, :]
    grad = jnp.zeros_like(out)

    def begin(part):
        hidden = dot_nn(normed, w_ref[1 + part])
        return hidden, dot_nt(cot, w_ref[1 + fold + part])

    for part in range(fold):
        hidden, pulled = begin(part)
        active, slope = gelu_parts(hidden + vec_ref[8 + part : 9 + part, :])
        active = active.astype(b16)
        pulled = (pulled * slope).astype(b16)
        out = out + dot_nn(active, w_ref[1 + fold + part])
        grad = grad + dot_nt(pulled, w_ref[1 + part])
        acc_ref[1 + part] += dot_nn(turned, pulled)
        acc_ref[1 + fold + part] += dot_tn(active, cot)
        sums_ref[8 + part : 9 + part, :] += jnp.sum(pulled.astype(f32), 0, keepdims=True)
    y_ref[...] = out.astype(b16)
    wide = cot.astype(f32)
    sums_ref[2:3, :] += jnp.sum(grad * unit, 0, keepdims=True)
    sums_ref[3:4, :] += jnp.sum(grad, 0, keepdims=True)
    sums_ref[7:8, :] += jnp.sum(wide, 0, keepdims=True)
    back = wide + norm_back(grad, unit, rstd, gain)
    r_ref[...] = back.astype(b16)
    low = back.astype(b16)
    sums_ref[6:7, :] += jnp.sum(low.astype(f32), 0, keepdims=True)
    d_ref[...] = dot_nt(w_ref[0], low).astype(b16)
    acc_ref[0] += dot_nn(o_ref[...], low)

    @pl.when(step == pl.num_programs(0) - 1)
    def send():
        count = 1 + 2 * fold
        copies = []
        for part in range(count):
            if part >= 2:
                copies[part - 2].wait()
            stage_ref[part % 2] = acc_ref[part].astype(b16)
            copy = pltpu.make_async_copy(stage_ref.at[part % 2], tiles_ref.at[part], sem_ref.at[part % 2])
            copy.start()
            copies.append(copy)
        copies[count - 2].wait()
        copies[count - 1].wait()


def feed(context, turned, x, cot, weights, vectors):
    tokens = x.shape[0]
    size = 256
    count = 1 + 2 * (FF // D)
    token_block = pl.BlockSpec((size, D), lambda i: (i, 0))
    turned_block = pl.BlockSpec((D, size), lambda i: (0, i))
    return pl.pallas_call(
        feed_kernel,
        grid=(tokens // size,),
        in_specs=[
            token_block,
            turned_block,
            token_block,
            token_block,
            pl.BlockSpec((count, D, D), lambda i: (0, 0, 0), pipeline_mode=pl.Buffered(1)),
            pl.BlockSpec((PIECES, D), lambda i: (0, 0)),
        ],
        out_specs=[
            token_block,
            token_block,
            turned_block,
            pl.BlockSpec((16, D), lambda i: (0, 0)),
            pl.BlockSpec(memory_space=pl.ANY),
        ],
        out_shape=[
            jax.ShapeDtypeStruct((tokens, D), b16),
            jax.ShapeDtypeStruct((tokens, D), b16),
            jax.ShapeDtypeStruct((D, tokens), b16),
            jax.ShapeDtypeStruct((16, D), f32),
            jax.ShapeDtypeStruct((count, D, D), b16),
        ],
        scratch_shapes=[
            pltpu.VMEM((count, D, D), f32),
            pltpu.VMEM((2, D, D), b16),
            pltpu.SemaphoreType.DMA((2,)),
        ],
        compiler_params=pltpu.CompilerParams(vmem_limit_bytes=60 * MIB),
        cost_estimate=pl.CostEstimate(
            flops=6 * count * tokens * D * D,
            bytes_accessed=18 * tokens * D + 4 * count * D * D,
            transcendentals=2 * tokens * FF,
        ),
        name="feed",
    )(context, turned, x, cot, weights, vectors)


MESH = pl.DeviceIdType.MESH
HALF = D // 2
FLOWS = 2
FLOW = HALF // FLOWS
NEAR = FLOW // 2
KEEP = NEAR // 2
WIDE = 3 * PAIR
REST = PIECES - 3
GROUPS = ((0, 1), (1, 2), (3, 3))
CHUNKS = len(GROUPS)


class Place:
    def __init__(self):
        self.me = lax.axis_index("dp")
        self.core = lax.axis_index("blk")
        self.bits = [lax.rem(self.me // weight, 2) for weight in (1, 2, 4, 8)]
        self.chips = [
            self.me + weight - 2 * weight * bit for weight, bit in zip((1, 2, 4, 8), self.bits)
        ]
        self.partners = [{"dp": chip} for chip in self.chips]
        low, high = self.bits[2:]
        self.inner = low != high
        self.across = {"dp": self.me + 4 - 8 * low + 8 - 16 * high}
        self.other = 1 - self.core
        self.twin = {"blk": self.other}

    def greet(self):
        barrier = pltpu.get_barrier_semaphore()
        for device in self.partners + [self.across, self.twin]:
            pl.semaphore_signal(barrier, 1, device_id=device, device_id_type=MESH)
        pl.semaphore_wait(barrier, 6)

    def flow(self, index):
        first, second = (0, 1) if index == 0 else (1, 0)
        base = index * FLOW
        near = base + self.bits[first] * NEAR
        far = base + NEAR - self.bits[first] * NEAR
        keep = near + self.bits[second] * KEEP
        give = near + KEEP - self.bits[second] * KEEP
        return first, second, near, far, keep, give


def remote(source, target, send, receive, device):
    return pltpu.make_async_remote_copy(
        src_ref=source,
        dst_ref=target,
        send_sem=send,
        recv_sem=receive,
        device_id=device,
        device_id_type=MESH,
    )


def rows_at(start, count):
    return pl.ds(pl.multiple_of(start, 16), count)


class Spread:
    def __init__(self, place, owner, rank, slots, land, gift, sems):
        self.place, self.owner, self.rank = place, owner, rank
        self.slots, self.land, self.gift, self.sems = slots, land, gift, sems

    def cols(self, chunk):
        return pl.ds(GROUPS[chunk][0] * PAIR, GROUPS[chunk][1] * PAIR)

    def first_copy(self, chunk, index):
        first, second, near, far, keep, give = self.place.flow(index)
        return remote(
            self.slots.at[:, rows_at(far, NEAR), self.cols(chunk)],
            self.land[chunk].at[index],
            self.sems[0].at[chunk, index, 0],
            self.sems[1].at[chunk, index, 0],
            self.place.partners[first],
        )

    def second_copy(self, chunk, index, which):
        first, second, near, far, keep, give = self.place.flow(index)
        if which == 0:
            source = self.slots.at[:, rows_at(give, KEEP), self.cols(chunk)]
        else:
            source = self.land[chunk].at[index, :, rows_at(give - near, KEEP)]
        return remote(
            source,
            self.gift[chunk].at[index, pl.ds(which * CAP, CAP)],
            self.sems[0].at[chunk, index, 1 + which],
            self.sems[1].at[chunk, index, 1 + which],
            self.place.partners[second],
        )

    def step(self, chunk, index):
        for flow in range(FLOWS):
            if index == 0:
                self.first_copy(chunk, flow).start()
                self.second_copy(chunk, flow, 0).start()
            if index == 1:
                self.first_copy(chunk, flow).wait()
                self.second_copy(chunk, flow, 1).start()
            if index == 2:
                self.second_copy(chunk, flow, 0).wait()
                self.second_copy(chunk, flow, 1).wait()

    def piece(self, tile, index, chunk, start, count):
        first, second, near, far, keep, give = self.place.flow(index)
        owner, rank = self.owner[tile], self.rank[tile]
        bits = [lax.rem(owner, 2), lax.rem(owner // 2, 2)]
        apart = [bit != mine for bit, mine in zip(bits, self.place.bits)]
        cols = pl.ds(start, count)
        mine = self.slots[rank, rows_at(keep, KEEP), pl.ds(GROUPS[chunk][0] * PAIR + start, count)]
        firsts = self.land[chunk][index, rank, rows_at(keep - near, KEEP), cols]
        gifts = self.gift[chunk][index, jnp.where(apart[first], CAP, 0) + rank, :, cols]
        value = jnp.where(apart[second], gifts, jnp.where(apart[first], firsts, mine))
        layer = owner // 4 == self.place.me // 4
        return jnp.where(layer, value, jnp.zeros_like(value))


class Column:
    steps = 4

    def __init__(self, place, kept, read, write, land, sems):
        self.place, self.kept, self.read, self.write = place, kept, read, write
        self.land, self.sems = land, sems

    def copy(self, index):
        target = self.land.at[index % 2]
        device = self.place.across if index == 1 else self.place.partners[2]
        return remote(
            self.kept, target, self.sems[0].at[index], self.sems[1].at[index], device
        )

    def add(self, index):
        self.write((self.read().astype(f32) + self.land[index].astype(f32)).astype(b16))


def column_step(place, columns, index):
    @pl.when(place.inner)
    def inner():
        for column in columns:
            if index == 1:
                column.copy(0).wait_recv()
                column.add(0)
                column.copy(1).start()
            if index == 2:
                column.copy(1).wait()
                column.add(1)
                column.copy(2).start()
            if index == 3:
                column.copy(2).wait_send()

    @pl.when(jnp.logical_not(place.inner))
    def outer():
        for column in columns:
            if index == 0:
                column.copy(0).start()
            if index == 1:
                column.copy(0).wait_send()
            if index == 3:
                column.copy(2).wait_recv()
                column.write(column.land[0])


class Item:
    steps = 7

    def __init__(self, place, work, land, sems, load, store=None):
        self.place, self.work, self.land, self.sems = place, work, land, sems
        self.load, self.store = load, store
        self.base = place.core * HALF

    def column(self, flow):
        rows = rows_at(self.base + self.place.flow(flow)[4], KEEP)

        def read():
            return self.work[:, rows]

        def write(value):
            self.work[:, rows] = value

        sems = (self.sems[0].at[flow], self.sems[1].at[flow])
        return Column(self.place, self.work.at[:, rows], read, write, self.land.at[flow], sems)

    def copy(self, flow, index):
        first, second, near, far, keep, give = self.place.flow(flow)
        kept = self.work.at[:, rows_at(self.base + keep, KEEP)]
        half = self.work.at[:, rows_at(self.base + near, NEAR)]
        source, device = [
            (kept, self.place.partners[second]),
            (half, self.place.partners[first]),
        ][index]
        return remote(
            source, source, self.sems[0].at[flow, 3 + index], self.sems[1].at[flow, 3 + index], device
        )

    def pair(self):
        rows = self.work.at[:, rows_at(self.base, HALF)]
        return remote(rows, rows, self.sems[0].at[0, 5], self.sems[1].at[0, 5], self.place.twin)

    def step(self, index):
        for flow in range(FLOWS):
            if index == 0:
                self.load(self.work, rows_at(self.base + self.place.flow(flow)[4], KEEP), flow)
        if index <= 3:
            column_step(self.place, [self.column(flow) for flow in range(FLOWS)], index)
        for flow in range(FLOWS):
            if 4 <= index <= 5:
                self.copy(flow, index - 4).wait()
            if 3 <= index <= 4:
                self.copy(flow, index - 3).start()
        if index == 5:
            self.pair().start()
        if index == 6:
            self.pair().wait()
            self.store().start()


REST_GROUPS = tuple((index, 1) for index in range(REST))
PAIR_CHUNK = (0, 1, 1, 2, 2, 2)
FRONT_PAIRS = (2, 3, 4, 5, 6, 7)
FRONT_REST = (6, 7, 8, 9, 10, 11, 12, 13, 14)
FRONT_LEAD = 9


def front_kernel(
    owner, lengths, master, vec_ref, x_in, c_in,
    x_out, c_out, n_out, one_out, two_out, q_ref, k_ref, v_ref, p_ref, r_ref, o_ref, ctx_ref,
    rank, rows_ref, normed, keys, turned_values, slots,
    land_one, land_two, land_three, gift_one, gift_two, gift_three,
    one, one_land, two, two_land,
    spread_send, spread_recv, one_send, one_recv, two_send, two_recv,
    swap_send, swap_recv, swap_local, store_sem,
):
    pair = pl.program_id(0)
    row = pl.program_id(1)
    grid_step = pair * 2 + row
    place = Place()
    rows, span = x_in.shape[0] // 2, x_in.shape[1]
    land = (land_one, land_two, land_three)
    gift = (gift_one, gift_two, gift_three)
    spread = Spread(place, owner, rank, slots, land, gift, (spread_send, spread_recv))

    def swaps(index):
        source, target = [(x_in, rows_ref), (c_in, c_out)][index]
        here = pl.ds(place.core * span, span)
        near = pltpu.make_async_copy(
            source.at[pl.ds(place.core * rows, rows)], target.at[:, here], swap_local.at[index]
        )
        far = remote(
            source.at[pl.ds(place.other * rows, rows)],
            target.at[:, here],
            swap_send.at[index],
            swap_recv.at[index],
            place.twin,
        )
        return near, far

    def row_store():
        return pltpu.make_async_copy(rows_ref, x_out, store_sem.at[PAIRS + REST])

    def normed_store():
        return pltpu.make_async_copy(normed, n_out, store_sem.at[PAIRS + REST + 1])

    def pair_item(group):
        span_of = pl.ds(group, 1)

        def load(work, where, flow):
            chunk = PAIR_CHUNK[group]
            for tile in range(3):
                part = spread.piece(tile, flow, chunk, (group - GROUPS[chunk][0]) * PAIR, PAIR)
                work[0, where, pl.ds(tile * PAIR, PAIR)] = part

        def store():
            return pltpu.make_async_copy(one.at[span_of], one_out.at[span_of], store_sem.at[group])

        sems = (one_send.at[group], one_recv.at[group])
        return Item(place, one.at[span_of], one_land.at[:, :, span_of], sems, load, store)

    def rest_item(group):
        first, count = REST_GROUPS[group]
        span_of = pl.ds(first, count)

        def load(work, where, flow):
            for index in range(count):
                for chunk, (start, wide) in enumerate(GROUPS):
                    part = spread.piece(3 + first + index, flow, chunk, 0, wide * PAIR)
                    work[index, where, pl.ds(start * PAIR, wide * PAIR)] = part

        def store():
            return pltpu.make_async_copy(
                two.at[span_of], two_out.at[span_of], store_sem.at[PAIRS + group]
            )

        sems = (two_send.at[group], two_recv.at[group])
        return Item(place, two.at[span_of], two_land.at[:, :, span_of], sems, load, store)

    def tick(number):
        for chunk in range(CHUNKS):
            if 0 <= number - chunk <= 2:
                spread.step(chunk, number - chunk)
        starts = [(pair_item, group, start) for group, start in enumerate(FRONT_PAIRS)]
        starts += [(rest_item, group, start) for group, start in enumerate(FRONT_REST)]
        for make, group, start in starts:
            if 0 <= number - start < Item.steps:
                make(group).step(number - start)

    @pl.when(grid_step == 0)
    def lead():
        slots[...] = master[...].astype(b16)
        for tile in range(PIECES):
            count = jnp.int32(0)
            for before in range(tile):
                count = count + (owner[before] == owner[tile]).astype(jnp.int32)
            rank[tile] = jnp.minimum(count, CAP - 1)
        place.greet()
        for copy in swaps(0):
            copy.start()
        tick(0)
        for copy in swaps(1):
            copy.start()
        for copy in swaps(0):
            copy.wait()
        row_store().start()

        def norm_rows(index, carry):
            where = pl.ds(index * 256, 256)
            for part in range(rows):
                unit, unused = norm_parts(rows_ref[part, where].astype(f32))
                low = (unit * vec_ref[0:1, :] + vec_ref[1:2, :]).astype(b16)
                normed[pl.ds(part * LEN + index * 256, 256)] = low
            return carry

        tick(1)
        lax.fori_loop(0, LEN // 256, norm_rows, 0)
        normed_store().start()
        for number in range(2, FRONT_LEAD):
            tick(number)

    for number in range(2 * PAIRS):
        pl.when(grid_step == number)(partial(tick, FRONT_LEAD + number))

    @pl.when(row == 0)
    def project():
        lanes = pl.ds(pl.multiple_of(pair * PAIR, PAIR), PAIR)
        weight = one[pair]

        def part(index, carry):
            where = pl.ds(pl.multiple_of(index * 512, 512), 512)
            both = dot_nn(normed[where], weight)
            queries = both[:, :PAIR] + vec_ref[4:5, lanes]
            queries = (queries * (HEAD_DIM**-0.5 * LOG2E)).astype(b16)
            q_ref[:, where] = queries.T
            low = both[:, PAIR : 2 * PAIR].astype(b16)
            keys[where] = low
            k_ref[:, where] = low.T
            values = (both[:, 2 * PAIR :] + vec_ref[5:6, lanes]).astype(b16)
            v_ref[where] = values
            turned_values[:, where] = values.T
            return carry

        lax.fori_loop(0, normed.shape[0] // 512, part, 0)

    half = LEN // 2
    start = pl.multiple_of(row * LEN, LEN)
    split = lengths[place.core * rows + row, 0] < LEN
    shift = jnp.where(split, jnp.float32(-1e30), jnp.float32(0.0))

    def scores(head, step):
        cols = pl.ds(pl.multiple_of(start + step * half, half), half)
        others = pl.ds(pl.multiple_of(start + (1 - step) * half, half), half)
        queries = q_ref[:, cols]
        near = dot_nn(head_only(keys[cols], head), queries)
        far = dot_nn(head_only(keys[others], head), queries) + shift
        return near, far

    for head, step in [(head, step) for head in range(2) for step in range(2)]:
        near, far = scores(head, step)
        part = slice(head * HEAD_DIM, (head + 1) * HEAD_DIM)
        top = jnp.maximum(jnp.max(near, 0, keepdims=True), jnp.max(far, 0, keepdims=True))
        near = jnp.exp2(near - top)
        far = jnp.exp2(far - top)
        total = jnp.sum(near, 0, keepdims=True) + jnp.sum(far, 0, keepdims=True)
        recip = 1.0 / total
        here = slice(step * half, (step + 1) * half)
        there = slice((1 - step) * half, (2 - step) * half)
        near, far = near.astype(b16), far.astype(b16)
        p_ref[head, here, here] = near
        p_ref[head, there, here] = far
        r_ref[0, head : head + 1, here] = recip
        cols = pl.ds(pl.multiple_of(start + step * half, half), half)
        others = pl.ds(pl.multiple_of(start + (1 - step) * half, half), half)
        out = dot_nn(turned_values[part, cols], near) + dot_nn(turned_values[part, others], far)
        o_ref[part, here] = (out * recip).astype(b16)
    ctx_ref[...] = o_ref[...].T

    @pl.when(grid_step == 2 * PAIRS - 1)
    def finish_copies():
        for copy in swaps(1):
            copy.wait()
        row_store().wait()
        normed_store().wait()
        for group in range(PAIRS):
            pair_item(group).store().wait()
        for group in range(REST):
            rest_item(group).store().wait()


def front(owner, lengths, master, vectors, inputs, cotangent):
    rows, span = inputs.shape[0] // 2, inputs.shape[1]
    tokens = rows * LEN
    any_spec = pl.BlockSpec(memory_space=pl.ANY)
    smem = pl.BlockSpec(memory_space=pltpu.SMEM)
    whole = jax.ShapeDtypeStruct((rows, LEN, D), b16)
    dma = pltpu.SemaphoreType.DMA
    return pl.pallas_call(
        front_kernel,
        grid=(PAIRS, rows),
        in_specs=[
            smem,
            smem,
            pl.BlockSpec((CAP, HALF, D), lambda h, r: (0, 0, 0), pipeline_mode=pl.Buffered(1)),
            pl.BlockSpec((PIECES, D), lambda h, r: (0, 0)),
            any_spec,
            any_spec,
        ],
        out_specs=[any_spec] * 5
        + [
            pl.BlockSpec((PAIR, tokens), lambda h, r: (h, 0)),
            pl.BlockSpec((PAIR, tokens), lambda h, r: (h, 0)),
            pl.BlockSpec((tokens, PAIR), lambda h, r: (0, h)),
            pl.BlockSpec((2, LEN, LEN), lambda h, r: (h * 2 + r, 0, 0)),
            pl.BlockSpec((1, 2, LEN), lambda h, r: (h * 2 + r, 0, 0)),
            pl.BlockSpec((PAIR, LEN), lambda h, r: (h, r)),
            pl.BlockSpec((LEN, PAIR), lambda h, r: (r, h)),
        ],
        out_shape=[
            whole,
            whole,
            jax.ShapeDtypeStruct((tokens, D), b16),
            jax.ShapeDtypeStruct((PAIRS, D, WIDE), b16),
            jax.ShapeDtypeStruct((REST, D, D), b16),
            jax.ShapeDtypeStruct((D, tokens), b16),
            jax.ShapeDtypeStruct((D, tokens), b16),
            jax.ShapeDtypeStruct((tokens, D), b16),
            jax.ShapeDtypeStruct((rows * HEADS, LEN, LEN), b16),
            jax.ShapeDtypeStruct((rows * PAIRS, 2, LEN), f32),
            jax.ShapeDtypeStruct((D, tokens), b16),
            jax.ShapeDtypeStruct((tokens, D), b16),
        ],
        scratch_shapes=[
            pltpu.SMEM((PIECES,), jnp.int32),
            pltpu.VMEM((rows, LEN, D), b16),
            pltpu.VMEM((tokens, D), b16),
            pltpu.VMEM((tokens, PAIR), b16),
            pltpu.VMEM((PAIR, tokens), b16),
            pltpu.VMEM((CAP, HALF, D), b16),
        ]
        + [pltpu.VMEM((FLOWS, CAP, NEAR, wide * PAIR), b16) for unused, wide in GROUPS]
        + [pltpu.VMEM((FLOWS, 2 * CAP, KEEP, wide * PAIR), b16) for unused, wide in GROUPS]
        + [
            pltpu.VMEM((PAIRS, D, WIDE), b16),
            pltpu.VMEM((FLOWS, 2, PAIRS, KEEP, WIDE), b16),
            pltpu.VMEM((REST, D, D), b16),
            pltpu.VMEM((FLOWS, 2, REST, KEEP, D), b16),
            dma((CHUNKS, FLOWS, 3)),
            dma((CHUNKS, FLOWS, 3)),
            dma((PAIRS, FLOWS, 6)),
            dma((PAIRS, FLOWS, 6)),
            dma((REST, FLOWS, 6)),
            dma((REST, FLOWS, 6)),
            dma((2,)),
            dma((2,)),
            dma((2,)),
            dma((PAIRS + REST + 2,)),
        ],
        compiler_params=pltpu.CompilerParams(
            collective_id=0, has_side_effects=True, vmem_limit_bytes=60 * MIB
        ),
        name="front",
    )(owner, lengths, master, vectors, inputs, cotangent)


class Sum:
    steps = 7

    def __init__(self, place, work, wide, narrow, sems, send_pair, add_own):
        self.place, self.work, self.wide, self.narrow, self.sems = place, work, wide, narrow, sems
        self.send_pair, self.add_own = send_pair, add_own

    def column(self, flow):
        rows = rows_at(self.place.flow(flow)[4], KEEP)

        def read():
            return self.work[:, rows]

        def write(value):
            self.work[:, rows] = value

        sems = (self.sems[0].at[flow, pl.ds(2, 3)], self.sems[1].at[flow, pl.ds(2, 3)])
        land = self.narrow.at[flow, pl.ds(1, 2)]
        return Column(self.place, self.work.at[:, rows], read, write, land, sems)

    def copy(self, flow, index):
        first, second, near, far, keep, give = self.place.flow(flow)
        source, target, device = [
            (self.work.at[:, rows_at(far, NEAR)], self.wide.at[flow], first),
            (self.work.at[:, rows_at(give, KEEP)], self.narrow.at[flow, 0], second),
        ][index]
        return remote(
            source,
            target,
            self.sems[0].at[flow, index],
            self.sems[1].at[flow, index],
            self.place.partners[device],
        )

    def add(self, rows, value):
        self.work[:, rows] = (self.work[:, rows].astype(f32) + value.astype(f32)).astype(b16)

    def step(self, index):
        if index == 0:
            self.send_pair().start()
        if index == 1:
            self.send_pair().wait()
            self.add_own()
        for flow in range(FLOWS):
            first, second, near, far, keep, give = self.place.flow(flow)
            if index == 1:
                self.copy(flow, 0).start()
            if index == 2:
                self.copy(flow, 0).wait()
                self.add(rows_at(near, NEAR), self.wide[flow])
                self.copy(flow, 1).start()
            if index == 3:
                self.copy(flow, 1).wait()
                self.add(rows_at(keep, KEEP), self.narrow[flow, 0])
        if index >= 3:
            columns = [self.column(flow) for flow in range(FLOWS)]
            column_step(self.place, columns, index - 3)


class Gather:
    steps = 3

    def __init__(self, place, work, narrow, wide, sems):
        self.place, self.work, self.narrow, self.wide = place, work, narrow, wide
        self.sems = sems

    def copy(self, flow, index):
        first, second, near, far, keep, give = self.place.flow(flow)
        rows, target, device = [
            (rows_at(keep, KEEP), self.narrow, second),
            (rows_at(near, NEAR), self.wide, first),
        ][index]
        return remote(
            self.work.at[:, rows],
            target.at[flow],
            self.sems[0].at[flow, 5 + index],
            self.sems[1].at[flow, 5 + index],
            self.place.partners[device],
        )

    def step(self, index):
        for flow in range(FLOWS):
            first, second, near, far, keep, give = self.place.flow(flow)
            if index > 0:
                self.copy(flow, index - 1).wait()
            if index == 1:
                self.work[:, rows_at(give, KEEP)] = self.narrow[flow]
            if index == 2:
                self.work[:, rows_at(far, NEAR)] = self.wide[flow]
            if index < 2:
                self.copy(flow, index).start()


class Hand:
    steps = 3

    def __init__(self, place, table, work, bag, gift, pack, last, own, out, sems, store_sems):
        self.place, self.table, self.work = place, table, work
        self.bag, self.gift, self.pack, self.last, self.own = bag, gift, pack, last, own
        self.out, self.sems, self.store_sems = out, sems, store_sems

    def tile(self, chip, rank, rows):
        return self.work[self.table[chip * CAP + rank], rows]

    def copy(self, flow, index):
        first, second = self.place.flow(flow)[:2]
        source, target, device = [
            (self.bag.at[flow], self.gift.at[flow], second),
            (self.pack.at[flow], self.last.at[flow], first),
        ][index]
        return remote(
            source,
            target,
            self.sems[0].at[flow, index],
            self.sems[1].at[flow, index],
            self.place.partners[device],
        )

    def stores(self, flow):
        first, second, near, far, keep, give = self.place.flow(flow)
        parts = [
            (self.own.at[flow], rows_at(keep, KEEP)),
            (self.gift.at[flow, pl.ds(0, CAP)], rows_at(give, KEEP)),
            (self.last.at[flow], rows_at(far, NEAR)),
        ]
        return [
            pltpu.make_async_copy(source, self.out.at[:, rows], self.store_sems.at[flow, index])
            for index, (source, rows) in enumerate(parts)
        ]

    def step(self, index):
        for flow in range(FLOWS):
            first, second, near, far, keep, give = self.place.flow(flow)
            rows = rows_at(keep, KEEP)
            if index == 0:
                beside = self.place.chips[second]
                across = beside + self.place.chips[first] - self.place.me
                for rank in range(CAP):
                    self.bag[flow, rank] = self.tile(beside, rank, rows)
                    self.bag[flow, CAP + rank] = self.tile(across, rank, rows)
                    self.own[flow, rank] = self.tile(self.place.me, rank, rows)
                self.copy(flow, 0).start()
            if index == 1:
                self.copy(flow, 0).wait()
                for rank in range(CAP):
                    mine = self.tile(self.place.chips[first], rank, rows)
                    self.pack[flow, rank, rows_at(keep - near, KEEP)] = mine
                    self.pack[flow, rank, rows_at(give - near, KEEP)] = self.gift[flow, CAP + rank]
                self.copy(flow, 1).start()
            if index == 2:
                self.copy(flow, 1).wait()
                for copy in self.stores(flow):
                    copy.start()


BACK_STEPS = 2 * PAIRS
BACK_TAIL = 4
BACK_PAIRS = tuple((index, 1) for index in range(PAIRS))
BACK_REST = (0, 0, 1, 2, 2, 3, 4, 4, 5)
BACK_HAND = 12


def back_kernel(
    table, p_ref, r_ref, v_ref, q_ref, k_ref, o_ref, g_ref, w_ref, n_ref, x_ref, z_ref, vec_ref,
    tiles_in, sums_in, y_in,
    y_out, i_out, pairs_out, slots_out, sums_ref,
    grad_sum, wide_sum, turned, block_out,
    two, two_wide, two_narrow, two_stage, one, one_wide, one_narrow, one_send_stage, one_stage,
    gather_narrow, gather_wide,
    bag, gift, pack, last, own, vec_land,
    two_send, two_recv, one_send, one_recv, hand_send, hand_recv, hand_store,
    pair_two_send, pair_two_recv, pair_one_send, pair_one_recv, load_sem, store_sem,
    swap_send, swap_recv, swap_local, vec_send, vec_recv,
):
    step = pl.program_id(0)
    place = Place()
    rows, span = y_in.shape[0], y_in.shape[1] // 2
    near_half = rows_at(place.core * HALF, HALF)
    far_half = rows_at(place.other * HALF, HALF)

    def load_two(group):
        first, count = REST_GROUPS[group]
        return pltpu.make_async_copy(
            tiles_in.at[pl.ds(first, count), near_half],
            two_stage.at[pl.ds(group % 3, 1)],
            load_sem.at[group % 3],
        )

    def rest_sum(group):
        first, count = REST_GROUPS[group]
        span_of = pl.ds(first, count)
        work = two.at[span_of]

        def send_pair():
            return remote(
                tiles_in.at[span_of, far_half],
                work,
                pair_two_send.at[group],
                pair_two_recv.at[group],
                place.twin,
            )

        def add_own():
            load_two(group).wait()
            work[...] = (work[...].astype(f32) + two_stage[group % 3].astype(f32)).astype(b16)

        sems = (two_send.at[group], two_recv.at[group])
        wide, narrow = two_wide.at[:, span_of], two_narrow.at[:, :, span_of]
        return Sum(place, work, wide, narrow, sems, send_pair, add_own)

    def pair_sum(group):
        first, count = BACK_PAIRS[group]
        span_of = pl.ds(first, count)
        work = one.at[span_of]

        def send_pair():
            return remote(
                one_send_stage.at[span_of],
                work,
                pair_one_send.at[group],
                pair_one_recv.at[group],
                place.twin,
            )

        def add_own():
            own = one_stage[span_of].astype(f32)
            work[...] = (work[...].astype(f32) + own).astype(b16)

        sems = (one_send.at[group], one_recv.at[group])
        wide, narrow = one_wide.at[:, span_of], one_narrow.at[:, :, span_of]
        return Sum(place, work, wide, narrow, sems, send_pair, add_own)

    def pair_gather(group):
        first, count = BACK_PAIRS[group]
        span_of = pl.ds(first, count)
        sems = (one_send.at[group], one_recv.at[group])
        narrow, wide = gather_narrow.at[:, span_of], gather_wide.at[:, span_of]
        return Gather(place, one.at[span_of], narrow, wide, sems)

    hand = Hand(
        place, table, two, bag, gift, pack, last, own, slots_out, (hand_send, hand_recv), hand_store
    )

    def pair_store(index, tile):
        return pltpu.make_async_copy(
            one.at[index, :, pl.ds(tile * PAIR, PAIR)],
            pairs_out.at[tile, :, pl.ds(index * PAIR, PAIR)],
            store_sem.at[index, tile],
        )

    def tick(number):
        for group, start in enumerate(BACK_REST):
            if 0 <= number - start < Sum.steps:
                rest_sum(group).step(number - start)
        for group, (first, count) in enumerate(BACK_PAIRS):
            start = 2 * (first + count)
            if 0 <= number - start < Sum.steps:
                pair_sum(group).step(number - start)
            if 0 <= number - start - Sum.steps + 1 < Gather.steps:
                pair_gather(group).step(number - start - Sum.steps + 1)
            if number == start + Sum.steps + 1:
                for index in range(first, first + count):
                    for tile in range(3):
                        pair_store(index, tile).start()
        if 0 <= number - BACK_HAND < Hand.steps:
            hand.step(number - BACK_HAND)
        for group, start in enumerate(BACK_REST):
            if number == max(start - 1, 0):
                load_two(group).start()

    def swap_y(index):
        there = pl.ds(place.core * rows, rows)
        if index == 0:
            return pltpu.make_async_copy(
                y_in.at[:, pl.ds(place.core * span, span)], y_out.at[there], swap_local.at[0]
            )
        return remote(
            y_in.at[:, pl.ds(place.other * span, span)],
            y_out.at[there],
            swap_send.at[0],
            swap_recv.at[0],
            place.twin,
        )

    @pl.when(step == 0)
    def lead():
        place.greet()
        for index in range(2):
            swap_y(index).start()
        sums_ref[...] = sums_in[...]

    for number in range(BACK_STEPS + BACK_TAIL):
        pl.when(step == number)(partial(tick, number))

    @pl.when(step < BACK_STEPS)
    def attention():
        pair, row = step // 2, lax.rem(step, 2)
        half = LEN // 2
        heads = []
        for head in range(2):
            part = slice(head * HEAD_DIM, (head + 1) * HEAD_DIM)
            values = head_only(v_ref[...], head)
            recip = r_ref[0, head : head + 1, :]
            grad = g_ref[part, :].astype(f32) * recip
            delta = jnp.sum(grad * o_ref[part, :].astype(f32), 0, keepdims=True)
            grad = grad.astype(b16)
            heads.append((values, grad, delta, jnp.concatenate([grad, grad], axis=0)))

        def raw(head, which):
            values, grad, delta, doubled = heads[head]
            return dot_nn(values, doubled[:, which * half : (which + 1) * half])

        units = [(head, which) for head in range(2) for which in range(2)]
        ready = raw(*units[0])
        for index, (head, which) in enumerate(units):
            slope = ready
            if index + 1 < len(units):
                ready = raw(*units[index + 1])
            values, grad, delta, doubled = heads[head]
            part = slice(head * HEAD_DIM, (head + 1) * HEAD_DIM)
            cols = slice(which * half, (which + 1) * half)
            weights = p_ref[head, :, cols]
            slope = (weights.astype(f32) * (slope - delta[:, cols])).astype(b16)
            value_grad = dot_nt(grad[:, cols], weights)
            key_grad = dot_nt(q_ref[part, cols], slope)
            query_grad = dot_nn(k_ref[part, :], slope) * (HEAD_DIM**-0.5)
            turned[part, cols] = query_grad.astype(b16)
            if which == 0:
                value_first, key_first = value_grad, key_grad
            else:
                value_grad, key_grad = value_first + value_grad, key_first + key_grad
                lower = slice(PAIR + head * HEAD_DIM, PAIR + (head + 1) * HEAD_DIM)
                turned[lower, :] = (key_grad * (1.0 / LOG2E)).astype(b16)
                lower = slice(2 * PAIR + head * HEAD_DIM, 2 * PAIR + (head + 1) * HEAD_DIM)
                turned[lower, :] = value_grad.astype(b16)
        where = pl.ds(pl.multiple_of(row * LEN, LEN), LEN)
        block = dot_nn(turned[...], n_ref[where])
        back = turned[...].T
        lanes = pl.ds(pl.multiple_of(pair * PAIR, PAIR), PAIR)
        ones = jnp.sum(back.astype(f32), 0, keepdims=True)
        sums_ref[4:5, lanes] += ones[:, :PAIR]
        sums_ref[5:6, lanes] += ones[:, 2 * PAIR :]
        term = dot_nt(back, w_ref[0])

        @pl.when(pair == 0)
        def begin():
            grad_sum[where] = term

        @pl.when(pair > 0)
        def add():
            grad_sum[where] += term

        @pl.when(row == 0)
        def keep():
            wide_sum[...] = block

        @pl.when(row == 1)
        def hand_on():
            whole = (wide_sum[...] + block).T
            low = whole.astype(b16)
            for core in range(2):

                @pl.when(place.core == core)
                def split():
                    one_stage[pair] = low[core * HALF : (core + 1) * HALF]
                    one_send_stage[pair] = low[(1 - core) * HALF : (2 - core) * HALF]

    def store_block(index):
        row, half = index // 2, index % 2
        target = i_out.at[place.core * rows + row]
        local = pltpu.make_async_copy(block_out.at[index], target, swap_local.at[1 + row])
        far = remote(
            block_out.at[index], target, swap_send.at[1 + row], swap_recv.at[1 + row], place.twin
        )
        return local, far, half

    for index in range(BACK_TAIL):

        @pl.when(step == BACK_STEPS + index)
        def close():
            size = LEN // 2
            grad = grad_sum[index * size : (index + 1) * size]
            unit, rstd = norm_parts(x_ref[...].astype(f32))
            sums_ref[0:1, :] += jnp.sum(grad * unit, 0, keepdims=True)
            sums_ref[1:2, :] += jnp.sum(grad, 0, keepdims=True)
            total = z_ref[...].astype(f32) + norm_back(grad, unit, rstd, vec_ref[0:1, :])
            block_out[index] = total.astype(b16)
            local, far, half = store_block(index)

            @pl.when(place.core == half)
            def keep():
                local.start()

            @pl.when(place.core != half)
            def give():
                far.start()

    @pl.when(step == BACK_STEPS + BACK_TAIL - 1)
    def drain():
        devices = [place.twin] + place.partners

        def vector(index):
            return remote(
                sums_ref, vec_land.at[index], vec_send.at[index], vec_recv.at[index], devices[index]
            )

        vector(0).start()
        for number in range(BACK_STEPS + BACK_TAIL, BACK_STEPS + Sum.steps + Gather.steps):
            tick(number)
            index = number - BACK_STEPS - BACK_TAIL
            if index < 5:
                vector(index).wait()
                sums_ref[...] += vec_land[index]
                if index < 4:
                    vector(index + 1).start()
        for index in range(2):
            swap_y(index).wait()
        for index in range(BACK_TAIL):
            local, far, half = store_block(index)

            @pl.when(place.core == half)
            def keep():
                local.wait()

            @pl.when(place.core != half)
            def give():
                far.wait()

        for index in range(PAIRS):
            for tile in range(3):
                pair_store(index, tile).wait()
        for flow in range(FLOWS):
            for copy in hand.stores(flow):
                copy.wait()


def back(table, attention, weights, normed, x, residual, vectors, tiles, sums, y):
    rows, length = y.shape[:2]
    tokens = rows * length
    any_spec = pl.BlockSpec(memory_space=pl.ANY)
    smem = pl.BlockSpec(memory_space=pltpu.SMEM)
    dma = pltpu.SemaphoreType.DMA

    def now(step):
        return jnp.minimum(step, BACK_STEPS - 1)

    def tail(step):
        return jnp.maximum(step - BACK_STEPS, 0)

    head_block = pl.BlockSpec((PAIR, LEN), lambda s: (now(s) // 2, lax.rem(now(s), 2)))
    tail_block = pl.BlockSpec((LEN // 2, D), lambda s: (tail(s), 0))
    whole = pl.BlockSpec((PIECES, D), lambda s: (0, 0))
    sums_block = pl.BlockSpec((16, D), lambda s: (0, 0))
    return pl.pallas_call(
        back_kernel,
        grid=(BACK_STEPS + BACK_TAIL,),
        in_specs=[
            smem,
            pl.BlockSpec((2, LEN, LEN), lambda s: (now(s), 0, 0)),
            pl.BlockSpec((1, 2, LEN), lambda s: (now(s), 0, 0)),
            pl.BlockSpec((LEN, PAIR), lambda s: (lax.rem(now(s), 2), now(s) // 2)),
            head_block,
            head_block,
            head_block,
            head_block,
            pl.BlockSpec((1, D, WIDE), lambda s: (now(s) // 2, 0, 0)),
            pl.BlockSpec((tokens, D), lambda s: (0, 0), pipeline_mode=pl.Buffered(1)),
            tail_block,
            tail_block,
            whole,
            any_spec,
            sums_block,
            any_spec,
        ],
        out_specs=[any_spec] * 4 + [sums_block],
        out_shape=[
            jax.ShapeDtypeStruct((2 * rows, length // 2, D), b16),
            jax.ShapeDtypeStruct((2 * rows, length // 2, D), b16),
            jax.ShapeDtypeStruct((3, HALF, D), b16),
            jax.ShapeDtypeStruct((CAP, HALF, D), b16),
            jax.ShapeDtypeStruct((16, D), f32),
        ],
        scratch_shapes=[
            pltpu.VMEM((tokens, D), f32),
            pltpu.VMEM((WIDE, D), f32),
            pltpu.VMEM((WIDE, LEN), b16),
            pltpu.VMEM((BACK_TAIL, LEN // 2, D), b16),
            pltpu.VMEM((REST, HALF, D), b16),
            pltpu.VMEM((FLOWS, REST, NEAR, D), b16),
            pltpu.VMEM((FLOWS, 3, REST, KEEP, D), b16),
            pltpu.VMEM((3, HALF, D), b16),
            pltpu.VMEM((PAIRS, HALF, WIDE), b16),
            pltpu.VMEM((FLOWS, PAIRS, NEAR, WIDE), b16),
            pltpu.VMEM((FLOWS, 3, PAIRS, KEEP, WIDE), b16),
            pltpu.VMEM((PAIRS, HALF, WIDE), b16),
            pltpu.VMEM((PAIRS, HALF, WIDE), b16),
            pltpu.VMEM((FLOWS, PAIRS, KEEP, WIDE), b16),
            pltpu.VMEM((FLOWS, PAIRS, NEAR, WIDE), b16),
            pltpu.VMEM((FLOWS, 2 * CAP, KEEP, D), b16),
            pltpu.VMEM((FLOWS, 2 * CAP, KEEP, D), b16),
            pltpu.VMEM((FLOWS, CAP, NEAR, D), b16),
            pltpu.VMEM((FLOWS, CAP, NEAR, D), b16),
            pltpu.VMEM((FLOWS, CAP, KEEP, D), b16),
            pltpu.VMEM((5, 16, D), f32),
            dma((REST, FLOWS, 5)),
            dma((REST, FLOWS, 5)),
            dma((PAIRS, FLOWS, 7)),
            dma((PAIRS, FLOWS, 7)),
            dma((FLOWS, 2)),
            dma((FLOWS, 2)),
            dma((FLOWS, 3)),
            dma((REST,)),
            dma((REST,)),
            dma((PAIRS,)),
            dma((PAIRS,)),
            dma((3,)),
            dma((PAIRS, 3)),
            dma((3,)),
            dma((3,)),
            dma((3,)),
            dma((5,)),
            dma((5,)),
        ],
        compiler_params=pltpu.CompilerParams(
            collective_id=1, has_side_effects=True, vmem_limit_bytes=62 * MIB
        ),
        name="back",
    )(table, *attention, weights, normed, x, residual, vectors, tiles, sums, y)


def update_kernel(tile_at, one, two, w_ref, m_ref, s_ref, y_in, i_in, w_out, m_out, s_out, y_out, i_out):
    step = pl.program_id(0)
    tile = tile_at[step // 2]
    grad = jnp.where(tile < 3, one[0], two[0]).astype(f32)
    parts = adam_step(w_ref[0], grad, m_ref[0], s_ref[0], RATE)
    for target, part in zip((w_out, m_out, s_out), parts):
        target[0] = jnp.where(tile >= 0, part, jnp.zeros_like(part))

    @pl.when(step < 4)
    def widen():
        y_out[...] = y_in[...].astype(f32)
        i_out[...] = i_in[...].astype(f32)


def update(tile_at, one, two, master, first, second, y, grad):
    tokens = y.shape[0]
    size = HALF // 2
    state = pl.BlockSpec((1, size, D), lambda s, tile_at: (s // 2, lax.rem(s, 2), 0))
    wide = pl.BlockSpec((tokens // 4, D), lambda s, tile_at: (jnp.minimum(s, 3), 0))
    return pl.pallas_call(
        update_kernel,
        grid_spec=pltpu.PrefetchScalarGridSpec(
            num_scalar_prefetch=1,
            grid=(CAP * 2,),
            in_specs=[
                pl.BlockSpec(
                    (1, size, D),
                    lambda s, tile_at: (jnp.clip(tile_at[s // 2], 0, 2), lax.rem(s, 2), 0),
                ),
                state,
                state,
                state,
                state,
                wide,
                wide,
            ],
            out_specs=[state] * 3 + [wide] * 2,
        ),
        out_shape=[jax.ShapeDtypeStruct(master.shape, f32)] * 3
        + [jax.ShapeDtypeStruct((tokens, D), f32)] * 2,
        compiler_params=pltpu.CompilerParams(vmem_limit_bytes=60 * MIB),
        name="update",
    )(tile_at, one, two, master, first, second, y, grad)


def shards_paired(
    inputs,
    cotangent,
    doc_lengths,
    owner_list,
    master,
    first_moment,
    second_moment,
    vectors,
    vector_first,
    vector_second,
):
    rows_here, span, width = inputs.shape
    place = lax.axis_index("blk")
    member = lax.axis_index("dp")
    rows_mine = rows_here // 2
    order = jnp.arange(PIECES)
    same_owner = owner_list[:, None] == owner_list[None, :]
    ranks = jnp.sum(same_owner & (order[None, :] < order[:, None]), axis=1).astype(jnp.int32)
    slot_of = owner_list * CAP + ranks
    front_outs = front(owner_list, doc_lengths, master, vectors, inputs, cotangent)
    x, cot, normed, weights_one, weights_two, queries, keys, values = front_outs[:8]
    weights, recips, context_turned, context = front_outs[8:]
    x = x.reshape(-1, width)
    cot = cot.reshape(-1, width)
    block_out, residual, grad_context, sums, tiles_two = feed(
        context, context_turned, x, cot, weights_two, vectors
    )
    hits = jnp.arange(16 * CAP)[:, None] == slot_of[None, :]
    tile_at = jnp.sum(jnp.where(hits, order[None, :] + 1, 0), axis=1).astype(jnp.int32) - 1
    table = jnp.maximum(tile_at - 3, 0)
    block_out, input_grad, total_one, total_two, vector_total = back(
        table,
        (weights, recips, values, queries, keys, context_turned, grad_context),
        weights_one,
        normed,
        x,
        residual,
        vectors,
        tiles_two,
        sums,
        block_out.reshape(rows_mine, LEN, width),
    )
    mine = lax.dynamic_slice_in_dim(tile_at, member * CAP, CAP, 0)
    *updated, block_out, input_grad = update(
        mine,
        total_one,
        total_two,
        master,
        first_moment,
        second_moment,
        block_out.reshape(-1, width),
        input_grad.reshape(-1, width),
    )
    columns = vector_first.shape[1]
    vector_cols = lax.dynamic_slice_in_dim(vectors, place * columns, columns, 1)
    vector_total = lax.dynamic_slice(vector_total, (0, place * columns), (PIECES, columns))
    updated_vectors = adam_step(vector_cols, vector_total, vector_first, vector_second, VEC_RATE)
    return (
        block_out.reshape(inputs.shape),
        input_grad.reshape(inputs.shape),
        *updated,
        *updated_vectors,
    )


def solution(mesh):
    in_specs = (
        P("dp", "blk", None),
        P("dp", "blk", None),
        P("dp", None),
        P(),
        P("dp", "blk", None),
        P("dp", "blk", None),
        P("dp", "blk", None),
        P(),
        P(None, "blk"),
        P(None, "blk"),
    )
    out_specs = (
        P("dp", "blk", None),
        P("dp", "blk", None),
        P("dp", "blk", None),
        P("dp", "blk", None),
        P("dp", "blk", None),
        P(None, "blk"),
        P(None, "blk"),
        P(None, "blk"),
    )
    paired = mesh.shape["blk"] == 2 and mesh.shape["dp"] == 16
    shards = shards_paired if paired else shards_any
    return jax.shard_map(shards, mesh=mesh, in_specs=in_specs, out_specs=out_specs, check_vma=False)
```

```python
from functools import partial

import jax
import jax.numpy as jnp
from jax import lax
from jax.experimental import pallas as pl
from jax.experimental.pallas import tpu as pltpu
from jax.sharding import PartitionSpec as P

D = 768
FF = 3072
HEADS = 12
HEAD_DIM = 64
LEN = 1024
CAP = 3
STEP = 10
PIECES = 12


EPS_NORM = 1e-05
BETA_ONE = 0.9
BETA_TWO = 0.999
RATE = 0.04
VEC_RATE = 0.25
DECAY = 0.01
ADAM_EPS = 1e-08


def normalize(values_in, gain, shift):
    center = jnp.mean(values_in, axis=-1, keepdims=True)
    offset = values_in - center
    spread = jnp.mean(offset * offset, axis=-1, keepdims=True)
    return offset * lax.rsqrt(spread + EPS_NORM) * gain + shift


def adam_step(weight, grad, first, second, rate):
    first_new = BETA_ONE * first + (1.0 - BETA_ONE) * grad
    second_new = BETA_TWO * second + (1.0 - BETA_TWO) * grad * grad
    corrected = (
        first_new
        / (1.0 - BETA_ONE**STEP)
        / (jnp.sqrt(second_new / (1.0 - BETA_TWO**STEP)) + ADAM_EPS)
    )
    return (weight - rate * (corrected + DECAY * weight), first_new, second_new)


def shards_any(
    inputs,
    cotangent,
    doc_lengths,
    owner_list,
    master,
    first_moment,
    second_moment,
    vectors,
    vector_first,
    vector_second,
):
    rows_here, span, width = inputs.shape
    tokens_here = rows_here * span
    fold = FF // D
    scale = HEAD_DIM ** (-0.5)
    place = lax.axis_index("blk")
    f32 = jnp.float32
    b16 = jnp.bfloat16
    order = jnp.arange(PIECES)
    same_owner = owner_list[:, None] == owner_list[None, :]
    ranks = jnp.sum(same_owner & (order[None, :] < order[:, None]), axis=1)
    slot_of = owner_list * CAP + ranks

    mine = (owner_list == lax.axis_index("dp"))[:, None, None]
    tile_rows = lax.psum(jnp.where(mine, master[ranks], 0.0).astype(b16), "dp")
    tiles = lax.all_gather(tile_rows, "blk", axis=1, tiled=True)
    query_weight = tiles[0]
    key_weight = tiles[1]
    value_weight = tiles[2]
    out_weight = tiles[3]
    up_weight = jnp.transpose(tiles[4 : 4 + fold], (1, 0, 2)).reshape(width, FF)
    down_weight = tiles[4 + fold :].reshape(FF, width)
    flat_in = inputs.reshape(tokens_here, width).astype(f32)
    normed_one = normalize(flat_in, vectors[0], vectors[1]).astype(b16)
    queries = (jnp.dot(normed_one, query_weight, preferred_element_type=f32) + vectors[4]).astype(
        b16
    )
    keys_here = jnp.dot(normed_one, key_weight, preferred_element_type=f32).astype(b16)
    values_here = (
        jnp.dot(normed_one, value_weight, preferred_element_type=f32) + vectors[5]
    ).astype(b16)
    query_heads = queries.reshape(rows_here, span, HEADS, HEAD_DIM)
    first_len = doc_lengths[:, 0]
    query_seg = (place * span + jnp.arange(span))[None, :] >= first_len[:, None]

    def block_scores(key_block, start):
        count = key_block.shape[1]
        key_heads = key_block.reshape(rows_here, count, HEADS, HEAD_DIM)
        raw = (
            jnp.einsum("rqhd,rkhd->rhqk", query_heads, key_heads, preferred_element_type=f32)
            * scale
        )
        key_seg = (start + jnp.arange(count))[None, :] >= first_len[:, None]
        allowed = query_seg[:, None, :, None] == key_seg[:, None, None, :]
        return (raw, allowed)

    key_rows = keys_here.reshape(rows_here, span, width)
    value_rows = values_here.reshape(rows_here, span, width)
    top = jnp.full((rows_here, HEADS, span), -1e30, f32)
    key_block = lax.all_gather(key_rows, "blk", axis=1, tiled=True)
    value_block = lax.all_gather(value_rows, "blk", axis=1, tiled=True)
    count = key_block.shape[1]
    raw, allowed = block_scores(key_block, jnp.int32(0))
    new_top = jnp.maximum(top, jnp.max(jnp.where(allowed, raw, -1e30), axis=-1))
    weights = jnp.where(allowed, jnp.exp(raw - new_top[..., None]), 0.0)
    value_heads = value_block.reshape(rows_here, count, HEADS, HEAD_DIM)
    update = jnp.einsum(
        "rhqk,rkhd->rhqd", weights.astype(b16), value_heads, preferred_element_type=f32
    )
    total = jnp.sum(weights, axis=-1)
    log_total = new_top + jnp.log(total)
    context_raw = update / total[..., None]
    context_low = jnp.transpose(context_raw, (0, 2, 1, 3)).reshape(tokens_here, width).astype(b16)
    residual = flat_in + (jnp.dot(context_low, out_weight, preferred_element_type=f32) + vectors[6])
    normed_two = normalize(residual, vectors[2], vectors[3]).astype(b16)
    hidden = jnp.dot(normed_two, up_weight, preferred_element_type=f32) + vectors[8:].reshape(FF)
    gelu_exact = partial(jax.nn.gelu, approximate=False)
    active, gelu_pull = jax.vjp(gelu_exact, hidden)
    active_low = active.astype(b16)
    block_out = (
        residual + (jnp.dot(active_low, down_weight, preferred_element_type=f32) + vectors[7])
    ).reshape(rows_here, span, width)
    grad_out = cotangent.reshape(tokens_here, width)
    down_grad = jnp.einsum("tf,td->fd", active_low, grad_out, preferred_element_type=f32)
    down_sum = jnp.sum(grad_out, axis=0, dtype=f32)
    grad_active = jnp.einsum("td,fd->tf", grad_out, down_weight, preferred_element_type=f32)
    grad_hidden = gelu_pull(grad_active)[0].astype(b16)
    up_grad = jnp.einsum("td,tf->df", normed_two, grad_hidden, preferred_element_type=f32)
    up_sum = jnp.sum(grad_hidden, axis=0, dtype=f32)
    ffn_tiles = jnp.concatenate(
        [
            jnp.transpose(up_grad.reshape(width, fold, width), (1, 0, 2)),
            down_grad.reshape(fold, width, width),
        ],
        axis=0,
    )
    grad_normed_two = jnp.einsum("tf,df->td", grad_hidden, up_weight, preferred_element_type=f32)
    unused, second_pull = jax.vjp(normalize, residual, vectors[2], vectors[3])
    residual_part, gain_two_grad, shift_two_grad = second_pull(grad_normed_two)
    grad_residual = grad_out.astype(f32) + residual_part
    grad_attended = grad_residual.astype(b16)
    out_grad = jnp.einsum("tm,td->md", context_low, grad_attended, preferred_element_type=f32)
    out_sum = jnp.sum(grad_attended, axis=0, dtype=f32)
    grad_context = jnp.einsum(
        "td,md->tm", grad_attended, out_weight, preferred_element_type=f32
    ).astype(b16)
    grad_heads = grad_context.reshape(rows_here, span, HEADS, HEAD_DIM)
    delta = jnp.einsum("rqhd,rhqd->rhq", grad_heads.astype(f32), context_raw)
    key_all, value_all = (
        lax.all_gather(key_rows, "blk", axis=1, tiled=True),
        lax.all_gather(value_rows, "blk", axis=1, tiled=True),
    )
    key_size = min(512, LEN)

    def back_block(index, carry):
        grad_query, key_total, value_total = carry
        start = index * key_size
        key_block = lax.dynamic_slice_in_dim(key_all, start, key_size, 1)
        value_block = lax.dynamic_slice_in_dim(value_all, start, key_size, 1)
        raw, allowed = block_scores(key_block, start)
        weights_back = jnp.where(allowed, jnp.exp(raw - log_total[..., None]), 0.0)
        key_heads = key_block.reshape(rows_here, key_size, HEADS, HEAD_DIM)
        value_heads = value_block.reshape(rows_here, key_size, HEADS, HEAD_DIM)
        value_grad = jnp.einsum(
            "rhqk,rqhd->rkhd", weights_back.astype(b16), grad_heads, preferred_element_type=f32
        )
        weight_grad = jnp.einsum(
            "rqhd,rkhd->rhqk", grad_heads, value_heads, preferred_element_type=f32
        )
        score_grad = (weights_back * (weight_grad - delta[..., None])).astype(b16)
        grad_query = (
            grad_query
            + jnp.einsum("rhqk,rkhd->rqhd", score_grad, key_heads, preferred_element_type=f32)
            * scale
        )
        key_grad = (
            jnp.einsum("rhqk,rqhd->rkhd", score_grad, query_heads, preferred_element_type=f32)
            * scale
        )
        key_total = lax.dynamic_update_slice_in_dim(
            key_total, key_grad.reshape(rows_here, key_size, width), start, 1
        )
        value_total = lax.dynamic_update_slice_in_dim(
            value_total, value_grad.reshape(rows_here, key_size, width), start, 1
        )
        return (grad_query, key_total, value_total)

    zero_rows = jnp.zeros((rows_here, LEN, width), f32)
    grad_query, key_total, value_total = lax.fori_loop(
        0,
        LEN // key_size,
        back_block,
        (jnp.zeros((rows_here, span, HEADS, HEAD_DIM), f32), zero_rows, zero_rows),
    )
    key_grad_here, value_grad_here = (
        lax.psum_scatter(
            key_total.astype(jnp.bfloat16), "blk", scatter_dimension=1, tiled=True
        ).astype(jnp.float32),
        lax.psum_scatter(
            value_total.astype(jnp.bfloat16), "blk", scatter_dimension=1, tiled=True
        ).astype(jnp.float32),
    )
    query_low = grad_query.reshape(tokens_here, width).astype(b16)
    key_low = key_grad_here.reshape(tokens_here, width).astype(b16)
    value_low = value_grad_here.reshape(tokens_here, width).astype(b16)
    query_tile = jnp.einsum("td,te->de", normed_one, query_low, preferred_element_type=f32)
    key_tile = jnp.einsum("td,te->de", normed_one, key_low, preferred_element_type=f32)
    value_tile = jnp.einsum("td,te->de", normed_one, value_low, preferred_element_type=f32)
    grad_normed_one = (
        jnp.einsum("te,de->td", query_low, query_weight, preferred_element_type=f32)
        + jnp.einsum("te,de->td", key_low, key_weight, preferred_element_type=f32)
        + jnp.einsum("te,de->td", value_low, value_weight, preferred_element_type=f32)
    )
    unused, first_pull = jax.vjp(normalize, flat_in, vectors[0], vectors[1])
    input_part, gain_one_grad, shift_one_grad = first_pull(grad_normed_one)
    input_grad = (grad_residual + input_part).reshape(rows_here, span, width)
    vector_grads = jnp.concatenate(
        [
            jnp.stack(
                [
                    gain_one_grad,
                    shift_one_grad,
                    gain_two_grad,
                    shift_two_grad,
                    jnp.sum(query_low, axis=0, dtype=f32),
                    jnp.sum(value_low, axis=0, dtype=f32),
                    out_sum,
                    down_sum,
                ]
            ),
            up_sum.reshape(fold, width),
        ],
        axis=0,
    )
    attn_tiles = jnp.stack([query_tile, key_tile, value_tile, out_grad])
    piece_share, vector_share = (
        lax.psum_scatter(
            jnp.concatenate([attn_tiles, ffn_tiles], axis=0).astype(jnp.bfloat16),
            "blk",
            scatter_dimension=1,
            tiled=True,
        ).astype(jnp.float32),
        lax.psum_scatter(
            vector_grads.astype(jnp.bfloat16), "blk", scatter_dimension=1, tiled=True
        ).astype(jnp.float32),
    )
    own_slots = lax.axis_index("dp") * CAP + jnp.arange(CAP)
    pick = (own_slots[:, None] == slot_of[None, :]).astype(f32)
    occupied = jnp.sum(pick, axis=1)[:, None, None]
    total_share, vector_total = (
        lax.psum(piece_share.astype(jnp.bfloat16), "dp").astype(jnp.float32),
        lax.psum(vector_share.astype(jnp.bfloat16), "dp").astype(jnp.float32),
    )
    slot_grads = jnp.einsum("cp,prd->crd", pick, total_share, precision=lax.Precision.HIGHEST)
    new_master, new_first, new_second = adam_step(
        master, slot_grads, first_moment, second_moment, RATE
    )
    columns = vector_first.shape[1]
    vector_cols = lax.dynamic_slice_in_dim(vectors, place * columns, columns, 1)
    new_vectors, new_vector_first, new_vector_second = adam_step(
        vector_cols, vector_total, vector_first, vector_second, VEC_RATE
    )
    return (
        block_out,
        input_grad,
        new_master * occupied,
        new_first * occupied,
        new_second * occupied,
        new_vectors,
        new_vector_first,
        new_vector_second,
    )


f32 = jnp.float32
b16 = jnp.bfloat16
LOG2E = 1.4426950408889634
MIB = 1024 * 1024
PAIRS = HEADS // 2
PAIR = 2 * HEAD_DIM


def dot_nn(left, right):
    return lax.dot_general(left, right, (((1,), (0,)), ((), ())), preferred_element_type=f32)


def dot_nt(left, right):
    return lax.dot_general(left, right, (((1,), (1,)), ((), ())), preferred_element_type=f32)


def dot_tn(left, right):
    return lax.dot_general(left, right, (((0,), (0,)), ((), ())), preferred_element_type=f32)


def norm_parts(values_in):
    center = jnp.mean(values_in, axis=-1, keepdims=True)
    offset = values_in - center
    spread = jnp.mean(offset * offset, axis=-1, keepdims=True)
    rstd = lax.rsqrt(spread + EPS_NORM)
    return offset * rstd, rstd


def norm_back(grad, unit, rstd, gain):
    scaled = grad * gain
    first = jnp.mean(scaled, axis=-1, keepdims=True)
    second = jnp.mean(scaled * unit, axis=-1, keepdims=True)
    return rstd * (scaled - first - unit * second)


def gelu_parts(value):
    bell = jnp.exp2(value * value * (-0.5 * LOG2E))
    ratio = pl.reciprocal(1.0 + (0.3275911 * 0.7071067811865476) * jnp.abs(value))
    poly = 0.5 * 1.061405429
    poly = poly * ratio + 0.5 * -1.453152027
    poly = poly * ratio + 0.5 * 1.421413741
    poly = poly * ratio + 0.5 * -0.284496736
    poly = poly * ratio + 0.5 * 0.254829592
    tail = poly * ratio * bell
    cdf = jnp.where(value >= 0.0, 1.0 - tail, tail)
    return value * cdf, cdf + value * (bell * 0.3989422804014327)


def head_only(block, head):
    lane = lax.broadcasted_iota(jnp.int32, block.shape, 1)
    keep = (lane >= head * HEAD_DIM) & (lane < (head + 1) * HEAD_DIM)
    return jnp.where(keep, block, jnp.zeros_like(block))


def feed_kernel(
    c_ref, o_ref, x_ref, g_ref, w_ref, vec_ref,
    y_ref, r_ref, d_ref, sums_ref, tiles_ref,
    acc_ref, stage_ref, sem_ref,
):
    fold = FF // D
    step = pl.program_id(0)

    @pl.when(step == 0)
    def clear():
        acc_ref[...] = jnp.zeros_like(acc_ref)
        sums_ref[...] = jnp.zeros_like(sums_ref)

    residual = x_ref[...].astype(f32) + (dot_nn(c_ref[...], w_ref[0]) + vec_ref[6:7, :])
    unit, rstd = norm_parts(residual)
    gain = vec_ref[2:3, :]
    normed = (unit * gain + vec_ref[3:4, :]).astype(b16)
    turned = normed.T
    cot = g_ref[...]
    out = residual + vec_ref[7:8, :]
    grad = jnp.zeros_like(out)

    for part in range(fold):
        hidden = dot_nn(normed, w_ref[1 + part]) + vec_ref[8 + part : 9 + part, :]
        pulled = dot_nt(cot, w_ref[1 + fold + part])
        active, slope = gelu_parts(hidden)
        active = active.astype(b16)
        pulled = (pulled * slope).astype(b16)
        out = out + dot_nn(active, w_ref[1 + fold + part])
        grad = grad + dot_nt(pulled, w_ref[1 + part])
        acc_ref[1 + part] += dot_nn(turned, pulled)
        acc_ref[1 + fold + part] += dot_tn(active, cot)
        sums_ref[8 + part : 9 + part, :] += jnp.sum(pulled.astype(f32), 0, keepdims=True)
    y_ref[...] = out.astype(b16)
    wide = cot.astype(f32)
    sums_ref[2:3, :] += jnp.sum(grad * unit, 0, keepdims=True)
    sums_ref[3:4, :] += jnp.sum(grad, 0, keepdims=True)
    sums_ref[7:8, :] += jnp.sum(wide, 0, keepdims=True)
    back = wide + norm_back(grad, unit, rstd, gain)
    r_ref[...] = back.astype(b16)
    low = back.astype(b16)
    sums_ref[6:7, :] += jnp.sum(low.astype(f32), 0, keepdims=True)
    d_ref[...] = dot_nt(w_ref[0], low).astype(b16)
    acc_ref[0] += dot_nn(o_ref[...], low)

    @pl.when(step == pl.num_programs(0) - 1)
    def send():
        count = 1 + 2 * fold
        copies = []
        for part in range(count):
            if part >= 2:
                copies[part - 2].wait()
            stage_ref[part % 2] = acc_ref[part].astype(b16)
            copy = pltpu.make_async_copy(stage_ref.at[part % 2], tiles_ref.at[part], sem_ref.at[part % 2])
            copy.start()
            copies.append(copy)
        copies[count - 2].wait()
        copies[count - 1].wait()


def feed(context, turned, x, cot, weights, vectors):
    tokens = x.shape[0]
    size = 512
    count = 1 + 2 * (FF // D)
    token_block = pl.BlockSpec((size, D), lambda i: (i, 0))
    turned_block = pl.BlockSpec((D, size), lambda i: (0, i))
    return pl.pallas_call(
        feed_kernel,
        grid=(tokens // size,),
        in_specs=[
            token_block,
            turned_block,
            token_block,
            token_block,
            pl.BlockSpec((count, D, D), lambda i: (0, 0, 0), pipeline_mode=pl.Buffered(1)),
            pl.BlockSpec((PIECES, D), lambda i: (0, 0)),
        ],
        out_specs=[
            token_block,
            token_block,
            turned_block,
            pl.BlockSpec((16, D), lambda i: (0, 0)),
            pl.BlockSpec(memory_space=pl.ANY),
        ],
        out_shape=[
            jax.ShapeDtypeStruct((tokens, D), b16),
            jax.ShapeDtypeStruct((tokens, D), b16),
            jax.ShapeDtypeStruct((D, tokens), b16),
            jax.ShapeDtypeStruct((16, D), f32),
            jax.ShapeDtypeStruct((count, D, D), b16),
        ],
        scratch_shapes=[
            pltpu.VMEM((count, D, D), f32),
            pltpu.VMEM((2, D, D), b16),
            pltpu.SemaphoreType.DMA((2,)),
        ],
        compiler_params=pltpu.CompilerParams(vmem_limit_bytes=63 * MIB),
        cost_estimate=pl.CostEstimate(
            flops=6 * count * tokens * D * D,
            bytes_accessed=18 * tokens * D + 4 * count * D * D,
            transcendentals=2 * tokens * FF,
        ),
        name="feed",
    )(context, turned, x, cot, weights, vectors)


MESH = pl.DeviceIdType.MESH
HALF = D // 2
FLOWS = 2
FLOW = HALF // FLOWS
NEAR = FLOW // 2
KEEP = NEAR // 2
WIDE = 3 * PAIR
REST = PIECES - 3
GROUPS = ((0, 1), (1, 2), (3, 3))
CHUNKS = len(GROUPS)


class Place:
    def __init__(self):
        self.me = lax.axis_index("dp")
        self.core = lax.axis_index("blk")
        self.bits = [lax.rem(self.me // weight, 2) for weight in (1, 2, 4, 8)]
        self.chips = [
            self.me + weight - 2 * weight * bit for weight, bit in zip((1, 2, 4, 8), self.bits)
        ]
        self.partners = [{"dp": chip} for chip in self.chips]
        low, high = self.bits[2:]
        self.inner = low != high
        self.across = {"dp": self.me + 4 - 8 * low + 8 - 16 * high}
        self.other = 1 - self.core
        self.twin = {"blk": self.other}

    def greet(self):
        barrier = pltpu.get_barrier_semaphore()
        for device in self.partners + [self.across, self.twin]:
            pl.semaphore_signal(barrier, 1, device_id=device, device_id_type=MESH)
        pl.semaphore_wait(barrier, 6)

    def flow(self, index):
        first, second = (0, 1) if index == 0 else (1, 0)
        base = index * FLOW
        near = base + self.bits[first] * NEAR
        far = base + NEAR - self.bits[first] * NEAR
        keep = near + self.bits[second] * KEEP
        give = near + KEEP - self.bits[second] * KEEP
        return first, second, near, far, keep, give


def remote(source, target, send, receive, device):
    return pltpu.make_async_remote_copy(
        src_ref=source,
        dst_ref=target,
        send_sem=send,
        recv_sem=receive,
        device_id=device,
        device_id_type=MESH,
    )


def rows_at(start, count):
    return pl.ds(pl.multiple_of(start, 16), count)


class Spread:
    def __init__(self, place, owner, rank, slots, land, gift, sems):
        self.place, self.owner, self.rank = place, owner, rank
        self.slots, self.land, self.gift, self.sems = slots, land, gift, sems

    def cols(self, chunk):
        return pl.ds(GROUPS[chunk][0] * PAIR, GROUPS[chunk][1] * PAIR)

    def first_copy(self, chunk, index):
        first, second, near, far, keep, give = self.place.flow(index)
        return remote(
            self.slots.at[:, rows_at(far, NEAR), self.cols(chunk)],
            self.land[chunk].at[index],
            self.sems[0].at[chunk, index, 0],
            self.sems[1].at[chunk, index, 0],
            self.place.partners[first],
        )

    def second_copy(self, chunk, index, which):
        first, second, near, far, keep, give = self.place.flow(index)
        if which == 0:
            source = self.slots.at[:, rows_at(give, KEEP), self.cols(chunk)]
        else:
            source = self.land[chunk].at[index, :, rows_at(give - near, KEEP)]
        return remote(
            source,
            self.gift[chunk].at[index, pl.ds(which * CAP, CAP)],
            self.sems[0].at[chunk, index, 1 + which],
            self.sems[1].at[chunk, index, 1 + which],
            self.place.partners[second],
        )

    def step(self, chunk, index):
        for flow in range(FLOWS):
            if index == 0:
                self.first_copy(chunk, flow).start()
                self.second_copy(chunk, flow, 0).start()
            if index == 1:
                self.first_copy(chunk, flow).wait()
                self.second_copy(chunk, flow, 1).start()
            if index == 2:
                self.second_copy(chunk, flow, 0).wait()
                self.second_copy(chunk, flow, 1).wait()

    def piece(self, tile, index, chunk, start, count):
        first, second, near, far, keep, give = self.place.flow(index)
        owner, rank = self.owner[tile], self.rank[tile]
        bits = [lax.rem(owner, 2), lax.rem(owner // 2, 2)]
        apart = [bit != mine for bit, mine in zip(bits, self.place.bits)]
        cols = pl.ds(start, count)
        mine = self.slots[rank, rows_at(keep, KEEP), pl.ds(GROUPS[chunk][0] * PAIR + start, count)]
        firsts = self.land[chunk][index, rank, rows_at(keep - near, KEEP), cols]
        gifts = self.gift[chunk][index, jnp.where(apart[first], CAP, 0) + rank, :, cols]
        value = jnp.where(apart[second], gifts, jnp.where(apart[first], firsts, mine))
        layer = owner // 4 == self.place.me // 4
        return jnp.where(layer, value, jnp.zeros_like(value))


class Column:
    steps = 4

    def __init__(self, place, kept, read, write, land, sems):
        self.place, self.kept, self.read, self.write = place, kept, read, write
        self.land, self.sems = land, sems

    def copy(self, index):
        target = self.land.at[index % 2]
        device = self.place.across if index == 1 else self.place.partners[2]
        return remote(
            self.kept, target, self.sems[0].at[index], self.sems[1].at[index], device
        )

    def add(self, index):
        self.write((self.read().astype(f32) + self.land[index].astype(f32)).astype(b16))


def column_step(place, columns, index):
    @pl.when(place.inner)
    def inner():
        for column in columns:
            if index == 1:
                column.copy(0).wait_recv()
                column.add(0)
                column.copy(1).start()
            if index == 2:
                column.copy(1).wait()
                column.add(1)
                column.copy(2).start()
            if index == 3:
                column.copy(2).wait_send()

    @pl.when(jnp.logical_not(place.inner))
    def outer():
        for column in columns:
            if index == 0:
                column.copy(0).start()
            if index == 1:
                column.copy(0).wait_send()
            if index == 3:
                column.copy(2).wait_recv()
                column.write(column.land[0])


class Item:
    steps = 7

    def __init__(self, place, work, land, sems, load, store=None):
        self.place, self.work, self.land, self.sems = place, work, land, sems
        self.load, self.store = load, store
        self.base = place.core * HALF

    def column(self, flow):
        rows = rows_at(self.base + self.place.flow(flow)[4], KEEP)

        def read():
            return self.work[:, rows]

        def write(value):
            self.work[:, rows] = value

        sems = (self.sems[0].at[flow], self.sems[1].at[flow])
        return Column(self.place, self.work.at[:, rows], read, write, self.land.at[flow], sems)

    def copy(self, flow, index):
        first, second, near, far, keep, give = self.place.flow(flow)
        kept = self.work.at[:, rows_at(self.base + keep, KEEP)]
        half = self.work.at[:, rows_at(self.base + near, NEAR)]
        source, device = [
            (kept, self.place.partners[second]),
            (half, self.place.partners[first]),
        ][index]
        return remote(
            source, source, self.sems[0].at[flow, 3 + index], self.sems[1].at[flow, 3 + index], device
        )

    def pair(self):
        rows = self.work.at[:, rows_at(self.base, HALF)]
        return remote(rows, rows, self.sems[0].at[0, 5], self.sems[1].at[0, 5], self.place.twin)

    def step(self, index):
        for flow in range(FLOWS):
            if index == 0:
                self.load(self.work, rows_at(self.base + self.place.flow(flow)[4], KEEP), flow)
        if index <= 3:
            column_step(self.place, [self.column(flow) for flow in range(FLOWS)], index)
        for flow in range(FLOWS):
            if 4 <= index <= 5:
                self.copy(flow, index - 4).wait()
            if 3 <= index <= 4:
                self.copy(flow, index - 3).start()
        if index == 5:
            self.pair().start()
        if index == 6:
            self.pair().wait()
            self.store().start()


REST_GROUPS = tuple((index, 1) for index in range(REST))
PAIR_CHUNK = (0, 1, 1, 2, 2, 2)
FRONT_PAIRS = (2, 4, 5, 6, 7, 8)
FRONT_REST = (6, 7, 8, 9, 10, 11, 12, 13, 14)
FRONT_LEAD = 9


def front_kernel(
    owner, lengths, master, vec_ref, x_in, c_in,
    x_out, c_out, n_out, one_out, two_out, q_ref, k_ref, v_ref, p_ref, r_ref, o_ref, ctx_ref,
    rank, rows_ref, normed, keys, turned_values, slots,
    land_one, land_two, land_three, gift_one, gift_two, gift_three,
    one, one_land, two, two_land,
    spread_send, spread_recv, one_send, one_recv, two_send, two_recv,
    swap_send, swap_recv, swap_local, store_sem,
):
    pair = pl.program_id(0)
    row = pl.program_id(1)
    grid_step = pair * 2 + row
    place = Place()
    rows, span = x_in.shape[0] // 2, x_in.shape[1]
    land = (land_one, land_two, land_three)
    gift = (gift_one, gift_two, gift_three)
    spread = Spread(place, owner, rank, slots, land, gift, (spread_send, spread_recv))

    def swaps(index):
        source, target = [(x_in, rows_ref), (c_in, c_out)][index]
        here = pl.ds(place.core * span, span)
        near = pltpu.make_async_copy(
            source.at[pl.ds(place.core * rows, rows)], target.at[:, here], swap_local.at[index]
        )
        far = remote(
            source.at[pl.ds(place.other * rows, rows)],
            target.at[:, here],
            swap_send.at[index],
            swap_recv.at[index],
            place.twin,
        )
        return near, far

    def row_store():
        return pltpu.make_async_copy(rows_ref, x_out, store_sem.at[PAIRS + REST])

    def normed_store():
        return pltpu.make_async_copy(normed, n_out, store_sem.at[PAIRS + REST + 1])

    def pair_item(group):
        span_of = pl.ds(group, 1)

        def load(work, where, flow):
            chunk = PAIR_CHUNK[group]
            for tile in range(3):
                part = spread.piece(tile, flow, chunk, (group - GROUPS[chunk][0]) * PAIR, PAIR)
                work[0, where, pl.ds(tile * PAIR, PAIR)] = part

        def store():
            return pltpu.make_async_copy(one.at[span_of], one_out.at[span_of], store_sem.at[group])

        sems = (one_send.at[group], one_recv.at[group])
        return Item(place, one.at[span_of], one_land.at[:, :, span_of], sems, load, store)

    def rest_item(group):
        first, count = REST_GROUPS[group]
        span_of = pl.ds(first, count)

        def load(work, where, flow):
            for index in range(count):
                for chunk, (start, wide) in enumerate(GROUPS):
                    part = spread.piece(3 + first + index, flow, chunk, 0, wide * PAIR)
                    work[index, where, pl.ds(start * PAIR, wide * PAIR)] = part

        def store():
            return pltpu.make_async_copy(
                two.at[span_of], two_out.at[span_of], store_sem.at[PAIRS + group]
            )

        sems = (two_send.at[group], two_recv.at[group])
        return Item(place, two.at[span_of], two_land.at[:, :, span_of], sems, load, store)

    def tick(number, odd):
        for chunk in range(CHUNKS):
            if odd == 0 and 0 <= number - 2 * chunk <= 2:
                spread.step(chunk, number - 2 * chunk)
        starts = [(pair_item, group, start) for group, start in enumerate(FRONT_PAIRS)]
        starts += [(rest_item, group, start) for group, start in enumerate(FRONT_REST)]
        for make, group, start in starts:
            if group % 2 == odd and 0 <= number - start < Item.steps:
                make(group).step(number - start)

    def both(number):
        tick(number, 0)
        tick(number, 1)

    @pl.when(grid_step == 0)
    def lead():
        slots[...] = master[...].astype(b16)
        for tile in range(PIECES):
            count = jnp.int32(0)
            for before in range(tile):
                count = count + (owner[before] == owner[tile]).astype(jnp.int32)
            rank[tile] = jnp.minimum(count, CAP - 1)
        place.greet()
        for copy in swaps(0):
            copy.start()
        both(0)
        for copy in swaps(1):
            copy.start()
        for copy in swaps(0):
            copy.wait()
        row_store().start()

        def norm_rows(index, carry):
            where = pl.ds(index * 256, 256)
            for part in range(rows):
                unit, unused = norm_parts(rows_ref[part, where].astype(f32))
                low = (unit * vec_ref[0:1, :] + vec_ref[1:2, :]).astype(b16)
                normed[pl.ds(part * LEN + index * 256, 256)] = low
            return carry

        both(1)
        lax.fori_loop(0, LEN // 256, norm_rows, 0)
        normed_store().start()
        for number in range(2, FRONT_LEAD):
            both(number)

    for number in range(2 * PAIRS):
        pl.when(grid_step == number)(partial(tick, FRONT_LEAD + number, 0))

    @pl.when(row == 0)
    def project():
        lanes = pl.ds(pl.multiple_of(pair * PAIR, PAIR), PAIR)
        weight = one[pair]

        def part(index, carry):
            where = pl.ds(pl.multiple_of(index * 512, 512), 512)
            both = dot_nn(normed[where], weight)
            queries = both[:, :PAIR] + vec_ref[4:5, lanes]
            queries = (queries * (HEAD_DIM**-0.5 * LOG2E)).astype(b16)
            q_ref[:, where] = queries.T
            low = both[:, PAIR : 2 * PAIR].astype(b16)
            keys[where] = low
            k_ref[:, where] = low.T
            values = (both[:, 2 * PAIR :] + vec_ref[5:6, lanes]).astype(b16)
            v_ref[where] = values
            turned_values[:, where] = values.T
            return carry

        lax.fori_loop(0, normed.shape[0] // 512, part, 0)

    half = LEN // 2
    start = pl.multiple_of(row * LEN, LEN)
    split = lengths[place.core * rows + row, 0] < LEN
    shift = jnp.where(split, jnp.float32(-1e30), jnp.float32(0.0))

    def scores(head, step):
        cols = pl.ds(pl.multiple_of(start + step * half, half), half)
        others = pl.ds(pl.multiple_of(start + (1 - step) * half, half), half)
        queries = q_ref[:, cols]
        near = dot_nn(head_only(keys[cols], head), queries)
        far = dot_nn(head_only(keys[others], head), queries) + shift
        return near, far

    for head, step in [(head, step) for head in range(2) for step in range(2)]:
        if (head, step) == (1, 0):
            for number in range(2 * PAIRS):
                pl.when(grid_step == number)(partial(tick, FRONT_LEAD + number, 1))
        near, far = scores(head, step)
        part = slice(head * HEAD_DIM, (head + 1) * HEAD_DIM)
        top = jnp.maximum(jnp.max(near, 0, keepdims=True), jnp.max(far, 0, keepdims=True))
        near = jnp.exp2(near - top)
        far = jnp.exp2(far - top)
        total = jnp.sum(near, 0, keepdims=True) + jnp.sum(far, 0, keepdims=True)
        recip = 1.0 / total
        here = slice(step * half, (step + 1) * half)
        there = slice((1 - step) * half, (2 - step) * half)
        near, far = near.astype(b16), far.astype(b16)
        p_ref[head, here, here] = near
        p_ref[head, there, here] = far
        r_ref[0, head : head + 1, here] = recip
        cols = pl.ds(pl.multiple_of(start + step * half, half), half)
        others = pl.ds(pl.multiple_of(start + (1 - step) * half, half), half)
        out = dot_nn(turned_values[part, cols], near) + dot_nn(turned_values[part, others], far)
        o_ref[part, here] = (out * recip).astype(b16)
    ctx_ref[...] = o_ref[...].T

    @pl.when(grid_step == 2 * PAIRS - 1)
    def finish_copies():
        for copy in swaps(1):
            copy.wait()
        row_store().wait()
        normed_store().wait()
        for group in range(PAIRS):
            pair_item(group).store().wait()
        for group in range(REST):
            rest_item(group).store().wait()


def front(owner, lengths, master, vectors, inputs, cotangent):
    rows, span = inputs.shape[0] // 2, inputs.shape[1]
    tokens = rows * LEN
    any_spec = pl.BlockSpec(memory_space=pl.ANY)
    smem = pl.BlockSpec(memory_space=pltpu.SMEM)
    whole = jax.ShapeDtypeStruct((rows, LEN, D), b16)
    dma = pltpu.SemaphoreType.DMA
    return pl.pallas_call(
        front_kernel,
        grid=(PAIRS, rows),
        in_specs=[
            smem,
            smem,
            pl.BlockSpec((CAP, HALF, D), lambda h, r: (0, 0, 0), pipeline_mode=pl.Buffered(1)),
            pl.BlockSpec((PIECES, D), lambda h, r: (0, 0)),
            any_spec,
            any_spec,
        ],
        out_specs=[any_spec] * 5
        + [
            pl.BlockSpec((PAIR, tokens), lambda h, r: (h, 0)),
            pl.BlockSpec((PAIR, tokens), lambda h, r: (h, 0)),
            pl.BlockSpec((tokens, PAIR), lambda h, r: (0, h)),
            pl.BlockSpec((2, LEN, LEN), lambda h, r: (h * 2 + r, 0, 0)),
            pl.BlockSpec((1, 2, LEN), lambda h, r: (h * 2 + r, 0, 0)),
            pl.BlockSpec((PAIR, LEN), lambda h, r: (h, r)),
            pl.BlockSpec((LEN, PAIR), lambda h, r: (r, h)),
        ],
        out_shape=[
            whole,
            whole,
            jax.ShapeDtypeStruct((tokens, D), b16),
            jax.ShapeDtypeStruct((PAIRS, D, WIDE), b16),
            jax.ShapeDtypeStruct((REST, D, D), b16),
            jax.ShapeDtypeStruct((D, tokens), b16),
            jax.ShapeDtypeStruct((D, tokens), b16),
            jax.ShapeDtypeStruct((tokens, D), b16),
            jax.ShapeDtypeStruct((rows * HEADS, LEN, LEN), b16),
            jax.ShapeDtypeStruct((rows * PAIRS, 2, LEN), f32),
            jax.ShapeDtypeStruct((D, tokens), b16),
            jax.ShapeDtypeStruct((tokens, D), b16),
        ],
        scratch_shapes=[
            pltpu.SMEM((PIECES,), jnp.int32),
            pltpu.VMEM((rows, LEN, D), b16),
            pltpu.VMEM((tokens, D), b16),
            pltpu.VMEM((tokens, PAIR), b16),
            pltpu.VMEM((PAIR, tokens), b16),
            pltpu.VMEM((CAP, HALF, D), b16),
        ]
        + [pltpu.VMEM((FLOWS, CAP, NEAR, wide * PAIR), b16) for unused, wide in GROUPS]
        + [pltpu.VMEM((FLOWS, 2 * CAP, KEEP, wide * PAIR), b16) for unused, wide in GROUPS]
        + [
            pltpu.VMEM((PAIRS, D, WIDE), b16),
            pltpu.VMEM((FLOWS, 2, PAIRS, KEEP, WIDE), b16),
            pltpu.VMEM((REST, D, D), b16),
            pltpu.VMEM((FLOWS, 2, REST, KEEP, D), b16),
            dma((CHUNKS, FLOWS, 3)),
            dma((CHUNKS, FLOWS, 3)),
            dma((PAIRS, FLOWS, 6)),
            dma((PAIRS, FLOWS, 6)),
            dma((REST, FLOWS, 6)),
            dma((REST, FLOWS, 6)),
            dma((2,)),
            dma((2,)),
            dma((2,)),
            dma((PAIRS + REST + 2,)),
        ],
        compiler_params=pltpu.CompilerParams(
            collective_id=0, has_side_effects=True, vmem_limit_bytes=60 * MIB
        ),
        name="front",
    )(owner, lengths, master, vectors, inputs, cotangent)


class Sum:
    steps = 7

    def __init__(self, place, work, wide, narrow, sems, send_pair, add_own):
        self.place, self.work, self.wide, self.narrow, self.sems = place, work, wide, narrow, sems
        self.send_pair, self.add_own = send_pair, add_own

    def column(self, flow):
        rows = rows_at(self.place.flow(flow)[4], KEEP)

        def read():
            return self.work[:, rows]

        def write(value):
            self.work[:, rows] = value

        sems = (self.sems[0].at[flow, pl.ds(2, 3)], self.sems[1].at[flow, pl.ds(2, 3)])
        land = self.narrow.at[flow, pl.ds(1, 2)]
        return Column(self.place, self.work.at[:, rows], read, write, land, sems)

    def copy(self, flow, index):
        first, second, near, far, keep, give = self.place.flow(flow)
        source, target, device = [
            (self.work.at[:, rows_at(far, NEAR)], self.wide.at[flow], first),
            (self.work.at[:, rows_at(give, KEEP)], self.narrow.at[flow, 0], second),
        ][index]
        return remote(
            source,
            target,
            self.sems[0].at[flow, index],
            self.sems[1].at[flow, index],
            self.place.partners[device],
        )

    def add(self, rows, value):
        self.work[:, rows] = (self.work[:, rows].astype(f32) + value.astype(f32)).astype(b16)

    def step(self, index):
        if index == 0:
            self.send_pair().start()
        if index == 1:
            self.send_pair().wait()
            self.add_own()
        for flow in range(FLOWS):
            first, second, near, far, keep, give = self.place.flow(flow)
            if index == 1:
                self.copy(flow, 0).start()
            if index == 2:
                self.copy(flow, 0).wait()
                self.add(rows_at(near, NEAR), self.wide[flow])
                self.copy(flow, 1).start()
            if index == 3:
                self.copy(flow, 1).wait()
                self.add(rows_at(keep, KEEP), self.narrow[flow, 0])
        if index >= 3:
            columns = [self.column(flow) for flow in range(FLOWS)]
            column_step(self.place, columns, index - 3)


class Gather:
    steps = 3

    def __init__(self, place, work, narrow, wide, sems):
        self.place, self.work, self.narrow, self.wide = place, work, narrow, wide
        self.sems = sems

    def copy(self, flow, index):
        first, second, near, far, keep, give = self.place.flow(flow)
        rows, target, device = [
            (rows_at(keep, KEEP), self.narrow, second),
            (rows_at(near, NEAR), self.wide, first),
        ][index]
        return remote(
            self.work.at[:, rows],
            target.at[flow],
            self.sems[0].at[flow, 5 + index],
            self.sems[1].at[flow, 5 + index],
            self.place.partners[device],
        )

    def step(self, index):
        for flow in range(FLOWS):
            first, second, near, far, keep, give = self.place.flow(flow)
            if index > 0:
                self.copy(flow, index - 1).wait()
            if index == 1:
                self.work[:, rows_at(give, KEEP)] = self.narrow[flow]
            if index == 2:
                self.work[:, rows_at(far, NEAR)] = self.wide[flow]
            if index < 2:
                self.copy(flow, index).start()


class Hand:
    steps = 3

    def __init__(self, place, table, work, bag, gift, pack, last, own, out, sems, store_sems):
        self.place, self.table, self.work = place, table, work
        self.bag, self.gift, self.pack, self.last, self.own = bag, gift, pack, last, own
        self.out, self.sems, self.store_sems = out, sems, store_sems

    def tile(self, chip, rank, rows):
        return self.work[self.table[chip * CAP + rank], rows]

    def copy(self, flow, index):
        first, second = self.place.flow(flow)[:2]
        source, target, device = [
            (self.bag.at[flow], self.gift.at[flow], second),
            (self.pack.at[flow], self.last.at[flow], first),
        ][index]
        return remote(
            source,
            target,
            self.sems[0].at[flow, index],
            self.sems[1].at[flow, index],
            self.place.partners[device],
        )

    def stores(self, flow):
        first, second, near, far, keep, give = self.place.flow(flow)
        parts = [
            (self.own.at[flow], rows_at(keep, KEEP)),
            (self.gift.at[flow, pl.ds(0, CAP)], rows_at(give, KEEP)),
            (self.last.at[flow], rows_at(far, NEAR)),
        ]
        return [
            pltpu.make_async_copy(source, self.out.at[:, rows], self.store_sems.at[flow, index])
            for index, (source, rows) in enumerate(parts)
        ]

    def step(self, index):
        for flow in range(FLOWS):
            first, second, near, far, keep, give = self.place.flow(flow)
            rows = rows_at(keep, KEEP)
            if index == 0:
                beside = self.place.chips[second]
                across = beside + self.place.chips[first] - self.place.me
                for rank in range(CAP):
                    self.bag[flow, rank] = self.tile(beside, rank, rows)
                    self.bag[flow, CAP + rank] = self.tile(across, rank, rows)
                    self.own[flow, rank] = self.tile(self.place.me, rank, rows)
                self.copy(flow, 0).start()
            if index == 1:
                self.copy(flow, 0).wait()
                for rank in range(CAP):
                    mine = self.tile(self.place.chips[first], rank, rows)
                    self.pack[flow, rank, rows_at(keep - near, KEEP)] = mine
                    self.pack[flow, rank, rows_at(give - near, KEEP)] = self.gift[flow, CAP + rank]
                self.copy(flow, 1).start()
            if index == 2:
                self.copy(flow, 1).wait()
                for copy in self.stores(flow):
                    copy.start()


BACK_STEPS = 2 * PAIRS
BACK_TAIL = 4
BACK_PAIRS = tuple((index, 1) for index in range(PAIRS))
BACK_REST = (0, 0, 1, 2, 2, 3, 4, 4, 5)
BACK_HAND = 12


def back_kernel(
    table, p_ref, r_ref, v_ref, q_ref, k_ref, o_ref, g_ref, w_ref, n_ref, x_ref, z_ref, vec_ref,
    tiles_in, sums_in, y_in,
    y_out, i_out, pairs_out, slots_out, sums_ref,
    grad_sum, wide_sum, turned, block_out,
    two, two_wide, two_narrow, two_stage, one, one_wide, one_narrow, one_send_stage, one_stage,
    gather_narrow, gather_wide,
    bag, gift, pack, last, own, vec_land,
    two_send, two_recv, one_send, one_recv, hand_send, hand_recv, hand_store,
    pair_two_send, pair_two_recv, pair_one_send, pair_one_recv, load_sem, store_sem,
    swap_send, swap_recv, swap_local, vec_send, vec_recv,
):
    step = pl.program_id(0)
    place = Place()
    rows, span = y_in.shape[0], y_in.shape[1] // 2
    near_half = rows_at(place.core * HALF, HALF)
    far_half = rows_at(place.other * HALF, HALF)

    def load_two(group):
        first, count = REST_GROUPS[group]
        return pltpu.make_async_copy(
            tiles_in.at[pl.ds(first, count), near_half],
            two_stage.at[pl.ds(group % 3, 1)],
            load_sem.at[group % 3],
        )

    def rest_sum(group):
        first, count = REST_GROUPS[group]
        span_of = pl.ds(first, count)
        work = two.at[span_of]

        def send_pair():
            return remote(
                tiles_in.at[span_of, far_half],
                work,
                pair_two_send.at[group],
                pair_two_recv.at[group],
                place.twin,
            )

        def add_own():
            load_two(group).wait()
            work[...] = (work[...].astype(f32) + two_stage[group % 3].astype(f32)).astype(b16)

        sems = (two_send.at[group], two_recv.at[group])
        wide, narrow = two_wide.at[:, span_of], two_narrow.at[:, :, span_of]
        return Sum(place, work, wide, narrow, sems, send_pair, add_own)

    def pair_sum(group):
        first, count = BACK_PAIRS[group]
        span_of = pl.ds(first, count)
        work = one.at[span_of]

        def send_pair():
            return remote(
                one_send_stage.at[span_of],
                work,
                pair_one_send.at[group],
                pair_one_recv.at[group],
                place.twin,
            )

        def add_own():
            own = one_stage[span_of].astype(f32)
            work[...] = (work[...].astype(f32) + own).astype(b16)

        sems = (one_send.at[group], one_recv.at[group])
        wide, narrow = one_wide.at[:, span_of], one_narrow.at[:, :, span_of]
        return Sum(place, work, wide, narrow, sems, send_pair, add_own)

    def pair_gather(group):
        first, count = BACK_PAIRS[group]
        span_of = pl.ds(first, count)
        sems = (one_send.at[group], one_recv.at[group])
        narrow, wide = gather_narrow.at[:, span_of], gather_wide.at[:, span_of]
        return Gather(place, one.at[span_of], narrow, wide, sems)

    hand = Hand(
        place, table, two, bag, gift, pack, last, own, slots_out, (hand_send, hand_recv), hand_store
    )

    def pair_store(index, tile):
        return pltpu.make_async_copy(
            one.at[index, :, pl.ds(tile * PAIR, PAIR)],
            pairs_out.at[tile, :, pl.ds(index * PAIR, PAIR)],
            store_sem.at[index, tile],
        )

    def tick(number, odd):
        for group, start in enumerate(BACK_REST):
            if group % 2 == odd and 0 <= number - start < Sum.steps:
                rest_sum(group).step(number - start)
        for group, (first, count) in enumerate(BACK_PAIRS):
            if group % 2 != odd:
                continue
            start = 2 * (first + count)
            if 0 <= number - start < Sum.steps:
                pair_sum(group).step(number - start)
            if 0 <= number - start - Sum.steps + 1 < Gather.steps:
                pair_gather(group).step(number - start - Sum.steps + 1)
            if number == start + Sum.steps + 1:
                for index in range(first, first + count):
                    for tile in range(3):
                        pair_store(index, tile).start()
        if odd == 0 and 0 <= number - BACK_HAND < Hand.steps:
            hand.step(number - BACK_HAND)
        for group, start in enumerate(BACK_REST):
            if odd == 1 and number == max(start - 1, 0):
                load_two(group).start()

    def both(number):
        tick(number, 0)
        tick(number, 1)

    def swap_y(index):
        there = pl.ds(place.core * rows, rows)
        if index == 0:
            return pltpu.make_async_copy(
                y_in.at[:, pl.ds(place.core * span, span)], y_out.at[there], swap_local.at[0]
            )
        return remote(
            y_in.at[:, pl.ds(place.other * span, span)],
            y_out.at[there],
            swap_send.at[0],
            swap_recv.at[0],
            place.twin,
        )

    @pl.when(step == 0)
    def lead():
        place.greet()
        for index in range(2):
            swap_y(index).start()
        sums_ref[...] = sums_in[...]

    for number in range(BACK_STEPS + BACK_TAIL):
        early = partial(tick, number, 0) if number < BACK_STEPS else partial(both, number)
        pl.when(step == number)(early)

    half = LEN // 2
    pair, row = step // 2, lax.rem(step, 2)

    def attention(head):
        part = slice(head * HEAD_DIM, (head + 1) * HEAD_DIM)
        values = head_only(v_ref[...], head)
        recip = r_ref[0, head : head + 1, :]
        grad = g_ref[part, :].astype(f32) * recip
        delta = jnp.sum(grad * o_ref[part, :].astype(f32), 0, keepdims=True)
        grad = grad.astype(b16)
        doubled = jnp.concatenate([grad, grad], axis=0)
        value_grad, key_grad = [], []
        for which in range(2):
            cols = slice(which * half, (which + 1) * half)
            weights = p_ref[head, :, cols]
            slope = dot_nn(values, doubled[:, cols]) - delta[:, cols]
            slope = (weights.astype(f32) * slope).astype(b16)
            value_grad.append(dot_nt(grad[:, cols], weights))
            key_grad.append(dot_nt(q_ref[part, cols], slope))
            query_grad = dot_nn(k_ref[part, :], slope) * (HEAD_DIM**-0.5)
            turned[part, cols] = query_grad.astype(b16)
        lower = slice(PAIR + head * HEAD_DIM, PAIR + (head + 1) * HEAD_DIM)
        turned[lower, :] = ((key_grad[0] + key_grad[1]) * (1.0 / LOG2E)).astype(b16)
        lower = slice(2 * PAIR + head * HEAD_DIM, 2 * PAIR + (head + 1) * HEAD_DIM)
        turned[lower, :] = (value_grad[0] + value_grad[1]).astype(b16)

    @pl.when(step < BACK_STEPS)
    def first_head():
        attention(0)

    for number in range(BACK_STEPS):
        pl.when(step == number)(partial(tick, number, 1))

    @pl.when(step < BACK_STEPS)
    def second_head():
        attention(1)
        where = pl.ds(pl.multiple_of(row * LEN, LEN), LEN)
        block = dot_nn(turned[...], n_ref[where])
        back = turned[...].T
        lanes = pl.ds(pl.multiple_of(pair * PAIR, PAIR), PAIR)
        ones = jnp.sum(back.astype(f32), 0, keepdims=True)
        sums_ref[4:5, lanes] += ones[:, :PAIR]
        sums_ref[5:6, lanes] += ones[:, 2 * PAIR :]
        term = dot_nt(back, w_ref[0])

        @pl.when(pair == 0)
        def begin():
            grad_sum[where] = term

        @pl.when(pair > 0)
        def add():
            grad_sum[where] += term

        @pl.when(row == 0)
        def keep():
            wide_sum[...] = block

        @pl.when(row == 1)
        def hand_on():
            whole = (wide_sum[...] + block).T
            low = whole.astype(b16)
            for core in range(2):

                @pl.when(place.core == core)
                def split():
                    one_stage[pair] = low[core * HALF : (core + 1) * HALF]
                    one_send_stage[pair] = low[(1 - core) * HALF : (2 - core) * HALF]

    def store_block(index):
        row, half = index // 2, index % 2
        target = i_out.at[place.core * rows + row]
        local = pltpu.make_async_copy(block_out.at[index], target, swap_local.at[1 + row])
        far = remote(
            block_out.at[index], target, swap_send.at[1 + row], swap_recv.at[1 + row], place.twin
        )
        return local, far, half

    for index in range(BACK_TAIL):

        @pl.when(step == BACK_STEPS + index)
        def close():
            size = LEN // 2
            grad = grad_sum[index * size : (index + 1) * size]
            unit, rstd = norm_parts(x_ref[...].astype(f32))
            sums_ref[0:1, :] += jnp.sum(grad * unit, 0, keepdims=True)
            sums_ref[1:2, :] += jnp.sum(grad, 0, keepdims=True)
            total = z_ref[...].astype(f32) + norm_back(grad, unit, rstd, vec_ref[0:1, :])
            block_out[index] = total.astype(b16)
            local, far, half = store_block(index)

            @pl.when(place.core == half)
            def keep():
                local.start()

            @pl.when(place.core != half)
            def give():
                far.start()

    @pl.when(step == BACK_STEPS + BACK_TAIL - 1)
    def drain():
        devices = [place.twin] + place.partners

        def vector(index):
            return remote(
                sums_ref, vec_land.at[index], vec_send.at[index], vec_recv.at[index], devices[index]
            )

        vector(0).start()
        for number in range(BACK_STEPS + BACK_TAIL, BACK_STEPS + Sum.steps + Gather.steps):
            both(number)
            index = number - BACK_STEPS - BACK_TAIL
            if index < 5:
                vector(index).wait()
                sums_ref[...] += vec_land[index]
                if index < 4:
                    vector(index + 1).start()
        for index in range(2):
            swap_y(index).wait()
        for index in range(BACK_TAIL):
            local, far, half = store_block(index)

            @pl.when(place.core == half)
            def keep():
                local.wait()

            @pl.when(place.core != half)
            def give():
                far.wait()

        for index in range(PAIRS):
            for tile in range(3):
                pair_store(index, tile).wait()
        for flow in range(FLOWS):
            for copy in hand.stores(flow):
                copy.wait()


def back(table, attention, weights, normed, x, residual, vectors, tiles, sums, y):
    rows, length = y.shape[:2]
    tokens = rows * length
    any_spec = pl.BlockSpec(memory_space=pl.ANY)
    smem = pl.BlockSpec(memory_space=pltpu.SMEM)
    dma = pltpu.SemaphoreType.DMA

    def now(step):
        return jnp.minimum(step, BACK_STEPS - 1)

    def tail(step):
        return jnp.maximum(step - BACK_STEPS, 0)

    head_block = pl.BlockSpec((PAIR, LEN), lambda s: (now(s) // 2, lax.rem(now(s), 2)))
    tail_block = pl.BlockSpec((LEN // 2, D), lambda s: (tail(s), 0))
    whole = pl.BlockSpec((PIECES, D), lambda s: (0, 0))
    sums_block = pl.BlockSpec((16, D), lambda s: (0, 0))
    return pl.pallas_call(
        back_kernel,
        grid=(BACK_STEPS + BACK_TAIL,),
        in_specs=[
            smem,
            pl.BlockSpec((2, LEN, LEN), lambda s: (now(s), 0, 0)),
            pl.BlockSpec((1, 2, LEN), lambda s: (now(s), 0, 0)),
            pl.BlockSpec((LEN, PAIR), lambda s: (lax.rem(now(s), 2), now(s) // 2)),
            head_block,
            head_block,
            head_block,
            head_block,
            pl.BlockSpec((1, D, WIDE), lambda s: (now(s) // 2, 0, 0)),
            pl.BlockSpec((tokens, D), lambda s: (0, 0), pipeline_mode=pl.Buffered(1)),
            tail_block,
            tail_block,
            whole,
            any_spec,
            sums_block,
            any_spec,
        ],
        out_specs=[any_spec] * 4 + [sums_block],
        out_shape=[
            jax.ShapeDtypeStruct((2 * rows, length // 2, D), b16),
            jax.ShapeDtypeStruct((2 * rows, length // 2, D), b16),
            jax.ShapeDtypeStruct((3, HALF, D), b16),
            jax.ShapeDtypeStruct((CAP, HALF, D), b16),
            jax.ShapeDtypeStruct((16, D), f32),
        ],
        scratch_shapes=[
            pltpu.VMEM((tokens, D), f32),
            pltpu.VMEM((WIDE, D), f32),
            pltpu.VMEM((WIDE, LEN), b16),
            pltpu.VMEM((BACK_TAIL, LEN // 2, D), b16),
            pltpu.VMEM((REST, HALF, D), b16),
            pltpu.VMEM((FLOWS, REST, NEAR, D), b16),
            pltpu.VMEM((FLOWS, 3, REST, KEEP, D), b16),
            pltpu.VMEM((3, HALF, D), b16),
            pltpu.VMEM((PAIRS, HALF, WIDE), b16),
            pltpu.VMEM((FLOWS, PAIRS, NEAR, WIDE), b16),
            pltpu.VMEM((FLOWS, 3, PAIRS, KEEP, WIDE), b16),
            pltpu.VMEM((PAIRS, HALF, WIDE), b16),
            pltpu.VMEM((PAIRS, HALF, WIDE), b16),
            pltpu.VMEM((FLOWS, PAIRS, KEEP, WIDE), b16),
            pltpu.VMEM((FLOWS, PAIRS, NEAR, WIDE), b16),
            pltpu.VMEM((FLOWS, 2 * CAP, KEEP, D), b16),
            pltpu.VMEM((FLOWS, 2 * CAP, KEEP, D), b16),
            pltpu.VMEM((FLOWS, CAP, NEAR, D), b16),
            pltpu.VMEM((FLOWS, CAP, NEAR, D), b16),
            pltpu.VMEM((FLOWS, CAP, KEEP, D), b16),
            pltpu.VMEM((5, 16, D), f32),
            dma((REST, FLOWS, 5)),
            dma((REST, FLOWS, 5)),
            dma((PAIRS, FLOWS, 7)),
            dma((PAIRS, FLOWS, 7)),
            dma((FLOWS, 2)),
            dma((FLOWS, 2)),
            dma((FLOWS, 3)),
            dma((REST,)),
            dma((REST,)),
            dma((PAIRS,)),
            dma((PAIRS,)),
            dma((3,)),
            dma((PAIRS, 3)),
            dma((3,)),
            dma((3,)),
            dma((3,)),
            dma((5,)),
            dma((5,)),
        ],
        compiler_params=pltpu.CompilerParams(
            collective_id=1, has_side_effects=True, vmem_limit_bytes=62 * MIB
        ),
        name="back",
    )(table, *attention, weights, normed, x, residual, vectors, tiles, sums, y)


def update_kernel(tile_at, one, two, w_ref, m_ref, s_ref, y_in, i_in, w_out, m_out, s_out, y_out, i_out):
    step = pl.program_id(0)
    tile = tile_at[step // 2]
    grad = jnp.where(tile < 3, one[0], two[0]).astype(f32)
    parts = adam_step(w_ref[0], grad, m_ref[0], s_ref[0], RATE)
    for target, part in zip((w_out, m_out, s_out), parts):
        target[0] = jnp.where(tile >= 0, part, jnp.zeros_like(part))

    @pl.when(step < 4)
    def widen():
        y_out[...] = y_in[...].astype(f32)
        i_out[...] = i_in[...].astype(f32)


def update(tile_at, one, two, master, first, second, y, grad):
    tokens = y.shape[0]
    size = HALF // 2
    state = pl.BlockSpec((1, size, D), lambda s, tile_at: (s // 2, lax.rem(s, 2), 0))
    wide = pl.BlockSpec((tokens // 4, D), lambda s, tile_at: (jnp.minimum(s, 3), 0))
    return pl.pallas_call(
        update_kernel,
        grid_spec=pltpu.PrefetchScalarGridSpec(
            num_scalar_prefetch=1,
            grid=(CAP * 2,),
            in_specs=[
                pl.BlockSpec(
                    (1, size, D),
                    lambda s, tile_at: (jnp.clip(tile_at[s // 2], 0, 2), lax.rem(s, 2), 0),
                ),
                state,
                state,
                state,
                state,
                wide,
                wide,
            ],
            out_specs=[state] * 3 + [wide] * 2,
        ),
        out_shape=[jax.ShapeDtypeStruct(master.shape, f32)] * 3
        + [jax.ShapeDtypeStruct((tokens, D), f32)] * 2,
        compiler_params=pltpu.CompilerParams(vmem_limit_bytes=60 * MIB),
        name="update",
    )(tile_at, one, two, master, first, second, y, grad)


def shards_paired(
    inputs,
    cotangent,
    doc_lengths,
    owner_list,
    master,
    first_moment,
    second_moment,
    vectors,
    vector_first,
    vector_second,
):
    rows_here, span, width = inputs.shape
    place = lax.axis_index("blk")
    member = lax.axis_index("dp")
    rows_mine = rows_here // 2
    order = jnp.arange(PIECES)
    same_owner = owner_list[:, None] == owner_list[None, :]
    ranks = jnp.sum(same_owner & (order[None, :] < order[:, None]), axis=1).astype(jnp.int32)
    slot_of = owner_list * CAP + ranks
    front_outs = front(owner_list, doc_lengths, master, vectors, inputs, cotangent)
    x, cot, normed, weights_one, weights_two, queries, keys, values = front_outs[:8]
    weights, recips, context_turned, context = front_outs[8:]
    x = x.reshape(-1, width)
    cot = cot.reshape(-1, width)
    block_out, residual, grad_context, sums, tiles_two = feed(
        context, context_turned, x, cot, weights_two, vectors
    )
    hits = jnp.arange(16 * CAP)[:, None] == slot_of[None, :]
    tile_at = jnp.sum(jnp.where(hits, order[None, :] + 1, 0), axis=1).astype(jnp.int32) - 1
    table = jnp.maximum(tile_at - 3, 0)
    block_out, input_grad, total_one, total_two, vector_total = back(
        table,
        (weights, recips, values, queries, keys, context_turned, grad_context),
        weights_one,
        normed,
        x,
        residual,
        vectors,
        tiles_two,
        sums,
        block_out.reshape(rows_mine, LEN, width),
    )
    mine = lax.dynamic_slice_in_dim(tile_at, member * CAP, CAP, 0)
    *updated, block_out, input_grad = update(
        mine,
        total_one,
        total_two,
        master,
        first_moment,
        second_moment,
        block_out.reshape(-1, width),
        input_grad.reshape(-1, width),
    )
    columns = vector_first.shape[1]
    vector_cols = lax.dynamic_slice_in_dim(vectors, place * columns, columns, 1)
    vector_total = lax.dynamic_slice(vector_total, (0, place * columns), (PIECES, columns))
    updated_vectors = adam_step(vector_cols, vector_total, vector_first, vector_second, VEC_RATE)
    return (
        block_out.reshape(inputs.shape),
        input_grad.reshape(inputs.shape),
        *updated,
        *updated_vectors,
    )


def solution(mesh):
    in_specs = (
        P("dp", "blk", None),
        P("dp", "blk", None),
        P("dp", None),
        P(),
        P("dp", "blk", None),
        P("dp", "blk", None),
        P("dp", "blk", None),
        P(),
        P(None, "blk"),
        P(None, "blk"),
    )
    out_specs = (
        P("dp", "blk", None),
        P("dp", "blk", None),
        P("dp", "blk", None),
        P("dp", "blk", None),
        P("dp", "blk", None),
        P(None, "blk"),
        P(None, "blk"),
        P(None, "blk"),
    )
    paired = mesh.shape["blk"] == 2 and mesh.shape["dp"] == 16
    shards = shards_paired if paired else shards_any
    return jax.shard_map(shards, mesh=mesh, in_specs=in_specs, out_specs=out_specs, check_vma=False)
```

```python
from functools import partial

import jax
import jax.numpy as jnp
from jax import lax
from jax.experimental import pallas as pl
from jax.experimental.pallas import tpu as pltpu
from jax.sharding import PartitionSpec as P

D = 768
FF = 3072
HEADS = 12
HEAD_DIM = 64
LEN = 1024
CAP = 3
STEP = 10
PIECES = 12


EPS_NORM = 1e-05
BETA_ONE = 0.9
BETA_TWO = 0.999
RATE = 0.04
VEC_RATE = 0.25
DECAY = 0.01
ADAM_EPS = 1e-08


def normalize(values_in, gain, shift):
    center = jnp.mean(values_in, axis=-1, keepdims=True)
    offset = values_in - center
    spread = jnp.mean(offset * offset, axis=-1, keepdims=True)
    return offset * lax.rsqrt(spread + EPS_NORM) * gain + shift


def adam_step(weight, grad, first, second, rate):
    first_new = BETA_ONE * first + (1.0 - BETA_ONE) * grad
    second_new = BETA_TWO * second + (1.0 - BETA_TWO) * grad * grad
    corrected = (
        first_new
        / (1.0 - BETA_ONE**STEP)
        / (jnp.sqrt(second_new / (1.0 - BETA_TWO**STEP)) + ADAM_EPS)
    )
    return (weight - rate * (corrected + DECAY * weight), first_new, second_new)


def shards_any(
    inputs,
    cotangent,
    doc_lengths,
    owner_list,
    master,
    first_moment,
    second_moment,
    vectors,
    vector_first,
    vector_second,
):
    rows_here, span, width = inputs.shape
    tokens_here = rows_here * span
    fold = FF // D
    scale = HEAD_DIM ** (-0.5)
    place = lax.axis_index("blk")
    f32 = jnp.float32
    b16 = jnp.bfloat16
    order = jnp.arange(PIECES)
    same_owner = owner_list[:, None] == owner_list[None, :]
    ranks = jnp.sum(same_owner & (order[None, :] < order[:, None]), axis=1)
    slot_of = owner_list * CAP + ranks

    mine = (owner_list == lax.axis_index("dp"))[:, None, None]
    tile_rows = lax.psum(jnp.where(mine, master[ranks], 0.0).astype(b16), "dp")
    tiles = lax.all_gather(tile_rows, "blk", axis=1, tiled=True)
    query_weight = tiles[0]
    key_weight = tiles[1]
    value_weight = tiles[2]
    out_weight = tiles[3]
    up_weight = jnp.transpose(tiles[4 : 4 + fold], (1, 0, 2)).reshape(width, FF)
    down_weight = tiles[4 + fold :].reshape(FF, width)
    flat_in = inputs.reshape(tokens_here, width).astype(f32)
    normed_one = normalize(flat_in, vectors[0], vectors[1]).astype(b16)
    queries = (jnp.dot(normed_one, query_weight, preferred_element_type=f32) + vectors[4]).astype(
        b16
    )
    keys_here = jnp.dot(normed_one, key_weight, preferred_element_type=f32).astype(b16)
    values_here = (
        jnp.dot(normed_one, value_weight, preferred_element_type=f32) + vectors[5]
    ).astype(b16)
    query_heads = queries.reshape(rows_here, span, HEADS, HEAD_DIM)
    first_len = doc_lengths[:, 0]
    query_seg = (place * span + jnp.arange(span))[None, :] >= first_len[:, None]

    def block_scores(key_block, start):
        count = key_block.shape[1]
        key_heads = key_block.reshape(rows_here, count, HEADS, HEAD_DIM)
        raw = (
            jnp.einsum("rqhd,rkhd->rhqk", query_heads, key_heads, preferred_element_type=f32)
            * scale
        )
        key_seg = (start + jnp.arange(count))[None, :] >= first_len[:, None]
        allowed = query_seg[:, None, :, None] == key_seg[:, None, None, :]
        return (raw, allowed)

    key_rows = keys_here.reshape(rows_here, span, width)
    value_rows = values_here.reshape(rows_here, span, width)
    top = jnp.full((rows_here, HEADS, span), -1e30, f32)
    key_block = lax.all_gather(key_rows, "blk", axis=1, tiled=True)
    value_block = lax.all_gather(value_rows, "blk", axis=1, tiled=True)
    count = key_block.shape[1]
    raw, allowed = block_scores(key_block, jnp.int32(0))
    new_top = jnp.maximum(top, jnp.max(jnp.where(allowed, raw, -1e30), axis=-1))
    weights = jnp.where(allowed, jnp.exp(raw - new_top[..., None]), 0.0)
    value_heads = value_block.reshape(rows_here, count, HEADS, HEAD_DIM)
    update = jnp.einsum(
        "rhqk,rkhd->rhqd", weights.astype(b16), value_heads, preferred_element_type=f32
    )
    total = jnp.sum(weights, axis=-1)
    log_total = new_top + jnp.log(total)
    context_raw = update / total[..., None]
    context_low = jnp.transpose(context_raw, (0, 2, 1, 3)).reshape(tokens_here, width).astype(b16)
    residual = flat_in + (jnp.dot(context_low, out_weight, preferred_element_type=f32) + vectors[6])
    normed_two = normalize(residual, vectors[2], vectors[3]).astype(b16)
    hidden = jnp.dot(normed_two, up_weight, preferred_element_type=f32) + vectors[8:].reshape(FF)
    gelu_exact = partial(jax.nn.gelu, approximate=False)
    active, gelu_pull = jax.vjp(gelu_exact, hidden)
    active_low = active.astype(b16)
    block_out = (
        residual + (jnp.dot(active_low, down_weight, preferred_element_type=f32) + vectors[7])
    ).reshape(rows_here, span, width)
    grad_out = cotangent.reshape(tokens_here, width)
    down_grad = jnp.einsum("tf,td->fd", active_low, grad_out, preferred_element_type=f32)
    down_sum = jnp.sum(grad_out, axis=0, dtype=f32)
    grad_active = jnp.einsum("td,fd->tf", grad_out, down_weight, preferred_element_type=f32)
    grad_hidden = gelu_pull(grad_active)[0].astype(b16)
    up_grad = jnp.einsum("td,tf->df", normed_two, grad_hidden, preferred_element_type=f32)
    up_sum = jnp.sum(grad_hidden, axis=0, dtype=f32)
    ffn_tiles = jnp.concatenate(
        [
            jnp.transpose(up_grad.reshape(width, fold, width), (1, 0, 2)),
            down_grad.reshape(fold, width, width),
        ],
        axis=0,
    )
    grad_normed_two = jnp.einsum("tf,df->td", grad_hidden, up_weight, preferred_element_type=f32)
    unused, second_pull = jax.vjp(normalize, residual, vectors[2], vectors[3])
    residual_part, gain_two_grad, shift_two_grad = second_pull(grad_normed_two)
    grad_residual = grad_out.astype(f32) + residual_part
    grad_attended = grad_residual.astype(b16)
    out_grad = jnp.einsum("tm,td->md", context_low, grad_attended, preferred_element_type=f32)
    out_sum = jnp.sum(grad_attended, axis=0, dtype=f32)
    grad_context = jnp.einsum(
        "td,md->tm", grad_attended, out_weight, preferred_element_type=f32
    ).astype(b16)
    grad_heads = grad_context.reshape(rows_here, span, HEADS, HEAD_DIM)
    delta = jnp.einsum("rqhd,rhqd->rhq", grad_heads.astype(f32), context_raw)
    key_all, value_all = (
        lax.all_gather(key_rows, "blk", axis=1, tiled=True),
        lax.all_gather(value_rows, "blk", axis=1, tiled=True),
    )
    key_size = min(512, LEN)

    def back_block(index, carry):
        grad_query, key_total, value_total = carry
        start = index * key_size
        key_block = lax.dynamic_slice_in_dim(key_all, start, key_size, 1)
        value_block = lax.dynamic_slice_in_dim(value_all, start, key_size, 1)
        raw, allowed = block_scores(key_block, start)
        weights_back = jnp.where(allowed, jnp.exp(raw - log_total[..., None]), 0.0)
        key_heads = key_block.reshape(rows_here, key_size, HEADS, HEAD_DIM)
        value_heads = value_block.reshape(rows_here, key_size, HEADS, HEAD_DIM)
        value_grad = jnp.einsum(
            "rhqk,rqhd->rkhd", weights_back.astype(b16), grad_heads, preferred_element_type=f32
        )
        weight_grad = jnp.einsum(
            "rqhd,rkhd->rhqk", grad_heads, value_heads, preferred_element_type=f32
        )
        score_grad = (weights_back * (weight_grad - delta[..., None])).astype(b16)
        grad_query = (
            grad_query
            + jnp.einsum("rhqk,rkhd->rqhd", score_grad, key_heads, preferred_element_type=f32)
            * scale
        )
        key_grad = (
            jnp.einsum("rhqk,rqhd->rkhd", score_grad, query_heads, preferred_element_type=f32)
            * scale
        )
        key_total = lax.dynamic_update_slice_in_dim(
            key_total, key_grad.reshape(rows_here, key_size, width), start, 1
        )
        value_total = lax.dynamic_update_slice_in_dim(
            value_total, value_grad.reshape(rows_here, key_size, width), start, 1
        )
        return (grad_query, key_total, value_total)

    zero_rows = jnp.zeros((rows_here, LEN, width), f32)
    grad_query, key_total, value_total = lax.fori_loop(
        0,
        LEN // key_size,
        back_block,
        (jnp.zeros((rows_here, span, HEADS, HEAD_DIM), f32), zero_rows, zero_rows),
    )
    key_grad_here, value_grad_here = (
        lax.psum_scatter(
            key_total.astype(jnp.bfloat16), "blk", scatter_dimension=1, tiled=True
        ).astype(jnp.float32),
        lax.psum_scatter(
            value_total.astype(jnp.bfloat16), "blk", scatter_dimension=1, tiled=True
        ).astype(jnp.float32),
    )
    query_low = grad_query.reshape(tokens_here, width).astype(b16)
    key_low = key_grad_here.reshape(tokens_here, width).astype(b16)
    value_low = value_grad_here.reshape(tokens_here, width).astype(b16)
    query_tile = jnp.einsum("td,te->de", normed_one, query_low, preferred_element_type=f32)
    key_tile = jnp.einsum("td,te->de", normed_one, key_low, preferred_element_type=f32)
    value_tile = jnp.einsum("td,te->de", normed_one, value_low, preferred_element_type=f32)
    grad_normed_one = (
        jnp.einsum("te,de->td", query_low, query_weight, preferred_element_type=f32)
        + jnp.einsum("te,de->td", key_low, key_weight, preferred_element_type=f32)
        + jnp.einsum("te,de->td", value_low, value_weight, preferred_element_type=f32)
    )
    unused, first_pull = jax.vjp(normalize, flat_in, vectors[0], vectors[1])
    input_part, gain_one_grad, shift_one_grad = first_pull(grad_normed_one)
    input_grad = (grad_residual + input_part).reshape(rows_here, span, width)
    vector_grads = jnp.concatenate(
        [
            jnp.stack(
                [
                    gain_one_grad,
                    shift_one_grad,
                    gain_two_grad,
                    shift_two_grad,
                    jnp.sum(query_low, axis=0, dtype=f32),
                    jnp.sum(value_low, axis=0, dtype=f32),
                    out_sum,
                    down_sum,
                ]
            ),
            up_sum.reshape(fold, width),
        ],
        axis=0,
    )
    attn_tiles = jnp.stack([query_tile, key_tile, value_tile, out_grad])
    piece_share, vector_share = (
        lax.psum_scatter(
            jnp.concatenate([attn_tiles, ffn_tiles], axis=0).astype(jnp.bfloat16),
            "blk",
            scatter_dimension=1,
            tiled=True,
        ).astype(jnp.float32),
        lax.psum_scatter(
            vector_grads.astype(jnp.bfloat16), "blk", scatter_dimension=1, tiled=True
        ).astype(jnp.float32),
    )
    own_slots = lax.axis_index("dp") * CAP + jnp.arange(CAP)
    pick = (own_slots[:, None] == slot_of[None, :]).astype(f32)
    occupied = jnp.sum(pick, axis=1)[:, None, None]
    total_share, vector_total = (
        lax.psum(piece_share.astype(jnp.bfloat16), "dp").astype(jnp.float32),
        lax.psum(vector_share.astype(jnp.bfloat16), "dp").astype(jnp.float32),
    )
    slot_grads = jnp.einsum("cp,prd->crd", pick, total_share, precision=lax.Precision.HIGHEST)
    new_master, new_first, new_second = adam_step(
        master, slot_grads, first_moment, second_moment, RATE
    )
    columns = vector_first.shape[1]
    vector_cols = lax.dynamic_slice_in_dim(vectors, place * columns, columns, 1)
    new_vectors, new_vector_first, new_vector_second = adam_step(
        vector_cols, vector_total, vector_first, vector_second, VEC_RATE
    )
    return (
        block_out,
        input_grad,
        new_master * occupied,
        new_first * occupied,
        new_second * occupied,
        new_vectors,
        new_vector_first,
        new_vector_second,
    )


f32 = jnp.float32
b16 = jnp.bfloat16
LOG2E = 1.4426950408889634
MIB = 1024 * 1024
PAIRS = HEADS // 2
PAIR = 2 * HEAD_DIM


def dot_nn(left, right):
    return lax.dot_general(left, right, (((1,), (0,)), ((), ())), preferred_element_type=f32)


def dot_nt(left, right):
    return lax.dot_general(left, right, (((1,), (1,)), ((), ())), preferred_element_type=f32)


def dot_tn(left, right):
    return lax.dot_general(left, right, (((0,), (0,)), ((), ())), preferred_element_type=f32)


def norm_parts(values_in):
    center = jnp.mean(values_in, axis=-1, keepdims=True)
    offset = values_in - center
    spread = jnp.mean(offset * offset, axis=-1, keepdims=True)
    rstd = lax.rsqrt(spread + EPS_NORM)
    return offset * rstd, rstd


def norm_back(grad, unit, rstd, gain):
    scaled = grad * gain
    first = jnp.mean(scaled, axis=-1, keepdims=True)
    second = jnp.mean(scaled * unit, axis=-1, keepdims=True)
    return rstd * (scaled - first - unit * second)


def gelu_parts(value):
    bell = jnp.exp2(value * value * (-0.5 * LOG2E))
    ratio = pl.reciprocal(1.0 + (0.3275911 * 0.7071067811865476) * jnp.abs(value))
    poly = 0.5 * 1.061405429
    poly = poly * ratio + 0.5 * -1.453152027
    poly = poly * ratio + 0.5 * 1.421413741
    poly = poly * ratio + 0.5 * -0.284496736
    poly = poly * ratio + 0.5 * 0.254829592
    tail = poly * ratio * bell
    cdf = jnp.where(value >= 0.0, 1.0 - tail, tail)
    return value * cdf, cdf + value * (bell * 0.3989422804014327)


def head_only(block, head):
    lane = lax.broadcasted_iota(jnp.int32, block.shape, 1)
    keep = (lane >= head * HEAD_DIM) & (lane < (head + 1) * HEAD_DIM)
    return jnp.where(keep, block, jnp.zeros_like(block))


def feed_kernel(
    c_ref, o_ref, x_ref, g_ref, w_ref, vec_ref,
    y_ref, r_ref, d_ref, sums_ref, tiles_ref,
    acc_ref, out_ref, grad_ref, stage_ref, sem_ref,
):
    fold = FF // D
    step = pl.program_id(0)

    @pl.when(step == 0)
    def clear():
        acc_ref[...] = jnp.zeros_like(acc_ref)
        sums_ref[...] = jnp.zeros_like(sums_ref)

    residual = x_ref[...].astype(f32) + (dot_nn(c_ref[...], w_ref[0]) + vec_ref[6:7, :])
    unit, rstd = norm_parts(residual)
    gain = vec_ref[2:3, :]
    normed = (unit * gain + vec_ref[3:4, :]).astype(b16)
    turned = normed.T
    cot = g_ref[...]
    out_ref[...] = residual + vec_ref[7:8, :]
    grad_ref[...] = jnp.zeros_like(grad_ref)

    def chunk(part, carry):
        hidden = dot_nn(normed, w_ref[1 + part]) + vec_ref[pl.ds(8 + part, 1), :]
        pulled = dot_nt(cot, w_ref[1 + fold + part])
        active, slope = gelu_parts(hidden)
        active = active.astype(b16)
        pulled = (pulled * slope).astype(b16)
        out_ref[...] += dot_nn(active, w_ref[1 + fold + part])
        grad_ref[...] += dot_nt(pulled, w_ref[1 + part])
        acc_ref[1 + part] += dot_nn(turned, pulled)
        acc_ref[1 + fold + part] += dot_tn(active, cot)
        sums_ref[pl.ds(8 + part, 1), :] += jnp.sum(pulled.astype(f32), 0, keepdims=True)
        return carry

    lax.fori_loop(0, fold, chunk, 0)
    grad = grad_ref[...]
    y_ref[...] = out_ref[...].astype(b16)
    wide = cot.astype(f32)
    sums_ref[2:3, :] += jnp.sum(grad * unit, 0, keepdims=True)
    sums_ref[3:4, :] += jnp.sum(grad, 0, keepdims=True)
    sums_ref[7:8, :] += jnp.sum(wide, 0, keepdims=True)
    back = wide + norm_back(grad, unit, rstd, gain)
    r_ref[...] = back.astype(b16)
    low = back.astype(b16)
    sums_ref[6:7, :] += jnp.sum(low.astype(f32), 0, keepdims=True)
    d_ref[...] = dot_nt(w_ref[0], low).astype(b16)
    acc_ref[0] += dot_nn(o_ref[...], low)

    @pl.when(step == pl.num_programs(0) - 1)
    def send():
        count = 1 + 2 * fold
        copies = []
        for part in range(count):
            if part >= 2:
                copies[part - 2].wait()
            stage_ref[part % 2] = acc_ref[part].astype(b16)
            copy = pltpu.make_async_copy(stage_ref.at[part % 2], tiles_ref.at[part], sem_ref.at[part % 2])
            copy.start()
            copies.append(copy)
        copies[count - 2].wait()
        copies[count - 1].wait()


def feed(context, turned, x, cot, weights, vectors):
    tokens = x.shape[0]
    size = 256
    count = 1 + 2 * (FF // D)
    token_block = pl.BlockSpec((size, D), lambda i: (i, 0))
    turned_block = pl.BlockSpec((D, size), lambda i: (0, i))
    return pl.pallas_call(
        feed_kernel,
        grid=(tokens // size,),
        in_specs=[
            token_block,
            turned_block,
            token_block,
            token_block,
            pl.BlockSpec((count, D, D), lambda i: (0, 0, 0), pipeline_mode=pl.Buffered(1)),
            pl.BlockSpec((PIECES, D), lambda i: (0, 0)),
        ],
        out_specs=[
            token_block,
            token_block,
            turned_block,
            pl.BlockSpec((16, D), lambda i: (0, 0)),
            pl.BlockSpec(memory_space=pl.ANY),
        ],
        out_shape=[
            jax.ShapeDtypeStruct((tokens, D), b16),
            jax.ShapeDtypeStruct((tokens, D), b16),
            jax.ShapeDtypeStruct((D, tokens), b16),
            jax.ShapeDtypeStruct((16, D), f32),
            jax.ShapeDtypeStruct((count, D, D), b16),
        ],
        scratch_shapes=[
            pltpu.VMEM((count, D, D), f32),
            pltpu.VMEM((size, D), f32),
            pltpu.VMEM((size, D), f32),
            pltpu.VMEM((2, D, D), b16),
            pltpu.SemaphoreType.DMA((2,)),
        ],
        compiler_params=pltpu.CompilerParams(vmem_limit_bytes=60 * MIB),
        cost_estimate=pl.CostEstimate(
            flops=6 * count * tokens * D * D,
            bytes_accessed=18 * tokens * D + 4 * count * D * D,
            transcendentals=2 * tokens * FF,
        ),
        name="feed",
    )(context, turned, x, cot, weights, vectors)


MESH = pl.DeviceIdType.MESH
HALF = D // 2
FLOWS = 2
FLOW = HALF // FLOWS
NEAR = FLOW // 2
KEEP = NEAR // 2
WIDE = 3 * PAIR
REST = PIECES - 3
GROUPS = ((0, 1), (1, 2), (3, 3))
CHUNKS = len(GROUPS)


def whole(value, unit):
    return value // unit if isinstance(value, int) else lax.div(value, unit)


def rest(value, unit):
    return value % unit if isinstance(value, int) else lax.rem(value, unit)


def either(condition, body):
    if isinstance(condition, bool):
        if condition:
            body()
    else:
        pl.when(condition)(body)


class Place:
    def __init__(self):
        self.me = lax.axis_index("dp")
        self.core = lax.axis_index("blk")
        self.bits = [lax.rem(self.me // weight, 2) for weight in (1, 2, 4, 8)]
        self.chips = [
            self.me + weight - 2 * weight * bit for weight, bit in zip((1, 2, 4, 8), self.bits)
        ]
        self.partners = [{"dp": chip} for chip in self.chips]
        low, high = self.bits[2:]
        self.inner = low != high
        self.across = {"dp": self.me + 4 - 8 * low + 8 - 16 * high}
        self.other = 1 - self.core
        self.twin = {"blk": self.other}

    def greet(self):
        barrier = pltpu.get_barrier_semaphore()
        for device in self.partners + [self.across, self.twin]:
            pl.semaphore_signal(barrier, 1, device_id=device, device_id_type=MESH)
        pl.semaphore_wait(barrier, 6)

    def flow(self, index):
        first, second = (0, 1) if index == 0 else (1, 0)
        base = index * FLOW
        near = base + self.bits[first] * NEAR
        far = base + NEAR - self.bits[first] * NEAR
        keep = near + self.bits[second] * KEEP
        give = near + KEEP - self.bits[second] * KEEP
        return first, second, near, far, keep, give


def remote(source, target, send, receive, device):
    return pltpu.make_async_remote_copy(
        src_ref=source,
        dst_ref=target,
        send_sem=send,
        recv_sem=receive,
        device_id=device,
        device_id_type=MESH,
    )


def rows_at(start, count):
    return pl.ds(pl.multiple_of(start, 16), count)


def lanes_at(start, count):
    return pl.ds(start if isinstance(start, int) else pl.multiple_of(start, PAIR), count)


class Spread:
    def __init__(self, place, owner, rank, slots, land, gift, sems):
        self.place, self.owner, self.rank = place, owner, rank
        self.slots, self.land, self.gift, self.sems = slots, land, gift, sems

    def cols(self, chunk):
        return pl.ds(GROUPS[chunk][0] * PAIR, GROUPS[chunk][1] * PAIR)

    def first_copy(self, chunk, index):
        first, second, near, far, keep, give = self.place.flow(index)
        return remote(
            self.slots.at[:, rows_at(far, NEAR), self.cols(chunk)],
            self.land[chunk].at[index],
            self.sems[0].at[chunk, index, 0],
            self.sems[1].at[chunk, index, 0],
            self.place.partners[first],
        )

    def second_copy(self, chunk, index, which):
        first, second, near, far, keep, give = self.place.flow(index)
        if which == 0:
            source = self.slots.at[:, rows_at(give, KEEP), self.cols(chunk)]
        else:
            source = self.land[chunk].at[index, :, rows_at(give - near, KEEP)]
        return remote(
            source,
            self.gift[chunk].at[index, pl.ds(which * CAP, CAP)],
            self.sems[0].at[chunk, index, 1 + which],
            self.sems[1].at[chunk, index, 1 + which],
            self.place.partners[second],
        )

    def step(self, chunk, index):
        for flow in range(FLOWS):
            if index == 0:
                self.first_copy(chunk, flow).start()
                self.second_copy(chunk, flow, 0).start()
            if index == 1:
                self.first_copy(chunk, flow).wait()
                self.second_copy(chunk, flow, 1).start()
            if index == 2:
                self.second_copy(chunk, flow, 0).wait()
                self.second_copy(chunk, flow, 1).wait()

    def piece(self, tile, index, chunk, start, count):
        first, second, near, far, keep, give = self.place.flow(index)
        owner, rank = self.owner[tile], self.rank[tile]
        bits = [lax.rem(owner, 2), lax.rem(owner // 2, 2)]
        apart = [bit != mine for bit, mine in zip(bits, self.place.bits)]
        cols = lanes_at(start, count)
        mine = self.slots[
            rank, rows_at(keep, KEEP), lanes_at(GROUPS[chunk][0] * PAIR + start, count)
        ]
        firsts = self.land[chunk][index, rank, rows_at(keep - near, KEEP), cols]
        gifts = self.gift[chunk][index, jnp.where(apart[first], CAP, 0) + rank, :, cols]
        value = jnp.where(apart[second], gifts, jnp.where(apart[first], firsts, mine))
        layer = owner // 4 == self.place.me // 4
        return jnp.where(layer, value, jnp.zeros_like(value))


class Column:
    steps = 4

    def __init__(self, place, kept, read, write, land, sems):
        self.place, self.kept, self.read, self.write = place, kept, read, write
        self.land, self.sems = land, sems

    def copy(self, index):
        target = self.land.at[index % 2]
        device = self.place.across if index == 1 else self.place.partners[2]
        return remote(
            self.kept, target, self.sems[0].at[index], self.sems[1].at[index], device
        )

    def add(self, index):
        self.write((self.read().astype(f32) + self.land[index].astype(f32)).astype(b16))


def column_step(place, columns, index):
    @pl.when(place.inner)
    def inner():
        for column in columns:
            if index == 1:
                column.copy(0).wait_recv()
                column.add(0)
                column.copy(1).start()
            if index == 2:
                column.copy(1).wait()
                column.add(1)
                column.copy(2).start()
            if index == 3:
                column.copy(2).wait_send()

    @pl.when(jnp.logical_not(place.inner))
    def outer():
        for column in columns:
            if index == 0:
                column.copy(0).start()
            if index == 1:
                column.copy(0).wait_send()
            if index == 3:
                column.copy(2).wait_recv()
                column.write(column.land[0])


class Item:
    steps = 7

    def __init__(self, place, work, land, sems, load, store=None):
        self.place, self.work, self.land, self.sems = place, work, land, sems
        self.load, self.store = load, store
        self.base = place.core * HALF

    def column(self, flow):
        rows = rows_at(self.base + self.place.flow(flow)[4], KEEP)

        def read():
            return self.work[:, rows]

        def write(value):
            self.work[:, rows] = value

        sems = (self.sems[0].at[flow], self.sems[1].at[flow])
        return Column(self.place, self.work.at[:, rows], read, write, self.land.at[flow], sems)

    def copy(self, flow, index):
        first, second, near, far, keep, give = self.place.flow(flow)
        kept = self.work.at[:, rows_at(self.base + keep, KEEP)]
        half = self.work.at[:, rows_at(self.base + near, NEAR)]
        source, device = [
            (kept, self.place.partners[second]),
            (half, self.place.partners[first]),
        ][index]
        return remote(
            source, source, self.sems[0].at[flow, 3 + index], self.sems[1].at[flow, 3 + index], device
        )

    def pair(self):
        rows = self.work.at[:, rows_at(self.base, HALF)]
        return remote(rows, rows, self.sems[0].at[0, 5], self.sems[1].at[0, 5], self.place.twin)

    def step(self, index):
        for flow in range(FLOWS):
            if index == 0:
                self.load(self.work, rows_at(self.base + self.place.flow(flow)[4], KEEP), flow)
        if index <= 3:
            column_step(self.place, [self.column(flow) for flow in range(FLOWS)], index)
        for flow in range(FLOWS):
            if 4 <= index <= 5:
                self.copy(flow, index - 4).wait()
            if 3 <= index <= 4:
                self.copy(flow, index - 3).start()
        if index == 5:
            self.pair().start()
        if index == 6:
            self.pair().wait()
            self.store().start()


RS_STARTS = (0, 2, 5)
PAIR_START, PAIR_PACE = 4, 3
REST_START, REST_PACE = 12, 2
LEAD = 17
HEAD_STEPS = 4 * PAIRS


def front_kernel(
    owner, lengths, master, vec_ref, x_in, c_in,
    x_out, c_out, n_out, one_out, two_out, q_ref, k_ref, v_ref, p_ref, r_ref, o_ref, ctx_ref,
    rank, rows_ref, normed, keys, turned_values, slots,
    land_one, land_two, land_three, gift_one, gift_two, gift_three,
    one, one_land, two, two_land,
    spread_send, spread_recv, one_send, one_recv, two_send, two_recv,
    swap_send, swap_recv, swap_local, store_sem,
):
    clock = pl.program_id(0)
    unit = jnp.maximum(clock - LEAD, 0)
    pair, row, head = unit // 4, lax.rem(unit // 2, 2), lax.rem(unit, 2)
    place = Place()
    rows, span = x_in.shape[0] // 2, x_in.shape[1]
    land = (land_one, land_two, land_three)
    gift = (gift_one, gift_two, gift_three)
    spread = Spread(place, owner, rank, slots, land, gift, (spread_send, spread_recv))

    def swaps(index):
        source, target = [(x_in, rows_ref), (c_in, c_out)][index]
        here = pl.ds(place.core * span, span)
        near = pltpu.make_async_copy(
            source.at[pl.ds(place.core * rows, rows)], target.at[:, here], swap_local.at[index]
        )
        far = remote(
            source.at[pl.ds(place.other * rows, rows)],
            target.at[:, here],
            swap_send.at[index],
            swap_recv.at[index],
            place.twin,
        )
        return near, far

    def row_store():
        return pltpu.make_async_copy(rows_ref, x_out, store_sem.at[PAIRS + REST])

    def normed_store():
        return pltpu.make_async_copy(normed, n_out, store_sem.at[PAIRS + REST + 1])

    def pair_item(index):
        span_of = pl.ds(index, 1)

        def load(work, where, flow):
            for chunk, (first, count) in enumerate(GROUPS):

                @pl.when((index >= first) & (index < first + count))
                def place_pieces():
                    for tile in range(3):
                        part = spread.piece(tile, flow, chunk, (index - first) * PAIR, PAIR)
                        work[0, where, pl.ds(tile * PAIR, PAIR)] = part

        def store():
            return pltpu.make_async_copy(one.at[span_of], one_out.at[span_of], store_sem.at[index])

        sems = (one_send.at[index], one_recv.at[index])
        return Item(place, one.at[span_of], one_land.at[:, :, span_of], sems, load, store)

    def rest_item(index):
        span_of = pl.ds(index, 1)

        def load(work, where, flow):
            for chunk, (start, wide) in enumerate(GROUPS):
                part = spread.piece(3 + index, flow, chunk, 0, wide * PAIR)
                work[0, where, pl.ds(start * PAIR, wide * PAIR)] = part

        def store():
            return pltpu.make_async_copy(
                two.at[span_of], two_out.at[span_of], store_sem.at[PAIRS + index]
            )

        sems = (two_send.at[index], two_recv.at[index])
        return Item(place, two.at[span_of], two_land.at[:, :, span_of], sems, load, store)

    @pl.when(clock == 0)
    def lead():
        slots[...] = master[...].astype(b16)
        for tile in range(PIECES):
            count = jnp.int32(0)
            for before in range(tile):
                count = count + (owner[before] == owner[tile]).astype(jnp.int32)
            rank[tile] = jnp.minimum(count, CAP - 1)
        place.greet()
        for copy in swaps(0):
            copy.start()

    for chunk, begin in enumerate(RS_STARTS):
        for index in range(3):
            pl.when(clock == begin + 2 * index)(partial(spread.step, chunk, index))

    @pl.when(clock == 1)
    def normalise():
        for copy in swaps(1):
            copy.start()
        for copy in swaps(0):
            copy.wait()
        row_store().start()

        def norm_rows(index, carry):
            where = pl.ds(index * 256, 256)
            for part in range(rows):
                unit, unused = norm_parts(rows_ref[part, where].astype(f32))
                low = (unit * vec_ref[0:1, :] + vec_ref[1:2, :]).astype(b16)
                normed[pl.ds(part * LEN + index * 256, 256)] = low
            return carry

        lax.fori_loop(0, LEN // 256, norm_rows, 0)
        normed_store().start()

    for index in reversed(range(Item.steps)):
        since = clock - PAIR_START - 2 * index
        number = whole(since, PAIR_PACE)

        @pl.when((since >= 0) & (lax.rem(since, PAIR_PACE) == 0) & (number < PAIRS))
        def move_pair():
            pair_item(number).step(index)

        since = clock - REST_START - 2 * index
        even = lax.rem(since, 4) == 0
        tile = jnp.where(even, whole(since, 4) * 2, whole(since, 4) * 2 + 1)

        @pl.when((since >= 0) & (even | (lax.rem(since, 4) == 3)) & (tile < REST))
        def move_rest():
            rest_item(tile).step(index)

    @pl.when((clock >= LEAD) & (row == 0) & (head == 0))
    def project():
        lanes = pl.ds(pl.multiple_of(pair * PAIR, PAIR), PAIR)
        weight = one[pair]

        def part(index, carry):
            where = pl.ds(pl.multiple_of(index * 512, 512), 512)
            both = dot_nn(normed[where], weight)
            queries = both[:, :PAIR] + vec_ref[4:5, lanes]
            queries = (queries * (HEAD_DIM**-0.5 * LOG2E)).astype(b16)
            q_ref[:, where] = queries.T
            low = both[:, PAIR : 2 * PAIR].astype(b16)
            keys[where] = low
            k_ref[:, where] = low.T
            values = (both[:, 2 * PAIR :] + vec_ref[5:6, lanes]).astype(b16)
            v_ref[where] = values
            turned_values[:, where] = values.T
            return carry

        lax.fori_loop(0, normed.shape[0] // 512, part, 0)

    @pl.when(clock >= LEAD)
    def attention():
        half = LEN // 2
        start = pl.multiple_of(row * LEN, LEN)
        split = lengths[place.core * rows + row, 0] < LEN
        shift = jnp.where(split, jnp.float32(-1e30), jnp.float32(0.0))
        part = pl.ds(pl.multiple_of(head * HEAD_DIM, HEAD_DIM), HEAD_DIM)
        for step in range(2):
            cols = pl.ds(pl.multiple_of(start + step * half, half), half)
            others = pl.ds(pl.multiple_of(start + (1 - step) * half, half), half)
            queries = q_ref[:, cols]
            near = dot_nn(head_only(keys[cols], head), queries)
            far = dot_nn(head_only(keys[others], head), queries) + shift
            top = jnp.maximum(jnp.max(near, 0, keepdims=True), jnp.max(far, 0, keepdims=True))
            near = jnp.exp2(near - top)
            far = jnp.exp2(far - top)
            total = jnp.sum(near, 0, keepdims=True) + jnp.sum(far, 0, keepdims=True)
            recip = 1.0 / total
            here = slice(step * half, (step + 1) * half)
            there = slice((1 - step) * half, (2 - step) * half)
            near, far = near.astype(b16), far.astype(b16)
            p_ref[0, here, here] = near
            p_ref[0, there, here] = far
            r_ref[0, :, here] = recip
            out = dot_nn(turned_values[part, cols], near)
            out = out + dot_nn(turned_values[part, others], far)
            o_ref[part, here] = (out * recip).astype(b16)

        @pl.when(head == 1)
        def turn():
            ctx_ref[...] = o_ref[...].T

    @pl.when(clock == LEAD + HEAD_STEPS - 1)
    def finish_copies():
        for copy in swaps(1):
            copy.wait()
        row_store().wait()
        normed_store().wait()
        for index in range(PAIRS):
            pair_item(index).store().wait()
        for index in range(REST):
            rest_item(index).store().wait()


def front(owner, lengths, master, vectors, inputs, cotangent):
    rows, span = inputs.shape[0] // 2, inputs.shape[1]
    tokens = rows * LEN
    any_spec = pl.BlockSpec(memory_space=pl.ANY)
    smem = pl.BlockSpec(memory_space=pltpu.SMEM)
    whole = jax.ShapeDtypeStruct((rows, LEN, D), b16)
    dma = pltpu.SemaphoreType.DMA

    def now(step):
        return jnp.maximum(step - LEAD, 0)

    return pl.pallas_call(
        front_kernel,
        grid=(LEAD + HEAD_STEPS,),
        in_specs=[
            smem,
            smem,
            pl.BlockSpec((CAP, HALF, D), lambda s: (0, 0, 0), pipeline_mode=pl.Buffered(1)),
            pl.BlockSpec((PIECES, D), lambda s: (0, 0)),
            any_spec,
            any_spec,
        ],
        out_specs=[any_spec] * 5
        + [
            pl.BlockSpec((PAIR, tokens), lambda s: (now(s) // 4, 0)),
            pl.BlockSpec((PAIR, tokens), lambda s: (now(s) // 4, 0)),
            pl.BlockSpec((tokens, PAIR), lambda s: (0, now(s) // 4)),
            pl.BlockSpec((1, LEN, LEN), lambda s: (now(s), 0, 0)),
            pl.BlockSpec((1, 1, LEN), lambda s: (now(s), 0, 0)),
            pl.BlockSpec((PAIR, LEN), lambda s: (now(s) // 4, lax.rem(now(s) // 2, 2))),
            pl.BlockSpec((LEN, PAIR), lambda s: (lax.rem(now(s) // 2, 2), now(s) // 4)),
        ],
        out_shape=[
            whole,
            whole,
            jax.ShapeDtypeStruct((tokens, D), b16),
            jax.ShapeDtypeStruct((PAIRS, D, WIDE), b16),
            jax.ShapeDtypeStruct((REST, D, D), b16),
            jax.ShapeDtypeStruct((D, tokens), b16),
            jax.ShapeDtypeStruct((D, tokens), b16),
            jax.ShapeDtypeStruct((tokens, D), b16),
            jax.ShapeDtypeStruct((rows * HEADS, LEN, LEN), b16),
            jax.ShapeDtypeStruct((rows * HEADS, 1, LEN), f32),
            jax.ShapeDtypeStruct((D, tokens), b16),
            jax.ShapeDtypeStruct((tokens, D), b16),
        ],
        scratch_shapes=[
            pltpu.SMEM((PIECES,), jnp.int32),
            pltpu.VMEM((rows, LEN, D), b16),
            pltpu.VMEM((tokens, D), b16),
            pltpu.VMEM((tokens, PAIR), b16),
            pltpu.VMEM((PAIR, tokens), b16),
            pltpu.VMEM((CAP, HALF, D), b16),
        ]
        + [pltpu.VMEM((FLOWS, CAP, NEAR, wide * PAIR), b16) for unused, wide in GROUPS]
        + [pltpu.VMEM((FLOWS, 2 * CAP, KEEP, wide * PAIR), b16) for unused, wide in GROUPS]
        + [
            pltpu.VMEM((PAIRS, D, WIDE), b16),
            pltpu.VMEM((FLOWS, 2, PAIRS, KEEP, WIDE), b16),
            pltpu.VMEM((REST, D, D), b16),
            pltpu.VMEM((FLOWS, 2, REST, KEEP, D), b16),
            dma((CHUNKS, FLOWS, 3)),
            dma((CHUNKS, FLOWS, 3)),
            dma((PAIRS, FLOWS, 6)),
            dma((PAIRS, FLOWS, 6)),
            dma((REST, FLOWS, 6)),
            dma((REST, FLOWS, 6)),
            dma((2,)),
            dma((2,)),
            dma((2,)),
            dma((PAIRS + REST + 2,)),
        ],
        compiler_params=pltpu.CompilerParams(
            collective_id=0, has_side_effects=True, vmem_limit_bytes=60 * MIB
        ),
        name="front",
    )(owner, lengths, master, vectors, inputs, cotangent)


class Sum:
    steps = 7

    def __init__(self, place, work, wide, narrow, sems, send_pair, add_own):
        self.place, self.work, self.wide, self.narrow, self.sems = place, work, wide, narrow, sems
        self.send_pair, self.add_own = send_pair, add_own

    def column(self, flow):
        rows = rows_at(self.place.flow(flow)[4], KEEP)

        def read():
            return self.work[:, rows]

        def write(value):
            self.work[:, rows] = value

        sems = (self.sems[0].at[flow, pl.ds(2, 3)], self.sems[1].at[flow, pl.ds(2, 3)])
        land = self.narrow.at[flow, pl.ds(1, 2)]
        return Column(self.place, self.work.at[:, rows], read, write, land, sems)

    def copy(self, flow, index):
        first, second, near, far, keep, give = self.place.flow(flow)
        source, target, device = [
            (self.work.at[:, rows_at(far, NEAR)], self.wide.at[flow], first),
            (self.work.at[:, rows_at(give, KEEP)], self.narrow.at[flow, 0], second),
        ][index]
        return remote(
            source,
            target,
            self.sems[0].at[flow, index],
            self.sems[1].at[flow, index],
            self.place.partners[device],
        )

    def add(self, rows, value):
        self.work[:, rows] = (self.work[:, rows].astype(f32) + value.astype(f32)).astype(b16)

    def step(self, index):
        if index == 0:
            self.send_pair().start()
        if index == 1:
            self.send_pair().wait()
            self.add_own()
        for flow in range(FLOWS):
            first, second, near, far, keep, give = self.place.flow(flow)
            if index == 1:
                self.copy(flow, 0).start()
            if index == 2:
                self.copy(flow, 0).wait()
                self.add(rows_at(near, NEAR), self.wide[flow])
                self.copy(flow, 1).start()
            if index == 3:
                self.copy(flow, 1).wait()
                self.add(rows_at(keep, KEEP), self.narrow[flow, 0])
        if index >= 3:
            columns = [self.column(flow) for flow in range(FLOWS)]
            column_step(self.place, columns, index - 3)


class Gather:
    steps = 3

    def __init__(self, place, work, narrow, wide, sems):
        self.place, self.work, self.narrow, self.wide = place, work, narrow, wide
        self.sems = sems

    def copy(self, flow, index):
        first, second, near, far, keep, give = self.place.flow(flow)
        rows, target, device = [
            (rows_at(keep, KEEP), self.narrow, second),
            (rows_at(near, NEAR), self.wide, first),
        ][index]
        return remote(
            self.work.at[:, rows],
            target.at[flow],
            self.sems[0].at[flow, 5 + index],
            self.sems[1].at[flow, 5 + index],
            self.place.partners[device],
        )

    def step(self, index):
        for flow in range(FLOWS):
            first, second, near, far, keep, give = self.place.flow(flow)
            if index > 0:
                self.copy(flow, index - 1).wait()
            if index == 1:
                self.work[:, rows_at(give, KEEP)] = self.narrow[flow]
            if index == 2:
                self.work[:, rows_at(far, NEAR)] = self.wide[flow]
            if index < 2:
                self.copy(flow, index).start()


class Hand:
    steps = 3

    def __init__(self, place, table, work, bag, gift, pack, last, own, out, sems, store_sems):
        self.place, self.table, self.work = place, table, work
        self.bag, self.gift, self.pack, self.last, self.own = bag, gift, pack, last, own
        self.out, self.sems, self.store_sems = out, sems, store_sems

    def tile(self, chip, rank, rows):
        return self.work[self.table[chip * CAP + rank], rows]

    def copy(self, flow, index):
        first, second = self.place.flow(flow)[:2]
        source, target, device = [
            (self.bag.at[flow], self.gift.at[flow], second),
            (self.pack.at[flow], self.last.at[flow], first),
        ][index]
        return remote(
            source,
            target,
            self.sems[0].at[flow, index],
            self.sems[1].at[flow, index],
            self.place.partners[device],
        )

    def stores(self, flow):
        first, second, near, far, keep, give = self.place.flow(flow)
        parts = [
            (self.own.at[flow], rows_at(keep, KEEP)),
            (self.gift.at[flow, pl.ds(0, CAP)], rows_at(give, KEEP)),
            (self.last.at[flow], rows_at(far, NEAR)),
        ]
        return [
            pltpu.make_async_copy(source, self.out.at[:, rows], self.store_sems.at[flow, index])
            for index, (source, rows) in enumerate(parts)
        ]

    def step(self, index):
        for flow in range(FLOWS):
            first, second, near, far, keep, give = self.place.flow(flow)
            rows = rows_at(keep, KEEP)
            if index == 0:
                beside = self.place.chips[second]
                across = beside + self.place.chips[first] - self.place.me
                for rank in range(CAP):
                    self.bag[flow, rank] = self.tile(beside, rank, rows)
                    self.bag[flow, CAP + rank] = self.tile(across, rank, rows)
                    self.own[flow, rank] = self.tile(self.place.me, rank, rows)
                self.copy(flow, 0).start()
            if index == 1:
                self.copy(flow, 0).wait()
                for rank in range(CAP):
                    mine = self.tile(self.place.chips[first], rank, rows)
                    self.pack[flow, rank, rows_at(keep - near, KEEP)] = mine
                    self.pack[flow, rank, rows_at(give - near, KEEP)] = self.gift[flow, CAP + rank]
                self.copy(flow, 1).start()
            if index == 2:
                self.copy(flow, 1).wait()
                for copy in self.stores(flow):
                    copy.start()


BACK_TAIL = 4
BACK_HAND = 25
BACK_DRAIN = HEAD_STEPS + BACK_TAIL
BACK_END = 4 * PAIRS + 2 * (Sum.steps + Gather.steps - 2) + 1


def back_kernel(
    table, p_ref, r_ref, v_ref, q_ref, k_ref, o_ref, g_ref, w_ref, n_ref, x_ref, z_ref, vec_ref,
    tiles_in, sums_in, y_in,
    y_out, i_out, pairs_out, slots_out, sums_ref,
    grad_sum, wide_sum, turned, block_out,
    two, two_wide, two_narrow, two_stage, one, one_wide, one_narrow, one_send_stage, one_stage,
    gather_narrow, gather_wide,
    bag, gift, pack, last, own, vec_land,
    two_send, two_recv, one_send, one_recv, hand_send, hand_recv, hand_store,
    pair_two_send, pair_two_recv, pair_one_send, pair_one_recv, load_sem, store_sem,
    swap_send, swap_recv, swap_local, vec_send, vec_recv,
):
    step = pl.program_id(0)
    place = Place()
    rows, span = y_in.shape[0], y_in.shape[1] // 2
    near_half = rows_at(place.core * HALF, HALF)
    far_half = rows_at(place.other * HALF, HALF)

    def load_two(index):
        slot = lax.rem(index, 3)
        return pltpu.make_async_copy(
            tiles_in.at[pl.ds(index, 1), near_half], two_stage.at[pl.ds(slot, 1)], load_sem.at[slot]
        )

    def rest_sum(index):
        span_of = pl.ds(index, 1)
        work = two.at[span_of]

        def send_pair():
            return remote(
                tiles_in.at[span_of, far_half],
                work,
                pair_two_send.at[index],
                pair_two_recv.at[index],
                place.twin,
            )

        def add_own():
            load_two(index).wait()
            own_rows = two_stage[pl.ds(lax.rem(index, 3), 1)].astype(f32)
            work[...] = (work[...].astype(f32) + own_rows).astype(b16)

        sems = (two_send.at[index], two_recv.at[index])
        wide, narrow = two_wide.at[:, span_of], two_narrow.at[:, :, span_of]
        return Sum(place, work, wide, narrow, sems, send_pair, add_own)

    def pair_sum(index):
        span_of = pl.ds(index, 1)
        work = one.at[span_of]

        def send_pair():
            return remote(
                one_send_stage.at[span_of],
                work,
                pair_one_send.at[index],
                pair_one_recv.at[index],
                place.twin,
            )

        def add_own():
            own_rows = one_stage[span_of].astype(f32)
            work[...] = (work[...].astype(f32) + own_rows).astype(b16)

        sems = (one_send.at[index], one_recv.at[index])
        wide, narrow = one_wide.at[:, span_of], one_narrow.at[:, :, span_of]
        return Sum(place, work, wide, narrow, sems, send_pair, add_own)

    def pair_gather(index):
        span_of = pl.ds(index, 1)
        sems = (one_send.at[index], one_recv.at[index])
        narrow, wide = gather_narrow.at[:, span_of], gather_wide.at[:, span_of]
        return Gather(place, one.at[span_of], narrow, wide, sems)

    hand = Hand(
        place, table, two, bag, gift, pack, last, own, slots_out, (hand_send, hand_recv), hand_store
    )

    def pair_store(index, tile):
        lanes = lanes_at(index * PAIR, PAIR)
        return pltpu.make_async_copy(
            one.at[index, :, pl.ds(tile * PAIR, PAIR)],
            pairs_out.at[tile, :, lanes],
            store_sem.at[index, tile],
        )

    def tick(clock, hands, rests):
        if rests:
            for index in reversed(range(Sum.steps)):
                since = clock - 2 * index
                tile = 2 * whole(since, 3) + rest(since, 3)

                @pl.when((since >= 0) & (rest(since, 3) < 2) & (tile < REST))
                def move_rest():
                    rest_sum(tile).step(index)

            since = clock + 2
            tile = 2 * whole(since, 3) + rest(since, 3)

            @pl.when((rest(since, 3) < 2) & (tile < REST))
            def load_ahead():
                load_two(tile).start()

        for index in reversed(range(Sum.steps + Gather.steps - 1)):
            since = clock - 4 - 2 * index
            number = whole(since, 4)

            def move_pair():
                if index < Sum.steps:
                    pair_sum(number).step(index)
                if index >= Sum.steps - 1:
                    pair_gather(number).step(index - Sum.steps + 1)
                if index == Sum.steps + Gather.steps - 2:
                    for tile in range(3):
                        pair_store(number, tile).start()

            either((since >= 0) & (rest(since, 4) == 0) & (number < PAIRS), move_pair)

        for index in hands:
            either(clock == BACK_HAND + 2 * index, partial(hand.step, index))

    def swap_y(index):
        there = pl.ds(place.core * rows, rows)
        if index == 0:
            return pltpu.make_async_copy(
                y_in.at[:, pl.ds(place.core * span, span)], y_out.at[there], swap_local.at[0]
            )
        return remote(
            y_in.at[:, pl.ds(place.other * span, span)],
            y_out.at[there],
            swap_send.at[0],
            swap_recv.at[0],
            place.twin,
        )

    @pl.when(step == 0)
    def lead():
        place.greet()
        for index in range(2):
            swap_y(index).start()
        sums_ref[...] = sums_in[...]

        load_two(0).start()
        load_two(1).start()

    tick(step, (0, 1), True)

    half = LEN // 2
    pair, row, head = step // 4, lax.rem(step // 2, 2), lax.rem(step, 2)

    @pl.when(step < HEAD_STEPS)
    def attention():
        part = pl.ds(pl.multiple_of(head * HEAD_DIM, HEAD_DIM), HEAD_DIM)
        values = head_only(v_ref[...], head)
        recip = r_ref[0]
        grad = g_ref[part, :].astype(f32) * recip
        delta = jnp.sum(grad * o_ref[part, :].astype(f32), 0, keepdims=True)
        grad = grad.astype(b16)
        doubled = jnp.concatenate([grad, grad], axis=0)
        value_grad, key_grad = [], []
        for which in range(2):
            cols = slice(which * half, (which + 1) * half)
            weights = p_ref[0, :, cols]
            slope = dot_nn(values, doubled[:, cols]) - delta[:, cols]
            slope = (weights.astype(f32) * slope).astype(b16)
            value_grad.append(dot_nt(grad[:, cols], weights))
            key_grad.append(dot_nt(q_ref[part, cols], slope))
            query_grad = dot_nn(k_ref[part, :], slope) * (HEAD_DIM**-0.5)
            turned[part, cols] = query_grad.astype(b16)
        lower = pl.ds(pl.multiple_of(PAIR + head * HEAD_DIM, HEAD_DIM), HEAD_DIM)
        turned[lower, :] = ((key_grad[0] + key_grad[1]) * (1.0 / LOG2E)).astype(b16)
        lower = pl.ds(pl.multiple_of(2 * PAIR + head * HEAD_DIM, HEAD_DIM), HEAD_DIM)
        turned[lower, :] = (value_grad[0] + value_grad[1]).astype(b16)

    @pl.when((step < HEAD_STEPS) & (head == 1))
    def weight_grads():
        where = pl.ds(pl.multiple_of(row * LEN, LEN), LEN)
        block = dot_nn(turned[...], n_ref[where])
        back = turned[...].T
        lanes = pl.ds(pl.multiple_of(pair * PAIR, PAIR), PAIR)
        ones = jnp.sum(back.astype(f32), 0, keepdims=True)
        sums_ref[4:5, lanes] += ones[:, :PAIR]
        sums_ref[5:6, lanes] += ones[:, 2 * PAIR :]
        term = dot_nt(back, w_ref[0])

        @pl.when(pair == 0)
        def begin():
            grad_sum[where] = term

        @pl.when(pair > 0)
        def add():
            grad_sum[where] += term

        @pl.when(row == 0)
        def keep():
            wide_sum[...] = block

        @pl.when(row == 1)
        def hand_on():
            whole = (wide_sum[...] + block).T
            low = whole.astype(b16)
            for core in range(2):

                @pl.when(place.core == core)
                def split():
                    one_stage[pair] = low[core * HALF : (core + 1) * HALF]
                    one_send_stage[pair] = low[(1 - core) * HALF : (2 - core) * HALF]

    def store_block(index):
        row, half = index // 2, index % 2
        target = i_out.at[place.core * rows + row]
        local = pltpu.make_async_copy(block_out.at[index], target, swap_local.at[1 + row])
        far = remote(
            block_out.at[index], target, swap_send.at[1 + row], swap_recv.at[1 + row], place.twin
        )
        return local, far, half

    for index in range(BACK_TAIL):

        @pl.when(step == HEAD_STEPS + index)
        def close():
            size = LEN // 2
            grad = grad_sum[index * size : (index + 1) * size]
            unit, rstd = norm_parts(x_ref[...].astype(f32))
            sums_ref[0:1, :] += jnp.sum(grad * unit, 0, keepdims=True)
            sums_ref[1:2, :] += jnp.sum(grad, 0, keepdims=True)
            total = z_ref[...].astype(f32) + norm_back(grad, unit, rstd, vec_ref[0:1, :])
            block_out[index] = total.astype(b16)
            local, far, half = store_block(index)

            @pl.when(place.core == half)
            def keep():
                local.start()

            @pl.when(place.core != half)
            def give():
                far.start()

    @pl.when(step == BACK_DRAIN - 1)
    def drain():
        devices = [place.twin] + place.partners

        def vector(index):
            return remote(
                sums_ref, vec_land.at[index], vec_send.at[index], vec_recv.at[index], devices[index]
            )

        vector(0).start()
        for index in range(BACK_END - BACK_DRAIN):
            tick(BACK_DRAIN + index, (2,), False)
            if index < 5:
                vector(index).wait()
                sums_ref[...] += vec_land[index]
                if index < 4:
                    vector(index + 1).start()
        for index in range(2):
            swap_y(index).wait()
        for index in range(BACK_TAIL):
            local, far, half = store_block(index)

            @pl.when(place.core == half)
            def keep():
                local.wait()

            @pl.when(place.core != half)
            def give():
                far.wait()

        for index in range(PAIRS):
            for tile in range(3):
                pair_store(index, tile).wait()
        for flow in range(FLOWS):
            for copy in hand.stores(flow):
                copy.wait()


def back(table, attention, weights, normed, x, residual, vectors, tiles, sums, y):
    rows, length = y.shape[:2]
    tokens = rows * length
    any_spec = pl.BlockSpec(memory_space=pl.ANY)
    smem = pl.BlockSpec(memory_space=pltpu.SMEM)
    dma = pltpu.SemaphoreType.DMA

    def now(step):
        return jnp.minimum(step, HEAD_STEPS - 1)

    def tail(step):
        return jnp.maximum(step - HEAD_STEPS, 0)

    head_block = pl.BlockSpec((PAIR, LEN), lambda s: (now(s) // 4, lax.rem(now(s) // 2, 2)))
    tail_block = pl.BlockSpec((LEN // 2, D), lambda s: (tail(s), 0))
    whole = pl.BlockSpec((PIECES, D), lambda s: (0, 0))
    sums_block = pl.BlockSpec((16, D), lambda s: (0, 0))
    return pl.pallas_call(
        back_kernel,
        grid=(BACK_DRAIN,),
        in_specs=[
            smem,
            pl.BlockSpec((1, LEN, LEN), lambda s: (now(s), 0, 0)),
            pl.BlockSpec((1, 1, LEN), lambda s: (now(s), 0, 0)),
            pl.BlockSpec((LEN, PAIR), lambda s: (lax.rem(now(s) // 2, 2), now(s) // 4)),
            head_block,
            head_block,
            head_block,
            head_block,
            pl.BlockSpec((1, D, WIDE), lambda s: (now(s) // 4, 0, 0)),
            pl.BlockSpec((tokens, D), lambda s: (0, 0), pipeline_mode=pl.Buffered(1)),
            tail_block,
            tail_block,
            whole,
            any_spec,
            sums_block,
            any_spec,
        ],
        out_specs=[any_spec] * 4 + [sums_block],
        out_shape=[
            jax.ShapeDtypeStruct((2 * rows, length // 2, D), b16),
            jax.ShapeDtypeStruct((2 * rows, length // 2, D), b16),
            jax.ShapeDtypeStruct((3, HALF, D), b16),
            jax.ShapeDtypeStruct((CAP, HALF, D), b16),
            jax.ShapeDtypeStruct((16, D), f32),
        ],
        scratch_shapes=[
            pltpu.VMEM((tokens, D), f32),
            pltpu.VMEM((WIDE, D), f32),
            pltpu.VMEM((WIDE, LEN), b16),
            pltpu.VMEM((BACK_TAIL, LEN // 2, D), b16),
            pltpu.VMEM((REST, HALF, D), b16),
            pltpu.VMEM((FLOWS, REST, NEAR, D), b16),
            pltpu.VMEM((FLOWS, 3, REST, KEEP, D), b16),
            pltpu.VMEM((3, HALF, D), b16),
            pltpu.VMEM((PAIRS, HALF, WIDE), b16),
            pltpu.VMEM((FLOWS, PAIRS, NEAR, WIDE), b16),
            pltpu.VMEM((FLOWS, 3, PAIRS, KEEP, WIDE), b16),
            pltpu.VMEM((PAIRS, HALF, WIDE), b16),
            pltpu.VMEM((PAIRS, HALF, WIDE), b16),
            pltpu.VMEM((FLOWS, PAIRS, KEEP, WIDE), b16),
            pltpu.VMEM((FLOWS, PAIRS, NEAR, WIDE), b16),
            pltpu.VMEM((FLOWS, 2 * CAP, KEEP, D), b16),
            pltpu.VMEM((FLOWS, 2 * CAP, KEEP, D), b16),
            pltpu.VMEM((FLOWS, CAP, NEAR, D), b16),
            pltpu.VMEM((FLOWS, CAP, NEAR, D), b16),
            pltpu.VMEM((FLOWS, CAP, KEEP, D), b16),
            pltpu.VMEM((5, 16, D), f32),
            dma((REST, FLOWS, 5)),
            dma((REST, FLOWS, 5)),
            dma((PAIRS, FLOWS, 7)),
            dma((PAIRS, FLOWS, 7)),
            dma((FLOWS, 2)),
            dma((FLOWS, 2)),
            dma((FLOWS, 3)),
            dma((REST,)),
            dma((REST,)),
            dma((PAIRS,)),
            dma((PAIRS,)),
            dma((3,)),
            dma((PAIRS, 3)),
            dma((3,)),
            dma((3,)),
            dma((3,)),
            dma((5,)),
            dma((5,)),
        ],
        compiler_params=pltpu.CompilerParams(
            collective_id=1, has_side_effects=True, vmem_limit_bytes=62 * MIB
        ),
        name="back",
    )(table, *attention, weights, normed, x, residual, vectors, tiles, sums, y)


def update_kernel(tile_at, one, two, w_ref, m_ref, s_ref, y_in, i_in, w_out, m_out, s_out, y_out, i_out):
    step = pl.program_id(0)
    tile = tile_at[step // 2]
    grad = jnp.where(tile < 3, one[0], two[0]).astype(f32)
    parts = adam_step(w_ref[0], grad, m_ref[0], s_ref[0], RATE)
    for target, part in zip((w_out, m_out, s_out), parts):
        target[0] = jnp.where(tile >= 0, part, jnp.zeros_like(part))

    @pl.when(step < 4)
    def widen():
        y_out[...] = y_in[...].astype(f32)
        i_out[...] = i_in[...].astype(f32)


def update(tile_at, one, two, master, first, second, y, grad):
    tokens = y.shape[0]
    size = HALF // 2
    state = pl.BlockSpec((1, size, D), lambda s, tile_at: (s // 2, lax.rem(s, 2), 0))
    wide = pl.BlockSpec((tokens // 4, D), lambda s, tile_at: (jnp.minimum(s, 3), 0))
    return pl.pallas_call(
        update_kernel,
        grid_spec=pltpu.PrefetchScalarGridSpec(
            num_scalar_prefetch=1,
            grid=(CAP * 2,),
            in_specs=[
                pl.BlockSpec(
                    (1, size, D),
                    lambda s, tile_at: (jnp.clip(tile_at[s // 2], 0, 2), lax.rem(s, 2), 0),
                ),
                state,
                state,
                state,
                state,
                wide,
                wide,
            ],
            out_specs=[state] * 3 + [wide] * 2,
        ),
        out_shape=[jax.ShapeDtypeStruct(master.shape, f32)] * 3
        + [jax.ShapeDtypeStruct((tokens, D), f32)] * 2,
        compiler_params=pltpu.CompilerParams(vmem_limit_bytes=60 * MIB),
        name="update",
    )(tile_at, one, two, master, first, second, y, grad)


def shards_paired(
    inputs,
    cotangent,
    doc_lengths,
    owner_list,
    master,
    first_moment,
    second_moment,
    vectors,
    vector_first,
    vector_second,
):
    rows_here, span, width = inputs.shape
    place = lax.axis_index("blk")
    member = lax.axis_index("dp")
    rows_mine = rows_here // 2
    order = jnp.arange(PIECES)
    same_owner = owner_list[:, None] == owner_list[None, :]
    ranks = jnp.sum(same_owner & (order[None, :] < order[:, None]), axis=1).astype(jnp.int32)
    slot_of = owner_list * CAP + ranks
    front_outs = front(owner_list, doc_lengths, master, vectors, inputs, cotangent)
    x, cot, normed, weights_one, weights_two, queries, keys, values = front_outs[:8]
    weights, recips, context_turned, context = front_outs[8:]
    x = x.reshape(-1, width)
    cot = cot.reshape(-1, width)
    block_out, residual, grad_context, sums, tiles_two = feed(
        context, context_turned, x, cot, weights_two, vectors
    )
    hits = jnp.arange(16 * CAP)[:, None] == slot_of[None, :]
    tile_at = jnp.sum(jnp.where(hits, order[None, :] + 1, 0), axis=1).astype(jnp.int32) - 1
    table = jnp.maximum(tile_at - 3, 0)
    block_out, input_grad, total_one, total_two, vector_total = back(
        table,
        (weights, recips, values, queries, keys, context_turned, grad_context),
        weights_one,
        normed,
        x,
        residual,
        vectors,
        tiles_two,
        sums,
        block_out.reshape(rows_mine, LEN, width),
    )
    mine = lax.dynamic_slice_in_dim(tile_at, member * CAP, CAP, 0)
    *updated, block_out, input_grad = update(
        mine,
        total_one,
        total_two,
        master,
        first_moment,
        second_moment,
        block_out.reshape(-1, width),
        input_grad.reshape(-1, width),
    )
    columns = vector_first.shape[1]
    vector_cols = lax.dynamic_slice_in_dim(vectors, place * columns, columns, 1)
    vector_total = lax.dynamic_slice(vector_total, (0, place * columns), (PIECES, columns))
    updated_vectors = adam_step(vector_cols, vector_total, vector_first, vector_second, VEC_RATE)
    return (
        block_out.reshape(inputs.shape),
        input_grad.reshape(inputs.shape),
        *updated,
        *updated_vectors,
    )


def solution(mesh):
    in_specs = (
        P("dp", "blk", None),
        P("dp", "blk", None),
        P("dp", None),
        P(),
        P("dp", "blk", None),
        P("dp", "blk", None),
        P("dp", "blk", None),
        P(),
        P(None, "blk"),
        P(None, "blk"),
    )
    out_specs = (
        P("dp", "blk", None),
        P("dp", "blk", None),
        P("dp", "blk", None),
        P("dp", "blk", None),
        P("dp", "blk", None),
        P(None, "blk"),
        P(None, "blk"),
        P(None, "blk"),
    )
    paired = mesh.shape["blk"] == 2 and mesh.shape["dp"] == 16
    shards = shards_paired if paired else shards_any
    return jax.shard_map(shards, mesh=mesh, in_specs=in_specs, out_specs=out_specs, check_vma=False)
```

```python
from functools import partial

import jax
import jax.numpy as jnp
from jax import lax
from jax.experimental import pallas as pl
from jax.experimental.pallas import tpu as pltpu
from jax.sharding import PartitionSpec as P

D = 768
FF = 3072
HEADS = 12
HEAD_DIM = 64
LEN = 1024
CAP = 3
STEP = 10
PIECES = 12


EPS_NORM = 1e-05
BETA_ONE = 0.9
BETA_TWO = 0.999
RATE = 0.04
VEC_RATE = 0.25
DECAY = 0.01
ADAM_EPS = 1e-08


def normalize(values_in, gain, shift):
    center = jnp.mean(values_in, axis=-1, keepdims=True)
    offset = values_in - center
    spread = jnp.mean(offset * offset, axis=-1, keepdims=True)
    return offset * lax.rsqrt(spread + EPS_NORM) * gain + shift


def adam_step(weight, grad, first, second, rate):
    first_new = BETA_ONE * first + (1.0 - BETA_ONE) * grad
    second_new = BETA_TWO * second + (1.0 - BETA_TWO) * grad * grad
    corrected = (
        first_new
        / (1.0 - BETA_ONE**STEP)
        / (jnp.sqrt(second_new / (1.0 - BETA_TWO**STEP)) + ADAM_EPS)
    )
    return (weight - rate * (corrected + DECAY * weight), first_new, second_new)


def shards_any(
    inputs,
    cotangent,
    doc_lengths,
    owner_list,
    master,
    first_moment,
    second_moment,
    vectors,
    vector_first,
    vector_second,
):
    rows_here, span, width = inputs.shape
    tokens_here = rows_here * span
    fold = FF // D
    scale = HEAD_DIM ** (-0.5)
    place = lax.axis_index("blk")
    f32 = jnp.float32
    b16 = jnp.bfloat16
    order = jnp.arange(PIECES)
    same_owner = owner_list[:, None] == owner_list[None, :]
    ranks = jnp.sum(same_owner & (order[None, :] < order[:, None]), axis=1)
    slot_of = owner_list * CAP + ranks

    mine = (owner_list == lax.axis_index("dp"))[:, None, None]
    tile_rows = lax.psum(jnp.where(mine, master[ranks], 0.0).astype(b16), "dp")
    tiles = lax.all_gather(tile_rows, "blk", axis=1, tiled=True)
    query_weight = tiles[0]
    key_weight = tiles[1]
    value_weight = tiles[2]
    out_weight = tiles[3]
    up_weight = jnp.transpose(tiles[4 : 4 + fold], (1, 0, 2)).reshape(width, FF)
    down_weight = tiles[4 + fold :].reshape(FF, width)
    flat_in = inputs.reshape(tokens_here, width).astype(f32)
    normed_one = normalize(flat_in, vectors[0], vectors[1]).astype(b16)
    queries = (jnp.dot(normed_one, query_weight, preferred_element_type=f32) + vectors[4]).astype(
        b16
    )
    keys_here = jnp.dot(normed_one, key_weight, preferred_element_type=f32).astype(b16)
    values_here = (
        jnp.dot(normed_one, value_weight, preferred_element_type=f32) + vectors[5]
    ).astype(b16)
    query_heads = queries.reshape(rows_here, span, HEADS, HEAD_DIM)
    first_len = doc_lengths[:, 0]
    query_seg = (place * span + jnp.arange(span))[None, :] >= first_len[:, None]

    def block_scores(key_block, start):
        count = key_block.shape[1]
        key_heads = key_block.reshape(rows_here, count, HEADS, HEAD_DIM)
        raw = (
            jnp.einsum("rqhd,rkhd->rhqk", query_heads, key_heads, preferred_element_type=f32)
            * scale
        )
        key_seg = (start + jnp.arange(count))[None, :] >= first_len[:, None]
        allowed = query_seg[:, None, :, None] == key_seg[:, None, None, :]
        return (raw, allowed)

    key_rows = keys_here.reshape(rows_here, span, width)
    value_rows = values_here.reshape(rows_here, span, width)
    top = jnp.full((rows_here, HEADS, span), -1e30, f32)
    key_block = lax.all_gather(key_rows, "blk", axis=1, tiled=True)
    value_block = lax.all_gather(value_rows, "blk", axis=1, tiled=True)
    count = key_block.shape[1]
    raw, allowed = block_scores(key_block, jnp.int32(0))
    new_top = jnp.maximum(top, jnp.max(jnp.where(allowed, raw, -1e30), axis=-1))
    weights = jnp.where(allowed, jnp.exp(raw - new_top[..., None]), 0.0)
    value_heads = value_block.reshape(rows_here, count, HEADS, HEAD_DIM)
    update = jnp.einsum(
        "rhqk,rkhd->rhqd", weights.astype(b16), value_heads, preferred_element_type=f32
    )
    total = jnp.sum(weights, axis=-1)
    log_total = new_top + jnp.log(total)
    context_raw = update / total[..., None]
    context_low = jnp.transpose(context_raw, (0, 2, 1, 3)).reshape(tokens_here, width).astype(b16)
    residual = flat_in + (jnp.dot(context_low, out_weight, preferred_element_type=f32) + vectors[6])
    normed_two = normalize(residual, vectors[2], vectors[3]).astype(b16)
    hidden = jnp.dot(normed_two, up_weight, preferred_element_type=f32) + vectors[8:].reshape(FF)
    gelu_exact = partial(jax.nn.gelu, approximate=False)
    active, gelu_pull = jax.vjp(gelu_exact, hidden)
    active_low = active.astype(b16)
    block_out = (
        residual + (jnp.dot(active_low, down_weight, preferred_element_type=f32) + vectors[7])
    ).reshape(rows_here, span, width)
    grad_out = cotangent.reshape(tokens_here, width)
    down_grad = jnp.einsum("tf,td->fd", active_low, grad_out, preferred_element_type=f32)
    down_sum = jnp.sum(grad_out, axis=0, dtype=f32)
    grad_active = jnp.einsum("td,fd->tf", grad_out, down_weight, preferred_element_type=f32)
    grad_hidden = gelu_pull(grad_active)[0].astype(b16)
    up_grad = jnp.einsum("td,tf->df", normed_two, grad_hidden, preferred_element_type=f32)
    up_sum = jnp.sum(grad_hidden, axis=0, dtype=f32)
    ffn_tiles = jnp.concatenate(
        [
            jnp.transpose(up_grad.reshape(width, fold, width), (1, 0, 2)),
            down_grad.reshape(fold, width, width),
        ],
        axis=0,
    )
    grad_normed_two = jnp.einsum("tf,df->td", grad_hidden, up_weight, preferred_element_type=f32)
    unused, second_pull = jax.vjp(normalize, residual, vectors[2], vectors[3])
    residual_part, gain_two_grad, shift_two_grad = second_pull(grad_normed_two)
    grad_residual = grad_out.astype(f32) + residual_part
    grad_attended = grad_residual.astype(b16)
    out_grad = jnp.einsum("tm,td->md", context_low, grad_attended, preferred_element_type=f32)
    out_sum = jnp.sum(grad_attended, axis=0, dtype=f32)
    grad_context = jnp.einsum(
        "td,md->tm", grad_attended, out_weight, preferred_element_type=f32
    ).astype(b16)
    grad_heads = grad_context.reshape(rows_here, span, HEADS, HEAD_DIM)
    delta = jnp.einsum("rqhd,rhqd->rhq", grad_heads.astype(f32), context_raw)
    key_all, value_all = (
        lax.all_gather(key_rows, "blk", axis=1, tiled=True),
        lax.all_gather(value_rows, "blk", axis=1, tiled=True),
    )
    key_size = min(512, LEN)

    def back_block(index, carry):
        grad_query, key_total, value_total = carry
        start = index * key_size
        key_block = lax.dynamic_slice_in_dim(key_all, start, key_size, 1)
        value_block = lax.dynamic_slice_in_dim(value_all, start, key_size, 1)
        raw, allowed = block_scores(key_block, start)
        weights_back = jnp.where(allowed, jnp.exp(raw - log_total[..., None]), 0.0)
        key_heads = key_block.reshape(rows_here, key_size, HEADS, HEAD_DIM)
        value_heads = value_block.reshape(rows_here, key_size, HEADS, HEAD_DIM)
        value_grad = jnp.einsum(
            "rhqk,rqhd->rkhd", weights_back.astype(b16), grad_heads, preferred_element_type=f32
        )
        weight_grad = jnp.einsum(
            "rqhd,rkhd->rhqk", grad_heads, value_heads, preferred_element_type=f32
        )
        score_grad = (weights_back * (weight_grad - delta[..., None])).astype(b16)
        grad_query = (
            grad_query
            + jnp.einsum("rhqk,rkhd->rqhd", score_grad, key_heads, preferred_element_type=f32)
            * scale
        )
        key_grad = (
            jnp.einsum("rhqk,rqhd->rkhd", score_grad, query_heads, preferred_element_type=f32)
            * scale
        )
        key_total = lax.dynamic_update_slice_in_dim(
            key_total, key_grad.reshape(rows_here, key_size, width), start, 1
        )
        value_total = lax.dynamic_update_slice_in_dim(
            value_total, value_grad.reshape(rows_here, key_size, width), start, 1
        )
        return (grad_query, key_total, value_total)

    zero_rows = jnp.zeros((rows_here, LEN, width), f32)
    grad_query, key_total, value_total = lax.fori_loop(
        0,
        LEN // key_size,
        back_block,
        (jnp.zeros((rows_here, span, HEADS, HEAD_DIM), f32), zero_rows, zero_rows),
    )
    key_grad_here, value_grad_here = (
        lax.psum_scatter(
            key_total.astype(jnp.bfloat16), "blk", scatter_dimension=1, tiled=True
        ).astype(jnp.float32),
        lax.psum_scatter(
            value_total.astype(jnp.bfloat16), "blk", scatter_dimension=1, tiled=True
        ).astype(jnp.float32),
    )
    query_low = grad_query.reshape(tokens_here, width).astype(b16)
    key_low = key_grad_here.reshape(tokens_here, width).astype(b16)
    value_low = value_grad_here.reshape(tokens_here, width).astype(b16)
    query_tile = jnp.einsum("td,te->de", normed_one, query_low, preferred_element_type=f32)
    key_tile = jnp.einsum("td,te->de", normed_one, key_low, preferred_element_type=f32)
    value_tile = jnp.einsum("td,te->de", normed_one, value_low, preferred_element_type=f32)
    grad_normed_one = (
        jnp.einsum("te,de->td", query_low, query_weight, preferred_element_type=f32)
        + jnp.einsum("te,de->td", key_low, key_weight, preferred_element_type=f32)
        + jnp.einsum("te,de->td", value_low, value_weight, preferred_element_type=f32)
    )
    unused, first_pull = jax.vjp(normalize, flat_in, vectors[0], vectors[1])
    input_part, gain_one_grad, shift_one_grad = first_pull(grad_normed_one)
    input_grad = (grad_residual + input_part).reshape(rows_here, span, width)
    vector_grads = jnp.concatenate(
        [
            jnp.stack(
                [
                    gain_one_grad,
                    shift_one_grad,
                    gain_two_grad,
                    shift_two_grad,
                    jnp.sum(query_low, axis=0, dtype=f32),
                    jnp.sum(value_low, axis=0, dtype=f32),
                    out_sum,
                    down_sum,
                ]
            ),
            up_sum.reshape(fold, width),
        ],
        axis=0,
    )
    attn_tiles = jnp.stack([query_tile, key_tile, value_tile, out_grad])
    piece_share, vector_share = (
        lax.psum_scatter(
            jnp.concatenate([attn_tiles, ffn_tiles], axis=0).astype(jnp.bfloat16),
            "blk",
            scatter_dimension=1,
            tiled=True,
        ).astype(jnp.float32),
        lax.psum_scatter(
            vector_grads.astype(jnp.bfloat16), "blk", scatter_dimension=1, tiled=True
        ).astype(jnp.float32),
    )
    own_slots = lax.axis_index("dp") * CAP + jnp.arange(CAP)
    pick = (own_slots[:, None] == slot_of[None, :]).astype(f32)
    occupied = jnp.sum(pick, axis=1)[:, None, None]
    total_share, vector_total = (
        lax.psum(piece_share.astype(jnp.bfloat16), "dp").astype(jnp.float32),
        lax.psum(vector_share.astype(jnp.bfloat16), "dp").astype(jnp.float32),
    )
    slot_grads = jnp.einsum("cp,prd->crd", pick, total_share, precision=lax.Precision.HIGHEST)
    new_master, new_first, new_second = adam_step(
        master, slot_grads, first_moment, second_moment, RATE
    )
    columns = vector_first.shape[1]
    vector_cols = lax.dynamic_slice_in_dim(vectors, place * columns, columns, 1)
    new_vectors, new_vector_first, new_vector_second = adam_step(
        vector_cols, vector_total, vector_first, vector_second, VEC_RATE
    )
    return (
        block_out,
        input_grad,
        new_master * occupied,
        new_first * occupied,
        new_second * occupied,
        new_vectors,
        new_vector_first,
        new_vector_second,
    )


f32 = jnp.float32
b16 = jnp.bfloat16
LOG2E = 1.4426950408889634
MIB = 1024 * 1024
PAIRS = HEADS // 2
PAIR = 2 * HEAD_DIM


def dot_nn(left, right):
    return lax.dot_general(left, right, (((1,), (0,)), ((), ())), preferred_element_type=f32)


def dot_nt(left, right):
    return lax.dot_general(left, right, (((1,), (1,)), ((), ())), preferred_element_type=f32)


def dot_tn(left, right):
    return lax.dot_general(left, right, (((0,), (0,)), ((), ())), preferred_element_type=f32)


def norm_parts(values_in):
    center = jnp.mean(values_in, axis=-1, keepdims=True)
    offset = values_in - center
    spread = jnp.mean(offset * offset, axis=-1, keepdims=True)
    rstd = lax.rsqrt(spread + EPS_NORM)
    return offset * rstd, rstd


def norm_back(grad, unit, rstd, gain):
    scaled = grad * gain
    first = jnp.mean(scaled, axis=-1, keepdims=True)
    second = jnp.mean(scaled * unit, axis=-1, keepdims=True)
    return rstd * (scaled - first - unit * second)


def gelu_parts(value):
    bell = jnp.exp2(value * value * (-0.5 * LOG2E))
    ratio = pl.reciprocal(1.0 + (0.3275911 * 0.7071067811865476) * jnp.abs(value))
    poly = 0.5 * 1.061405429
    poly = poly * ratio + 0.5 * -1.453152027
    poly = poly * ratio + 0.5 * 1.421413741
    poly = poly * ratio + 0.5 * -0.284496736
    poly = poly * ratio + 0.5 * 0.254829592
    tail = poly * ratio * bell
    cdf = jnp.where(value >= 0.0, 1.0 - tail, tail)
    return value * cdf, cdf + value * (bell * 0.3989422804014327)


def head_only(block, head):
    lane = lax.broadcasted_iota(jnp.int32, block.shape, 1)
    keep = (lane >= head * HEAD_DIM) & (lane < (head + 1) * HEAD_DIM)
    return jnp.where(keep, block, jnp.zeros_like(block))


def feed_kernel(
    c_ref, o_ref, x_ref, g_ref, w_ref, vec_ref,
    y_ref, r_ref, d_ref, sums_ref, tiles_ref,
    acc_ref, unit_ref, rstd_ref, normed, out_ref, grad_ref,
    hidden_ref, pulled_ref, active_ref, slope_ref, stage_ref, sem_ref,
):
    fold = FF // D
    step = pl.program_id(0)
    blocks = [slice(start, start + 16) for start in range(0, x_ref.shape[0], 16)]

    @pl.when(step == 0)
    def clear():
        acc_ref[...] = jnp.zeros_like(acc_ref)
        sums_ref[...] = jnp.zeros_like(sums_ref)

    def eights(value):
        return jnp.sum(value.reshape(-1, 8, D), axis=0)

    def add_sum(row, value):
        sums_ref[row : row + 1, :] += jnp.sum(value, 0, keepdims=True)

    out_ref[...] = dot_nn(c_ref[...], w_ref[0])
    gain = vec_ref[2:3, :]
    for rows in blocks:
        residual = x_ref[rows].astype(f32) + (out_ref[rows] + vec_ref[6:7, :])
        unit, rstd = norm_parts(residual)
        unit_ref[rows] = unit
        rstd_ref[rows] = jnp.broadcast_to(rstd, (16, 128))
        normed[rows] = (unit * gain + vec_ref[3:4, :]).astype(b16)
        out_ref[rows] = residual + vec_ref[7:8, :]
    turned = normed[...].T
    cot = g_ref[...]

    def begin(part):
        hidden_ref[part % 2] = dot_nn(normed[...], w_ref[1 + part])
        pulled_ref[part % 2] = dot_nt(cot, w_ref[1 + fold + part])

    begin(0)
    for part in range(fold):
        slot = part % 2
        if part + 1 < fold:
            begin(part + 1)
        total = jnp.zeros((8, D), f32)
        for rows in blocks:
            active, slope = gelu_parts(hidden_ref[slot, rows] + vec_ref[8 + part : 9 + part, :])
            active_ref[slot, rows] = active.astype(b16)
            pulled = (pulled_ref[slot, rows] * slope).astype(b16)
            slope_ref[slot, rows] = pulled
            total = total + eights(pulled.astype(f32))
        add_sum(8 + part, total)
        out_ref[...] += dot_nn(active_ref[slot], w_ref[1 + fold + part])
        grad = dot_nt(slope_ref[slot], w_ref[1 + part])
        grad_ref[...] = grad if part == 0 else grad_ref[...] + grad
        acc_ref[1 + part] += dot_nn(turned, slope_ref[slot])
        acc_ref[1 + fold + part] += dot_tn(active_ref[slot], cot)
    y_ref[...] = out_ref[...].astype(b16)
    totals = [jnp.zeros((8, D), f32) for unused in range(4)]
    for rows in blocks:
        grad, unit, wide = grad_ref[rows], unit_ref[rows], g_ref[rows].astype(f32)
        back = wide + norm_back(grad, unit, rstd_ref[rows, 0:1], gain)
        low = back.astype(b16)
        r_ref[rows] = low
        terms = (grad * unit, grad, low.astype(f32), wide)
        totals = [total + eights(term) for total, term in zip(totals, terms)]
    for row, total in zip((2, 3, 6, 7), totals):
        add_sum(row, total)
    low = r_ref[...]
    d_ref[...] = dot_nt(w_ref[0], low).astype(b16)
    acc_ref[0] += dot_nn(o_ref[...], low)

    @pl.when(step == pl.num_programs(0) - 1)
    def send():
        count = 1 + 2 * fold
        copies = []
        for part in range(count):
            if part >= 2:
                copies[part - 2].wait()
            stage_ref[part % 2] = acc_ref[part].astype(b16)
            copy = pltpu.make_async_copy(stage_ref.at[part % 2], tiles_ref.at[part], sem_ref.at[part % 2])
            copy.start()
            copies.append(copy)
        copies[count - 2].wait()
        copies[count - 1].wait()


def feed(context, turned, x, cot, weights, vectors):
    tokens = x.shape[0]
    size = 256
    count = 1 + 2 * (FF // D)
    token_block = pl.BlockSpec((size, D), lambda i: (i, 0))
    turned_block = pl.BlockSpec((D, size), lambda i: (0, i))
    return pl.pallas_call(
        feed_kernel,
        grid=(tokens // size,),
        in_specs=[
            token_block,
            turned_block,
            token_block,
            token_block,
            pl.BlockSpec((count, D, D), lambda i: (0, 0, 0), pipeline_mode=pl.Buffered(1)),
            pl.BlockSpec((PIECES, D), lambda i: (0, 0)),
        ],
        out_specs=[
            token_block,
            token_block,
            turned_block,
            pl.BlockSpec((16, D), lambda i: (0, 0)),
            pl.BlockSpec(memory_space=pl.ANY),
        ],
        out_shape=[
            jax.ShapeDtypeStruct((tokens, D), b16),
            jax.ShapeDtypeStruct((tokens, D), b16),
            jax.ShapeDtypeStruct((D, tokens), b16),
            jax.ShapeDtypeStruct((16, D), f32),
            jax.ShapeDtypeStruct((count, D, D), b16),
        ],
        scratch_shapes=[
            pltpu.VMEM((count, D, D), f32),
            pltpu.VMEM((size, D), f32),
            pltpu.VMEM((size, 128), f32),
            pltpu.VMEM((size, D), b16),
            pltpu.VMEM((size, D), f32),
            pltpu.VMEM((size, D), f32),
            pltpu.VMEM((2, size, D), f32),
            pltpu.VMEM((2, size, D), f32),
            pltpu.VMEM((2, size, D), b16),
            pltpu.VMEM((2, size, D), b16),
            pltpu.VMEM((2, D, D), b16),
            pltpu.SemaphoreType.DMA((2,)),
        ],
        compiler_params=pltpu.CompilerParams(vmem_limit_bytes=60 * MIB),
        cost_estimate=pl.CostEstimate(
            flops=6 * count * tokens * D * D,
            bytes_accessed=18 * tokens * D + 4 * count * D * D,
            transcendentals=2 * tokens * FF,
        ),
        name="feed",
    )(context, turned, x, cot, weights, vectors)


MESH = pl.DeviceIdType.MESH
HALF = D // 2
FLOWS = 2
FLOW = HALF // FLOWS
NEAR = FLOW // 2
KEEP = NEAR // 2
WIDE = 3 * PAIR
REST = PIECES - 3
GROUPS = ((0, 1), (1, 2), (3, 3))
CHUNKS = len(GROUPS)


class Place:
    def __init__(self):
        self.me = lax.axis_index("dp")
        self.core = lax.axis_index("blk")
        self.bits = [lax.rem(self.me // weight, 2) for weight in (1, 2, 4, 8)]
        self.chips = [
            self.me + weight - 2 * weight * bit for weight, bit in zip((1, 2, 4, 8), self.bits)
        ]
        self.partners = [{"dp": chip} for chip in self.chips]
        low, high = self.bits[2:]
        self.inner = low != high
        self.across = {"dp": self.me + 4 - 8 * low + 8 - 16 * high}
        self.other = 1 - self.core
        self.twin = {"blk": self.other}

    def greet(self):
        barrier = pltpu.get_barrier_semaphore()
        for device in self.partners + [self.across, self.twin]:
            pl.semaphore_signal(barrier, 1, device_id=device, device_id_type=MESH)
        pl.semaphore_wait(barrier, 6)

    def flow(self, index):
        first, second = (0, 1) if index == 0 else (1, 0)
        base = index * FLOW
        near = base + self.bits[first] * NEAR
        far = base + NEAR - self.bits[first] * NEAR
        keep = near + self.bits[second] * KEEP
        give = near + KEEP - self.bits[second] * KEEP
        return first, second, near, far, keep, give


def remote(source, target, send, receive, device):
    return pltpu.make_async_remote_copy(
        src_ref=source,
        dst_ref=target,
        send_sem=send,
        recv_sem=receive,
        device_id=device,
        device_id_type=MESH,
    )


def rows_at(start, count):
    return pl.ds(pl.multiple_of(start, 16), count)


class Spread:
    def __init__(self, place, owner, rank, slots, land, gift, sems):
        self.place, self.owner, self.rank = place, owner, rank
        self.slots, self.land, self.gift, self.sems = slots, land, gift, sems

    def cols(self, chunk):
        return pl.ds(GROUPS[chunk][0] * PAIR, GROUPS[chunk][1] * PAIR)

    def first_copy(self, chunk, index):
        first, second, near, far, keep, give = self.place.flow(index)
        return remote(
            self.slots.at[:, rows_at(far, NEAR), self.cols(chunk)],
            self.land[chunk].at[index],
            self.sems[0].at[chunk, index, 0],
            self.sems[1].at[chunk, index, 0],
            self.place.partners[first],
        )

    def second_copy(self, chunk, index, which):
        first, second, near, far, keep, give = self.place.flow(index)
        if which == 0:
            source = self.slots.at[:, rows_at(give, KEEP), self.cols(chunk)]
        else:
            source = self.land[chunk].at[index, :, rows_at(give - near, KEEP)]
        return remote(
            source,
            self.gift[chunk].at[index, pl.ds(which * CAP, CAP)],
            self.sems[0].at[chunk, index, 1 + which],
            self.sems[1].at[chunk, index, 1 + which],
            self.place.partners[second],
        )

    def step(self, chunk, index):
        for flow in range(FLOWS):
            if index == 0:
                self.first_copy(chunk, flow).start()
                self.second_copy(chunk, flow, 0).start()
            if index == 1:
                self.first_copy(chunk, flow).wait()
                self.second_copy(chunk, flow, 1).start()
            if index == 2:
                self.second_copy(chunk, flow, 0).wait()
                self.second_copy(chunk, flow, 1).wait()

    def piece(self, tile, index, chunk, start, count):
        first, second, near, far, keep, give = self.place.flow(index)
        owner, rank = self.owner[tile], self.rank[tile]
        bits = [lax.rem(owner, 2), lax.rem(owner // 2, 2)]
        apart = [bit != mine for bit, mine in zip(bits, self.place.bits)]
        cols = pl.ds(start, count)
        mine = self.slots[rank, rows_at(keep, KEEP), pl.ds(GROUPS[chunk][0] * PAIR + start, count)]
        firsts = self.land[chunk][index, rank, rows_at(keep - near, KEEP), cols]
        gifts = self.gift[chunk][index, jnp.where(apart[first], CAP, 0) + rank, :, cols]
        value = jnp.where(apart[second], gifts, jnp.where(apart[first], firsts, mine))
        layer = owner // 4 == self.place.me // 4
        return jnp.where(layer, value, jnp.zeros_like(value))


class Column:
    steps = 4

    def __init__(self, place, kept, read, write, land, sems):
        self.place, self.kept, self.read, self.write = place, kept, read, write
        self.land, self.sems = land, sems

    def copy(self, index):
        target = self.land.at[index % 2]
        device = self.place.across if index == 1 else self.place.partners[2]
        return remote(
            self.kept, target, self.sems[0].at[index], self.sems[1].at[index], device
        )

    def add(self, index):
        self.write((self.read().astype(f32) + self.land[index].astype(f32)).astype(b16))


def column_step(place, columns, index):
    @pl.when(place.inner)
    def inner():
        for column in columns:
            if index == 1:
                column.copy(0).wait_recv()
                column.add(0)
                column.copy(1).start()
            if index == 2:
                column.copy(1).wait()
                column.add(1)
                column.copy(2).start()
            if index == 3:
                column.copy(2).wait_send()

    @pl.when(jnp.logical_not(place.inner))
    def outer():
        for column in columns:
            if index == 0:
                column.copy(0).start()
            if index == 1:
                column.copy(0).wait_send()
            if index == 3:
                column.copy(2).wait_recv()
                column.write(column.land[0])


class Item:
    steps = 7

    def __init__(self, place, work, land, sems, load, store=None):
        self.place, self.work, self.land, self.sems = place, work, land, sems
        self.load, self.store = load, store
        self.base = place.core * HALF

    def column(self, flow):
        rows = rows_at(self.base + self.place.flow(flow)[4], KEEP)

        def read():
            return self.work[:, rows]

        def write(value):
            self.work[:, rows] = value

        sems = (self.sems[0].at[flow], self.sems[1].at[flow])
        return Column(self.place, self.work.at[:, rows], read, write, self.land.at[flow], sems)

    def copy(self, flow, index):
        first, second, near, far, keep, give = self.place.flow(flow)
        kept = self.work.at[:, rows_at(self.base + keep, KEEP)]
        half = self.work.at[:, rows_at(self.base + near, NEAR)]
        source, device = [
            (kept, self.place.partners[second]),
            (half, self.place.partners[first]),
        ][index]
        return remote(
            source, source, self.sems[0].at[flow, 3 + index], self.sems[1].at[flow, 3 + index], device
        )

    def pair(self):
        rows = self.work.at[:, rows_at(self.base, HALF)]
        return remote(rows, rows, self.sems[0].at[0, 5], self.sems[1].at[0, 5], self.place.twin)

    def step(self, index):
        for flow in range(FLOWS):
            if index == 0:
                self.load(self.work, rows_at(self.base + self.place.flow(flow)[4], KEEP), flow)
        if index <= 3:
            column_step(self.place, [self.column(flow) for flow in range(FLOWS)], index)
        for flow in range(FLOWS):
            if 4 <= index <= 5:
                self.copy(flow, index - 4).wait()
            if 3 <= index <= 4:
                self.copy(flow, index - 3).start()
        if index == 5:
            self.pair().start()
        if index == 6:
            self.pair().wait()
            self.store().start()


REST_GROUPS = tuple((index, 1) for index in range(REST))
PAIR_CHUNK = (0, 1, 1, 2, 2, 2)
FRONT_PAIRS = (2, 4, 5, 6, 7, 8)
FRONT_REST = (6, 7, 8, 9, 10, 11, 12, 13, 14)
FRONT_LEAD = 9


def front_kernel(
    owner, lengths, master, vec_ref, x_in, c_in,
    x_out, c_out, n_out, one_out, two_out, q_ref, k_ref, v_ref, p_ref, r_ref, o_ref, ctx_ref,
    rank, rows_ref, normed, keys, turned_values, scores, slots,
    land_one, land_two, land_three, gift_one, gift_two, gift_three,
    one, one_land, two, two_land,
    spread_send, spread_recv, one_send, one_recv, two_send, two_recv,
    swap_send, swap_recv, swap_local, store_sem,
):
    pair = pl.program_id(0)
    row = pl.program_id(1)
    grid_step = pair * 2 + row
    place = Place()
    rows, span = x_in.shape[0] // 2, x_in.shape[1]
    land = (land_one, land_two, land_three)
    gift = (gift_one, gift_two, gift_three)
    spread = Spread(place, owner, rank, slots, land, gift, (spread_send, spread_recv))

    def swaps(index):
        source, target = [(x_in, rows_ref), (c_in, c_out)][index]
        here = pl.ds(place.core * span, span)
        near = pltpu.make_async_copy(
            source.at[pl.ds(place.core * rows, rows)], target.at[:, here], swap_local.at[index]
        )
        far = remote(
            source.at[pl.ds(place.other * rows, rows)],
            target.at[:, here],
            swap_send.at[index],
            swap_recv.at[index],
            place.twin,
        )
        return near, far

    def row_store():
        return pltpu.make_async_copy(rows_ref, x_out, store_sem.at[PAIRS + REST])

    def normed_store():
        return pltpu.make_async_copy(normed, n_out, store_sem.at[PAIRS + REST + 1])

    def pair_item(group):
        span_of = pl.ds(group, 1)

        def load(work, where, flow):
            chunk = PAIR_CHUNK[group]
            for tile in range(3):
                part = spread.piece(tile, flow, chunk, (group - GROUPS[chunk][0]) * PAIR, PAIR)
                work[0, where, pl.ds(tile * PAIR, PAIR)] = part

        def store():
            return pltpu.make_async_copy(one.at[span_of], one_out.at[span_of], store_sem.at[group])

        sems = (one_send.at[group], one_recv.at[group])
        return Item(place, one.at[span_of], one_land.at[:, :, span_of], sems, load, store)

    def rest_item(group):
        first, count = REST_GROUPS[group]
        span_of = pl.ds(first, count)

        def load(work, where, flow):
            for index in range(count):
                for chunk, (start, wide) in enumerate(GROUPS):
                    part = spread.piece(3 + first + index, flow, chunk, 0, wide * PAIR)
                    work[index, where, pl.ds(start * PAIR, wide * PAIR)] = part

        def store():
            return pltpu.make_async_copy(
                two.at[span_of], two_out.at[span_of], store_sem.at[PAIRS + group]
            )

        sems = (two_send.at[group], two_recv.at[group])
        return Item(place, two.at[span_of], two_land.at[:, :, span_of], sems, load, store)

    def tick(number, odd):
        for chunk in range(CHUNKS):
            if odd == 0 and 0 <= number - 2 * chunk <= 2:
                spread.step(chunk, number - 2 * chunk)
        starts = [(pair_item, group, start) for group, start in enumerate(FRONT_PAIRS)]
        starts += [(rest_item, group, start) for group, start in enumerate(FRONT_REST)]
        for make, group, start in starts:
            if group % 2 == odd and 0 <= number - start < Item.steps:
                make(group).step(number - start)

    def both(number):
        tick(number, 0)
        tick(number, 1)

    @pl.when(grid_step == 0)
    def lead():
        slots[...] = master[...].astype(b16)
        for tile in range(PIECES):
            count = jnp.int32(0)
            for before in range(tile):
                count = count + (owner[before] == owner[tile]).astype(jnp.int32)
            rank[tile] = jnp.minimum(count, CAP - 1)
        place.greet()
        for copy in swaps(0):
            copy.start()
        both(0)
        for copy in swaps(1):
            copy.start()
        for copy in swaps(0):
            copy.wait()
        row_store().start()

        def norm_rows(index, carry):
            for part in range(rows):
                for block in range(4):
                    where = pl.ds(pl.multiple_of(index * 128 + block * 32, 32), 32)
                    unit, unused = norm_parts(rows_ref[part, where].astype(f32))
                    low = (unit * vec_ref[0:1, :] + vec_ref[1:2, :]).astype(b16)
                    normed[pl.ds(pl.multiple_of(part * LEN + index * 128 + block * 32, 32), 32)] = low
            return carry

        both(1)
        lax.fori_loop(0, LEN // 128, norm_rows, 0)
        normed_store().start()
        for number in range(2, FRONT_LEAD):
            both(number)

    for number in range(2 * PAIRS):
        pl.when(grid_step == number)(partial(tick, FRONT_LEAD + number, 0))

    @pl.when(row == 0)
    def project():
        lanes = pl.ds(pl.multiple_of(pair * PAIR, PAIR), PAIR)
        weight = one[pair]

        def part(index, carry):
            where = pl.ds(pl.multiple_of(index * 512, 512), 512)
            both = dot_nn(normed[where], weight)
            queries = both[:, :PAIR] + vec_ref[4:5, lanes]
            queries = (queries * (HEAD_DIM**-0.5 * LOG2E)).astype(b16)
            q_ref[:, where] = queries.T
            low = both[:, PAIR : 2 * PAIR].astype(b16)
            keys[where] = low
            k_ref[:, where] = low.T
            values = (both[:, 2 * PAIR :] + vec_ref[5:6, lanes]).astype(b16)
            v_ref[where] = values
            turned_values[:, where] = values.T
            return carry

        lax.fori_loop(0, normed.shape[0] // 512, part, 0)

    half = LEN // 2
    start = pl.multiple_of(row * LEN, LEN)
    split = lengths[place.core * rows + row, 0] < LEN
    shift = jnp.where(split, jnp.float32(-1e30), jnp.float32(0.0))

    quarter = LEN // 4
    for head, step in [(head, step) for head in range(2) for step in range(2)]:
        if (head, step) == (1, 0):
            for number in range(2 * PAIRS):
                pl.when(grid_step == number)(partial(tick, FRONT_LEAD + number, 1))
        part = slice(head * HEAD_DIM, (head + 1) * HEAD_DIM)
        here = slice(step * half, (step + 1) * half)
        queries = q_ref[:, pl.ds(pl.multiple_of(start + step * half, half), half)]
        peak = None
        for block in range(4):
            rows_here = pl.ds(pl.multiple_of(start + block * quarter, quarter), quarter)
            raw = dot_nn(head_only(keys[rows_here], head), queries)
            if block // 2 != step:
                raw = raw + shift
            scores[step, block * quarter : (block + 1) * quarter] = raw
            best = jnp.max(raw.reshape(-1, 8, half), axis=0)
            peak = best if peak is None else jnp.maximum(peak, best)
        top = jnp.max(peak, 0, keepdims=True)
        total = jnp.zeros((8, half), f32)
        for block in range(LEN // 64):
            rows_here = slice(block * 64, (block + 1) * 64)
            value = jnp.exp2(scores[step, rows_here] - top)
            total = total + jnp.sum(value.reshape(-1, 8, half), axis=0)
            p_ref[head, rows_here, here] = value.astype(b16)
        recip = 1.0 / jnp.sum(total, 0, keepdims=True)
        r_ref[0, head : head + 1, here] = recip
        out = dot_nn(turned_values[part, pl.ds(start, LEN)], p_ref[head, :, here])
        o_ref[part, here] = (out * recip).astype(b16)
    ctx_ref[...] = o_ref[...].T

    @pl.when(grid_step == 2 * PAIRS - 1)
    def finish_copies():
        for copy in swaps(1):
            copy.wait()
        row_store().wait()
        normed_store().wait()
        for group in range(PAIRS):
            pair_item(group).store().wait()
        for group in range(REST):
            rest_item(group).store().wait()


def front(owner, lengths, master, vectors, inputs, cotangent):
    rows, span = inputs.shape[0] // 2, inputs.shape[1]
    tokens = rows * LEN
    any_spec = pl.BlockSpec(memory_space=pl.ANY)
    smem = pl.BlockSpec(memory_space=pltpu.SMEM)
    whole = jax.ShapeDtypeStruct((rows, LEN, D), b16)
    dma = pltpu.SemaphoreType.DMA
    return pl.pallas_call(
        front_kernel,
        grid=(PAIRS, rows),
        in_specs=[
            smem,
            smem,
            pl.BlockSpec((CAP, HALF, D), lambda h, r: (0, 0, 0), pipeline_mode=pl.Buffered(1)),
            pl.BlockSpec((PIECES, D), lambda h, r: (0, 0)),
            any_spec,
            any_spec,
        ],
        out_specs=[any_spec] * 5
        + [
            pl.BlockSpec((PAIR, tokens), lambda h, r: (h, 0)),
            pl.BlockSpec((PAIR, tokens), lambda h, r: (h, 0)),
            pl.BlockSpec((tokens, PAIR), lambda h, r: (0, h)),
            pl.BlockSpec((2, LEN, LEN), lambda h, r: (h * 2 + r, 0, 0)),
            pl.BlockSpec((1, 2, LEN), lambda h, r: (h * 2 + r, 0, 0)),
            pl.BlockSpec((PAIR, LEN), lambda h, r: (h, r)),
            pl.BlockSpec((LEN, PAIR), lambda h, r: (r, h)),
        ],
        out_shape=[
            whole,
            whole,
            jax.ShapeDtypeStruct((tokens, D), b16),
            jax.ShapeDtypeStruct((PAIRS, D, WIDE), b16),
            jax.ShapeDtypeStruct((REST, D, D), b16),
            jax.ShapeDtypeStruct((D, tokens), b16),
            jax.ShapeDtypeStruct((D, tokens), b16),
            jax.ShapeDtypeStruct((tokens, D), b16),
            jax.ShapeDtypeStruct((rows * HEADS, LEN, LEN), b16),
            jax.ShapeDtypeStruct((rows * PAIRS, 2, LEN), f32),
            jax.ShapeDtypeStruct((D, tokens), b16),
            jax.ShapeDtypeStruct((tokens, D), b16),
        ],
        scratch_shapes=[
            pltpu.SMEM((PIECES,), jnp.int32),
            pltpu.VMEM((rows, LEN, D), b16),
            pltpu.VMEM((tokens, D), b16),
            pltpu.VMEM((tokens, PAIR), b16),
            pltpu.VMEM((PAIR, tokens), b16),
            pltpu.VMEM((2, LEN, LEN // 2), f32),
            pltpu.VMEM((CAP, HALF, D), b16),
        ]
        + [pltpu.VMEM((FLOWS, CAP, NEAR, wide * PAIR), b16) for unused, wide in GROUPS]
        + [pltpu.VMEM((FLOWS, 2 * CAP, KEEP, wide * PAIR), b16) for unused, wide in GROUPS]
        + [
            pltpu.VMEM((PAIRS, D, WIDE), b16),
            pltpu.VMEM((FLOWS, 2, PAIRS, KEEP, WIDE), b16),
            pltpu.VMEM((REST, D, D), b16),
            pltpu.VMEM((FLOWS, 2, REST, KEEP, D), b16),
            dma((CHUNKS, FLOWS, 3)),
            dma((CHUNKS, FLOWS, 3)),
            dma((PAIRS, FLOWS, 6)),
            dma((PAIRS, FLOWS, 6)),
            dma((REST, FLOWS, 6)),
            dma((REST, FLOWS, 6)),
            dma((2,)),
            dma((2,)),
            dma((2,)),
            dma((PAIRS + REST + 2,)),
        ],
        compiler_params=pltpu.CompilerParams(
            collective_id=0, has_side_effects=True, vmem_limit_bytes=60 * MIB
        ),
        name="front",
    )(owner, lengths, master, vectors, inputs, cotangent)


class Sum:
    steps = 7

    def __init__(self, place, work, wide, narrow, sems, send_pair, add_own):
        self.place, self.work, self.wide, self.narrow, self.sems = place, work, wide, narrow, sems
        self.send_pair, self.add_own = send_pair, add_own

    def column(self, flow):
        rows = rows_at(self.place.flow(flow)[4], KEEP)

        def read():
            return self.work[:, rows]

        def write(value):
            self.work[:, rows] = value

        sems = (self.sems[0].at[flow, pl.ds(2, 3)], self.sems[1].at[flow, pl.ds(2, 3)])
        land = self.narrow.at[flow, pl.ds(1, 2)]
        return Column(self.place, self.work.at[:, rows], read, write, land, sems)

    def copy(self, flow, index):
        first, second, near, far, keep, give = self.place.flow(flow)
        source, target, device = [
            (self.work.at[:, rows_at(far, NEAR)], self.wide.at[flow], first),
            (self.work.at[:, rows_at(give, KEEP)], self.narrow.at[flow, 0], second),
        ][index]
        return remote(
            source,
            target,
            self.sems[0].at[flow, index],
            self.sems[1].at[flow, index],
            self.place.partners[device],
        )

    def add(self, rows, value):
        self.work[:, rows] = (self.work[:, rows].astype(f32) + value.astype(f32)).astype(b16)

    def step(self, index):
        if index == 0:
            self.send_pair().start()
        if index == 1:
            self.send_pair().wait()
            self.add_own()
        for flow in range(FLOWS):
            first, second, near, far, keep, give = self.place.flow(flow)
            if index == 1:
                self.copy(flow, 0).start()
            if index == 2:
                self.copy(flow, 0).wait()
                self.add(rows_at(near, NEAR), self.wide[flow])
                self.copy(flow, 1).start()
            if index == 3:
                self.copy(flow, 1).wait()
                self.add(rows_at(keep, KEEP), self.narrow[flow, 0])
        if index >= 3:
            columns = [self.column(flow) for flow in range(FLOWS)]
            column_step(self.place, columns, index - 3)


class Gather:
    steps = 3

    def __init__(self, place, work, narrow, wide, sems):
        self.place, self.work, self.narrow, self.wide = place, work, narrow, wide
        self.sems = sems

    def copy(self, flow, index):
        first, second, near, far, keep, give = self.place.flow(flow)
        rows, target, device = [
            (rows_at(keep, KEEP), self.narrow, second),
            (rows_at(near, NEAR), self.wide, first),
        ][index]
        return remote(
            self.work.at[:, rows],
            target.at[flow],
            self.sems[0].at[flow, 5 + index],
            self.sems[1].at[flow, 5 + index],
            self.place.partners[device],
        )

    def step(self, index):
        for flow in range(FLOWS):
            first, second, near, far, keep, give = self.place.flow(flow)
            if index > 0:
                self.copy(flow, index - 1).wait()
            if index == 1:
                self.work[:, rows_at(give, KEEP)] = self.narrow[flow]
            if index == 2:
                self.work[:, rows_at(far, NEAR)] = self.wide[flow]
            if index < 2:
                self.copy(flow, index).start()


class Hand:
    steps = 3

    def __init__(self, place, table, work, bag, gift, pack, last, own, out, sems, store_sems):
        self.place, self.table, self.work = place, table, work
        self.bag, self.gift, self.pack, self.last, self.own = bag, gift, pack, last, own
        self.out, self.sems, self.store_sems = out, sems, store_sems

    def tile(self, chip, rank, rows):
        return self.work[self.table[chip * CAP + rank], rows]

    def copy(self, flow, index):
        first, second = self.place.flow(flow)[:2]
        source, target, device = [
            (self.bag.at[flow], self.gift.at[flow], second),
            (self.pack.at[flow], self.last.at[flow], first),
        ][index]
        return remote(
            source,
            target,
            self.sems[0].at[flow, index],
            self.sems[1].at[flow, index],
            self.place.partners[device],
        )

    def stores(self, flow):
        first, second, near, far, keep, give = self.place.flow(flow)
        parts = [
            (self.own.at[flow], rows_at(keep, KEEP)),
            (self.gift.at[flow, pl.ds(0, CAP)], rows_at(give, KEEP)),
            (self.last.at[flow], rows_at(far, NEAR)),
        ]
        return [
            pltpu.make_async_copy(source, self.out.at[:, rows], self.store_sems.at[flow, index])
            for index, (source, rows) in enumerate(parts)
        ]

    def step(self, index):
        for flow in range(FLOWS):
            first, second, near, far, keep, give = self.place.flow(flow)
            rows = rows_at(keep, KEEP)
            if index == 0:
                beside = self.place.chips[second]
                across = beside + self.place.chips[first] - self.place.me
                for rank in range(CAP):
                    self.bag[flow, rank] = self.tile(beside, rank, rows)
                    self.bag[flow, CAP + rank] = self.tile(across, rank, rows)
                    self.own[flow, rank] = self.tile(self.place.me, rank, rows)
                self.copy(flow, 0).start()
            if index == 1:
                self.copy(flow, 0).wait()
                for rank in range(CAP):
                    mine = self.tile(self.place.chips[first], rank, rows)
                    self.pack[flow, rank, rows_at(keep - near, KEEP)] = mine
                    self.pack[flow, rank, rows_at(give - near, KEEP)] = self.gift[flow, CAP + rank]
                self.copy(flow, 1).start()
            if index == 2:
                self.copy(flow, 1).wait()
                for copy in self.stores(flow):
                    copy.start()


BACK_STEPS = 2 * PAIRS
BACK_TAIL = 4
BACK_PAIRS = tuple((index, 1) for index in range(PAIRS))
BACK_REST = (0, 0, 1, 2, 2, 3, 4, 4, 5)
BACK_HAND = 12


def back_kernel(
    table, p_ref, r_ref, v_ref, q_ref, k_ref, o_ref, g_ref, w_ref, n_ref, x_ref, z_ref, vec_ref,
    tiles_in, sums_in, y_in,
    y_out, i_out, pairs_out, slots_out, sums_ref,
    grad_sum, wide_sum, turned, slopes, block_out,
    two, two_wide, two_narrow, two_stage, one, one_wide, one_narrow, one_send_stage, one_stage,
    gather_narrow, gather_wide,
    bag, gift, pack, last, own, vec_land,
    two_send, two_recv, one_send, one_recv, hand_send, hand_recv, hand_store,
    pair_two_send, pair_two_recv, pair_one_send, pair_one_recv, load_sem, store_sem,
    swap_send, swap_recv, swap_local, vec_send, vec_recv,
):
    step = pl.program_id(0)
    place = Place()
    rows, span = y_in.shape[0], y_in.shape[1] // 2
    near_half = rows_at(place.core * HALF, HALF)
    far_half = rows_at(place.other * HALF, HALF)

    def load_two(group):
        first, count = REST_GROUPS[group]
        return pltpu.make_async_copy(
            tiles_in.at[pl.ds(first, count), near_half],
            two_stage.at[pl.ds(group % 3, 1)],
            load_sem.at[group % 3],
        )

    def rest_sum(group):
        first, count = REST_GROUPS[group]
        span_of = pl.ds(first, count)
        work = two.at[span_of]

        def send_pair():
            return remote(
                tiles_in.at[span_of, far_half],
                work,
                pair_two_send.at[group],
                pair_two_recv.at[group],
                place.twin,
            )

        def add_own():
            load_two(group).wait()
            work[...] = (work[...].astype(f32) + two_stage[group % 3].astype(f32)).astype(b16)

        sems = (two_send.at[group], two_recv.at[group])
        wide, narrow = two_wide.at[:, span_of], two_narrow.at[:, :, span_of]
        return Sum(place, work, wide, narrow, sems, send_pair, add_own)

    def pair_sum(group):
        first, count = BACK_PAIRS[group]
        span_of = pl.ds(first, count)
        work = one.at[span_of]

        def send_pair():
            return remote(
                one_send_stage.at[pl.ds(group % 2, 1)],
                work,
                pair_one_send.at[group],
                pair_one_recv.at[group],
                place.twin,
            )

        def add_own():
            own = one_stage[group % 2].astype(f32)
            work[...] = (work[...].astype(f32) + own).astype(b16)

        sems = (one_send.at[group], one_recv.at[group])
        wide, narrow = one_wide.at[:, span_of], one_narrow.at[:, :, span_of]
        return Sum(place, work, wide, narrow, sems, send_pair, add_own)

    def pair_gather(group):
        first, count = BACK_PAIRS[group]
        span_of = pl.ds(first, count)
        sems = (one_send.at[group], one_recv.at[group])
        narrow, wide = gather_narrow.at[:, span_of], gather_wide.at[:, span_of]
        return Gather(place, one.at[span_of], narrow, wide, sems)

    hand = Hand(
        place, table, two, bag, gift, pack, last, own, slots_out, (hand_send, hand_recv), hand_store
    )

    def pair_store(index, tile):
        return pltpu.make_async_copy(
            one.at[index, :, pl.ds(tile * PAIR, PAIR)],
            pairs_out.at[tile, :, pl.ds(index * PAIR, PAIR)],
            store_sem.at[index, tile],
        )

    def tick(number, odd):
        for group, start in enumerate(BACK_REST):
            if group % 2 == odd and 0 <= number - start < Sum.steps:
                rest_sum(group).step(number - start)
        for group, (first, count) in enumerate(BACK_PAIRS):
            if group % 2 != odd:
                continue
            start = 2 * (first + count)
            if 0 <= number - start < Sum.steps:
                pair_sum(group).step(number - start)
            if 0 <= number - start - Sum.steps + 1 < Gather.steps:
                pair_gather(group).step(number - start - Sum.steps + 1)
            if number == start + Sum.steps + 1:
                for index in range(first, first + count):
                    for tile in range(3):
                        pair_store(index, tile).start()
        if odd == 0 and 0 <= number - BACK_HAND < Hand.steps:
            hand.step(number - BACK_HAND)
        for group, start in enumerate(BACK_REST):
            if odd == 1 and number == max(start - 1, 0):
                load_two(group).start()

    def both(number):
        tick(number, 0)
        tick(number, 1)

    def swap_y(index):
        there = pl.ds(place.core * rows, rows)
        if index == 0:
            return pltpu.make_async_copy(
                y_in.at[:, pl.ds(place.core * span, span)], y_out.at[there], swap_local.at[0]
            )
        return remote(
            y_in.at[:, pl.ds(place.other * span, span)],
            y_out.at[there],
            swap_send.at[0],
            swap_recv.at[0],
            place.twin,
        )

    @pl.when(step == 0)
    def lead():
        place.greet()
        for index in range(2):
            swap_y(index).start()
        sums_ref[...] = sums_in[...]

    for number in range(BACK_STEPS + BACK_TAIL):
        early = partial(tick, number, 0) if number < BACK_STEPS else partial(both, number)
        pl.when(step == number)(early)

    half = LEN // 2
    pair, row = step // 2, lax.rem(step, 2)

    def attention(head):
        part = slice(head * HEAD_DIM, (head + 1) * HEAD_DIM)
        values = head_only(v_ref[...], head)
        recip = r_ref[0, head : head + 1, :]
        grad = g_ref[part, :].astype(f32) * recip
        delta = jnp.sum(grad * o_ref[part, :].astype(f32), 0, keepdims=True)
        grad = grad.astype(b16)
        doubled = jnp.concatenate([grad, grad], axis=0)
        value_grad, key_grad = [], []
        quarter = LEN // 4
        for which in range(2):
            cols = slice(which * half, (which + 1) * half)
            shift = delta[:, cols]
            for block in range(4):
                raw = dot_nn(values[block * quarter : (block + 1) * quarter], doubled[:, cols])
                for small in range(quarter // 64):
                    rows_here = slice(block * quarter + small * 64, block * quarter + (small + 1) * 64)
                    slope = raw[small * 64 : (small + 1) * 64] - shift
                    slope = p_ref[head, rows_here, cols].astype(f32) * slope
                    slopes[rows_here] = slope.astype(b16)
            value_grad.append(dot_nt(grad[:, cols], p_ref[head, :, cols]))
            key_grad.append(dot_nt(q_ref[part, cols], slopes[...]))
            query_grad = dot_nn(k_ref[part, :], slopes[...]) * (HEAD_DIM**-0.5)
            turned[part, cols] = query_grad.astype(b16)
        lower = slice(PAIR + head * HEAD_DIM, PAIR + (head + 1) * HEAD_DIM)
        turned[lower, :] = ((key_grad[0] + key_grad[1]) * (1.0 / LOG2E)).astype(b16)
        lower = slice(2 * PAIR + head * HEAD_DIM, 2 * PAIR + (head + 1) * HEAD_DIM)
        turned[lower, :] = (value_grad[0] + value_grad[1]).astype(b16)

    @pl.when(step < BACK_STEPS)
    def first_head():
        attention(0)

    for number in range(BACK_STEPS):
        pl.when(step == number)(partial(tick, number, 1))

    @pl.when(step < BACK_STEPS)
    def second_head():
        attention(1)
        where = pl.ds(pl.multiple_of(row * LEN, LEN), LEN)
        block = dot_nn(turned[...], n_ref[where])
        back = turned[...].T
        lanes = pl.ds(pl.multiple_of(pair * PAIR, PAIR), PAIR)
        ones = jnp.sum(back.astype(f32), 0, keepdims=True)
        sums_ref[4:5, lanes] += ones[:, :PAIR]
        sums_ref[5:6, lanes] += ones[:, 2 * PAIR :]
        term = dot_nt(back, w_ref[0])

        @pl.when(pair == 0)
        def begin():
            grad_sum[where] = term

        @pl.when(pair > 0)
        def add():
            grad_sum[where] += term

        @pl.when(row == 0)
        def keep():
            wide_sum[...] = block

        @pl.when(row == 1)
        def hand_on():
            whole = (wide_sum[...] + block).T
            low = whole.astype(b16)
            for core in range(2):

                @pl.when(place.core == core)
                def split():
                    slot = lax.rem(pair, 2)
                    one_stage[slot] = low[core * HALF : (core + 1) * HALF]
                    one_send_stage[slot] = low[(1 - core) * HALF : (2 - core) * HALF]

    def store_block(index):
        row, half = index // 2, index % 2
        target = i_out.at[place.core * rows + row]
        local = pltpu.make_async_copy(block_out.at[half], target, swap_local.at[1 + row])
        far = remote(
            block_out.at[half], target, swap_send.at[1 + row], swap_recv.at[1 + row], place.twin
        )
        return local, far, half

    def wait_block(index):
        local, far, half = store_block(index)

        @pl.when(place.core == half)
        def keep():
            local.wait()

        @pl.when(place.core != half)
        def give():
            far.wait()

    for index in range(BACK_TAIL):

        @pl.when(step == BACK_STEPS + index)
        def close():
            size = LEN // 2
            if index >= 2:
                wait_block(index - 2)
            gain_sum = jnp.zeros((8, D), f32)
            shift_sum = jnp.zeros((8, D), f32)
            for block in range(size // 16):
                rows_here = slice(block * 16, (block + 1) * 16)
                grad = grad_sum[index * size + block * 16 : index * size + (block + 1) * 16]
                unit, rstd = norm_parts(x_ref[rows_here].astype(f32))
                gain_sum = gain_sum + jnp.sum((grad * unit).reshape(-1, 8, D), axis=0)
                shift_sum = shift_sum + jnp.sum(grad.reshape(-1, 8, D), axis=0)
                total = norm_back(grad, unit, rstd, vec_ref[0:1, :])
                block_out[index % 2, rows_here] = (z_ref[rows_here].astype(f32) + total).astype(b16)
            sums_ref[0:1, :] += jnp.sum(gain_sum, 0, keepdims=True)
            sums_ref[1:2, :] += jnp.sum(shift_sum, 0, keepdims=True)
            local, far, half = store_block(index)

            @pl.when(place.core == half)
            def keep():
                local.start()

            @pl.when(place.core != half)
            def give():
                far.start()

    @pl.when(step == BACK_STEPS + BACK_TAIL - 1)
    def drain():
        devices = [place.twin] + place.partners

        def vector(index):
            return remote(
                sums_ref, vec_land.at[index], vec_send.at[index], vec_recv.at[index], devices[index]
            )

        vector(0).start()
        for number in range(BACK_STEPS + BACK_TAIL, BACK_STEPS + Sum.steps + Gather.steps):
            both(number)
            index = number - BACK_STEPS - BACK_TAIL
            if index < 5:
                vector(index).wait()
                sums_ref[...] += vec_land[index]
                if index < 4:
                    vector(index + 1).start()
        for index in range(2):
            swap_y(index).wait()
        for index in range(2, BACK_TAIL):
            wait_block(index)
        for index in range(PAIRS):
            for tile in range(3):
                pair_store(index, tile).wait()
        for flow in range(FLOWS):
            for copy in hand.stores(flow):
                copy.wait()


def back(table, attention, weights, normed, x, residual, vectors, tiles, sums, y):
    rows, length = y.shape[:2]
    tokens = rows * length
    any_spec = pl.BlockSpec(memory_space=pl.ANY)
    smem = pl.BlockSpec(memory_space=pltpu.SMEM)
    dma = pltpu.SemaphoreType.DMA

    def now(step):
        return jnp.minimum(step, BACK_STEPS - 1)

    def tail(step):
        return jnp.maximum(step - BACK_STEPS, 0)

    head_block = pl.BlockSpec((PAIR, LEN), lambda s: (now(s) // 2, lax.rem(now(s), 2)))
    tail_block = pl.BlockSpec((LEN // 2, D), lambda s: (tail(s), 0))
    whole = pl.BlockSpec((PIECES, D), lambda s: (0, 0))
    sums_block = pl.BlockSpec((16, D), lambda s: (0, 0))
    return pl.pallas_call(
        back_kernel,
        grid=(BACK_STEPS + BACK_TAIL,),
        in_specs=[
            smem,
            pl.BlockSpec((2, LEN, LEN), lambda s: (now(s), 0, 0)),
            pl.BlockSpec((1, 2, LEN), lambda s: (now(s), 0, 0)),
            pl.BlockSpec((LEN, PAIR), lambda s: (lax.rem(now(s), 2), now(s) // 2)),
            head_block,
            head_block,
            head_block,
            head_block,
            pl.BlockSpec((1, D, WIDE), lambda s: (now(s) // 2, 0, 0)),
            pl.BlockSpec((tokens, D), lambda s: (0, 0), pipeline_mode=pl.Buffered(1)),
            tail_block,
            tail_block,
            whole,
            any_spec,
            sums_block,
            any_spec,
        ],
        out_specs=[any_spec] * 4 + [sums_block],
        out_shape=[
            jax.ShapeDtypeStruct((2 * rows, length // 2, D), b16),
            jax.ShapeDtypeStruct((2 * rows, length // 2, D), b16),
            jax.ShapeDtypeStruct((3, HALF, D), b16),
            jax.ShapeDtypeStruct((CAP, HALF, D), b16),
            jax.ShapeDtypeStruct((16, D), f32),
        ],
        scratch_shapes=[
            pltpu.VMEM((tokens, D), f32),
            pltpu.VMEM((WIDE, D), f32),
            pltpu.VMEM((WIDE, LEN), b16),
            pltpu.VMEM((LEN, LEN // 2), b16),
            pltpu.VMEM((2, LEN // 2, D), b16),
            pltpu.VMEM((REST, HALF, D), b16),
            pltpu.VMEM((FLOWS, REST, NEAR, D), b16),
            pltpu.VMEM((FLOWS, 3, REST, KEEP, D), b16),
            pltpu.VMEM((3, HALF, D), b16),
            pltpu.VMEM((PAIRS, HALF, WIDE), b16),
            pltpu.VMEM((FLOWS, PAIRS, NEAR, WIDE), b16),
            pltpu.VMEM((FLOWS, 3, PAIRS, KEEP, WIDE), b16),
            pltpu.VMEM((2, HALF, WIDE), b16),
            pltpu.VMEM((2, HALF, WIDE), b16),
            pltpu.VMEM((FLOWS, PAIRS, KEEP, WIDE), b16),
            pltpu.VMEM((FLOWS, PAIRS, NEAR, WIDE), b16),
            pltpu.VMEM((FLOWS, 2 * CAP, KEEP, D), b16),
            pltpu.VMEM((FLOWS, 2 * CAP, KEEP, D), b16),
            pltpu.VMEM((FLOWS, CAP, NEAR, D), b16),
            pltpu.VMEM((FLOWS, CAP, NEAR, D), b16),
            pltpu.VMEM((FLOWS, CAP, KEEP, D), b16),
            pltpu.VMEM((5, 16, D), f32),
            dma((REST, FLOWS, 5)),
            dma((REST, FLOWS, 5)),
            dma((PAIRS, FLOWS, 7)),
            dma((PAIRS, FLOWS, 7)),
            dma((FLOWS, 2)),
            dma((FLOWS, 2)),
            dma((FLOWS, 3)),
            dma((REST,)),
            dma((REST,)),
            dma((PAIRS,)),
            dma((PAIRS,)),
            dma((3,)),
            dma((PAIRS, 3)),
            dma((3,)),
            dma((3,)),
            dma((3,)),
            dma((5,)),
            dma((5,)),
        ],
        compiler_params=pltpu.CompilerParams(
            collective_id=1, has_side_effects=True, vmem_limit_bytes=62 * MIB
        ),
        name="back",
    )(table, *attention, weights, normed, x, residual, vectors, tiles, sums, y)


def update_kernel(tile_at, one, two, w_ref, m_ref, s_ref, y_in, i_in, w_out, m_out, s_out, y_out, i_out):
    step = pl.program_id(0)
    tile = tile_at[step // 2]
    grad = jnp.where(tile < 3, one[0], two[0]).astype(f32)
    parts = adam_step(w_ref[0], grad, m_ref[0], s_ref[0], RATE)
    for target, part in zip((w_out, m_out, s_out), parts):
        target[0] = jnp.where(tile >= 0, part, jnp.zeros_like(part))

    @pl.when(step < 4)
    def widen():
        y_out[...] = y_in[...].astype(f32)
        i_out[...] = i_in[...].astype(f32)


def update(tile_at, one, two, master, first, second, y, grad):
    tokens = y.shape[0]
    size = HALF // 2
    state = pl.BlockSpec((1, size, D), lambda s, tile_at: (s // 2, lax.rem(s, 2), 0))
    wide = pl.BlockSpec((tokens // 4, D), lambda s, tile_at: (jnp.minimum(s, 3), 0))
    return pl.pallas_call(
        update_kernel,
        grid_spec=pltpu.PrefetchScalarGridSpec(
            num_scalar_prefetch=1,
            grid=(CAP * 2,),
            in_specs=[
                pl.BlockSpec(
                    (1, size, D),
                    lambda s, tile_at: (jnp.clip(tile_at[s // 2], 0, 2), lax.rem(s, 2), 0),
                ),
                state,
                state,
                state,
                state,
                wide,
                wide,
            ],
            out_specs=[state] * 3 + [wide] * 2,
        ),
        out_shape=[jax.ShapeDtypeStruct(master.shape, f32)] * 3
        + [jax.ShapeDtypeStruct((tokens, D), f32)] * 2,
        compiler_params=pltpu.CompilerParams(vmem_limit_bytes=60 * MIB),
        name="update",
    )(tile_at, one, two, master, first, second, y, grad)


def shards_paired(
    inputs,
    cotangent,
    doc_lengths,
    owner_list,
    master,
    first_moment,
    second_moment,
    vectors,
    vector_first,
    vector_second,
):
    rows_here, span, width = inputs.shape
    place = lax.axis_index("blk")
    member = lax.axis_index("dp")
    rows_mine = rows_here // 2
    order = jnp.arange(PIECES)
    same_owner = owner_list[:, None] == owner_list[None, :]
    ranks = jnp.sum(same_owner & (order[None, :] < order[:, None]), axis=1).astype(jnp.int32)
    slot_of = owner_list * CAP + ranks
    front_outs = front(owner_list, doc_lengths, master, vectors, inputs, cotangent)
    x, cot, normed, weights_one, weights_two, queries, keys, values = front_outs[:8]
    weights, recips, context_turned, context = front_outs[8:]
    x = x.reshape(-1, width)
    cot = cot.reshape(-1, width)
    block_out, residual, grad_context, sums, tiles_two = feed(
        context, context_turned, x, cot, weights_two, vectors
    )
    hits = jnp.arange(16 * CAP)[:, None] == slot_of[None, :]
    tile_at = jnp.sum(jnp.where(hits, order[None, :] + 1, 0), axis=1).astype(jnp.int32) - 1
    table = jnp.maximum(tile_at - 3, 0)
    block_out, input_grad, total_one, total_two, vector_total = back(
        table,
        (weights, recips, values, queries, keys, context_turned, grad_context),
        weights_one,
        normed,
        x,
        residual,
        vectors,
        tiles_two,
        sums,
        block_out.reshape(rows_mine, LEN, width),
    )
    mine = lax.dynamic_slice_in_dim(tile_at, member * CAP, CAP, 0)
    *updated, block_out, input_grad = update(
        mine,
        total_one,
        total_two,
        master,
        first_moment,
        second_moment,
        block_out.reshape(-1, width),
        input_grad.reshape(-1, width),
    )
    columns = vector_first.shape[1]
    vector_cols = lax.dynamic_slice_in_dim(vectors, place * columns, columns, 1)
    vector_total = lax.dynamic_slice(vector_total, (0, place * columns), (PIECES, columns))
    updated_vectors = adam_step(vector_cols, vector_total, vector_first, vector_second, VEC_RATE)
    return (
        block_out.reshape(inputs.shape),
        input_grad.reshape(inputs.shape),
        *updated,
        *updated_vectors,
    )


def solution(mesh):
    in_specs = (
        P("dp", "blk", None),
        P("dp", "blk", None),
        P("dp", None),
        P(),
        P("dp", "blk", None),
        P("dp", "blk", None),
        P("dp", "blk", None),
        P(),
        P(None, "blk"),
        P(None, "blk"),
    )
    out_specs = (
        P("dp", "blk", None),
        P("dp", "blk", None),
        P("dp", "blk", None),
        P("dp", "blk", None),
        P("dp", "blk", None),
        P(None, "blk"),
        P(None, "blk"),
        P(None, "blk"),
    )
    paired = mesh.shape["blk"] == 2 and mesh.shape["dp"] == 16
    shards = shards_paired if paired else shards_any
    return jax.shard_map(shards, mesh=mesh, in_specs=in_specs, out_specs=out_specs, check_vma=False)
```

```python
from functools import partial

import jax
import jax.numpy as jnp
from jax import lax
from jax.experimental import pallas as pl
from jax.experimental.pallas import tpu as pltpu
from jax.sharding import PartitionSpec as P

D = 768
FF = 3072
HEADS = 12
HEAD_DIM = 64
LEN = 1024
CAP = 3
STEP = 10
PIECES = 12


EPS_NORM = 1e-05
BETA_ONE = 0.9
BETA_TWO = 0.999
RATE = 0.04
VEC_RATE = 0.25
DECAY = 0.01
ADAM_EPS = 1e-08


def normalize(values_in, gain, shift):
    center = jnp.mean(values_in, axis=-1, keepdims=True)
    offset = values_in - center
    spread = jnp.mean(offset * offset, axis=-1, keepdims=True)
    return offset * lax.rsqrt(spread + EPS_NORM) * gain + shift


def adam_step(weight, grad, first, second, rate):
    first_new = BETA_ONE * first + (1.0 - BETA_ONE) * grad
    second_new = BETA_TWO * second + (1.0 - BETA_TWO) * grad * grad
    corrected = (
        first_new
        / (1.0 - BETA_ONE**STEP)
        / (jnp.sqrt(second_new / (1.0 - BETA_TWO**STEP)) + ADAM_EPS)
    )
    return (weight - rate * (corrected + DECAY * weight), first_new, second_new)


def shards_any(
    inputs,
    cotangent,
    doc_lengths,
    owner_list,
    master,
    first_moment,
    second_moment,
    vectors,
    vector_first,
    vector_second,
):
    rows_here, span, width = inputs.shape
    tokens_here = rows_here * span
    fold = FF // D
    scale = HEAD_DIM ** (-0.5)
    place = lax.axis_index("blk")
    f32 = jnp.float32
    b16 = jnp.bfloat16
    order = jnp.arange(PIECES)
    same_owner = owner_list[:, None] == owner_list[None, :]
    ranks = jnp.sum(same_owner & (order[None, :] < order[:, None]), axis=1)
    slot_of = owner_list * CAP + ranks

    mine = (owner_list == lax.axis_index("dp"))[:, None, None]
    tile_rows = lax.psum(jnp.where(mine, master[ranks], 0.0).astype(b16), "dp")
    tiles = lax.all_gather(tile_rows, "blk", axis=1, tiled=True)
    query_weight = tiles[0]
    key_weight = tiles[1]
    value_weight = tiles[2]
    out_weight = tiles[3]
    up_weight = jnp.transpose(tiles[4 : 4 + fold], (1, 0, 2)).reshape(width, FF)
    down_weight = tiles[4 + fold :].reshape(FF, width)
    flat_in = inputs.reshape(tokens_here, width).astype(f32)
    normed_one = normalize(flat_in, vectors[0], vectors[1]).astype(b16)
    queries = (jnp.dot(normed_one, query_weight, preferred_element_type=f32) + vectors[4]).astype(
        b16
    )
    keys_here = jnp.dot(normed_one, key_weight, preferred_element_type=f32).astype(b16)
    values_here = (
        jnp.dot(normed_one, value_weight, preferred_element_type=f32) + vectors[5]
    ).astype(b16)
    query_heads = queries.reshape(rows_here, span, HEADS, HEAD_DIM)
    first_len = doc_lengths[:, 0]
    query_seg = (place * span + jnp.arange(span))[None, :] >= first_len[:, None]

    def block_scores(key_block, start):
        count = key_block.shape[1]
        key_heads = key_block.reshape(rows_here, count, HEADS, HEAD_DIM)
        raw = (
            jnp.einsum("rqhd,rkhd->rhqk", query_heads, key_heads, preferred_element_type=f32)
            * scale
        )
        key_seg = (start + jnp.arange(count))[None, :] >= first_len[:, None]
        allowed = query_seg[:, None, :, None] == key_seg[:, None, None, :]
        return (raw, allowed)

    key_rows = keys_here.reshape(rows_here, span, width)
    value_rows = values_here.reshape(rows_here, span, width)
    top = jnp.full((rows_here, HEADS, span), -1e30, f32)
    key_block = lax.all_gather(key_rows, "blk", axis=1, tiled=True)
    value_block = lax.all_gather(value_rows, "blk", axis=1, tiled=True)
    count = key_block.shape[1]
    raw, allowed = block_scores(key_block, jnp.int32(0))
    new_top = jnp.maximum(top, jnp.max(jnp.where(allowed, raw, -1e30), axis=-1))
    weights = jnp.where(allowed, jnp.exp(raw - new_top[..., None]), 0.0)
    value_heads = value_block.reshape(rows_here, count, HEADS, HEAD_DIM)
    update = jnp.einsum(
        "rhqk,rkhd->rhqd", weights.astype(b16), value_heads, preferred_element_type=f32
    )
    total = jnp.sum(weights, axis=-1)
    log_total = new_top + jnp.log(total)
    context_raw = update / total[..., None]
    context_low = jnp.transpose(context_raw, (0, 2, 1, 3)).reshape(tokens_here, width).astype(b16)
    residual = flat_in + (jnp.dot(context_low, out_weight, preferred_element_type=f32) + vectors[6])
    normed_two = normalize(residual, vectors[2], vectors[3]).astype(b16)
    hidden = jnp.dot(normed_two, up_weight, preferred_element_type=f32) + vectors[8:].reshape(FF)
    gelu_exact = partial(jax.nn.gelu, approximate=False)
    active, gelu_pull = jax.vjp(gelu_exact, hidden)
    active_low = active.astype(b16)
    block_out = (
        residual + (jnp.dot(active_low, down_weight, preferred_element_type=f32) + vectors[7])
    ).reshape(rows_here, span, width)
    grad_out = cotangent.reshape(tokens_here, width)
    down_grad = jnp.einsum("tf,td->fd", active_low, grad_out, preferred_element_type=f32)
    down_sum = jnp.sum(grad_out, axis=0, dtype=f32)
    grad_active = jnp.einsum("td,fd->tf", grad_out, down_weight, preferred_element_type=f32)
    grad_hidden = gelu_pull(grad_active)[0].astype(b16)
    up_grad = jnp.einsum("td,tf->df", normed_two, grad_hidden, preferred_element_type=f32)
    up_sum = jnp.sum(grad_hidden, axis=0, dtype=f32)
    ffn_tiles = jnp.concatenate(
        [
            jnp.transpose(up_grad.reshape(width, fold, width), (1, 0, 2)),
            down_grad.reshape(fold, width, width),
        ],
        axis=0,
    )
    grad_normed_two = jnp.einsum("tf,df->td", grad_hidden, up_weight, preferred_element_type=f32)
    unused, second_pull = jax.vjp(normalize, residual, vectors[2], vectors[3])
    residual_part, gain_two_grad, shift_two_grad = second_pull(grad_normed_two)
    grad_residual = grad_out.astype(f32) + residual_part
    grad_attended = grad_residual.astype(b16)
    out_grad = jnp.einsum("tm,td->md", context_low, grad_attended, preferred_element_type=f32)
    out_sum = jnp.sum(grad_attended, axis=0, dtype=f32)
    grad_context = jnp.einsum(
        "td,md->tm", grad_attended, out_weight, preferred_element_type=f32
    ).astype(b16)
    grad_heads = grad_context.reshape(rows_here, span, HEADS, HEAD_DIM)
    delta = jnp.einsum("rqhd,rhqd->rhq", grad_heads.astype(f32), context_raw)
    key_all, value_all = (
        lax.all_gather(key_rows, "blk", axis=1, tiled=True),
        lax.all_gather(value_rows, "blk", axis=1, tiled=True),
    )
    key_size = min(512, LEN)

    def back_block(index, carry):
        grad_query, key_total, value_total = carry
        start = index * key_size
        key_block = lax.dynamic_slice_in_dim(key_all, start, key_size, 1)
        value_block = lax.dynamic_slice_in_dim(value_all, start, key_size, 1)
        raw, allowed = block_scores(key_block, start)
        weights_back = jnp.where(allowed, jnp.exp(raw - log_total[..., None]), 0.0)
        key_heads = key_block.reshape(rows_here, key_size, HEADS, HEAD_DIM)
        value_heads = value_block.reshape(rows_here, key_size, HEADS, HEAD_DIM)
        value_grad = jnp.einsum(
            "rhqk,rqhd->rkhd", weights_back.astype(b16), grad_heads, preferred_element_type=f32
        )
        weight_grad = jnp.einsum(
            "rqhd,rkhd->rhqk", grad_heads, value_heads, preferred_element_type=f32
        )
        score_grad = (weights_back * (weight_grad - delta[..., None])).astype(b16)
        grad_query = (
            grad_query
            + jnp.einsum("rhqk,rkhd->rqhd", score_grad, key_heads, preferred_element_type=f32)
            * scale
        )
        key_grad = (
            jnp.einsum("rhqk,rqhd->rkhd", score_grad, query_heads, preferred_element_type=f32)
            * scale
        )
        key_total = lax.dynamic_update_slice_in_dim(
            key_total, key_grad.reshape(rows_here, key_size, width), start, 1
        )
        value_total = lax.dynamic_update_slice_in_dim(
            value_total, value_grad.reshape(rows_here, key_size, width), start, 1
        )
        return (grad_query, key_total, value_total)

    zero_rows = jnp.zeros((rows_here, LEN, width), f32)
    grad_query, key_total, value_total = lax.fori_loop(
        0,
        LEN // key_size,
        back_block,
        (jnp.zeros((rows_here, span, HEADS, HEAD_DIM), f32), zero_rows, zero_rows),
    )
    key_grad_here, value_grad_here = (
        lax.psum_scatter(
            key_total.astype(jnp.bfloat16), "blk", scatter_dimension=1, tiled=True
        ).astype(jnp.float32),
        lax.psum_scatter(
            value_total.astype(jnp.bfloat16), "blk", scatter_dimension=1, tiled=True
        ).astype(jnp.float32),
    )
    query_low = grad_query.reshape(tokens_here, width).astype(b16)
    key_low = key_grad_here.reshape(tokens_here, width).astype(b16)
    value_low = value_grad_here.reshape(tokens_here, width).astype(b16)
    query_tile = jnp.einsum("td,te->de", normed_one, query_low, preferred_element_type=f32)
    key_tile = jnp.einsum("td,te->de", normed_one, key_low, preferred_element_type=f32)
    value_tile = jnp.einsum("td,te->de", normed_one, value_low, preferred_element_type=f32)
    grad_normed_one = (
        jnp.einsum("te,de->td", query_low, query_weight, preferred_element_type=f32)
        + jnp.einsum("te,de->td", key_low, key_weight, preferred_element_type=f32)
        + jnp.einsum("te,de->td", value_low, value_weight, preferred_element_type=f32)
    )
    unused, first_pull = jax.vjp(normalize, flat_in, vectors[0], vectors[1])
    input_part, gain_one_grad, shift_one_grad = first_pull(grad_normed_one)
    input_grad = (grad_residual + input_part).reshape(rows_here, span, width)
    vector_grads = jnp.concatenate(
        [
            jnp.stack(
                [
                    gain_one_grad,
                    shift_one_grad,
                    gain_two_grad,
                    shift_two_grad,
                    jnp.sum(query_low, axis=0, dtype=f32),
                    jnp.sum(value_low, axis=0, dtype=f32),
                    out_sum,
                    down_sum,
                ]
            ),
            up_sum.reshape(fold, width),
        ],
        axis=0,
    )
    attn_tiles = jnp.stack([query_tile, key_tile, value_tile, out_grad])
    piece_share, vector_share = (
        lax.psum_scatter(
            jnp.concatenate([attn_tiles, ffn_tiles], axis=0).astype(jnp.bfloat16),
            "blk",
            scatter_dimension=1,
            tiled=True,
        ).astype(jnp.float32),
        lax.psum_scatter(
            vector_grads.astype(jnp.bfloat16), "blk", scatter_dimension=1, tiled=True
        ).astype(jnp.float32),
    )
    own_slots = lax.axis_index("dp") * CAP + jnp.arange(CAP)
    pick = (own_slots[:, None] == slot_of[None, :]).astype(f32)
    occupied = jnp.sum(pick, axis=1)[:, None, None]
    total_share, vector_total = (
        lax.psum(piece_share.astype(jnp.bfloat16), "dp").astype(jnp.float32),
        lax.psum(vector_share.astype(jnp.bfloat16), "dp").astype(jnp.float32),
    )
    slot_grads = jnp.einsum("cp,prd->crd", pick, total_share, precision=lax.Precision.HIGHEST)
    new_master, new_first, new_second = adam_step(
        master, slot_grads, first_moment, second_moment, RATE
    )
    columns = vector_first.shape[1]
    vector_cols = lax.dynamic_slice_in_dim(vectors, place * columns, columns, 1)
    new_vectors, new_vector_first, new_vector_second = adam_step(
        vector_cols, vector_total, vector_first, vector_second, VEC_RATE
    )
    return (
        block_out,
        input_grad,
        new_master * occupied,
        new_first * occupied,
        new_second * occupied,
        new_vectors,
        new_vector_first,
        new_vector_second,
    )


f32 = jnp.float32
b16 = jnp.bfloat16
LOG2E = 1.4426950408889634
MIB = 1024 * 1024
PAIRS = HEADS // 2
PAIR = 2 * HEAD_DIM


def dot_nn(left, right):
    return lax.dot_general(left, right, (((1,), (0,)), ((), ())), preferred_element_type=f32)


def dot_nt(left, right):
    return lax.dot_general(left, right, (((1,), (1,)), ((), ())), preferred_element_type=f32)


def dot_tn(left, right):
    return lax.dot_general(left, right, (((0,), (0,)), ((), ())), preferred_element_type=f32)


def norm_parts(values_in):
    center = jnp.mean(values_in, axis=-1, keepdims=True)
    offset = values_in - center
    spread = jnp.mean(offset * offset, axis=-1, keepdims=True)
    rstd = lax.rsqrt(spread + EPS_NORM)
    return offset * rstd, rstd


def norm_back(grad, unit, rstd, gain):
    scaled = grad * gain
    first = jnp.mean(scaled, axis=-1, keepdims=True)
    second = jnp.mean(scaled * unit, axis=-1, keepdims=True)
    return rstd * (scaled - first - unit * second)


def gelu_parts(value):
    bell = jnp.exp2(value * value * (-0.5 * LOG2E))
    ratio = pl.reciprocal(1.0 + (0.3275911 * 0.7071067811865476) * jnp.abs(value))
    poly = 0.5 * 1.061405429
    poly = poly * ratio + 0.5 * -1.453152027
    poly = poly * ratio + 0.5 * 1.421413741
    poly = poly * ratio + 0.5 * -0.284496736
    poly = poly * ratio + 0.5 * 0.254829592
    tail = poly * ratio * bell
    cdf = jnp.where(value >= 0.0, 1.0 - tail, tail)
    return value * cdf, cdf + value * (bell * 0.3989422804014327)


def head_only(block, head):
    lane = lax.broadcasted_iota(jnp.int32, block.shape, 1)
    keep = (lane >= head * HEAD_DIM) & (lane < (head + 1) * HEAD_DIM)
    return jnp.where(keep, block, jnp.zeros_like(block))


MESH = pl.DeviceIdType.MESH
HALF = D // 2
FLOWS = 2
FLOW = HALF // FLOWS
NEAR = FLOW // 2
KEEP = NEAR // 2
WIDE = 3 * PAIR
EARLY = (3, 4, 5, 8, 9)
LATE = (6, 7, 10, 11)
REST = len(EARLY)
GROUPS = ((0, 1), (1, 2), (3, 3))
CHUNKS = len(GROUPS)


class Place:
    def __init__(self):
        self.me = lax.axis_index("dp")
        self.core = lax.axis_index("blk")
        self.bits = [lax.rem(self.me // weight, 2) for weight in (1, 2, 4, 8)]
        self.chips = [
            self.me + weight - 2 * weight * bit for weight, bit in zip((1, 2, 4, 8), self.bits)
        ]
        self.partners = [{"dp": chip} for chip in self.chips]
        low, high = self.bits[2:]
        self.inner = low != high
        self.across = {"dp": self.me + 4 - 8 * low + 8 - 16 * high}
        self.other = 1 - self.core
        self.twin = {"blk": self.other}

    def greet(self):
        barrier = pltpu.get_barrier_semaphore()
        for device in self.partners + [self.across, self.twin]:
            pl.semaphore_signal(barrier, 1, device_id=device, device_id_type=MESH)
        pl.semaphore_wait(barrier, 6)

    def flow(self, index):
        first, second = (0, 1) if index == 0 else (1, 0)
        base = index * FLOW
        near = base + self.bits[first] * NEAR
        far = base + NEAR - self.bits[first] * NEAR
        keep = near + self.bits[second] * KEEP
        give = near + KEEP - self.bits[second] * KEEP
        return first, second, near, far, keep, give


def remote(source, target, send, receive, device):
    return pltpu.make_async_remote_copy(
        src_ref=source,
        dst_ref=target,
        send_sem=send,
        recv_sem=receive,
        device_id=device,
        device_id_type=MESH,
    )


def rows_at(start, count):
    return pl.ds(pl.multiple_of(start, 16), count)


class Spread:
    def __init__(self, place, owner, rank, slots, land, gift, sems):
        self.place, self.owner, self.rank = place, owner, rank
        self.slots, self.land, self.gift, self.sems = slots, land, gift, sems

    def cols(self, chunk):
        return pl.ds(GROUPS[chunk][0] * PAIR, GROUPS[chunk][1] * PAIR)

    def first_copy(self, chunk, index):
        first, second, near, far, keep, give = self.place.flow(index)
        return remote(
            self.slots.at[:, rows_at(far, NEAR), self.cols(chunk)],
            self.land[chunk].at[index],
            self.sems[0].at[chunk, index, 0],
            self.sems[1].at[chunk, index, 0],
            self.place.partners[first],
        )

    def second_copy(self, chunk, index, which):
        first, second, near, far, keep, give = self.place.flow(index)
        if which == 0:
            source = self.slots.at[:, rows_at(give, KEEP), self.cols(chunk)]
        else:
            source = self.land[chunk].at[index, :, rows_at(give - near, KEEP)]
        return remote(
            source,
            self.gift[chunk].at[index, pl.ds(which * CAP, CAP)],
            self.sems[0].at[chunk, index, 1 + which],
            self.sems[1].at[chunk, index, 1 + which],
            self.place.partners[second],
        )

    def step(self, chunk, index):
        for flow in range(FLOWS):
            if index == 0:
                self.first_copy(chunk, flow).start()
                self.second_copy(chunk, flow, 0).start()
            if index == 1:
                self.first_copy(chunk, flow).wait()
                self.second_copy(chunk, flow, 1).start()
            if index == 2:
                self.second_copy(chunk, flow, 0).wait()
                self.second_copy(chunk, flow, 1).wait()

    def piece(self, tile, index, chunk, start, count):
        first, second, near, far, keep, give = self.place.flow(index)
        owner, rank = self.owner[tile], self.rank[tile]
        bits = [lax.rem(owner, 2), lax.rem(owner // 2, 2)]
        apart = [bit != mine for bit, mine in zip(bits, self.place.bits)]
        cols = pl.ds(start, count)
        mine = self.slots[rank, rows_at(keep, KEEP), pl.ds(GROUPS[chunk][0] * PAIR + start, count)]
        firsts = self.land[chunk][index, rank, rows_at(keep - near, KEEP), cols]
        gifts = self.gift[chunk][index, jnp.where(apart[first], CAP, 0) + rank, :, cols]
        value = jnp.where(apart[second], gifts, jnp.where(apart[first], firsts, mine))
        layer = owner // 4 == self.place.me // 4
        return jnp.where(layer, value, jnp.zeros_like(value))


class Column:
    steps = 4

    def __init__(self, place, kept, read, write, land, sems):
        self.place, self.kept, self.read, self.write = place, kept, read, write
        self.land, self.sems = land, sems

    def copy(self, index):
        target = self.land.at[index % 2]
        device = self.place.across if index == 1 else self.place.partners[2]
        return remote(
            self.kept, target, self.sems[0].at[index], self.sems[1].at[index], device
        )

    def add(self, index):
        self.write((self.read().astype(f32) + self.land[index].astype(f32)).astype(b16))


def column_step(place, columns, index):
    @pl.when(place.inner)
    def inner():
        for column in columns:
            if index == 1:
                column.copy(0).wait_recv()
                column.add(0)
                column.copy(1).start()
            if index == 2:
                column.copy(1).wait()
                column.add(1)
                column.copy(2).start()
            if index == 3:
                column.copy(2).wait_send()

    @pl.when(jnp.logical_not(place.inner))
    def outer():
        for column in columns:
            if index == 0:
                column.copy(0).start()
            if index == 1:
                column.copy(0).wait_send()
            if index == 3:
                column.copy(2).wait_recv()
                column.write(column.land[0])


class Item:
    steps = 7

    def __init__(self, place, work, land, sems, load, store=None):
        self.place, self.work, self.land, self.sems = place, work, land, sems
        self.load, self.store = load, store
        self.base = place.core * HALF

    def column(self, flow):
        rows = rows_at(self.base + self.place.flow(flow)[4], KEEP)

        def read():
            return self.work[:, rows]

        def write(value):
            self.work[:, rows] = value

        sems = (self.sems[0].at[flow], self.sems[1].at[flow])
        return Column(self.place, self.work.at[:, rows], read, write, self.land.at[flow], sems)

    def copy(self, flow, index):
        first, second, near, far, keep, give = self.place.flow(flow)
        kept = self.work.at[:, rows_at(self.base + keep, KEEP)]
        half = self.work.at[:, rows_at(self.base + near, NEAR)]
        source, device = [
            (kept, self.place.partners[second]),
            (half, self.place.partners[first]),
        ][index]
        return remote(
            source, source, self.sems[0].at[flow, 3 + index], self.sems[1].at[flow, 3 + index], device
        )

    def pair(self):
        rows = self.work.at[:, rows_at(self.base, HALF)]
        return remote(rows, rows, self.sems[0].at[0, 5], self.sems[1].at[0, 5], self.place.twin)

    def step(self, index):
        for flow in range(FLOWS):
            if index == 0:
                self.load(self.work, rows_at(self.base + self.place.flow(flow)[4], KEEP), flow)
        if index <= 3:
            column_step(self.place, [self.column(flow) for flow in range(FLOWS)], index)
        for flow in range(FLOWS):
            if 4 <= index <= 5:
                self.copy(flow, index - 4).wait()
            if 3 <= index <= 4:
                self.copy(flow, index - 3).start()
        if index == 5:
            self.pair().start()
        if index == 6:
            self.pair().wait()
            self.store().start()


PAIR_CHUNK = (0, 1, 1, 2, 2, 2)
FRONT_PAIRS = (2, 4, 5, 6, 7, 8)
FRONT_REST = (7, 9, 10, 12, 13)
FRONT_LATE = 11
FRONT_LEAD = 9


def front_kernel(
    owner, lengths, master, vec_ref, x_in, c_in,
    x_out, c_out, n_out, one_out, two_out, late_out, q_ref, k_ref, v_ref, p_ref, r_ref, o_ref, ctx_ref,
    rank, rows_ref, normed, keys, turned_values, scores, slots,
    land_one, land_two, land_three, gift_one, gift_two, gift_three,
    one, one_land, two, two_land, late,
    spread_send, spread_recv, one_send, one_recv, two_send, two_recv,
    swap_send, swap_recv, swap_local, store_sem,
):
    pair = pl.program_id(0)
    row = pl.program_id(1)
    grid_step = pair * 2 + row
    place = Place()
    rows, span = x_in.shape[0] // 2, x_in.shape[1]
    land = (land_one, land_two, land_three)
    gift = (gift_one, gift_two, gift_three)
    spread = Spread(place, owner, rank, slots, land, gift, (spread_send, spread_recv))

    def swaps(index):
        source, target = [(x_in, rows_ref), (c_in, c_out)][index]
        here = pl.ds(place.core * span, span)
        near = pltpu.make_async_copy(
            source.at[pl.ds(place.core * rows, rows)], target.at[:, here], swap_local.at[index]
        )
        far = remote(
            source.at[pl.ds(place.other * rows, rows)],
            target.at[:, here],
            swap_send.at[index],
            swap_recv.at[index],
            place.twin,
        )
        return near, far

    def row_store():
        return pltpu.make_async_copy(rows_ref, x_out, store_sem.at[PAIRS + REST])

    def normed_store():
        return pltpu.make_async_copy(normed, n_out, store_sem.at[PAIRS + REST + 1])

    def pair_item(group):
        span_of = pl.ds(group, 1)

        def load(work, where, flow):
            chunk = PAIR_CHUNK[group]
            for tile in range(3):
                part = spread.piece(tile, flow, chunk, (group - GROUPS[chunk][0]) * PAIR, PAIR)
                work[0, where, pl.ds(tile * PAIR, PAIR)] = part

        def store():
            return pltpu.make_async_copy(one.at[span_of], one_out.at[span_of], store_sem.at[group])

        sems = (one_send.at[group], one_recv.at[group])
        return Item(place, one.at[span_of], one_land.at[:, :, span_of], sems, load, store)

    def rest_item(index):
        span_of = pl.ds(index, 1)

        def load(work, where, flow):
            for chunk, (start, wide) in enumerate(GROUPS):
                part = spread.piece(EARLY[index], flow, chunk, 0, wide * PAIR)
                work[0, where, pl.ds(start * PAIR, wide * PAIR)] = part

        def store():
            return pltpu.make_async_copy(
                two.at[span_of], two_out.at[span_of], store_sem.at[PAIRS + index]
            )

        sems = (two_send.at[index], two_recv.at[index])
        return Item(place, two.at[span_of], two_land.at[:, :, span_of], sems, load, store)

    def late_store():
        return pltpu.make_async_copy(late, late_out, store_sem.at[PAIRS + REST + 2])

    def late_pieces():
        for index, tile in enumerate(LATE):
            for flow in range(FLOWS):
                for chunk, (start, wide) in enumerate(GROUPS):
                    part = spread.piece(tile, flow, chunk, 0, wide * PAIR)
                    late[index, flow, :, pl.ds(start * PAIR, wide * PAIR)] = part
        late_store().start()

    def tick(number, odd):
        for chunk in range(CHUNKS):
            if odd == 0 and 0 <= number - 2 * chunk <= 2:
                spread.step(chunk, number - 2 * chunk)
        starts = [(pair_item, group, start) for group, start in enumerate(FRONT_PAIRS)]
        starts += [(rest_item, group, start) for group, start in enumerate(FRONT_REST)]
        for make, group, start in starts:
            if group % 2 == odd and 0 <= number - start < Item.steps:
                make(group).step(number - start)
        if number == FRONT_LATE and odd == 1:
            late_pieces()

    def both(number):
        tick(number, 0)
        tick(number, 1)

    @pl.when(grid_step == 0)
    def lead():
        slots[...] = master[...].astype(b16)
        for tile in range(PIECES):
            count = jnp.int32(0)
            for before in range(tile):
                count = count + (owner[before] == owner[tile]).astype(jnp.int32)
            rank[tile] = jnp.minimum(count, CAP - 1)
        place.greet()
        for copy in swaps(0):
            copy.start()
        both(0)
        for copy in swaps(1):
            copy.start()
        for copy in swaps(0):
            copy.wait()
        row_store().start()

        def norm_rows(index, carry):
            for part in range(rows):
                for block in range(4):
                    where = pl.ds(pl.multiple_of(index * 128 + block * 32, 32), 32)
                    unit, unused = norm_parts(rows_ref[part, where].astype(f32))
                    low = (unit * vec_ref[0:1, :] + vec_ref[1:2, :]).astype(b16)
                    normed[pl.ds(pl.multiple_of(part * LEN + index * 128 + block * 32, 32), 32)] = low
            return carry

        both(1)
        lax.fori_loop(0, LEN // 128, norm_rows, 0)
        normed_store().start()
        for number in range(2, FRONT_LEAD):
            both(number)

    for number in range(2 * PAIRS):
        pl.when(grid_step == number)(partial(tick, FRONT_LEAD + number, 0))

    @pl.when(row == 0)
    def project():
        lanes = pl.ds(pl.multiple_of(pair * PAIR, PAIR), PAIR)
        weight = one[pair]

        def part(index, carry):
            where = pl.ds(pl.multiple_of(index * 512, 512), 512)
            both = dot_nn(normed[where], weight)
            queries = both[:, :PAIR] + vec_ref[4:5, lanes]
            queries = (queries * (HEAD_DIM**-0.5 * LOG2E)).astype(b16)
            q_ref[:, where] = queries.T
            low = both[:, PAIR : 2 * PAIR].astype(b16)
            keys[where] = low
            k_ref[:, where] = low.T
            values = (both[:, 2 * PAIR :] + vec_ref[5:6, lanes]).astype(b16)
            v_ref[where] = values
            turned_values[:, where] = values.T
            return carry

        lax.fori_loop(0, normed.shape[0] // 512, part, 0)

    half = LEN // 2
    start = pl.multiple_of(row * LEN, LEN)
    split = lengths[place.core * rows + row, 0] < LEN
    shift = jnp.where(split, jnp.float32(-1e30), jnp.float32(0.0))

    quarter = LEN // 4
    for head, step in [(head, step) for head in range(2) for step in range(2)]:
        if (head, step) == (1, 0):
            for number in range(2 * PAIRS):
                pl.when(grid_step == number)(partial(tick, FRONT_LEAD + number, 1))
        part = slice(head * HEAD_DIM, (head + 1) * HEAD_DIM)
        here = slice(step * half, (step + 1) * half)
        queries = q_ref[:, pl.ds(pl.multiple_of(start + step * half, half), half)]
        peak = None
        for block in range(4):
            rows_here = pl.ds(pl.multiple_of(start + block * quarter, quarter), quarter)
            raw = dot_nn(head_only(keys[rows_here], head), queries)
            if block // 2 != step:
                raw = raw + shift
            scores[step, block * quarter : (block + 1) * quarter] = raw
            best = jnp.max(raw.reshape(-1, 8, half), axis=0)
            peak = best if peak is None else jnp.maximum(peak, best)
        top = jnp.max(peak, 0, keepdims=True)
        total = jnp.zeros((8, half), f32)
        for block in range(LEN // 64):
            rows_here = slice(block * 64, (block + 1) * 64)
            value = jnp.exp2(scores[step, rows_here] - top)
            total = total + jnp.sum(value.reshape(-1, 8, half), axis=0)
            p_ref[head, rows_here, here] = value.astype(b16)
        recip = 1.0 / jnp.sum(total, 0, keepdims=True)
        r_ref[0, head : head + 1, here] = recip
        out = dot_nn(turned_values[part, pl.ds(start, LEN)], p_ref[head, :, here])
        o_ref[part, here] = (out * recip).astype(b16)
    ctx_ref[...] = o_ref[...].T

    @pl.when(grid_step == 2 * PAIRS - 1)
    def finish_copies():
        for copy in swaps(1):
            copy.wait()
        row_store().wait()
        normed_store().wait()
        for group in range(PAIRS):
            pair_item(group).store().wait()
        for group in range(REST):
            rest_item(group).store().wait()
        late_store().wait()


def front(owner, lengths, master, vectors, inputs, cotangent):
    rows, span = inputs.shape[0] // 2, inputs.shape[1]
    tokens = rows * LEN
    any_spec = pl.BlockSpec(memory_space=pl.ANY)
    smem = pl.BlockSpec(memory_space=pltpu.SMEM)
    whole = jax.ShapeDtypeStruct((rows, LEN, D), b16)
    dma = pltpu.SemaphoreType.DMA
    return pl.pallas_call(
        front_kernel,
        grid=(PAIRS, rows),
        in_specs=[
            smem,
            smem,
            pl.BlockSpec((CAP, HALF, D), lambda h, r: (0, 0, 0), pipeline_mode=pl.Buffered(1)),
            pl.BlockSpec((PIECES, D), lambda h, r: (0, 0)),
            any_spec,
            any_spec,
        ],
        out_specs=[any_spec] * 6
        + [
            pl.BlockSpec((PAIR, tokens), lambda h, r: (h, 0)),
            pl.BlockSpec((PAIR, tokens), lambda h, r: (h, 0)),
            pl.BlockSpec((tokens, PAIR), lambda h, r: (0, h)),
            pl.BlockSpec((2, LEN, LEN), lambda h, r: (h * 2 + r, 0, 0)),
            pl.BlockSpec((1, 2, LEN), lambda h, r: (h * 2 + r, 0, 0)),
            pl.BlockSpec((PAIR, LEN), lambda h, r: (h, r)),
            pl.BlockSpec((LEN, PAIR), lambda h, r: (r, h)),
        ],
        out_shape=[
            whole,
            whole,
            jax.ShapeDtypeStruct((tokens, D), b16),
            jax.ShapeDtypeStruct((PAIRS, D, WIDE), b16),
            jax.ShapeDtypeStruct((REST, D, D), b16),
            jax.ShapeDtypeStruct((len(LATE), FLOWS, KEEP, D), b16),
            jax.ShapeDtypeStruct((D, tokens), b16),
            jax.ShapeDtypeStruct((D, tokens), b16),
            jax.ShapeDtypeStruct((tokens, D), b16),
            jax.ShapeDtypeStruct((rows * HEADS, LEN, LEN), b16),
            jax.ShapeDtypeStruct((rows * PAIRS, 2, LEN), f32),
            jax.ShapeDtypeStruct((D, tokens), b16),
            jax.ShapeDtypeStruct((tokens, D), b16),
        ],
        scratch_shapes=[
            pltpu.SMEM((PIECES,), jnp.int32),
            pltpu.VMEM((rows, LEN, D), b16),
            pltpu.VMEM((tokens, D), b16),
            pltpu.VMEM((tokens, PAIR), b16),
            pltpu.VMEM((PAIR, tokens), b16),
            pltpu.VMEM((2, LEN, LEN // 2), f32),
            pltpu.VMEM((CAP, HALF, D), b16),
        ]
        + [pltpu.VMEM((FLOWS, CAP, NEAR, wide * PAIR), b16) for unused, wide in GROUPS]
        + [pltpu.VMEM((FLOWS, 2 * CAP, KEEP, wide * PAIR), b16) for unused, wide in GROUPS]
        + [
            pltpu.VMEM((PAIRS, D, WIDE), b16),
            pltpu.VMEM((FLOWS, 2, PAIRS, KEEP, WIDE), b16),
            pltpu.VMEM((REST, D, D), b16),
            pltpu.VMEM((FLOWS, 2, REST, KEEP, D), b16),
            pltpu.VMEM((len(LATE), FLOWS, KEEP, D), b16),
            dma((CHUNKS, FLOWS, 3)),
            dma((CHUNKS, FLOWS, 3)),
            dma((PAIRS, FLOWS, 6)),
            dma((PAIRS, FLOWS, 6)),
            dma((REST, FLOWS, 6)),
            dma((REST, FLOWS, 6)),
            dma((2,)),
            dma((2,)),
            dma((2,)),
            dma((PAIRS + REST + 3,)),
        ],
        compiler_params=pltpu.CompilerParams(
            collective_id=0, has_side_effects=True, vmem_limit_bytes=60 * MIB
        ),
        name="front",
    )(owner, lengths, master, vectors, inputs, cotangent)


class Sum:
    steps = 7

    def __init__(self, place, work, wide, narrow, sems, send_pair, add_own):
        self.place, self.work, self.wide, self.narrow, self.sems = place, work, wide, narrow, sems
        self.send_pair, self.add_own = send_pair, add_own

    def column(self, flow):
        rows = rows_at(self.place.flow(flow)[4], KEEP)

        def read():
            return self.work[:, rows]

        def write(value):
            self.work[:, rows] = value

        sems = (self.sems[0].at[flow, pl.ds(2, 3)], self.sems[1].at[flow, pl.ds(2, 3)])
        land = self.narrow.at[flow, pl.ds(1, 2)]
        return Column(self.place, self.work.at[:, rows], read, write, land, sems)

    def copy(self, flow, index):
        first, second, near, far, keep, give = self.place.flow(flow)
        source, target, device = [
            (self.work.at[:, rows_at(far, NEAR)], self.wide.at[flow], first),
            (self.work.at[:, rows_at(give, KEEP)], self.narrow.at[flow, 0], second),
        ][index]
        return remote(
            source,
            target,
            self.sems[0].at[flow, index],
            self.sems[1].at[flow, index],
            self.place.partners[device],
        )

    def add(self, rows, value):
        self.work[:, rows] = (self.work[:, rows].astype(f32) + value.astype(f32)).astype(b16)

    def step(self, index):
        if index == 0:
            self.send_pair().start()
        if index == 1:
            self.send_pair().wait()
            self.add_own()
        for flow in range(FLOWS):
            first, second, near, far, keep, give = self.place.flow(flow)
            if index == 1:
                self.copy(flow, 0).start()
            if index == 2:
                self.copy(flow, 0).wait()
                self.add(rows_at(near, NEAR), self.wide[flow])
                self.copy(flow, 1).start()
            if index == 3:
                self.copy(flow, 1).wait()
                self.add(rows_at(keep, KEEP), self.narrow[flow, 0])
        if index >= 3:
            columns = [self.column(flow) for flow in range(FLOWS)]
            column_step(self.place, columns, index - 3)


class Gather:
    steps = 3

    def __init__(self, place, work, narrow, wide, sems):
        self.place, self.work, self.narrow, self.wide = place, work, narrow, wide
        self.sems = sems

    def copy(self, flow, index):
        first, second, near, far, keep, give = self.place.flow(flow)
        rows, target, device = [
            (rows_at(keep, KEEP), self.narrow, second),
            (rows_at(near, NEAR), self.wide, first),
        ][index]
        return remote(
            self.work.at[:, rows],
            target.at[flow],
            self.sems[0].at[flow, 5 + index],
            self.sems[1].at[flow, 5 + index],
            self.place.partners[device],
        )

    def step(self, index):
        for flow in range(FLOWS):
            first, second, near, far, keep, give = self.place.flow(flow)
            if index > 0:
                self.copy(flow, index - 1).wait()
            if index == 1:
                self.work[:, rows_at(give, KEEP)] = self.narrow[flow]
            if index == 2:
                self.work[:, rows_at(far, NEAR)] = self.wide[flow]
            if index < 2:
                self.copy(flow, index).start()


class Hand:
    steps = 3

    def __init__(self, place, table, kept, bag, gift, pack, last, own, out, sems, store_sems):
        self.place, self.table, self.kept = place, table, kept
        self.bag, self.gift, self.pack, self.last, self.own = bag, gift, pack, last, own
        self.out, self.sems, self.store_sems = out, sems, store_sems

    def tile(self, chip, rank, flow):
        return self.kept[self.table[chip * CAP + rank], flow]

    def copy(self, flow, index):
        first, second = self.place.flow(flow)[:2]
        source, target, device = [
            (self.bag.at[flow], self.gift.at[flow], second),
            (self.pack.at[flow], self.last.at[flow], first),
        ][index]
        return remote(
            source,
            target,
            self.sems[0].at[flow, index],
            self.sems[1].at[flow, index],
            self.place.partners[device],
        )

    def stores(self, flow):
        first, second, near, far, keep, give = self.place.flow(flow)
        parts = [
            (self.own.at[flow], rows_at(keep, KEEP)),
            (self.gift.at[flow, pl.ds(0, CAP)], rows_at(give, KEEP)),
            (self.last.at[flow], rows_at(far, NEAR)),
        ]
        return [
            pltpu.make_async_copy(source, self.out.at[:, rows], self.store_sems.at[flow, index])
            for index, (source, rows) in enumerate(parts)
        ]

    def step(self, index):
        for flow in range(FLOWS):
            first, second, near, far, keep, give = self.place.flow(flow)
            if index == 0:
                beside = self.place.chips[second]
                across = beside + self.place.chips[first] - self.place.me
                for rank in range(CAP):
                    self.bag[flow, rank] = self.tile(beside, rank, flow)
                    self.bag[flow, CAP + rank] = self.tile(across, rank, flow)
                    self.own[flow, rank] = self.tile(self.place.me, rank, flow)
                self.copy(flow, 0).start()
            if index == 1:
                self.copy(flow, 0).wait()
                for rank in range(CAP):
                    mine = self.tile(self.place.chips[first], rank, flow)
                    self.pack[flow, rank, rows_at(keep - near, KEEP)] = mine
                    self.pack[flow, rank, rows_at(give - near, KEEP)] = self.gift[flow, CAP + rank]
                self.copy(flow, 1).start()
            if index == 2:
                self.copy(flow, 1).wait()
                for copy in self.stores(flow):
                    copy.start()


FEED_SIZE = 256
FEED_PARTS = 2
FEED_TILES = 2 * FEED_PARTS


def eights(value):
    return jnp.sum(value.reshape(-1, 8, D), axis=0)


def add_sum(sums_ref, row, value):
    sums_ref[row : row + 1, :] += jnp.sum(value, 0, keepdims=True)


def row_blocks():
    return [slice(start, start + 16) for start in range(0, FEED_SIZE, 16)]


def feed_chunk(part, up, down, bias, normed, turned, cot, out_ref, grad_ref, acc_ref, first, scratch):
    hidden_ref, pulled_ref, active_ref, slope_ref = scratch
    hidden_ref[part] = dot_nn(normed, up)
    pulled_ref[part] = dot_nt(cot, down)
    total = jnp.zeros((8, D), f32)
    for rows in row_blocks():
        active, slope = gelu_parts(hidden_ref[part, rows] + bias)
        active_ref[part, rows] = active.astype(b16)
        pulled = (pulled_ref[part, rows] * slope).astype(b16)
        slope_ref[part, rows] = pulled
        total = total + eights(pulled.astype(f32))
    out_ref[...] += dot_nn(active_ref[part], down)
    grad_ref[...] += dot_nt(slope_ref[part], up)
    acc_ref[first + part] += dot_nn(turned, slope_ref[part])
    acc_ref[first + FEED_PARTS + part] += dot_tn(active_ref[part], cot)
    return total


def send_tiles(acc_ref, stage_ref, tiles_ref, sem_ref):
    copies = []
    for part in range(acc_ref.shape[0]):
        if part >= 2:
            copies[part - 2].wait()
        stage_ref[part % 2] = acc_ref[part].astype(b16)
        copy = pltpu.make_async_copy(
            stage_ref.at[part % 2], tiles_ref.at[part], sem_ref.at[part % 2]
        )
        copy.start()
        copies.append(copy)
    copies[-2].wait()
    copies[-1].wait()


def feed_one_kernel(
    c_ref, x_ref, g_ref, w_ref, vec_ref, pieces,
    out_ref, grad_ref, normed, unit_ref, rstd_ref, sums_ref, late_out, tiles_ref,
    acc_ref, stage_ref, hidden_ref, pulled_ref, active_ref, slope_ref, late, late_land,
    sem_ref, late_send, late_recv, store_sem,
):
    step = pl.program_id(0)
    place = Place()
    scratch = (hidden_ref, pulled_ref, active_ref, slope_ref)

    def item(index):
        span_of = pl.ds(index, 1)

        def load(work, where, flow):
            work[0, where] = pieces[index, flow]

        def store():
            return pltpu.make_async_copy(late.at[span_of], late_out.at[span_of], store_sem.at[index])

        sems = (late_send.at[index], late_recv.at[index])
        return Item(place, late.at[span_of], late_land.at[:, :, span_of], sems, load, store)

    def tick(number):
        for index in range(len(LATE)):
            since = number - index
            if since >= 0 and since % 2 == 0 and since // 2 < Item.steps:
                item(index).step(since // 2)

    @pl.when(step == 0)
    def clear():
        place.greet()
        acc_ref[...] = jnp.zeros_like(acc_ref)
        sums_ref[...] = jnp.zeros_like(sums_ref)

    for number in range(8):
        pl.when(step == number)(partial(tick, 2 * number))
    out_ref[...] = dot_nn(c_ref[...], w_ref[0])
    gain = vec_ref[2:3, :]
    for rows in row_blocks():
        residual = x_ref[rows].astype(f32) + (out_ref[rows] + vec_ref[6:7, :])
        unit, rstd = norm_parts(residual)
        unit_ref[rows] = unit.astype(b16)
        rstd_ref[rows] = jnp.broadcast_to(rstd, (16, 128))
        normed[rows] = (unit * gain + vec_ref[3:4, :]).astype(b16)
        out_ref[rows] = residual + vec_ref[7:8, :]
    grad_ref[...] = jnp.zeros_like(grad_ref)
    turned = normed[...].T
    for part in range(FEED_PARTS):
        if part == 1:
            for number in range(8):
                pl.when(step == number)(partial(tick, 2 * number + 1))
        total = feed_chunk(
            part, w_ref[1 + part], w_ref[1 + FEED_PARTS + part], vec_ref[8 + part : 9 + part, :],
            normed[...], turned, g_ref[...], out_ref, grad_ref, acc_ref, 0, scratch,
        )
        add_sum(sums_ref, 8 + part, total)

    @pl.when(step == pl.num_programs(0) - 1)
    def send():
        send_tiles(acc_ref, stage_ref, tiles_ref, sem_ref)
        for index in range(len(LATE)):
            item(index).store().wait()


def feed_scratch(count):
    return [
        pltpu.VMEM((count, D, D), f32),
        pltpu.VMEM((2, D, D), b16),
        pltpu.VMEM((FEED_PARTS, FEED_SIZE, D), f32),
        pltpu.VMEM((FEED_PARTS, FEED_SIZE, D), f32),
        pltpu.VMEM((FEED_PARTS, FEED_SIZE, D), b16),
        pltpu.VMEM((FEED_PARTS, FEED_SIZE, D), b16),
    ]


def feed_one(context, x, cot, early, vectors, pieces):
    tokens = x.shape[0]
    count = len(LATE)
    dma = pltpu.SemaphoreType.DMA
    token_block = pl.BlockSpec((FEED_SIZE, D), lambda i: (i, 0))
    any_spec = pl.BlockSpec(memory_space=pl.ANY)
    once = pl.Buffered(1)
    return pl.pallas_call(
        feed_one_kernel,
        grid=(tokens // FEED_SIZE,),
        in_specs=[
            token_block,
            token_block,
            token_block,
            pl.BlockSpec((REST, D, D), lambda i: (0, 0, 0), pipeline_mode=once),
            pl.BlockSpec((PIECES, D), lambda i: (0, 0)),
            pl.BlockSpec((count, FLOWS, KEEP, D), lambda i: (0, 0, 0, 0), pipeline_mode=once),
        ],
        out_specs=[
            token_block,
            token_block,
            token_block,
            token_block,
            pl.BlockSpec((FEED_SIZE, 128), lambda i: (i, 0)),
            pl.BlockSpec((16, D), lambda i: (0, 0)),
            any_spec,
            any_spec,
        ],
        out_shape=[
            jax.ShapeDtypeStruct((tokens, D), f32),
            jax.ShapeDtypeStruct((tokens, D), f32),
            jax.ShapeDtypeStruct((tokens, D), b16),
            jax.ShapeDtypeStruct((tokens, D), b16),
            jax.ShapeDtypeStruct((tokens, 128), f32),
            jax.ShapeDtypeStruct((16, D), f32),
            jax.ShapeDtypeStruct((count, D, D), b16),
            jax.ShapeDtypeStruct((FEED_TILES, D, D), b16),
        ],
        scratch_shapes=feed_scratch(FEED_TILES)
        + [
            pltpu.VMEM((count, D, D), b16),
            pltpu.VMEM((FLOWS, 2, count, KEEP, D), b16),
            dma((2,)),
            dma((count, FLOWS, 6)),
            dma((count, FLOWS, 6)),
            dma((count,)),
        ],
        compiler_params=pltpu.CompilerParams(
            collective_id=1, has_side_effects=True, vmem_limit_bytes=60 * MIB
        ),
        name="feed_one",
    )(context, x, cot, early, vectors, pieces)


def feed_two_kernel(
    out_in, grad_in, normed, unit_ref, rstd_ref, g_ref, o_ref, w_out, w_ref, vec_ref, sums_in, tiles_in,
    y_ref, r_ref, d_ref, sums_ref, tiles_ref, kept_ref,
    acc_ref, stage_ref, hidden_ref, pulled_ref, active_ref, slope_ref, out_ref, grad_ref,
    work, wide, narrow, own_stage,
    sem_ref, sum_send, sum_recv, pair_send, pair_recv, load_sem,
):
    step = pl.program_id(0)
    place = Place()
    scratch = (hidden_ref, pulled_ref, active_ref, slope_ref)
    near_half = rows_at(place.core * HALF, HALF)
    far_half = rows_at(place.other * HALF, HALF)

    def load_own(index):
        return pltpu.make_async_copy(
            tiles_in.at[index, near_half], own_stage.at[index], load_sem.at[index]
        )

    def tile_sum(index):
        span_of = pl.ds(index, 1)

        def send_pair():
            return remote(
                tiles_in.at[span_of, far_half],
                work.at[span_of],
                pair_send.at[index],
                pair_recv.at[index],
                place.twin,
            )

        def add_own():
            load_own(index).wait()
            total = work[index].astype(f32) + own_stage[index].astype(f32)
            work[index] = total.astype(b16)

        sems = (sum_send.at[index], sum_recv.at[index])
        parts = (wide.at[:, span_of], narrow.at[:, :, span_of])
        return Sum(place, work.at[span_of], *parts, sems, send_pair, add_own)

    def tick(number):
        for index in range(FEED_TILES):
            since = number - index
            if since >= 0 and since % 2 == 0 and since // 2 < Sum.steps:
                tile_sum(index).step(since // 2)
                if since // 2 == Sum.steps - 1:
                    for flow in range(FLOWS):
                        rows_kept = rows_at(place.flow(flow)[4], KEEP)
                        kept_ref[index, flow] = work[index, rows_kept]

    @pl.when(step == 0)
    def clear():
        for index in range(FEED_TILES):
            load_own(index).start()
        place.greet()
        acc_ref[...] = jnp.zeros_like(acc_ref)
        sums_ref[...] = sums_in[...]

    for number in range(8):
        pl.when(step == number)(partial(tick, 2 * number))
    out_ref[...] = out_in[...]
    grad_ref[...] = grad_in[...]
    turned = normed[...].T
    for part in range(FEED_PARTS):
        if part == 1:
            for number in range(8):
                pl.when(step == number)(partial(tick, 2 * number + 1))
        row = 8 + FEED_PARTS + part
        total = feed_chunk(
            part, w_ref[part], w_ref[FEED_PARTS + part], vec_ref[row : row + 1, :],
            normed[...], turned, g_ref[...], out_ref, grad_ref, acc_ref, 1, scratch,
        )
        add_sum(sums_ref, row, total)
    y_ref[...] = out_ref[...].astype(b16)
    gain = vec_ref[2:3, :]
    totals = [jnp.zeros((8, D), f32) for unused in range(4)]
    for rows in row_blocks():
        grad, unit, cot = grad_ref[rows], unit_ref[rows].astype(f32), g_ref[rows].astype(f32)
        back = cot + norm_back(grad, unit, rstd_ref[rows, 0:1], gain)
        low = back.astype(b16)
        r_ref[rows] = low
        terms = (grad * unit, grad, low.astype(f32), cot)
        totals = [total + eights(term) for total, term in zip(totals, terms)]
    for row, total in zip((2, 3, 6, 7), totals):
        add_sum(sums_ref, row, total)
    low = r_ref[...]
    d_ref[...] = dot_nt(w_out[0], low).astype(b16)
    acc_ref[0] += dot_nn(o_ref[...], low)

    @pl.when(step == pl.num_programs(0) - 1)
    def send():
        send_tiles(acc_ref, stage_ref, tiles_ref, sem_ref)


def feed_two(out, grad, normed, unit, rstd, cot, turned, early, late, vectors, sums, tiles):
    tokens = cot.shape[0]
    count = len(LATE)
    dma = pltpu.SemaphoreType.DMA
    token_block = pl.BlockSpec((FEED_SIZE, D), lambda i: (i, 0))
    turned_block = pl.BlockSpec((D, FEED_SIZE), lambda i: (0, i))
    any_spec = pl.BlockSpec(memory_space=pl.ANY)
    sums_block = pl.BlockSpec((16, D), lambda i: (0, 0))
    once = pl.Buffered(1)
    return pl.pallas_call(
        feed_two_kernel,
        grid=(tokens // FEED_SIZE,),
        in_specs=[
            token_block,
            token_block,
            token_block,
            token_block,
            pl.BlockSpec((FEED_SIZE, 128), lambda i: (i, 0)),
            token_block,
            turned_block,
            pl.BlockSpec((1, D, D), lambda i: (0, 0, 0), pipeline_mode=once),
            pl.BlockSpec((count, D, D), lambda i: (0, 0, 0), pipeline_mode=once),
            pl.BlockSpec((PIECES, D), lambda i: (0, 0)),
            sums_block,
            any_spec,
        ],
        out_specs=[
            token_block,
            token_block,
            turned_block,
            sums_block,
            any_spec,
            pl.BlockSpec((FEED_TILES, FLOWS, KEEP, D), lambda i: (0, 0, 0, 0)),
        ],
        out_shape=[
            jax.ShapeDtypeStruct((tokens, D), b16),
            jax.ShapeDtypeStruct((tokens, D), b16),
            jax.ShapeDtypeStruct((D, tokens), b16),
            jax.ShapeDtypeStruct((16, D), f32),
            jax.ShapeDtypeStruct((1 + FEED_TILES, D, D), b16),
            jax.ShapeDtypeStruct((FEED_TILES, FLOWS, KEEP, D), b16),
        ],
        scratch_shapes=feed_scratch(1 + FEED_TILES)
        + [
            pltpu.VMEM((FEED_SIZE, D), f32),
            pltpu.VMEM((FEED_SIZE, D), f32),
            pltpu.VMEM((FEED_TILES, HALF, D), b16),
            pltpu.VMEM((FLOWS, FEED_TILES, NEAR, D), b16),
            pltpu.VMEM((FLOWS, 3, FEED_TILES, KEEP, D), b16),
            pltpu.VMEM((FEED_TILES, HALF, D), b16),
            dma((2,)),
            dma((FEED_TILES, FLOWS, 5)),
            dma((FEED_TILES, FLOWS, 5)),
            dma((FEED_TILES,)),
            dma((FEED_TILES,)),
            dma((FEED_TILES,)),
        ],
        compiler_params=pltpu.CompilerParams(
            collective_id=2, has_side_effects=True, vmem_limit_bytes=60 * MIB
        ),
        name="feed_two",
    )(out, grad, normed, unit, rstd, cot, turned, early, late, vectors, sums, tiles)


BACK_STEPS = 2 * PAIRS
BACK_TAIL = 4
BACK_PAIRS = tuple((index, 1) for index in range(PAIRS))
BACK_REST = (0, 1, 1, 2, 3)
BACK_HAND = 10


def back_kernel(
    table, p_ref, r_ref, v_ref, q_ref, k_ref, o_ref, g_ref, w_ref, n_ref, x_ref, z_ref, vec_ref,
    tiles_in, kept_in, sums_in, y_in,
    y_out, i_out, pairs_out, slots_out, sums_ref,
    grad_sum, wide_sum, turned, slopes, block_out,
    two, two_wide, two_narrow, two_stage, one, one_wide, one_narrow, one_send_stage, one_stage,
    gather_narrow, gather_wide,
    kept, bag, gift, pack, last, own, vec_land,
    two_send, two_recv, one_send, one_recv, hand_send, hand_recv, hand_store,
    pair_two_send, pair_two_recv, pair_one_send, pair_one_recv, load_sem, kept_sem, store_sem,
    swap_send, swap_recv, swap_local, vec_send, vec_recv,
):
    step = pl.program_id(0)
    place = Place()
    rows, span = y_in.shape[0], y_in.shape[1] // 2
    near_half = rows_at(place.core * HALF, HALF)
    far_half = rows_at(place.other * HALF, HALF)

    def load_two(index):
        return pltpu.make_async_copy(
            tiles_in.at[pl.ds(index, 1), near_half],
            two_stage.at[pl.ds(index % 3, 1)],
            load_sem.at[index % 3],
        )

    def rest_sum(index):
        work = two.at[pl.ds(index, 1)]

        def send_pair():
            return remote(
                tiles_in.at[pl.ds(index, 1), far_half],
                work,
                pair_two_send.at[index],
                pair_two_recv.at[index],
                place.twin,
            )

        def add_own():
            load_two(index).wait()
            work[...] = (work[...].astype(f32) + two_stage[index % 3].astype(f32)).astype(b16)

        sems = (two_send.at[index], two_recv.at[index])
        wide, narrow = two_wide.at[:, pl.ds(index, 1)], two_narrow.at[:, :, pl.ds(index, 1)]
        return Sum(place, work, wide, narrow, sems, send_pair, add_own)

    def keep_total(index):
        for flow in range(FLOWS):
            rows_kept = rows_at(place.flow(flow)[4], KEEP)
            kept[len(LATE) + index, flow] = two[index, rows_kept]

    def load_kept():
        return pltpu.make_async_copy(kept_in, kept.at[pl.ds(0, len(LATE))], kept_sem.at[0])

    def pair_sum(group):
        first, count = BACK_PAIRS[group]
        span_of = pl.ds(first, count)
        work = one.at[span_of]

        def send_pair():
            return remote(
                one_send_stage.at[pl.ds(group % 2, 1)],
                work,
                pair_one_send.at[group],
                pair_one_recv.at[group],
                place.twin,
            )

        def add_own():
            own = one_stage[group % 2].astype(f32)
            work[...] = (work[...].astype(f32) + own).astype(b16)

        sems = (one_send.at[group], one_recv.at[group])
        wide, narrow = one_wide.at[:, span_of], one_narrow.at[:, :, span_of]
        return Sum(place, work, wide, narrow, sems, send_pair, add_own)

    def pair_gather(group):
        first, count = BACK_PAIRS[group]
        span_of = pl.ds(first, count)
        sems = (one_send.at[group], one_recv.at[group])
        narrow, wide = gather_narrow.at[:, span_of], gather_wide.at[:, span_of]
        return Gather(place, one.at[span_of], narrow, wide, sems)

    hand = Hand(
        place, table, kept, bag, gift, pack, last, own, slots_out, (hand_send, hand_recv), hand_store
    )

    def pair_store(index, tile):
        return pltpu.make_async_copy(
            one.at[index, :, pl.ds(tile * PAIR, PAIR)],
            pairs_out.at[tile, :, pl.ds(index * PAIR, PAIR)],
            store_sem.at[index, tile],
        )

    def tick(number, odd):
        for group, start in enumerate(BACK_REST):
            if group % 2 == odd and 0 <= number - start < Sum.steps:
                rest_sum(group).step(number - start)
                if number - start == Sum.steps - 1:
                    keep_total(group)
        for group, (first, count) in enumerate(BACK_PAIRS):
            if group % 2 != odd:
                continue
            start = 2 * (first + count)
            if 0 <= number - start < Sum.steps:
                pair_sum(group).step(number - start)
            if 0 <= number - start - Sum.steps + 1 < Gather.steps:
                pair_gather(group).step(number - start - Sum.steps + 1)
            if number == start + Sum.steps + 1:
                for index in range(first, first + count):
                    for tile in range(3):
                        pair_store(index, tile).start()
        if odd == 0 and 0 <= number - BACK_HAND < Hand.steps:
            if number == BACK_HAND:
                load_kept().wait()
            hand.step(number - BACK_HAND)
        for group, start in enumerate(BACK_REST):
            if odd == 1 and number == max(start - 1, 0):
                load_two(group).start()

    def both(number):
        tick(number, 0)
        tick(number, 1)

    def swap_y(index):
        there = pl.ds(place.core * rows, rows)
        if index == 0:
            return pltpu.make_async_copy(
                y_in.at[:, pl.ds(place.core * span, span)], y_out.at[there], swap_local.at[0]
            )
        return remote(
            y_in.at[:, pl.ds(place.other * span, span)],
            y_out.at[there],
            swap_send.at[0],
            swap_recv.at[0],
            place.twin,
        )

    @pl.when(step == 0)
    def lead():
        place.greet()
        load_kept().start()
        for index in range(2):
            swap_y(index).start()
        sums_ref[...] = sums_in[...]

    for number in range(BACK_STEPS + BACK_TAIL):
        early = partial(tick, number, 0) if number < BACK_STEPS else partial(both, number)
        pl.when(step == number)(early)

    half = LEN // 2
    pair, row = step // 2, lax.rem(step, 2)

    def attention(head):
        part = slice(head * HEAD_DIM, (head + 1) * HEAD_DIM)
        values = head_only(v_ref[...], head)
        recip = r_ref[0, head : head + 1, :]
        grad = g_ref[part, :].astype(f32) * recip
        delta = jnp.sum(grad * o_ref[part, :].astype(f32), 0, keepdims=True)
        grad = grad.astype(b16)
        doubled = jnp.concatenate([grad, grad], axis=0)
        value_grad, key_grad = [], []
        quarter = LEN // 4
        for which in range(2):
            cols = slice(which * half, (which + 1) * half)
            shift = delta[:, cols]
            for block in range(4):
                raw = dot_nn(values[block * quarter : (block + 1) * quarter], doubled[:, cols])
                for small in range(quarter // 64):
                    rows_here = slice(block * quarter + small * 64, block * quarter + (small + 1) * 64)
                    slope = raw[small * 64 : (small + 1) * 64] - shift
                    slope = p_ref[head, rows_here, cols].astype(f32) * slope
                    slopes[rows_here] = slope.astype(b16)
            value_grad.append(dot_nt(grad[:, cols], p_ref[head, :, cols]))
            key_grad.append(dot_nt(q_ref[part, cols], slopes[...]))
            query_grad = dot_nn(k_ref[part, :], slopes[...]) * (HEAD_DIM**-0.5)
            turned[part, cols] = query_grad.astype(b16)
        lower = slice(PAIR + head * HEAD_DIM, PAIR + (head + 1) * HEAD_DIM)
        turned[lower, :] = ((key_grad[0] + key_grad[1]) * (1.0 / LOG2E)).astype(b16)
        lower = slice(2 * PAIR + head * HEAD_DIM, 2 * PAIR + (head + 1) * HEAD_DIM)
        turned[lower, :] = (value_grad[0] + value_grad[1]).astype(b16)

    @pl.when(step < BACK_STEPS)
    def first_head():
        attention(0)

    for number in range(BACK_STEPS):
        pl.when(step == number)(partial(tick, number, 1))

    @pl.when(step < BACK_STEPS)
    def second_head():
        attention(1)
        where = pl.ds(pl.multiple_of(row * LEN, LEN), LEN)
        block = dot_nn(turned[...], n_ref[where])
        back = turned[...].T
        lanes = pl.ds(pl.multiple_of(pair * PAIR, PAIR), PAIR)
        ones = jnp.sum(back.astype(f32), 0, keepdims=True)
        sums_ref[4:5, lanes] += ones[:, :PAIR]
        sums_ref[5:6, lanes] += ones[:, 2 * PAIR :]
        term = dot_nt(back, w_ref[0])

        @pl.when(pair == 0)
        def begin():
            grad_sum[where] = term

        @pl.when(pair > 0)
        def add():
            grad_sum[where] += term

        @pl.when(row == 0)
        def keep():
            wide_sum[...] = block

        @pl.when(row == 1)
        def hand_on():
            whole = (wide_sum[...] + block).T
            low = whole.astype(b16)
            for core in range(2):

                @pl.when(place.core == core)
                def split():
                    slot = lax.rem(pair, 2)
                    one_stage[slot] = low[core * HALF : (core + 1) * HALF]
                    one_send_stage[slot] = low[(1 - core) * HALF : (2 - core) * HALF]

    def store_block(index):
        row, half = index // 2, index % 2
        target = i_out.at[place.core * rows + row]
        local = pltpu.make_async_copy(block_out.at[half], target, swap_local.at[1 + row])
        far = remote(
            block_out.at[half], target, swap_send.at[1 + row], swap_recv.at[1 + row], place.twin
        )
        return local, far, half

    def wait_block(index):
        local, far, half = store_block(index)

        @pl.when(place.core == half)
        def keep():
            local.wait()

        @pl.when(place.core != half)
        def give():
            far.wait()

    for index in range(BACK_TAIL):

        @pl.when(step == BACK_STEPS + index)
        def close():
            size = LEN // 2
            if index >= 2:
                wait_block(index - 2)
            gain_sum = jnp.zeros((8, D), f32)
            shift_sum = jnp.zeros((8, D), f32)
            for block in range(size // 16):
                rows_here = slice(block * 16, (block + 1) * 16)
                grad = grad_sum[index * size + block * 16 : index * size + (block + 1) * 16]
                unit, rstd = norm_parts(x_ref[rows_here].astype(f32))
                gain_sum = gain_sum + jnp.sum((grad * unit).reshape(-1, 8, D), axis=0)
                shift_sum = shift_sum + jnp.sum(grad.reshape(-1, 8, D), axis=0)
                total = norm_back(grad, unit, rstd, vec_ref[0:1, :])
                block_out[index % 2, rows_here] = (z_ref[rows_here].astype(f32) + total).astype(b16)
            sums_ref[0:1, :] += jnp.sum(gain_sum, 0, keepdims=True)
            sums_ref[1:2, :] += jnp.sum(shift_sum, 0, keepdims=True)
            local, far, half = store_block(index)

            @pl.when(place.core == half)
            def keep():
                local.start()

            @pl.when(place.core != half)
            def give():
                far.start()

    @pl.when(step == BACK_STEPS + BACK_TAIL - 1)
    def drain():
        devices = [place.twin] + place.partners

        def vector(index):
            return remote(
                sums_ref, vec_land.at[index], vec_send.at[index], vec_recv.at[index], devices[index]
            )

        vector(0).start()
        for number in range(BACK_STEPS + BACK_TAIL, BACK_STEPS + Sum.steps + Gather.steps):
            both(number)
            index = number - BACK_STEPS - BACK_TAIL
            if index < 5:
                vector(index).wait()
                sums_ref[...] += vec_land[index]
                if index < 4:
                    vector(index + 1).start()
        for index in range(2):
            swap_y(index).wait()
        for index in range(2, BACK_TAIL):
            wait_block(index)
        for index in range(PAIRS):
            for tile in range(3):
                pair_store(index, tile).wait()
        for flow in range(FLOWS):
            for copy in hand.stores(flow):
                copy.wait()


def back(table, attention, weights, normed, x, residual, vectors, tiles, kept, sums, y):
    rows, length = y.shape[:2]
    tokens = rows * length
    any_spec = pl.BlockSpec(memory_space=pl.ANY)
    smem = pl.BlockSpec(memory_space=pltpu.SMEM)
    dma = pltpu.SemaphoreType.DMA

    def now(step):
        return jnp.minimum(step, BACK_STEPS - 1)

    def tail(step):
        return jnp.maximum(step - BACK_STEPS, 0)

    head_block = pl.BlockSpec((PAIR, LEN), lambda s: (now(s) // 2, lax.rem(now(s), 2)))
    tail_block = pl.BlockSpec((LEN // 2, D), lambda s: (tail(s), 0))
    whole = pl.BlockSpec((PIECES, D), lambda s: (0, 0))
    sums_block = pl.BlockSpec((16, D), lambda s: (0, 0))
    return pl.pallas_call(
        back_kernel,
        grid=(BACK_STEPS + BACK_TAIL,),
        in_specs=[
            smem,
            pl.BlockSpec((2, LEN, LEN), lambda s: (now(s), 0, 0)),
            pl.BlockSpec((1, 2, LEN), lambda s: (now(s), 0, 0)),
            pl.BlockSpec((LEN, PAIR), lambda s: (lax.rem(now(s), 2), now(s) // 2)),
            head_block,
            head_block,
            head_block,
            head_block,
            pl.BlockSpec((1, D, WIDE), lambda s: (now(s) // 2, 0, 0)),
            pl.BlockSpec((tokens, D), lambda s: (0, 0), pipeline_mode=pl.Buffered(1)),
            tail_block,
            tail_block,
            whole,
            any_spec,
            any_spec,
            sums_block,
            any_spec,
        ],
        out_specs=[any_spec] * 4 + [sums_block],
        out_shape=[
            jax.ShapeDtypeStruct((2 * rows, length // 2, D), b16),
            jax.ShapeDtypeStruct((2 * rows, length // 2, D), b16),
            jax.ShapeDtypeStruct((3, HALF, D), b16),
            jax.ShapeDtypeStruct((CAP, HALF, D), b16),
            jax.ShapeDtypeStruct((16, D), f32),
        ],
        scratch_shapes=[
            pltpu.VMEM((tokens, D), f32),
            pltpu.VMEM((WIDE, D), f32),
            pltpu.VMEM((WIDE, LEN), b16),
            pltpu.VMEM((LEN, LEN // 2), b16),
            pltpu.VMEM((2, LEN // 2, D), b16),
            pltpu.VMEM((REST, HALF, D), b16),
            pltpu.VMEM((FLOWS, REST, NEAR, D), b16),
            pltpu.VMEM((FLOWS, 3, REST, KEEP, D), b16),
            pltpu.VMEM((3, HALF, D), b16),
            pltpu.VMEM((PAIRS, HALF, WIDE), b16),
            pltpu.VMEM((FLOWS, PAIRS, NEAR, WIDE), b16),
            pltpu.VMEM((FLOWS, 3, PAIRS, KEEP, WIDE), b16),
            pltpu.VMEM((2, HALF, WIDE), b16),
            pltpu.VMEM((2, HALF, WIDE), b16),
            pltpu.VMEM((FLOWS, PAIRS, KEEP, WIDE), b16),
            pltpu.VMEM((FLOWS, PAIRS, NEAR, WIDE), b16),
            pltpu.VMEM((len(LATE) + REST, FLOWS, KEEP, D), b16),
            pltpu.VMEM((FLOWS, 2 * CAP, KEEP, D), b16),
            pltpu.VMEM((FLOWS, 2 * CAP, KEEP, D), b16),
            pltpu.VMEM((FLOWS, CAP, NEAR, D), b16),
            pltpu.VMEM((FLOWS, CAP, NEAR, D), b16),
            pltpu.VMEM((FLOWS, CAP, KEEP, D), b16),
            pltpu.VMEM((5, 16, D), f32),
            dma((REST, FLOWS, 5)),
            dma((REST, FLOWS, 5)),
            dma((PAIRS, FLOWS, 7)),
            dma((PAIRS, FLOWS, 7)),
            dma((FLOWS, 2)),
            dma((FLOWS, 2)),
            dma((FLOWS, 3)),
            dma((REST,)),
            dma((REST,)),
            dma((PAIRS,)),
            dma((PAIRS,)),
            dma((3,)),
            dma((1,)),
            dma((PAIRS, 3)),
            dma((3,)),
            dma((3,)),
            dma((3,)),
            dma((5,)),
            dma((5,)),
        ],
        compiler_params=pltpu.CompilerParams(
            collective_id=3, has_side_effects=True, vmem_limit_bytes=62 * MIB
        ),
        name="back",
    )(table, *attention, weights, normed, x, residual, vectors, tiles, kept, sums, y)


def update_kernel(tile_at, one, two, w_ref, m_ref, s_ref, y_in, i_in, w_out, m_out, s_out, y_out, i_out):
    step = pl.program_id(0)
    tile = tile_at[step // 2]
    grad = jnp.where(tile < 3, one[0], two[0]).astype(f32)
    parts = adam_step(w_ref[0], grad, m_ref[0], s_ref[0], RATE)
    for target, part in zip((w_out, m_out, s_out), parts):
        target[0] = jnp.where(tile >= 0, part, jnp.zeros_like(part))

    @pl.when(step < 4)
    def widen():
        y_out[...] = y_in[...].astype(f32)
        i_out[...] = i_in[...].astype(f32)


def update(tile_at, one, two, master, first, second, y, grad):
    tokens = y.shape[0]
    size = HALF // 2
    state = pl.BlockSpec((1, size, D), lambda s, tile_at: (s // 2, lax.rem(s, 2), 0))
    wide = pl.BlockSpec((tokens // 4, D), lambda s, tile_at: (jnp.minimum(s, 3), 0))
    return pl.pallas_call(
        update_kernel,
        grid_spec=pltpu.PrefetchScalarGridSpec(
            num_scalar_prefetch=1,
            grid=(CAP * 2,),
            in_specs=[
                pl.BlockSpec(
                    (1, size, D),
                    lambda s, tile_at: (jnp.clip(tile_at[s // 2], 0, 2), lax.rem(s, 2), 0),
                ),
                state,
                state,
                state,
                state,
                wide,
                wide,
            ],
            out_specs=[state] * 3 + [wide] * 2,
        ),
        out_shape=[jax.ShapeDtypeStruct(master.shape, f32)] * 3
        + [jax.ShapeDtypeStruct((tokens, D), f32)] * 2,
        compiler_params=pltpu.CompilerParams(vmem_limit_bytes=60 * MIB),
        name="update",
    )(tile_at, one, two, master, first, second, y, grad)


def shards_paired(
    inputs,
    cotangent,
    doc_lengths,
    owner_list,
    master,
    first_moment,
    second_moment,
    vectors,
    vector_first,
    vector_second,
):
    rows_here, span, width = inputs.shape
    place = lax.axis_index("blk")
    member = lax.axis_index("dp")
    rows_mine = rows_here // 2
    order = jnp.arange(PIECES)
    same_owner = owner_list[:, None] == owner_list[None, :]
    ranks = jnp.sum(same_owner & (order[None, :] < order[:, None]), axis=1).astype(jnp.int32)
    slot_of = owner_list * CAP + ranks
    front_outs = front(owner_list, doc_lengths, master, vectors, inputs, cotangent)
    x, cot, normed, weights_one, early, pieces, queries, keys, values = front_outs[:9]
    weights, recips, context_turned, context = front_outs[9:]
    x = x.reshape(-1, width)
    cot = cot.reshape(-1, width)
    out, grad, normed_two, unit, rstd, sums, late, tiles_one = feed_one(
        context, x, cot, early, vectors, pieces
    )
    block_out, residual, grad_context, sums, tiles_two, kept = feed_two(
        out, grad, normed_two, unit, rstd, cot, context_turned, early, late, vectors, sums, tiles_one
    )
    hits = jnp.arange(16 * CAP)[:, None] == slot_of[None, :]
    tile_at = jnp.sum(jnp.where(hits, order[None, :] + 1, 0), axis=1).astype(jnp.int32) - 1
    spot = [0] * PIECES
    for index, tile in enumerate((4, 5, 8, 9) + (3,) + LATE):
        spot[tile] = index
    table = jnp.sum(jnp.where(hits, jnp.array(spot)[None, :], 0), axis=1).astype(jnp.int32)
    block_out, input_grad, total_one, total_two, vector_total = back(
        table,
        (weights, recips, values, queries, keys, context_turned, grad_context),
        weights_one,
        normed,
        x,
        residual,
        vectors,
        tiles_two,
        kept,
        sums,
        block_out.reshape(rows_mine, LEN, width),
    )
    mine = lax.dynamic_slice_in_dim(tile_at, member * CAP, CAP, 0)
    *updated, block_out, input_grad = update(
        mine,
        total_one,
        total_two,
        master,
        first_moment,
        second_moment,
        block_out.reshape(-1, width),
        input_grad.reshape(-1, width),
    )
    columns = vector_first.shape[1]
    vector_cols = lax.dynamic_slice_in_dim(vectors, place * columns, columns, 1)
    vector_total = lax.dynamic_slice(vector_total, (0, place * columns), (PIECES, columns))
    updated_vectors = adam_step(vector_cols, vector_total, vector_first, vector_second, VEC_RATE)
    return (
        block_out.reshape(inputs.shape),
        input_grad.reshape(inputs.shape),
        *updated,
        *updated_vectors,
    )


def solution(mesh):
    in_specs = (
        P("dp", "blk", None),
        P("dp", "blk", None),
        P("dp", None),
        P(),
        P("dp", "blk", None),
        P("dp", "blk", None),
        P("dp", "blk", None),
        P(),
        P(None, "blk"),
        P(None, "blk"),
    )
    out_specs = (
        P("dp", "blk", None),
        P("dp", "blk", None),
        P("dp", "blk", None),
        P("dp", "blk", None),
        P("dp", "blk", None),
        P(None, "blk"),
        P(None, "blk"),
        P(None, "blk"),
    )
    paired = mesh.shape["blk"] == 2 and mesh.shape["dp"] == 16
    shards = shards_paired if paired else shards_any
    return jax.shard_map(shards, mesh=mesh, in_specs=in_specs, out_specs=out_specs, check_vma=False)
```

```python
from functools import partial

import jax
import jax.numpy as jnp
from jax import lax
from jax.experimental import pallas as pl
from jax.experimental.pallas import tpu as pltpu
from jax.sharding import PartitionSpec as P

D = 768
FF = 3072
HEADS = 12
HEAD_DIM = 64
LEN = 1024
CAP = 3
STEP = 10
PIECES = 12


EPS_NORM = 1e-05
BETA_ONE = 0.9
BETA_TWO = 0.999
RATE = 0.04
VEC_RATE = 0.25
DECAY = 0.01
ADAM_EPS = 1e-08


def normalize(values_in, gain, shift):
    center = jnp.mean(values_in, axis=-1, keepdims=True)
    offset = values_in - center
    spread = jnp.mean(offset * offset, axis=-1, keepdims=True)
    return offset * lax.rsqrt(spread + EPS_NORM) * gain + shift


def adam_step(weight, grad, first, second, rate):
    first_new = BETA_ONE * first + (1.0 - BETA_ONE) * grad
    second_new = BETA_TWO * second + (1.0 - BETA_TWO) * grad * grad
    corrected = (
        first_new
        / (1.0 - BETA_ONE**STEP)
        / (jnp.sqrt(second_new / (1.0 - BETA_TWO**STEP)) + ADAM_EPS)
    )
    return (weight - rate * (corrected + DECAY * weight), first_new, second_new)


def shards_any(
    inputs,
    cotangent,
    doc_lengths,
    owner_list,
    master,
    first_moment,
    second_moment,
    vectors,
    vector_first,
    vector_second,
):
    rows_here, span, width = inputs.shape
    tokens_here = rows_here * span
    fold = FF // D
    scale = HEAD_DIM ** (-0.5)
    place = lax.axis_index("blk")
    f32 = jnp.float32
    b16 = jnp.bfloat16
    order = jnp.arange(PIECES)
    same_owner = owner_list[:, None] == owner_list[None, :]
    ranks = jnp.sum(same_owner & (order[None, :] < order[:, None]), axis=1)
    slot_of = owner_list * CAP + ranks

    mine = (owner_list == lax.axis_index("dp"))[:, None, None]
    tile_rows = lax.psum(jnp.where(mine, master[ranks], 0.0).astype(b16), "dp")
    tiles = lax.all_gather(tile_rows, "blk", axis=1, tiled=True)
    query_weight = tiles[0]
    key_weight = tiles[1]
    value_weight = tiles[2]
    out_weight = tiles[3]
    up_weight = jnp.transpose(tiles[4 : 4 + fold], (1, 0, 2)).reshape(width, FF)
    down_weight = tiles[4 + fold :].reshape(FF, width)
    flat_in = inputs.reshape(tokens_here, width).astype(f32)
    normed_one = normalize(flat_in, vectors[0], vectors[1]).astype(b16)
    queries = (jnp.dot(normed_one, query_weight, preferred_element_type=f32) + vectors[4]).astype(
        b16
    )
    keys_here = jnp.dot(normed_one, key_weight, preferred_element_type=f32).astype(b16)
    values_here = (
        jnp.dot(normed_one, value_weight, preferred_element_type=f32) + vectors[5]
    ).astype(b16)
    query_heads = queries.reshape(rows_here, span, HEADS, HEAD_DIM)
    first_len = doc_lengths[:, 0]
    query_seg = (place * span + jnp.arange(span))[None, :] >= first_len[:, None]

    def block_scores(key_block, start):
        count = key_block.shape[1]
        key_heads = key_block.reshape(rows_here, count, HEADS, HEAD_DIM)
        raw = (
            jnp.einsum("rqhd,rkhd->rhqk", query_heads, key_heads, preferred_element_type=f32)
            * scale
        )
        key_seg = (start + jnp.arange(count))[None, :] >= first_len[:, None]
        allowed = query_seg[:, None, :, None] == key_seg[:, None, None, :]
        return (raw, allowed)

    key_rows = keys_here.reshape(rows_here, span, width)
    value_rows = values_here.reshape(rows_here, span, width)
    top = jnp.full((rows_here, HEADS, span), -1e30, f32)
    key_block = lax.all_gather(key_rows, "blk", axis=1, tiled=True)
    value_block = lax.all_gather(value_rows, "blk", axis=1, tiled=True)
    count = key_block.shape[1]
    raw, allowed = block_scores(key_block, jnp.int32(0))
    new_top = jnp.maximum(top, jnp.max(jnp.where(allowed, raw, -1e30), axis=-1))
    weights = jnp.where(allowed, jnp.exp(raw - new_top[..., None]), 0.0)
    value_heads = value_block.reshape(rows_here, count, HEADS, HEAD_DIM)
    update = jnp.einsum(
        "rhqk,rkhd->rhqd", weights.astype(b16), value_heads, preferred_element_type=f32
    )
    total = jnp.sum(weights, axis=-1)
    log_total = new_top + jnp.log(total)
    context_raw = update / total[..., None]
    context_low = jnp.transpose(context_raw, (0, 2, 1, 3)).reshape(tokens_here, width).astype(b16)
    residual = flat_in + (jnp.dot(context_low, out_weight, preferred_element_type=f32) + vectors[6])
    normed_two = normalize(residual, vectors[2], vectors[3]).astype(b16)
    hidden = jnp.dot(normed_two, up_weight, preferred_element_type=f32) + vectors[8:].reshape(FF)
    gelu_exact = partial(jax.nn.gelu, approximate=False)
    active, gelu_pull = jax.vjp(gelu_exact, hidden)
    active_low = active.astype(b16)
    block_out = (
        residual + (jnp.dot(active_low, down_weight, preferred_element_type=f32) + vectors[7])
    ).reshape(rows_here, span, width)
    grad_out = cotangent.reshape(tokens_here, width)
    down_grad = jnp.einsum("tf,td->fd", active_low, grad_out, preferred_element_type=f32)
    down_sum = jnp.sum(grad_out, axis=0, dtype=f32)
    grad_active = jnp.einsum("td,fd->tf", grad_out, down_weight, preferred_element_type=f32)
    grad_hidden = gelu_pull(grad_active)[0].astype(b16)
    up_grad = jnp.einsum("td,tf->df", normed_two, grad_hidden, preferred_element_type=f32)
    up_sum = jnp.sum(grad_hidden, axis=0, dtype=f32)
    ffn_tiles = jnp.concatenate(
        [
            jnp.transpose(up_grad.reshape(width, fold, width), (1, 0, 2)),
            down_grad.reshape(fold, width, width),
        ],
        axis=0,
    )
    grad_normed_two = jnp.einsum("tf,df->td", grad_hidden, up_weight, preferred_element_type=f32)
    unused, second_pull = jax.vjp(normalize, residual, vectors[2], vectors[3])
    residual_part, gain_two_grad, shift_two_grad = second_pull(grad_normed_two)
    grad_residual = grad_out.astype(f32) + residual_part
    grad_attended = grad_residual.astype(b16)
    out_grad = jnp.einsum("tm,td->md", context_low, grad_attended, preferred_element_type=f32)
    out_sum = jnp.sum(grad_attended, axis=0, dtype=f32)
    grad_context = jnp.einsum(
        "td,md->tm", grad_attended, out_weight, preferred_element_type=f32
    ).astype(b16)
    grad_heads = grad_context.reshape(rows_here, span, HEADS, HEAD_DIM)
    delta = jnp.einsum("rqhd,rhqd->rhq", grad_heads.astype(f32), context_raw)
    key_all, value_all = (
        lax.all_gather(key_rows, "blk", axis=1, tiled=True),
        lax.all_gather(value_rows, "blk", axis=1, tiled=True),
    )
    key_size = min(512, LEN)

    def back_block(index, carry):
        grad_query, key_total, value_total = carry
        start = index * key_size
        key_block = lax.dynamic_slice_in_dim(key_all, start, key_size, 1)
        value_block = lax.dynamic_slice_in_dim(value_all, start, key_size, 1)
        raw, allowed = block_scores(key_block, start)
        weights_back = jnp.where(allowed, jnp.exp(raw - log_total[..., None]), 0.0)
        key_heads = key_block.reshape(rows_here, key_size, HEADS, HEAD_DIM)
        value_heads = value_block.reshape(rows_here, key_size, HEADS, HEAD_DIM)
        value_grad = jnp.einsum(
            "rhqk,rqhd->rkhd", weights_back.astype(b16), grad_heads, preferred_element_type=f32
        )
        weight_grad = jnp.einsum(
            "rqhd,rkhd->rhqk", grad_heads, value_heads, preferred_element_type=f32
        )
        score_grad = (weights_back * (weight_grad - delta[..., None])).astype(b16)
        grad_query = (
            grad_query
            + jnp.einsum("rhqk,rkhd->rqhd", score_grad, key_heads, preferred_element_type=f32)
            * scale
        )
        key_grad = (
            jnp.einsum("rhqk,rqhd->rkhd", score_grad, query_heads, preferred_element_type=f32)
            * scale
        )
        key_total = lax.dynamic_update_slice_in_dim(
            key_total, key_grad.reshape(rows_here, key_size, width), start, 1
        )
        value_total = lax.dynamic_update_slice_in_dim(
            value_total, value_grad.reshape(rows_here, key_size, width), start, 1
        )
        return (grad_query, key_total, value_total)

    zero_rows = jnp.zeros((rows_here, LEN, width), f32)
    grad_query, key_total, value_total = lax.fori_loop(
        0,
        LEN // key_size,
        back_block,
        (jnp.zeros((rows_here, span, HEADS, HEAD_DIM), f32), zero_rows, zero_rows),
    )
    key_grad_here, value_grad_here = (
        lax.psum_scatter(
            key_total.astype(jnp.bfloat16), "blk", scatter_dimension=1, tiled=True
        ).astype(jnp.float32),
        lax.psum_scatter(
            value_total.astype(jnp.bfloat16), "blk", scatter_dimension=1, tiled=True
        ).astype(jnp.float32),
    )
    query_low = grad_query.reshape(tokens_here, width).astype(b16)
    key_low = key_grad_here.reshape(tokens_here, width).astype(b16)
    value_low = value_grad_here.reshape(tokens_here, width).astype(b16)
    query_tile = jnp.einsum("td,te->de", normed_one, query_low, preferred_element_type=f32)
    key_tile = jnp.einsum("td,te->de", normed_one, key_low, preferred_element_type=f32)
    value_tile = jnp.einsum("td,te->de", normed_one, value_low, preferred_element_type=f32)
    grad_normed_one = (
        jnp.einsum("te,de->td", query_low, query_weight, preferred_element_type=f32)
        + jnp.einsum("te,de->td", key_low, key_weight, preferred_element_type=f32)
        + jnp.einsum("te,de->td", value_low, value_weight, preferred_element_type=f32)
    )
    unused, first_pull = jax.vjp(normalize, flat_in, vectors[0], vectors[1])
    input_part, gain_one_grad, shift_one_grad = first_pull(grad_normed_one)
    input_grad = (grad_residual + input_part).reshape(rows_here, span, width)
    vector_grads = jnp.concatenate(
        [
            jnp.stack(
                [
                    gain_one_grad,
                    shift_one_grad,
                    gain_two_grad,
                    shift_two_grad,
                    jnp.sum(query_low, axis=0, dtype=f32),
                    jnp.sum(value_low, axis=0, dtype=f32),
                    out_sum,
                    down_sum,
                ]
            ),
            up_sum.reshape(fold, width),
        ],
        axis=0,
    )
    attn_tiles = jnp.stack([query_tile, key_tile, value_tile, out_grad])
    piece_share, vector_share = (
        lax.psum_scatter(
            jnp.concatenate([attn_tiles, ffn_tiles], axis=0).astype(jnp.bfloat16),
            "blk",
            scatter_dimension=1,
            tiled=True,
        ).astype(jnp.float32),
        lax.psum_scatter(
            vector_grads.astype(jnp.bfloat16), "blk", scatter_dimension=1, tiled=True
        ).astype(jnp.float32),
    )
    own_slots = lax.axis_index("dp") * CAP + jnp.arange(CAP)
    pick = (own_slots[:, None] == slot_of[None, :]).astype(f32)
    occupied = jnp.sum(pick, axis=1)[:, None, None]
    total_share, vector_total = (
        lax.psum(piece_share.astype(jnp.bfloat16), "dp").astype(jnp.float32),
        lax.psum(vector_share.astype(jnp.bfloat16), "dp").astype(jnp.float32),
    )
    slot_grads = jnp.einsum("cp,prd->crd", pick, total_share, precision=lax.Precision.HIGHEST)
    new_master, new_first, new_second = adam_step(
        master, slot_grads, first_moment, second_moment, RATE
    )
    columns = vector_first.shape[1]
    vector_cols = lax.dynamic_slice_in_dim(vectors, place * columns, columns, 1)
    new_vectors, new_vector_first, new_vector_second = adam_step(
        vector_cols, vector_total, vector_first, vector_second, VEC_RATE
    )
    return (
        block_out,
        input_grad,
        new_master * occupied,
        new_first * occupied,
        new_second * occupied,
        new_vectors,
        new_vector_first,
        new_vector_second,
    )


f32 = jnp.float32
b16 = jnp.bfloat16
LOG2E = 1.4426950408889634
MIB = 1024 * 1024
PAIRS = HEADS // 2
PAIR = 2 * HEAD_DIM


def dot_nn(left, right):
    return lax.dot_general(left, right, (((1,), (0,)), ((), ())), preferred_element_type=f32)


def dot_nt(left, right):
    return lax.dot_general(left, right, (((1,), (1,)), ((), ())), preferred_element_type=f32)


def dot_tn(left, right):
    return lax.dot_general(left, right, (((0,), (0,)), ((), ())), preferred_element_type=f32)


def norm_parts(values_in):
    center = jnp.mean(values_in, axis=-1, keepdims=True)
    offset = values_in - center
    spread = jnp.mean(offset * offset, axis=-1, keepdims=True)
    rstd = lax.rsqrt(spread + EPS_NORM)
    return offset * rstd, rstd


def norm_back(grad, unit, rstd, gain):
    scaled = grad * gain
    first = jnp.mean(scaled, axis=-1, keepdims=True)
    second = jnp.mean(scaled * unit, axis=-1, keepdims=True)
    return rstd * (scaled - first - unit * second)


def gelu_parts(value):
    bell = jnp.exp2(value * value * (-0.5 * LOG2E))
    ratio = pl.reciprocal(1.0 + (0.3275911 * 0.7071067811865476) * jnp.abs(value))
    poly = 0.5 * 1.061405429
    poly = poly * ratio + 0.5 * -1.453152027
    poly = poly * ratio + 0.5 * 1.421413741
    poly = poly * ratio + 0.5 * -0.284496736
    poly = poly * ratio + 0.5 * 0.254829592
    tail = poly * ratio * bell
    cdf = jnp.where(value >= 0.0, 1.0 - tail, tail)
    return value * cdf, cdf + value * (bell * 0.3989422804014327)


def head_only(block, head):
    lane = lax.broadcasted_iota(jnp.int32, block.shape, 1)
    keep = (lane >= head * HEAD_DIM) & (lane < (head + 1) * HEAD_DIM)
    return jnp.where(keep, block, jnp.zeros_like(block))


def feed_kernel(
    c_ref, o_ref, x_ref, g_ref, w_ref, vec_ref,
    y_ref, r_ref, d_ref, sums_ref, tiles_ref,
    acc_ref, unit_ref, rstd_ref, normed, out_ref, grad_ref,
    hidden_ref, pulled_ref, active_ref, slope_ref, stage_ref, sem_ref,
):
    fold = FF // D
    step = pl.program_id(0)
    blocks = [slice(start, start + 16) for start in range(0, x_ref.shape[0], 16)]

    @pl.when(step == 0)
    def clear():
        acc_ref[...] = jnp.zeros_like(acc_ref)
        sums_ref[...] = jnp.zeros_like(sums_ref)

    def eights(value):
        return jnp.sum(value.reshape(-1, 8, D), axis=0)

    def add_sum(row, value):
        sums_ref[row : row + 1, :] += jnp.sum(value, 0, keepdims=True)

    out_ref[...] = dot_nn(c_ref[...], w_ref[0])
    gain = vec_ref[2:3, :]
    for rows in blocks:
        residual = x_ref[rows].astype(f32) + (out_ref[rows] + vec_ref[6:7, :])
        unit, rstd = norm_parts(residual)
        unit_ref[rows] = unit
        rstd_ref[rows] = jnp.broadcast_to(rstd, (16, 128))
        normed[rows] = (unit * gain + vec_ref[3:4, :]).astype(b16)
        out_ref[rows] = residual + vec_ref[7:8, :]
    turned = normed[...].T
    cot = g_ref[...]

    def begin(part):
        def hidden():
            hidden_ref[part % 2] = dot_nn(normed[...], w_ref[1 + part])

        def pulled():
            pulled_ref[part % 2] = dot_nt(cot, w_ref[1 + fold + part])

        return [hidden, pulled]

    def end(part):
        slot = part % 2

        def out():
            out_ref[...] += dot_nn(active_ref[slot], w_ref[1 + fold + part])

        def back():
            grad = dot_nt(slope_ref[slot], w_ref[1 + part])
            grad_ref[...] = grad if part == 0 else grad_ref[...] + grad

        def up():
            acc_ref[1 + part] += dot_nn(turned, slope_ref[slot])

        def down():
            acc_ref[1 + fold + part] += dot_tn(active_ref[slot], cot)

        return [out, back, up, down]

    for work in begin(0):
        work()
    for part in range(fold):
        slot = part % 2
        work = end(part - 1) if part > 0 else []
        work = work + (begin(part + 1) if part + 1 < fold else [])
        total = jnp.zeros((8, D), f32)
        for index, rows in enumerate(blocks):
            if index * len(work) // len(blocks) != (index - 1) * len(work) // len(blocks):
                work[index * len(work) // len(blocks)]()
            active, slope = gelu_parts(hidden_ref[slot, rows] + vec_ref[8 + part : 9 + part, :])
            active_ref[slot, rows] = active.astype(b16)
            pulled = (pulled_ref[slot, rows] * slope).astype(b16)
            slope_ref[slot, rows] = pulled
            total = total + eights(pulled.astype(f32))
        add_sum(8 + part, total)
    for work in end(fold - 1):
        work()
    y_ref[...] = out_ref[...].astype(b16)
    totals = [jnp.zeros((8, D), f32) for unused in range(4)]
    for rows in blocks:
        grad, unit, wide = grad_ref[rows], unit_ref[rows], g_ref[rows].astype(f32)
        back = wide + norm_back(grad, unit, rstd_ref[rows, 0:1], gain)
        low = back.astype(b16)
        r_ref[rows] = low
        terms = (grad * unit, grad, low.astype(f32), wide)
        totals = [total + eights(term) for total, term in zip(totals, terms)]
    for row, total in zip((2, 3, 6, 7), totals):
        add_sum(row, total)
    low = r_ref[...]
    d_ref[...] = dot_nt(w_ref[0], low).astype(b16)
    acc_ref[0] += dot_nn(o_ref[...], low)

    @pl.when(step == pl.num_programs(0) - 1)
    def send():
        count = 1 + 2 * fold
        copies = []
        for part in range(count):
            if part >= 2:
                copies[part - 2].wait()
            stage_ref[part % 2] = acc_ref[part].astype(b16)
            copy = pltpu.make_async_copy(stage_ref.at[part % 2], tiles_ref.at[part], sem_ref.at[part % 2])
            copy.start()
            copies.append(copy)
        copies[count - 2].wait()
        copies[count - 1].wait()


def feed(context, turned, x, cot, weights, vectors):
    tokens = x.shape[0]
    size = 256
    count = 1 + 2 * (FF // D)
    token_block = pl.BlockSpec((size, D), lambda i: (i, 0))
    turned_block = pl.BlockSpec((D, size), lambda i: (0, i))
    return pl.pallas_call(
        feed_kernel,
        grid=(tokens // size,),
        in_specs=[
            token_block,
            turned_block,
            token_block,
            token_block,
            pl.BlockSpec((count, D, D), lambda i: (0, 0, 0), pipeline_mode=pl.Buffered(1)),
            pl.BlockSpec((PIECES, D), lambda i: (0, 0)),
        ],
        out_specs=[
            token_block,
            token_block,
            turned_block,
            pl.BlockSpec((16, D), lambda i: (0, 0)),
            pl.BlockSpec(memory_space=pl.ANY),
        ],
        out_shape=[
            jax.ShapeDtypeStruct((tokens, D), b16),
            jax.ShapeDtypeStruct((tokens, D), b16),
            jax.ShapeDtypeStruct((D, tokens), b16),
            jax.ShapeDtypeStruct((16, D), f32),
            jax.ShapeDtypeStruct((count, D, D), b16),
        ],
        scratch_shapes=[
            pltpu.VMEM((count, D, D), f32),
            pltpu.VMEM((size, D), f32),
            pltpu.VMEM((size, 128), f32),
            pltpu.VMEM((size, D), b16),
            pltpu.VMEM((size, D), f32),
            pltpu.VMEM((size, D), f32),
            pltpu.VMEM((2, size, D), f32),
            pltpu.VMEM((2, size, D), f32),
            pltpu.VMEM((2, size, D), b16),
            pltpu.VMEM((2, size, D), b16),
            pltpu.VMEM((2, D, D), b16),
            pltpu.SemaphoreType.DMA((2,)),
        ],
        compiler_params=pltpu.CompilerParams(vmem_limit_bytes=60 * MIB),
        cost_estimate=pl.CostEstimate(
            flops=6 * count * tokens * D * D,
            bytes_accessed=18 * tokens * D + 4 * count * D * D,
            transcendentals=2 * tokens * FF,
        ),
        name="feed",
    )(context, turned, x, cot, weights, vectors)


MESH = pl.DeviceIdType.MESH
HALF = D // 2
FLOWS = 2
FLOW = HALF // FLOWS
NEAR = FLOW // 2
KEEP = NEAR // 2
WIDE = 3 * PAIR
REST = PIECES - 3
GROUPS = ((0, 1), (1, 2), (3, 3))
CHUNKS = len(GROUPS)


class Place:
    def __init__(self):
        self.me = lax.axis_index("dp")
        self.core = lax.axis_index("blk")
        self.bits = [lax.rem(self.me // weight, 2) for weight in (1, 2, 4, 8)]
        self.chips = [
            self.me + weight - 2 * weight * bit for weight, bit in zip((1, 2, 4, 8), self.bits)
        ]
        self.partners = [{"dp": chip} for chip in self.chips]
        low, high = self.bits[2:]
        self.inner = low != high
        self.across = {"dp": self.me + 4 - 8 * low + 8 - 16 * high}
        self.other = 1 - self.core
        self.twin = {"blk": self.other}

    def greet(self):
        barrier = pltpu.get_barrier_semaphore()
        for device in self.partners + [self.across, self.twin]:
            pl.semaphore_signal(barrier, 1, device_id=device, device_id_type=MESH)
        pl.semaphore_wait(barrier, 6)

    def flow(self, index):
        first, second = (0, 1) if index == 0 else (1, 0)
        base = index * FLOW
        near = base + self.bits[first] * NEAR
        far = base + NEAR - self.bits[first] * NEAR
        keep = near + self.bits[second] * KEEP
        give = near + KEEP - self.bits[second] * KEEP
        return first, second, near, far, keep, give


def remote(source, target, send, receive, device):
    return pltpu.make_async_remote_copy(
        src_ref=source,
        dst_ref=target,
        send_sem=send,
        recv_sem=receive,
        device_id=device,
        device_id_type=MESH,
    )


def rows_at(start, count):
    return pl.ds(pl.multiple_of(start, 16), count)


class Spread:
    def __init__(self, place, owner, rank, slots, land, gift, sems):
        self.place, self.owner, self.rank = place, owner, rank
        self.slots, self.land, self.gift, self.sems = slots, land, gift, sems

    def cols(self, chunk):
        return pl.ds(GROUPS[chunk][0] * PAIR, GROUPS[chunk][1] * PAIR)

    def first_copy(self, chunk, index):
        first, second, near, far, keep, give = self.place.flow(index)
        return remote(
            self.slots.at[:, rows_at(far, NEAR), self.cols(chunk)],
            self.land[chunk].at[index],
            self.sems[0].at[chunk, index, 0],
            self.sems[1].at[chunk, index, 0],
            self.place.partners[first],
        )

    def second_copy(self, chunk, index, which):
        first, second, near, far, keep, give = self.place.flow(index)
        if which == 0:
            source = self.slots.at[:, rows_at(give, KEEP), self.cols(chunk)]
        else:
            source = self.land[chunk].at[index, :, rows_at(give - near, KEEP)]
        return remote(
            source,
            self.gift[chunk].at[index, pl.ds(which * CAP, CAP)],
            self.sems[0].at[chunk, index, 1 + which],
            self.sems[1].at[chunk, index, 1 + which],
            self.place.partners[second],
        )

    def step(self, chunk, index):
        for flow in range(FLOWS):
            if index == 0:
                self.first_copy(chunk, flow).start()
                self.second_copy(chunk, flow, 0).start()
            if index == 1:
                self.first_copy(chunk, flow).wait()
                self.second_copy(chunk, flow, 1).start()
            if index == 2:
                self.second_copy(chunk, flow, 0).wait()
                self.second_copy(chunk, flow, 1).wait()

    def piece(self, tile, index, chunk, start, count):
        first, second, near, far, keep, give = self.place.flow(index)
        owner, rank = self.owner[tile], self.rank[tile]
        bits = [lax.rem(owner, 2), lax.rem(owner // 2, 2)]
        apart = [bit != mine for bit, mine in zip(bits, self.place.bits)]
        cols = pl.ds(start, count)
        mine = self.slots[rank, rows_at(keep, KEEP), pl.ds(GROUPS[chunk][0] * PAIR + start, count)]
        firsts = self.land[chunk][index, rank, rows_at(keep - near, KEEP), cols]
        gifts = self.gift[chunk][index, jnp.where(apart[first], CAP, 0) + rank, :, cols]
        value = jnp.where(apart[second], gifts, jnp.where(apart[first], firsts, mine))
        layer = owner // 4 == self.place.me // 4
        return jnp.where(layer, value, jnp.zeros_like(value))


class Column:
    steps = 4

    def __init__(self, place, kept, read, write, land, sems):
        self.place, self.kept, self.read, self.write = place, kept, read, write
        self.land, self.sems = land, sems

    def copy(self, index):
        target = self.land.at[index % 2]
        device = self.place.across if index == 1 else self.place.partners[2]
        return remote(
            self.kept, target, self.sems[0].at[index], self.sems[1].at[index], device
        )

    def add(self, index):
        self.write((self.read().astype(f32) + self.land[index].astype(f32)).astype(b16))


def column_step(place, columns, index):
    @pl.when(place.inner)
    def inner():
        for column in columns:
            if index == 1:
                column.copy(0).wait_recv()
                column.add(0)
                column.copy(1).start()
            if index == 2:
                column.copy(1).wait()
                column.add(1)
                column.copy(2).start()
            if index == 3:
                column.copy(2).wait_send()

    @pl.when(jnp.logical_not(place.inner))
    def outer():
        for column in columns:
            if index == 0:
                column.copy(0).start()
            if index == 1:
                column.copy(0).wait_send()
            if index == 3:
                column.copy(2).wait_recv()
                column.write(column.land[0])


class Item:
    steps = 7

    def __init__(self, place, work, land, sems, load, store=None):
        self.place, self.work, self.land, self.sems = place, work, land, sems
        self.load, self.store = load, store
        self.base = place.core * HALF

    def column(self, flow):
        rows = rows_at(self.base + self.place.flow(flow)[4], KEEP)

        def read():
            return self.work[:, rows]

        def write(value):
            self.work[:, rows] = value

        sems = (self.sems[0].at[flow], self.sems[1].at[flow])
        return Column(self.place, self.work.at[:, rows], read, write, self.land.at[flow], sems)

    def copy(self, flow, index):
        first, second, near, far, keep, give = self.place.flow(flow)
        kept = self.work.at[:, rows_at(self.base + keep, KEEP)]
        half = self.work.at[:, rows_at(self.base + near, NEAR)]
        source, device = [
            (kept, self.place.partners[second]),
            (half, self.place.partners[first]),
        ][index]
        return remote(
            source, source, self.sems[0].at[flow, 3 + index], self.sems[1].at[flow, 3 + index], device
        )

    def pair(self):
        rows = self.work.at[:, rows_at(self.base, HALF)]
        return remote(rows, rows, self.sems[0].at[0, 5], self.sems[1].at[0, 5], self.place.twin)

    def step(self, index):
        for flow in range(FLOWS):
            if index == 0:
                self.load(self.work, rows_at(self.base + self.place.flow(flow)[4], KEEP), flow)
        if index <= 3:
            column_step(self.place, [self.column(flow) for flow in range(FLOWS)], index)
        for flow in range(FLOWS):
            if 4 <= index <= 5:
                self.copy(flow, index - 4).wait()
            if 3 <= index <= 4:
                self.copy(flow, index - 3).start()
        if index == 5:
            self.pair().start()
        if index == 6:
            self.pair().wait()
            self.store().start()


REST_GROUPS = tuple((index, 1) for index in range(REST))
PAIR_CHUNK = (0, 1, 1, 2, 2, 2)
FRONT_PAIRS = (2, 4, 5, 6, 7, 8)
FRONT_REST = (6, 7, 8, 9, 10, 11, 12, 13, 14)
FRONT_LEAD = 9


def front_kernel(
    owner, lengths, master, vec_ref, x_in, c_in,
    x_out, c_out, n_out, one_out, two_out, q_ref, k_ref, v_ref, p_ref, r_ref, o_ref, ctx_ref,
    rank, rows_ref, normed, keys, turned_values, scores, slots,
    land_one, land_two, land_three, gift_one, gift_two, gift_three,
    one, one_land, two, two_land,
    spread_send, spread_recv, one_send, one_recv, two_send, two_recv,
    swap_send, swap_recv, swap_local, store_sem,
):
    pair = pl.program_id(0)
    row = pl.program_id(1)
    grid_step = pair * 2 + row
    place = Place()
    rows, span = x_in.shape[0] // 2, x_in.shape[1]
    land = (land_one, land_two, land_three)
    gift = (gift_one, gift_two, gift_three)
    spread = Spread(place, owner, rank, slots, land, gift, (spread_send, spread_recv))

    def swaps(index):
        source, target = [(x_in, rows_ref), (c_in, c_out)][index]
        here = pl.ds(place.core * span, span)
        near = pltpu.make_async_copy(
            source.at[pl.ds(place.core * rows, rows)], target.at[:, here], swap_local.at[index]
        )
        far = remote(
            source.at[pl.ds(place.other * rows, rows)],
            target.at[:, here],
            swap_send.at[index],
            swap_recv.at[index],
            place.twin,
        )
        return near, far

    def row_store():
        return pltpu.make_async_copy(rows_ref, x_out, store_sem.at[PAIRS + REST])

    def normed_store():
        return pltpu.make_async_copy(normed, n_out, store_sem.at[PAIRS + REST + 1])

    def pair_item(group):
        span_of = pl.ds(group, 1)

        def load(work, where, flow):
            chunk = PAIR_CHUNK[group]
            for tile in range(3):
                part = spread.piece(tile, flow, chunk, (group - GROUPS[chunk][0]) * PAIR, PAIR)
                work[0, where, pl.ds(tile * PAIR, PAIR)] = part

        def store():
            return pltpu.make_async_copy(one.at[span_of], one_out.at[span_of], store_sem.at[group])

        sems = (one_send.at[group], one_recv.at[group])
        return Item(place, one.at[span_of], one_land.at[:, :, span_of], sems, load, store)

    def rest_item(group):
        first, count = REST_GROUPS[group]
        span_of = pl.ds(first, count)

        def load(work, where, flow):
            for index in range(count):
                for chunk, (start, wide) in enumerate(GROUPS):
                    part = spread.piece(3 + first + index, flow, chunk, 0, wide * PAIR)
                    work[index, where, pl.ds(start * PAIR, wide * PAIR)] = part

        def store():
            return pltpu.make_async_copy(
                two.at[span_of], two_out.at[span_of], store_sem.at[PAIRS + group]
            )

        sems = (two_send.at[group], two_recv.at[group])
        return Item(place, two.at[span_of], two_land.at[:, :, span_of], sems, load, store)

    def tick(number, odd):
        for chunk in range(CHUNKS):
            if odd == 0 and 0 <= number - 2 * chunk <= 2:
                spread.step(chunk, number - 2 * chunk)
        starts = [(pair_item, group, start) for group, start in enumerate(FRONT_PAIRS)]
        starts += [(rest_item, group, start) for group, start in enumerate(FRONT_REST)]
        for make, group, start in starts:
            if group % 2 == odd and 0 <= number - start < Item.steps:
                make(group).step(number - start)

    def both(number):
        tick(number, 0)
        tick(number, 1)

    @pl.when(grid_step == 0)
    def lead():
        slots[...] = master[...].astype(b16)
        for tile in range(PIECES):
            count = jnp.int32(0)
            for before in range(tile):
                count = count + (owner[before] == owner[tile]).astype(jnp.int32)
            rank[tile] = jnp.minimum(count, CAP - 1)
        place.greet()
        for copy in swaps(0):
            copy.start()
        both(0)
        for copy in swaps(1):
            copy.start()
        for copy in swaps(0):
            copy.wait()
        row_store().start()

        def norm_rows(index, carry):
            for part in range(rows):
                for block in range(4):
                    where = pl.ds(pl.multiple_of(index * 128 + block * 32, 32), 32)
                    unit, unused = norm_parts(rows_ref[part, where].astype(f32))
                    low = (unit * vec_ref[0:1, :] + vec_ref[1:2, :]).astype(b16)
                    normed[pl.ds(pl.multiple_of(part * LEN + index * 128 + block * 32, 32), 32)] = low
            return carry

        both(1)
        lax.fori_loop(0, LEN // 128, norm_rows, 0)
        normed_store().start()
        for number in range(2, FRONT_LEAD):
            both(number)

    for number in range(2 * PAIRS):
        pl.when(grid_step == number)(partial(tick, FRONT_LEAD + number, 0))

    @pl.when(row == 0)
    def project():
        lanes = pl.ds(pl.multiple_of(pair * PAIR, PAIR), PAIR)
        weight = one[pair]

        def part(index, carry):
            where = pl.ds(pl.multiple_of(index * 512, 512), 512)
            both = dot_nn(normed[where], weight)
            queries = both[:, :PAIR] + vec_ref[4:5, lanes]
            queries = (queries * (HEAD_DIM**-0.5 * LOG2E)).astype(b16)
            q_ref[:, where] = queries.T
            low = both[:, PAIR : 2 * PAIR].astype(b16)
            keys[where] = low
            k_ref[:, where] = low.T
            values = (both[:, 2 * PAIR :] + vec_ref[5:6, lanes]).astype(b16)
            v_ref[where] = values
            turned_values[:, where] = values.T
            return carry

        lax.fori_loop(0, normed.shape[0] // 512, part, 0)

    half = LEN // 2
    start = pl.multiple_of(row * LEN, LEN)
    split = lengths[place.core * rows + row, 0] < LEN
    shift = jnp.where(split, jnp.float32(-1e30), jnp.float32(0.0))

    quarter = LEN // 4
    units = [(head, step) for head in range(2) for step in range(2)]

    def score_block(unit, block, peak):
        head, step = units[unit]
        rows_here = pl.ds(pl.multiple_of(start + block * quarter, quarter), quarter)
        queries = q_ref[:, pl.ds(pl.multiple_of(start + step * half, half), half)]
        raw = dot_nn(head_only(keys[rows_here], head), queries)
        if block // 2 != step:
            raw = raw + shift
        scores[unit % 2, block * quarter : (block + 1) * quarter] = raw
        best = jnp.max(raw.reshape(-1, 8, half), axis=0)
        return best if peak is None else jnp.maximum(peak, best)

    def context_block(unit, block, total):
        head, step = units[unit]
        part = slice(head * HEAD_DIM, (head + 1) * HEAD_DIM)
        cols = pl.ds(pl.multiple_of(start + block * quarter, quarter), quarter)
        here = slice(step * half, (step + 1) * half)
        term = dot_nn(
            turned_values[part, cols], p_ref[head, block * quarter : (block + 1) * quarter, here]
        )
        return term if total is None else total + term

    def context_store(unit, total, recip):
        head, step = units[unit]
        part = slice(head * HEAD_DIM, (head + 1) * HEAD_DIM)
        o_ref[part, step * half : (step + 1) * half] = (total * recip).astype(b16)

    peak = None
    for block in range(4):
        peak = score_block(0, block, peak)
    before = None
    for unit, (head, step) in enumerate(units):
        if unit == 2:
            for number in range(2 * PAIRS):
                pl.when(grid_step == number)(partial(tick, FRONT_LEAD + number, 1))
        here = slice(step * half, (step + 1) * half)
        top = jnp.max(peak, 0, keepdims=True)
        total = jnp.zeros((8, half), f32)
        peak, context = None, None
        for block in range(4):
            if unit + 1 < len(units):
                peak = score_block(unit + 1, block, peak)
            for small in range(4 * block, 4 * block + 4):
                rows_here = slice(small * 64, (small + 1) * 64)
                value = jnp.exp2(scores[unit % 2, rows_here] - top)
                total = total + jnp.sum(value.reshape(-1, 8, half), axis=0)
                p_ref[head, rows_here, here] = value.astype(b16)
            if unit > 0:
                context = context_block(unit - 1, block, context)
        if unit > 0:
            context_store(unit - 1, context, before)
        before = 1.0 / jnp.sum(total, 0, keepdims=True)
        r_ref[0, head : head + 1, here] = before
    context = None
    for block in range(4):
        context = context_block(3, block, context)
    context_store(3, context, before)
    ctx_ref[...] = o_ref[...].T

    @pl.when(grid_step == 2 * PAIRS - 1)
    def finish_copies():
        for copy in swaps(1):
            copy.wait()
        row_store().wait()
        normed_store().wait()
        for group in range(PAIRS):
            pair_item(group).store().wait()
        for group in range(REST):
            rest_item(group).store().wait()


def front(owner, lengths, master, vectors, inputs, cotangent):
    rows, span = inputs.shape[0] // 2, inputs.shape[1]
    tokens = rows * LEN
    any_spec = pl.BlockSpec(memory_space=pl.ANY)
    smem = pl.BlockSpec(memory_space=pltpu.SMEM)
    whole = jax.ShapeDtypeStruct((rows, LEN, D), b16)
    dma = pltpu.SemaphoreType.DMA
    return pl.pallas_call(
        front_kernel,
        grid=(PAIRS, rows),
        in_specs=[
            smem,
            smem,
            pl.BlockSpec((CAP, HALF, D), lambda h, r: (0, 0, 0), pipeline_mode=pl.Buffered(1)),
            pl.BlockSpec((PIECES, D), lambda h, r: (0, 0)),
            any_spec,
            any_spec,
        ],
        out_specs=[any_spec] * 5
        + [
            pl.BlockSpec((PAIR, tokens), lambda h, r: (h, 0)),
            pl.BlockSpec((PAIR, tokens), lambda h, r: (h, 0)),
            pl.BlockSpec((tokens, PAIR), lambda h, r: (0, h)),
            pl.BlockSpec((2, LEN, LEN), lambda h, r: (h * 2 + r, 0, 0)),
            pl.BlockSpec((1, 2, LEN), lambda h, r: (h * 2 + r, 0, 0)),
            pl.BlockSpec((PAIR, LEN), lambda h, r: (h, r)),
            pl.BlockSpec((LEN, PAIR), lambda h, r: (r, h)),
        ],
        out_shape=[
            whole,
            whole,
            jax.ShapeDtypeStruct((tokens, D), b16),
            jax.ShapeDtypeStruct((PAIRS, D, WIDE), b16),
            jax.ShapeDtypeStruct((REST, D, D), b16),
            jax.ShapeDtypeStruct((D, tokens), b16),
            jax.ShapeDtypeStruct((D, tokens), b16),
            jax.ShapeDtypeStruct((tokens, D), b16),
            jax.ShapeDtypeStruct((rows * HEADS, LEN, LEN), b16),
            jax.ShapeDtypeStruct((rows * PAIRS, 2, LEN), f32),
            jax.ShapeDtypeStruct((D, tokens), b16),
            jax.ShapeDtypeStruct((tokens, D), b16),
        ],
        scratch_shapes=[
            pltpu.SMEM((PIECES,), jnp.int32),
            pltpu.VMEM((rows, LEN, D), b16),
            pltpu.VMEM((tokens, D), b16),
            pltpu.VMEM((tokens, PAIR), b16),
            pltpu.VMEM((PAIR, tokens), b16),
            pltpu.VMEM((2, LEN, LEN // 2), f32),
            pltpu.VMEM((CAP, HALF, D), b16),
        ]
        + [pltpu.VMEM((FLOWS, CAP, NEAR, wide * PAIR), b16) for unused, wide in GROUPS]
        + [pltpu.VMEM((FLOWS, 2 * CAP, KEEP, wide * PAIR), b16) for unused, wide in GROUPS]
        + [
            pltpu.VMEM((PAIRS, D, WIDE), b16),
            pltpu.VMEM((FLOWS, 2, PAIRS, KEEP, WIDE), b16),
            pltpu.VMEM((REST, D, D), b16),
            pltpu.VMEM((FLOWS, 2, REST, KEEP, D), b16),
            dma((CHUNKS, FLOWS, 3)),
            dma((CHUNKS, FLOWS, 3)),
            dma((PAIRS, FLOWS, 6)),
            dma((PAIRS, FLOWS, 6)),
            dma((REST, FLOWS, 6)),
            dma((REST, FLOWS, 6)),
            dma((2,)),
            dma((2,)),
            dma((2,)),
            dma((PAIRS + REST + 2,)),
        ],
        compiler_params=pltpu.CompilerParams(
            collective_id=0, has_side_effects=True, vmem_limit_bytes=60 * MIB
        ),
        name="front",
    )(owner, lengths, master, vectors, inputs, cotangent)


class Sum:
    steps = 7

    def __init__(self, place, work, wide, narrow, sems, send_pair, add_own):
        self.place, self.work, self.wide, self.narrow, self.sems = place, work, wide, narrow, sems
        self.send_pair, self.add_own = send_pair, add_own

    def column(self, flow):
        rows = rows_at(self.place.flow(flow)[4], KEEP)

        def read():
            return self.work[:, rows]

        def write(value):
            self.work[:, rows] = value

        sems = (self.sems[0].at[flow, pl.ds(2, 3)], self.sems[1].at[flow, pl.ds(2, 3)])
        land = self.narrow.at[flow, pl.ds(1, 2)]
        return Column(self.place, self.work.at[:, rows], read, write, land, sems)

    def copy(self, flow, index):
        first, second, near, far, keep, give = self.place.flow(flow)
        source, target, device = [
            (self.work.at[:, rows_at(far, NEAR)], self.wide.at[flow], first),
            (self.work.at[:, rows_at(give, KEEP)], self.narrow.at[flow, 0], second),
        ][index]
        return remote(
            source,
            target,
            self.sems[0].at[flow, index],
            self.sems[1].at[flow, index],
            self.place.partners[device],
        )

    def add(self, rows, value):
        self.work[:, rows] = (self.work[:, rows].astype(f32) + value.astype(f32)).astype(b16)

    def step(self, index):
        if index == 0:
            self.send_pair().start()
        if index == 1:
            self.send_pair().wait()
            self.add_own()
        for flow in range(FLOWS):
            first, second, near, far, keep, give = self.place.flow(flow)
            if index == 1:
                self.copy(flow, 0).start()
            if index == 2:
                self.copy(flow, 0).wait()
                self.add(rows_at(near, NEAR), self.wide[flow])
                self.copy(flow, 1).start()
            if index == 3:
                self.copy(flow, 1).wait()
                self.add(rows_at(keep, KEEP), self.narrow[flow, 0])
        if index >= 3:
            columns = [self.column(flow) for flow in range(FLOWS)]
            column_step(self.place, columns, index - 3)


class Gather:
    steps = 3

    def __init__(self, place, work, narrow, wide, sems):
        self.place, self.work, self.narrow, self.wide = place, work, narrow, wide
        self.sems = sems

    def copy(self, flow, index):
        first, second, near, far, keep, give = self.place.flow(flow)
        rows, target, device = [
            (rows_at(keep, KEEP), self.narrow, second),
            (rows_at(near, NEAR), self.wide, first),
        ][index]
        return remote(
            self.work.at[:, rows],
            target.at[flow],
            self.sems[0].at[flow, 5 + index],
            self.sems[1].at[flow, 5 + index],
            self.place.partners[device],
        )

    def step(self, index):
        for flow in range(FLOWS):
            first, second, near, far, keep, give = self.place.flow(flow)
            if index > 0:
                self.copy(flow, index - 1).wait()
            if index == 1:
                self.work[:, rows_at(give, KEEP)] = self.narrow[flow]
            if index == 2:
                self.work[:, rows_at(far, NEAR)] = self.wide[flow]
            if index < 2:
                self.copy(flow, index).start()


class Hand:
    steps = 3

    def __init__(self, place, table, work, bag, gift, pack, last, own, out, sems, store_sems):
        self.place, self.table, self.work = place, table, work
        self.bag, self.gift, self.pack, self.last, self.own = bag, gift, pack, last, own
        self.out, self.sems, self.store_sems = out, sems, store_sems

    def tile(self, chip, rank, rows):
        return self.work[self.table[chip * CAP + rank], rows]

    def copy(self, flow, index):
        first, second = self.place.flow(flow)[:2]
        source, target, device = [
            (self.bag.at[flow], self.gift.at[flow], second),
            (self.pack.at[flow], self.last.at[flow], first),
        ][index]
        return remote(
            source,
            target,
            self.sems[0].at[flow, index],
            self.sems[1].at[flow, index],
            self.place.partners[device],
        )

    def stores(self, flow):
        first, second, near, far, keep, give = self.place.flow(flow)
        parts = [
            (self.own.at[flow], rows_at(keep, KEEP)),
            (self.gift.at[flow, pl.ds(0, CAP)], rows_at(give, KEEP)),
            (self.last.at[flow], rows_at(far, NEAR)),
        ]
        return [
            pltpu.make_async_copy(source, self.out.at[:, rows], self.store_sems.at[flow, index])
            for index, (source, rows) in enumerate(parts)
        ]

    def step(self, index):
        for flow in range(FLOWS):
            first, second, near, far, keep, give = self.place.flow(flow)
            rows = rows_at(keep, KEEP)
            if index == 0:
                beside = self.place.chips[second]
                across = beside + self.place.chips[first] - self.place.me
                for rank in range(CAP):
                    self.bag[flow, rank] = self.tile(beside, rank, rows)
                    self.bag[flow, CAP + rank] = self.tile(across, rank, rows)
                    self.own[flow, rank] = self.tile(self.place.me, rank, rows)
                self.copy(flow, 0).start()
            if index == 1:
                self.copy(flow, 0).wait()
                for rank in range(CAP):
                    mine = self.tile(self.place.chips[first], rank, rows)
                    self.pack[flow, rank, rows_at(keep - near, KEEP)] = mine
                    self.pack[flow, rank, rows_at(give - near, KEEP)] = self.gift[flow, CAP + rank]
                self.copy(flow, 1).start()
            if index == 2:
                self.copy(flow, 1).wait()
                for copy in self.stores(flow):
                    copy.start()


BACK_STEPS = 2 * PAIRS
BACK_TAIL = 4
BACK_PAIRS = tuple((index, 1) for index in range(PAIRS))
BACK_REST = (0, 0, 1, 2, 2, 3, 4, 4, 5)
BACK_HAND = 12


def back_kernel(
    table, p_ref, r_ref, v_ref, q_ref, k_ref, o_ref, g_ref, w_ref, n_ref, x_ref, z_ref, vec_ref,
    tiles_in, sums_in, y_in,
    y_out, i_out, pairs_out, slots_out, sums_ref,
    grad_sum, wide_sum, turned, slopes, block_out,
    two, two_wide, two_narrow, two_stage, one, one_wide, one_narrow, one_send_stage, one_stage,
    gather_narrow, gather_wide,
    bag, gift, pack, last, own, vec_land,
    two_send, two_recv, one_send, one_recv, hand_send, hand_recv, hand_store,
    pair_two_send, pair_two_recv, pair_one_send, pair_one_recv, load_sem, store_sem,
    swap_send, swap_recv, swap_local, vec_send, vec_recv,
):
    step = pl.program_id(0)
    place = Place()
    rows, span = y_in.shape[0], y_in.shape[1] // 2
    near_half = rows_at(place.core * HALF, HALF)
    far_half = rows_at(place.other * HALF, HALF)

    def load_two(group):
        first, count = REST_GROUPS[group]
        return pltpu.make_async_copy(
            tiles_in.at[pl.ds(first, count), near_half],
            two_stage.at[pl.ds(group % 3, 1)],
            load_sem.at[group % 3],
        )

    def rest_sum(group):
        first, count = REST_GROUPS[group]
        span_of = pl.ds(first, count)
        work = two.at[span_of]

        def send_pair():
            return remote(
                tiles_in.at[span_of, far_half],
                work,
                pair_two_send.at[group],
                pair_two_recv.at[group],
                place.twin,
            )

        def add_own():
            load_two(group).wait()
            work[...] = (work[...].astype(f32) + two_stage[group % 3].astype(f32)).astype(b16)

        sems = (two_send.at[group], two_recv.at[group])
        wide, narrow = two_wide.at[:, span_of], two_narrow.at[:, :, span_of]
        return Sum(place, work, wide, narrow, sems, send_pair, add_own)

    def pair_sum(group):
        first, count = BACK_PAIRS[group]
        span_of = pl.ds(first, count)
        work = one.at[span_of]

        def send_pair():
            return remote(
                one_send_stage.at[pl.ds(group % 2, 1)],
                work,
                pair_one_send.at[group],
                pair_one_recv.at[group],
                place.twin,
            )

        def add_own():
            own = one_stage[group % 2].astype(f32)
            work[...] = (work[...].astype(f32) + own).astype(b16)

        sems = (one_send.at[group], one_recv.at[group])
        wide, narrow = one_wide.at[:, span_of], one_narrow.at[:, :, span_of]
        return Sum(place, work, wide, narrow, sems, send_pair, add_own)

    def pair_gather(group):
        first, count = BACK_PAIRS[group]
        span_of = pl.ds(first, count)
        sems = (one_send.at[group], one_recv.at[group])
        narrow, wide = gather_narrow.at[:, span_of], gather_wide.at[:, span_of]
        return Gather(place, one.at[span_of], narrow, wide, sems)

    hand = Hand(
        place, table, two, bag, gift, pack, last, own, slots_out, (hand_send, hand_recv), hand_store
    )

    def pair_store(index, tile):
        return pltpu.make_async_copy(
            one.at[index, :, pl.ds(tile * PAIR, PAIR)],
            pairs_out.at[tile, :, pl.ds(index * PAIR, PAIR)],
            store_sem.at[index, tile],
        )

    def tick(number, odd):
        for group, start in enumerate(BACK_REST):
            if group % 2 == odd and 0 <= number - start < Sum.steps:
                rest_sum(group).step(number - start)
        for group, (first, count) in enumerate(BACK_PAIRS):
            if group % 2 != odd:
                continue
            start = 2 * (first + count)
            if 0 <= number - start < Sum.steps:
                pair_sum(group).step(number - start)
            if 0 <= number - start - Sum.steps + 1 < Gather.steps:
                pair_gather(group).step(number - start - Sum.steps + 1)
            if number == start + Sum.steps + 1:
                for index in range(first, first + count):
                    for tile in range(3):
                        pair_store(index, tile).start()
        if odd == 0 and 0 <= number - BACK_HAND < Hand.steps:
            hand.step(number - BACK_HAND)
        for group, start in enumerate(BACK_REST):
            if odd == 1 and number == max(start - 1, 0):
                load_two(group).start()

    def both(number):
        tick(number, 0)
        tick(number, 1)

    def swap_y(index):
        there = pl.ds(place.core * rows, rows)
        if index == 0:
            return pltpu.make_async_copy(
                y_in.at[:, pl.ds(place.core * span, span)], y_out.at[there], swap_local.at[0]
            )
        return remote(
            y_in.at[:, pl.ds(place.other * span, span)],
            y_out.at[there],
            swap_send.at[0],
            swap_recv.at[0],
            place.twin,
        )

    @pl.when(step == 0)
    def lead():
        place.greet()
        for index in range(2):
            swap_y(index).start()
        sums_ref[...] = sums_in[...]

    for number in range(BACK_STEPS + BACK_TAIL):
        early = partial(tick, number, 0) if number < BACK_STEPS else partial(both, number)
        pl.when(step == number)(early)

    half = LEN // 2
    pair, row = step // 2, lax.rem(step, 2)

    quarter = LEN // 4

    def attention_inputs(head):
        part = slice(head * HEAD_DIM, (head + 1) * HEAD_DIM)
        values = head_only(v_ref[...], head)
        recip = r_ref[0, head : head + 1, :]
        grad = g_ref[part, :].astype(f32) * recip
        delta = jnp.sum(grad * o_ref[part, :].astype(f32), 0, keepdims=True)
        grad = grad.astype(b16)
        return values, grad, delta, jnp.concatenate([grad, grad], axis=0)

    def attention(head):
        part = slice(head * HEAD_DIM, (head + 1) * HEAD_DIM)
        values, grad, delta, doubled = attention_inputs(head)
        units = [(which, block) for which in range(2) for block in range(4)]
        value_grad, key_grad, query_grad = {}, {}, {}

        def raw_block(unit):
            which, block = units[unit]
            cols = slice(which * half, (which + 1) * half)
            return dot_nn(values[block * quarter : (block + 1) * quarter], doubled[:, cols])

        def slope_block(unit, raw):
            which, block = units[unit]
            cols = slice(which * half, (which + 1) * half)
            for small in range(4):
                rows_here = slice(small * 64, (small + 1) * 64)
                rows_all = slice(block * quarter + small * 64, block * quarter + (small + 1) * 64)
                slope = p_ref[head, rows_all, cols].astype(f32) * (raw[rows_here] - delta[:, cols])
                slopes[unit % 2, rows_here] = slope.astype(b16)

        def add(totals, key, term):
            totals[key] = totals[key] + term if key in totals else term

        def grad_block(unit):
            which, block = units[unit]
            cols = slice(which * half, (which + 1) * half)
            rows_all = slice(block * quarter, (block + 1) * quarter)
            slope = slopes[unit % 2]
            add(value_grad, block, dot_nt(grad[:, cols], p_ref[head, rows_all, cols]))
            add(key_grad, block, dot_nt(q_ref[part, cols], slope))
            add(query_grad, which, dot_nn(k_ref[part, rows_all], slope))

        raw = raw_block(0)
        for unit in range(len(units)):
            after = raw_block(unit + 1) if unit + 1 < len(units) else None
            slope_block(unit, raw)
            if unit > 0:
                grad_block(unit - 1)
            raw = after
        grad_block(len(units) - 1)
        for which in range(2):
            total = query_grad[which] * (HEAD_DIM**-0.5)
            turned[part, which * half : (which + 1) * half] = total.astype(b16)
        for block in range(4):
            rows_all = slice(block * quarter, (block + 1) * quarter)
            lower = slice(PAIR + head * HEAD_DIM, PAIR + (head + 1) * HEAD_DIM)
            turned[lower, rows_all] = (key_grad[block] * (1.0 / LOG2E)).astype(b16)
            lower = slice(2 * PAIR + head * HEAD_DIM, 2 * PAIR + (head + 1) * HEAD_DIM)
            turned[lower, rows_all] = value_grad[block].astype(b16)

    @pl.when(step < BACK_STEPS)
    def first_head():
        attention(0)

    for number in range(BACK_STEPS):
        pl.when(step == number)(partial(tick, number, 1))

    @pl.when(step < BACK_STEPS)
    def second_head():
        attention(1)
        where = pl.ds(pl.multiple_of(row * LEN, LEN), LEN)
        block = dot_nn(turned[...], n_ref[where])
        back = turned[...].T
        lanes = pl.ds(pl.multiple_of(pair * PAIR, PAIR), PAIR)
        ones = jnp.sum(back.astype(f32), 0, keepdims=True)
        sums_ref[4:5, lanes] += ones[:, :PAIR]
        sums_ref[5:6, lanes] += ones[:, 2 * PAIR :]
        term = dot_nt(back, w_ref[0])

        @pl.when(pair == 0)
        def begin():
            grad_sum[where] = term

        @pl.when(pair > 0)
        def add():
            grad_sum[where] += term

        @pl.when(row == 0)
        def keep():
            wide_sum[...] = block

        @pl.when(row == 1)
        def hand_on():
            whole = (wide_sum[...] + block).T
            low = whole.astype(b16)
            for core in range(2):

                @pl.when(place.core == core)
                def split():
                    slot = lax.rem(pair, 2)
                    one_stage[slot] = low[core * HALF : (core + 1) * HALF]
                    one_send_stage[slot] = low[(1 - core) * HALF : (2 - core) * HALF]

    def store_block(index):
        row, half = index // 2, index % 2
        target = i_out.at[place.core * rows + row]
        local = pltpu.make_async_copy(block_out.at[half], target, swap_local.at[1 + row])
        far = remote(
            block_out.at[half], target, swap_send.at[1 + row], swap_recv.at[1 + row], place.twin
        )
        return local, far, half

    def wait_block(index):
        local, far, half = store_block(index)

        @pl.when(place.core == half)
        def keep():
            local.wait()

        @pl.when(place.core != half)
        def give():
            far.wait()

    for index in range(BACK_TAIL):

        @pl.when(step == BACK_STEPS + index)
        def close():
            size = LEN // 2
            if index >= 2:
                wait_block(index - 2)
            gain_sum = jnp.zeros((8, D), f32)
            shift_sum = jnp.zeros((8, D), f32)
            for block in range(size // 16):
                rows_here = slice(block * 16, (block + 1) * 16)
                grad = grad_sum[index * size + block * 16 : index * size + (block + 1) * 16]
                unit, rstd = norm_parts(x_ref[rows_here].astype(f32))
                gain_sum = gain_sum + jnp.sum((grad * unit).reshape(-1, 8, D), axis=0)
                shift_sum = shift_sum + jnp.sum(grad.reshape(-1, 8, D), axis=0)
                total = norm_back(grad, unit, rstd, vec_ref[0:1, :])
                block_out[index % 2, rows_here] = (z_ref[rows_here].astype(f32) + total).astype(b16)
            sums_ref[0:1, :] += jnp.sum(gain_sum, 0, keepdims=True)
            sums_ref[1:2, :] += jnp.sum(shift_sum, 0, keepdims=True)
            local, far, half = store_block(index)

            @pl.when(place.core == half)
            def keep():
                local.start()

            @pl.when(place.core != half)
            def give():
                far.start()

    @pl.when(step == BACK_STEPS + BACK_TAIL - 1)
    def drain():
        devices = [place.twin] + place.partners

        def vector(index):
            return remote(
                sums_ref, vec_land.at[index], vec_send.at[index], vec_recv.at[index], devices[index]
            )

        vector(0).start()
        for number in range(BACK_STEPS + BACK_TAIL, BACK_STEPS + Sum.steps + Gather.steps):
            both(number)
            index = number - BACK_STEPS - BACK_TAIL
            if index < 5:
                vector(index).wait()
                sums_ref[...] += vec_land[index]
                if index < 4:
                    vector(index + 1).start()
        for index in range(2):
            swap_y(index).wait()
        for index in range(2, BACK_TAIL):
            wait_block(index)
        for index in range(PAIRS):
            for tile in range(3):
                pair_store(index, tile).wait()
        for flow in range(FLOWS):
            for copy in hand.stores(flow):
                copy.wait()


def back(table, attention, weights, normed, x, residual, vectors, tiles, sums, y):
    rows, length = y.shape[:2]
    tokens = rows * length
    any_spec = pl.BlockSpec(memory_space=pl.ANY)
    smem = pl.BlockSpec(memory_space=pltpu.SMEM)
    dma = pltpu.SemaphoreType.DMA

    def now(step):
        return jnp.minimum(step, BACK_STEPS - 1)

    def tail(step):
        return jnp.maximum(step - BACK_STEPS, 0)

    head_block = pl.BlockSpec((PAIR, LEN), lambda s: (now(s) // 2, lax.rem(now(s), 2)))
    tail_block = pl.BlockSpec((LEN // 2, D), lambda s: (tail(s), 0))
    whole = pl.BlockSpec((PIECES, D), lambda s: (0, 0))
    sums_block = pl.BlockSpec((16, D), lambda s: (0, 0))
    return pl.pallas_call(
        back_kernel,
        grid=(BACK_STEPS + BACK_TAIL,),
        in_specs=[
            smem,
            pl.BlockSpec((2, LEN, LEN), lambda s: (now(s), 0, 0)),
            pl.BlockSpec((1, 2, LEN), lambda s: (now(s), 0, 0)),
            pl.BlockSpec((LEN, PAIR), lambda s: (lax.rem(now(s), 2), now(s) // 2)),
            head_block,
            head_block,
            head_block,
            head_block,
            pl.BlockSpec((1, D, WIDE), lambda s: (now(s) // 2, 0, 0)),
            pl.BlockSpec((tokens, D), lambda s: (0, 0), pipeline_mode=pl.Buffered(1)),
            tail_block,
            tail_block,
            whole,
            any_spec,
            sums_block,
            any_spec,
        ],
        out_specs=[any_spec] * 4 + [sums_block],
        out_shape=[
            jax.ShapeDtypeStruct((2 * rows, length // 2, D), b16),
            jax.ShapeDtypeStruct((2 * rows, length // 2, D), b16),
            jax.ShapeDtypeStruct((3, HALF, D), b16),
            jax.ShapeDtypeStruct((CAP, HALF, D), b16),
            jax.ShapeDtypeStruct((16, D), f32),
        ],
        scratch_shapes=[
            pltpu.VMEM((tokens, D), f32),
            pltpu.VMEM((WIDE, D), f32),
            pltpu.VMEM((WIDE, LEN), b16),
            pltpu.VMEM((2, LEN // 4, LEN // 2), b16),
            pltpu.VMEM((2, LEN // 2, D), b16),
            pltpu.VMEM((REST, HALF, D), b16),
            pltpu.VMEM((FLOWS, REST, NEAR, D), b16),
            pltpu.VMEM((FLOWS, 3, REST, KEEP, D), b16),
            pltpu.VMEM((3, HALF, D), b16),
            pltpu.VMEM((PAIRS, HALF, WIDE), b16),
            pltpu.VMEM((FLOWS, PAIRS, NEAR, WIDE), b16),
            pltpu.VMEM((FLOWS, 3, PAIRS, KEEP, WIDE), b16),
            pltpu.VMEM((2, HALF, WIDE), b16),
            pltpu.VMEM((2, HALF, WIDE), b16),
            pltpu.VMEM((FLOWS, PAIRS, KEEP, WIDE), b16),
            pltpu.VMEM((FLOWS, PAIRS, NEAR, WIDE), b16),
            pltpu.VMEM((FLOWS, 2 * CAP, KEEP, D), b16),
            pltpu.VMEM((FLOWS, 2 * CAP, KEEP, D), b16),
            pltpu.VMEM((FLOWS, CAP, NEAR, D), b16),
            pltpu.VMEM((FLOWS, CAP, NEAR, D), b16),
            pltpu.VMEM((FLOWS, CAP, KEEP, D), b16),
            pltpu.VMEM((5, 16, D), f32),
            dma((REST, FLOWS, 5)),
            dma((REST, FLOWS, 5)),
            dma((PAIRS, FLOWS, 7)),
            dma((PAIRS, FLOWS, 7)),
            dma((FLOWS, 2)),
            dma((FLOWS, 2)),
            dma((FLOWS, 3)),
            dma((REST,)),
            dma((REST,)),
            dma((PAIRS,)),
            dma((PAIRS,)),
            dma((3,)),
            dma((PAIRS, 3)),
            dma((3,)),
            dma((3,)),
            dma((3,)),
            dma((5,)),
            dma((5,)),
        ],
        compiler_params=pltpu.CompilerParams(
            collective_id=1, has_side_effects=True, vmem_limit_bytes=62 * MIB
        ),
        name="back",
    )(table, *attention, weights, normed, x, residual, vectors, tiles, sums, y)


def update_kernel(tile_at, one, two, w_ref, m_ref, s_ref, y_in, i_in, w_out, m_out, s_out, y_out, i_out):
    step = pl.program_id(0)
    tile = tile_at[step // 2]
    grad = jnp.where(tile < 3, one[0], two[0]).astype(f32)
    parts = adam_step(w_ref[0], grad, m_ref[0], s_ref[0], RATE)
    for target, part in zip((w_out, m_out, s_out), parts):
        target[0] = jnp.where(tile >= 0, part, jnp.zeros_like(part))

    @pl.when(step < 4)
    def widen():
        y_out[...] = y_in[...].astype(f32)
        i_out[...] = i_in[...].astype(f32)


def update(tile_at, one, two, master, first, second, y, grad):
    tokens = y.shape[0]
    size = HALF // 2
    state = pl.BlockSpec((1, size, D), lambda s, tile_at: (s // 2, lax.rem(s, 2), 0))
    wide = pl.BlockSpec((tokens // 4, D), lambda s, tile_at: (jnp.minimum(s, 3), 0))
    return pl.pallas_call(
        update_kernel,
        grid_spec=pltpu.PrefetchScalarGridSpec(
            num_scalar_prefetch=1,
            grid=(CAP * 2,),
            in_specs=[
                pl.BlockSpec(
                    (1, size, D),
                    lambda s, tile_at: (jnp.clip(tile_at[s // 2], 0, 2), lax.rem(s, 2), 0),
                ),
                state,
                state,
                state,
                state,
                wide,
                wide,
            ],
            out_specs=[state] * 3 + [wide] * 2,
        ),
        out_shape=[jax.ShapeDtypeStruct(master.shape, f32)] * 3
        + [jax.ShapeDtypeStruct((tokens, D), f32)] * 2,
        compiler_params=pltpu.CompilerParams(vmem_limit_bytes=60 * MIB),
        name="update",
    )(tile_at, one, two, master, first, second, y, grad)


def shards_paired(
    inputs,
    cotangent,
    doc_lengths,
    owner_list,
    master,
    first_moment,
    second_moment,
    vectors,
    vector_first,
    vector_second,
):
    rows_here, span, width = inputs.shape
    place = lax.axis_index("blk")
    member = lax.axis_index("dp")
    rows_mine = rows_here // 2
    order = jnp.arange(PIECES)
    same_owner = owner_list[:, None] == owner_list[None, :]
    ranks = jnp.sum(same_owner & (order[None, :] < order[:, None]), axis=1).astype(jnp.int32)
    slot_of = owner_list * CAP + ranks
    front_outs = front(owner_list, doc_lengths, master, vectors, inputs, cotangent)
    x, cot, normed, weights_one, weights_two, queries, keys, values = front_outs[:8]
    weights, recips, context_turned, context = front_outs[8:]
    x = x.reshape(-1, width)
    cot = cot.reshape(-1, width)
    block_out, residual, grad_context, sums, tiles_two = feed(
        context, context_turned, x, cot, weights_two, vectors
    )
    hits = jnp.arange(16 * CAP)[:, None] == slot_of[None, :]
    tile_at = jnp.sum(jnp.where(hits, order[None, :] + 1, 0), axis=1).astype(jnp.int32) - 1
    table = jnp.maximum(tile_at - 3, 0)
    block_out, input_grad, total_one, total_two, vector_total = back(
        table,
        (weights, recips, values, queries, keys, context_turned, grad_context),
        weights_one,
        normed,
        x,
        residual,
        vectors,
        tiles_two,
        sums,
        block_out.reshape(rows_mine, LEN, width),
    )
    mine = lax.dynamic_slice_in_dim(tile_at, member * CAP, CAP, 0)
    *updated, block_out, input_grad = update(
        mine,
        total_one,
        total_two,
        master,
        first_moment,
        second_moment,
        block_out.reshape(-1, width),
        input_grad.reshape(-1, width),
    )
    columns = vector_first.shape[1]
    vector_cols = lax.dynamic_slice_in_dim(vectors, place * columns, columns, 1)
    vector_total = lax.dynamic_slice(vector_total, (0, place * columns), (PIECES, columns))
    updated_vectors = adam_step(vector_cols, vector_total, vector_first, vector_second, VEC_RATE)
    return (
        block_out.reshape(inputs.shape),
        input_grad.reshape(inputs.shape),
        *updated,
        *updated_vectors,
    )


def solution(mesh):
    in_specs = (
        P("dp", "blk", None),
        P("dp", "blk", None),
        P("dp", None),
        P(),
        P("dp", "blk", None),
        P("dp", "blk", None),
        P("dp", "blk", None),
        P(),
        P(None, "blk"),
        P(None, "blk"),
    )
    out_specs = (
        P("dp", "blk", None),
        P("dp", "blk", None),
        P("dp", "blk", None),
        P("dp", "blk", None),
        P("dp", "blk", None),
        P(None, "blk"),
        P(None, "blk"),
        P(None, "blk"),
    )
    paired = mesh.shape["blk"] == 2 and mesh.shape["dp"] == 16
    shards = shards_paired if paired else shards_any
    return jax.shard_map(shards, mesh=mesh, in_specs=in_specs, out_specs=out_specs, check_vma=False)
```

```python
from functools import partial

import jax
import jax.numpy as jnp
from jax import lax
from jax.experimental import pallas as pl
from jax.experimental.pallas import tpu as pltpu
from jax.sharding import PartitionSpec as P

D = 768
FF = 3072
HEADS = 12
HEAD_DIM = 64
LEN = 1024
CAP = 3
STEP = 10
PIECES = 12


EPS_NORM = 1e-05
BETA_ONE = 0.9
BETA_TWO = 0.999
RATE = 0.04
VEC_RATE = 0.25
DECAY = 0.01
ADAM_EPS = 1e-08


def normalize(values_in, gain, shift):
    center = jnp.mean(values_in, axis=-1, keepdims=True)
    offset = values_in - center
    spread = jnp.mean(offset * offset, axis=-1, keepdims=True)
    return offset * lax.rsqrt(spread + EPS_NORM) * gain + shift


def adam_step(weight, grad, first, second, rate):
    first_new = BETA_ONE * first + (1.0 - BETA_ONE) * grad
    second_new = BETA_TWO * second + (1.0 - BETA_TWO) * grad * grad
    corrected = (
        first_new
        / (1.0 - BETA_ONE**STEP)
        / (jnp.sqrt(second_new / (1.0 - BETA_TWO**STEP)) + ADAM_EPS)
    )
    return (weight - rate * (corrected + DECAY * weight), first_new, second_new)


def shards_any(
    inputs,
    cotangent,
    doc_lengths,
    owner_list,
    master,
    first_moment,
    second_moment,
    vectors,
    vector_first,
    vector_second,
):
    rows_here, span, width = inputs.shape
    tokens_here = rows_here * span
    fold = FF // D
    scale = HEAD_DIM ** (-0.5)
    place = lax.axis_index("blk")
    f32 = jnp.float32
    b16 = jnp.bfloat16
    order = jnp.arange(PIECES)
    same_owner = owner_list[:, None] == owner_list[None, :]
    ranks = jnp.sum(same_owner & (order[None, :] < order[:, None]), axis=1)
    slot_of = owner_list * CAP + ranks

    mine = (owner_list == lax.axis_index("dp"))[:, None, None]
    tile_rows = lax.psum(jnp.where(mine, master[ranks], 0.0).astype(b16), "dp")
    tiles = lax.all_gather(tile_rows, "blk", axis=1, tiled=True)
    query_weight = tiles[0]
    key_weight = tiles[1]
    value_weight = tiles[2]
    out_weight = tiles[3]
    up_weight = jnp.transpose(tiles[4 : 4 + fold], (1, 0, 2)).reshape(width, FF)
    down_weight = tiles[4 + fold :].reshape(FF, width)
    flat_in = inputs.reshape(tokens_here, width).astype(f32)
    normed_one = normalize(flat_in, vectors[0], vectors[1]).astype(b16)
    queries = (jnp.dot(normed_one, query_weight, preferred_element_type=f32) + vectors[4]).astype(
        b16
    )
    keys_here = jnp.dot(normed_one, key_weight, preferred_element_type=f32).astype(b16)
    values_here = (
        jnp.dot(normed_one, value_weight, preferred_element_type=f32) + vectors[5]
    ).astype(b16)
    query_heads = queries.reshape(rows_here, span, HEADS, HEAD_DIM)
    first_len = doc_lengths[:, 0]
    query_seg = (place * span + jnp.arange(span))[None, :] >= first_len[:, None]

    def block_scores(key_block, start):
        count = key_block.shape[1]
        key_heads = key_block.reshape(rows_here, count, HEADS, HEAD_DIM)
        raw = (
            jnp.einsum("rqhd,rkhd->rhqk", query_heads, key_heads, preferred_element_type=f32)
            * scale
        )
        key_seg = (start + jnp.arange(count))[None, :] >= first_len[:, None]
        allowed = query_seg[:, None, :, None] == key_seg[:, None, None, :]
        return (raw, allowed)

    key_rows = keys_here.reshape(rows_here, span, width)
    value_rows = values_here.reshape(rows_here, span, width)
    top = jnp.full((rows_here, HEADS, span), -1e30, f32)
    key_block = lax.all_gather(key_rows, "blk", axis=1, tiled=True)
    value_block = lax.all_gather(value_rows, "blk", axis=1, tiled=True)
    count = key_block.shape[1]
    raw, allowed = block_scores(key_block, jnp.int32(0))
    new_top = jnp.maximum(top, jnp.max(jnp.where(allowed, raw, -1e30), axis=-1))
    weights = jnp.where(allowed, jnp.exp(raw - new_top[..., None]), 0.0)
    value_heads = value_block.reshape(rows_here, count, HEADS, HEAD_DIM)
    update = jnp.einsum(
        "rhqk,rkhd->rhqd", weights.astype(b16), value_heads, preferred_element_type=f32
    )
    total = jnp.sum(weights, axis=-1)
    log_total = new_top + jnp.log(total)
    context_raw = update / total[..., None]
    context_low = jnp.transpose(context_raw, (0, 2, 1, 3)).reshape(tokens_here, width).astype(b16)
    residual = flat_in + (jnp.dot(context_low, out_weight, preferred_element_type=f32) + vectors[6])
    normed_two = normalize(residual, vectors[2], vectors[3]).astype(b16)
    hidden = jnp.dot(normed_two, up_weight, preferred_element_type=f32) + vectors[8:].reshape(FF)
    gelu_exact = partial(jax.nn.gelu, approximate=False)
    active, gelu_pull = jax.vjp(gelu_exact, hidden)
    active_low = active.astype(b16)
    block_out = (
        residual + (jnp.dot(active_low, down_weight, preferred_element_type=f32) + vectors[7])
    ).reshape(rows_here, span, width)
    grad_out = cotangent.reshape(tokens_here, width)
    down_grad = jnp.einsum("tf,td->fd", active_low, grad_out, preferred_element_type=f32)
    down_sum = jnp.sum(grad_out, axis=0, dtype=f32)
    grad_active = jnp.einsum("td,fd->tf", grad_out, down_weight, preferred_element_type=f32)
    grad_hidden = gelu_pull(grad_active)[0].astype(b16)
    up_grad = jnp.einsum("td,tf->df", normed_two, grad_hidden, preferred_element_type=f32)
    up_sum = jnp.sum(grad_hidden, axis=0, dtype=f32)
    ffn_tiles = jnp.concatenate(
        [
            jnp.transpose(up_grad.reshape(width, fold, width), (1, 0, 2)),
            down_grad.reshape(fold, width, width),
        ],
        axis=0,
    )
    grad_normed_two = jnp.einsum("tf,df->td", grad_hidden, up_weight, preferred_element_type=f32)
    unused, second_pull = jax.vjp(normalize, residual, vectors[2], vectors[3])
    residual_part, gain_two_grad, shift_two_grad = second_pull(grad_normed_two)
    grad_residual = grad_out.astype(f32) + residual_part
    grad_attended = grad_residual.astype(b16)
    out_grad = jnp.einsum("tm,td->md", context_low, grad_attended, preferred_element_type=f32)
    out_sum = jnp.sum(grad_attended, axis=0, dtype=f32)
    grad_context = jnp.einsum(
        "td,md->tm", grad_attended, out_weight, preferred_element_type=f32
    ).astype(b16)
    grad_heads = grad_context.reshape(rows_here, span, HEADS, HEAD_DIM)
    delta = jnp.einsum("rqhd,rhqd->rhq", grad_heads.astype(f32), context_raw)
    key_all, value_all = (
        lax.all_gather(key_rows, "blk", axis=1, tiled=True),
        lax.all_gather(value_rows, "blk", axis=1, tiled=True),
    )
    key_size = min(512, LEN)

    def back_block(index, carry):
        grad_query, key_total, value_total = carry
        start = index * key_size
        key_block = lax.dynamic_slice_in_dim(key_all, start, key_size, 1)
        value_block = lax.dynamic_slice_in_dim(value_all, start, key_size, 1)
        raw, allowed = block_scores(key_block, start)
        weights_back = jnp.where(allowed, jnp.exp(raw - log_total[..., None]), 0.0)
        key_heads = key_block.reshape(rows_here, key_size, HEADS, HEAD_DIM)
        value_heads = value_block.reshape(rows_here, key_size, HEADS, HEAD_DIM)
        value_grad = jnp.einsum(
            "rhqk,rqhd->rkhd", weights_back.astype(b16), grad_heads, preferred_element_type=f32
        )
        weight_grad = jnp.einsum(
            "rqhd,rkhd->rhqk", grad_heads, value_heads, preferred_element_type=f32
        )
        score_grad = (weights_back * (weight_grad - delta[..., None])).astype(b16)
        grad_query = (
            grad_query
            + jnp.einsum("rhqk,rkhd->rqhd", score_grad, key_heads, preferred_element_type=f32)
            * scale
        )
        key_grad = (
            jnp.einsum("rhqk,rqhd->rkhd", score_grad, query_heads, preferred_element_type=f32)
            * scale
        )
        key_total = lax.dynamic_update_slice_in_dim(
            key_total, key_grad.reshape(rows_here, key_size, width), start, 1
        )
        value_total = lax.dynamic_update_slice_in_dim(
            value_total, value_grad.reshape(rows_here, key_size, width), start, 1
        )
        return (grad_query, key_total, value_total)

    zero_rows = jnp.zeros((rows_here, LEN, width), f32)
    grad_query, key_total, value_total = lax.fori_loop(
        0,
        LEN // key_size,
        back_block,
        (jnp.zeros((rows_here, span, HEADS, HEAD_DIM), f32), zero_rows, zero_rows),
    )
    key_grad_here, value_grad_here = (
        lax.psum_scatter(
            key_total.astype(jnp.bfloat16), "blk", scatter_dimension=1, tiled=True
        ).astype(jnp.float32),
        lax.psum_scatter(
            value_total.astype(jnp.bfloat16), "blk", scatter_dimension=1, tiled=True
        ).astype(jnp.float32),
    )
    query_low = grad_query.reshape(tokens_here, width).astype(b16)
    key_low = key_grad_here.reshape(tokens_here, width).astype(b16)
    value_low = value_grad_here.reshape(tokens_here, width).astype(b16)
    query_tile = jnp.einsum("td,te->de", normed_one, query_low, preferred_element_type=f32)
    key_tile = jnp.einsum("td,te->de", normed_one, key_low, preferred_element_type=f32)
    value_tile = jnp.einsum("td,te->de", normed_one, value_low, preferred_element_type=f32)
    grad_normed_one = (
        jnp.einsum("te,de->td", query_low, query_weight, preferred_element_type=f32)
        + jnp.einsum("te,de->td", key_low, key_weight, preferred_element_type=f32)
        + jnp.einsum("te,de->td", value_low, value_weight, preferred_element_type=f32)
    )
    unused, first_pull = jax.vjp(normalize, flat_in, vectors[0], vectors[1])
    input_part, gain_one_grad, shift_one_grad = first_pull(grad_normed_one)
    input_grad = (grad_residual + input_part).reshape(rows_here, span, width)
    vector_grads = jnp.concatenate(
        [
            jnp.stack(
                [
                    gain_one_grad,
                    shift_one_grad,
                    gain_two_grad,
                    shift_two_grad,
                    jnp.sum(query_low, axis=0, dtype=f32),
                    jnp.sum(value_low, axis=0, dtype=f32),
                    out_sum,
                    down_sum,
                ]
            ),
            up_sum.reshape(fold, width),
        ],
        axis=0,
    )
    attn_tiles = jnp.stack([query_tile, key_tile, value_tile, out_grad])
    piece_share, vector_share = (
        lax.psum_scatter(
            jnp.concatenate([attn_tiles, ffn_tiles], axis=0).astype(jnp.bfloat16),
            "blk",
            scatter_dimension=1,
            tiled=True,
        ).astype(jnp.float32),
        lax.psum_scatter(
            vector_grads.astype(jnp.bfloat16), "blk", scatter_dimension=1, tiled=True
        ).astype(jnp.float32),
    )
    own_slots = lax.axis_index("dp") * CAP + jnp.arange(CAP)
    pick = (own_slots[:, None] == slot_of[None, :]).astype(f32)
    occupied = jnp.sum(pick, axis=1)[:, None, None]
    total_share, vector_total = (
        lax.psum(piece_share.astype(jnp.bfloat16), "dp").astype(jnp.float32),
        lax.psum(vector_share.astype(jnp.bfloat16), "dp").astype(jnp.float32),
    )
    slot_grads = jnp.einsum("cp,prd->crd", pick, total_share, precision=lax.Precision.HIGHEST)
    new_master, new_first, new_second = adam_step(
        master, slot_grads, first_moment, second_moment, RATE
    )
    columns = vector_first.shape[1]
    vector_cols = lax.dynamic_slice_in_dim(vectors, place * columns, columns, 1)
    new_vectors, new_vector_first, new_vector_second = adam_step(
        vector_cols, vector_total, vector_first, vector_second, VEC_RATE
    )
    return (
        block_out,
        input_grad,
        new_master * occupied,
        new_first * occupied,
        new_second * occupied,
        new_vectors,
        new_vector_first,
        new_vector_second,
    )


f32 = jnp.float32
b16 = jnp.bfloat16
LOG2E = 1.4426950408889634
MIB = 1024 * 1024
PAIRS = HEADS // 2
PAIR = 2 * HEAD_DIM


def dot_nn(left, right):
    return lax.dot_general(left, right, (((1,), (0,)), ((), ())), preferred_element_type=f32)


def dot_nt(left, right):
    return lax.dot_general(left, right, (((1,), (1,)), ((), ())), preferred_element_type=f32)


def dot_tn(left, right):
    return lax.dot_general(left, right, (((0,), (0,)), ((), ())), preferred_element_type=f32)


def norm_parts(values_in):
    center = jnp.mean(values_in, axis=-1, keepdims=True)
    offset = values_in - center
    spread = jnp.mean(offset * offset, axis=-1, keepdims=True)
    rstd = lax.rsqrt(spread + EPS_NORM)
    return offset * rstd, rstd


def norm_back(grad, unit, rstd, gain):
    scaled = grad * gain
    first = jnp.mean(scaled, axis=-1, keepdims=True)
    second = jnp.mean(scaled * unit, axis=-1, keepdims=True)
    return rstd * (scaled - first - unit * second)


def gelu_parts(value):
    bell = jnp.exp2(value * value * (-0.5 * LOG2E))
    ratio = pl.reciprocal(1.0 + (0.3275911 * 0.7071067811865476) * jnp.abs(value))
    poly = 0.5 * 1.061405429
    poly = poly * ratio + 0.5 * -1.453152027
    poly = poly * ratio + 0.5 * 1.421413741
    poly = poly * ratio + 0.5 * -0.284496736
    poly = poly * ratio + 0.5 * 0.254829592
    tail = poly * ratio * bell
    cdf = jnp.where(value >= 0.0, 1.0 - tail, tail)
    return value * cdf, cdf + value * (bell * 0.3989422804014327)


def head_only(block, head):
    lane = lax.broadcasted_iota(jnp.int32, block.shape, 1)
    keep = (lane >= head * HEAD_DIM) & (lane < (head + 1) * HEAD_DIM)
    return jnp.where(keep, block, jnp.zeros_like(block))


def feed_kernel(
    c_ref, o_ref, x_ref, g_ref, w_ref, vec_ref,
    y_ref, r_ref, d_ref, sums_ref, tiles_ref,
    acc_ref, unit_ref, rstd_ref, normed, out_ref, grad_ref,
    hidden_ref, pulled_ref, active_ref, slope_ref, stage_ref, sem_ref,
):
    fold = FF // D
    step = pl.program_id(0)
    blocks = [slice(start, start + 16) for start in range(0, x_ref.shape[0], 16)]

    @pl.when(step == 0)
    def clear():
        acc_ref[...] = jnp.zeros_like(acc_ref)
        sums_ref[...] = jnp.zeros_like(sums_ref)

    def eights(value):
        return jnp.sum(value.reshape(-1, 8, D), axis=0)

    def add_sum(row, value):
        sums_ref[row : row + 1, :] += jnp.sum(value, 0, keepdims=True)

    out_ref[...] = dot_nn(c_ref[...], w_ref[0])
    gain = vec_ref[2:3, :]
    for rows in blocks:
        residual = x_ref[rows].astype(f32) + (out_ref[rows] + vec_ref[6:7, :])
        unit, rstd = norm_parts(residual)
        unit_ref[rows] = unit
        rstd_ref[rows] = jnp.broadcast_to(rstd, (16, 128))
        normed[rows] = (unit * gain + vec_ref[3:4, :]).astype(b16)
        out_ref[rows] = residual + vec_ref[7:8, :]
    turned = normed[...].T
    cot = g_ref[...]

    def begin(part):
        def hidden():
            hidden_ref[part % 2] = dot_nn(normed[...], w_ref[1 + part])

        def pulled():
            pulled_ref[part % 2] = dot_nt(cot, w_ref[1 + fold + part])

        return [hidden, pulled]

    def end(part):
        slot = part % 2

        def out():
            out_ref[...] += dot_nn(active_ref[slot], w_ref[1 + fold + part])

        def back():
            grad = dot_nt(slope_ref[slot], w_ref[1 + part])
            grad_ref[...] = grad if part == 0 else grad_ref[...] + grad

        def up():
            acc_ref[1 + part] += dot_nn(turned, slope_ref[slot])

        def down():
            acc_ref[1 + fold + part] += dot_tn(active_ref[slot], cot)

        return [out, back, up, down]

    for work in begin(0):
        work()
    for part in range(fold):
        slot = part % 2
        work = end(part - 1) if part > 0 else []
        work = work + (begin(part + 1) if part + 1 < fold else [])
        total = jnp.zeros((8, D), f32)
        for index, rows in enumerate(blocks):
            if index * len(work) // len(blocks) != (index - 1) * len(work) // len(blocks):
                work[index * len(work) // len(blocks)]()
            active, slope = gelu_parts(hidden_ref[slot, rows] + vec_ref[8 + part : 9 + part, :])
            active_ref[slot, rows] = active.astype(b16)
            pulled = (pulled_ref[slot, rows] * slope).astype(b16)
            slope_ref[slot, rows] = pulled
            total = total + eights(pulled.astype(f32))
        add_sum(8 + part, total)
    for work in end(fold - 1):
        work()
    y_ref[...] = out_ref[...].astype(b16)
    totals = [jnp.zeros((8, D), f32) for unused in range(4)]
    for rows in blocks:
        grad, unit, wide = grad_ref[rows], unit_ref[rows], g_ref[rows].astype(f32)
        back = wide + norm_back(grad, unit, rstd_ref[rows, 0:1], gain)
        low = back.astype(b16)
        r_ref[rows] = low
        terms = (grad * unit, grad, low.astype(f32), wide)
        totals = [total + eights(term) for total, term in zip(totals, terms)]
    for row, total in zip((2, 3, 6, 7), totals):
        add_sum(row, total)
    low = r_ref[...]
    d_ref[...] = dot_nt(w_ref[0], low).astype(b16)
    acc_ref[0] += dot_nn(o_ref[...], low)

    @pl.when(step == pl.num_programs(0) - 1)
    def send():
        count = 1 + 2 * fold
        copies = []
        for part in range(count):
            if part >= 2:
                copies[part - 2].wait()
            stage_ref[part % 2] = acc_ref[part].astype(b16)
            copy = pltpu.make_async_copy(stage_ref.at[part % 2], tiles_ref.at[part], sem_ref.at[part % 2])
            copy.start()
            copies.append(copy)
        copies[count - 2].wait()
        copies[count - 1].wait()


def feed(context, turned, x, cot, weights, vectors):
    tokens = x.shape[0]
    size = 128
    count = 1 + 2 * (FF // D)
    token_block = pl.BlockSpec((size, D), lambda i: (i, 0))
    turned_block = pl.BlockSpec((D, size), lambda i: (0, i))
    return pl.pallas_call(
        feed_kernel,
        grid=(tokens // size,),
        in_specs=[
            token_block,
            turned_block,
            token_block,
            token_block,
            pl.BlockSpec((count, D, D), lambda i: (0, 0, 0), pipeline_mode=pl.Buffered(1)),
            pl.BlockSpec((PIECES, D), lambda i: (0, 0)),
        ],
        out_specs=[
            token_block,
            token_block,
            turned_block,
            pl.BlockSpec((16, D), lambda i: (0, 0)),
            pl.BlockSpec(memory_space=pl.ANY),
        ],
        out_shape=[
            jax.ShapeDtypeStruct((tokens, D), b16),
            jax.ShapeDtypeStruct((tokens, D), b16),
            jax.ShapeDtypeStruct((D, tokens), b16),
            jax.ShapeDtypeStruct((16, D), f32),
            jax.ShapeDtypeStruct((count, D, D), b16),
        ],
        scratch_shapes=[
            pltpu.VMEM((count, D, D), f32),
            pltpu.VMEM((size, D), f32),
            pltpu.VMEM((size, 128), f32),
            pltpu.VMEM((size, D), b16),
            pltpu.VMEM((size, D), f32),
            pltpu.VMEM((size, D), f32),
            pltpu.VMEM((2, size, D), f32),
            pltpu.VMEM((2, size, D), f32),
            pltpu.VMEM((2, size, D), b16),
            pltpu.VMEM((2, size, D), b16),
            pltpu.VMEM((2, D, D), b16),
            pltpu.SemaphoreType.DMA((2,)),
        ],
        compiler_params=pltpu.CompilerParams(vmem_limit_bytes=60 * MIB),
        cost_estimate=pl.CostEstimate(
            flops=6 * count * tokens * D * D,
            bytes_accessed=18 * tokens * D + 4 * count * D * D,
            transcendentals=2 * tokens * FF,
        ),
        name="feed",
    )(context, turned, x, cot, weights, vectors)


MESH = pl.DeviceIdType.MESH
HALF = D // 2
FLOWS = 2
FLOW = HALF // FLOWS
NEAR = FLOW // 2
KEEP = NEAR // 2
WIDE = 3 * PAIR
REST = PIECES - 3
GROUPS = ((0, 1), (1, 2), (3, 3))
CHUNKS = len(GROUPS)


class Place:
    def __init__(self):
        self.me = lax.axis_index("dp")
        self.core = lax.axis_index("blk")
        self.bits = [lax.rem(self.me // weight, 2) for weight in (1, 2, 4, 8)]
        self.chips = [
            self.me + weight - 2 * weight * bit for weight, bit in zip((1, 2, 4, 8), self.bits)
        ]
        self.partners = [{"dp": chip} for chip in self.chips]
        low, high = self.bits[2:]
        self.inner = low != high
        self.across = {"dp": self.me + 4 - 8 * low + 8 - 16 * high}
        self.other = 1 - self.core
        self.twin = {"blk": self.other}
        self.seat = self.bits[0] + 2 * self.bits[1]
        layer = [self.chips[0], self.chips[1], self.chips[0] + self.chips[1] - self.me]
        self.layer = [{"dp": chip} for chip in layer]
        self.layer_chips = layer
        self.layer_twins = [{"dp": chip, "blk": self.other} for chip in layer]
        self.layer_seats = [
            self.seat + 1 - 2 * self.bits[0],
            self.seat + 2 - 4 * self.bits[1],
            3 - self.seat,
        ]
        self.column = [{"dp": lax.rem(self.me + 4 * ahead, 16)} for ahead in (1, 2, 3)]

    def greet(self):
        barrier = pltpu.get_barrier_semaphore()
        for device in self.layer + self.layer_twins + self.column + [self.twin]:
            pl.semaphore_signal(barrier, 1, device_id=device, device_id_type=MESH)
        pl.semaphore_wait(barrier, 10)

    def flow(self, index):
        first, second = (0, 1) if index == 0 else (1, 0)
        base = index * FLOW
        near = base + self.bits[first] * NEAR
        far = base + NEAR - self.bits[first] * NEAR
        keep = near + self.bits[second] * KEEP
        give = near + KEEP - self.bits[second] * KEEP
        return first, second, near, far, keep, give


def remote(source, target, send, receive, device):
    return pltpu.make_async_remote_copy(
        src_ref=source,
        dst_ref=target,
        send_sem=send,
        recv_sem=receive,
        device_id=device,
        device_id_type=MESH,
    )


def rows_at(start, count):
    return pl.ds(pl.multiple_of(start, 16), count)


class Spread:
    def __init__(self, place, owner, rank, slots, land, gift, sems):
        self.place, self.owner, self.rank = place, owner, rank
        self.slots, self.land, self.gift, self.sems = slots, land, gift, sems

    def cols(self, chunk):
        return pl.ds(GROUPS[chunk][0] * PAIR, GROUPS[chunk][1] * PAIR)

    def first_copy(self, chunk, index):
        first, second, near, far, keep, give = self.place.flow(index)
        return remote(
            self.slots.at[:, rows_at(far, NEAR), self.cols(chunk)],
            self.land[chunk].at[index],
            self.sems[0].at[chunk, index, 0],
            self.sems[1].at[chunk, index, 0],
            self.place.partners[first],
        )

    def second_copy(self, chunk, index, which):
        first, second, near, far, keep, give = self.place.flow(index)
        if which == 0:
            source = self.slots.at[:, rows_at(give, KEEP), self.cols(chunk)]
        else:
            source = self.land[chunk].at[index, :, rows_at(give - near, KEEP)]
        return remote(
            source,
            self.gift[chunk].at[index, pl.ds(which * CAP, CAP)],
            self.sems[0].at[chunk, index, 1 + which],
            self.sems[1].at[chunk, index, 1 + which],
            self.place.partners[second],
        )

    def step(self, chunk, index):
        for flow in range(FLOWS):
            if index == 0:
                self.first_copy(chunk, flow).start()
                self.second_copy(chunk, flow, 0).start()
            if index == 1:
                self.first_copy(chunk, flow).wait()
                self.second_copy(chunk, flow, 1).start()
            if index == 2:
                self.second_copy(chunk, flow, 0).wait()
                self.second_copy(chunk, flow, 1).wait()

    def piece(self, tile, index, chunk, start, count):
        first, second, near, far, keep, give = self.place.flow(index)
        owner, rank = self.owner[tile], self.rank[tile]
        bits = [lax.rem(owner, 2), lax.rem(owner // 2, 2)]
        apart = [bit != mine for bit, mine in zip(bits, self.place.bits)]
        cols = pl.ds(start, count)
        mine = self.slots[rank, rows_at(keep, KEEP), pl.ds(GROUPS[chunk][0] * PAIR + start, count)]
        firsts = self.land[chunk][index, rank, rows_at(keep - near, KEEP), cols]
        gifts = self.gift[chunk][index, jnp.where(apart[first], CAP, 0) + rank, :, cols]
        value = jnp.where(apart[second], gifts, jnp.where(apart[first], firsts, mine))
        layer = owner // 4 == self.place.me // 4
        return jnp.where(layer, value, jnp.zeros_like(value))


class Column:
    steps = 4

    def __init__(self, place, kept, read, write, land, sems):
        self.place, self.kept, self.read, self.write = place, kept, read, write
        self.land, self.sems = land, sems

    def copy(self, index):
        target = self.land.at[index % 2]
        device = self.place.across if index == 1 else self.place.partners[2]
        return remote(
            self.kept, target, self.sems[0].at[index], self.sems[1].at[index], device
        )

    def add(self, index):
        self.write((self.read().astype(f32) + self.land[index].astype(f32)).astype(b16))


def column_step(place, columns, index):
    @pl.when(place.inner)
    def inner():
        for column in columns:
            if index == 1:
                column.copy(0).wait_recv()
                column.add(0)
                column.copy(1).start()
            if index == 2:
                column.copy(1).wait()
                column.add(1)
                column.copy(2).start()
            if index == 3:
                column.copy(2).wait_send()

    @pl.when(jnp.logical_not(place.inner))
    def outer():
        for column in columns:
            if index == 0:
                column.copy(0).start()
            if index == 1:
                column.copy(0).wait_send()
            if index == 3:
                column.copy(2).wait_recv()
                column.write(column.land[0])


class Item:
    steps = 7

    def __init__(self, place, work, land, sems, load, store=None):
        self.place, self.work, self.land, self.sems = place, work, land, sems
        self.load, self.store = load, store
        self.base = place.core * HALF

    def column(self, flow):
        rows = rows_at(self.base + self.place.flow(flow)[4], KEEP)

        def read():
            return self.work[:, rows]

        def write(value):
            self.work[:, rows] = value

        sems = (self.sems[0].at[flow], self.sems[1].at[flow])
        return Column(self.place, self.work.at[:, rows], read, write, self.land.at[flow], sems)

    def copy(self, flow, index):
        first, second, near, far, keep, give = self.place.flow(flow)
        kept = self.work.at[:, rows_at(self.base + keep, KEEP)]
        half = self.work.at[:, rows_at(self.base + near, NEAR)]
        source, device = [
            (kept, self.place.partners[second]),
            (half, self.place.partners[first]),
        ][index]
        return remote(
            source, source, self.sems[0].at[flow, 3 + index], self.sems[1].at[flow, 3 + index], device
        )

    def pair(self):
        rows = self.work.at[:, rows_at(self.base, HALF)]
        return remote(rows, rows, self.sems[0].at[0, 5], self.sems[1].at[0, 5], self.place.twin)

    def step(self, index):
        for flow in range(FLOWS):
            if index == 0:
                self.load(self.work, rows_at(self.base + self.place.flow(flow)[4], KEEP), flow)
        if index <= 3:
            column_step(self.place, [self.column(flow) for flow in range(FLOWS)], index)
        for flow in range(FLOWS):
            if 4 <= index <= 5:
                self.copy(flow, index - 4).wait()
            if 3 <= index <= 4:
                self.copy(flow, index - 3).start()
        if index == 5:
            self.pair().start()
        if index == 6:
            self.pair().wait()
            self.store().start()


REST_GROUPS = tuple((index, 1) for index in range(REST))
PAIR_CHUNK = (0, 1, 1, 2, 2, 2)
FRONT_PAIRS = (0, 0, 2, 3, 5, 6)
DIRECT = 2
FRONT_REST = (4, 5, 5, 6, 7, 7, 8, 9, 9)
SEAT = HALF // 4


class Direct:
    steps = 5

    def __init__(self, pair, spread, work, slot_land, sum_land, sems, store):
        self.pair, self.spread, self.place, self.work = pair, spread, spread.place, work
        self.slot_land, self.sum_land, self.sems, self.store = slot_land, sum_land, sems, store
        self.cols = pl.ds(pair * PAIR, PAIR)

    def copies(self, index):
        place, work = self.place, self.work
        here = work.at[rows_at(place.core * HALF + place.seat * SEAT, SEAT)]
        if index == 0:
            slots = self.spread.slots
            plan = [
                (slots.at[:, rows_at(seat * SEAT, SEAT), self.cols], self.slot_land.at[number], device)
                for number, (seat, device) in enumerate(zip(place.layer_seats, place.layer))
            ]
        elif index == 1:
            plan = [
                (here, self.sum_land.at[number], device)
                for number, device in enumerate(place.column)
            ]
        elif index == 2:
            devices = place.layer + ([place.twin] + place.layer_twins if self.pair == 0 else [])
            plan = [(here, here, device) for device in devices]
        else:
            whole = work.at[rows_at(place.core * HALF, HALF)]
            plan = [(whole, whole, place.twin)] if self.pair > 0 else []
        base = 3 * index
        return [
            remote(source, target, self.sems[0].at[base + number], self.sems[1].at[base + number], device)
            for number, (source, target, device) in enumerate(plan)
        ]

    def piece(self, tile):
        spread, place = self.spread, self.place
        owner, rank = spread.owner[tile], spread.rank[tile]
        apart = [
            (lax.rem(owner // weight, 2) != bit).astype(jnp.int32)
            for weight, bit in zip((1, 2), place.bits)
        ]
        apart = apart[0] + 2 * apart[1]
        mine = spread.slots[rank, rows_at(place.seat * SEAT, SEAT), self.cols]
        given = self.slot_land[jnp.maximum(apart - 1, 0), rank]
        value = jnp.where(apart == 0, mine, given)
        return jnp.where(owner // 4 == place.me // 4, value, jnp.zeros_like(value))

    def step(self, index):
        rows = rows_at(self.place.core * HALF + self.place.seat * SEAT, SEAT)
        last = 3 if self.pair == 0 else 4
        if 0 < index <= last:
            for copy in self.copies(index - 1):
                copy.wait()
        if index == 1:
            for tile in range(3):
                self.work[rows, pl.ds(tile * PAIR, PAIR)] = self.piece(tile)
        if index == 2:
            total = self.work[rows].astype(f32)
            for number in range(3):
                total = total + self.sum_land[number].astype(f32)
            self.work[rows] = total.astype(b16)
        if index < last:
            for copy in self.copies(index):
                copy.start()
        if index == last:
            self.store().start()


FRONT_LEAD = 4
FRONT_CHUNKS = (2, 0, 1)


def front_kernel(
    owner, lengths, master, vec_ref, x_in, c_in,
    x_out, c_out, n_out, one_out, two_out, q_ref, k_ref, v_ref, p_ref, r_ref, o_ref, ctx_ref,
    rank, rows_ref, normed, keys, turned_values, scores, slots,
    land_one, land_two, land_three, gift_one, gift_two, gift_three,
    one, one_land, two, two_land, slot_land_one, slot_land_two, sum_land,
    spread_send, spread_recv, one_send, one_recv, two_send, two_recv,
    direct_send, direct_recv, swap_send, swap_recv, swap_local, store_sem,
):
    pair = pl.program_id(0)
    row = pl.program_id(1)
    grid_step = pair * 2 + row
    place = Place()
    rows, span = x_in.shape[0] // 2, x_in.shape[1]
    land = (land_one, land_two, land_three)
    gift = (gift_one, gift_two, gift_three)
    spread = Spread(place, owner, rank, slots, land, gift, (spread_send, spread_recv))

    def swaps(index):
        source, target = [(x_in, rows_ref), (c_in, c_out)][index]
        here = pl.ds(place.core * span, span)
        near = pltpu.make_async_copy(
            source.at[pl.ds(place.core * rows, rows)], target.at[:, here], swap_local.at[index]
        )
        far = remote(
            source.at[pl.ds(place.other * rows, rows)],
            target.at[:, here],
            swap_send.at[index],
            swap_recv.at[index],
            place.twin,
        )
        return near, far

    def row_store():
        return pltpu.make_async_copy(rows_ref, x_out, store_sem.at[PAIRS + REST])

    def normed_store():
        return pltpu.make_async_copy(normed, n_out, store_sem.at[PAIRS + REST + 1])

    def pair_item(group):
        span_of = pl.ds(group, 1)

        def load(work, where, flow):
            chunk = PAIR_CHUNK[group]
            for tile in range(3):
                part = spread.piece(tile, flow, chunk, (group - GROUPS[chunk][0]) * PAIR, PAIR)
                work[0, where, pl.ds(tile * PAIR, PAIR)] = part

        def store():
            return pltpu.make_async_copy(one.at[span_of], one_out.at[span_of], store_sem.at[group])

        sems = (one_send.at[group], one_recv.at[group])
        return Item(place, one.at[span_of], one_land.at[:, :, span_of], sems, load, store)

    def rest_item(group):
        first, count = REST_GROUPS[group]
        span_of = pl.ds(first, count)

        def load(work, where, flow):
            for index in range(count):
                for chunk, (start, wide) in enumerate(GROUPS):
                    part = spread.piece(3 + first + index, flow, chunk, 0, wide * PAIR)
                    work[index, where, pl.ds(start * PAIR, wide * PAIR)] = part

        def store():
            return pltpu.make_async_copy(
                two.at[span_of], two_out.at[span_of], store_sem.at[PAIRS + group]
            )

        sems = (two_send.at[group], two_recv.at[group])
        return Item(place, two.at[span_of], two_land.at[:, :, span_of], sems, load, store)

    def early_pair(index):
        sems = (direct_send.at[index], direct_recv.at[index])
        lands = ((slot_land_one, slot_land_two)[index], sum_land.at[index])
        return Direct(index, spread, one.at[index], *lands, sems, pair_item(index).store)

    def tick(number, odd):
        if odd == 0 and number < Direct.steps:
            for index in range(DIRECT):
                early_pair(index).step(number)
        for chunk in range(CHUNKS):
            begin = FRONT_CHUNKS[chunk]
            if odd == 0 and 0 <= number - begin <= 2:
                spread.step(chunk, number - begin)
        starts = [(pair_item, group, start) for group, start in enumerate(FRONT_PAIRS) if group >= DIRECT]
        starts += [(rest_item, group, start) for group, start in enumerate(FRONT_REST)]
        for make, group, start in starts:
            if group % 2 == odd and 0 <= number - start < Item.steps:
                make(group).step(number - start)

    def both(number):
        tick(number, 0)
        tick(number, 1)

    @pl.when(grid_step == 0)
    def lead():
        slots[...] = master[...].astype(b16)
        for tile in range(PIECES):
            count = jnp.int32(0)
            for before in range(tile):
                count = count + (owner[before] == owner[tile]).astype(jnp.int32)
            rank[tile] = jnp.minimum(count, CAP - 1)
        place.greet()
        for copy in swaps(0):
            copy.start()
        both(0)
        for copy in swaps(1):
            copy.start()
        for copy in swaps(0):
            copy.wait()
        row_store().start()

        def norm_rows(index, carry):
            for part in range(rows):
                for block in range(4):
                    where = pl.ds(pl.multiple_of(index * 128 + block * 32, 32), 32)
                    unit, unused = norm_parts(rows_ref[part, where].astype(f32))
                    low = (unit * vec_ref[0:1, :] + vec_ref[1:2, :]).astype(b16)
                    normed[pl.ds(pl.multiple_of(part * LEN + index * 128 + block * 32, 32), 32)] = low
            return carry

        both(1)
        lax.fori_loop(0, LEN // 128, norm_rows, 0)
        normed_store().start()
        for number in range(2, FRONT_LEAD):
            both(number)

    for number in range(2 * PAIRS):
        pl.when(grid_step == number)(partial(tick, FRONT_LEAD + number, 0))

    @pl.when(row == 0)
    def project():
        lanes = pl.ds(pl.multiple_of(pair * PAIR, PAIR), PAIR)
        weight = one[pair]

        def part(index, carry):
            where = pl.ds(pl.multiple_of(index * 512, 512), 512)
            both = dot_nn(normed[where], weight)
            queries = both[:, :PAIR] + vec_ref[4:5, lanes]
            queries = (queries * (HEAD_DIM**-0.5 * LOG2E)).astype(b16)
            q_ref[:, where] = queries.T
            low = both[:, PAIR : 2 * PAIR].astype(b16)
            keys[where] = low
            k_ref[:, where] = low.T
            values = (both[:, 2 * PAIR :] + vec_ref[5:6, lanes]).astype(b16)
            v_ref[where] = values
            turned_values[:, where] = values.T
            return carry

        lax.fori_loop(0, normed.shape[0] // 512, part, 0)

    half = LEN // 2
    start = pl.multiple_of(row * LEN, LEN)
    split = lengths[place.core * rows + row, 0] < LEN
    shift = jnp.where(split, jnp.float32(-1e30), jnp.float32(0.0))

    quarter = LEN // 4
    units = [(head, step) for head in range(2) for step in range(2)]

    def score_block(unit, block, peak):
        head, step = units[unit]
        rows_here = pl.ds(pl.multiple_of(start + block * quarter, quarter), quarter)
        queries = q_ref[:, pl.ds(pl.multiple_of(start + step * half, half), half)]
        raw = dot_nn(head_only(keys[rows_here], head), queries)
        if block // 2 != step:
            raw = raw + shift
        scores[unit % 2, block * quarter : (block + 1) * quarter] = raw
        best = jnp.max(raw.reshape(-1, 8, half), axis=0)
        return best if peak is None else jnp.maximum(peak, best)

    def context_block(unit, block, total):
        head, step = units[unit]
        part = slice(head * HEAD_DIM, (head + 1) * HEAD_DIM)
        cols = pl.ds(pl.multiple_of(start + block * quarter, quarter), quarter)
        here = slice(step * half, (step + 1) * half)
        term = dot_nn(
            turned_values[part, cols], p_ref[head, block * quarter : (block + 1) * quarter, here]
        )
        return term if total is None else total + term

    def context_store(unit, total, recip):
        head, step = units[unit]
        part = slice(head * HEAD_DIM, (head + 1) * HEAD_DIM)
        o_ref[part, step * half : (step + 1) * half] = (total * recip).astype(b16)

    peak = None
    for block in range(4):
        peak = score_block(0, block, peak)
    before = None
    for unit, (head, step) in enumerate(units):
        if unit == 2:
            for number in range(2 * PAIRS):
                pl.when(grid_step == number)(partial(tick, FRONT_LEAD + number, 1))
        here = slice(step * half, (step + 1) * half)
        top = jnp.max(peak, 0, keepdims=True)
        total = jnp.zeros((8, half), f32)
        peak, context = None, None
        for block in range(4):
            if unit + 1 < len(units):
                peak = score_block(unit + 1, block, peak)
            for small in range(4 * block, 4 * block + 4):
                rows_here = slice(small * 64, (small + 1) * 64)
                value = jnp.exp2(scores[unit % 2, rows_here] - top)
                total = total + jnp.sum(value.reshape(-1, 8, half), axis=0)
                p_ref[head, rows_here, here] = value.astype(b16)
            if unit > 0:
                context = context_block(unit - 1, block, context)
        if unit > 0:
            context_store(unit - 1, context, before)
        before = 1.0 / jnp.sum(total, 0, keepdims=True)
        r_ref[0, head : head + 1, here] = before
    context = None
    for block in range(4):
        context = context_block(3, block, context)
    context_store(3, context, before)
    ctx_ref[...] = o_ref[...].T

    @pl.when(grid_step == 2 * PAIRS - 1)
    def finish_copies():
        for copy in swaps(1):
            copy.wait()
        row_store().wait()
        normed_store().wait()
        for group in range(PAIRS):
            pair_item(group).store().wait()
        for group in range(REST):
            rest_item(group).store().wait()


def front(owner, lengths, master, vectors, inputs, cotangent):
    rows, span = inputs.shape[0] // 2, inputs.shape[1]
    tokens = rows * LEN
    any_spec = pl.BlockSpec(memory_space=pl.ANY)
    smem = pl.BlockSpec(memory_space=pltpu.SMEM)
    whole = jax.ShapeDtypeStruct((rows, LEN, D), b16)
    dma = pltpu.SemaphoreType.DMA
    return pl.pallas_call(
        front_kernel,
        grid=(PAIRS, rows),
        in_specs=[
            smem,
            smem,
            pl.BlockSpec((CAP, HALF, D), lambda h, r: (0, 0, 0), pipeline_mode=pl.Buffered(1)),
            pl.BlockSpec((PIECES, D), lambda h, r: (0, 0)),
            any_spec,
            any_spec,
        ],
        out_specs=[any_spec] * 5
        + [
            pl.BlockSpec((PAIR, tokens), lambda h, r: (h, 0)),
            pl.BlockSpec((PAIR, tokens), lambda h, r: (h, 0)),
            pl.BlockSpec((tokens, PAIR), lambda h, r: (0, h)),
            pl.BlockSpec((2, LEN, LEN), lambda h, r: (h * 2 + r, 0, 0)),
            pl.BlockSpec((1, 2, LEN), lambda h, r: (h * 2 + r, 0, 0)),
            pl.BlockSpec((PAIR, LEN), lambda h, r: (h, r)),
            pl.BlockSpec((LEN, PAIR), lambda h, r: (r, h)),
        ],
        out_shape=[
            whole,
            whole,
            jax.ShapeDtypeStruct((tokens, D), b16),
            jax.ShapeDtypeStruct((PAIRS, D, WIDE), b16),
            jax.ShapeDtypeStruct((REST, D, D), b16),
            jax.ShapeDtypeStruct((D, tokens), b16),
            jax.ShapeDtypeStruct((D, tokens), b16),
            jax.ShapeDtypeStruct((tokens, D), b16),
            jax.ShapeDtypeStruct((rows * HEADS, LEN, LEN), b16),
            jax.ShapeDtypeStruct((rows * PAIRS, 2, LEN), f32),
            jax.ShapeDtypeStruct((D, tokens), b16),
            jax.ShapeDtypeStruct((tokens, D), b16),
        ],
        scratch_shapes=[
            pltpu.SMEM((PIECES,), jnp.int32),
            pltpu.VMEM((rows, LEN, D), b16),
            pltpu.VMEM((tokens, D), b16),
            pltpu.VMEM((tokens, PAIR), b16),
            pltpu.VMEM((PAIR, tokens), b16),
            pltpu.VMEM((2, LEN, LEN // 2), f32),
            pltpu.VMEM((CAP, HALF, D), b16),
        ]
        + [pltpu.VMEM((FLOWS, CAP, NEAR, wide * PAIR), b16) for unused, wide in GROUPS]
        + [pltpu.VMEM((FLOWS, 2 * CAP, KEEP, wide * PAIR), b16) for unused, wide in GROUPS]
        + [
            pltpu.VMEM((PAIRS, D, WIDE), b16),
            pltpu.VMEM((FLOWS, 2, PAIRS, KEEP, WIDE), b16),
            pltpu.VMEM((REST, D, D), b16),
            pltpu.VMEM((FLOWS, 2, REST, KEEP, D), b16),
            pltpu.VMEM((3, CAP, SEAT, PAIR), b16),
            pltpu.VMEM((3, CAP, SEAT, PAIR), b16),
            pltpu.VMEM((DIRECT, 3, SEAT, WIDE), b16),
            dma((CHUNKS, FLOWS, 3)),
            dma((CHUNKS, FLOWS, 3)),
            dma((PAIRS, FLOWS, 6)),
            dma((PAIRS, FLOWS, 6)),
            dma((REST, FLOWS, 6)),
            dma((REST, FLOWS, 6)),
            dma((DIRECT, 13)),
            dma((DIRECT, 13)),
            dma((2,)),
            dma((2,)),
            dma((2,)),
            dma((PAIRS + REST + 2,)),
        ],
        compiler_params=pltpu.CompilerParams(
            collective_id=0, has_side_effects=True, vmem_limit_bytes=60 * MIB
        ),
        name="front",
    )(owner, lengths, master, vectors, inputs, cotangent)


class Sum:
    steps = 7

    def __init__(self, place, work, wide, narrow, sems, send_pair, add_own):
        self.place, self.work, self.wide, self.narrow, self.sems = place, work, wide, narrow, sems
        self.send_pair, self.add_own = send_pair, add_own

    def column(self, flow):
        rows = rows_at(self.place.flow(flow)[4], KEEP)

        def read():
            return self.work[:, rows]

        def write(value):
            self.work[:, rows] = value

        sems = (self.sems[0].at[flow, pl.ds(2, 3)], self.sems[1].at[flow, pl.ds(2, 3)])
        land = self.narrow.at[flow, pl.ds(1, 2)]
        return Column(self.place, self.work.at[:, rows], read, write, land, sems)

    def copy(self, flow, index):
        first, second, near, far, keep, give = self.place.flow(flow)
        source, target, device = [
            (self.work.at[:, rows_at(far, NEAR)], self.wide.at[flow], first),
            (self.work.at[:, rows_at(give, KEEP)], self.narrow.at[flow, 0], second),
        ][index]
        return remote(
            source,
            target,
            self.sems[0].at[flow, index],
            self.sems[1].at[flow, index],
            self.place.partners[device],
        )

    def add(self, rows, value):
        self.work[:, rows] = (self.work[:, rows].astype(f32) + value.astype(f32)).astype(b16)

    def step(self, index):
        if index == 0:
            self.send_pair().start()
        if index == 1:
            self.send_pair().wait()
            self.add_own()
        for flow in range(FLOWS):
            first, second, near, far, keep, give = self.place.flow(flow)
            if index == 1:
                self.copy(flow, 0).start()
            if index == 2:
                self.copy(flow, 0).wait()
                self.add(rows_at(near, NEAR), self.wide[flow])
                self.copy(flow, 1).start()
            if index == 3:
                self.copy(flow, 1).wait()
                self.add(rows_at(keep, KEEP), self.narrow[flow, 0])
        if index >= 3:
            columns = [self.column(flow) for flow in range(FLOWS)]
            column_step(self.place, columns, index - 3)


class DirectSum:
    steps = 5

    def __init__(self, place, work, land, sems, send_pair, add_own):
        self.place, self.work, self.land, self.sems = place, work, land, sems
        self.send_pair, self.add_own = send_pair, add_own

    def copies(self, index):
        place = self.place
        here = self.work.at[rows_at(place.seat * SEAT, SEAT)]
        if index == 0:
            sources = [self.work.at[rows_at(seat * SEAT, SEAT)] for seat in place.layer_seats]
        else:
            sources = [here] * 3
        devices = place.column if index == 1 else place.layer
        return [
            remote(
                source,
                self.land.at[index, number],
                self.sems[0].at[3 * index + number],
                self.sems[1].at[3 * index + number],
                device,
            )
            for number, (source, device) in enumerate(zip(sources, devices))
        ]

    def step(self, index):
        rows = rows_at(self.place.seat * SEAT, SEAT)
        if index == 0:
            self.send_pair().start()
        if index == 1:
            self.send_pair().wait()
            self.add_own()
        if index >= 2:
            for copy in self.copies(index - 2):
                copy.wait()
        if 2 <= index <= 3:
            total = self.work[rows].astype(f32)
            for number in range(3):
                total = total + self.land[index - 2, number].astype(f32)
            self.work[rows] = total.astype(b16)
        if 1 <= index <= 3:
            for copy in self.copies(index - 1):
                copy.start()
        if index == 4:
            for number, seat in enumerate(self.place.layer_seats):
                self.work[rows_at(seat * SEAT, SEAT)] = self.land[2, number]


class Hand:
    steps = 2

    def __init__(self, place, table, work, bag, gift, own, out, sems, store_sems):
        self.place, self.table, self.work = place, table, work
        self.bag, self.gift, self.own = bag, gift, own
        self.out, self.sems, self.store_sems = out, sems, store_sems

    def copy(self, number):
        return remote(
            self.bag.at[number],
            self.gift.at[number],
            self.sems[0].at[number],
            self.sems[1].at[number],
            self.place.layer[number],
        )

    def kept(self, seat, flow):
        low, high = lax.rem(seat, 2), seat // 2
        first, second = (low, high) if flow == 0 else (high, low)
        return rows_at(flow * FLOW + first * NEAR + second * KEEP, KEEP)

    def stores(self):
        parts = [(self.own, self.place.seat)]
        parts += [(self.gift.at[number], seat) for number, seat in enumerate(self.place.layer_seats)]
        return [
            pltpu.make_async_copy(
                source.at[flow], self.out.at[:, self.kept(seat, flow)], self.store_sems.at[index, flow]
            )
            for index, (source, seat) in enumerate(parts)
            for flow in range(FLOWS)
        ]

    def step(self, index):
        if index == 0:
            chips = [self.place.me] + self.place.layer_chips
            for number, chip in enumerate(chips):
                for flow in range(FLOWS):
                    rows = self.kept(self.place.seat, flow)
                    for rank in range(CAP):
                        value = self.work[self.table[chip * CAP + rank], rows]
                        if number == 0:
                            self.own[flow, rank] = value
                        else:
                            self.bag[number - 1, flow, rank] = value
                if number > 0:
                    self.copy(number - 1).start()
        if index == 1:
            for number in range(3):
                self.copy(number).wait()
            for copy in self.stores():
                copy.start()


BACK_STEPS = 2 * PAIRS
BACK_TAIL = 4
BACK_REST = (0, 0, 1, 2, 2, 3, 4, 4, 5)
BACK_HAND = 12


def back_kernel(
    table, p_ref, r_ref, v_ref, q_ref, k_ref, o_ref, g_ref, w_ref, n_ref, x_ref, z_ref, vec_ref,
    tiles_in, sums_in, y_in,
    y_out, i_out, pairs_out, slots_out, sums_ref,
    grad_sum, wide_sum, turned, slopes, block_out,
    two, two_wide, two_narrow, two_stage, one, one_land, one_send_stage, one_stage,
    bag, gift, own, vec_land,
    two_send, two_recv, one_send, one_recv, hand_send, hand_recv, hand_store,
    pair_two_send, pair_two_recv, pair_one_send, pair_one_recv, load_sem, store_sem,
    swap_send, swap_recv, swap_local, vec_send, vec_recv,
):
    step = pl.program_id(0)
    place = Place()
    rows, span = y_in.shape[0], y_in.shape[1] // 2
    near_half = rows_at(place.core * HALF, HALF)
    far_half = rows_at(place.other * HALF, HALF)

    def load_two(group):
        first, count = REST_GROUPS[group]
        return pltpu.make_async_copy(
            tiles_in.at[pl.ds(first, count), near_half],
            two_stage.at[pl.ds(group % 3, 1)],
            load_sem.at[group % 3],
        )

    def rest_sum(group):
        first, count = REST_GROUPS[group]
        span_of = pl.ds(first, count)
        work = two.at[span_of]

        def send_pair():
            return remote(
                tiles_in.at[span_of, far_half],
                work,
                pair_two_send.at[group],
                pair_two_recv.at[group],
                place.twin,
            )

        def add_own():
            load_two(group).wait()
            work[...] = (work[...].astype(f32) + two_stage[group % 3].astype(f32)).astype(b16)

        sems = (two_send.at[group], two_recv.at[group])
        wide, narrow = two_wide.at[:, span_of], two_narrow.at[:, :, span_of]
        return Sum(place, work, wide, narrow, sems, send_pair, add_own)

    def pair_sum(index):
        work = one.at[index]

        def send_pair():
            return remote(
                one_send_stage.at[index % 2],
                work,
                pair_one_send.at[index],
                pair_one_recv.at[index],
                place.twin,
            )

        def add_own():
            work[...] = (work[...].astype(f32) + one_stage[index % 2].astype(f32)).astype(b16)

        sems = (one_send.at[index], one_recv.at[index])
        return DirectSum(place, work, one_land.at[index], sems, send_pair, add_own)

    hand = Hand(
        place, table, two, bag, gift, own, slots_out, (hand_send, hand_recv), hand_store
    )

    def pair_store(index, tile):
        return pltpu.make_async_copy(
            one.at[index, :, pl.ds(tile * PAIR, PAIR)],
            pairs_out.at[tile, :, pl.ds(index * PAIR, PAIR)],
            store_sem.at[index, tile],
        )

    def tick(number, odd):
        for group, start in enumerate(BACK_REST):
            if group % 2 == odd and 0 <= number - start < Sum.steps:
                rest_sum(group).step(number - start)
        for index in range(PAIRS):
            since = number - 2 * index - 2
            if index % 2 == odd and 0 <= since < DirectSum.steps:
                pair_sum(index).step(since)
                if since == DirectSum.steps - 1:
                    for tile in range(3):
                        pair_store(index, tile).start()
        if odd == 0 and 0 <= number - BACK_HAND < Hand.steps:
            hand.step(number - BACK_HAND)
        for group, start in enumerate(BACK_REST):
            if odd == 1 and number == max(start - 1, 0):
                load_two(group).start()

    def both(number):
        tick(number, 0)
        tick(number, 1)

    def swap_y(index):
        there = pl.ds(place.core * rows, rows)
        if index == 0:
            return pltpu.make_async_copy(
                y_in.at[:, pl.ds(place.core * span, span)], y_out.at[there], swap_local.at[0]
            )
        return remote(
            y_in.at[:, pl.ds(place.other * span, span)],
            y_out.at[there],
            swap_send.at[0],
            swap_recv.at[0],
            place.twin,
        )

    @pl.when(step == 0)
    def lead():
        place.greet()
        for index in range(2):
            swap_y(index).start()
        sums_ref[...] = sums_in[...]

    for number in range(BACK_STEPS + BACK_TAIL):
        early = partial(tick, number, 0) if number < BACK_STEPS else partial(both, number)
        pl.when(step == number)(early)

    half = LEN // 2
    pair, row = step // 2, lax.rem(step, 2)

    quarter = LEN // 4

    def attention_inputs(head):
        part = slice(head * HEAD_DIM, (head + 1) * HEAD_DIM)
        values = head_only(v_ref[...], head)
        recip = r_ref[0, head : head + 1, :]
        grad = g_ref[part, :].astype(f32) * recip
        delta = jnp.sum(grad * o_ref[part, :].astype(f32), 0, keepdims=True)
        grad = grad.astype(b16)
        return values, grad, delta, jnp.concatenate([grad, grad], axis=0)

    def attention(head):
        part = slice(head * HEAD_DIM, (head + 1) * HEAD_DIM)
        values, grad, delta, doubled = attention_inputs(head)
        units = [(which, block) for which in range(2) for block in range(4)]
        value_grad, key_grad, query_grad = {}, {}, {}

        def raw_block(unit):
            which, block = units[unit]
            cols = slice(which * half, (which + 1) * half)
            return dot_nn(values[block * quarter : (block + 1) * quarter], doubled[:, cols])

        def slope_block(unit, raw):
            which, block = units[unit]
            cols = slice(which * half, (which + 1) * half)
            for small in range(4):
                rows_here = slice(small * 64, (small + 1) * 64)
                rows_all = slice(block * quarter + small * 64, block * quarter + (small + 1) * 64)
                slope = p_ref[head, rows_all, cols].astype(f32) * (raw[rows_here] - delta[:, cols])
                slopes[unit % 2, rows_here] = slope.astype(b16)

        def add(totals, key, term):
            totals[key] = totals[key] + term if key in totals else term

        def grad_block(unit):
            which, block = units[unit]
            cols = slice(which * half, (which + 1) * half)
            rows_all = slice(block * quarter, (block + 1) * quarter)
            slope = slopes[unit % 2]
            add(value_grad, block, dot_nt(grad[:, cols], p_ref[head, rows_all, cols]))
            add(key_grad, block, dot_nt(q_ref[part, cols], slope))
            add(query_grad, which, dot_nn(k_ref[part, rows_all], slope))

        raw = raw_block(0)
        for unit in range(len(units)):
            after = raw_block(unit + 1) if unit + 1 < len(units) else None
            slope_block(unit, raw)
            if unit > 0:
                grad_block(unit - 1)
            raw = after
        grad_block(len(units) - 1)
        for which in range(2):
            total = query_grad[which] * (HEAD_DIM**-0.5)
            turned[part, which * half : (which + 1) * half] = total.astype(b16)
        for block in range(4):
            rows_all = slice(block * quarter, (block + 1) * quarter)
            lower = slice(PAIR + head * HEAD_DIM, PAIR + (head + 1) * HEAD_DIM)
            turned[lower, rows_all] = (key_grad[block] * (1.0 / LOG2E)).astype(b16)
            lower = slice(2 * PAIR + head * HEAD_DIM, 2 * PAIR + (head + 1) * HEAD_DIM)
            turned[lower, rows_all] = value_grad[block].astype(b16)

    @pl.when(step < BACK_STEPS)
    def first_head():
        attention(0)

    for number in range(BACK_STEPS):
        pl.when(step == number)(partial(tick, number, 1))

    @pl.when(step < BACK_STEPS)
    def second_head():
        attention(1)
        where = pl.ds(pl.multiple_of(row * LEN, LEN), LEN)
        block = dot_nn(turned[...], n_ref[where])
        back = turned[...].T
        lanes = pl.ds(pl.multiple_of(pair * PAIR, PAIR), PAIR)
        ones = jnp.sum(back.astype(f32), 0, keepdims=True)
        sums_ref[4:5, lanes] += ones[:, :PAIR]
        sums_ref[5:6, lanes] += ones[:, 2 * PAIR :]
        term = dot_nt(back, w_ref[0])

        @pl.when(pair == 0)
        def begin():
            grad_sum[where] = term

        @pl.when(pair > 0)
        def add():
            grad_sum[where] += term

        @pl.when(row == 0)
        def keep():
            wide_sum[...] = block

        @pl.when(row == 1)
        def hand_on():
            whole = (wide_sum[...] + block).T
            low = whole.astype(b16)
            for core in range(2):

                @pl.when(place.core == core)
                def split():
                    slot = lax.rem(pair, 2)
                    one_stage[slot] = low[core * HALF : (core + 1) * HALF]
                    one_send_stage[slot] = low[(1 - core) * HALF : (2 - core) * HALF]

    def store_block(index):
        row, half = index // 2, index % 2
        target = i_out.at[place.core * rows + row]
        local = pltpu.make_async_copy(block_out.at[half], target, swap_local.at[1 + row])
        far = remote(
            block_out.at[half], target, swap_send.at[1 + row], swap_recv.at[1 + row], place.twin
        )
        return local, far, half

    def wait_block(index):
        local, far, half = store_block(index)

        @pl.when(place.core == half)
        def keep():
            local.wait()

        @pl.when(place.core != half)
        def give():
            far.wait()

    for index in range(BACK_TAIL):

        @pl.when(step == BACK_STEPS + index)
        def close():
            size = LEN // 2
            if index >= 2:
                wait_block(index - 2)
            gain_sum = jnp.zeros((8, D), f32)
            shift_sum = jnp.zeros((8, D), f32)
            for block in range(size // 16):
                rows_here = slice(block * 16, (block + 1) * 16)
                grad = grad_sum[index * size + block * 16 : index * size + (block + 1) * 16]
                unit, rstd = norm_parts(x_ref[rows_here].astype(f32))
                gain_sum = gain_sum + jnp.sum((grad * unit).reshape(-1, 8, D), axis=0)
                shift_sum = shift_sum + jnp.sum(grad.reshape(-1, 8, D), axis=0)
                total = norm_back(grad, unit, rstd, vec_ref[0:1, :])
                block_out[index % 2, rows_here] = (z_ref[rows_here].astype(f32) + total).astype(b16)
            sums_ref[0:1, :] += jnp.sum(gain_sum, 0, keepdims=True)
            sums_ref[1:2, :] += jnp.sum(shift_sum, 0, keepdims=True)
            local, far, half = store_block(index)

            @pl.when(place.core == half)
            def keep():
                local.start()

            @pl.when(place.core != half)
            def give():
                far.start()

    @pl.when(step == BACK_STEPS + BACK_TAIL - 1)
    def drain():
        rounds = [place.layer + [place.twin] + place.layer_twins, place.column]

        def vectors(index):
            base = 7 * index
            return [
                remote(
                    sums_ref,
                    vec_land.at[base + number],
                    vec_send.at[base + number],
                    vec_recv.at[base + number],
                    device,
                )
                for number, device in enumerate(rounds[index])
            ]

        for copy in vectors(0):
            copy.start()
        for index in range(2):
            both(BACK_STEPS + BACK_TAIL + index)
            for copy in vectors(index):
                copy.wait()
            total = sums_ref[...]
            for number in range(len(rounds[index])):
                total = total + vec_land[7 * index + number]
            sums_ref[...] = total
            if index == 0:
                for copy in vectors(1):
                    copy.start()
        for index in range(2):
            swap_y(index).wait()
        for index in range(2, BACK_TAIL):
            wait_block(index)
        for index in range(PAIRS):
            for tile in range(3):
                pair_store(index, tile).wait()
        for copy in hand.stores():
            copy.wait()


def back(table, attention, weights, normed, x, residual, vectors, tiles, sums, y):
    rows, length = y.shape[:2]
    tokens = rows * length
    any_spec = pl.BlockSpec(memory_space=pl.ANY)
    smem = pl.BlockSpec(memory_space=pltpu.SMEM)
    dma = pltpu.SemaphoreType.DMA

    def now(step):
        return jnp.minimum(step, BACK_STEPS - 1)

    def tail(step):
        return jnp.maximum(step - BACK_STEPS, 0)

    head_block = pl.BlockSpec((PAIR, LEN), lambda s: (now(s) // 2, lax.rem(now(s), 2)))
    tail_block = pl.BlockSpec((LEN // 2, D), lambda s: (tail(s), 0))
    whole = pl.BlockSpec((PIECES, D), lambda s: (0, 0))
    sums_block = pl.BlockSpec((16, D), lambda s: (0, 0))
    return pl.pallas_call(
        back_kernel,
        grid=(BACK_STEPS + BACK_TAIL,),
        in_specs=[
            smem,
            pl.BlockSpec((2, LEN, LEN), lambda s: (now(s), 0, 0)),
            pl.BlockSpec((1, 2, LEN), lambda s: (now(s), 0, 0)),
            pl.BlockSpec((LEN, PAIR), lambda s: (lax.rem(now(s), 2), now(s) // 2)),
            head_block,
            head_block,
            head_block,
            head_block,
            pl.BlockSpec((1, D, WIDE), lambda s: (now(s) // 2, 0, 0)),
            pl.BlockSpec((tokens, D), lambda s: (0, 0), pipeline_mode=pl.Buffered(1)),
            tail_block,
            tail_block,
            whole,
            any_spec,
            sums_block,
            any_spec,
        ],
        out_specs=[any_spec] * 4 + [sums_block],
        out_shape=[
            jax.ShapeDtypeStruct((2 * rows, length // 2, D), b16),
            jax.ShapeDtypeStruct((2 * rows, length // 2, D), b16),
            jax.ShapeDtypeStruct((3, HALF, D), b16),
            jax.ShapeDtypeStruct((CAP, HALF, D), b16),
            jax.ShapeDtypeStruct((16, D), f32),
        ],
        scratch_shapes=[
            pltpu.VMEM((tokens, D), f32),
            pltpu.VMEM((WIDE, D), f32),
            pltpu.VMEM((WIDE, LEN), b16),
            pltpu.VMEM((2, LEN // 4, LEN // 2), b16),
            pltpu.VMEM((2, LEN // 2, D), b16),
            pltpu.VMEM((REST, HALF, D), b16),
            pltpu.VMEM((FLOWS, REST, NEAR, D), b16),
            pltpu.VMEM((FLOWS, 3, REST, KEEP, D), b16),
            pltpu.VMEM((3, HALF, D), b16),
            pltpu.VMEM((PAIRS, HALF, WIDE), b16),
            pltpu.VMEM((PAIRS, 3, 3, SEAT, WIDE), b16),
            pltpu.VMEM((2, HALF, WIDE), b16),
            pltpu.VMEM((2, HALF, WIDE), b16),
            pltpu.VMEM((3, FLOWS, CAP, KEEP, D), b16),
            pltpu.VMEM((3, FLOWS, CAP, KEEP, D), b16),
            pltpu.VMEM((FLOWS, CAP, KEEP, D), b16),
            pltpu.VMEM((10, 16, D), f32),
            dma((REST, FLOWS, 5)),
            dma((REST, FLOWS, 5)),
            dma((PAIRS, 9)),
            dma((PAIRS, 9)),
            dma((3,)),
            dma((3,)),
            dma((4, FLOWS)),
            dma((REST,)),
            dma((REST,)),
            dma((PAIRS,)),
            dma((PAIRS,)),
            dma((3,)),
            dma((PAIRS, 3)),
            dma((3,)),
            dma((3,)),
            dma((3,)),
            dma((10,)),
            dma((10,)),
        ],
        compiler_params=pltpu.CompilerParams(
            collective_id=1, has_side_effects=True, vmem_limit_bytes=62 * MIB
        ),
        name="back",
    )(table, *attention, weights, normed, x, residual, vectors, tiles, sums, y)


def update_kernel(tile_at, one, two, w_ref, m_ref, s_ref, y_in, i_in, w_out, m_out, s_out, y_out, i_out):
    step = pl.program_id(0)
    tile = tile_at[step // 2]
    grad = jnp.where(tile < 3, one[0], two[0]).astype(f32)
    parts = adam_step(w_ref[0], grad, m_ref[0], s_ref[0], RATE)
    for target, part in zip((w_out, m_out, s_out), parts):
        target[0] = jnp.where(tile >= 0, part, jnp.zeros_like(part))

    @pl.when(step < 4)
    def widen():
        y_out[...] = y_in[...].astype(f32)
        i_out[...] = i_in[...].astype(f32)


def update(tile_at, one, two, master, first, second, y, grad):
    tokens = y.shape[0]
    size = HALF // 2
    state = pl.BlockSpec((1, size, D), lambda s, tile_at: (s // 2, lax.rem(s, 2), 0))
    wide = pl.BlockSpec((tokens // 4, D), lambda s, tile_at: (jnp.minimum(s, 3), 0))
    return pl.pallas_call(
        update_kernel,
        grid_spec=pltpu.PrefetchScalarGridSpec(
            num_scalar_prefetch=1,
            grid=(CAP * 2,),
            in_specs=[
                pl.BlockSpec(
                    (1, size, D),
                    lambda s, tile_at: (jnp.clip(tile_at[s // 2], 0, 2), lax.rem(s, 2), 0),
                ),
                state,
                state,
                state,
                state,
                wide,
                wide,
            ],
            out_specs=[state] * 3 + [wide] * 2,
        ),
        out_shape=[jax.ShapeDtypeStruct(master.shape, f32)] * 3
        + [jax.ShapeDtypeStruct((tokens, D), f32)] * 2,
        compiler_params=pltpu.CompilerParams(vmem_limit_bytes=60 * MIB),
        name="update",
    )(tile_at, one, two, master, first, second, y, grad)


def shards_paired(
    inputs,
    cotangent,
    doc_lengths,
    owner_list,
    master,
    first_moment,
    second_moment,
    vectors,
    vector_first,
    vector_second,
):
    rows_here, span, width = inputs.shape
    place = lax.axis_index("blk")
    member = lax.axis_index("dp")
    rows_mine = rows_here // 2
    order = jnp.arange(PIECES)
    same_owner = owner_list[:, None] == owner_list[None, :]
    ranks = jnp.sum(same_owner & (order[None, :] < order[:, None]), axis=1).astype(jnp.int32)
    slot_of = owner_list * CAP + ranks
    front_outs = front(owner_list, doc_lengths, master, vectors, inputs, cotangent)
    x, cot, normed, weights_one, weights_two, queries, keys, values = front_outs[:8]
    weights, recips, context_turned, context = front_outs[8:]
    x = x.reshape(-1, width)
    cot = cot.reshape(-1, width)
    block_out, residual, grad_context, sums, tiles_two = feed(
        context, context_turned, x, cot, weights_two, vectors
    )
    hits = jnp.arange(16 * CAP)[:, None] == slot_of[None, :]
    tile_at = jnp.sum(jnp.where(hits, order[None, :] + 1, 0), axis=1).astype(jnp.int32) - 1
    table = jnp.maximum(tile_at - 3, 0)
    block_out, input_grad, total_one, total_two, vector_total = back(
        table,
        (weights, recips, values, queries, keys, context_turned, grad_context),
        weights_one,
        normed,
        x,
        residual,
        vectors,
        tiles_two,
        sums,
        block_out.reshape(rows_mine, LEN, width),
    )
    mine = lax.dynamic_slice_in_dim(tile_at, member * CAP, CAP, 0)
    *updated, block_out, input_grad = update(
        mine,
        total_one,
        total_two,
        master,
        first_moment,
        second_moment,
        block_out.reshape(-1, width),
        input_grad.reshape(-1, width),
    )
    columns = vector_first.shape[1]
    vector_cols = lax.dynamic_slice_in_dim(vectors, place * columns, columns, 1)
    vector_total = lax.dynamic_slice(vector_total, (0, place * columns), (PIECES, columns))
    updated_vectors = adam_step(vector_cols, vector_total, vector_first, vector_second, VEC_RATE)
    return (
        block_out.reshape(inputs.shape),
        input_grad.reshape(inputs.shape),
        *updated,
        *updated_vectors,
    )


def solution(mesh):
    in_specs = (
        P("dp", "blk", None),
        P("dp", "blk", None),
        P("dp", None),
        P(),
        P("dp", "blk", None),
        P("dp", "blk", None),
        P("dp", "blk", None),
        P(),
        P(None, "blk"),
        P(None, "blk"),
    )
    out_specs = (
        P("dp", "blk", None),
        P("dp", "blk", None),
        P("dp", "blk", None),
        P("dp", "blk", None),
        P("dp", "blk", None),
        P(None, "blk"),
        P(None, "blk"),
        P(None, "blk"),
    )
    paired = mesh.shape["blk"] == 2 and mesh.shape["dp"] == 16
    shards = shards_paired if paired else shards_any
    return jax.shard_map(shards, mesh=mesh, in_specs=in_specs, out_specs=out_specs, check_vma=False)
```

```python
from functools import partial

import jax
import jax.numpy as jnp
from jax import lax
from jax.experimental import pallas as pl
from jax.experimental.pallas import tpu as pltpu
from jax.sharding import PartitionSpec as P

D = 768
FF = 3072
HEADS = 12
HEAD_DIM = 64
LEN = 1024
CAP = 3
STEP = 10
PIECES = 12


EPS_NORM = 1e-05
BETA_ONE = 0.9
BETA_TWO = 0.999
RATE = 0.04
VEC_RATE = 0.25
DECAY = 0.01
ADAM_EPS = 1e-08


def normalize(values_in, gain, shift):
    center = jnp.mean(values_in, axis=-1, keepdims=True)
    offset = values_in - center
    spread = jnp.mean(offset * offset, axis=-1, keepdims=True)
    return offset * lax.rsqrt(spread + EPS_NORM) * gain + shift


def adam_step(weight, grad, first, second, rate):
    first_new = BETA_ONE * first + (1.0 - BETA_ONE) * grad
    second_new = BETA_TWO * second + (1.0 - BETA_TWO) * grad * grad
    corrected = (
        first_new
        / (1.0 - BETA_ONE**STEP)
        / (jnp.sqrt(second_new / (1.0 - BETA_TWO**STEP)) + ADAM_EPS)
    )
    return (weight - rate * (corrected + DECAY * weight), first_new, second_new)


def shards_any(
    inputs,
    cotangent,
    doc_lengths,
    owner_list,
    master,
    first_moment,
    second_moment,
    vectors,
    vector_first,
    vector_second,
):
    rows_here, span, width = inputs.shape
    tokens_here = rows_here * span
    fold = FF // D
    scale = HEAD_DIM ** (-0.5)
    place = lax.axis_index("blk")
    f32 = jnp.float32
    b16 = jnp.bfloat16
    order = jnp.arange(PIECES)
    same_owner = owner_list[:, None] == owner_list[None, :]
    ranks = jnp.sum(same_owner & (order[None, :] < order[:, None]), axis=1)
    slot_of = owner_list * CAP + ranks

    mine = (owner_list == lax.axis_index("dp"))[:, None, None]
    tile_rows = lax.psum(jnp.where(mine, master[ranks], 0.0).astype(b16), "dp")
    tiles = lax.all_gather(tile_rows, "blk", axis=1, tiled=True)
    query_weight = tiles[0]
    key_weight = tiles[1]
    value_weight = tiles[2]
    out_weight = tiles[3]
    up_weight = jnp.transpose(tiles[4 : 4 + fold], (1, 0, 2)).reshape(width, FF)
    down_weight = tiles[4 + fold :].reshape(FF, width)
    flat_in = inputs.reshape(tokens_here, width).astype(f32)
    normed_one = normalize(flat_in, vectors[0], vectors[1]).astype(b16)
    queries = (jnp.dot(normed_one, query_weight, preferred_element_type=f32) + vectors[4]).astype(
        b16
    )
    keys_here = jnp.dot(normed_one, key_weight, preferred_element_type=f32).astype(b16)
    values_here = (
        jnp.dot(normed_one, value_weight, preferred_element_type=f32) + vectors[5]
    ).astype(b16)
    query_heads = queries.reshape(rows_here, span, HEADS, HEAD_DIM)
    first_len = doc_lengths[:, 0]
    query_seg = (place * span + jnp.arange(span))[None, :] >= first_len[:, None]

    def block_scores(key_block, start):
        count = key_block.shape[1]
        key_heads = key_block.reshape(rows_here, count, HEADS, HEAD_DIM)
        raw = (
            jnp.einsum("rqhd,rkhd->rhqk", query_heads, key_heads, preferred_element_type=f32)
            * scale
        )
        key_seg = (start + jnp.arange(count))[None, :] >= first_len[:, None]
        allowed = query_seg[:, None, :, None] == key_seg[:, None, None, :]
        return (raw, allowed)

    key_rows = keys_here.reshape(rows_here, span, width)
    value_rows = values_here.reshape(rows_here, span, width)
    top = jnp.full((rows_here, HEADS, span), -1e30, f32)
    key_block = lax.all_gather(key_rows, "blk", axis=1, tiled=True)
    value_block = lax.all_gather(value_rows, "blk", axis=1, tiled=True)
    count = key_block.shape[1]
    raw, allowed = block_scores(key_block, jnp.int32(0))
    new_top = jnp.maximum(top, jnp.max(jnp.where(allowed, raw, -1e30), axis=-1))
    weights = jnp.where(allowed, jnp.exp(raw - new_top[..., None]), 0.0)
    value_heads = value_block.reshape(rows_here, count, HEADS, HEAD_DIM)
    update = jnp.einsum(
        "rhqk,rkhd->rhqd", weights.astype(b16), value_heads, preferred_element_type=f32
    )
    total = jnp.sum(weights, axis=-1)
    log_total = new_top + jnp.log(total)
    context_raw = update / total[..., None]
    context_low = jnp.transpose(context_raw, (0, 2, 1, 3)).reshape(tokens_here, width).astype(b16)
    residual = flat_in + (jnp.dot(context_low, out_weight, preferred_element_type=f32) + vectors[6])
    normed_two = normalize(residual, vectors[2], vectors[3]).astype(b16)
    hidden = jnp.dot(normed_two, up_weight, preferred_element_type=f32) + vectors[8:].reshape(FF)
    gelu_exact = partial(jax.nn.gelu, approximate=False)
    active, gelu_pull = jax.vjp(gelu_exact, hidden)
    active_low = active.astype(b16)
    block_out = (
        residual + (jnp.dot(active_low, down_weight, preferred_element_type=f32) + vectors[7])
    ).reshape(rows_here, span, width)
    grad_out = cotangent.reshape(tokens_here, width)
    down_grad = jnp.einsum("tf,td->fd", active_low, grad_out, preferred_element_type=f32)
    down_sum = jnp.sum(grad_out, axis=0, dtype=f32)
    grad_active = jnp.einsum("td,fd->tf", grad_out, down_weight, preferred_element_type=f32)
    grad_hidden = gelu_pull(grad_active)[0].astype(b16)
    up_grad = jnp.einsum("td,tf->df", normed_two, grad_hidden, preferred_element_type=f32)
    up_sum = jnp.sum(grad_hidden, axis=0, dtype=f32)
    ffn_tiles = jnp.concatenate(
        [
            jnp.transpose(up_grad.reshape(width, fold, width), (1, 0, 2)),
            down_grad.reshape(fold, width, width),
        ],
        axis=0,
    )
    grad_normed_two = jnp.einsum("tf,df->td", grad_hidden, up_weight, preferred_element_type=f32)
    unused, second_pull = jax.vjp(normalize, residual, vectors[2], vectors[3])
    residual_part, gain_two_grad, shift_two_grad = second_pull(grad_normed_two)
    grad_residual = grad_out.astype(f32) + residual_part
    grad_attended = grad_residual.astype(b16)
    out_grad = jnp.einsum("tm,td->md", context_low, grad_attended, preferred_element_type=f32)
    out_sum = jnp.sum(grad_attended, axis=0, dtype=f32)
    grad_context = jnp.einsum(
        "td,md->tm", grad_attended, out_weight, preferred_element_type=f32
    ).astype(b16)
    grad_heads = grad_context.reshape(rows_here, span, HEADS, HEAD_DIM)
    delta = jnp.einsum("rqhd,rhqd->rhq", grad_heads.astype(f32), context_raw)
    key_all, value_all = (
        lax.all_gather(key_rows, "blk", axis=1, tiled=True),
        lax.all_gather(value_rows, "blk", axis=1, tiled=True),
    )
    key_size = min(512, LEN)

    def back_block(index, carry):
        grad_query, key_total, value_total = carry
        start = index * key_size
        key_block = lax.dynamic_slice_in_dim(key_all, start, key_size, 1)
        value_block = lax.dynamic_slice_in_dim(value_all, start, key_size, 1)
        raw, allowed = block_scores(key_block, start)
        weights_back = jnp.where(allowed, jnp.exp(raw - log_total[..., None]), 0.0)
        key_heads = key_block.reshape(rows_here, key_size, HEADS, HEAD_DIM)
        value_heads = value_block.reshape(rows_here, key_size, HEADS, HEAD_DIM)
        value_grad = jnp.einsum(
            "rhqk,rqhd->rkhd", weights_back.astype(b16), grad_heads, preferred_element_type=f32
        )
        weight_grad = jnp.einsum(
            "rqhd,rkhd->rhqk", grad_heads, value_heads, preferred_element_type=f32
        )
        score_grad = (weights_back * (weight_grad - delta[..., None])).astype(b16)
        grad_query = (
            grad_query
            + jnp.einsum("rhqk,rkhd->rqhd", score_grad, key_heads, preferred_element_type=f32)
            * scale
        )
        key_grad = (
            jnp.einsum("rhqk,rqhd->rkhd", score_grad, query_heads, preferred_element_type=f32)
            * scale
        )
        key_total = lax.dynamic_update_slice_in_dim(
            key_total, key_grad.reshape(rows_here, key_size, width), start, 1
        )
        value_total = lax.dynamic_update_slice_in_dim(
            value_total, value_grad.reshape(rows_here, key_size, width), start, 1
        )
        return (grad_query, key_total, value_total)

    zero_rows = jnp.zeros((rows_here, LEN, width), f32)
    grad_query, key_total, value_total = lax.fori_loop(
        0,
        LEN // key_size,
        back_block,
        (jnp.zeros((rows_here, span, HEADS, HEAD_DIM), f32), zero_rows, zero_rows),
    )
    key_grad_here, value_grad_here = (
        lax.psum_scatter(
            key_total.astype(jnp.bfloat16), "blk", scatter_dimension=1, tiled=True
        ).astype(jnp.float32),
        lax.psum_scatter(
            value_total.astype(jnp.bfloat16), "blk", scatter_dimension=1, tiled=True
        ).astype(jnp.float32),
    )
    query_low = grad_query.reshape(tokens_here, width).astype(b16)
    key_low = key_grad_here.reshape(tokens_here, width).astype(b16)
    value_low = value_grad_here.reshape(tokens_here, width).astype(b16)
    query_tile = jnp.einsum("td,te->de", normed_one, query_low, preferred_element_type=f32)
    key_tile = jnp.einsum("td,te->de", normed_one, key_low, preferred_element_type=f32)
    value_tile = jnp.einsum("td,te->de", normed_one, value_low, preferred_element_type=f32)
    grad_normed_one = (
        jnp.einsum("te,de->td", query_low, query_weight, preferred_element_type=f32)
        + jnp.einsum("te,de->td", key_low, key_weight, preferred_element_type=f32)
        + jnp.einsum("te,de->td", value_low, value_weight, preferred_element_type=f32)
    )
    unused, first_pull = jax.vjp(normalize, flat_in, vectors[0], vectors[1])
    input_part, gain_one_grad, shift_one_grad = first_pull(grad_normed_one)
    input_grad = (grad_residual + input_part).reshape(rows_here, span, width)
    vector_grads = jnp.concatenate(
        [
            jnp.stack(
                [
                    gain_one_grad,
                    shift_one_grad,
                    gain_two_grad,
                    shift_two_grad,
                    jnp.sum(query_low, axis=0, dtype=f32),
                    jnp.sum(value_low, axis=0, dtype=f32),
                    out_sum,
                    down_sum,
                ]
            ),
            up_sum.reshape(fold, width),
        ],
        axis=0,
    )
    attn_tiles = jnp.stack([query_tile, key_tile, value_tile, out_grad])
    piece_share, vector_share = (
        lax.psum_scatter(
            jnp.concatenate([attn_tiles, ffn_tiles], axis=0).astype(jnp.bfloat16),
            "blk",
            scatter_dimension=1,
            tiled=True,
        ).astype(jnp.float32),
        lax.psum_scatter(
            vector_grads.astype(jnp.bfloat16), "blk", scatter_dimension=1, tiled=True
        ).astype(jnp.float32),
    )
    own_slots = lax.axis_index("dp") * CAP + jnp.arange(CAP)
    pick = (own_slots[:, None] == slot_of[None, :]).astype(f32)
    occupied = jnp.sum(pick, axis=1)[:, None, None]
    total_share, vector_total = (
        lax.psum(piece_share.astype(jnp.bfloat16), "dp").astype(jnp.float32),
        lax.psum(vector_share.astype(jnp.bfloat16), "dp").astype(jnp.float32),
    )
    slot_grads = jnp.einsum("cp,prd->crd", pick, total_share, precision=lax.Precision.HIGHEST)
    new_master, new_first, new_second = adam_step(
        master, slot_grads, first_moment, second_moment, RATE
    )
    columns = vector_first.shape[1]
    vector_cols = lax.dynamic_slice_in_dim(vectors, place * columns, columns, 1)
    new_vectors, new_vector_first, new_vector_second = adam_step(
        vector_cols, vector_total, vector_first, vector_second, VEC_RATE
    )
    return (
        block_out,
        input_grad,
        new_master * occupied,
        new_first * occupied,
        new_second * occupied,
        new_vectors,
        new_vector_first,
        new_vector_second,
    )


f32 = jnp.float32
b16 = jnp.bfloat16
LOG2E = 1.4426950408889634
MIB = 1024 * 1024
PAIRS = HEADS // 2
PAIR = 2 * HEAD_DIM


def dot_nn(left, right):
    return lax.dot_general(left, right, (((1,), (0,)), ((), ())), preferred_element_type=f32)


def dot_nt(left, right):
    return lax.dot_general(left, right, (((1,), (1,)), ((), ())), preferred_element_type=f32)


def dot_tn(left, right):
    return lax.dot_general(left, right, (((0,), (0,)), ((), ())), preferred_element_type=f32)


def norm_parts(values_in):
    center = jnp.mean(values_in, axis=-1, keepdims=True)
    offset = values_in - center
    spread = jnp.mean(offset * offset, axis=-1, keepdims=True)
    rstd = lax.rsqrt(spread + EPS_NORM)
    return offset * rstd, rstd


def norm_back(grad, unit, rstd, gain):
    scaled = grad * gain
    first = jnp.mean(scaled, axis=-1, keepdims=True)
    second = jnp.mean(scaled * unit, axis=-1, keepdims=True)
    return rstd * (scaled - first - unit * second)


def gelu_parts(value):
    bell = jnp.exp2(value * value * (-0.5 * LOG2E))
    ratio = pl.reciprocal(1.0 + (0.3275911 * 0.7071067811865476) * jnp.abs(value))
    poly = 0.5 * 1.061405429
    poly = poly * ratio + 0.5 * -1.453152027
    poly = poly * ratio + 0.5 * 1.421413741
    poly = poly * ratio + 0.5 * -0.284496736
    poly = poly * ratio + 0.5 * 0.254829592
    tail = poly * ratio * bell
    cdf = jnp.where(value >= 0.0, 1.0 - tail, tail)
    return value * cdf, cdf + value * (bell * 0.3989422804014327)


def head_only(block, head):
    lane = lax.broadcasted_iota(jnp.int32, block.shape, 1)
    keep = (lane >= head * HEAD_DIM) & (lane < (head + 1) * HEAD_DIM)
    return jnp.where(keep, block, jnp.zeros_like(block))


def feed_kernel(
    c_ref, o_ref, x_ref, g_ref, w_ref, vec_ref,
    y_ref, r_ref, d_ref, sums_ref, tiles_ref,
    acc_ref, unit_ref, rstd_ref, normed, out_ref, grad_ref,
    hidden_ref, pulled_ref, active_ref, slope_ref, stage_ref, sem_ref,
):
    fold = FF // D
    step = pl.program_id(0)
    blocks = [slice(start, start + 16) for start in range(0, x_ref.shape[0], 16)]

    @pl.when(step == 0)
    def clear():
        acc_ref[...] = jnp.zeros_like(acc_ref)
        sums_ref[...] = jnp.zeros_like(sums_ref)

    def eights(value):
        return jnp.sum(value.reshape(-1, 8, D), axis=0)

    def add_sum(row, value):
        sums_ref[row : row + 1, :] += jnp.sum(value, 0, keepdims=True)

    out_ref[...] = dot_nn(c_ref[...], w_ref[0])
    gain = vec_ref[2:3, :]
    for rows in blocks:
        residual = x_ref[rows].astype(f32) + (out_ref[rows] + vec_ref[6:7, :])
        unit, rstd = norm_parts(residual)
        unit_ref[rows] = unit.astype(b16)
        rstd_ref[rows] = jnp.broadcast_to(rstd, (16, 128))
        normed[rows] = (unit * gain + vec_ref[3:4, :]).astype(b16)
        out_ref[rows] = residual + vec_ref[7:8, :]
    turned = normed[...].T
    cot = g_ref[...]

    def begin(part):
        def hidden():
            hidden_ref[part % 2] = dot_nn(normed[...], w_ref[1 + part])

        def pulled():
            pulled_ref[part % 2] = dot_nt(cot, w_ref[1 + fold + part])

        return [hidden, pulled]

    def end(part):
        slot = part % 2

        def out():
            out_ref[...] += dot_nn(active_ref[slot], w_ref[1 + fold + part])

        def back():
            grad = dot_nt(slope_ref[slot], w_ref[1 + part])
            grad_ref[...] = grad if part == 0 else grad_ref[...] + grad

        def up():
            acc_ref[1 + part] += dot_nn(turned, slope_ref[slot])

        def down():
            acc_ref[1 + fold + part] += dot_tn(active_ref[slot], cot)

        return [out, back, up, down]

    for work in begin(0):
        work()
    for part in range(fold):
        slot = part % 2
        work = end(part - 1) if part > 0 else []
        work = work + (begin(part + 1) if part + 1 < fold else [])
        total = jnp.zeros((8, D), f32)
        for index, rows in enumerate(blocks):
            if index * len(work) // len(blocks) != (index - 1) * len(work) // len(blocks):
                work[index * len(work) // len(blocks)]()
            active, slope = gelu_parts(hidden_ref[slot, rows] + vec_ref[8 + part : 9 + part, :])
            active_ref[slot, rows] = active.astype(b16)
            pulled = (pulled_ref[slot, rows] * slope).astype(b16)
            slope_ref[slot, rows] = pulled
            total = total + eights(pulled.astype(f32))
        add_sum(8 + part, total)
    for work in end(fold - 1):
        work()
    y_ref[...] = out_ref[...].astype(b16)
    totals = [jnp.zeros((8, D), f32) for unused in range(4)]
    for rows in blocks:
        grad, unit, wide = grad_ref[rows], unit_ref[rows].astype(f32), g_ref[rows].astype(f32)
        back = wide + norm_back(grad, unit, rstd_ref[rows, 0:1], gain)
        low = back.astype(b16)
        r_ref[rows] = low
        terms = (grad * unit, grad, low.astype(f32), wide)
        totals = [total + eights(term) for total, term in zip(totals, terms)]
    for row, total in zip((2, 3, 6, 7), totals):
        add_sum(row, total)
    low = r_ref[...]
    d_ref[...] = dot_nt(w_ref[0], low).astype(b16)
    acc_ref[0] += dot_nn(o_ref[...], low)

    @pl.when(step == pl.num_programs(0) - 1)
    def send():
        for part in range(1 + 2 * fold):
            stage_ref[0] = acc_ref[part].astype(b16)
            copy = pltpu.make_async_copy(stage_ref.at[0], tiles_ref.at[part], sem_ref.at[0])
            copy.start()
            copy.wait()


def feed(context, turned, x, cot, weights, vectors):
    tokens = x.shape[0]
    size = 512
    count = 1 + 2 * (FF // D)
    token_block = pl.BlockSpec((size, D), lambda i: (i, 0))
    turned_block = pl.BlockSpec((D, size), lambda i: (0, i))
    return pl.pallas_call(
        feed_kernel,
        grid=(tokens // size,),
        in_specs=[
            pl.BlockSpec((size, D), lambda i: (i, 0), pipeline_mode=pl.Buffered(1)),
            pl.BlockSpec((D, size), lambda i: (0, i), pipeline_mode=pl.Buffered(1)),
            pl.BlockSpec((size, D), lambda i: (i, 0), pipeline_mode=pl.Buffered(1)),
            token_block,
            pl.BlockSpec((count, D, D), lambda i: (0, 0, 0), pipeline_mode=pl.Buffered(1)),
            pl.BlockSpec((PIECES, D), lambda i: (0, 0)),
        ],
        out_specs=[
            token_block,
            token_block,
            turned_block,
            pl.BlockSpec((16, D), lambda i: (0, 0)),
            pl.BlockSpec(memory_space=pl.ANY),
        ],
        out_shape=[
            jax.ShapeDtypeStruct((tokens, D), b16),
            jax.ShapeDtypeStruct((tokens, D), b16),
            jax.ShapeDtypeStruct((D, tokens), b16),
            jax.ShapeDtypeStruct((16, D), f32),
            jax.ShapeDtypeStruct((count, D, D), b16),
        ],
        scratch_shapes=[
            pltpu.VMEM((count, D, D), f32),
            pltpu.VMEM((size, D), b16),
            pltpu.VMEM((size, 128), f32),
            pltpu.VMEM((size, D), b16),
            pltpu.VMEM((size, D), f32),
            pltpu.VMEM((size, D), f32),
            pltpu.VMEM((2, size, D), f32),
            pltpu.VMEM((2, size, D), f32),
            pltpu.VMEM((2, size, D), b16),
            pltpu.VMEM((2, size, D), b16),
            pltpu.VMEM((1, D, D), b16),
            pltpu.SemaphoreType.DMA((1,)),
        ],
        compiler_params=pltpu.CompilerParams(vmem_limit_bytes=60 * MIB),
        cost_estimate=pl.CostEstimate(
            flops=6 * count * tokens * D * D,
            bytes_accessed=18 * tokens * D + 4 * count * D * D,
            transcendentals=2 * tokens * FF,
        ),
        name="feed",
    )(context, turned, x, cot, weights, vectors)


MESH = pl.DeviceIdType.MESH
HALF = D // 2
FLOWS = 2
FLOW = HALF // FLOWS
NEAR = FLOW // 2
KEEP = NEAR // 2
WIDE = 3 * PAIR
REST = PIECES - 3
GROUPS = ((0, 1), (1, 2), (3, 3))
CHUNKS = len(GROUPS)


class Place:
    def __init__(self):
        self.me = lax.axis_index("dp")
        self.core = lax.axis_index("blk")
        self.bits = [lax.rem(self.me // weight, 2) for weight in (1, 2, 4, 8)]
        self.chips = [
            self.me + weight - 2 * weight * bit for weight, bit in zip((1, 2, 4, 8), self.bits)
        ]
        self.partners = [{"dp": chip} for chip in self.chips]
        low, high = self.bits[2:]
        self.inner = low != high
        self.across = {"dp": self.me + 4 - 8 * low + 8 - 16 * high}
        self.other = 1 - self.core
        self.twin = {"blk": self.other}

    def greet(self):
        barrier = pltpu.get_barrier_semaphore()
        for device in self.partners + [self.across, self.twin]:
            pl.semaphore_signal(barrier, 1, device_id=device, device_id_type=MESH)
        pl.semaphore_wait(barrier, 6)

    def flow(self, index):
        first, second = (0, 1) if index == 0 else (1, 0)
        base = index * FLOW
        near = base + self.bits[first] * NEAR
        far = base + NEAR - self.bits[first] * NEAR
        keep = near + self.bits[second] * KEEP
        give = near + KEEP - self.bits[second] * KEEP
        return first, second, near, far, keep, give


def remote(source, target, send, receive, device):
    return pltpu.make_async_remote_copy(
        src_ref=source,
        dst_ref=target,
        send_sem=send,
        recv_sem=receive,
        device_id=device,
        device_id_type=MESH,
    )


def rows_at(start, count):
    return pl.ds(pl.multiple_of(start, 16), count)


class Spread:
    def __init__(self, place, owner, rank, slots, land, gift, sems):
        self.place, self.owner, self.rank = place, owner, rank
        self.slots, self.land, self.gift, self.sems = slots, land, gift, sems

    def cols(self, chunk):
        return pl.ds(GROUPS[chunk][0] * PAIR, GROUPS[chunk][1] * PAIR)

    def first_copy(self, chunk, index):
        first, second, near, far, keep, give = self.place.flow(index)
        return remote(
            self.slots.at[:, rows_at(far, NEAR), self.cols(chunk)],
            self.land[chunk].at[index],
            self.sems[0].at[chunk, index, 0],
            self.sems[1].at[chunk, index, 0],
            self.place.partners[first],
        )

    def second_copy(self, chunk, index, which):
        first, second, near, far, keep, give = self.place.flow(index)
        if which == 0:
            source = self.slots.at[:, rows_at(give, KEEP), self.cols(chunk)]
        else:
            source = self.land[chunk].at[index, :, rows_at(give - near, KEEP)]
        return remote(
            source,
            self.gift[chunk].at[index, pl.ds(which * CAP, CAP)],
            self.sems[0].at[chunk, index, 1 + which],
            self.sems[1].at[chunk, index, 1 + which],
            self.place.partners[second],
        )

    def step(self, chunk, index):
        for flow in range(FLOWS):
            if index == 0:
                self.first_copy(chunk, flow).start()
                self.second_copy(chunk, flow, 0).start()
            if index == 1:
                self.first_copy(chunk, flow).wait()
                self.second_copy(chunk, flow, 1).start()
            if index == 2:
                self.second_copy(chunk, flow, 0).wait()
                self.second_copy(chunk, flow, 1).wait()

    def piece(self, tile, index, chunk, start, count):
        first, second, near, far, keep, give = self.place.flow(index)
        owner, rank = self.owner[tile], self.rank[tile]
        bits = [lax.rem(owner, 2), lax.rem(owner // 2, 2)]
        apart = [bit != mine for bit, mine in zip(bits, self.place.bits)]
        cols = pl.ds(start, count)
        mine = self.slots[rank, rows_at(keep, KEEP), pl.ds(GROUPS[chunk][0] * PAIR + start, count)]
        firsts = self.land[chunk][index, rank, rows_at(keep - near, KEEP), cols]
        gifts = self.gift[chunk][index, jnp.where(apart[first], CAP, 0) + rank, :, cols]
        value = jnp.where(apart[second], gifts, jnp.where(apart[first], firsts, mine))
        layer = owner // 4 == self.place.me // 4
        return jnp.where(layer, value, jnp.zeros_like(value))


class Column:
    steps = 4

    def __init__(self, place, kept, read, write, land, sems):
        self.place, self.kept, self.read, self.write = place, kept, read, write
        self.land, self.sems = land, sems

    def copy(self, index):
        target = self.land.at[index % 2]
        device = self.place.across if index == 1 else self.place.partners[2]
        return remote(
            self.kept, target, self.sems[0].at[index], self.sems[1].at[index], device
        )

    def add(self, index):
        self.write((self.read().astype(f32) + self.land[index].astype(f32)).astype(b16))


def column_step(place, columns, index):
    @pl.when(place.inner)
    def inner():
        for column in columns:
            if index == 1:
                column.copy(0).wait_recv()
                column.add(0)
                column.copy(1).start()
            if index == 2:
                column.copy(1).wait()
                column.add(1)
                column.copy(2).start()
            if index == 3:
                column.copy(2).wait_send()

    @pl.when(jnp.logical_not(place.inner))
    def outer():
        for column in columns:
            if index == 0:
                column.copy(0).start()
            if index == 1:
                column.copy(0).wait_send()
            if index == 3:
                column.copy(2).wait_recv()
                column.write(column.land[0])


class Item:
    steps = 8

    def __init__(self, place, work, land, sems, load, store=None):
        self.place, self.work, self.land, self.sems = place, work, land, sems
        self.load, self.store = load, store
        self.base = place.core * HALF

    def column(self, flow):
        rows = rows_at(self.base + self.place.flow(flow)[4], KEEP)

        def read():
            return self.work[:, rows]

        def write(value):
            self.work[:, rows] = value

        sems = (self.sems[0].at[flow], self.sems[1].at[flow])
        return Column(self.place, self.work.at[:, rows], read, write, self.land.at[flow], sems)

    def copy(self, flow, index):
        first, second, near, far, keep, give = self.place.flow(flow)
        kept = self.work.at[:, rows_at(self.base + keep, KEEP)]
        half = self.work.at[:, rows_at(self.base + near, NEAR)]
        source, device = [
            (kept, self.place.partners[second]),
            (half, self.place.partners[first]),
        ][index]
        return remote(
            source, source, self.sems[0].at[flow, 3 + index], self.sems[1].at[flow, 3 + index], device
        )

    def pair(self):
        rows = self.work.at[:, rows_at(self.base, HALF)]
        return remote(rows, rows, self.sems[0].at[0, 5], self.sems[1].at[0, 5], self.place.twin)

    def step(self, index):
        for flow in range(FLOWS):
            if index == 0:
                self.load(self.work, rows_at(self.base + self.place.flow(flow)[4], KEEP), flow)
        if index <= 3:
            column_step(self.place, [self.column(flow) for flow in range(FLOWS)], index)
        for flow in range(FLOWS):
            if 5 <= index <= 6:
                self.copy(flow, index - 5).wait()
            if 4 <= index <= 5:
                self.copy(flow, index - 4).start()
        if index == 6:
            self.pair().start()
        if index == 7:
            self.pair().wait()
            self.store().start()


REST_GROUPS = tuple((index, 1) for index in range(REST))
PAIR_CHUNK = (0, 1, 1, 2, 2, 2)
FRONT_PAIRS = tuple((begin, begin + 3, 1) for begin in (2, 4, 5, 6, 7, 8))
FRONT_REST = (
    (6, 9, 2), (6, 9, 2), (7, 10, 2), (7, 11, 2), (8, 12, 2), (8, 13, 2), (9, 14, 2), (10, 15, 2), (11, 15, 2)
)
FRONT_LEAD = 9


def front_kernel(
    owner, lengths, master, vec_ref, x_in, c_in,
    x_out, c_out, n_out, one_out, two_out, q_ref, k_ref, v_ref, p_ref, r_ref, o_ref, ctx_ref,
    rank, rows_ref, normed, keys, turned_values, scores, slots,
    land_one, land_two, land_three, gift_one, gift_two, gift_three,
    one, one_land, two, two_land,
    spread_send, spread_recv, one_send, one_recv, two_send, two_recv,
    swap_send, swap_recv, swap_local, store_sem,
):
    pair = pl.program_id(0)
    row = pl.program_id(1)
    grid_step = pair * 2 + row
    place = Place()
    rows, span = x_in.shape[0] // 2, x_in.shape[1]
    land = (land_one, land_two, land_three)
    gift = (gift_one, gift_two, gift_three)
    spread = Spread(place, owner, rank, slots, land, gift, (spread_send, spread_recv))

    def swaps(index):
        source, target = [(x_in, rows_ref), (c_in, c_out)][index]
        here = pl.ds(place.core * span, span)
        near = pltpu.make_async_copy(
            source.at[pl.ds(place.core * rows, rows)], target.at[:, here], swap_local.at[index]
        )
        far = remote(
            source.at[pl.ds(place.other * rows, rows)],
            target.at[:, here],
            swap_send.at[index],
            swap_recv.at[index],
            place.twin,
        )
        return near, far

    def row_store():
        return pltpu.make_async_copy(rows_ref, x_out, store_sem.at[PAIRS + REST])

    def normed_store():
        return pltpu.make_async_copy(normed, n_out, store_sem.at[PAIRS + REST + 1])

    def pair_item(group):
        span_of = pl.ds(group, 1)

        def load(work, where, flow):
            chunk = PAIR_CHUNK[group]
            for tile in range(3):
                part = spread.piece(tile, flow, chunk, (group - GROUPS[chunk][0]) * PAIR, PAIR)
                work[0, where, pl.ds(tile * PAIR, PAIR)] = part

        def store():
            return pltpu.make_async_copy(one.at[span_of], one_out.at[span_of], store_sem.at[group])

        sems = (one_send.at[group], one_recv.at[group])
        return Item(place, one.at[span_of], one_land.at[:, :, span_of], sems, load, store)

    def rest_item(group):
        first, count = REST_GROUPS[group]
        span_of = pl.ds(first, count)

        def load(work, where, flow):
            for index in range(count):
                for chunk, (start, wide) in enumerate(GROUPS):
                    part = spread.piece(3 + first + index, flow, chunk, 0, wide * PAIR)
                    work[index, where, pl.ds(start * PAIR, wide * PAIR)] = part

        def store():
            return pltpu.make_async_copy(
                two.at[span_of], two_out.at[span_of], store_sem.at[PAIRS + group]
            )

        sems = (two_send.at[group], two_recv.at[group])
        return Item(place, two.at[span_of], two_land.at[:, :, span_of], sems, load, store)

    def tick(number, odd):
        for chunk in range(CHUNKS):
            if odd == 0 and 0 <= number - 2 * chunk <= 2:
                spread.step(chunk, number - 2 * chunk)
        starts = [(pair_item, group, start) for group, start in enumerate(FRONT_PAIRS)]
        starts += [(rest_item, group, start) for group, start in enumerate(FRONT_REST)]
        for make, group, (begin, gather, pace) in starts:
            ticks = [begin, begin + 1, begin + 2, begin + 3]
            ticks += [gather, gather + pace, gather + 2 * pace, gather + 2 * pace + 1]
            for index, when in enumerate(ticks):
                if group % 2 == odd and number == when:
                    make(group).step(index)

    def both(number):
        tick(number, 0)
        tick(number, 1)

    @pl.when(grid_step == 0)
    def lead():
        slots[...] = master[...].astype(b16)
        for tile in range(PIECES):
            count = jnp.int32(0)
            for before in range(tile):
                count = count + (owner[before] == owner[tile]).astype(jnp.int32)
            rank[tile] = jnp.minimum(count, CAP - 1)
        place.greet()
        for copy in swaps(0):
            copy.start()
        both(0)
        for copy in swaps(1):
            copy.start()
        for copy in swaps(0):
            copy.wait()
        row_store().start()

        def norm_rows(index, carry):
            for part in range(rows):
                for block in range(4):
                    where = pl.ds(pl.multiple_of(index * 128 + block * 32, 32), 32)
                    unit, unused = norm_parts(rows_ref[part, where].astype(f32))
                    low = (unit * vec_ref[0:1, :] + vec_ref[1:2, :]).astype(b16)
                    normed[pl.ds(pl.multiple_of(part * LEN + index * 128 + block * 32, 32), 32)] = low
            return carry

        both(1)
        lax.fori_loop(0, LEN // 128, norm_rows, 0)
        normed_store().start()
        for number in range(2, FRONT_LEAD):
            both(number)

    for number in range(2 * PAIRS):
        pl.when(grid_step == number)(partial(tick, FRONT_LEAD + number, 0))

    @pl.when(row == 0)
    def project():
        lanes = pl.ds(pl.multiple_of(pair * PAIR, PAIR), PAIR)
        weight = one[pair]

        def part(index, carry):
            where = pl.ds(pl.multiple_of(index * 512, 512), 512)
            both = dot_nn(normed[where], weight)
            queries = both[:, :PAIR] + vec_ref[4:5, lanes]
            queries = (queries * (HEAD_DIM**-0.5 * LOG2E)).astype(b16)
            q_ref[:, where] = queries.T
            low = both[:, PAIR : 2 * PAIR].astype(b16)
            keys[where] = low
            k_ref[:, where] = low.T
            values = (both[:, 2 * PAIR :] + vec_ref[5:6, lanes]).astype(b16)
            v_ref[where] = values
            turned_values[:, where] = values.T
            return carry

        lax.fori_loop(0, normed.shape[0] // 512, part, 0)

    half = LEN // 2
    start = pl.multiple_of(row * LEN, LEN)
    split = lengths[place.core * rows + row, 0] < LEN
    shift = jnp.where(split, jnp.float32(-1e30), jnp.float32(0.0))

    quarter = LEN // 4
    units = [(head, step) for head in range(2) for step in range(2)]

    def score_block(unit, block, peak):
        head, step = units[unit]
        rows_here = pl.ds(pl.multiple_of(start + block * quarter, quarter), quarter)
        queries = q_ref[:, pl.ds(pl.multiple_of(start + step * half, half), half)]
        raw = dot_nn(head_only(keys[rows_here], head), queries)
        if block // 2 != step:
            raw = raw + shift
        scores[unit % 2, block * quarter : (block + 1) * quarter] = raw
        best = jnp.max(raw.reshape(-1, 8, half), axis=0)
        return best if peak is None else jnp.maximum(peak, best)

    def context_block(unit, block, total):
        head, step = units[unit]
        part = slice(head * HEAD_DIM, (head + 1) * HEAD_DIM)
        cols = pl.ds(pl.multiple_of(start + block * quarter, quarter), quarter)
        here = slice(step * half, (step + 1) * half)
        term = dot_nn(
            turned_values[part, cols], p_ref[head, block * quarter : (block + 1) * quarter, here]
        )
        return term if total is None else total + term

    def context_store(unit, total, recip):
        head, step = units[unit]
        part = slice(head * HEAD_DIM, (head + 1) * HEAD_DIM)
        o_ref[part, step * half : (step + 1) * half] = (total * recip).astype(b16)

    peak = None
    for block in range(4):
        peak = score_block(0, block, peak)
    before = None
    for unit, (head, step) in enumerate(units):
        if unit == 2:
            for number in range(2 * PAIRS):
                pl.when(grid_step == number)(partial(tick, FRONT_LEAD + number, 1))
        here = slice(step * half, (step + 1) * half)
        top = jnp.max(peak, 0, keepdims=True)
        total = jnp.zeros((8, half), f32)
        peak, context = None, None
        for block in range(4):
            if unit + 1 < len(units):
                peak = score_block(unit + 1, block, peak)
            for small in range(4 * block, 4 * block + 4):
                rows_here = slice(small * 64, (small + 1) * 64)
                value = jnp.exp2(scores[unit % 2, rows_here] - top)
                total = total + jnp.sum(value.reshape(-1, 8, half), axis=0)
                p_ref[head, rows_here, here] = value.astype(b16)
            if unit > 0:
                context = context_block(unit - 1, block, context)
        if unit > 0:
            context_store(unit - 1, context, before)
        before = 1.0 / jnp.sum(total, 0, keepdims=True)
        r_ref[0, head : head + 1, here] = before
    context = None
    for block in range(4):
        context = context_block(3, block, context)
    context_store(3, context, before)
    ctx_ref[...] = o_ref[...].T

    @pl.when(grid_step == 2 * PAIRS - 1)
    def finish_copies():
        for copy in swaps(1):
            copy.wait()
        row_store().wait()
        normed_store().wait()
        for group in range(PAIRS):
            pair_item(group).store().wait()
        for group in range(REST):
            rest_item(group).store().wait()


def front(owner, lengths, master, vectors, inputs, cotangent):
    rows, span = inputs.shape[0] // 2, inputs.shape[1]
    tokens = rows * LEN
    any_spec = pl.BlockSpec(memory_space=pl.ANY)
    smem = pl.BlockSpec(memory_space=pltpu.SMEM)
    whole = jax.ShapeDtypeStruct((rows, LEN, D), b16)
    dma = pltpu.SemaphoreType.DMA
    return pl.pallas_call(
        front_kernel,
        grid=(PAIRS, rows),
        in_specs=[
            smem,
            smem,
            pl.BlockSpec((CAP, HALF, D), lambda h, r: (0, 0, 0), pipeline_mode=pl.Buffered(1)),
            pl.BlockSpec((PIECES, D), lambda h, r: (0, 0)),
            any_spec,
            any_spec,
        ],
        out_specs=[any_spec] * 5
        + [
            pl.BlockSpec((PAIR, tokens), lambda h, r: (h, 0)),
            pl.BlockSpec((PAIR, tokens), lambda h, r: (h, 0)),
            pl.BlockSpec((tokens, PAIR), lambda h, r: (0, h)),
            pl.BlockSpec((2, LEN, LEN), lambda h, r: (h * 2 + r, 0, 0)),
            pl.BlockSpec((1, 2, LEN), lambda h, r: (h * 2 + r, 0, 0)),
            pl.BlockSpec((PAIR, LEN), lambda h, r: (h, r)),
            pl.BlockSpec((LEN, PAIR), lambda h, r: (r, h)),
        ],
        out_shape=[
            whole,
            whole,
            jax.ShapeDtypeStruct((tokens, D), b16),
            jax.ShapeDtypeStruct((PAIRS, D, WIDE), b16),
            jax.ShapeDtypeStruct((REST, D, D), b16),
            jax.ShapeDtypeStruct((D, tokens), b16),
            jax.ShapeDtypeStruct((D, tokens), b16),
            jax.ShapeDtypeStruct((tokens, D), b16),
            jax.ShapeDtypeStruct((rows * HEADS, LEN, LEN), b16),
            jax.ShapeDtypeStruct((rows * PAIRS, 2, LEN), f32),
            jax.ShapeDtypeStruct((D, tokens), b16),
            jax.ShapeDtypeStruct((tokens, D), b16),
        ],
        scratch_shapes=[
            pltpu.SMEM((PIECES,), jnp.int32),
            pltpu.VMEM((rows, LEN, D), b16),
            pltpu.VMEM((tokens, D), b16),
            pltpu.VMEM((tokens, PAIR), b16),
            pltpu.VMEM((PAIR, tokens), b16),
            pltpu.VMEM((2, LEN, LEN // 2), f32),
            pltpu.VMEM((CAP, HALF, D), b16),
        ]
        + [pltpu.VMEM((FLOWS, CAP, NEAR, wide * PAIR), b16) for unused, wide in GROUPS]
        + [pltpu.VMEM((FLOWS, 2 * CAP, KEEP, wide * PAIR), b16) for unused, wide in GROUPS]
        + [
            pltpu.VMEM((PAIRS, D, WIDE), b16),
            pltpu.VMEM((FLOWS, 2, PAIRS, KEEP, WIDE), b16),
            pltpu.VMEM((REST, D, D), b16),
            pltpu.VMEM((FLOWS, 2, REST, KEEP, D), b16),
            dma((CHUNKS, FLOWS, 3)),
            dma((CHUNKS, FLOWS, 3)),
            dma((PAIRS, FLOWS, 6)),
            dma((PAIRS, FLOWS, 6)),
            dma((REST, FLOWS, 6)),
            dma((REST, FLOWS, 6)),
            dma((2,)),
            dma((2,)),
            dma((2,)),
            dma((PAIRS + REST + 2,)),
        ],
        compiler_params=pltpu.CompilerParams(
            collective_id=0, has_side_effects=True, vmem_limit_bytes=60 * MIB
        ),
        name="front",
    )(owner, lengths, master, vectors, inputs, cotangent)


class Sum:
    steps = 7

    def __init__(self, place, work, wide, narrow, sems, send_pair, add_own):
        self.place, self.work, self.wide, self.narrow, self.sems = place, work, wide, narrow, sems
        self.send_pair, self.add_own = send_pair, add_own

    def column(self, flow):
        rows = rows_at(self.place.flow(flow)[4], KEEP)

        def read():
            return self.work[:, rows]

        def write(value):
            self.work[:, rows] = value

        sems = (self.sems[0].at[flow, pl.ds(2, 3)], self.sems[1].at[flow, pl.ds(2, 3)])
        land = self.narrow.at[flow, pl.ds(1, 2)]
        return Column(self.place, self.work.at[:, rows], read, write, land, sems)

    def copy(self, flow, index):
        first, second, near, far, keep, give = self.place.flow(flow)
        source, target, device = [
            (self.work.at[:, rows_at(far, NEAR)], self.wide.at[flow], first),
            (self.work.at[:, rows_at(give, KEEP)], self.narrow.at[flow, 0], second),
        ][index]
        return remote(
            source,
            target,
            self.sems[0].at[flow, index],
            self.sems[1].at[flow, index],
            self.place.partners[device],
        )

    def add(self, rows, value):
        self.work[:, rows] = (self.work[:, rows].astype(f32) + value.astype(f32)).astype(b16)

    def step(self, index):
        if index == 0:
            self.send_pair().start()
        if index == 1:
            self.send_pair().wait()
            self.add_own()
        for flow in range(FLOWS):
            first, second, near, far, keep, give = self.place.flow(flow)
            if index == 1:
                self.copy(flow, 0).start()
            if index == 2:
                self.copy(flow, 0).wait()
                self.add(rows_at(near, NEAR), self.wide[flow])
                self.copy(flow, 1).start()
            if index == 3:
                self.copy(flow, 1).wait()
                self.add(rows_at(keep, KEEP), self.narrow[flow, 0])
        if index >= 3:
            columns = [self.column(flow) for flow in range(FLOWS)]
            column_step(self.place, columns, index - 3)


class Gather:
    steps = 3

    def __init__(self, place, work, narrow, wide, sems):
        self.place, self.work, self.narrow, self.wide = place, work, narrow, wide
        self.sems = sems

    def copy(self, flow, index):
        first, second, near, far, keep, give = self.place.flow(flow)
        rows, target, device = [
            (rows_at(keep, KEEP), self.narrow, second),
            (rows_at(near, NEAR), self.wide, first),
        ][index]
        return remote(
            self.work.at[:, rows],
            target.at[flow],
            self.sems[0].at[flow, 5 + index],
            self.sems[1].at[flow, 5 + index],
            self.place.partners[device],
        )

    def step(self, index):
        for flow in range(FLOWS):
            first, second, near, far, keep, give = self.place.flow(flow)
            if index > 0:
                self.copy(flow, index - 1).wait()
            if index == 1:
                self.work[:, rows_at(give, KEEP)] = self.narrow[flow]
            if index == 2:
                self.work[:, rows_at(far, NEAR)] = self.wide[flow]
            if index < 2:
                self.copy(flow, index).start()


class Hand:
    steps = 3

    def __init__(self, place, table, work, bag, gift, pack, last, own, out, sems, store_sems):
        self.place, self.table, self.work = place, table, work
        self.bag, self.gift, self.pack, self.last, self.own = bag, gift, pack, last, own
        self.out, self.sems, self.store_sems = out, sems, store_sems

    def tile(self, chip, rank, rows):
        return self.work[self.table[chip * CAP + rank], rows]

    def copy(self, flow, index):
        first, second = self.place.flow(flow)[:2]
        source, target, device = [
            (self.bag.at[flow], self.gift.at[flow], second),
            (self.pack.at[flow], self.last.at[flow], first),
        ][index]
        return remote(
            source,
            target,
            self.sems[0].at[flow, index],
            self.sems[1].at[flow, index],
            self.place.partners[device],
        )

    def stores(self, flow):
        first, second, near, far, keep, give = self.place.flow(flow)
        parts = [
            (self.own.at[flow], rows_at(keep, KEEP)),
            (self.gift.at[flow, pl.ds(0, CAP)], rows_at(give, KEEP)),
            (self.last.at[flow], rows_at(far, NEAR)),
        ]
        return [
            pltpu.make_async_copy(source, self.out.at[:, rows], self.store_sems.at[flow, index])
            for index, (source, rows) in enumerate(parts)
        ]

    def step(self, index):
        for flow in range(FLOWS):
            first, second, near, far, keep, give = self.place.flow(flow)
            rows = rows_at(keep, KEEP)
            if index == 0:
                beside = self.place.chips[second]
                across = beside + self.place.chips[first] - self.place.me
                for rank in range(CAP):
                    self.bag[flow, rank] = self.tile(beside, rank, rows)
                    self.bag[flow, CAP + rank] = self.tile(across, rank, rows)
                    self.own[flow, rank] = self.tile(self.place.me, rank, rows)
                self.copy(flow, 0).start()
            if index == 1:
                self.copy(flow, 0).wait()
                for rank in range(CAP):
                    mine = self.tile(self.place.chips[first], rank, rows)
                    self.pack[flow, rank, rows_at(keep - near, KEEP)] = mine
                    self.pack[flow, rank, rows_at(give - near, KEEP)] = self.gift[flow, CAP + rank]
                self.copy(flow, 1).start()
            if index == 2:
                self.copy(flow, 1).wait()
                for copy in self.stores(flow):
                    copy.start()


BACK_STEPS = 2 * PAIRS
BACK_TAIL = 4
BACK_PAIRS = tuple((index, 1) for index in range(PAIRS))
BACK_REST = (0, 1, 2, 3, 4, 5, 6, 7, 8)
BACK_HAND = 15


def back_kernel(
    table, p_ref, r_ref, v_ref, q_ref, k_ref, o_ref, g_ref, w_ref, n_ref, x_ref, z_ref, vec_ref,
    tiles_in, sums_in, y_in,
    y_out, i_out, pairs_out, slots_out, sums_ref,
    grad_sum, wide_sum, turned, slopes, block_out,
    two, two_wide, two_narrow, two_stage, one, one_wide, one_narrow, one_send_stage, one_stage,
    gather_narrow, gather_wide,
    bag, gift, pack, last, own, vec_land,
    two_send, two_recv, one_send, one_recv, hand_send, hand_recv, hand_store,
    pair_two_send, pair_two_recv, pair_one_send, pair_one_recv, load_sem, store_sem,
    swap_send, swap_recv, swap_local, vec_send, vec_recv,
):
    step = pl.program_id(0)
    place = Place()
    rows, span = y_in.shape[0], y_in.shape[1] // 2
    near_half = rows_at(place.core * HALF, HALF)
    far_half = rows_at(place.other * HALF, HALF)

    def load_two(group):
        first, count = REST_GROUPS[group]
        return pltpu.make_async_copy(
            tiles_in.at[pl.ds(first, count), near_half],
            two_stage.at[pl.ds(group % 3, 1)],
            load_sem.at[group % 3],
        )

    def rest_sum(group):
        first, count = REST_GROUPS[group]
        span_of = pl.ds(first, count)
        work = two.at[span_of]

        def send_pair():
            return remote(
                tiles_in.at[span_of, far_half],
                work,
                pair_two_send.at[group],
                pair_two_recv.at[group],
                place.twin,
            )

        def add_own():
            load_two(group).wait()
            work[...] = (work[...].astype(f32) + two_stage[group % 3].astype(f32)).astype(b16)

        sems = (two_send.at[group], two_recv.at[group])
        wide, narrow = two_wide.at[:, span_of], two_narrow.at[:, :, span_of]
        return Sum(place, work, wide, narrow, sems, send_pair, add_own)

    def pair_sum(group):
        first, count = BACK_PAIRS[group]
        span_of = pl.ds(first, count)
        work = one.at[span_of]

        def send_pair():
            return remote(
                one_send_stage.at[pl.ds(group % 2, 1)],
                work,
                pair_one_send.at[group],
                pair_one_recv.at[group],
                place.twin,
            )

        def add_own():
            own = one_stage[group % 2].astype(f32)
            work[...] = (work[...].astype(f32) + own).astype(b16)

        sems = (one_send.at[group], one_recv.at[group])
        wide, narrow = one_wide.at[:, span_of], one_narrow.at[:, :, span_of]
        return Sum(place, work, wide, narrow, sems, send_pair, add_own)

    def pair_gather(group):
        first, count = BACK_PAIRS[group]
        span_of = pl.ds(first, count)
        sems = (one_send.at[group], one_recv.at[group])
        narrow, wide = gather_narrow.at[:, span_of], gather_wide.at[:, span_of]
        return Gather(place, one.at[span_of], narrow, wide, sems)

    hand = Hand(
        place, table, two, bag, gift, pack, last, own, slots_out, (hand_send, hand_recv), hand_store
    )

    def pair_store(index, tile):
        return pltpu.make_async_copy(
            one.at[index, :, pl.ds(tile * PAIR, PAIR)],
            pairs_out.at[tile, :, pl.ds(index * PAIR, PAIR)],
            store_sem.at[index, tile],
        )

    def tick(number, odd):
        for group, start in enumerate(BACK_REST):
            if group % 2 == odd and 0 <= number - start < Sum.steps:
                rest_sum(group).step(number - start)
        for group, (first, count) in enumerate(BACK_PAIRS):
            if group % 2 != odd:
                continue
            start = 2 * (first + count)
            if 0 <= number - start < Sum.steps:
                pair_sum(group).step(number - start)
            if 0 <= number - start - Sum.steps + 1 < Gather.steps:
                pair_gather(group).step(number - start - Sum.steps + 1)
            if number == start + Sum.steps + 1:
                for index in range(first, first + count):
                    for tile in range(3):
                        pair_store(index, tile).start()
        if odd == 0 and 0 <= number - BACK_HAND < Hand.steps:
            hand.step(number - BACK_HAND)
        for group, start in enumerate(BACK_REST):
            if odd == 1 and number == max(start - 1, 0):
                load_two(group).start()

    def both(number):
        tick(number, 0)
        tick(number, 1)

    def swap_y(index):
        there = pl.ds(place.core * rows, rows)
        if index == 0:
            return pltpu.make_async_copy(
                y_in.at[:, pl.ds(place.core * span, span)], y_out.at[there], swap_local.at[0]
            )
        return remote(
            y_in.at[:, pl.ds(place.other * span, span)],
            y_out.at[there],
            swap_send.at[0],
            swap_recv.at[0],
            place.twin,
        )

    @pl.when(step == 0)
    def lead():
        place.greet()
        for index in range(2):
            swap_y(index).start()
        sums_ref[...] = sums_in[...]

    for number in range(BACK_STEPS + BACK_TAIL):
        early = partial(tick, number, 0) if number < BACK_STEPS else partial(both, number)
        pl.when(step == number)(early)

    half = LEN // 2
    pair, row = step // 2, lax.rem(step, 2)

    quarter = LEN // 4

    def attention_inputs(head):
        part = slice(head * HEAD_DIM, (head + 1) * HEAD_DIM)
        values = head_only(v_ref[...], head)
        recip = r_ref[0, head : head + 1, :]
        grad = g_ref[part, :].astype(f32) * recip
        delta = jnp.sum(grad * o_ref[part, :].astype(f32), 0, keepdims=True)
        grad = grad.astype(b16)
        return values, grad, delta, jnp.concatenate([grad, grad], axis=0)

    def attention(head):
        part = slice(head * HEAD_DIM, (head + 1) * HEAD_DIM)
        values, grad, delta, doubled = attention_inputs(head)
        units = [(which, block) for which in range(2) for block in range(4)]
        value_grad, key_grad, query_grad = {}, {}, {}

        def raw_block(unit):
            which, block = units[unit]
            cols = slice(which * half, (which + 1) * half)
            return dot_nn(values[block * quarter : (block + 1) * quarter], doubled[:, cols])

        def slope_block(unit, raw):
            which, block = units[unit]
            cols = slice(which * half, (which + 1) * half)
            for small in range(4):
                rows_here = slice(small * 64, (small + 1) * 64)
                rows_all = slice(block * quarter + small * 64, block * quarter + (small + 1) * 64)
                slope = p_ref[head, rows_all, cols].astype(f32) * (raw[rows_here] - delta[:, cols])
                slopes[unit % 2, rows_here] = slope.astype(b16)

        def add(totals, key, term):
            totals[key] = totals[key] + term if key in totals else term

        def grad_block(unit):
            which, block = units[unit]
            cols = slice(which * half, (which + 1) * half)
            rows_all = slice(block * quarter, (block + 1) * quarter)
            slope = slopes[unit % 2]
            add(value_grad, block, dot_nt(grad[:, cols], p_ref[head, rows_all, cols]))
            add(key_grad, block, dot_nt(q_ref[part, cols], slope))
            add(query_grad, which, dot_nn(k_ref[part, rows_all], slope))

        raw = raw_block(0)
        for unit in range(len(units)):
            after = raw_block(unit + 1) if unit + 1 < len(units) else None
            slope_block(unit, raw)
            if unit > 0:
                grad_block(unit - 1)
            raw = after
        grad_block(len(units) - 1)
        for which in range(2):
            total = query_grad[which] * (HEAD_DIM**-0.5)
            turned[part, which * half : (which + 1) * half] = total.astype(b16)
        for block in range(4):
            rows_all = slice(block * quarter, (block + 1) * quarter)
            lower = slice(PAIR + head * HEAD_DIM, PAIR + (head + 1) * HEAD_DIM)
            turned[lower, rows_all] = (key_grad[block] * (1.0 / LOG2E)).astype(b16)
            lower = slice(2 * PAIR + head * HEAD_DIM, 2 * PAIR + (head + 1) * HEAD_DIM)
            turned[lower, rows_all] = value_grad[block].astype(b16)

    @pl.when(step < BACK_STEPS)
    def first_head():
        attention(0)

    for number in range(BACK_STEPS):
        pl.when(step == number)(partial(tick, number, 1))

    @pl.when(step < BACK_STEPS)
    def second_head():
        attention(1)
        where = pl.ds(pl.multiple_of(row * LEN, LEN), LEN)
        block = dot_nn(turned[...], n_ref[where])
        back = turned[...].T
        lanes = pl.ds(pl.multiple_of(pair * PAIR, PAIR), PAIR)
        ones = jnp.sum(back.astype(f32), 0, keepdims=True)
        sums_ref[4:5, lanes] += ones[:, :PAIR]
        sums_ref[5:6, lanes] += ones[:, 2 * PAIR :]
        term = dot_nt(back, w_ref[0])

        @pl.when(pair == 0)
        def begin():
            grad_sum[where] = term

        @pl.when(pair > 0)
        def add():
            grad_sum[where] += term

        @pl.when(row == 0)
        def keep():
            wide_sum[...] = block

        @pl.when(row == 1)
        def hand_on():
            whole = (wide_sum[...] + block).T
            low = whole.astype(b16)
            for core in range(2):

                @pl.when(place.core == core)
                def split():
                    slot = lax.rem(pair, 2)
                    one_stage[slot] = low[core * HALF : (core + 1) * HALF]
                    one_send_stage[slot] = low[(1 - core) * HALF : (2 - core) * HALF]

    def store_block(index):
        row, half = index // 2, index % 2
        target = i_out.at[place.core * rows + row]
        local = pltpu.make_async_copy(block_out.at[half], target, swap_local.at[1 + row])
        far = remote(
            block_out.at[half], target, swap_send.at[1 + row], swap_recv.at[1 + row], place.twin
        )
        return local, far, half

    def wait_block(index):
        local, far, half = store_block(index)

        @pl.when(place.core == half)
        def keep():
            local.wait()

        @pl.when(place.core != half)
        def give():
            far.wait()

    for index in range(BACK_TAIL):

        @pl.when(step == BACK_STEPS + index)
        def close():
            size = LEN // 2
            if index >= 2:
                wait_block(index - 2)
            gain_sum = jnp.zeros((8, D), f32)
            shift_sum = jnp.zeros((8, D), f32)
            for block in range(size // 16):
                rows_here = slice(block * 16, (block + 1) * 16)
                grad = grad_sum[index * size + block * 16 : index * size + (block + 1) * 16]
                unit, rstd = norm_parts(x_ref[rows_here].astype(f32))
                gain_sum = gain_sum + jnp.sum((grad * unit).reshape(-1, 8, D), axis=0)
                shift_sum = shift_sum + jnp.sum(grad.reshape(-1, 8, D), axis=0)
                total = norm_back(grad, unit, rstd, vec_ref[0:1, :])
                block_out[index % 2, rows_here] = (z_ref[rows_here].astype(f32) + total).astype(b16)
            sums_ref[0:1, :] += jnp.sum(gain_sum, 0, keepdims=True)
            sums_ref[1:2, :] += jnp.sum(shift_sum, 0, keepdims=True)
            local, far, half = store_block(index)

            @pl.when(place.core == half)
            def keep():
                local.start()

            @pl.when(place.core != half)
            def give():
                far.start()

    @pl.when(step == BACK_STEPS + BACK_TAIL - 1)
    def drain():
        devices = [place.twin] + place.partners

        def vector(index):
            return remote(
                sums_ref, vec_land.at[index], vec_send.at[index], vec_recv.at[index], devices[index]
            )

        vector(0).start()
        for number in range(BACK_STEPS + BACK_TAIL, BACK_STEPS + Sum.steps + Gather.steps):
            both(number)
            index = number - BACK_STEPS - BACK_TAIL
            if index < 5:
                vector(index).wait()
                sums_ref[...] += vec_land[index]
                if index < 4:
                    vector(index + 1).start()
        for index in range(2):
            swap_y(index).wait()
        for index in range(2, BACK_TAIL):
            wait_block(index)
        for index in range(PAIRS):
            for tile in range(3):
                pair_store(index, tile).wait()
        for flow in range(FLOWS):
            for copy in hand.stores(flow):
                copy.wait()


def back(table, attention, weights, normed, x, residual, vectors, tiles, sums, y):
    rows, length = y.shape[:2]
    tokens = rows * length
    any_spec = pl.BlockSpec(memory_space=pl.ANY)
    smem = pl.BlockSpec(memory_space=pltpu.SMEM)
    dma = pltpu.SemaphoreType.DMA

    def now(step):
        return jnp.minimum(step, BACK_STEPS - 1)

    def tail(step):
        return jnp.maximum(step - BACK_STEPS, 0)

    head_block = pl.BlockSpec((PAIR, LEN), lambda s: (now(s) // 2, lax.rem(now(s), 2)))
    tail_block = pl.BlockSpec((LEN // 2, D), lambda s: (tail(s), 0))
    whole = pl.BlockSpec((PIECES, D), lambda s: (0, 0))
    sums_block = pl.BlockSpec((16, D), lambda s: (0, 0))
    return pl.pallas_call(
        back_kernel,
        grid=(BACK_STEPS + BACK_TAIL,),
        in_specs=[
            smem,
            pl.BlockSpec((2, LEN, LEN), lambda s: (now(s), 0, 0)),
            pl.BlockSpec((1, 2, LEN), lambda s: (now(s), 0, 0)),
            pl.BlockSpec((LEN, PAIR), lambda s: (lax.rem(now(s), 2), now(s) // 2)),
            head_block,
            head_block,
            head_block,
            head_block,
            pl.BlockSpec((1, D, WIDE), lambda s: (now(s) // 2, 0, 0)),
            pl.BlockSpec((tokens, D), lambda s: (0, 0), pipeline_mode=pl.Buffered(1)),
            tail_block,
            tail_block,
            whole,
            any_spec,
            sums_block,
            any_spec,
        ],
        out_specs=[any_spec] * 4 + [sums_block],
        out_shape=[
            jax.ShapeDtypeStruct((2 * rows, length // 2, D), b16),
            jax.ShapeDtypeStruct((2 * rows, length // 2, D), b16),
            jax.ShapeDtypeStruct((3, HALF, D), b16),
            jax.ShapeDtypeStruct((CAP, HALF, D), b16),
            jax.ShapeDtypeStruct((16, D), f32),
        ],
        scratch_shapes=[
            pltpu.VMEM((tokens, D), f32),
            pltpu.VMEM((WIDE, D), f32),
            pltpu.VMEM((WIDE, LEN), b16),
            pltpu.VMEM((2, LEN // 4, LEN // 2), b16),
            pltpu.VMEM((2, LEN // 2, D), b16),
            pltpu.VMEM((REST, HALF, D), b16),
            pltpu.VMEM((FLOWS, REST, NEAR, D), b16),
            pltpu.VMEM((FLOWS, 3, REST, KEEP, D), b16),
            pltpu.VMEM((3, HALF, D), b16),
            pltpu.VMEM((PAIRS, HALF, WIDE), b16),
            pltpu.VMEM((FLOWS, PAIRS, NEAR, WIDE), b16),
            pltpu.VMEM((FLOWS, 3, PAIRS, KEEP, WIDE), b16),
            pltpu.VMEM((2, HALF, WIDE), b16),
            pltpu.VMEM((2, HALF, WIDE), b16),
            pltpu.VMEM((FLOWS, PAIRS, KEEP, WIDE), b16),
            pltpu.VMEM((FLOWS, PAIRS, NEAR, WIDE), b16),
            pltpu.VMEM((FLOWS, 2 * CAP, KEEP, D), b16),
            pltpu.VMEM((FLOWS, 2 * CAP, KEEP, D), b16),
            pltpu.VMEM((FLOWS, CAP, NEAR, D), b16),
            pltpu.VMEM((FLOWS, CAP, NEAR, D), b16),
            pltpu.VMEM((FLOWS, CAP, KEEP, D), b16),
            pltpu.VMEM((5, 16, D), f32),
            dma((REST, FLOWS, 5)),
            dma((REST, FLOWS, 5)),
            dma((PAIRS, FLOWS, 7)),
            dma((PAIRS, FLOWS, 7)),
            dma((FLOWS, 2)),
            dma((FLOWS, 2)),
            dma((FLOWS, 3)),
            dma((REST,)),
            dma((REST,)),
            dma((PAIRS,)),
            dma((PAIRS,)),
            dma((3,)),
            dma((PAIRS, 3)),
            dma((3,)),
            dma((3,)),
            dma((3,)),
            dma((5,)),
            dma((5,)),
        ],
        compiler_params=pltpu.CompilerParams(
            collective_id=1, has_side_effects=True, vmem_limit_bytes=62 * MIB
        ),
        name="back",
    )(table, *attention, weights, normed, x, residual, vectors, tiles, sums, y)


def update_kernel(tile_at, one, two, w_ref, m_ref, s_ref, y_in, i_in, w_out, m_out, s_out, y_out, i_out):
    step = pl.program_id(0)
    tile = tile_at[step // 2]
    grad = jnp.where(tile < 3, one[0], two[0]).astype(f32)
    parts = adam_step(w_ref[0], grad, m_ref[0], s_ref[0], RATE)
    for target, part in zip((w_out, m_out, s_out), parts):
        target[0] = jnp.where(tile >= 0, part, jnp.zeros_like(part))

    @pl.when(step < 4)
    def widen():
        y_out[...] = y_in[...].astype(f32)
        i_out[...] = i_in[...].astype(f32)


def update(tile_at, one, two, master, first, second, y, grad):
    tokens = y.shape[0]
    size = HALF // 2
    state = pl.BlockSpec((1, size, D), lambda s, tile_at: (s // 2, lax.rem(s, 2), 0))
    wide = pl.BlockSpec((tokens // 4, D), lambda s, tile_at: (jnp.minimum(s, 3), 0))
    return pl.pallas_call(
        update_kernel,
        grid_spec=pltpu.PrefetchScalarGridSpec(
            num_scalar_prefetch=1,
            grid=(CAP * 2,),
            in_specs=[
                pl.BlockSpec(
                    (1, size, D),
                    lambda s, tile_at: (jnp.clip(tile_at[s // 2], 0, 2), lax.rem(s, 2), 0),
                ),
                state,
                state,
                state,
                state,
                wide,
                wide,
            ],
            out_specs=[state] * 3 + [wide] * 2,
        ),
        out_shape=[jax.ShapeDtypeStruct(master.shape, f32)] * 3
        + [jax.ShapeDtypeStruct((tokens, D), f32)] * 2,
        compiler_params=pltpu.CompilerParams(vmem_limit_bytes=60 * MIB),
        name="update",
    )(tile_at, one, two, master, first, second, y, grad)


def shards_paired(
    inputs,
    cotangent,
    doc_lengths,
    owner_list,
    master,
    first_moment,
    second_moment,
    vectors,
    vector_first,
    vector_second,
):
    rows_here, span, width = inputs.shape
    place = lax.axis_index("blk")
    member = lax.axis_index("dp")
    rows_mine = rows_here // 2
    order = jnp.arange(PIECES)
    same_owner = owner_list[:, None] == owner_list[None, :]
    ranks = jnp.sum(same_owner & (order[None, :] < order[:, None]), axis=1).astype(jnp.int32)
    slot_of = owner_list * CAP + ranks
    front_outs = front(owner_list, doc_lengths, master, vectors, inputs, cotangent)
    x, cot, normed, weights_one, weights_two, queries, keys, values = front_outs[:8]
    weights, recips, context_turned, context = front_outs[8:]
    x = x.reshape(-1, width)
    cot = cot.reshape(-1, width)
    block_out, residual, grad_context, sums, tiles_two = feed(
        context, context_turned, x, cot, weights_two, vectors
    )
    hits = jnp.arange(16 * CAP)[:, None] == slot_of[None, :]
    tile_at = jnp.sum(jnp.where(hits, order[None, :] + 1, 0), axis=1).astype(jnp.int32) - 1
    table = jnp.maximum(tile_at - 3, 0)
    block_out, input_grad, total_one, total_two, vector_total = back(
        table,
        (weights, recips, values, queries, keys, context_turned, grad_context),
        weights_one,
        normed,
        x,
        residual,
        vectors,
        tiles_two,
        sums,
        block_out.reshape(rows_mine, LEN, width),
    )
    mine = lax.dynamic_slice_in_dim(tile_at, member * CAP, CAP, 0)
    *updated, block_out, input_grad = update(
        mine,
        total_one,
        total_two,
        master,
        first_moment,
        second_moment,
        block_out.reshape(-1, width),
        input_grad.reshape(-1, width),
    )
    columns = vector_first.shape[1]
    vector_cols = lax.dynamic_slice_in_dim(vectors, place * columns, columns, 1)
    vector_total = lax.dynamic_slice(vector_total, (0, place * columns), (PIECES, columns))
    updated_vectors = adam_step(vector_cols, vector_total, vector_first, vector_second, VEC_RATE)
    return (
        block_out.reshape(inputs.shape),
        input_grad.reshape(inputs.shape),
        *updated,
        *updated_vectors,
    )


def solution(mesh):
    in_specs = (
        P("dp", "blk", None),
        P("dp", "blk", None),
        P("dp", None),
        P(),
        P("dp", "blk", None),
        P("dp", "blk", None),
        P("dp", "blk", None),
        P(),
        P(None, "blk"),
        P(None, "blk"),
    )
    out_specs = (
        P("dp", "blk", None),
        P("dp", "blk", None),
        P("dp", "blk", None),
        P("dp", "blk", None),
        P("dp", "blk", None),
        P(None, "blk"),
        P(None, "blk"),
        P(None, "blk"),
    )
    paired = mesh.shape["blk"] == 2 and mesh.shape["dp"] == 16
    shards = shards_paired if paired else shards_any
    return jax.shard_map(shards, mesh=mesh, in_specs=in_specs, out_specs=out_specs, check_vma=False)
```

```python
from functools import partial

import jax
import jax.numpy as jnp
from jax import lax
from jax.experimental import pallas as pl
from jax.experimental.pallas import tpu as pltpu
from jax.sharding import PartitionSpec as P

D = 768
FF = 3072
HEADS = 12
HEAD_DIM = 64
LEN = 1024
CAP = 3
STEP = 10
PIECES = 12


EPS_NORM = 1e-05
BETA_ONE = 0.9
BETA_TWO = 0.999
RATE = 0.04
VEC_RATE = 0.25
DECAY = 0.01
ADAM_EPS = 1e-08


def normalize(values_in, gain, shift):
    center = jnp.mean(values_in, axis=-1, keepdims=True)
    offset = values_in - center
    spread = jnp.mean(offset * offset, axis=-1, keepdims=True)
    return offset * lax.rsqrt(spread + EPS_NORM) * gain + shift


def adam_step(weight, grad, first, second, rate):
    first_new = BETA_ONE * first + (1.0 - BETA_ONE) * grad
    second_new = BETA_TWO * second + (1.0 - BETA_TWO) * grad * grad
    corrected = (
        first_new
        / (1.0 - BETA_ONE**STEP)
        / (jnp.sqrt(second_new / (1.0 - BETA_TWO**STEP)) + ADAM_EPS)
    )
    return (weight - rate * (corrected + DECAY * weight), first_new, second_new)


def shards_any(
    inputs,
    cotangent,
    doc_lengths,
    owner_list,
    master,
    first_moment,
    second_moment,
    vectors,
    vector_first,
    vector_second,
):
    rows_here, span, width = inputs.shape
    tokens_here = rows_here * span
    fold = FF // D
    scale = HEAD_DIM ** (-0.5)
    place = lax.axis_index("blk")
    f32 = jnp.float32
    b16 = jnp.bfloat16
    order = jnp.arange(PIECES)
    same_owner = owner_list[:, None] == owner_list[None, :]
    ranks = jnp.sum(same_owner & (order[None, :] < order[:, None]), axis=1)
    slot_of = owner_list * CAP + ranks

    mine = (owner_list == lax.axis_index("dp"))[:, None, None]
    tile_rows = lax.psum(jnp.where(mine, master[ranks], 0.0).astype(b16), "dp")
    tiles = lax.all_gather(tile_rows, "blk", axis=1, tiled=True)
    query_weight = tiles[0]
    key_weight = tiles[1]
    value_weight = tiles[2]
    out_weight = tiles[3]
    up_weight = jnp.transpose(tiles[4 : 4 + fold], (1, 0, 2)).reshape(width, FF)
    down_weight = tiles[4 + fold :].reshape(FF, width)
    flat_in = inputs.reshape(tokens_here, width).astype(f32)
    normed_one = normalize(flat_in, vectors[0], vectors[1]).astype(b16)
    queries = (jnp.dot(normed_one, query_weight, preferred_element_type=f32) + vectors[4]).astype(
        b16
    )
    keys_here = jnp.dot(normed_one, key_weight, preferred_element_type=f32).astype(b16)
    values_here = (
        jnp.dot(normed_one, value_weight, preferred_element_type=f32) + vectors[5]
    ).astype(b16)
    query_heads = queries.reshape(rows_here, span, HEADS, HEAD_DIM)
    first_len = doc_lengths[:, 0]
    query_seg = (place * span + jnp.arange(span))[None, :] >= first_len[:, None]

    def block_scores(key_block, start):
        count = key_block.shape[1]
        key_heads = key_block.reshape(rows_here, count, HEADS, HEAD_DIM)
        raw = (
            jnp.einsum("rqhd,rkhd->rhqk", query_heads, key_heads, preferred_element_type=f32)
            * scale
        )
        key_seg = (start + jnp.arange(count))[None, :] >= first_len[:, None]
        allowed = query_seg[:, None, :, None] == key_seg[:, None, None, :]
        return (raw, allowed)

    key_rows = keys_here.reshape(rows_here, span, width)
    value_rows = values_here.reshape(rows_here, span, width)
    top = jnp.full((rows_here, HEADS, span), -1e30, f32)
    key_block = lax.all_gather(key_rows, "blk", axis=1, tiled=True)
    value_block = lax.all_gather(value_rows, "blk", axis=1, tiled=True)
    count = key_block.shape[1]
    raw, allowed = block_scores(key_block, jnp.int32(0))
    new_top = jnp.maximum(top, jnp.max(jnp.where(allowed, raw, -1e30), axis=-1))
    weights = jnp.where(allowed, jnp.exp(raw - new_top[..., None]), 0.0)
    value_heads = value_block.reshape(rows_here, count, HEADS, HEAD_DIM)
    update = jnp.einsum(
        "rhqk,rkhd->rhqd", weights.astype(b16), value_heads, preferred_element_type=f32
    )
    total = jnp.sum(weights, axis=-1)
    log_total = new_top + jnp.log(total)
    context_raw = update / total[..., None]
    context_low = jnp.transpose(context_raw, (0, 2, 1, 3)).reshape(tokens_here, width).astype(b16)
    residual = flat_in + (jnp.dot(context_low, out_weight, preferred_element_type=f32) + vectors[6])
    normed_two = normalize(residual, vectors[2], vectors[3]).astype(b16)
    hidden = jnp.dot(normed_two, up_weight, preferred_element_type=f32) + vectors[8:].reshape(FF)
    gelu_exact = partial(jax.nn.gelu, approximate=False)
    active, gelu_pull = jax.vjp(gelu_exact, hidden)
    active_low = active.astype(b16)
    block_out = (
        residual + (jnp.dot(active_low, down_weight, preferred_element_type=f32) + vectors[7])
    ).reshape(rows_here, span, width)
    grad_out = cotangent.reshape(tokens_here, width)
    down_grad = jnp.einsum("tf,td->fd", active_low, grad_out, preferred_element_type=f32)
    down_sum = jnp.sum(grad_out, axis=0, dtype=f32)
    grad_active = jnp.einsum("td,fd->tf", grad_out, down_weight, preferred_element_type=f32)
    grad_hidden = gelu_pull(grad_active)[0].astype(b16)
    up_grad = jnp.einsum("td,tf->df", normed_two, grad_hidden, preferred_element_type=f32)
    up_sum = jnp.sum(grad_hidden, axis=0, dtype=f32)
    ffn_tiles = jnp.concatenate(
        [
            jnp.transpose(up_grad.reshape(width, fold, width), (1, 0, 2)),
            down_grad.reshape(fold, width, width),
        ],
        axis=0,
    )
    grad_normed_two = jnp.einsum("tf,df->td", grad_hidden, up_weight, preferred_element_type=f32)
    unused, second_pull = jax.vjp(normalize, residual, vectors[2], vectors[3])
    residual_part, gain_two_grad, shift_two_grad = second_pull(grad_normed_two)
    grad_residual = grad_out.astype(f32) + residual_part
    grad_attended = grad_residual.astype(b16)
    out_grad = jnp.einsum("tm,td->md", context_low, grad_attended, preferred_element_type=f32)
    out_sum = jnp.sum(grad_attended, axis=0, dtype=f32)
    grad_context = jnp.einsum(
        "td,md->tm", grad_attended, out_weight, preferred_element_type=f32
    ).astype(b16)
    grad_heads = grad_context.reshape(rows_here, span, HEADS, HEAD_DIM)
    delta = jnp.einsum("rqhd,rhqd->rhq", grad_heads.astype(f32), context_raw)
    key_all, value_all = (
        lax.all_gather(key_rows, "blk", axis=1, tiled=True),
        lax.all_gather(value_rows, "blk", axis=1, tiled=True),
    )
    key_size = min(512, LEN)

    def back_block(index, carry):
        grad_query, key_total, value_total = carry
        start = index * key_size
        key_block = lax.dynamic_slice_in_dim(key_all, start, key_size, 1)
        value_block = lax.dynamic_slice_in_dim(value_all, start, key_size, 1)
        raw, allowed = block_scores(key_block, start)
        weights_back = jnp.where(allowed, jnp.exp(raw - log_total[..., None]), 0.0)
        key_heads = key_block.reshape(rows_here, key_size, HEADS, HEAD_DIM)
        value_heads = value_block.reshape(rows_here, key_size, HEADS, HEAD_DIM)
        value_grad = jnp.einsum(
            "rhqk,rqhd->rkhd", weights_back.astype(b16), grad_heads, preferred_element_type=f32
        )
        weight_grad = jnp.einsum(
            "rqhd,rkhd->rhqk", grad_heads, value_heads, preferred_element_type=f32
        )
        score_grad = (weights_back * (weight_grad - delta[..., None])).astype(b16)
        grad_query = (
            grad_query
            + jnp.einsum("rhqk,rkhd->rqhd", score_grad, key_heads, preferred_element_type=f32)
            * scale
        )
        key_grad = (
            jnp.einsum("rhqk,rqhd->rkhd", score_grad, query_heads, preferred_element_type=f32)
            * scale
        )
        key_total = lax.dynamic_update_slice_in_dim(
            key_total, key_grad.reshape(rows_here, key_size, width), start, 1
        )
        value_total = lax.dynamic_update_slice_in_dim(
            value_total, value_grad.reshape(rows_here, key_size, width), start, 1
        )
        return (grad_query, key_total, value_total)

    zero_rows = jnp.zeros((rows_here, LEN, width), f32)
    grad_query, key_total, value_total = lax.fori_loop(
        0,
        LEN // key_size,
        back_block,
        (jnp.zeros((rows_here, span, HEADS, HEAD_DIM), f32), zero_rows, zero_rows),
    )
    key_grad_here, value_grad_here = (
        lax.psum_scatter(
            key_total.astype(jnp.bfloat16), "blk", scatter_dimension=1, tiled=True
        ).astype(jnp.float32),
        lax.psum_scatter(
            value_total.astype(jnp.bfloat16), "blk", scatter_dimension=1, tiled=True
        ).astype(jnp.float32),
    )
    query_low = grad_query.reshape(tokens_here, width).astype(b16)
    key_low = key_grad_here.reshape(tokens_here, width).astype(b16)
    value_low = value_grad_here.reshape(tokens_here, width).astype(b16)
    query_tile = jnp.einsum("td,te->de", normed_one, query_low, preferred_element_type=f32)
    key_tile = jnp.einsum("td,te->de", normed_one, key_low, preferred_element_type=f32)
    value_tile = jnp.einsum("td,te->de", normed_one, value_low, preferred_element_type=f32)
    grad_normed_one = (
        jnp.einsum("te,de->td", query_low, query_weight, preferred_element_type=f32)
        + jnp.einsum("te,de->td", key_low, key_weight, preferred_element_type=f32)
        + jnp.einsum("te,de->td", value_low, value_weight, preferred_element_type=f32)
    )
    unused, first_pull = jax.vjp(normalize, flat_in, vectors[0], vectors[1])
    input_part, gain_one_grad, shift_one_grad = first_pull(grad_normed_one)
    input_grad = (grad_residual + input_part).reshape(rows_here, span, width)
    vector_grads = jnp.concatenate(
        [
            jnp.stack(
                [
                    gain_one_grad,
                    shift_one_grad,
                    gain_two_grad,
                    shift_two_grad,
                    jnp.sum(query_low, axis=0, dtype=f32),
                    jnp.sum(value_low, axis=0, dtype=f32),
                    out_sum,
                    down_sum,
                ]
            ),
            up_sum.reshape(fold, width),
        ],
        axis=0,
    )
    attn_tiles = jnp.stack([query_tile, key_tile, value_tile, out_grad])
    piece_share, vector_share = (
        lax.psum_scatter(
            jnp.concatenate([attn_tiles, ffn_tiles], axis=0).astype(jnp.bfloat16),
            "blk",
            scatter_dimension=1,
            tiled=True,
        ).astype(jnp.float32),
        lax.psum_scatter(
            vector_grads.astype(jnp.bfloat16), "blk", scatter_dimension=1, tiled=True
        ).astype(jnp.float32),
    )
    own_slots = lax.axis_index("dp") * CAP + jnp.arange(CAP)
    pick = (own_slots[:, None] == slot_of[None, :]).astype(f32)
    occupied = jnp.sum(pick, axis=1)[:, None, None]
    total_share, vector_total = (
        lax.psum(piece_share.astype(jnp.bfloat16), "dp").astype(jnp.float32),
        lax.psum(vector_share.astype(jnp.bfloat16), "dp").astype(jnp.float32),
    )
    slot_grads = jnp.einsum("cp,prd->crd", pick, total_share, precision=lax.Precision.HIGHEST)
    new_master, new_first, new_second = adam_step(
        master, slot_grads, first_moment, second_moment, RATE
    )
    columns = vector_first.shape[1]
    vector_cols = lax.dynamic_slice_in_dim(vectors, place * columns, columns, 1)
    new_vectors, new_vector_first, new_vector_second = adam_step(
        vector_cols, vector_total, vector_first, vector_second, VEC_RATE
    )
    return (
        block_out,
        input_grad,
        new_master * occupied,
        new_first * occupied,
        new_second * occupied,
        new_vectors,
        new_vector_first,
        new_vector_second,
    )


f32 = jnp.float32
b16 = jnp.bfloat16
LOG2E = 1.4426950408889634
MIB = 1024 * 1024
PAIRS = HEADS // 2
PAIR = 2 * HEAD_DIM


def dot_nn(left, right):
    return lax.dot_general(left, right, (((1,), (0,)), ((), ())), preferred_element_type=f32)


def dot_nt(left, right):
    return lax.dot_general(left, right, (((1,), (1,)), ((), ())), preferred_element_type=f32)


def dot_tn(left, right):
    return lax.dot_general(left, right, (((0,), (0,)), ((), ())), preferred_element_type=f32)


def norm_parts(values_in):
    center = jnp.mean(values_in, axis=-1, keepdims=True)
    offset = values_in - center
    spread = jnp.mean(offset * offset, axis=-1, keepdims=True)
    rstd = lax.rsqrt(spread + EPS_NORM)
    return offset * rstd, rstd


def norm_back(grad, unit, rstd, gain):
    scaled = grad * gain
    first = jnp.mean(scaled, axis=-1, keepdims=True)
    second = jnp.mean(scaled * unit, axis=-1, keepdims=True)
    return rstd * (scaled - first - unit * second)


def gelu_parts(value):
    bell = jnp.exp2(value * value * (-0.5 * LOG2E))
    ratio = pl.reciprocal(1.0 + (0.3275911 * 0.7071067811865476) * jnp.abs(value))
    poly = 0.5 * 1.061405429
    poly = poly * ratio + 0.5 * -1.453152027
    poly = poly * ratio + 0.5 * 1.421413741
    poly = poly * ratio + 0.5 * -0.284496736
    poly = poly * ratio + 0.5 * 0.254829592
    tail = poly * ratio * bell
    cdf = jnp.where(value >= 0.0, 1.0 - tail, tail)
    return value * cdf, cdf + value * (bell * 0.3989422804014327)


def head_only(block, head):
    lane = lax.broadcasted_iota(jnp.int32, block.shape, 1)
    keep = (lane >= head * HEAD_DIM) & (lane < (head + 1) * HEAD_DIM)
    return jnp.where(keep, block, jnp.zeros_like(block))


def feed_kernel(
    c_ref, o_ref, x_ref, g_ref, w_ref, vec_ref,
    y_ref, r_ref, d_ref, sums_ref, tiles_ref,
    acc_ref, unit_ref, rstd_ref, normed, turned_ref, out_ref, grad_ref,
    hidden_ref, pulled_ref, active_ref, slope_ref, stage_ref, sem_ref,
):
    fold = FF // D
    step = pl.program_id(0)
    blocks = [slice(start, start + 16) for start in range(0, x_ref.shape[0], 16)]

    @pl.when(step == 0)
    def clear():
        acc_ref[...] = jnp.zeros_like(acc_ref)
        sums_ref[...] = jnp.zeros_like(sums_ref)

    def eights(value):
        return jnp.sum(value.reshape(-1, 8, D), axis=0)

    def add_sum(row, value):
        sums_ref[row : row + 1, :] += jnp.sum(value, 0, keepdims=True)

    out_ref[...] = dot_nn(c_ref[...], w_ref[0])
    gain = vec_ref[2:3, :]
    for rows in blocks:
        residual = x_ref[rows].astype(f32) + (out_ref[rows] + vec_ref[6:7, :])
        unit, rstd = norm_parts(residual)
        unit_ref[rows] = unit.astype(b16)
        rstd_ref[rows] = jnp.broadcast_to(rstd, (16, 128))
        normed[rows] = (unit * gain + vec_ref[3:4, :]).astype(b16)
        out_ref[rows] = residual + vec_ref[7:8, :]
    turned_ref[...] = normed[...].T

    def begin(part):
        def hidden():
            hidden_ref[part % 2] = dot_nn(normed[...], w_ref[1 + part])

        def pulled():
            pulled_ref[part % 2] = dot_nt(g_ref[...], w_ref[1 + fold + part])

        return [hidden, pulled]

    def end(part):
        slot = part % 2

        def out():
            out_ref[...] += dot_nn(active_ref[slot], w_ref[1 + fold + part])

        def back():
            grad = dot_nt(slope_ref[slot], w_ref[1 + part])
            grad_ref[...] = grad if part == 0 else grad_ref[...] + grad

        def up():
            acc_ref[1 + part] += dot_nn(turned_ref[...], slope_ref[slot])

        def down():
            acc_ref[1 + fold + part] += dot_tn(active_ref[slot], g_ref[...])

        return [out, back, up, down]

    for work in begin(0):
        work()

    def chunk(part):
        slot = part % 2
        work = end(part - 1) if part > 0 else []
        work = work + (begin(part + 1) if part + 1 < fold else [])
        total = jnp.zeros((8, D), f32)
        for index, rows in enumerate(blocks):
            if index * len(work) // len(blocks) != (index - 1) * len(work) // len(blocks):
                work[index * len(work) // len(blocks)]()
            active, slope = gelu_parts(hidden_ref[slot, rows] + vec_ref[8 + part : 9 + part, :])
            active_ref[slot, rows] = active.astype(b16)
            pulled = (pulled_ref[slot, rows] * slope).astype(b16)
            slope_ref[slot, rows] = pulled
            total = total + eights(pulled.astype(f32))
        add_sum(8 + part, total)

    for part in range(fold):
        pl.when(step >= 0)(partial(chunk, part))

    @pl.when(step >= 0)
    def last():
        for work in end(fold - 1):
            work()

    y_ref[...] = out_ref[...].astype(b16)
    totals = [jnp.zeros((8, D), f32) for unused in range(4)]
    for rows in blocks:
        grad, unit, wide = grad_ref[rows], unit_ref[rows].astype(f32), g_ref[rows].astype(f32)
        back = wide + norm_back(grad, unit, rstd_ref[rows, 0:1], gain)
        low = back.astype(b16)
        r_ref[rows] = low
        terms = (grad * unit, grad, low.astype(f32), wide)
        totals = [total + eights(term) for total, term in zip(totals, terms)]
    for row, total in zip((2, 3, 6, 7), totals):
        add_sum(row, total)
    low = r_ref[...]
    d_ref[...] = dot_nt(w_ref[0], low).astype(b16)
    acc_ref[0] += dot_nn(o_ref[...], low)

    @pl.when(step == pl.num_programs(0) - 1)
    def send():
        for part in range(1 + 2 * fold):
            stage_ref[0] = acc_ref[part].astype(b16)
            copy = pltpu.make_async_copy(stage_ref.at[0], tiles_ref.at[part], sem_ref.at[0])
            copy.start()
            copy.wait()


def feed(context, turned, x, cot, weights, vectors):
    tokens = x.shape[0]
    size = 512
    count = 1 + 2 * (FF // D)
    token_block = pl.BlockSpec((size, D), lambda i: (i, 0))
    turned_block = pl.BlockSpec((D, size), lambda i: (0, i))
    return pl.pallas_call(
        feed_kernel,
        grid=(tokens // size,),
        in_specs=[
            pl.BlockSpec((size, D), lambda i: (i, 0), pipeline_mode=pl.Buffered(1)),
            pl.BlockSpec((D, size), lambda i: (0, i), pipeline_mode=pl.Buffered(1)),
            pl.BlockSpec((size, D), lambda i: (i, 0), pipeline_mode=pl.Buffered(1)),
            token_block,
            pl.BlockSpec((count, D, D), lambda i: (0, 0, 0), pipeline_mode=pl.Buffered(1)),
            pl.BlockSpec((PIECES, D), lambda i: (0, 0)),
        ],
        out_specs=[
            token_block,
            token_block,
            turned_block,
            pl.BlockSpec((16, D), lambda i: (0, 0)),
            pl.BlockSpec(memory_space=pl.ANY),
        ],
        out_shape=[
            jax.ShapeDtypeStruct((tokens, D), b16),
            jax.ShapeDtypeStruct((tokens, D), b16),
            jax.ShapeDtypeStruct((D, tokens), b16),
            jax.ShapeDtypeStruct((16, D), f32),
            jax.ShapeDtypeStruct((count, D, D), b16),
        ],
        scratch_shapes=[
            pltpu.VMEM((count, D, D), f32),
            pltpu.VMEM((size, D), b16),
            pltpu.VMEM((size, 128), f32),
            pltpu.VMEM((size, D), b16),
            pltpu.VMEM((D, size), b16),
            pltpu.VMEM((size, D), f32),
            pltpu.VMEM((size, D), f32),
            pltpu.VMEM((2, size, D), f32),
            pltpu.VMEM((2, size, D), f32),
            pltpu.VMEM((2, size, D), b16),
            pltpu.VMEM((2, size, D), b16),
            pltpu.VMEM((1, D, D), b16),
            pltpu.SemaphoreType.DMA((1,)),
        ],
        compiler_params=pltpu.CompilerParams(vmem_limit_bytes=60 * MIB),
        cost_estimate=pl.CostEstimate(
            flops=6 * count * tokens * D * D,
            bytes_accessed=18 * tokens * D + 4 * count * D * D,
            transcendentals=2 * tokens * FF,
        ),
        name="feed",
    )(context, turned, x, cot, weights, vectors)


MESH = pl.DeviceIdType.MESH
HALF = D // 2
FLOWS = 2
FLOW = HALF // FLOWS
NEAR = FLOW // 2
KEEP = NEAR // 2
WIDE = 3 * PAIR
REST = PIECES - 3
GROUPS = ((0, 1), (1, 2), (3, 3))
CHUNKS = len(GROUPS)


class Place:
    def __init__(self):
        self.me = lax.axis_index("dp")
        self.core = lax.axis_index("blk")
        self.bits = [lax.rem(self.me // weight, 2) for weight in (1, 2, 4, 8)]
        self.chips = [
            self.me + weight - 2 * weight * bit for weight, bit in zip((1, 2, 4, 8), self.bits)
        ]
        self.partners = [{"dp": chip} for chip in self.chips]
        low, high = self.bits[2:]
        self.inner = low != high
        self.across = {"dp": self.me + 4 - 8 * low + 8 - 16 * high}
        self.other = 1 - self.core
        self.twin = {"blk": self.other}

    def greet(self):
        barrier = pltpu.get_barrier_semaphore()
        for device in self.partners + [self.across, self.twin]:
            pl.semaphore_signal(barrier, 1, device_id=device, device_id_type=MESH)
        pl.semaphore_wait(barrier, 6)

    def flow(self, index):
        first, second = (0, 1) if index == 0 else (1, 0)
        base = index * FLOW
        near = base + self.bits[first] * NEAR
        far = base + NEAR - self.bits[first] * NEAR
        keep = near + self.bits[second] * KEEP
        give = near + KEEP - self.bits[second] * KEEP
        return first, second, near, far, keep, give


def remote(source, target, send, receive, device):
    return pltpu.make_async_remote_copy(
        src_ref=source,
        dst_ref=target,
        send_sem=send,
        recv_sem=receive,
        device_id=device,
        device_id_type=MESH,
    )


def rows_at(start, count):
    return pl.ds(pl.multiple_of(start, 16), count)


class Spread:
    def __init__(self, place, owner, rank, slots, land, gift, sems):
        self.place, self.owner, self.rank = place, owner, rank
        self.slots, self.land, self.gift, self.sems = slots, land, gift, sems

    def cols(self, chunk):
        return pl.ds(GROUPS[chunk][0] * PAIR, GROUPS[chunk][1] * PAIR)

    def first_copy(self, chunk, index):
        first, second, near, far, keep, give = self.place.flow(index)
        return remote(
            self.slots.at[:, rows_at(far, NEAR), self.cols(chunk)],
            self.land[chunk].at[index],
            self.sems[0].at[chunk, index, 0],
            self.sems[1].at[chunk, index, 0],
            self.place.partners[first],
        )

    def second_copy(self, chunk, index, which):
        first, second, near, far, keep, give = self.place.flow(index)
        if which == 0:
            source = self.slots.at[:, rows_at(give, KEEP), self.cols(chunk)]
        else:
            source = self.land[chunk].at[index, :, rows_at(give - near, KEEP)]
        return remote(
            source,
            self.gift[chunk].at[index, pl.ds(which * CAP, CAP)],
            self.sems[0].at[chunk, index, 1 + which],
            self.sems[1].at[chunk, index, 1 + which],
            self.place.partners[second],
        )

    def step(self, chunk, index):
        for flow in range(FLOWS):
            if index == 0:
                self.first_copy(chunk, flow).start()
                self.second_copy(chunk, flow, 0).start()
            if index == 1:
                self.first_copy(chunk, flow).wait()
                self.second_copy(chunk, flow, 1).start()
            if index == 2:
                self.second_copy(chunk, flow, 0).wait()
                self.second_copy(chunk, flow, 1).wait()

    def piece(self, tile, index, chunk, start, count):
        first, second, near, far, keep, give = self.place.flow(index)
        owner, rank = self.owner[tile], self.rank[tile]
        bits = [lax.rem(owner, 2), lax.rem(owner // 2, 2)]
        apart = [bit != mine for bit, mine in zip(bits, self.place.bits)]
        cols = pl.ds(start, count)
        mine = self.slots[rank, rows_at(keep, KEEP), pl.ds(GROUPS[chunk][0] * PAIR + start, count)]
        firsts = self.land[chunk][index, rank, rows_at(keep - near, KEEP), cols]
        gifts = self.gift[chunk][index, jnp.where(apart[first], CAP, 0) + rank, :, cols]
        value = jnp.where(apart[second], gifts, jnp.where(apart[first], firsts, mine))
        layer = owner // 4 == self.place.me // 4
        return jnp.where(layer, value, jnp.zeros_like(value))


class Column:
    steps = 4

    def __init__(self, place, kept, read, write, land, sems):
        self.place, self.kept, self.read, self.write = place, kept, read, write
        self.land, self.sems = land, sems

    def copy(self, index):
        target = self.land.at[index % 2]
        device = self.place.across if index == 1 else self.place.partners[2]
        return remote(
            self.kept, target, self.sems[0].at[index], self.sems[1].at[index], device
        )

    def add(self, index):
        self.write((self.read().astype(f32) + self.land[index].astype(f32)).astype(b16))


def column_step(place, columns, index):
    @pl.when(place.inner)
    def inner():
        for column in columns:
            if index == 1:
                column.copy(0).wait_recv()
                column.add(0)
                column.copy(1).start()
            if index == 2:
                column.copy(1).wait()
                column.add(1)
                column.copy(2).start()
            if index == 3:
                column.copy(2).wait_send()

    @pl.when(jnp.logical_not(place.inner))
    def outer():
        for column in columns:
            if index == 0:
                column.copy(0).start()
            if index == 1:
                column.copy(0).wait_send()
            if index == 3:
                column.copy(2).wait_recv()
                column.write(column.land[0])


class Item:
    steps = 8

    def __init__(self, place, work, land, sems, load, store=None):
        self.place, self.work, self.land, self.sems = place, work, land, sems
        self.load, self.store = load, store
        self.base = place.core * HALF

    def column(self, flow):
        rows = rows_at(self.base + self.place.flow(flow)[4], KEEP)

        def read():
            return self.work[:, rows]

        def write(value):
            self.work[:, rows] = value

        sems = (self.sems[0].at[flow], self.sems[1].at[flow])
        return Column(self.place, self.work.at[:, rows], read, write, self.land.at[flow], sems)

    def copy(self, flow, index):
        first, second, near, far, keep, give = self.place.flow(flow)
        kept = self.work.at[:, rows_at(self.base + keep, KEEP)]
        half = self.work.at[:, rows_at(self.base + near, NEAR)]
        source, device = [
            (kept, self.place.partners[second]),
            (half, self.place.partners[first]),
        ][index]
        return remote(
            source, source, self.sems[0].at[flow, 3 + index], self.sems[1].at[flow, 3 + index], device
        )

    def pair(self):
        rows = self.work.at[:, rows_at(self.base, HALF)]
        return remote(rows, rows, self.sems[0].at[0, 5], self.sems[1].at[0, 5], self.place.twin)

    def step(self, index):
        for flow in range(FLOWS):
            if index == 0:
                self.load(self.work, rows_at(self.base + self.place.flow(flow)[4], KEEP), flow)
        if index <= 3:
            column_step(self.place, [self.column(flow) for flow in range(FLOWS)], index)
        for flow in range(FLOWS):
            if 5 <= index <= 6:
                self.copy(flow, index - 5).wait()
            if 4 <= index <= 5:
                self.copy(flow, index - 4).start()
        if index == 6:
            self.pair().start()
        if index == 7:
            self.pair().wait()
            self.store().start()


REST_GROUPS = tuple((index, 1) for index in range(REST))
PAIR_CHUNK = (0, 1, 1, 2, 2, 2)
FRONT_PAIRS = (2, 4, 6, 8, 9, 10)
FRONT_REST = (8, 9, 9, 10, 11, 11, 12, 13, 14)
FRONT_LEAD = 9


def front_kernel(
    owner, lengths, master, vec_ref, x_in, c_in,
    x_out, c_out, n_out, one_out, two_out, q_ref, k_ref, v_ref, p_ref, r_ref, o_ref, ctx_ref,
    rank, rows_ref, normed, keys, turned_values, scores, slots,
    land_one, land_two, land_three, gift_one, gift_two, gift_three,
    one, one_land, two, two_land,
    spread_send, spread_recv, one_send, one_recv, two_send, two_recv,
    swap_send, swap_recv, swap_local, store_sem,
):
    pair = pl.program_id(0)
    row = pl.program_id(1)
    grid_step = pair * 2 + row
    place = Place()
    rows, span = x_in.shape[0] // 2, x_in.shape[1]
    land = (land_one, land_two, land_three)
    gift = (gift_one, gift_two, gift_three)
    spread = Spread(place, owner, rank, slots, land, gift, (spread_send, spread_recv))

    def swaps(index):
        source, target = [(x_in, rows_ref), (c_in, c_out)][index]
        here = pl.ds(place.core * span, span)
        near = pltpu.make_async_copy(
            source.at[pl.ds(place.core * rows, rows)], target.at[:, here], swap_local.at[index]
        )
        far = remote(
            source.at[pl.ds(place.other * rows, rows)],
            target.at[:, here],
            swap_send.at[index],
            swap_recv.at[index],
            place.twin,
        )
        return near, far

    def row_store():
        return pltpu.make_async_copy(rows_ref, x_out, store_sem.at[PAIRS + REST])

    def normed_store():
        return pltpu.make_async_copy(normed, n_out, store_sem.at[PAIRS + REST + 1])

    def pair_item(group):
        span_of = pl.ds(group, 1)

        def load(work, where, flow):
            chunk = PAIR_CHUNK[group]
            for tile in range(3):
                part = spread.piece(tile, flow, chunk, (group - GROUPS[chunk][0]) * PAIR, PAIR)
                work[0, where, pl.ds(tile * PAIR, PAIR)] = part

        def store():
            return pltpu.make_async_copy(one.at[span_of], one_out.at[span_of], store_sem.at[group])

        sems = (one_send.at[group], one_recv.at[group])
        return Item(place, one.at[span_of], one_land.at[:, :, span_of], sems, load, store)

    def rest_item(group):
        first, count = REST_GROUPS[group]
        span_of = pl.ds(first, count)

        def load(work, where, flow):
            for index in range(count):
                for chunk, (start, wide) in enumerate(GROUPS):
                    part = spread.piece(3 + first + index, flow, chunk, 0, wide * PAIR)
                    work[index, where, pl.ds(start * PAIR, wide * PAIR)] = part

        def store():
            return pltpu.make_async_copy(
                two.at[span_of], two_out.at[span_of], store_sem.at[PAIRS + group]
            )

        sems = (two_send.at[group], two_recv.at[group])
        return Item(place, two.at[span_of], two_land.at[:, :, span_of], sems, load, store)

    def tick(number, odd):
        for chunk in range(CHUNKS):
            if odd == 0 and 0 <= number - 2 * chunk <= 2:
                spread.step(chunk, number - 2 * chunk)
        starts = [(pair_item, group, start) for group, start in enumerate(FRONT_PAIRS)]
        starts += [(rest_item, group, start) for group, start in enumerate(FRONT_REST)]
        for make, group, begin in starts:
            ticks = [begin, begin + 1, begin + 2, begin + 3]
            ticks += [begin + 3, begin + 4, begin + 5, begin + 6]
            for index, when in enumerate(ticks):
                if group % 2 == odd and number == when:
                    make(group).step(index)

    def both(number):
        tick(number, 0)
        tick(number, 1)

    @pl.when(grid_step == 0)
    def lead():
        slots[...] = master[...].astype(b16)
        for tile in range(PIECES):
            count = jnp.int32(0)
            for before in range(tile):
                count = count + (owner[before] == owner[tile]).astype(jnp.int32)
            rank[tile] = jnp.minimum(count, CAP - 1)
        place.greet()
        for copy in swaps(0):
            copy.start()
        both(0)
        for copy in swaps(1):
            copy.start()
        for copy in swaps(0):
            copy.wait()
        row_store().start()

        def norm_rows(index, carry):
            for part in range(rows):
                for block in range(4):
                    where = pl.ds(pl.multiple_of(index * 128 + block * 32, 32), 32)
                    unit, unused = norm_parts(rows_ref[part, where].astype(f32))
                    low = (unit * vec_ref[0:1, :] + vec_ref[1:2, :]).astype(b16)
                    normed[pl.ds(pl.multiple_of(part * LEN + index * 128 + block * 32, 32), 32)] = low
            return carry

        both(1)
        lax.fori_loop(0, LEN // 128, norm_rows, 0)
        normed_store().start()
        for number in range(2, FRONT_LEAD):
            both(number)

    for number in range(2 * PAIRS):
        pl.when(grid_step == number)(partial(tick, FRONT_LEAD + number, 0))

    @pl.when(row == 0)
    def project():
        lanes = pl.ds(pl.multiple_of(pair * PAIR, PAIR), PAIR)
        weight = one[pair]

        def part(index, carry):
            where = pl.ds(pl.multiple_of(index * 512, 512), 512)
            both = dot_nn(normed[where], weight)
            queries = both[:, :PAIR] + vec_ref[4:5, lanes]
            queries = (queries * (HEAD_DIM**-0.5 * LOG2E)).astype(b16)
            q_ref[:, where] = queries.T
            low = both[:, PAIR : 2 * PAIR].astype(b16)
            keys[where] = low
            k_ref[:, where] = low.T
            values = (both[:, 2 * PAIR :] + vec_ref[5:6, lanes]).astype(b16)
            v_ref[where] = values
            turned_values[:, where] = values.T
            return carry

        lax.fori_loop(0, normed.shape[0] // 512, part, 0)

    half = LEN // 2
    start = pl.multiple_of(row * LEN, LEN)
    split = lengths[place.core * rows + row, 0] < LEN
    shift = jnp.where(split, jnp.float32(-1e30), jnp.float32(0.0))

    quarter = LEN // 4
    units = [(head, step) for head in range(2) for step in range(2)]

    def score_block(unit, block, peak):
        head, step = units[unit]
        rows_here = pl.ds(pl.multiple_of(start + block * quarter, quarter), quarter)
        queries = q_ref[:, pl.ds(pl.multiple_of(start + step * half, half), half)]
        raw = dot_nn(head_only(keys[rows_here], head), queries)
        if block // 2 != step:
            raw = raw + shift
        scores[unit % 2, block * quarter : (block + 1) * quarter] = raw
        best = jnp.max(raw.reshape(-1, 8, half), axis=0)
        return best if peak is None else jnp.maximum(peak, best)

    def context_block(unit, block, total):
        head, step = units[unit]
        part = slice(head * HEAD_DIM, (head + 1) * HEAD_DIM)
        cols = pl.ds(pl.multiple_of(start + block * quarter, quarter), quarter)
        here = slice(step * half, (step + 1) * half)
        term = dot_nn(
            turned_values[part, cols], p_ref[head, block * quarter : (block + 1) * quarter, here]
        )
        return term if total is None else total + term

    def context_store(unit, total, recip):
        head, step = units[unit]
        part = slice(head * HEAD_DIM, (head + 1) * HEAD_DIM)
        o_ref[part, step * half : (step + 1) * half] = (total * recip).astype(b16)

    peak = None
    for block in range(4):
        peak = score_block(0, block, peak)
    before = None
    for unit, (head, step) in enumerate(units):
        if unit == 2:
            for number in range(2 * PAIRS):
                pl.when(grid_step == number)(partial(tick, FRONT_LEAD + number, 1))
        here = slice(step * half, (step + 1) * half)
        top = jnp.max(peak, 0, keepdims=True)
        total = jnp.zeros((8, half), f32)
        peak, context = None, None
        for block in range(4):
            if unit + 1 < len(units):
                peak = score_block(unit + 1, block, peak)
            for small in range(4 * block, 4 * block + 4):
                rows_here = slice(small * 64, (small + 1) * 64)
                value = jnp.exp2(scores[unit % 2, rows_here] - top)
                total = total + jnp.sum(value.reshape(-1, 8, half), axis=0)
                p_ref[head, rows_here, here] = value.astype(b16)
            if unit > 0:
                context = context_block(unit - 1, block, context)
        if unit > 0:
            context_store(unit - 1, context, before)
        before = 1.0 / jnp.sum(total, 0, keepdims=True)
        r_ref[0, head : head + 1, here] = before
    context = None
    for block in range(4):
        context = context_block(3, block, context)
    context_store(3, context, before)
    ctx_ref[...] = o_ref[...].T

    @pl.when(grid_step == 2 * PAIRS - 1)
    def finish_copies():
        for copy in swaps(1):
            copy.wait()
        row_store().wait()
        normed_store().wait()
        for group in range(PAIRS):
            pair_item(group).store().wait()
        for group in range(REST):
            rest_item(group).store().wait()


def front(owner, lengths, master, vectors, inputs, cotangent):
    rows, span = inputs.shape[0] // 2, inputs.shape[1]
    tokens = rows * LEN
    any_spec = pl.BlockSpec(memory_space=pl.ANY)
    smem = pl.BlockSpec(memory_space=pltpu.SMEM)
    whole = jax.ShapeDtypeStruct((rows, LEN, D), b16)
    dma = pltpu.SemaphoreType.DMA
    return pl.pallas_call(
        front_kernel,
        grid=(PAIRS, rows),
        in_specs=[
            smem,
            smem,
            pl.BlockSpec((CAP, HALF, D), lambda h, r: (0, 0, 0), pipeline_mode=pl.Buffered(1)),
            pl.BlockSpec((PIECES, D), lambda h, r: (0, 0)),
            any_spec,
            any_spec,
        ],
        out_specs=[any_spec] * 5
        + [
            pl.BlockSpec((PAIR, tokens), lambda h, r: (h, 0)),
            pl.BlockSpec((PAIR, tokens), lambda h, r: (h, 0)),
            pl.BlockSpec((tokens, PAIR), lambda h, r: (0, h)),
            pl.BlockSpec((2, LEN, LEN), lambda h, r: (h * 2 + r, 0, 0)),
            pl.BlockSpec((1, 2, LEN), lambda h, r: (h * 2 + r, 0, 0)),
            pl.BlockSpec((PAIR, LEN), lambda h, r: (h, r)),
            pl.BlockSpec((LEN, PAIR), lambda h, r: (r, h)),
        ],
        out_shape=[
            whole,
            whole,
            jax.ShapeDtypeStruct((tokens, D), b16),
            jax.ShapeDtypeStruct((PAIRS, D, WIDE), b16),
            jax.ShapeDtypeStruct((REST, D, D), b16),
            jax.ShapeDtypeStruct((D, tokens), b16),
            jax.ShapeDtypeStruct((D, tokens), b16),
            jax.ShapeDtypeStruct((tokens, D), b16),
            jax.ShapeDtypeStruct((rows * HEADS, LEN, LEN), b16),
            jax.ShapeDtypeStruct((rows * PAIRS, 2, LEN), f32),
            jax.ShapeDtypeStruct((D, tokens), b16),
            jax.ShapeDtypeStruct((tokens, D), b16),
        ],
        scratch_shapes=[
            pltpu.SMEM((PIECES,), jnp.int32),
            pltpu.VMEM((rows, LEN, D), b16),
            pltpu.VMEM((tokens, D), b16),
            pltpu.VMEM((tokens, PAIR), b16),
            pltpu.VMEM((PAIR, tokens), b16),
            pltpu.VMEM((2, LEN, LEN // 2), f32),
            pltpu.VMEM((CAP, HALF, D), b16),
        ]
        + [pltpu.VMEM((FLOWS, CAP, NEAR, wide * PAIR), b16) for unused, wide in GROUPS]
        + [pltpu.VMEM((FLOWS, 2 * CAP, KEEP, wide * PAIR), b16) for unused, wide in GROUPS]
        + [
            pltpu.VMEM((PAIRS, D, WIDE), b16),
            pltpu.VMEM((FLOWS, 2, PAIRS, KEEP, WIDE), b16),
            pltpu.VMEM((REST, D, D), b16),
            pltpu.VMEM((FLOWS, 2, REST, KEEP, D), b16),
            dma((CHUNKS, FLOWS, 3)),
            dma((CHUNKS, FLOWS, 3)),
            dma((PAIRS, FLOWS, 6)),
            dma((PAIRS, FLOWS, 6)),
            dma((REST, FLOWS, 6)),
            dma((REST, FLOWS, 6)),
            dma((2,)),
            dma((2,)),
            dma((2,)),
            dma((PAIRS + REST + 2,)),
        ],
        compiler_params=pltpu.CompilerParams(
            collective_id=0, has_side_effects=True, vmem_limit_bytes=60 * MIB
        ),
        name="front",
    )(owner, lengths, master, vectors, inputs, cotangent)


class Sum:
    steps = 7

    def __init__(self, place, work, wide, narrow, sems, send_pair, add_own):
        self.place, self.work, self.wide, self.narrow, self.sems = place, work, wide, narrow, sems
        self.send_pair, self.add_own = send_pair, add_own

    def column(self, flow):
        rows = rows_at(self.place.flow(flow)[4], KEEP)

        def read():
            return self.work[:, rows]

        def write(value):
            self.work[:, rows] = value

        sems = (self.sems[0].at[flow, pl.ds(2, 3)], self.sems[1].at[flow, pl.ds(2, 3)])
        land = self.narrow.at[flow, pl.ds(1, 2)]
        return Column(self.place, self.work.at[:, rows], read, write, land, sems)

    def copy(self, flow, index):
        first, second, near, far, keep, give = self.place.flow(flow)
        source, target, device = [
            (self.work.at[:, rows_at(far, NEAR)], self.wide.at[flow], first),
            (self.work.at[:, rows_at(give, KEEP)], self.narrow.at[flow, 0], second),
        ][index]
        return remote(
            source,
            target,
            self.sems[0].at[flow, index],
            self.sems[1].at[flow, index],
            self.place.partners[device],
        )

    def add(self, rows, value):
        self.work[:, rows] = (self.work[:, rows].astype(f32) + value.astype(f32)).astype(b16)

    def step(self, index):
        if index == 0:
            self.send_pair().start()
        if index == 1:
            self.send_pair().wait()
            self.add_own()
        for flow in range(FLOWS):
            first, second, near, far, keep, give = self.place.flow(flow)
            if index == 1:
                self.copy(flow, 0).start()
            if index == 2:
                self.copy(flow, 0).wait()
                self.add(rows_at(near, NEAR), self.wide[flow])
                self.copy(flow, 1).start()
            if index == 3:
                self.copy(flow, 1).wait()
                self.add(rows_at(keep, KEEP), self.narrow[flow, 0])
        if index >= 3:
            columns = [self.column(flow) for flow in range(FLOWS)]
            column_step(self.place, columns, index - 3)


class Gather:
    steps = 3

    def __init__(self, place, work, narrow, wide, sems):
        self.place, self.work, self.narrow, self.wide = place, work, narrow, wide
        self.sems = sems

    def copy(self, flow, index):
        first, second, near, far, keep, give = self.place.flow(flow)
        rows, target, device = [
            (rows_at(keep, KEEP), self.narrow, second),
            (rows_at(near, NEAR), self.wide, first),
        ][index]
        return remote(
            self.work.at[:, rows],
            target.at[flow],
            self.sems[0].at[flow, 5 + index],
            self.sems[1].at[flow, 5 + index],
            self.place.partners[device],
        )

    def step(self, index):
        for flow in range(FLOWS):
            first, second, near, far, keep, give = self.place.flow(flow)
            if index > 0:
                self.copy(flow, index - 1).wait()
            if index == 1:
                self.work[:, rows_at(give, KEEP)] = self.narrow[flow]
            if index == 2:
                self.work[:, rows_at(far, NEAR)] = self.wide[flow]
            if index < 2:
                self.copy(flow, index).start()


class Hand:
    steps = 3

    def __init__(self, place, table, work, bag, gift, pack, last, own, out, sems, store_sems):
        self.place, self.table, self.work = place, table, work
        self.bag, self.gift, self.pack, self.last, self.own = bag, gift, pack, last, own
        self.out, self.sems, self.store_sems = out, sems, store_sems

    def tile(self, chip, rank, rows):
        return self.work[self.table[chip * CAP + rank], rows]

    def copy(self, flow, index):
        first, second = self.place.flow(flow)[:2]
        source, target, device = [
            (self.bag.at[flow], self.gift.at[flow], second),
            (self.pack.at[flow], self.last.at[flow], first),
        ][index]
        return remote(
            source,
            target,
            self.sems[0].at[flow, index],
            self.sems[1].at[flow, index],
            self.place.partners[device],
        )

    def stores(self, flow):
        first, second, near, far, keep, give = self.place.flow(flow)
        parts = [
            (self.own.at[flow], rows_at(keep, KEEP)),
            (self.gift.at[flow, pl.ds(0, CAP)], rows_at(give, KEEP)),
            (self.last.at[flow], rows_at(far, NEAR)),
        ]
        return [
            pltpu.make_async_copy(source, self.out.at[:, rows], self.store_sems.at[flow, index])
            for index, (source, rows) in enumerate(parts)
        ]

    def step(self, index):
        for flow in range(FLOWS):
            first, second, near, far, keep, give = self.place.flow(flow)
            rows = rows_at(keep, KEEP)
            if index == 0:
                beside = self.place.chips[second]
                across = beside + self.place.chips[first] - self.place.me
                for rank in range(CAP):
                    self.bag[flow, rank] = self.tile(beside, rank, rows)
                    self.bag[flow, CAP + rank] = self.tile(across, rank, rows)
                    self.own[flow, rank] = self.tile(self.place.me, rank, rows)
                self.copy(flow, 0).start()
            if index == 1:
                self.copy(flow, 0).wait()
                for rank in range(CAP):
                    mine = self.tile(self.place.chips[first], rank, rows)
                    self.pack[flow, rank, rows_at(keep - near, KEEP)] = mine
                    self.pack[flow, rank, rows_at(give - near, KEEP)] = self.gift[flow, CAP + rank]
                self.copy(flow, 1).start()
            if index == 2:
                self.copy(flow, 1).wait()
                for copy in self.stores(flow):
                    copy.start()


BACK_STEPS = 2 * PAIRS
BACK_TAIL = 4
BACK_PAIRS = tuple((index, 1) for index in range(PAIRS))
BACK_REST = (0, 1, 2, 3, 4, 5, 6, 7, 8)
BACK_HAND = 15


def back_kernel(
    table, p_ref, r_ref, v_ref, q_ref, k_ref, o_ref, g_ref, w_ref, n_ref, x_ref, z_ref, vec_ref,
    tiles_in, sums_in, y_in,
    y_out, i_out, pairs_out, slots_out, sums_ref,
    grad_sum, wide_sum, turned, slopes, block_out,
    two, two_wide, two_narrow, two_stage, one, one_wide, one_narrow, one_send_stage, one_stage,
    gather_narrow, gather_wide,
    bag, gift, pack, last, own, vec_land,
    two_send, two_recv, one_send, one_recv, hand_send, hand_recv, hand_store,
    pair_two_send, pair_two_recv, pair_one_send, pair_one_recv, load_sem, store_sem,
    swap_send, swap_recv, swap_local, vec_send, vec_recv,
):
    step = pl.program_id(0)
    place = Place()
    rows, span = y_in.shape[0], y_in.shape[1] // 2
    near_half = rows_at(place.core * HALF, HALF)
    far_half = rows_at(place.other * HALF, HALF)

    def load_two(group):
        first, count = REST_GROUPS[group]
        return pltpu.make_async_copy(
            tiles_in.at[pl.ds(first, count), near_half],
            two_stage.at[pl.ds(group % 3, 1)],
            load_sem.at[group % 3],
        )

    def rest_sum(group):
        first, count = REST_GROUPS[group]
        span_of = pl.ds(first, count)
        work = two.at[span_of]

        def send_pair():
            return remote(
                tiles_in.at[span_of, far_half],
                work,
                pair_two_send.at[group],
                pair_two_recv.at[group],
                place.twin,
            )

        def add_own():
            load_two(group).wait()
            work[...] = (work[...].astype(f32) + two_stage[group % 3].astype(f32)).astype(b16)

        sems = (two_send.at[group], two_recv.at[group])
        wide, narrow = two_wide.at[:, span_of], two_narrow.at[:, :, span_of]
        return Sum(place, work, wide, narrow, sems, send_pair, add_own)

    def pair_sum(group):
        first, count = BACK_PAIRS[group]
        span_of = pl.ds(first, count)
        work = one.at[span_of]

        def send_pair():
            return remote(
                one_send_stage.at[pl.ds(group % 2, 1)],
                work,
                pair_one_send.at[group],
                pair_one_recv.at[group],
                place.twin,
            )

        def add_own():
            own = one_stage[group % 2].astype(f32)
            work[...] = (work[...].astype(f32) + own).astype(b16)

        sems = (one_send.at[group], one_recv.at[group])
        wide, narrow = one_wide.at[:, span_of], one_narrow.at[:, :, span_of]
        return Sum(place, work, wide, narrow, sems, send_pair, add_own)

    def pair_gather(group):
        first, count = BACK_PAIRS[group]
        span_of = pl.ds(first, count)
        sems = (one_send.at[group], one_recv.at[group])
        narrow, wide = gather_narrow.at[:, span_of], gather_wide.at[:, span_of]
        return Gather(place, one.at[span_of], narrow, wide, sems)

    hand = Hand(
        place, table, two, bag, gift, pack, last, own, slots_out, (hand_send, hand_recv), hand_store
    )

    def pair_store(index, tile):
        return pltpu.make_async_copy(
            one.at[index, :, pl.ds(tile * PAIR, PAIR)],
            pairs_out.at[tile, :, pl.ds(index * PAIR, PAIR)],
            store_sem.at[index, tile],
        )

    def tick(number, odd):
        for group, start in enumerate(BACK_REST):
            if group % 2 == odd and 0 <= number - start < Sum.steps:
                rest_sum(group).step(number - start)
        for group, (first, count) in enumerate(BACK_PAIRS):
            if group % 2 != odd:
                continue
            start = 2 * (first + count)
            if 0 <= number - start < Sum.steps:
                pair_sum(group).step(number - start)
            if 0 <= number - start - Sum.steps + 1 < Gather.steps:
                pair_gather(group).step(number - start - Sum.steps + 1)
            if number == start + Sum.steps + 1:
                for index in range(first, first + count):
                    for tile in range(3):
                        pair_store(index, tile).start()
        if odd == 0 and 0 <= number - BACK_HAND < Hand.steps:
            hand.step(number - BACK_HAND)
        for group, start in enumerate(BACK_REST):
            if odd == 1 and number == max(start - 1, 0):
                load_two(group).start()

    def both(number):
        tick(number, 0)
        tick(number, 1)

    def swap_y(index):
        there = pl.ds(place.core * rows, rows)
        if index == 0:
            return pltpu.make_async_copy(
                y_in.at[:, pl.ds(place.core * span, span)], y_out.at[there], swap_local.at[0]
            )
        return remote(
            y_in.at[:, pl.ds(place.other * span, span)],
            y_out.at[there],
            swap_send.at[0],
            swap_recv.at[0],
            place.twin,
        )

    @pl.when(step == 0)
    def lead():
        place.greet()
        for index in range(2):
            swap_y(index).start()
        sums_ref[...] = sums_in[...]

    for number in range(BACK_STEPS + BACK_TAIL):
        early = partial(tick, number, 0) if number < BACK_STEPS else partial(both, number)
        pl.when(step == number)(early)

    half = LEN // 2
    pair, row = step // 2, lax.rem(step, 2)

    quarter = LEN // 4

    def attention_inputs(head):
        part = slice(head * HEAD_DIM, (head + 1) * HEAD_DIM)
        values = head_only(v_ref[...], head)
        recip = r_ref[0, head : head + 1, :]
        grad = g_ref[part, :].astype(f32) * recip
        delta = jnp.sum(grad * o_ref[part, :].astype(f32), 0, keepdims=True)
        grad = grad.astype(b16)
        return values, grad, delta, jnp.concatenate([grad, grad], axis=0)

    def attention(head):
        part = slice(head * HEAD_DIM, (head + 1) * HEAD_DIM)
        values, grad, delta, doubled = attention_inputs(head)
        units = [(which, block) for which in range(2) for block in range(4)]
        value_grad, key_grad, query_grad = {}, {}, {}

        def raw_block(unit):
            which, block = units[unit]
            cols = slice(which * half, (which + 1) * half)
            return dot_nn(values[block * quarter : (block + 1) * quarter], doubled[:, cols])

        def slope_block(unit, raw):
            which, block = units[unit]
            cols = slice(which * half, (which + 1) * half)
            for small in range(4):
                rows_here = slice(small * 64, (small + 1) * 64)
                rows_all = slice(block * quarter + small * 64, block * quarter + (small + 1) * 64)
                slope = p_ref[head, rows_all, cols].astype(f32) * (raw[rows_here] - delta[:, cols])
                slopes[unit % 2, rows_here] = slope.astype(b16)

        def add(totals, key, term):
            totals[key] = totals[key] + term if key in totals else term

        def grad_block(unit):
            which, block = units[unit]
            cols = slice(which * half, (which + 1) * half)
            rows_all = slice(block * quarter, (block + 1) * quarter)
            slope = slopes[unit % 2]
            add(value_grad, block, dot_nt(grad[:, cols], p_ref[head, rows_all, cols]))
            add(key_grad, block, dot_nt(q_ref[part, cols], slope))
            add(query_grad, which, dot_nn(k_ref[part, rows_all], slope))

        raw = raw_block(0)
        for unit in range(len(units)):
            after = raw_block(unit + 1) if unit + 1 < len(units) else None
            slope_block(unit, raw)
            if unit > 0:
                grad_block(unit - 1)
            raw = after
        grad_block(len(units) - 1)
        for which in range(2):
            total = query_grad[which] * (HEAD_DIM**-0.5)
            turned[part, which * half : (which + 1) * half] = total.astype(b16)
        for block in range(4):
            rows_all = slice(block * quarter, (block + 1) * quarter)
            lower = slice(PAIR + head * HEAD_DIM, PAIR + (head + 1) * HEAD_DIM)
            turned[lower, rows_all] = (key_grad[block] * (1.0 / LOG2E)).astype(b16)
            lower = slice(2 * PAIR + head * HEAD_DIM, 2 * PAIR + (head + 1) * HEAD_DIM)
            turned[lower, rows_all] = value_grad[block].astype(b16)

    @pl.when(step < BACK_STEPS)
    def first_head():
        attention(0)

    for number in range(BACK_STEPS):
        pl.when(step == number)(partial(tick, number, 1))

    @pl.when(step < BACK_STEPS)
    def second_head():
        attention(1)
        where = pl.ds(pl.multiple_of(row * LEN, LEN), LEN)
        block = dot_nn(turned[...], n_ref[where])
        back = turned[...].T
        lanes = pl.ds(pl.multiple_of(pair * PAIR, PAIR), PAIR)
        ones = jnp.sum(back.astype(f32), 0, keepdims=True)
        sums_ref[4:5, lanes] += ones[:, :PAIR]
        sums_ref[5:6, lanes] += ones[:, 2 * PAIR :]
        term = dot_nt(back, w_ref[0])

        @pl.when(pair == 0)
        def begin():
            grad_sum[where] = term

        @pl.when(pair > 0)
        def add():
            grad_sum[where] += term

        @pl.when(row == 0)
        def keep():
            wide_sum[...] = block

        @pl.when(row == 1)
        def hand_on():
            whole = (wide_sum[...] + block).T
            low = whole.astype(b16)
            for core in range(2):

                @pl.when(place.core == core)
                def split():
                    slot = lax.rem(pair, 2)
                    one_stage[slot] = low[core * HALF : (core + 1) * HALF]
                    one_send_stage[slot] = low[(1 - core) * HALF : (2 - core) * HALF]

    def store_block(index):
        row, half = index // 2, index % 2
        target = i_out.at[place.core * rows + row]
        local = pltpu.make_async_copy(block_out.at[half], target, swap_local.at[1 + row])
        far = remote(
            block_out.at[half], target, swap_send.at[1 + row], swap_recv.at[1 + row], place.twin
        )
        return local, far, half

    def wait_block(index):
        local, far, half = store_block(index)

        @pl.when(place.core == half)
        def keep():
            local.wait()

        @pl.when(place.core != half)
        def give():
            far.wait()

    for index in range(BACK_TAIL):

        @pl.when(step == BACK_STEPS + index)
        def close():
            size = LEN // 2
            if index >= 2:
                wait_block(index - 2)
            gain_sum = jnp.zeros((8, D), f32)
            shift_sum = jnp.zeros((8, D), f32)
            for block in range(size // 16):
                rows_here = slice(block * 16, (block + 1) * 16)
                grad = grad_sum[index * size + block * 16 : index * size + (block + 1) * 16]
                unit, rstd = norm_parts(x_ref[rows_here].astype(f32))
                gain_sum = gain_sum + jnp.sum((grad * unit).reshape(-1, 8, D), axis=0)
                shift_sum = shift_sum + jnp.sum(grad.reshape(-1, 8, D), axis=0)
                total = norm_back(grad, unit, rstd, vec_ref[0:1, :])
                block_out[index % 2, rows_here] = (z_ref[rows_here].astype(f32) + total).astype(b16)
            sums_ref[0:1, :] += jnp.sum(gain_sum, 0, keepdims=True)
            sums_ref[1:2, :] += jnp.sum(shift_sum, 0, keepdims=True)
            local, far, half = store_block(index)

            @pl.when(place.core == half)
            def keep():
                local.start()

            @pl.when(place.core != half)
            def give():
                far.start()

    @pl.when(step == BACK_STEPS + BACK_TAIL - 1)
    def drain():
        devices = [place.twin] + place.partners

        def vector(index):
            return remote(
                sums_ref, vec_land.at[index], vec_send.at[index], vec_recv.at[index], devices[index]
            )

        vector(0).start()
        for number in range(BACK_STEPS + BACK_TAIL, BACK_STEPS + Sum.steps + Gather.steps):
            both(number)
            index = number - BACK_STEPS - BACK_TAIL
            if index < 5:
                vector(index).wait()
                sums_ref[...] += vec_land[index]
                if index < 4:
                    vector(index + 1).start()
        for index in range(2):
            swap_y(index).wait()
        for index in range(2, BACK_TAIL):
            wait_block(index)
        for index in range(PAIRS):
            for tile in range(3):
                pair_store(index, tile).wait()
        for flow in range(FLOWS):
            for copy in hand.stores(flow):
                copy.wait()


def back(table, attention, weights, normed, x, residual, vectors, tiles, sums, y):
    rows, length = y.shape[:2]
    tokens = rows * length
    any_spec = pl.BlockSpec(memory_space=pl.ANY)
    smem = pl.BlockSpec(memory_space=pltpu.SMEM)
    dma = pltpu.SemaphoreType.DMA

    def now(step):
        return jnp.minimum(step, BACK_STEPS - 1)

    def tail(step):
        return jnp.maximum(step - BACK_STEPS, 0)

    head_block = pl.BlockSpec((PAIR, LEN), lambda s: (now(s) // 2, lax.rem(now(s), 2)))
    tail_block = pl.BlockSpec((LEN // 2, D), lambda s: (tail(s), 0))
    whole = pl.BlockSpec((PIECES, D), lambda s: (0, 0))
    sums_block = pl.BlockSpec((16, D), lambda s: (0, 0))
    return pl.pallas_call(
        back_kernel,
        grid=(BACK_STEPS + BACK_TAIL,),
        in_specs=[
            smem,
            pl.BlockSpec((2, LEN, LEN), lambda s: (now(s), 0, 0)),
            pl.BlockSpec((1, 2, LEN), lambda s: (now(s), 0, 0)),
            pl.BlockSpec((LEN, PAIR), lambda s: (lax.rem(now(s), 2), now(s) // 2)),
            head_block,
            head_block,
            head_block,
            head_block,
            pl.BlockSpec((1, D, WIDE), lambda s: (now(s) // 2, 0, 0)),
            pl.BlockSpec((tokens, D), lambda s: (0, 0), pipeline_mode=pl.Buffered(1)),
            tail_block,
            tail_block,
            whole,
            any_spec,
            sums_block,
            any_spec,
        ],
        out_specs=[any_spec] * 4 + [sums_block],
        out_shape=[
            jax.ShapeDtypeStruct((2 * rows, length // 2, D), b16),
            jax.ShapeDtypeStruct((2 * rows, length // 2, D), b16),
            jax.ShapeDtypeStruct((3, HALF, D), b16),
            jax.ShapeDtypeStruct((CAP, HALF, D), b16),
            jax.ShapeDtypeStruct((16, D), f32),
        ],
        scratch_shapes=[
            pltpu.VMEM((tokens, D), f32),
            pltpu.VMEM((WIDE, D), f32),
            pltpu.VMEM((WIDE, LEN), b16),
            pltpu.VMEM((2, LEN // 4, LEN // 2), b16),
            pltpu.VMEM((2, LEN // 2, D), b16),
            pltpu.VMEM((REST, HALF, D), b16),
            pltpu.VMEM((FLOWS, REST, NEAR, D), b16),
            pltpu.VMEM((FLOWS, 3, REST, KEEP, D), b16),
            pltpu.VMEM((3, HALF, D), b16),
            pltpu.VMEM((PAIRS, HALF, WIDE), b16),
            pltpu.VMEM((FLOWS, PAIRS, NEAR, WIDE), b16),
            pltpu.VMEM((FLOWS, 3, PAIRS, KEEP, WIDE), b16),
            pltpu.VMEM((2, HALF, WIDE), b16),
            pltpu.VMEM((2, HALF, WIDE), b16),
            pltpu.VMEM((FLOWS, PAIRS, KEEP, WIDE), b16),
            pltpu.VMEM((FLOWS, PAIRS, NEAR, WIDE), b16),
            pltpu.VMEM((FLOWS, 2 * CAP, KEEP, D), b16),
            pltpu.VMEM((FLOWS, 2 * CAP, KEEP, D), b16),
            pltpu.VMEM((FLOWS, CAP, NEAR, D), b16),
            pltpu.VMEM((FLOWS, CAP, NEAR, D), b16),
            pltpu.VMEM((FLOWS, CAP, KEEP, D), b16),
            pltpu.VMEM((5, 16, D), f32),
            dma((REST, FLOWS, 5)),
            dma((REST, FLOWS, 5)),
            dma((PAIRS, FLOWS, 7)),
            dma((PAIRS, FLOWS, 7)),
            dma((FLOWS, 2)),
            dma((FLOWS, 2)),
            dma((FLOWS, 3)),
            dma((REST,)),
            dma((REST,)),
            dma((PAIRS,)),
            dma((PAIRS,)),
            dma((3,)),
            dma((PAIRS, 3)),
            dma((3,)),
            dma((3,)),
            dma((3,)),
            dma((5,)),
            dma((5,)),
        ],
        compiler_params=pltpu.CompilerParams(
            collective_id=1, has_side_effects=True, vmem_limit_bytes=62 * MIB
        ),
        name="back",
    )(table, *attention, weights, normed, x, residual, vectors, tiles, sums, y)


def update_kernel(tile_at, one, two, w_ref, m_ref, s_ref, y_in, i_in, w_out, m_out, s_out, y_out, i_out):
    step = pl.program_id(0)
    tile = tile_at[step // 2]
    grad = jnp.where(tile < 3, one[0], two[0]).astype(f32)
    parts = adam_step(w_ref[0], grad, m_ref[0], s_ref[0], RATE)
    for target, part in zip((w_out, m_out, s_out), parts):
        target[0] = jnp.where(tile >= 0, part, jnp.zeros_like(part))

    @pl.when(step < 4)
    def widen():
        y_out[...] = y_in[...].astype(f32)
        i_out[...] = i_in[...].astype(f32)


def update(tile_at, one, two, master, first, second, y, grad):
    tokens = y.shape[0]
    size = HALF // 2
    state = pl.BlockSpec((1, size, D), lambda s, tile_at: (s // 2, lax.rem(s, 2), 0))
    wide = pl.BlockSpec((tokens // 4, D), lambda s, tile_at: (jnp.minimum(s, 3), 0))
    return pl.pallas_call(
        update_kernel,
        grid_spec=pltpu.PrefetchScalarGridSpec(
            num_scalar_prefetch=1,
            grid=(CAP * 2,),
            in_specs=[
                pl.BlockSpec(
                    (1, size, D),
                    lambda s, tile_at: (jnp.clip(tile_at[s // 2], 0, 2), lax.rem(s, 2), 0),
                ),
                state,
                state,
                state,
                state,
                wide,
                wide,
            ],
            out_specs=[state] * 3 + [wide] * 2,
        ),
        out_shape=[jax.ShapeDtypeStruct(master.shape, f32)] * 3
        + [jax.ShapeDtypeStruct((tokens, D), f32)] * 2,
        compiler_params=pltpu.CompilerParams(vmem_limit_bytes=60 * MIB),
        name="update",
    )(tile_at, one, two, master, first, second, y, grad)


def shards_paired(
    inputs,
    cotangent,
    doc_lengths,
    owner_list,
    master,
    first_moment,
    second_moment,
    vectors,
    vector_first,
    vector_second,
):
    rows_here, span, width = inputs.shape
    place = lax.axis_index("blk")
    member = lax.axis_index("dp")
    rows_mine = rows_here // 2
    order = jnp.arange(PIECES)
    same_owner = owner_list[:, None] == owner_list[None, :]
    ranks = jnp.sum(same_owner & (order[None, :] < order[:, None]), axis=1).astype(jnp.int32)
    slot_of = owner_list * CAP + ranks
    front_outs = front(owner_list, doc_lengths, master, vectors, inputs, cotangent)
    x, cot, normed, weights_one, weights_two, queries, keys, values = front_outs[:8]
    weights, recips, context_turned, context = front_outs[8:]
    x = x.reshape(-1, width)
    cot = cot.reshape(-1, width)
    block_out, residual, grad_context, sums, tiles_two = feed(
        context, context_turned, x, cot, weights_two, vectors
    )
    hits = jnp.arange(16 * CAP)[:, None] == slot_of[None, :]
    tile_at = jnp.sum(jnp.where(hits, order[None, :] + 1, 0), axis=1).astype(jnp.int32) - 1
    table = jnp.maximum(tile_at - 3, 0)
    block_out, input_grad, total_one, total_two, vector_total = back(
        table,
        (weights, recips, values, queries, keys, context_turned, grad_context),
        weights_one,
        normed,
        x,
        residual,
        vectors,
        tiles_two,
        sums,
        block_out.reshape(rows_mine, LEN, width),
    )
    mine = lax.dynamic_slice_in_dim(tile_at, member * CAP, CAP, 0)
    *updated, block_out, input_grad = update(
        mine,
        total_one,
        total_two,
        master,
        first_moment,
        second_moment,
        block_out.reshape(-1, width),
        input_grad.reshape(-1, width),
    )
    columns = vector_first.shape[1]
    vector_cols = lax.dynamic_slice_in_dim(vectors, place * columns, columns, 1)
    vector_total = lax.dynamic_slice(vector_total, (0, place * columns), (PIECES, columns))
    updated_vectors = adam_step(vector_cols, vector_total, vector_first, vector_second, VEC_RATE)
    return (
        block_out.reshape(inputs.shape),
        input_grad.reshape(inputs.shape),
        *updated,
        *updated_vectors,
    )


def solution(mesh):
    in_specs = (
        P("dp", "blk", None),
        P("dp", "blk", None),
        P("dp", None),
        P(),
        P("dp", "blk", None),
        P("dp", "blk", None),
        P("dp", "blk", None),
        P(),
        P(None, "blk"),
        P(None, "blk"),
    )
    out_specs = (
        P("dp", "blk", None),
        P("dp", "blk", None),
        P("dp", "blk", None),
        P("dp", "blk", None),
        P("dp", "blk", None),
        P(None, "blk"),
        P(None, "blk"),
        P(None, "blk"),
    )
    paired = mesh.shape["blk"] == 2 and mesh.shape["dp"] == 16
    shards = shards_paired if paired else shards_any
    return jax.shard_map(shards, mesh=mesh, in_specs=in_specs, out_specs=out_specs, check_vma=False)
```

```python
from functools import partial

import jax
import jax.numpy as jnp
from jax import lax
from jax.experimental import pallas as pl
from jax.experimental.pallas import tpu as pltpu
from jax.sharding import PartitionSpec as P

D = 768
FF = 3072
HEADS = 12
HEAD_DIM = 64
LEN = 1024
CAP = 3
STEP = 10
PIECES = 12


EPS_NORM = 1e-05
BETA_ONE = 0.9
BETA_TWO = 0.999
RATE = 0.04
VEC_RATE = 0.25
DECAY = 0.01
ADAM_EPS = 1e-08


def normalize(values_in, gain, shift):
    center = jnp.mean(values_in, axis=-1, keepdims=True)
    offset = values_in - center
    spread = jnp.mean(offset * offset, axis=-1, keepdims=True)
    return offset * lax.rsqrt(spread + EPS_NORM) * gain + shift


def adam_step(weight, grad, first, second, rate):
    first_new = BETA_ONE * first + (1.0 - BETA_ONE) * grad
    second_new = BETA_TWO * second + (1.0 - BETA_TWO) * grad * grad
    corrected = (
        first_new
        / (1.0 - BETA_ONE**STEP)
        / (jnp.sqrt(second_new / (1.0 - BETA_TWO**STEP)) + ADAM_EPS)
    )
    return (weight - rate * (corrected + DECAY * weight), first_new, second_new)


def shards_any(
    inputs,
    cotangent,
    doc_lengths,
    owner_list,
    master,
    first_moment,
    second_moment,
    vectors,
    vector_first,
    vector_second,
):
    rows_here, span, width = inputs.shape
    tokens_here = rows_here * span
    fold = FF // D
    scale = HEAD_DIM ** (-0.5)
    place = lax.axis_index("blk")
    f32 = jnp.float32
    b16 = jnp.bfloat16
    order = jnp.arange(PIECES)
    same_owner = owner_list[:, None] == owner_list[None, :]
    ranks = jnp.sum(same_owner & (order[None, :] < order[:, None]), axis=1)
    slot_of = owner_list * CAP + ranks

    mine = (owner_list == lax.axis_index("dp"))[:, None, None]
    tile_rows = lax.psum(jnp.where(mine, master[ranks], 0.0).astype(b16), "dp")
    tiles = lax.all_gather(tile_rows, "blk", axis=1, tiled=True)
    query_weight = tiles[0]
    key_weight = tiles[1]
    value_weight = tiles[2]
    out_weight = tiles[3]
    up_weight = jnp.transpose(tiles[4 : 4 + fold], (1, 0, 2)).reshape(width, FF)
    down_weight = tiles[4 + fold :].reshape(FF, width)
    flat_in = inputs.reshape(tokens_here, width).astype(f32)
    normed_one = normalize(flat_in, vectors[0], vectors[1]).astype(b16)
    queries = (jnp.dot(normed_one, query_weight, preferred_element_type=f32) + vectors[4]).astype(
        b16
    )
    keys_here = jnp.dot(normed_one, key_weight, preferred_element_type=f32).astype(b16)
    values_here = (
        jnp.dot(normed_one, value_weight, preferred_element_type=f32) + vectors[5]
    ).astype(b16)
    query_heads = queries.reshape(rows_here, span, HEADS, HEAD_DIM)
    first_len = doc_lengths[:, 0]
    query_seg = (place * span + jnp.arange(span))[None, :] >= first_len[:, None]

    def block_scores(key_block, start):
        count = key_block.shape[1]
        key_heads = key_block.reshape(rows_here, count, HEADS, HEAD_DIM)
        raw = (
            jnp.einsum("rqhd,rkhd->rhqk", query_heads, key_heads, preferred_element_type=f32)
            * scale
        )
        key_seg = (start + jnp.arange(count))[None, :] >= first_len[:, None]
        allowed = query_seg[:, None, :, None] == key_seg[:, None, None, :]
        return (raw, allowed)

    key_rows = keys_here.reshape(rows_here, span, width)
    value_rows = values_here.reshape(rows_here, span, width)
    top = jnp.full((rows_here, HEADS, span), -1e30, f32)
    key_block = lax.all_gather(key_rows, "blk", axis=1, tiled=True)
    value_block = lax.all_gather(value_rows, "blk", axis=1, tiled=True)
    count = key_block.shape[1]
    raw, allowed = block_scores(key_block, jnp.int32(0))
    new_top = jnp.maximum(top, jnp.max(jnp.where(allowed, raw, -1e30), axis=-1))
    weights = jnp.where(allowed, jnp.exp(raw - new_top[..., None]), 0.0)
    value_heads = value_block.reshape(rows_here, count, HEADS, HEAD_DIM)
    update = jnp.einsum(
        "rhqk,rkhd->rhqd", weights.astype(b16), value_heads, preferred_element_type=f32
    )
    total = jnp.sum(weights, axis=-1)
    log_total = new_top + jnp.log(total)
    context_raw = update / total[..., None]
    context_low = jnp.transpose(context_raw, (0, 2, 1, 3)).reshape(tokens_here, width).astype(b16)
    residual = flat_in + (jnp.dot(context_low, out_weight, preferred_element_type=f32) + vectors[6])
    normed_two = normalize(residual, vectors[2], vectors[3]).astype(b16)
    hidden = jnp.dot(normed_two, up_weight, preferred_element_type=f32) + vectors[8:].reshape(FF)
    gelu_exact = partial(jax.nn.gelu, approximate=False)
    active, gelu_pull = jax.vjp(gelu_exact, hidden)
    active_low = active.astype(b16)
    block_out = (
        residual + (jnp.dot(active_low, down_weight, preferred_element_type=f32) + vectors[7])
    ).reshape(rows_here, span, width)
    grad_out = cotangent.reshape(tokens_here, width)
    down_grad = jnp.einsum("tf,td->fd", active_low, grad_out, preferred_element_type=f32)
    down_sum = jnp.sum(grad_out, axis=0, dtype=f32)
    grad_active = jnp.einsum("td,fd->tf", grad_out, down_weight, preferred_element_type=f32)
    grad_hidden = gelu_pull(grad_active)[0].astype(b16)
    up_grad = jnp.einsum("td,tf->df", normed_two, grad_hidden, preferred_element_type=f32)
    up_sum = jnp.sum(grad_hidden, axis=0, dtype=f32)
    ffn_tiles = jnp.concatenate(
        [
            jnp.transpose(up_grad.reshape(width, fold, width), (1, 0, 2)),
            down_grad.reshape(fold, width, width),
        ],
        axis=0,
    )
    grad_normed_two = jnp.einsum("tf,df->td", grad_hidden, up_weight, preferred_element_type=f32)
    unused, second_pull = jax.vjp(normalize, residual, vectors[2], vectors[3])
    residual_part, gain_two_grad, shift_two_grad = second_pull(grad_normed_two)
    grad_residual = grad_out.astype(f32) + residual_part
    grad_attended = grad_residual.astype(b16)
    out_grad = jnp.einsum("tm,td->md", context_low, grad_attended, preferred_element_type=f32)
    out_sum = jnp.sum(grad_attended, axis=0, dtype=f32)
    grad_context = jnp.einsum(
        "td,md->tm", grad_attended, out_weight, preferred_element_type=f32
    ).astype(b16)
    grad_heads = grad_context.reshape(rows_here, span, HEADS, HEAD_DIM)
    delta = jnp.einsum("rqhd,rhqd->rhq", grad_heads.astype(f32), context_raw)
    key_all, value_all = (
        lax.all_gather(key_rows, "blk", axis=1, tiled=True),
        lax.all_gather(value_rows, "blk", axis=1, tiled=True),
    )
    key_size = min(512, LEN)

    def back_block(index, carry):
        grad_query, key_total, value_total = carry
        start = index * key_size
        key_block = lax.dynamic_slice_in_dim(key_all, start, key_size, 1)
        value_block = lax.dynamic_slice_in_dim(value_all, start, key_size, 1)
        raw, allowed = block_scores(key_block, start)
        weights_back = jnp.where(allowed, jnp.exp(raw - log_total[..., None]), 0.0)
        key_heads = key_block.reshape(rows_here, key_size, HEADS, HEAD_DIM)
        value_heads = value_block.reshape(rows_here, key_size, HEADS, HEAD_DIM)
        value_grad = jnp.einsum(
            "rhqk,rqhd->rkhd", weights_back.astype(b16), grad_heads, preferred_element_type=f32
        )
        weight_grad = jnp.einsum(
            "rqhd,rkhd->rhqk", grad_heads, value_heads, preferred_element_type=f32
        )
        score_grad = (weights_back * (weight_grad - delta[..., None])).astype(b16)
        grad_query = (
            grad_query
            + jnp.einsum("rhqk,rkhd->rqhd", score_grad, key_heads, preferred_element_type=f32)
            * scale
        )
        key_grad = (
            jnp.einsum("rhqk,rqhd->rkhd", score_grad, query_heads, preferred_element_type=f32)
            * scale
        )
        key_total = lax.dynamic_update_slice_in_dim(
            key_total, key_grad.reshape(rows_here, key_size, width), start, 1
        )
        value_total = lax.dynamic_update_slice_in_dim(
            value_total, value_grad.reshape(rows_here, key_size, width), start, 1
        )
        return (grad_query, key_total, value_total)

    zero_rows = jnp.zeros((rows_here, LEN, width), f32)
    grad_query, key_total, value_total = lax.fori_loop(
        0,
        LEN // key_size,
        back_block,
        (jnp.zeros((rows_here, span, HEADS, HEAD_DIM), f32), zero_rows, zero_rows),
    )
    key_grad_here, value_grad_here = (
        lax.psum_scatter(
            key_total.astype(jnp.bfloat16), "blk", scatter_dimension=1, tiled=True
        ).astype(jnp.float32),
        lax.psum_scatter(
            value_total.astype(jnp.bfloat16), "blk", scatter_dimension=1, tiled=True
        ).astype(jnp.float32),
    )
    query_low = grad_query.reshape(tokens_here, width).astype(b16)
    key_low = key_grad_here.reshape(tokens_here, width).astype(b16)
    value_low = value_grad_here.reshape(tokens_here, width).astype(b16)
    query_tile = jnp.einsum("td,te->de", normed_one, query_low, preferred_element_type=f32)
    key_tile = jnp.einsum("td,te->de", normed_one, key_low, preferred_element_type=f32)
    value_tile = jnp.einsum("td,te->de", normed_one, value_low, preferred_element_type=f32)
    grad_normed_one = (
        jnp.einsum("te,de->td", query_low, query_weight, preferred_element_type=f32)
        + jnp.einsum("te,de->td", key_low, key_weight, preferred_element_type=f32)
        + jnp.einsum("te,de->td", value_low, value_weight, preferred_element_type=f32)
    )
    unused, first_pull = jax.vjp(normalize, flat_in, vectors[0], vectors[1])
    input_part, gain_one_grad, shift_one_grad = first_pull(grad_normed_one)
    input_grad = (grad_residual + input_part).reshape(rows_here, span, width)
    vector_grads = jnp.concatenate(
        [
            jnp.stack(
                [
                    gain_one_grad,
                    shift_one_grad,
                    gain_two_grad,
                    shift_two_grad,
                    jnp.sum(query_low, axis=0, dtype=f32),
                    jnp.sum(value_low, axis=0, dtype=f32),
                    out_sum,
                    down_sum,
                ]
            ),
            up_sum.reshape(fold, width),
        ],
        axis=0,
    )
    attn_tiles = jnp.stack([query_tile, key_tile, value_tile, out_grad])
    piece_share, vector_share = (
        lax.psum_scatter(
            jnp.concatenate([attn_tiles, ffn_tiles], axis=0).astype(jnp.bfloat16),
            "blk",
            scatter_dimension=1,
            tiled=True,
        ).astype(jnp.float32),
        lax.psum_scatter(
            vector_grads.astype(jnp.bfloat16), "blk", scatter_dimension=1, tiled=True
        ).astype(jnp.float32),
    )
    own_slots = lax.axis_index("dp") * CAP + jnp.arange(CAP)
    pick = (own_slots[:, None] == slot_of[None, :]).astype(f32)
    occupied = jnp.sum(pick, axis=1)[:, None, None]
    total_share, vector_total = (
        lax.psum(piece_share.astype(jnp.bfloat16), "dp").astype(jnp.float32),
        lax.psum(vector_share.astype(jnp.bfloat16), "dp").astype(jnp.float32),
    )
    slot_grads = jnp.einsum("cp,prd->crd", pick, total_share, precision=lax.Precision.HIGHEST)
    new_master, new_first, new_second = adam_step(
        master, slot_grads, first_moment, second_moment, RATE
    )
    columns = vector_first.shape[1]
    vector_cols = lax.dynamic_slice_in_dim(vectors, place * columns, columns, 1)
    new_vectors, new_vector_first, new_vector_second = adam_step(
        vector_cols, vector_total, vector_first, vector_second, VEC_RATE
    )
    return (
        block_out,
        input_grad,
        new_master * occupied,
        new_first * occupied,
        new_second * occupied,
        new_vectors,
        new_vector_first,
        new_vector_second,
    )


f32 = jnp.float32
b16 = jnp.bfloat16
LOG2E = 1.4426950408889634
MIB = 1024 * 1024
PAIRS = HEADS // 2
PAIR = 2 * HEAD_DIM


def dot_nn(left, right):
    return lax.dot_general(left, right, (((1,), (0,)), ((), ())), preferred_element_type=f32)


def dot_nt(left, right):
    return lax.dot_general(left, right, (((1,), (1,)), ((), ())), preferred_element_type=f32)


def dot_tn(left, right):
    return lax.dot_general(left, right, (((0,), (0,)), ((), ())), preferred_element_type=f32)


def norm_parts(values_in):
    center = jnp.mean(values_in, axis=-1, keepdims=True)
    offset = values_in - center
    spread = jnp.mean(offset * offset, axis=-1, keepdims=True)
    rstd = lax.rsqrt(spread + EPS_NORM)
    return offset * rstd, rstd


def norm_back(grad, unit, rstd, gain):
    scaled = grad * gain
    first = jnp.mean(scaled, axis=-1, keepdims=True)
    second = jnp.mean(scaled * unit, axis=-1, keepdims=True)
    return rstd * (scaled - first - unit * second)


def gelu_parts(value):
    bell = jnp.exp2(value * value * (-0.5 * LOG2E))
    ratio = pl.reciprocal(1.0 + (0.3275911 * 0.7071067811865476) * jnp.abs(value))
    poly = 0.5 * 1.061405429
    poly = poly * ratio + 0.5 * -1.453152027
    poly = poly * ratio + 0.5 * 1.421413741
    poly = poly * ratio + 0.5 * -0.284496736
    poly = poly * ratio + 0.5 * 0.254829592
    tail = poly * ratio * bell
    cdf = jnp.where(value >= 0.0, 1.0 - tail, tail)
    return value * cdf, cdf + value * (bell * 0.3989422804014327)


def head_only(block, head):
    lane = lax.broadcasted_iota(jnp.int32, block.shape, 1)
    keep = (lane >= head * HEAD_DIM) & (lane < (head + 1) * HEAD_DIM)
    return jnp.where(keep, block, jnp.zeros_like(block))


def feed_kernel(
    c_ref, o_ref, x_ref, g_ref, w_ref, vec_ref,
    y_ref, r_ref, d_ref, sums_ref, tiles_ref,
    acc_ref, stage_ref, sem_ref,
):
    fold = FF // D
    step = pl.program_id(0)

    @pl.when(step == 0)
    def clear():
        acc_ref[...] = jnp.zeros_like(acc_ref)
        sums_ref[...] = jnp.zeros_like(sums_ref)

    residual = x_ref[...].astype(f32) + (dot_nn(c_ref[...], w_ref[0]) + vec_ref[6:7, :])
    unit, rstd = norm_parts(residual)
    gain = vec_ref[2:3, :]
    normed = (unit * gain + vec_ref[3:4, :]).astype(b16)
    turned = normed.T
    cot = g_ref[...]
    out = residual + vec_ref[7:8, :]
    grad = jnp.zeros_like(out)

    for part in range(fold):
        hidden = dot_nn(normed, w_ref[1 + part]) + vec_ref[8 + part : 9 + part, :]
        pulled = dot_nt(cot, w_ref[1 + fold + part])
        active, slope = gelu_parts(hidden)
        active = active.astype(b16)
        pulled = (pulled * slope).astype(b16)
        out = out + dot_nn(active, w_ref[1 + fold + part])
        grad = grad + dot_nt(pulled, w_ref[1 + part])
        acc_ref[1 + part] += dot_nn(turned, pulled)
        acc_ref[1 + fold + part] += dot_tn(active, cot)
        sums_ref[8 + part : 9 + part, :] += jnp.sum(pulled.astype(f32), 0, keepdims=True)
    y_ref[...] = out.astype(b16)
    wide = cot.astype(f32)
    sums_ref[2:3, :] += jnp.sum(grad * unit, 0, keepdims=True)
    sums_ref[3:4, :] += jnp.sum(grad, 0, keepdims=True)
    sums_ref[7:8, :] += jnp.sum(wide, 0, keepdims=True)
    back = wide + norm_back(grad, unit, rstd, gain)
    r_ref[...] = back.astype(b16)
    low = back.astype(b16)
    sums_ref[6:7, :] += jnp.sum(low.astype(f32), 0, keepdims=True)
    d_ref[...] = dot_nt(w_ref[0], low).astype(b16)
    acc_ref[0] += dot_nn(o_ref[...], low)

    @pl.when(step == pl.num_programs(0) - 1)
    def send():
        count = 1 + 2 * fold
        copies = []
        for part in range(count):
            if part >= 2:
                copies[part - 2].wait()
            stage_ref[part % 2] = acc_ref[part].astype(b16)
            copy = pltpu.make_async_copy(stage_ref.at[part % 2], tiles_ref.at[part], sem_ref.at[part % 2])
            copy.start()
            copies.append(copy)
        copies[count - 2].wait()
        copies[count - 1].wait()


def feed(context, turned, x, cot, weights, vectors):
    tokens = x.shape[0]
    size = 256
    count = 1 + 2 * (FF // D)
    token_block = pl.BlockSpec((size, D), lambda i: (i, 0))
    turned_block = pl.BlockSpec((D, size), lambda i: (0, i))
    return pl.pallas_call(
        feed_kernel,
        grid=(tokens // size,),
        in_specs=[
            token_block,
            turned_block,
            token_block,
            token_block,
            pl.BlockSpec((count, D, D), lambda i: (0, 0, 0), pipeline_mode=pl.Buffered(1)),
            pl.BlockSpec((PIECES, D), lambda i: (0, 0)),
        ],
        out_specs=[
            token_block,
            token_block,
            turned_block,
            pl.BlockSpec((16, D), lambda i: (0, 0)),
            pl.BlockSpec(memory_space=pl.ANY),
        ],
        out_shape=[
            jax.ShapeDtypeStruct((tokens, D), b16),
            jax.ShapeDtypeStruct((tokens, D), b16),
            jax.ShapeDtypeStruct((D, tokens), b16),
            jax.ShapeDtypeStruct((16, D), f32),
            jax.ShapeDtypeStruct((count, D, D), b16),
        ],
        scratch_shapes=[
            pltpu.VMEM((count, D, D), f32),
            pltpu.VMEM((2, D, D), b16),
            pltpu.SemaphoreType.DMA((2,)),
        ],
        compiler_params=pltpu.CompilerParams(vmem_limit_bytes=60 * MIB),
        cost_estimate=pl.CostEstimate(
            flops=6 * count * tokens * D * D,
            bytes_accessed=18 * tokens * D + 4 * count * D * D,
            transcendentals=2 * tokens * FF,
        ),
        name="feed",
    )(context, turned, x, cot, weights, vectors)


MESH = pl.DeviceIdType.MESH
HALF = D // 2
FLOWS = 2
FLOW = HALF // FLOWS
NEAR = FLOW // 2
KEEP = NEAR // 2
WIDE = 3 * PAIR
REST = PIECES - 3
GROUPS = ((0, 1), (1, 2), (3, 3))
CHUNKS = len(GROUPS)


class Place:
    def __init__(self):
        self.me = lax.axis_index("dp")
        self.core = lax.axis_index("blk")
        self.bits = [lax.rem(self.me // weight, 2) for weight in (1, 2, 4, 8)]
        self.chips = [
            self.me + weight - 2 * weight * bit for weight, bit in zip((1, 2, 4, 8), self.bits)
        ]
        self.partners = [{"dp": chip} for chip in self.chips]
        low, high = self.bits[2:]
        self.inner = low != high
        self.across = {"dp": self.me + 4 - 8 * low + 8 - 16 * high}
        self.other = 1 - self.core
        self.twin = {"blk": self.other}

    def greet(self):
        barrier = pltpu.get_barrier_semaphore()
        for device in self.partners + [self.across, self.twin]:
            pl.semaphore_signal(barrier, 1, device_id=device, device_id_type=MESH)
        pl.semaphore_wait(barrier, 6)

    def flow(self, index):
        first, second = (0, 1) if index == 0 else (1, 0)
        base = index * FLOW
        near = base + self.bits[first] * NEAR
        far = base + NEAR - self.bits[first] * NEAR
        keep = near + self.bits[second] * KEEP
        give = near + KEEP - self.bits[second] * KEEP
        return first, second, near, far, keep, give


def remote(source, target, send, receive, device):
    return pltpu.make_async_remote_copy(
        src_ref=source,
        dst_ref=target,
        send_sem=send,
        recv_sem=receive,
        device_id=device,
        device_id_type=MESH,
    )


def rows_at(start, count):
    return pl.ds(pl.multiple_of(start, 16), count)


class Spread:
    def __init__(self, place, owner, rank, slots, land, gift, sems):
        self.place, self.owner, self.rank = place, owner, rank
        self.slots, self.land, self.gift, self.sems = slots, land, gift, sems

    def cols(self, chunk):
        return pl.ds(GROUPS[chunk][0] * PAIR, GROUPS[chunk][1] * PAIR)

    def first_copy(self, chunk, index):
        first, second, near, far, keep, give = self.place.flow(index)
        return remote(
            self.slots.at[:, rows_at(far, NEAR), self.cols(chunk)],
            self.land[chunk].at[index],
            self.sems[0].at[chunk, index, 0],
            self.sems[1].at[chunk, index, 0],
            self.place.partners[first],
        )

    def second_copy(self, chunk, index, which):
        first, second, near, far, keep, give = self.place.flow(index)
        if which == 0:
            source = self.slots.at[:, rows_at(give, KEEP), self.cols(chunk)]
        else:
            source = self.land[chunk].at[index, :, rows_at(give - near, KEEP)]
        return remote(
            source,
            self.gift[chunk].at[index, pl.ds(which * CAP, CAP)],
            self.sems[0].at[chunk, index, 1 + which],
            self.sems[1].at[chunk, index, 1 + which],
            self.place.partners[second],
        )

    def step(self, chunk, index):
        for flow in range(FLOWS):
            if index == 0:
                self.first_copy(chunk, flow).start()
                self.second_copy(chunk, flow, 0).start()
            if index == 1:
                self.first_copy(chunk, flow).wait()
                self.second_copy(chunk, flow, 1).start()
            if index == 2:
                self.second_copy(chunk, flow, 0).wait()
                self.second_copy(chunk, flow, 1).wait()

    def piece(self, tile, index, chunk, start, count):
        first, second, near, far, keep, give = self.place.flow(index)
        owner, rank = self.owner[tile], self.rank[tile]
        bits = [lax.rem(owner, 2), lax.rem(owner // 2, 2)]
        apart = [bit != mine for bit, mine in zip(bits, self.place.bits)]
        cols = pl.ds(start, count)
        mine = self.slots[rank, rows_at(keep, KEEP), pl.ds(GROUPS[chunk][0] * PAIR + start, count)]
        firsts = self.land[chunk][index, rank, rows_at(keep - near, KEEP), cols]
        gifts = self.gift[chunk][index, jnp.where(apart[first], CAP, 0) + rank, :, cols]
        value = jnp.where(apart[second], gifts, jnp.where(apart[first], firsts, mine))
        layer = owner // 4 == self.place.me // 4
        return jnp.where(layer, value, jnp.zeros_like(value))


class Column:
    steps = 4

    def __init__(self, place, kept, land, sems):
        self.place, self.kept, self.land, self.sems = place, kept, land, sems

    def copy(self, index):
        device = self.place.across if index == 1 else self.place.partners[2]
        return remote(
            self.kept, self.land.at[index % 2], self.sems[0].at[index], self.sems[1].at[index], device
        )

    def add(self, index):
        self.kept[...] = (self.kept[...].astype(f32) + self.land[index].astype(f32)).astype(b16)


def both_flows(flow):
    return pl.ds(flow * KEEP, KEEP)


def column_step(place, column, index):
    @pl.when(place.inner)
    def inner():
        if index == 1:
            column.copy(0).wait_recv()
            column.add(0)
            column.copy(1).start()
        if index == 2:
            column.copy(1).wait()
            column.add(1)
            column.copy(2).start()
        if index == 3:
            column.copy(2).wait_send()

    @pl.when(jnp.logical_not(place.inner))
    def outer():
        if index == 0:
            column.copy(0).start()
        if index == 1:
            column.copy(0).wait_send()
        if index == 3:
            column.copy(2).wait_recv()
            column.kept[...] = column.land[0]


class Item:
    steps = 7

    def __init__(self, place, work, kept, land, sems, load, store=None):
        self.place, self.work, self.kept, self.land, self.sems = place, work, kept, land, sems
        self.load, self.store = load, store
        self.base = place.core * HALF

    def copy(self, flow, index):
        first, second, near, far, keep, give = self.place.flow(flow)
        kept = self.work.at[:, rows_at(self.base + keep, KEEP)]
        half = self.work.at[:, rows_at(self.base + near, NEAR)]
        source, device = [
            (kept, self.place.partners[second]),
            (half, self.place.partners[first]),
        ][index]
        number = 3 + 2 * flow + index
        return remote(source, source, self.sems[0].at[number], self.sems[1].at[number], device)

    def pair(self):
        rows = self.work.at[:, rows_at(self.base, HALF)]
        return remote(rows, rows, self.sems[0].at[7], self.sems[1].at[7], self.place.twin)

    def step(self, index):
        if index == 0:
            for flow in range(FLOWS):
                self.load(self.kept, both_flows(flow), flow)
        if index <= 3:
            column_step(self.place, Column(self.place, self.kept, self.land, self.sems), index)
        for flow in range(FLOWS):
            if index == 3:
                rows = rows_at(self.base + self.place.flow(flow)[4], KEEP)
                self.work[:, rows] = self.kept[:, both_flows(flow)]
            if 4 <= index <= 5:
                self.copy(flow, index - 4).wait()
            if 3 <= index <= 4:
                self.copy(flow, index - 3).start()
        if index == 5:
            self.pair().start()
        if index == 6:
            self.pair().wait()
            self.store().start()


REST_GROUPS = tuple((index, 1) for index in range(REST))
PAIR_CHUNK = (0, 1, 1, 2, 2, 2)
FRONT_PAIRS = (2, 4, 5, 6, 7, 8)
FRONT_REST = (6, 7, 8, 9, 10, 11, 12, 13, 14)
FRONT_LEAD = 9


def front_kernel(
    owner, lengths, master, vec_ref, x_in, c_in,
    x_out, c_out, n_out, one_out, two_out, q_ref, k_ref, v_ref, p_ref, r_ref, o_ref, ctx_ref,
    rank, rows_ref, normed, keys, turned_values, scores, slots,
    land_one, land_two, land_three, gift_one, gift_two, gift_three,
    one, one_kept, one_land, two, two_kept, two_land,
    spread_send, spread_recv, one_send, one_recv, two_send, two_recv,
    swap_send, swap_recv, swap_local, store_sem,
):
    pair = pl.program_id(0)
    row = pl.program_id(1)
    grid_step = pair * 2 + row
    place = Place()
    rows, span = x_in.shape[0] // 2, x_in.shape[1]
    land = (land_one, land_two, land_three)
    gift = (gift_one, gift_two, gift_three)
    spread = Spread(place, owner, rank, slots, land, gift, (spread_send, spread_recv))

    def swaps(index):
        source, target = [(x_in, rows_ref), (c_in, c_out)][index]
        here = pl.ds(place.core * span, span)
        near = pltpu.make_async_copy(
            source.at[pl.ds(place.core * rows, rows)], target.at[:, here], swap_local.at[index]
        )
        far = remote(
            source.at[pl.ds(place.other * rows, rows)],
            target.at[:, here],
            swap_send.at[index],
            swap_recv.at[index],
            place.twin,
        )
        return near, far

    def row_store():
        return pltpu.make_async_copy(rows_ref, x_out, store_sem.at[PAIRS + REST])

    def normed_store():
        return pltpu.make_async_copy(normed, n_out, store_sem.at[PAIRS + REST + 1])

    def pair_item(group):
        span_of = pl.ds(group, 1)

        def load(work, where, flow):
            chunk = PAIR_CHUNK[group]
            for tile in range(3):
                part = spread.piece(tile, flow, chunk, (group - GROUPS[chunk][0]) * PAIR, PAIR)
                work[0, where, pl.ds(tile * PAIR, PAIR)] = part

        def store():
            return pltpu.make_async_copy(one.at[span_of], one_out.at[span_of], store_sem.at[group])

        sems = (one_send.at[group], one_recv.at[group])
        return Item(place, one.at[span_of], one_kept.at[span_of], one_land.at[:, span_of], sems, load, store)

    def rest_item(group):
        first, count = REST_GROUPS[group]
        span_of = pl.ds(first, count)

        def load(work, where, flow):
            for index in range(count):
                for chunk, (start, wide) in enumerate(GROUPS):
                    part = spread.piece(3 + first + index, flow, chunk, 0, wide * PAIR)
                    work[index, where, pl.ds(start * PAIR, wide * PAIR)] = part

        def store():
            return pltpu.make_async_copy(
                two.at[span_of], two_out.at[span_of], store_sem.at[PAIRS + group]
            )

        sems = (two_send.at[group], two_recv.at[group])
        return Item(place, two.at[span_of], two_kept.at[span_of], two_land.at[:, span_of], sems, load, store)

    def tick(number, odd):
        for chunk in range(CHUNKS):
            if odd == 0 and 0 <= number - 2 * chunk <= 2:
                spread.step(chunk, number - 2 * chunk)
        starts = [(pair_item, group, start) for group, start in enumerate(FRONT_PAIRS)]
        starts += [(rest_item, group, start) for group, start in enumerate(FRONT_REST)]
        for make, group, start in starts:
            if group % 2 == odd and 0 <= number - start < Item.steps:
                make(group).step(number - start)

    def both(number):
        tick(number, 0)
        tick(number, 1)

    @pl.when(grid_step == 0)
    def lead():
        slots[...] = master[...].astype(b16)
        for tile in range(PIECES):
            count = jnp.int32(0)
            for before in range(tile):
                count = count + (owner[before] == owner[tile]).astype(jnp.int32)
            rank[tile] = jnp.minimum(count, CAP - 1)
        place.greet()
        for copy in swaps(0):
            copy.start()
        both(0)
        for copy in swaps(1):
            copy.start()
        for copy in swaps(0):
            copy.wait()
        row_store().start()

        def norm_rows(index, carry):
            for part in range(rows):
                for block in range(4):
                    where = pl.ds(pl.multiple_of(index * 128 + block * 32, 32), 32)
                    unit, unused = norm_parts(rows_ref[part, where].astype(f32))
                    low = (unit * vec_ref[0:1, :] + vec_ref[1:2, :]).astype(b16)
                    normed[pl.ds(pl.multiple_of(part * LEN + index * 128 + block * 32, 32), 32)] = low
            return carry

        both(1)
        lax.fori_loop(0, LEN // 128, norm_rows, 0)
        normed_store().start()
        for number in range(2, FRONT_LEAD):
            both(number)

    for number in range(2 * PAIRS):
        pl.when(grid_step == number)(partial(tick, FRONT_LEAD + number, 0))

    @pl.when(row == 0)
    def project():
        lanes = pl.ds(pl.multiple_of(pair * PAIR, PAIR), PAIR)
        weight = one[pair]

        def part(index, carry):
            where = pl.ds(pl.multiple_of(index * 512, 512), 512)
            both = dot_nn(normed[where], weight)
            queries = both[:, :PAIR] + vec_ref[4:5, lanes]
            queries = (queries * (HEAD_DIM**-0.5 * LOG2E)).astype(b16)
            q_ref[:, where] = queries.T
            low = both[:, PAIR : 2 * PAIR].astype(b16)
            keys[where] = low
            k_ref[:, where] = low.T
            values = (both[:, 2 * PAIR :] + vec_ref[5:6, lanes]).astype(b16)
            v_ref[where] = values
            turned_values[:, where] = values.T
            return carry

        lax.fori_loop(0, normed.shape[0] // 512, part, 0)

    half = LEN // 2
    start = pl.multiple_of(row * LEN, LEN)
    split = lengths[place.core * rows + row, 0] < LEN
    shift = jnp.where(split, jnp.float32(-1e30), jnp.float32(0.0))

    quarter = LEN // 4
    units = [(head, step) for head in range(2) for step in range(2)]

    def score_block(unit, block, peak):
        head, step = units[unit]
        rows_here = pl.ds(pl.multiple_of(start + block * quarter, quarter), quarter)
        queries = q_ref[:, pl.ds(pl.multiple_of(start + step * half, half), half)]
        raw = dot_nn(head_only(keys[rows_here], head), queries)
        if block // 2 != step:
            raw = raw + shift
        scores[unit % 2, block * quarter : (block + 1) * quarter] = raw
        best = jnp.max(raw.reshape(-1, 8, half), axis=0)
        return best if peak is None else jnp.maximum(peak, best)

    def context_block(unit, block, total):
        head, step = units[unit]
        part = slice(head * HEAD_DIM, (head + 1) * HEAD_DIM)
        cols = pl.ds(pl.multiple_of(start + block * quarter, quarter), quarter)
        here = slice(step * half, (step + 1) * half)
        term = dot_nn(
            turned_values[part, cols], p_ref[head, block * quarter : (block + 1) * quarter, here]
        )
        return term if total is None else total + term

    def context_store(unit, total, recip):
        head, step = units[unit]
        part = slice(head * HEAD_DIM, (head + 1) * HEAD_DIM)
        o_ref[part, step * half : (step + 1) * half] = (total * recip).astype(b16)

    peak = None
    for block in range(4):
        peak = score_block(0, block, peak)
    before = None
    for unit, (head, step) in enumerate(units):
        if unit == 2:
            for number in range(2 * PAIRS):
                pl.when(grid_step == number)(partial(tick, FRONT_LEAD + number, 1))
        here = slice(step * half, (step + 1) * half)
        top = jnp.max(peak, 0, keepdims=True)
        total = jnp.zeros((8, half), f32)
        peak, context = None, None
        for block in range(4):
            if unit + 1 < len(units):
                peak = score_block(unit + 1, block, peak)
            for small in range(4 * block, 4 * block + 4):
                rows_here = slice(small * 64, (small + 1) * 64)
                value = jnp.exp2(scores[unit % 2, rows_here] - top)
                total = total + jnp.sum(value.reshape(-1, 8, half), axis=0)
                p_ref[head, rows_here, here] = value.astype(b16)
            if unit > 0:
                context = context_block(unit - 1, block, context)
        if unit > 0:
            context_store(unit - 1, context, before)
        before = 1.0 / jnp.sum(total, 0, keepdims=True)
        r_ref[0, head : head + 1, here] = before
    context = None
    for block in range(4):
        context = context_block(3, block, context)
    context_store(3, context, before)
    ctx_ref[...] = o_ref[...].T

    @pl.when(grid_step == 2 * PAIRS - 1)
    def finish_copies():
        for copy in swaps(1):
            copy.wait()
        row_store().wait()
        normed_store().wait()
        for group in range(PAIRS):
            pair_item(group).store().wait()
        for group in range(REST):
            rest_item(group).store().wait()


def front(owner, lengths, master, vectors, inputs, cotangent):
    rows, span = inputs.shape[0] // 2, inputs.shape[1]
    tokens = rows * LEN
    any_spec = pl.BlockSpec(memory_space=pl.ANY)
    smem = pl.BlockSpec(memory_space=pltpu.SMEM)
    whole = jax.ShapeDtypeStruct((rows, LEN, D), b16)
    dma = pltpu.SemaphoreType.DMA
    return pl.pallas_call(
        front_kernel,
        grid=(PAIRS, rows),
        in_specs=[
            smem,
            smem,
            pl.BlockSpec((CAP, HALF, D), lambda h, r: (0, 0, 0), pipeline_mode=pl.Buffered(1)),
            pl.BlockSpec((PIECES, D), lambda h, r: (0, 0)),
            any_spec,
            any_spec,
        ],
        out_specs=[any_spec] * 5
        + [
            pl.BlockSpec((PAIR, tokens), lambda h, r: (h, 0)),
            pl.BlockSpec((PAIR, tokens), lambda h, r: (h, 0)),
            pl.BlockSpec((tokens, PAIR), lambda h, r: (0, h)),
            pl.BlockSpec((2, LEN, LEN), lambda h, r: (h * 2 + r, 0, 0)),
            pl.BlockSpec((1, 2, LEN), lambda h, r: (h * 2 + r, 0, 0)),
            pl.BlockSpec((PAIR, LEN), lambda h, r: (h, r)),
            pl.BlockSpec((LEN, PAIR), lambda h, r: (r, h)),
        ],
        out_shape=[
            whole,
            whole,
            jax.ShapeDtypeStruct((tokens, D), b16),
            jax.ShapeDtypeStruct((PAIRS, D, WIDE), b16),
            jax.ShapeDtypeStruct((REST, D, D), b16),
            jax.ShapeDtypeStruct((D, tokens), b16),
            jax.ShapeDtypeStruct((D, tokens), b16),
            jax.ShapeDtypeStruct((tokens, D), b16),
            jax.ShapeDtypeStruct((rows * HEADS, LEN, LEN), b16),
            jax.ShapeDtypeStruct((rows * PAIRS, 2, LEN), f32),
            jax.ShapeDtypeStruct((D, tokens), b16),
            jax.ShapeDtypeStruct((tokens, D), b16),
        ],
        scratch_shapes=[
            pltpu.SMEM((PIECES,), jnp.int32),
            pltpu.VMEM((rows, LEN, D), b16),
            pltpu.VMEM((tokens, D), b16),
            pltpu.VMEM((tokens, PAIR), b16),
            pltpu.VMEM((PAIR, tokens), b16),
            pltpu.VMEM((2, LEN, LEN // 2), f32),
            pltpu.VMEM((CAP, HALF, D), b16),
        ]
        + [pltpu.VMEM((FLOWS, CAP, NEAR, wide * PAIR), b16) for unused, wide in GROUPS]
        + [pltpu.VMEM((FLOWS, 2 * CAP, KEEP, wide * PAIR), b16) for unused, wide in GROUPS]
        + [
            pltpu.VMEM((PAIRS, D, WIDE), b16),
            pltpu.VMEM((PAIRS, NEAR, WIDE), b16),
            pltpu.VMEM((2, PAIRS, NEAR, WIDE), b16),
            pltpu.VMEM((REST, D, D), b16),
            pltpu.VMEM((REST, NEAR, D), b16),
            pltpu.VMEM((2, REST, NEAR, D), b16),
            dma((CHUNKS, FLOWS, 3)),
            dma((CHUNKS, FLOWS, 3)),
            dma((PAIRS, 8)),
            dma((PAIRS, 8)),
            dma((REST, 8)),
            dma((REST, 8)),
            dma((2,)),
            dma((2,)),
            dma((2,)),
            dma((PAIRS + REST + 2,)),
        ],
        compiler_params=pltpu.CompilerParams(
            collective_id=0, has_side_effects=True, vmem_limit_bytes=60 * MIB
        ),
        name="front",
    )(owner, lengths, master, vectors, inputs, cotangent)


class Sum:
    steps = 7

    def __init__(self, place, work, kept, wide, narrow, land, sems, send_pair, add_own):
        self.place, self.work, self.kept, self.sems = place, work, kept, sems
        self.wide, self.narrow, self.land = wide, narrow, land
        self.send_pair, self.add_own = send_pair, add_own

    def copy(self, flow, index):
        first, second, near, far, keep, give = self.place.flow(flow)
        source, target, device = [
            (self.work.at[:, rows_at(far, NEAR)], self.wide.at[flow], first),
            (self.work.at[:, rows_at(give, KEEP)], self.narrow.at[flow], second),
        ][index]
        number = 3 + 2 * flow + index
        return remote(
            source,
            target,
            self.sems[0].at[number],
            self.sems[1].at[number],
            self.place.partners[device],
        )

    def step(self, index):
        if index == 0:
            self.send_pair().start()
        if index == 1:
            self.send_pair().wait()
            self.add_own()
        for flow in range(FLOWS):
            first, second, near, far, keep, give = self.place.flow(flow)
            if index == 1:
                self.copy(flow, 0).start()
            if index == 2:
                self.copy(flow, 0).wait()
                rows = rows_at(near, NEAR)
                total = self.work[:, rows].astype(f32) + self.wide[flow].astype(f32)
                self.work[:, rows] = total.astype(b16)
                self.copy(flow, 1).start()
            if index == 3:
                self.copy(flow, 1).wait()
                total = self.work[:, rows_at(keep, KEEP)].astype(f32) + self.narrow[flow].astype(f32)
                self.kept[:, both_flows(flow)] = total.astype(b16)
        if index >= 3:
            column_step(self.place, Column(self.place, self.kept, self.land, self.sems), index - 3)


class Gather:
    steps = 3

    def __init__(self, place, work, kept, narrow, wide, sems):
        self.place, self.work, self.kept = place, work, kept
        self.narrow, self.wide, self.sems = narrow, wide, sems

    def copy(self, flow, index):
        first, second, near, far, keep, give = self.place.flow(flow)
        source, target, device = [
            (self.kept.at[:, both_flows(flow)], self.narrow, second),
            (self.work.at[:, rows_at(near, NEAR)], self.wide, first),
        ][index]
        number = 7 + 2 * flow + index
        return remote(
            source,
            target.at[flow],
            self.sems[0].at[number],
            self.sems[1].at[number],
            self.place.partners[device],
        )

    def step(self, index):
        for flow in range(FLOWS):
            first, second, near, far, keep, give = self.place.flow(flow)
            if index == 0:
                self.work[:, rows_at(keep, KEEP)] = self.kept[:, both_flows(flow)]
            if index > 0:
                self.copy(flow, index - 1).wait()
            if index == 1:
                self.work[:, rows_at(give, KEEP)] = self.narrow[flow]
            if index == 2:
                self.work[:, rows_at(far, NEAR)] = self.wide[flow]
            if index < 2:
                self.copy(flow, index).start()


class Hand:
    steps = 3

    def __init__(self, place, table, kept, bag, gift, pack, last, own, out, sems, store_sems):
        self.place, self.table, self.kept = place, table, kept
        self.bag, self.gift, self.pack, self.last, self.own = bag, gift, pack, last, own
        self.out, self.sems, self.store_sems = out, sems, store_sems

    def tile(self, chip, rank, flow):
        return self.kept[self.table[chip * CAP + rank], both_flows(flow)]

    def copy(self, flow, index):
        first, second = self.place.flow(flow)[:2]
        source, target, device = [
            (self.bag.at[flow], self.gift.at[flow], second),
            (self.pack.at[flow], self.last.at[flow], first),
        ][index]
        return remote(
            source,
            target,
            self.sems[0].at[flow, index],
            self.sems[1].at[flow, index],
            self.place.partners[device],
        )

    def stores(self, flow):
        first, second, near, far, keep, give = self.place.flow(flow)
        parts = [
            (self.own.at[flow], rows_at(keep, KEEP)),
            (self.gift.at[flow, pl.ds(0, CAP)], rows_at(give, KEEP)),
            (self.last.at[flow], rows_at(far, NEAR)),
        ]
        return [
            pltpu.make_async_copy(source, self.out.at[:, rows], self.store_sems.at[flow, index])
            for index, (source, rows) in enumerate(parts)
        ]

    def step(self, index):
        for flow in range(FLOWS):
            first, second, near, far, keep, give = self.place.flow(flow)
            if index == 0:
                beside = self.place.chips[second]
                across = beside + self.place.chips[first] - self.place.me
                for rank in range(CAP):
                    self.bag[flow, rank] = self.tile(beside, rank, flow)
                    self.bag[flow, CAP + rank] = self.tile(across, rank, flow)
                    self.own[flow, rank] = self.tile(self.place.me, rank, flow)
                self.copy(flow, 0).start()
            if index == 1:
                self.copy(flow, 0).wait()
                for rank in range(CAP):
                    mine = self.tile(self.place.chips[first], rank, flow)
                    self.pack[flow, rank, rows_at(keep - near, KEEP)] = mine
                    self.pack[flow, rank, rows_at(give - near, KEEP)] = self.gift[flow, CAP + rank]
                self.copy(flow, 1).start()
            if index == 2:
                self.copy(flow, 1).wait()
                for copy in self.stores(flow):
                    copy.start()


BACK_STEPS = 2 * PAIRS
BACK_TAIL = 4
BACK_PAIRS = tuple((index, 1) for index in range(PAIRS))
BACK_REST = (0, 1, 2, 3, 4, 5, 6, 7, 8)
BACK_HAND = 15


def back_kernel(
    table, p_ref, r_ref, v_ref, q_ref, k_ref, o_ref, g_ref, w_ref, n_ref, x_ref, z_ref, vec_ref,
    tiles_in, sums_in, y_in,
    y_out, i_out, pairs_out, slots_out, sums_ref,
    grad_sum, wide_sum, turned, slopes, block_out,
    two, two_kept, two_wide, two_narrow, two_land, two_stage,
    one, one_kept, one_wide, one_narrow, one_land, one_send_stage, one_stage,
    gather_narrow, gather_wide,
    bag, gift, pack, last, own, vec_land,
    two_send, two_recv, one_send, one_recv, hand_send, hand_recv, hand_store,
    pair_two_send, pair_two_recv, pair_one_send, pair_one_recv, load_sem, store_sem,
    swap_send, swap_recv, swap_local, vec_send, vec_recv,
):
    step = pl.program_id(0)
    place = Place()
    rows, span = y_in.shape[0], y_in.shape[1] // 2
    near_half = rows_at(place.core * HALF, HALF)
    far_half = rows_at(place.other * HALF, HALF)

    def load_two(group):
        first, count = REST_GROUPS[group]
        return pltpu.make_async_copy(
            tiles_in.at[pl.ds(first, count), near_half],
            two_stage.at[pl.ds(group % 2, 1)],
            load_sem.at[group % 2],
        )

    def rest_sum(group):
        first, count = REST_GROUPS[group]
        span_of = pl.ds(first, count)
        work = two.at[span_of]

        def send_pair():
            return remote(
                tiles_in.at[span_of, far_half],
                work,
                pair_two_send.at[group],
                pair_two_recv.at[group],
                place.twin,
            )

        def add_own():
            load_two(group).wait()
            work[...] = (work[...].astype(f32) + two_stage[group % 2].astype(f32)).astype(b16)

        sems = (two_send.at[group], two_recv.at[group])
        parts = (two_kept.at[span_of], two_wide.at[:, span_of], two_narrow.at[:, span_of])
        return Sum(place, work, *parts, two_land.at[:, span_of], sems, send_pair, add_own)

    def pair_sum(group):
        first, count = BACK_PAIRS[group]
        span_of = pl.ds(first, count)
        work = one.at[span_of]

        def send_pair():
            return remote(
                one_send_stage.at[pl.ds(group % 2, 1)],
                work,
                pair_one_send.at[group],
                pair_one_recv.at[group],
                place.twin,
            )

        def add_own():
            own = one_stage[group % 2].astype(f32)
            work[...] = (work[...].astype(f32) + own).astype(b16)

        sems = (one_send.at[group], one_recv.at[group])
        parts = (one_kept.at[span_of], one_wide.at[:, span_of], one_narrow.at[:, span_of])
        return Sum(place, work, *parts, one_land.at[:, span_of], sems, send_pair, add_own)

    def pair_gather(group):
        first, count = BACK_PAIRS[group]
        span_of = pl.ds(first, count)
        sems = (one_send.at[group], one_recv.at[group])
        narrow, wide = gather_narrow.at[:, span_of], gather_wide.at[:, span_of]
        return Gather(place, one.at[span_of], one_kept.at[span_of], narrow, wide, sems)

    hand = Hand(
        place, table, two_kept, bag, gift, pack, last, own, slots_out, (hand_send, hand_recv), hand_store
    )

    def pair_store(index, tile):
        return pltpu.make_async_copy(
            one.at[index, :, pl.ds(tile * PAIR, PAIR)],
            pairs_out.at[tile, :, pl.ds(index * PAIR, PAIR)],
            store_sem.at[index, tile],
        )

    def tick(number, odd):
        for group, start in enumerate(BACK_REST):
            if group % 2 == odd and 0 <= number - start < Sum.steps:
                rest_sum(group).step(number - start)
        for group, (first, count) in enumerate(BACK_PAIRS):
            if group % 2 != odd:
                continue
            start = 2 * (first + count)
            if 0 <= number - start < Sum.steps:
                pair_sum(group).step(number - start)
            if 0 <= number - start - Sum.steps + 1 < Gather.steps:
                pair_gather(group).step(number - start - Sum.steps + 1)
            if number == start + Sum.steps + 1:
                for index in range(first, first + count):
                    for tile in range(3):
                        pair_store(index, tile).start()
        if odd == 0 and 0 <= number - BACK_HAND < Hand.steps:
            hand.step(number - BACK_HAND)
        for group, start in enumerate(BACK_REST):
            if odd == 1 and number == max(start - 1, 0):
                load_two(group).start()

    def both(number):
        tick(number, 0)
        tick(number, 1)

    def swap_y(index):
        there = pl.ds(place.core * rows, rows)
        if index == 0:
            return pltpu.make_async_copy(
                y_in.at[:, pl.ds(place.core * span, span)], y_out.at[there], swap_local.at[0]
            )
        return remote(
            y_in.at[:, pl.ds(place.other * span, span)],
            y_out.at[there],
            swap_send.at[0],
            swap_recv.at[0],
            place.twin,
        )

    @pl.when(step == 0)
    def lead():
        place.greet()
        for index in range(2):
            swap_y(index).start()
        sums_ref[...] = sums_in[...]

    for number in range(BACK_STEPS + BACK_TAIL):
        early = partial(tick, number, 0) if number < BACK_STEPS else partial(both, number)
        pl.when(step == number)(early)

    half = LEN // 2
    pair, row = step // 2, lax.rem(step, 2)

    quarter = LEN // 4

    def attention_inputs(head):
        part = slice(head * HEAD_DIM, (head + 1) * HEAD_DIM)
        values = head_only(v_ref[...], head)
        recip = r_ref[0, head : head + 1, :]
        grad = g_ref[part, :].astype(f32) * recip
        delta = jnp.sum(grad * o_ref[part, :].astype(f32), 0, keepdims=True)
        grad = grad.astype(b16)
        return values, grad, delta, jnp.concatenate([grad, grad], axis=0)

    def attention(head):
        part = slice(head * HEAD_DIM, (head + 1) * HEAD_DIM)
        values, grad, delta, doubled = attention_inputs(head)
        units = [(which, block) for which in range(2) for block in range(4)]
        value_grad, key_grad, query_grad = {}, {}, {}

        def raw_block(unit):
            which, block = units[unit]
            cols = slice(which * half, (which + 1) * half)
            return dot_nn(values[block * quarter : (block + 1) * quarter], doubled[:, cols])

        def slope_block(unit, raw):
            which, block = units[unit]
            cols = slice(which * half, (which + 1) * half)
            for small in range(4):
                rows_here = slice(small * 64, (small + 1) * 64)
                rows_all = slice(block * quarter + small * 64, block * quarter + (small + 1) * 64)
                slope = p_ref[head, rows_all, cols].astype(f32) * (raw[rows_here] - delta[:, cols])
                slopes[unit % 2, rows_here] = slope.astype(b16)

        def add(totals, key, term):
            totals[key] = totals[key] + term if key in totals else term

        def grad_block(unit):
            which, block = units[unit]
            cols = slice(which * half, (which + 1) * half)
            rows_all = slice(block * quarter, (block + 1) * quarter)
            slope = slopes[unit % 2]
            add(value_grad, block, dot_nt(grad[:, cols], p_ref[head, rows_all, cols]))
            add(key_grad, block, dot_nt(q_ref[part, cols], slope))
            add(query_grad, which, dot_nn(k_ref[part, rows_all], slope))

        raw = raw_block(0)
        for unit in range(len(units)):
            after = raw_block(unit + 1) if unit + 1 < len(units) else None
            slope_block(unit, raw)
            if unit > 0:
                grad_block(unit - 1)
            raw = after
        grad_block(len(units) - 1)
        for which in range(2):
            total = query_grad[which] * (HEAD_DIM**-0.5)
            turned[part, which * half : (which + 1) * half] = total.astype(b16)
        for block in range(4):
            rows_all = slice(block * quarter, (block + 1) * quarter)
            lower = slice(PAIR + head * HEAD_DIM, PAIR + (head + 1) * HEAD_DIM)
            turned[lower, rows_all] = (key_grad[block] * (1.0 / LOG2E)).astype(b16)
            lower = slice(2 * PAIR + head * HEAD_DIM, 2 * PAIR + (head + 1) * HEAD_DIM)
            turned[lower, rows_all] = value_grad[block].astype(b16)

    @pl.when(step < BACK_STEPS)
    def first_head():
        attention(0)

    for number in range(BACK_STEPS):
        pl.when(step == number)(partial(tick, number, 1))

    @pl.when(step < BACK_STEPS)
    def second_head():
        attention(1)
        where = pl.ds(pl.multiple_of(row * LEN, LEN), LEN)
        block = dot_nn(turned[...], n_ref[where])
        back = turned[...].T
        lanes = pl.ds(pl.multiple_of(pair * PAIR, PAIR), PAIR)
        ones = jnp.sum(back.astype(f32), 0, keepdims=True)
        sums_ref[4:5, lanes] += ones[:, :PAIR]
        sums_ref[5:6, lanes] += ones[:, 2 * PAIR :]
        term = dot_nt(back, w_ref[0])

        @pl.when(pair == 0)
        def begin():
            grad_sum[where] = term

        @pl.when(pair > 0)
        def add():
            grad_sum[where] += term

        @pl.when(row == 0)
        def keep():
            wide_sum[...] = block

        @pl.when(row == 1)
        def hand_on():
            whole = (wide_sum[...] + block).T
            low = whole.astype(b16)
            for core in range(2):

                @pl.when(place.core == core)
                def split():
                    slot = lax.rem(pair, 2)
                    one_stage[slot] = low[core * HALF : (core + 1) * HALF]
                    one_send_stage[slot] = low[(1 - core) * HALF : (2 - core) * HALF]

    def store_block(index):
        row, half = index // 2, index % 2
        target = i_out.at[place.core * rows + row]
        local = pltpu.make_async_copy(block_out.at[half], target, swap_local.at[1 + row])
        far = remote(
            block_out.at[half], target, swap_send.at[1 + row], swap_recv.at[1 + row], place.twin
        )
        return local, far, half

    def wait_block(index):
        local, far, half = store_block(index)

        @pl.when(place.core == half)
        def keep():
            local.wait()

        @pl.when(place.core != half)
        def give():
            far.wait()

    for index in range(BACK_TAIL):

        @pl.when(step == BACK_STEPS + index)
        def close():
            size = LEN // 2
            if index >= 2:
                wait_block(index - 2)
            gain_sum = jnp.zeros((8, D), f32)
            shift_sum = jnp.zeros((8, D), f32)
            for block in range(size // 16):
                rows_here = slice(block * 16, (block + 1) * 16)
                grad = grad_sum[index * size + block * 16 : index * size + (block + 1) * 16]
                unit, rstd = norm_parts(x_ref[rows_here].astype(f32))
                gain_sum = gain_sum + jnp.sum((grad * unit).reshape(-1, 8, D), axis=0)
                shift_sum = shift_sum + jnp.sum(grad.reshape(-1, 8, D), axis=0)
                total = norm_back(grad, unit, rstd, vec_ref[0:1, :])
                block_out[index % 2, rows_here] = (z_ref[rows_here].astype(f32) + total).astype(b16)
            sums_ref[0:1, :] += jnp.sum(gain_sum, 0, keepdims=True)
            sums_ref[1:2, :] += jnp.sum(shift_sum, 0, keepdims=True)
            local, far, half = store_block(index)

            @pl.when(place.core == half)
            def keep():
                local.start()

            @pl.when(place.core != half)
            def give():
                far.start()

    @pl.when(step == BACK_STEPS + BACK_TAIL - 1)
    def drain():
        devices = [place.twin] + place.partners

        def vector(index):
            return remote(
                sums_ref, vec_land.at[index], vec_send.at[index], vec_recv.at[index], devices[index]
            )

        vector(0).start()
        for number in range(BACK_STEPS + BACK_TAIL, BACK_STEPS + Sum.steps + Gather.steps):
            both(number)
            index = number - BACK_STEPS - BACK_TAIL
            if index < 5:
                vector(index).wait()
                sums_ref[...] += vec_land[index]
                if index < 4:
                    vector(index + 1).start()
        for index in range(2):
            swap_y(index).wait()
        for index in range(2, BACK_TAIL):
            wait_block(index)
        for index in range(PAIRS):
            for tile in range(3):
                pair_store(index, tile).wait()
        for flow in range(FLOWS):
            for copy in hand.stores(flow):
                copy.wait()


def back(table, attention, weights, normed, x, residual, vectors, tiles, sums, y):
    rows, length = y.shape[:2]
    tokens = rows * length
    any_spec = pl.BlockSpec(memory_space=pl.ANY)
    smem = pl.BlockSpec(memory_space=pltpu.SMEM)
    dma = pltpu.SemaphoreType.DMA

    def now(step):
        return jnp.minimum(step, BACK_STEPS - 1)

    def tail(step):
        return jnp.maximum(step - BACK_STEPS, 0)

    head_block = pl.BlockSpec((PAIR, LEN), lambda s: (now(s) // 2, lax.rem(now(s), 2)))
    tail_block = pl.BlockSpec((LEN // 2, D), lambda s: (tail(s), 0))
    whole = pl.BlockSpec((PIECES, D), lambda s: (0, 0))
    sums_block = pl.BlockSpec((16, D), lambda s: (0, 0))
    return pl.pallas_call(
        back_kernel,
        grid=(BACK_STEPS + BACK_TAIL,),
        in_specs=[
            smem,
            pl.BlockSpec((2, LEN, LEN), lambda s: (now(s), 0, 0)),
            pl.BlockSpec((1, 2, LEN), lambda s: (now(s), 0, 0)),
            pl.BlockSpec((LEN, PAIR), lambda s: (lax.rem(now(s), 2), now(s) // 2)),
            head_block,
            head_block,
            head_block,
            head_block,
            pl.BlockSpec((1, D, WIDE), lambda s: (now(s) // 2, 0, 0)),
            pl.BlockSpec((tokens, D), lambda s: (0, 0), pipeline_mode=pl.Buffered(1)),
            tail_block,
            tail_block,
            whole,
            any_spec,
            sums_block,
            any_spec,
        ],
        out_specs=[any_spec] * 4 + [sums_block],
        out_shape=[
            jax.ShapeDtypeStruct((2 * rows, length // 2, D), b16),
            jax.ShapeDtypeStruct((2 * rows, length // 2, D), b16),
            jax.ShapeDtypeStruct((3, HALF, D), b16),
            jax.ShapeDtypeStruct((CAP, HALF, D), b16),
            jax.ShapeDtypeStruct((16, D), f32),
        ],
        scratch_shapes=[
            pltpu.VMEM((tokens, D), f32),
            pltpu.VMEM((WIDE, D), f32),
            pltpu.VMEM((WIDE, LEN), b16),
            pltpu.VMEM((2, LEN // 4, LEN // 2), b16),
            pltpu.VMEM((2, LEN // 2, D), b16),
            pltpu.VMEM((REST, HALF, D), b16),
            pltpu.VMEM((REST, NEAR, D), b16),
            pltpu.VMEM((FLOWS, REST, NEAR, D), b16),
            pltpu.VMEM((FLOWS, REST, KEEP, D), b16),
            pltpu.VMEM((2, REST, NEAR, D), b16),
            pltpu.VMEM((2, HALF, D), b16),
            pltpu.VMEM((PAIRS, HALF, WIDE), b16),
            pltpu.VMEM((PAIRS, NEAR, WIDE), b16),
            pltpu.VMEM((FLOWS, PAIRS, NEAR, WIDE), b16),
            pltpu.VMEM((FLOWS, PAIRS, KEEP, WIDE), b16),
            pltpu.VMEM((2, PAIRS, NEAR, WIDE), b16),
            pltpu.VMEM((2, HALF, WIDE), b16),
            pltpu.VMEM((2, HALF, WIDE), b16),
            pltpu.VMEM((FLOWS, PAIRS, KEEP, WIDE), b16),
            pltpu.VMEM((FLOWS, PAIRS, NEAR, WIDE), b16),
            pltpu.VMEM((FLOWS, 2 * CAP, KEEP, D), b16),
            pltpu.VMEM((FLOWS, 2 * CAP, KEEP, D), b16),
            pltpu.VMEM((FLOWS, CAP, NEAR, D), b16),
            pltpu.VMEM((FLOWS, CAP, NEAR, D), b16),
            pltpu.VMEM((FLOWS, CAP, KEEP, D), b16),
            pltpu.VMEM((5, 16, D), f32),
            dma((REST, 7)),
            dma((REST, 7)),
            dma((PAIRS, 11)),
            dma((PAIRS, 11)),
            dma((FLOWS, 2)),
            dma((FLOWS, 2)),
            dma((FLOWS, 3)),
            dma((REST,)),
            dma((REST,)),
            dma((PAIRS,)),
            dma((PAIRS,)),
            dma((3,)),
            dma((PAIRS, 3)),
            dma((3,)),
            dma((3,)),
            dma((3,)),
            dma((5,)),
            dma((5,)),
        ],
        compiler_params=pltpu.CompilerParams(
            collective_id=1, has_side_effects=True, vmem_limit_bytes=62 * MIB
        ),
        name="back",
    )(table, *attention, weights, normed, x, residual, vectors, tiles, sums, y)


def update_kernel(tile_at, one, two, w_ref, m_ref, s_ref, y_in, i_in, w_out, m_out, s_out, y_out, i_out):
    step = pl.program_id(0)
    tile = tile_at[step // 2]
    grad = jnp.where(tile < 3, one[0], two[0]).astype(f32)
    parts = adam_step(w_ref[0], grad, m_ref[0], s_ref[0], RATE)
    for target, part in zip((w_out, m_out, s_out), parts):
        target[0] = jnp.where(tile >= 0, part, jnp.zeros_like(part))

    @pl.when(step < 4)
    def widen():
        y_out[...] = y_in[...].astype(f32)
        i_out[...] = i_in[...].astype(f32)


def update(tile_at, one, two, master, first, second, y, grad):
    tokens = y.shape[0]
    size = HALF // 2
    state = pl.BlockSpec((1, size, D), lambda s, tile_at: (s // 2, lax.rem(s, 2), 0))
    wide = pl.BlockSpec((tokens // 4, D), lambda s, tile_at: (jnp.minimum(s, 3), 0))
    return pl.pallas_call(
        update_kernel,
        grid_spec=pltpu.PrefetchScalarGridSpec(
            num_scalar_prefetch=1,
            grid=(CAP * 2,),
            in_specs=[
                pl.BlockSpec(
                    (1, size, D),
                    lambda s, tile_at: (jnp.clip(tile_at[s // 2], 0, 2), lax.rem(s, 2), 0),
                ),
                state,
                state,
                state,
                state,
                wide,
                wide,
            ],
            out_specs=[state] * 3 + [wide] * 2,
        ),
        out_shape=[jax.ShapeDtypeStruct(master.shape, f32)] * 3
        + [jax.ShapeDtypeStruct((tokens, D), f32)] * 2,
        compiler_params=pltpu.CompilerParams(vmem_limit_bytes=60 * MIB),
        name="update",
    )(tile_at, one, two, master, first, second, y, grad)


def shards_paired(
    inputs,
    cotangent,
    doc_lengths,
    owner_list,
    master,
    first_moment,
    second_moment,
    vectors,
    vector_first,
    vector_second,
):
    rows_here, span, width = inputs.shape
    place = lax.axis_index("blk")
    member = lax.axis_index("dp")
    rows_mine = rows_here // 2
    order = jnp.arange(PIECES)
    same_owner = owner_list[:, None] == owner_list[None, :]
    ranks = jnp.sum(same_owner & (order[None, :] < order[:, None]), axis=1).astype(jnp.int32)
    slot_of = owner_list * CAP + ranks
    front_outs = front(owner_list, doc_lengths, master, vectors, inputs, cotangent)
    x, cot, normed, weights_one, weights_two, queries, keys, values = front_outs[:8]
    weights, recips, context_turned, context = front_outs[8:]
    x = x.reshape(-1, width)
    cot = cot.reshape(-1, width)
    block_out, residual, grad_context, sums, tiles_two = feed(
        context, context_turned, x, cot, weights_two, vectors
    )
    hits = jnp.arange(16 * CAP)[:, None] == slot_of[None, :]
    tile_at = jnp.sum(jnp.where(hits, order[None, :] + 1, 0), axis=1).astype(jnp.int32) - 1
    table = jnp.maximum(tile_at - 3, 0)
    block_out, input_grad, total_one, total_two, vector_total = back(
        table,
        (weights, recips, values, queries, keys, context_turned, grad_context),
        weights_one,
        normed,
        x,
        residual,
        vectors,
        tiles_two,
        sums,
        block_out.reshape(rows_mine, LEN, width),
    )
    mine = lax.dynamic_slice_in_dim(tile_at, member * CAP, CAP, 0)
    *updated, block_out, input_grad = update(
        mine,
        total_one,
        total_two,
        master,
        first_moment,
        second_moment,
        block_out.reshape(-1, width),
        input_grad.reshape(-1, width),
    )
    columns = vector_first.shape[1]
    vector_cols = lax.dynamic_slice_in_dim(vectors, place * columns, columns, 1)
    vector_total = lax.dynamic_slice(vector_total, (0, place * columns), (PIECES, columns))
    updated_vectors = adam_step(vector_cols, vector_total, vector_first, vector_second, VEC_RATE)
    return (
        block_out.reshape(inputs.shape),
        input_grad.reshape(inputs.shape),
        *updated,
        *updated_vectors,
    )


def solution(mesh):
    in_specs = (
        P("dp", "blk", None),
        P("dp", "blk", None),
        P("dp", None),
        P(),
        P("dp", "blk", None),
        P("dp", "blk", None),
        P("dp", "blk", None),
        P(),
        P(None, "blk"),
        P(None, "blk"),
    )
    out_specs = (
        P("dp", "blk", None),
        P("dp", "blk", None),
        P("dp", "blk", None),
        P("dp", "blk", None),
        P("dp", "blk", None),
        P(None, "blk"),
        P(None, "blk"),
        P(None, "blk"),
    )
    paired = mesh.shape["blk"] == 2 and mesh.shape["dp"] == 16
    shards = shards_paired if paired else shards_any
    return jax.shard_map(shards, mesh=mesh, in_specs=in_specs, out_specs=out_specs, check_vma=False)
```

```python
from functools import partial

import jax
import jax.numpy as jnp
from jax import lax
from jax.experimental import pallas as pl
from jax.experimental.pallas import tpu as pltpu
from jax.sharding import PartitionSpec as P

D = 768
FF = 3072
HEADS = 12
HEAD_DIM = 64
LEN = 1024
CAP = 3
STEP = 10
PIECES = 12


EPS_NORM = 1e-05
BETA_ONE = 0.9
BETA_TWO = 0.999
RATE = 0.04
VEC_RATE = 0.25
DECAY = 0.01
ADAM_EPS = 1e-08


def normalize(values_in, gain, shift):
    center = jnp.mean(values_in, axis=-1, keepdims=True)
    offset = values_in - center
    spread = jnp.mean(offset * offset, axis=-1, keepdims=True)
    return offset * lax.rsqrt(spread + EPS_NORM) * gain + shift


def adam_step(weight, grad, first, second, rate):
    first_new = BETA_ONE * first + (1.0 - BETA_ONE) * grad
    second_new = BETA_TWO * second + (1.0 - BETA_TWO) * grad * grad
    corrected = (
        first_new
        / (1.0 - BETA_ONE**STEP)
        / (jnp.sqrt(second_new / (1.0 - BETA_TWO**STEP)) + ADAM_EPS)
    )
    return (weight - rate * (corrected + DECAY * weight), first_new, second_new)


def shards_any(
    inputs,
    cotangent,
    doc_lengths,
    owner_list,
    master,
    first_moment,
    second_moment,
    vectors,
    vector_first,
    vector_second,
):
    rows_here, span, width = inputs.shape
    tokens_here = rows_here * span
    fold = FF // D
    scale = HEAD_DIM ** (-0.5)
    place = lax.axis_index("blk")
    f32 = jnp.float32
    b16 = jnp.bfloat16
    order = jnp.arange(PIECES)
    same_owner = owner_list[:, None] == owner_list[None, :]
    ranks = jnp.sum(same_owner & (order[None, :] < order[:, None]), axis=1)
    slot_of = owner_list * CAP + ranks

    mine = (owner_list == lax.axis_index("dp"))[:, None, None]
    tile_rows = lax.psum(jnp.where(mine, master[ranks], 0.0).astype(b16), "dp")
    tiles = lax.all_gather(tile_rows, "blk", axis=1, tiled=True)
    query_weight = tiles[0]
    key_weight = tiles[1]
    value_weight = tiles[2]
    out_weight = tiles[3]
    up_weight = jnp.transpose(tiles[4 : 4 + fold], (1, 0, 2)).reshape(width, FF)
    down_weight = tiles[4 + fold :].reshape(FF, width)
    flat_in = inputs.reshape(tokens_here, width).astype(f32)
    normed_one = normalize(flat_in, vectors[0], vectors[1]).astype(b16)
    queries = (jnp.dot(normed_one, query_weight, preferred_element_type=f32) + vectors[4]).astype(
        b16
    )
    keys_here = jnp.dot(normed_one, key_weight, preferred_element_type=f32).astype(b16)
    values_here = (
        jnp.dot(normed_one, value_weight, preferred_element_type=f32) + vectors[5]
    ).astype(b16)
    query_heads = queries.reshape(rows_here, span, HEADS, HEAD_DIM)
    first_len = doc_lengths[:, 0]
    query_seg = (place * span + jnp.arange(span))[None, :] >= first_len[:, None]

    def block_scores(key_block, start):
        count = key_block.shape[1]
        key_heads = key_block.reshape(rows_here, count, HEADS, HEAD_DIM)
        raw = (
            jnp.einsum("rqhd,rkhd->rhqk", query_heads, key_heads, preferred_element_type=f32)
            * scale
        )
        key_seg = (start + jnp.arange(count))[None, :] >= first_len[:, None]
        allowed = query_seg[:, None, :, None] == key_seg[:, None, None, :]
        return (raw, allowed)

    key_rows = keys_here.reshape(rows_here, span, width)
    value_rows = values_here.reshape(rows_here, span, width)
    top = jnp.full((rows_here, HEADS, span), -1e30, f32)
    key_block = lax.all_gather(key_rows, "blk", axis=1, tiled=True)
    value_block = lax.all_gather(value_rows, "blk", axis=1, tiled=True)
    count = key_block.shape[1]
    raw, allowed = block_scores(key_block, jnp.int32(0))
    new_top = jnp.maximum(top, jnp.max(jnp.where(allowed, raw, -1e30), axis=-1))
    weights = jnp.where(allowed, jnp.exp(raw - new_top[..., None]), 0.0)
    value_heads = value_block.reshape(rows_here, count, HEADS, HEAD_DIM)
    update = jnp.einsum(
        "rhqk,rkhd->rhqd", weights.astype(b16), value_heads, preferred_element_type=f32
    )
    total = jnp.sum(weights, axis=-1)
    log_total = new_top + jnp.log(total)
    context_raw = update / total[..., None]
    context_low = jnp.transpose(context_raw, (0, 2, 1, 3)).reshape(tokens_here, width).astype(b16)
    residual = flat_in + (jnp.dot(context_low, out_weight, preferred_element_type=f32) + vectors[6])
    normed_two = normalize(residual, vectors[2], vectors[3]).astype(b16)
    hidden = jnp.dot(normed_two, up_weight, preferred_element_type=f32) + vectors[8:].reshape(FF)
    gelu_exact = partial(jax.nn.gelu, approximate=False)
    active, gelu_pull = jax.vjp(gelu_exact, hidden)
    active_low = active.astype(b16)
    block_out = (
        residual + (jnp.dot(active_low, down_weight, preferred_element_type=f32) + vectors[7])
    ).reshape(rows_here, span, width)
    grad_out = cotangent.reshape(tokens_here, width)
    down_grad = jnp.einsum("tf,td->fd", active_low, grad_out, preferred_element_type=f32)
    down_sum = jnp.sum(grad_out, axis=0, dtype=f32)
    grad_active = jnp.einsum("td,fd->tf", grad_out, down_weight, preferred_element_type=f32)
    grad_hidden = gelu_pull(grad_active)[0].astype(b16)
    up_grad = jnp.einsum("td,tf->df", normed_two, grad_hidden, preferred_element_type=f32)
    up_sum = jnp.sum(grad_hidden, axis=0, dtype=f32)
    ffn_tiles = jnp.concatenate(
        [
            jnp.transpose(up_grad.reshape(width, fold, width), (1, 0, 2)),
            down_grad.reshape(fold, width, width),
        ],
        axis=0,
    )
    grad_normed_two = jnp.einsum("tf,df->td", grad_hidden, up_weight, preferred_element_type=f32)
    unused, second_pull = jax.vjp(normalize, residual, vectors[2], vectors[3])
    residual_part, gain_two_grad, shift_two_grad = second_pull(grad_normed_two)
    grad_residual = grad_out.astype(f32) + residual_part
    grad_attended = grad_residual.astype(b16)
    out_grad = jnp.einsum("tm,td->md", context_low, grad_attended, preferred_element_type=f32)
    out_sum = jnp.sum(grad_attended, axis=0, dtype=f32)
    grad_context = jnp.einsum(
        "td,md->tm", grad_attended, out_weight, preferred_element_type=f32
    ).astype(b16)
    grad_heads = grad_context.reshape(rows_here, span, HEADS, HEAD_DIM)
    delta = jnp.einsum("rqhd,rhqd->rhq", grad_heads.astype(f32), context_raw)
    key_all, value_all = (
        lax.all_gather(key_rows, "blk", axis=1, tiled=True),
        lax.all_gather(value_rows, "blk", axis=1, tiled=True),
    )
    key_size = min(512, LEN)

    def back_block(index, carry):
        grad_query, key_total, value_total = carry
        start = index * key_size
        key_block = lax.dynamic_slice_in_dim(key_all, start, key_size, 1)
        value_block = lax.dynamic_slice_in_dim(value_all, start, key_size, 1)
        raw, allowed = block_scores(key_block, start)
        weights_back = jnp.where(allowed, jnp.exp(raw - log_total[..., None]), 0.0)
        key_heads = key_block.reshape(rows_here, key_size, HEADS, HEAD_DIM)
        value_heads = value_block.reshape(rows_here, key_size, HEADS, HEAD_DIM)
        value_grad = jnp.einsum(
            "rhqk,rqhd->rkhd", weights_back.astype(b16), grad_heads, preferred_element_type=f32
        )
        weight_grad = jnp.einsum(
            "rqhd,rkhd->rhqk", grad_heads, value_heads, preferred_element_type=f32
        )
        score_grad = (weights_back * (weight_grad - delta[..., None])).astype(b16)
        grad_query = (
            grad_query
            + jnp.einsum("rhqk,rkhd->rqhd", score_grad, key_heads, preferred_element_type=f32)
            * scale
        )
        key_grad = (
            jnp.einsum("rhqk,rqhd->rkhd", score_grad, query_heads, preferred_element_type=f32)
            * scale
        )
        key_total = lax.dynamic_update_slice_in_dim(
            key_total, key_grad.reshape(rows_here, key_size, width), start, 1
        )
        value_total = lax.dynamic_update_slice_in_dim(
            value_total, value_grad.reshape(rows_here, key_size, width), start, 1
        )
        return (grad_query, key_total, value_total)

    zero_rows = jnp.zeros((rows_here, LEN, width), f32)
    grad_query, key_total, value_total = lax.fori_loop(
        0,
        LEN // key_size,
        back_block,
        (jnp.zeros((rows_here, span, HEADS, HEAD_DIM), f32), zero_rows, zero_rows),
    )
    key_grad_here, value_grad_here = (
        lax.psum_scatter(
            key_total.astype(jnp.bfloat16), "blk", scatter_dimension=1, tiled=True
        ).astype(jnp.float32),
        lax.psum_scatter(
            value_total.astype(jnp.bfloat16), "blk", scatter_dimension=1, tiled=True
        ).astype(jnp.float32),
    )
    query_low = grad_query.reshape(tokens_here, width).astype(b16)
    key_low = key_grad_here.reshape(tokens_here, width).astype(b16)
    value_low = value_grad_here.reshape(tokens_here, width).astype(b16)
    query_tile = jnp.einsum("td,te->de", normed_one, query_low, preferred_element_type=f32)
    key_tile = jnp.einsum("td,te->de", normed_one, key_low, preferred_element_type=f32)
    value_tile = jnp.einsum("td,te->de", normed_one, value_low, preferred_element_type=f32)
    grad_normed_one = (
        jnp.einsum("te,de->td", query_low, query_weight, preferred_element_type=f32)
        + jnp.einsum("te,de->td", key_low, key_weight, preferred_element_type=f32)
        + jnp.einsum("te,de->td", value_low, value_weight, preferred_element_type=f32)
    )
    unused, first_pull = jax.vjp(normalize, flat_in, vectors[0], vectors[1])
    input_part, gain_one_grad, shift_one_grad = first_pull(grad_normed_one)
    input_grad = (grad_residual + input_part).reshape(rows_here, span, width)
    vector_grads = jnp.concatenate(
        [
            jnp.stack(
                [
                    gain_one_grad,
                    shift_one_grad,
                    gain_two_grad,
                    shift_two_grad,
                    jnp.sum(query_low, axis=0, dtype=f32),
                    jnp.sum(value_low, axis=0, dtype=f32),
                    out_sum,
                    down_sum,
                ]
            ),
            up_sum.reshape(fold, width),
        ],
        axis=0,
    )
    attn_tiles = jnp.stack([query_tile, key_tile, value_tile, out_grad])
    piece_share, vector_share = (
        lax.psum_scatter(
            jnp.concatenate([attn_tiles, ffn_tiles], axis=0).astype(jnp.bfloat16),
            "blk",
            scatter_dimension=1,
            tiled=True,
        ).astype(jnp.float32),
        lax.psum_scatter(
            vector_grads.astype(jnp.bfloat16), "blk", scatter_dimension=1, tiled=True
        ).astype(jnp.float32),
    )
    own_slots = lax.axis_index("dp") * CAP + jnp.arange(CAP)
    pick = (own_slots[:, None] == slot_of[None, :]).astype(f32)
    occupied = jnp.sum(pick, axis=1)[:, None, None]
    total_share, vector_total = (
        lax.psum(piece_share.astype(jnp.bfloat16), "dp").astype(jnp.float32),
        lax.psum(vector_share.astype(jnp.bfloat16), "dp").astype(jnp.float32),
    )
    slot_grads = jnp.einsum("cp,prd->crd", pick, total_share, precision=lax.Precision.HIGHEST)
    new_master, new_first, new_second = adam_step(
        master, slot_grads, first_moment, second_moment, RATE
    )
    columns = vector_first.shape[1]
    vector_cols = lax.dynamic_slice_in_dim(vectors, place * columns, columns, 1)
    new_vectors, new_vector_first, new_vector_second = adam_step(
        vector_cols, vector_total, vector_first, vector_second, VEC_RATE
    )
    return (
        block_out,
        input_grad,
        new_master * occupied,
        new_first * occupied,
        new_second * occupied,
        new_vectors,
        new_vector_first,
        new_vector_second,
    )


f32 = jnp.float32
b16 = jnp.bfloat16
LOG2E = 1.4426950408889634
MIB = 1024 * 1024
PAIRS = HEADS // 2
PAIR = 2 * HEAD_DIM


def dot_nn(left, right):
    return lax.dot_general(left, right, (((1,), (0,)), ((), ())), preferred_element_type=f32)


def dot_nt(left, right):
    return lax.dot_general(left, right, (((1,), (1,)), ((), ())), preferred_element_type=f32)


def dot_tn(left, right):
    return lax.dot_general(left, right, (((0,), (0,)), ((), ())), preferred_element_type=f32)


def norm_parts(values_in):
    center = jnp.mean(values_in, axis=-1, keepdims=True)
    offset = values_in - center
    spread = jnp.mean(offset * offset, axis=-1, keepdims=True)
    rstd = lax.rsqrt(spread + EPS_NORM)
    return offset * rstd, rstd


def norm_back(grad, unit, rstd, gain):
    scaled = grad * gain
    first = jnp.mean(scaled, axis=-1, keepdims=True)
    second = jnp.mean(scaled * unit, axis=-1, keepdims=True)
    return rstd * (scaled - first - unit * second)


def gelu_parts(value):
    bell = jnp.exp2(value * value * (-0.5 * LOG2E))
    ratio = pl.reciprocal(1.0 + (0.3275911 * 0.7071067811865476) * jnp.abs(value))
    poly = 0.5 * 1.061405429
    poly = poly * ratio + 0.5 * -1.453152027
    poly = poly * ratio + 0.5 * 1.421413741
    poly = poly * ratio + 0.5 * -0.284496736
    poly = poly * ratio + 0.5 * 0.254829592
    tail = poly * ratio * bell
    cdf = jnp.where(value >= 0.0, 1.0 - tail, tail)
    return value * cdf, cdf + value * (bell * 0.3989422804014327)


def head_only(block, head):
    lane = lax.broadcasted_iota(jnp.int32, block.shape, 1)
    keep = (lane >= head * HEAD_DIM) & (lane < (head + 1) * HEAD_DIM)
    return jnp.where(keep, block, jnp.zeros_like(block))


def feed_kernel(
    c_ref, o_ref, x_ref, g_ref, w_ref, vec_ref,
    y_ref, r_ref, d_ref, sums_ref, tiles_ref,
    acc_ref, turned_ref, stage_ref, sem_ref,
):
    fold = FF // D
    step = pl.program_id(0)

    @pl.when(step == 0)
    def clear():
        acc_ref[...] = jnp.zeros_like(acc_ref)
        sums_ref[...] = jnp.zeros_like(sums_ref)

        def turn(part, carry):
            turned_ref[part] = w_ref[1 + part].T
            return carry

        lax.fori_loop(0, 2 * fold, turn, 0)

    residual = x_ref[...].astype(f32) + (dot_nn(c_ref[...], w_ref[0]) + vec_ref[6:7, :])
    unit, rstd = norm_parts(residual)
    gain = vec_ref[2:3, :]
    normed = (unit * gain + vec_ref[3:4, :]).astype(b16)
    turned = normed.T
    cot = g_ref[...]
    out = residual + vec_ref[7:8, :]
    grad = jnp.zeros_like(out)

    for part in range(fold):
        hidden = dot_nn(normed, w_ref[1 + part]) + vec_ref[8 + part : 9 + part, :]
        pulled = dot_nn(cot, turned_ref[fold + part])
        active, slope = gelu_parts(hidden)
        active = active.astype(b16)
        pulled = (pulled * slope).astype(b16)
        out = out + dot_nn(active, w_ref[1 + fold + part])
        grad = grad + dot_nn(pulled, turned_ref[part])
        acc_ref[1 + part] += dot_nn(turned, pulled)
        acc_ref[1 + fold + part] += dot_tn(active, cot)
        sums_ref[8 + part : 9 + part, :] += jnp.sum(pulled.astype(f32), 0, keepdims=True)
    y_ref[...] = out.astype(b16)
    wide = cot.astype(f32)
    sums_ref[2:3, :] += jnp.sum(grad * unit, 0, keepdims=True)
    sums_ref[3:4, :] += jnp.sum(grad, 0, keepdims=True)
    sums_ref[7:8, :] += jnp.sum(wide, 0, keepdims=True)
    back = wide + norm_back(grad, unit, rstd, gain)
    r_ref[...] = back.astype(b16)
    low = back.astype(b16)
    sums_ref[6:7, :] += jnp.sum(low.astype(f32), 0, keepdims=True)
    d_ref[...] = dot_nt(w_ref[0], low).astype(b16)
    acc_ref[0] += dot_nn(o_ref[...], low)

    @pl.when(step == pl.num_programs(0) - 1)
    def send():
        count = 1 + 2 * fold
        copies = []
        for part in range(count):
            if part >= 2:
                copies[part - 2].wait()
            stage_ref[part % 2] = acc_ref[part].astype(b16)
            copy = pltpu.make_async_copy(stage_ref.at[part % 2], tiles_ref.at[part], sem_ref.at[part % 2])
            copy.start()
            copies.append(copy)
        copies[count - 2].wait()
        copies[count - 1].wait()


def feed(context, turned, x, cot, weights, vectors):
    tokens = x.shape[0]
    size = 256
    count = 1 + 2 * (FF // D)
    token_block = pl.BlockSpec((size, D), lambda i: (i, 0))
    turned_block = pl.BlockSpec((D, size), lambda i: (0, i))
    return pl.pallas_call(
        feed_kernel,
        grid=(tokens // size,),
        in_specs=[
            token_block,
            turned_block,
            token_block,
            token_block,
            pl.BlockSpec((count, D, D), lambda i: (0, 0, 0), pipeline_mode=pl.Buffered(1)),
            pl.BlockSpec((PIECES, D), lambda i: (0, 0)),
        ],
        out_specs=[
            token_block,
            token_block,
            turned_block,
            pl.BlockSpec((16, D), lambda i: (0, 0)),
            pl.BlockSpec(memory_space=pl.ANY),
        ],
        out_shape=[
            jax.ShapeDtypeStruct((tokens, D), b16),
            jax.ShapeDtypeStruct((tokens, D), b16),
            jax.ShapeDtypeStruct((D, tokens), b16),
            jax.ShapeDtypeStruct((16, D), f32),
            jax.ShapeDtypeStruct((count, D, D), b16),
        ],
        scratch_shapes=[
            pltpu.VMEM((count, D, D), f32),
            pltpu.VMEM((count - 1, D, D), b16),
            pltpu.VMEM((2, D, D), b16),
            pltpu.SemaphoreType.DMA((2,)),
        ],
        compiler_params=pltpu.CompilerParams(vmem_limit_bytes=62 * MIB),
        cost_estimate=pl.CostEstimate(
            flops=6 * count * tokens * D * D,
            bytes_accessed=18 * tokens * D + 4 * count * D * D,
            transcendentals=2 * tokens * FF,
        ),
        name="feed",
    )(context, turned, x, cot, weights, vectors)


MESH = pl.DeviceIdType.MESH
HALF = D // 2
FLOWS = 2
FLOW = HALF // FLOWS
NEAR = FLOW // 2
KEEP = NEAR // 2
WIDE = 3 * PAIR
REST = PIECES - 3
GROUPS = ((0, 1), (1, 2), (3, 3))
CHUNKS = len(GROUPS)


class Place:
    def __init__(self):
        self.me = lax.axis_index("dp")
        self.core = lax.axis_index("blk")
        self.bits = [lax.rem(self.me // weight, 2) for weight in (1, 2, 4, 8)]
        self.chips = [
            self.me + weight - 2 * weight * bit for weight, bit in zip((1, 2, 4, 8), self.bits)
        ]
        self.partners = [{"dp": chip} for chip in self.chips]
        low, high = self.bits[2:]
        self.inner = low != high
        self.across = {"dp": self.me + 4 - 8 * low + 8 - 16 * high}
        self.other = 1 - self.core
        self.twin = {"blk": self.other}

    def greet(self):
        barrier = pltpu.get_barrier_semaphore()
        for device in self.partners + [self.across, self.twin]:
            pl.semaphore_signal(barrier, 1, device_id=device, device_id_type=MESH)
        pl.semaphore_wait(barrier, 6)

    def flow(self, index):
        first, second = (0, 1) if index == 0 else (1, 0)
        base = index * FLOW
        near = base + self.bits[first] * NEAR
        far = base + NEAR - self.bits[first] * NEAR
        keep = near + self.bits[second] * KEEP
        give = near + KEEP - self.bits[second] * KEEP
        return first, second, near, far, keep, give


def remote(source, target, send, receive, device):
    return pltpu.make_async_remote_copy(
        src_ref=source,
        dst_ref=target,
        send_sem=send,
        recv_sem=receive,
        device_id=device,
        device_id_type=MESH,
    )


def rows_at(start, count):
    return pl.ds(pl.multiple_of(start, 16), count)


class Spread:
    def __init__(self, place, owner, rank, slots, land, gift, sems):
        self.place, self.owner, self.rank = place, owner, rank
        self.slots, self.land, self.gift, self.sems = slots, land, gift, sems

    def cols(self, chunk):
        return pl.ds(GROUPS[chunk][0] * PAIR, GROUPS[chunk][1] * PAIR)

    def first_copy(self, chunk, index):
        first, second, near, far, keep, give = self.place.flow(index)
        return remote(
            self.slots.at[:, rows_at(far, NEAR), self.cols(chunk)],
            self.land[chunk].at[index],
            self.sems[0].at[chunk, index, 0],
            self.sems[1].at[chunk, index, 0],
            self.place.partners[first],
        )

    def second_copy(self, chunk, index, which):
        first, second, near, far, keep, give = self.place.flow(index)
        if which == 0:
            source = self.slots.at[:, rows_at(give, KEEP), self.cols(chunk)]
        else:
            source = self.land[chunk].at[index, :, rows_at(give - near, KEEP)]
        return remote(
            source,
            self.gift[chunk].at[index, pl.ds(which * CAP, CAP)],
            self.sems[0].at[chunk, index, 1 + which],
            self.sems[1].at[chunk, index, 1 + which],
            self.place.partners[second],
        )

    def step(self, chunk, index):
        for flow in range(FLOWS):
            if index == 0:
                self.first_copy(chunk, flow).start()
                self.second_copy(chunk, flow, 0).start()
            if index == 1:
                self.first_copy(chunk, flow).wait()
                self.second_copy(chunk, flow, 1).start()
            if index == 2:
                self.second_copy(chunk, flow, 0).wait()
                self.second_copy(chunk, flow, 1).wait()

    def piece(self, tile, index, chunk, start, count):
        first, second, near, far, keep, give = self.place.flow(index)
        owner, rank = self.owner[tile], self.rank[tile]
        bits = [lax.rem(owner, 2), lax.rem(owner // 2, 2)]
        apart = [bit != mine for bit, mine in zip(bits, self.place.bits)]
        cols = pl.ds(start, count)
        mine = self.slots[rank, rows_at(keep, KEEP), pl.ds(GROUPS[chunk][0] * PAIR + start, count)]
        firsts = self.land[chunk][index, rank, rows_at(keep - near, KEEP), cols]
        gifts = self.gift[chunk][index, jnp.where(apart[first], CAP, 0) + rank, :, cols]
        value = jnp.where(apart[second], gifts, jnp.where(apart[first], firsts, mine))
        layer = owner // 4 == self.place.me // 4
        return jnp.where(layer, value, jnp.zeros_like(value))


class Column:
    steps = 4

    def __init__(self, place, kept, land, sems):
        self.place, self.kept, self.land, self.sems = place, kept, land, sems

    def copy(self, index):
        device = self.place.across if index == 1 else self.place.partners[2]
        return remote(
            self.kept, self.land.at[index % 2], self.sems[0].at[index], self.sems[1].at[index], device
        )

    def add(self, index):
        self.kept[...] = (self.kept[...].astype(f32) + self.land[index].astype(f32)).astype(b16)


def both_flows(flow):
    return pl.ds(flow * KEEP, KEEP)


def column_step(place, column, index):
    @pl.when(place.inner)
    def inner():
        if index == 1:
            column.copy(0).wait_recv()
            column.add(0)
            column.copy(1).start()
        if index == 2:
            column.copy(1).wait()
            column.add(1)
            column.copy(2).start()
        if index == 3:
            column.copy(2).wait_send()

    @pl.when(jnp.logical_not(place.inner))
    def outer():
        if index == 0:
            column.copy(0).start()
        if index == 1:
            column.copy(0).wait_send()
        if index == 3:
            column.copy(2).wait_recv()
            column.kept[...] = column.land[0]


class Item:
    steps = 7

    def __init__(self, place, work, kept, land, sems, load, store=None):
        self.place, self.work, self.kept, self.land, self.sems = place, work, kept, land, sems
        self.load, self.store = load, store
        self.base = place.core * HALF

    def copy(self, flow, index):
        first, second, near, far, keep, give = self.place.flow(flow)
        kept = self.work.at[:, rows_at(self.base + keep, KEEP)]
        half = self.work.at[:, rows_at(self.base + near, NEAR)]
        source, device = [
            (kept, self.place.partners[second]),
            (half, self.place.partners[first]),
        ][index]
        number = 3 + 2 * flow + index
        return remote(source, source, self.sems[0].at[number], self.sems[1].at[number], device)

    def pair(self):
        rows = self.work.at[:, rows_at(self.base, HALF)]
        return remote(rows, rows, self.sems[0].at[7], self.sems[1].at[7], self.place.twin)

    def step(self, index):
        if index == 0:
            for flow in range(FLOWS):
                self.load(self.kept, both_flows(flow), flow)
        if index <= 3:
            column_step(self.place, Column(self.place, self.kept, self.land, self.sems), index)
        for flow in range(FLOWS):
            if index == 3:
                rows = rows_at(self.base + self.place.flow(flow)[4], KEEP)
                self.work[:, rows] = self.kept[:, both_flows(flow)]
            if 4 <= index <= 5:
                self.copy(flow, index - 4).wait()
            if 3 <= index <= 4:
                self.copy(flow, index - 3).start()
        if index == 5:
            self.pair().start()
        if index == 6:
            self.pair().wait()
            self.store().start()


REST_GROUPS = tuple((index, 1) for index in range(REST))
PAIR_CHUNK = (0, 1, 1, 2, 2, 2)
FRONT_PAIRS = (2, 4, 5, 6, 7, 8)
FRONT_REST = (6, 7, 8, 9, 10, 11, 12, 13, 14)
FRONT_LEAD = 9


def front_kernel(
    owner, lengths, master, vec_ref, x_in, c_in,
    x_out, c_out, n_out, one_out, two_out, q_ref, k_ref, v_ref, p_ref, r_ref, o_ref, ctx_ref,
    rank, rows_ref, normed, keys, turned_values, scores, slots,
    land_one, land_two, land_three, gift_one, gift_two, gift_three,
    one, one_kept, one_land, two, two_kept, two_land,
    spread_send, spread_recv, one_send, one_recv, two_send, two_recv,
    swap_send, swap_recv, swap_local, store_sem,
):
    pair = pl.program_id(0)
    row = pl.program_id(1)
    grid_step = pair * 2 + row
    place = Place()
    rows, span = x_in.shape[0] // 2, x_in.shape[1]
    land = (land_one, land_two, land_three)
    gift = (gift_one, gift_two, gift_three)
    spread = Spread(place, owner, rank, slots, land, gift, (spread_send, spread_recv))

    def swaps(index):
        source, target = [(x_in, rows_ref), (c_in, c_out)][index]
        here = pl.ds(place.core * span, span)
        near = pltpu.make_async_copy(
            source.at[pl.ds(place.core * rows, rows)], target.at[:, here], swap_local.at[index]
        )
        far = remote(
            source.at[pl.ds(place.other * rows, rows)],
            target.at[:, here],
            swap_send.at[index],
            swap_recv.at[index],
            place.twin,
        )
        return near, far

    def row_store():
        return pltpu.make_async_copy(rows_ref, x_out, store_sem.at[PAIRS + REST])

    def normed_store():
        return pltpu.make_async_copy(normed, n_out, store_sem.at[PAIRS + REST + 1])

    def pair_item(group):
        span_of = pl.ds(group, 1)

        def load(work, where, flow):
            chunk = PAIR_CHUNK[group]
            for tile in range(3):
                part = spread.piece(tile, flow, chunk, (group - GROUPS[chunk][0]) * PAIR, PAIR)
                work[0, where, pl.ds(tile * PAIR, PAIR)] = part

        def store():
            return pltpu.make_async_copy(one.at[span_of], one_out.at[span_of], store_sem.at[group])

        sems = (one_send.at[group], one_recv.at[group])
        return Item(place, one.at[span_of], one_kept.at[span_of], one_land.at[:, span_of], sems, load, store)

    def rest_item(group):
        first, count = REST_GROUPS[group]
        span_of = pl.ds(first, count)

        def load(work, where, flow):
            for index in range(count):
                for chunk, (start, wide) in enumerate(GROUPS):
                    part = spread.piece(3 + first + index, flow, chunk, 0, wide * PAIR)
                    work[index, where, pl.ds(start * PAIR, wide * PAIR)] = part

        def store():
            return pltpu.make_async_copy(
                two.at[span_of], two_out.at[span_of], store_sem.at[PAIRS + group]
            )

        sems = (two_send.at[group], two_recv.at[group])
        return Item(place, two.at[span_of], two_kept.at[span_of], two_land.at[:, span_of], sems, load, store)

    def tick(number, odd):
        for chunk in range(CHUNKS):
            if odd == 0 and 0 <= number - 2 * chunk <= 2:
                spread.step(chunk, number - 2 * chunk)
        starts = [(pair_item, group, start) for group, start in enumerate(FRONT_PAIRS)]
        starts += [(rest_item, group, start) for group, start in enumerate(FRONT_REST)]
        for make, group, start in starts:
            if group % 2 == odd and 0 <= number - start < Item.steps:
                make(group).step(number - start)

    def both(number):
        tick(number, 0)
        tick(number, 1)

    @pl.when(grid_step == 0)
    def lead():
        slots[...] = master[...].astype(b16)
        for tile in range(PIECES):
            count = jnp.int32(0)
            for before in range(tile):
                count = count + (owner[before] == owner[tile]).astype(jnp.int32)
            rank[tile] = jnp.minimum(count, CAP - 1)
        place.greet()
        for copy in swaps(0):
            copy.start()
        both(0)
        for copy in swaps(1):
            copy.start()
        for copy in swaps(0):
            copy.wait()
        row_store().start()

        def norm_rows(index, carry):
            for part in range(rows):
                for block in range(4):
                    where = pl.ds(pl.multiple_of(index * 128 + block * 32, 32), 32)
                    unit, unused = norm_parts(rows_ref[part, where].astype(f32))
                    low = (unit * vec_ref[0:1, :] + vec_ref[1:2, :]).astype(b16)
                    normed[pl.ds(pl.multiple_of(part * LEN + index * 128 + block * 32, 32), 32)] = low
            return carry

        for number in range(1, FRONT_LEAD):
            both(number)
            lax.fori_loop(number - 1, number, norm_rows, 0)
        normed_store().start()

    for number in range(2 * PAIRS):
        pl.when(grid_step == number)(partial(tick, FRONT_LEAD + number, 0))

    @pl.when(row == 0)
    def project():
        lanes = pl.ds(pl.multiple_of(pair * PAIR, PAIR), PAIR)
        weight = one[pair]

        def part(index, carry):
            where = pl.ds(pl.multiple_of(index * 512, 512), 512)
            both = dot_nn(normed[where], weight)
            queries = both[:, :PAIR] + vec_ref[4:5, lanes]
            queries = (queries * (HEAD_DIM**-0.5 * LOG2E)).astype(b16)
            q_ref[:, where] = queries.T
            low = both[:, PAIR : 2 * PAIR].astype(b16)
            keys[where] = low
            k_ref[:, where] = low.T
            values = (both[:, 2 * PAIR :] + vec_ref[5:6, lanes]).astype(b16)
            v_ref[where] = values
            turned_values[:, where] = values.T
            return carry

        lax.fori_loop(0, normed.shape[0] // 512, part, 0)

    half = LEN // 2
    start = pl.multiple_of(row * LEN, LEN)
    split = lengths[place.core * rows + row, 0] < LEN
    shift = jnp.where(split, jnp.float32(-1e30), jnp.float32(0.0))

    quarter = LEN // 4
    units = [(head, step) for head in range(2) for step in range(2)]

    def score_block(unit, block, peak):
        head, step = units[unit]
        rows_here = pl.ds(pl.multiple_of(start + block * quarter, quarter), quarter)
        queries = q_ref[:, pl.ds(pl.multiple_of(start + step * half, half), half)]
        raw = dot_nn(head_only(keys[rows_here], head), queries)
        if block // 2 != step:
            raw = raw + shift
        scores[unit % 2, block * quarter : (block + 1) * quarter] = raw
        best = jnp.max(raw.reshape(-1, 8, half), axis=0)
        return best if peak is None else jnp.maximum(peak, best)

    def context_block(unit, block, total):
        head, step = units[unit]
        part = slice(head * HEAD_DIM, (head + 1) * HEAD_DIM)
        cols = pl.ds(pl.multiple_of(start + block * quarter, quarter), quarter)
        here = slice(step * half, (step + 1) * half)
        term = dot_nn(
            turned_values[part, cols], p_ref[head, block * quarter : (block + 1) * quarter, here]
        )
        return term if total is None else total + term

    def context_store(unit, total, recip):
        head, step = units[unit]
        part = slice(head * HEAD_DIM, (head + 1) * HEAD_DIM)
        o_ref[part, step * half : (step + 1) * half] = (total * recip).astype(b16)

    peak = None
    for block in range(4):
        peak = score_block(0, block, peak)
    before = None
    for unit, (head, step) in enumerate(units):
        if unit == 2:
            for number in range(2 * PAIRS):
                pl.when(grid_step == number)(partial(tick, FRONT_LEAD + number, 1))
        here = slice(step * half, (step + 1) * half)
        top = jnp.max(peak, 0, keepdims=True)
        total = jnp.zeros((8, half), f32)
        peak, context = None, None
        for block in range(4):
            if unit + 1 < len(units):
                peak = score_block(unit + 1, block, peak)
            for small in range(4 * block, 4 * block + 4):
                rows_here = slice(small * 64, (small + 1) * 64)
                value = jnp.exp2(scores[unit % 2, rows_here] - top)
                total = total + jnp.sum(value.reshape(-1, 8, half), axis=0)
                p_ref[head, rows_here, here] = value.astype(b16)
            if unit > 0:
                context = context_block(unit - 1, block, context)
        if unit > 0:
            context_store(unit - 1, context, before)
        before = 1.0 / jnp.sum(total, 0, keepdims=True)
        r_ref[0, head : head + 1, here] = before
    context = None
    for block in range(4):
        context = context_block(3, block, context)
    context_store(3, context, before)
    ctx_ref[...] = o_ref[...].T

    @pl.when(grid_step == 2 * PAIRS - 1)
    def finish_copies():
        for copy in swaps(1):
            copy.wait()
        row_store().wait()
        normed_store().wait()
        for group in range(PAIRS):
            pair_item(group).store().wait()
        for group in range(REST):
            rest_item(group).store().wait()


def front(owner, lengths, master, vectors, inputs, cotangent):
    rows, span = inputs.shape[0] // 2, inputs.shape[1]
    tokens = rows * LEN
    any_spec = pl.BlockSpec(memory_space=pl.ANY)
    smem = pl.BlockSpec(memory_space=pltpu.SMEM)
    whole = jax.ShapeDtypeStruct((rows, LEN, D), b16)
    dma = pltpu.SemaphoreType.DMA
    return pl.pallas_call(
        front_kernel,
        grid=(PAIRS, rows),
        in_specs=[
            smem,
            smem,
            pl.BlockSpec((CAP, HALF, D), lambda h, r: (0, 0, 0), pipeline_mode=pl.Buffered(1)),
            pl.BlockSpec((PIECES, D), lambda h, r: (0, 0)),
            any_spec,
            any_spec,
        ],
        out_specs=[any_spec] * 5
        + [
            pl.BlockSpec((PAIR, tokens), lambda h, r: (h, 0)),
            pl.BlockSpec((PAIR, tokens), lambda h, r: (h, 0)),
            pl.BlockSpec((tokens, PAIR), lambda h, r: (0, h)),
            pl.BlockSpec((2, LEN, LEN), lambda h, r: (h * 2 + r, 0, 0)),
            pl.BlockSpec((1, 2, LEN), lambda h, r: (h * 2 + r, 0, 0)),
            pl.BlockSpec((PAIR, LEN), lambda h, r: (h, r)),
            pl.BlockSpec((LEN, PAIR), lambda h, r: (r, h)),
        ],
        out_shape=[
            whole,
            whole,
            jax.ShapeDtypeStruct((tokens, D), b16),
            jax.ShapeDtypeStruct((PAIRS, D, WIDE), b16),
            jax.ShapeDtypeStruct((REST, D, D), b16),
            jax.ShapeDtypeStruct((D, tokens), b16),
            jax.ShapeDtypeStruct((D, tokens), b16),
            jax.ShapeDtypeStruct((tokens, D), b16),
            jax.ShapeDtypeStruct((rows * HEADS, LEN, LEN), b16),
            jax.ShapeDtypeStruct((rows * PAIRS, 2, LEN), f32),
            jax.ShapeDtypeStruct((D, tokens), b16),
            jax.ShapeDtypeStruct((tokens, D), b16),
        ],
        scratch_shapes=[
            pltpu.SMEM((PIECES,), jnp.int32),
            pltpu.VMEM((rows, LEN, D), b16),
            pltpu.VMEM((tokens, D), b16),
            pltpu.VMEM((tokens, PAIR), b16),
            pltpu.VMEM((PAIR, tokens), b16),
            pltpu.VMEM((2, LEN, LEN // 2), f32),
            pltpu.VMEM((CAP, HALF, D), b16),
        ]
        + [pltpu.VMEM((FLOWS, CAP, NEAR, wide * PAIR), b16) for unused, wide in GROUPS]
        + [pltpu.VMEM((FLOWS, 2 * CAP, KEEP, wide * PAIR), b16) for unused, wide in GROUPS]
        + [
            pltpu.VMEM((PAIRS, D, WIDE), b16),
            pltpu.VMEM((PAIRS, NEAR, WIDE), b16),
            pltpu.VMEM((2, PAIRS, NEAR, WIDE), b16),
            pltpu.VMEM((REST, D, D), b16),
            pltpu.VMEM((REST, NEAR, D), b16),
            pltpu.VMEM((2, REST, NEAR, D), b16),
            dma((CHUNKS, FLOWS, 3)),
            dma((CHUNKS, FLOWS, 3)),
            dma((PAIRS, 8)),
            dma((PAIRS, 8)),
            dma((REST, 8)),
            dma((REST, 8)),
            dma((2,)),
            dma((2,)),
            dma((2,)),
            dma((PAIRS + REST + 2,)),
        ],
        compiler_params=pltpu.CompilerParams(
            collective_id=0, has_side_effects=True, vmem_limit_bytes=60 * MIB
        ),
        name="front",
    )(owner, lengths, master, vectors, inputs, cotangent)


class Sum:
    steps = 7

    def __init__(self, place, work, kept, wide, narrow, land, sems, send_pair, add_own):
        self.place, self.work, self.kept, self.sems = place, work, kept, sems
        self.wide, self.narrow, self.land = wide, narrow, land
        self.send_pair, self.add_own = send_pair, add_own

    def copy(self, flow, index):
        first, second, near, far, keep, give = self.place.flow(flow)
        source, target, device = [
            (self.work.at[:, rows_at(far, NEAR)], self.wide.at[flow], first),
            (self.work.at[:, rows_at(give, KEEP)], self.narrow.at[flow], second),
        ][index]
        number = 3 + 2 * flow + index
        return remote(
            source,
            target,
            self.sems[0].at[number],
            self.sems[1].at[number],
            self.place.partners[device],
        )

    def step(self, index):
        if index == 0:
            self.send_pair().start()
        if index == 1:
            self.send_pair().wait()
            self.add_own()
        for flow in range(FLOWS):
            first, second, near, far, keep, give = self.place.flow(flow)
            if index == 1:
                self.copy(flow, 0).start()
            if index == 2:
                self.copy(flow, 0).wait()
                rows = rows_at(near, NEAR)
                total = self.work[:, rows].astype(f32) + self.wide[flow].astype(f32)
                self.work[:, rows] = total.astype(b16)
                self.copy(flow, 1).start()
            if index == 3:
                self.copy(flow, 1).wait()
                total = self.work[:, rows_at(keep, KEEP)].astype(f32) + self.narrow[flow].astype(f32)
                self.kept[:, both_flows(flow)] = total.astype(b16)
        if index >= 3:
            column_step(self.place, Column(self.place, self.kept, self.land, self.sems), index - 3)


class Gather:
    steps = 3

    def __init__(self, place, work, kept, narrow, wide, sems):
        self.place, self.work, self.kept = place, work, kept
        self.narrow, self.wide, self.sems = narrow, wide, sems

    def copy(self, flow, index):
        first, second, near, far, keep, give = self.place.flow(flow)
        source, target, device = [
            (self.kept.at[:, both_flows(flow)], self.narrow, second),
            (self.work.at[:, rows_at(near, NEAR)], self.wide, first),
        ][index]
        number = 7 + 2 * flow + index
        return remote(
            source,
            target.at[flow],
            self.sems[0].at[number],
            self.sems[1].at[number],
            self.place.partners[device],
        )

    def step(self, index):
        for flow in range(FLOWS):
            first, second, near, far, keep, give = self.place.flow(flow)
            if index == 0:
                self.work[:, rows_at(keep, KEEP)] = self.kept[:, both_flows(flow)]
            if index > 0:
                self.copy(flow, index - 1).wait()
            if index == 1:
                self.work[:, rows_at(give, KEEP)] = self.narrow[flow]
            if index == 2:
                self.work[:, rows_at(far, NEAR)] = self.wide[flow]
            if index < 2:
                self.copy(flow, index).start()


class Hand:
    steps = 3

    def __init__(self, place, table, kept, bag, gift, pack, last, own, out, sems, store_sems):
        self.place, self.table, self.kept = place, table, kept
        self.bag, self.gift, self.pack, self.last, self.own = bag, gift, pack, last, own
        self.out, self.sems, self.store_sems = out, sems, store_sems

    def tile(self, chip, rank, flow):
        return self.kept[self.table[chip * CAP + rank], both_flows(flow)]

    def copy(self, flow, index):
        first, second = self.place.flow(flow)[:2]
        source, target, device = [
            (self.bag.at[flow], self.gift.at[flow], second),
            (self.pack.at[flow], self.last.at[flow], first),
        ][index]
        return remote(
            source,
            target,
            self.sems[0].at[flow, index],
            self.sems[1].at[flow, index],
            self.place.partners[device],
        )

    def stores(self, flow):
        first, second, near, far, keep, give = self.place.flow(flow)
        parts = [
            (self.own.at[flow], rows_at(keep, KEEP)),
            (self.gift.at[flow, pl.ds(0, CAP)], rows_at(give, KEEP)),
            (self.last.at[flow], rows_at(far, NEAR)),
        ]
        return [
            pltpu.make_async_copy(source, self.out.at[:, rows], self.store_sems.at[flow, index])
            for index, (source, rows) in enumerate(parts)
        ]

    def step(self, index):
        for flow in range(FLOWS):
            first, second, near, far, keep, give = self.place.flow(flow)
            if index == 0:
                beside = self.place.chips[second]
                across = beside + self.place.chips[first] - self.place.me
                for rank in range(CAP):
                    self.bag[flow, rank] = self.tile(beside, rank, flow)
                    self.bag[flow, CAP + rank] = self.tile(across, rank, flow)
                    self.own[flow, rank] = self.tile(self.place.me, rank, flow)
                self.copy(flow, 0).start()
            if index == 1:
                self.copy(flow, 0).wait()
                for rank in range(CAP):
                    mine = self.tile(self.place.chips[first], rank, flow)
                    self.pack[flow, rank, rows_at(keep - near, KEEP)] = mine
                    self.pack[flow, rank, rows_at(give - near, KEEP)] = self.gift[flow, CAP + rank]
                self.copy(flow, 1).start()
            if index == 2:
                self.copy(flow, 1).wait()
                for copy in self.stores(flow):
                    copy.start()


BACK_STEPS = 2 * PAIRS
BACK_TAIL = 4
BACK_PAIRS = tuple((index, 1) for index in range(PAIRS))
BACK_REST = (0, 1, 2, 3, 4, 5, 6, 7, 8)
BACK_HAND = 15


def back_kernel(
    table, p_ref, r_ref, v_ref, q_ref, k_ref, o_ref, g_ref, w_ref, n_ref, x_ref, z_ref, vec_ref,
    tiles_in, sums_in, y_in,
    y_out, i_out, pairs_out, slots_out, sums_ref,
    grad_sum, wide_sum, turned, slopes, block_out,
    two, two_kept, two_wide, two_narrow, two_land, two_stage,
    one, one_kept, one_wide, one_narrow, one_land, one_send_stage, one_stage,
    gather_narrow, gather_wide,
    bag, gift, pack, last, own, vec_land,
    two_send, two_recv, one_send, one_recv, hand_send, hand_recv, hand_store,
    pair_two_send, pair_two_recv, pair_one_send, pair_one_recv, load_sem, store_sem,
    swap_send, swap_recv, swap_local, vec_send, vec_recv,
):
    step = pl.program_id(0)
    place = Place()
    rows, span = y_in.shape[0], y_in.shape[1] // 2
    near_half = rows_at(place.core * HALF, HALF)
    far_half = rows_at(place.other * HALF, HALF)

    def load_two(group):
        first, count = REST_GROUPS[group]
        return pltpu.make_async_copy(
            tiles_in.at[pl.ds(first, count), near_half],
            two_stage.at[pl.ds(group % 2, 1)],
            load_sem.at[group % 2],
        )

    def rest_sum(group):
        first, count = REST_GROUPS[group]
        span_of = pl.ds(first, count)
        work = two.at[span_of]

        def send_pair():
            return remote(
                tiles_in.at[span_of, far_half],
                work,
                pair_two_send.at[group],
                pair_two_recv.at[group],
                place.twin,
            )

        def add_own():
            load_two(group).wait()
            work[...] = (work[...].astype(f32) + two_stage[group % 2].astype(f32)).astype(b16)

        sems = (two_send.at[group], two_recv.at[group])
        parts = (two_kept.at[span_of], two_wide.at[:, span_of], two_narrow.at[:, span_of])
        return Sum(place, work, *parts, two_land.at[:, span_of], sems, send_pair, add_own)

    def pair_sum(group):
        first, count = BACK_PAIRS[group]
        span_of = pl.ds(first, count)
        work = one.at[span_of]

        def send_pair():
            return remote(
                one_send_stage.at[pl.ds(group % 2, 1)],
                work,
                pair_one_send.at[group],
                pair_one_recv.at[group],
                place.twin,
            )

        def add_own():
            own = one_stage[group % 2].astype(f32)
            work[...] = (work[...].astype(f32) + own).astype(b16)

        sems = (one_send.at[group], one_recv.at[group])
        parts = (one_kept.at[span_of], one_wide.at[:, span_of], one_narrow.at[:, span_of])
        return Sum(place, work, *parts, one_land.at[:, span_of], sems, send_pair, add_own)

    def pair_gather(group):
        first, count = BACK_PAIRS[group]
        span_of = pl.ds(first, count)
        sems = (one_send.at[group], one_recv.at[group])
        narrow, wide = gather_narrow.at[:, span_of], gather_wide.at[:, span_of]
        return Gather(place, one.at[span_of], one_kept.at[span_of], narrow, wide, sems)

    hand = Hand(
        place, table, two_kept, bag, gift, pack, last, own, slots_out, (hand_send, hand_recv), hand_store
    )

    def pair_store(index, tile):
        return pltpu.make_async_copy(
            one.at[index, :, pl.ds(tile * PAIR, PAIR)],
            pairs_out.at[tile, :, pl.ds(index * PAIR, PAIR)],
            store_sem.at[index, tile],
        )

    def tick(number, odd):
        for group, start in enumerate(BACK_REST):
            if group % 2 == odd and 0 <= number - start < Sum.steps:
                rest_sum(group).step(number - start)
        for group, (first, count) in enumerate(BACK_PAIRS):
            if group % 2 != odd:
                continue
            start = 2 * (first + count)
            if 0 <= number - start < Sum.steps:
                pair_sum(group).step(number - start)
            if 0 <= number - start - Sum.steps + 1 < Gather.steps:
                pair_gather(group).step(number - start - Sum.steps + 1)
            if number == start + Sum.steps + 1:
                for index in range(first, first + count):
                    for tile in range(3):
                        pair_store(index, tile).start()
        if odd == 0 and 0 <= number - BACK_HAND < Hand.steps:
            hand.step(number - BACK_HAND)
        for group, start in enumerate(BACK_REST):
            if odd == 1 and number == max(start - 1, 0):
                load_two(group).start()

    def both(number):
        tick(number, 0)
        tick(number, 1)

    def swap_y(index):
        there = pl.ds(place.core * rows, rows)
        if index == 0:
            return pltpu.make_async_copy(
                y_in.at[:, pl.ds(place.core * span, span)], y_out.at[there], swap_local.at[0]
            )
        return remote(
            y_in.at[:, pl.ds(place.other * span, span)],
            y_out.at[there],
            swap_send.at[0],
            swap_recv.at[0],
            place.twin,
        )

    @pl.when(step == 0)
    def lead():
        place.greet()
        for index in range(2):
            swap_y(index).start()
        sums_ref[...] = sums_in[...]

    for number in range(BACK_STEPS + BACK_TAIL):
        early = partial(tick, number, 0) if number < BACK_STEPS else partial(both, number)
        pl.when(step == number)(early)

    half = LEN // 2
    pair, row = step // 2, lax.rem(step, 2)

    quarter = LEN // 4

    def attention_inputs(head):
        part = slice(head * HEAD_DIM, (head + 1) * HEAD_DIM)
        values = head_only(v_ref[...], head)
        recip = r_ref[0, head : head + 1, :]
        grad = g_ref[part, :].astype(f32) * recip
        delta = jnp.sum(grad * o_ref[part, :].astype(f32), 0, keepdims=True)
        grad = grad.astype(b16)
        return values, grad, delta, jnp.concatenate([grad, grad], axis=0)

    def attention(head):
        part = slice(head * HEAD_DIM, (head + 1) * HEAD_DIM)
        values, grad, delta, doubled = attention_inputs(head)
        units = [(which, block) for which in range(2) for block in range(4)]
        value_grad, key_grad, query_grad = {}, {}, {}

        def raw_block(unit):
            which, block = units[unit]
            cols = slice(which * half, (which + 1) * half)
            return dot_nn(values[block * quarter : (block + 1) * quarter], doubled[:, cols])

        def slope_block(unit, raw):
            which, block = units[unit]
            cols = slice(which * half, (which + 1) * half)
            for small in range(4):
                rows_here = slice(small * 64, (small + 1) * 64)
                rows_all = slice(block * quarter + small * 64, block * quarter + (small + 1) * 64)
                slope = p_ref[head, rows_all, cols].astype(f32) * (raw[rows_here] - delta[:, cols])
                slopes[unit % 2, rows_here] = slope.astype(b16)

        def add(totals, key, term):
            totals[key] = totals[key] + term if key in totals else term

        def grad_block(unit):
            which, block = units[unit]
            cols = slice(which * half, (which + 1) * half)
            rows_all = slice(block * quarter, (block + 1) * quarter)
            slope = slopes[unit % 2]
            add(value_grad, block, dot_nt(grad[:, cols], p_ref[head, rows_all, cols]))
            add(key_grad, block, dot_nt(q_ref[part, cols], slope))
            add(query_grad, which, dot_nn(k_ref[part, rows_all], slope))

        raw = raw_block(0)
        for unit in range(len(units)):
            after = raw_block(unit + 1) if unit + 1 < len(units) else None
            slope_block(unit, raw)
            if unit > 0:
                grad_block(unit - 1)
            raw = after
        grad_block(len(units) - 1)
        for which in range(2):
            total = query_grad[which] * (HEAD_DIM**-0.5)
            turned[part, which * half : (which + 1) * half] = total.astype(b16)
        for block in range(4):
            rows_all = slice(block * quarter, (block + 1) * quarter)
            lower = slice(PAIR + head * HEAD_DIM, PAIR + (head + 1) * HEAD_DIM)
            turned[lower, rows_all] = (key_grad[block] * (1.0 / LOG2E)).astype(b16)
            lower = slice(2 * PAIR + head * HEAD_DIM, 2 * PAIR + (head + 1) * HEAD_DIM)
            turned[lower, rows_all] = value_grad[block].astype(b16)

    @pl.when(step < BACK_STEPS)
    def first_head():
        attention(0)

    for number in range(BACK_STEPS):
        pl.when(step == number)(partial(tick, number, 1))

    @pl.when(step < BACK_STEPS)
    def second_head():
        attention(1)
        where = pl.ds(pl.multiple_of(row * LEN, LEN), LEN)
        block = dot_nn(turned[...], n_ref[where])
        back = turned[...].T
        lanes = pl.ds(pl.multiple_of(pair * PAIR, PAIR), PAIR)
        ones = jnp.sum(back.astype(f32), 0, keepdims=True)
        sums_ref[4:5, lanes] += ones[:, :PAIR]
        sums_ref[5:6, lanes] += ones[:, 2 * PAIR :]
        term = dot_nt(back, w_ref[0])

        @pl.when(pair == 0)
        def begin():
            grad_sum[where] = term

        @pl.when(pair > 0)
        def add():
            grad_sum[where] += term

        @pl.when(row == 0)
        def keep():
            wide_sum[...] = block

        @pl.when(row == 1)
        def hand_on():
            whole = (wide_sum[...] + block).T
            low = whole.astype(b16)
            for core in range(2):

                @pl.when(place.core == core)
                def split():
                    slot = lax.rem(pair, 2)
                    one_stage[slot] = low[core * HALF : (core + 1) * HALF]
                    one_send_stage[slot] = low[(1 - core) * HALF : (2 - core) * HALF]

    def store_block(index):
        row, half = index // 2, index % 2
        target = i_out.at[place.core * rows + row]
        local = pltpu.make_async_copy(block_out.at[half], target, swap_local.at[1 + row])
        far = remote(
            block_out.at[half], target, swap_send.at[1 + row], swap_recv.at[1 + row], place.twin
        )
        return local, far, half

    def wait_block(index):
        local, far, half = store_block(index)

        @pl.when(place.core == half)
        def keep():
            local.wait()

        @pl.when(place.core != half)
        def give():
            far.wait()

    for index in range(BACK_TAIL):

        @pl.when(step == BACK_STEPS + index)
        def close():
            size = LEN // 2
            if index >= 2:
                wait_block(index - 2)
            gain_sum = jnp.zeros((8, D), f32)
            shift_sum = jnp.zeros((8, D), f32)
            for block in range(size // 16):
                rows_here = slice(block * 16, (block + 1) * 16)
                grad = grad_sum[index * size + block * 16 : index * size + (block + 1) * 16]
                unit, rstd = norm_parts(x_ref[rows_here].astype(f32))
                gain_sum = gain_sum + jnp.sum((grad * unit).reshape(-1, 8, D), axis=0)
                shift_sum = shift_sum + jnp.sum(grad.reshape(-1, 8, D), axis=0)
                total = norm_back(grad, unit, rstd, vec_ref[0:1, :])
                block_out[index % 2, rows_here] = (z_ref[rows_here].astype(f32) + total).astype(b16)
            sums_ref[0:1, :] += jnp.sum(gain_sum, 0, keepdims=True)
            sums_ref[1:2, :] += jnp.sum(shift_sum, 0, keepdims=True)
            local, far, half = store_block(index)

            @pl.when(place.core == half)
            def keep():
                local.start()

            @pl.when(place.core != half)
            def give():
                far.start()

    @pl.when(step == BACK_STEPS + BACK_TAIL - 1)
    def drain():
        devices = [place.twin] + place.partners

        def vector(index):
            return remote(
                sums_ref, vec_land.at[index], vec_send.at[index], vec_recv.at[index], devices[index]
            )

        vector(0).start()
        for number in range(BACK_STEPS + BACK_TAIL, BACK_STEPS + Sum.steps + Gather.steps):
            both(number)
            index = number - BACK_STEPS - BACK_TAIL
            if index < 5:
                vector(index).wait()
                sums_ref[...] += vec_land[index]
                if index < 4:
                    vector(index + 1).start()
        for index in range(2):
            swap_y(index).wait()
        for index in range(2, BACK_TAIL):
            wait_block(index)
        for index in range(PAIRS):
            for tile in range(3):
                pair_store(index, tile).wait()
        for flow in range(FLOWS):
            for copy in hand.stores(flow):
                copy.wait()


def back(table, attention, weights, normed, x, residual, vectors, tiles, sums, y):
    rows, length = y.shape[:2]
    tokens = rows * length
    any_spec = pl.BlockSpec(memory_space=pl.ANY)
    smem = pl.BlockSpec(memory_space=pltpu.SMEM)
    dma = pltpu.SemaphoreType.DMA

    def now(step):
        return jnp.minimum(step, BACK_STEPS - 1)

    def tail(step):
        return jnp.maximum(step - BACK_STEPS, 0)

    head_block = pl.BlockSpec((PAIR, LEN), lambda s: (now(s) // 2, lax.rem(now(s), 2)))
    tail_block = pl.BlockSpec((LEN // 2, D), lambda s: (tail(s), 0))
    whole = pl.BlockSpec((PIECES, D), lambda s: (0, 0))
    sums_block = pl.BlockSpec((16, D), lambda s: (0, 0))
    return pl.pallas_call(
        back_kernel,
        grid=(BACK_STEPS + BACK_TAIL,),
        in_specs=[
            smem,
            pl.BlockSpec((2, LEN, LEN), lambda s: (now(s), 0, 0)),
            pl.BlockSpec((1, 2, LEN), lambda s: (now(s), 0, 0)),
            pl.BlockSpec((LEN, PAIR), lambda s: (lax.rem(now(s), 2), now(s) // 2)),
            head_block,
            head_block,
            head_block,
            head_block,
            pl.BlockSpec((1, D, WIDE), lambda s: (now(s) // 2, 0, 0)),
            pl.BlockSpec((tokens, D), lambda s: (0, 0), pipeline_mode=pl.Buffered(1)),
            tail_block,
            tail_block,
            whole,
            any_spec,
            sums_block,
            any_spec,
        ],
        out_specs=[any_spec] * 4 + [sums_block],
        out_shape=[
            jax.ShapeDtypeStruct((2 * rows, length // 2, D), b16),
            jax.ShapeDtypeStruct((2 * rows, length // 2, D), b16),
            jax.ShapeDtypeStruct((3, HALF, D), b16),
            jax.ShapeDtypeStruct((CAP, HALF, D), b16),
            jax.ShapeDtypeStruct((16, D), f32),
        ],
        scratch_shapes=[
            pltpu.VMEM((tokens, D), f32),
            pltpu.VMEM((WIDE, D), f32),
            pltpu.VMEM((WIDE, LEN), b16),
            pltpu.VMEM((2, LEN // 4, LEN // 2), b16),
            pltpu.VMEM((2, LEN // 2, D), b16),
            pltpu.VMEM((REST, HALF, D), b16),
            pltpu.VMEM((REST, NEAR, D), b16),
            pltpu.VMEM((FLOWS, REST, NEAR, D), b16),
            pltpu.VMEM((FLOWS, REST, KEEP, D), b16),
            pltpu.VMEM((2, REST, NEAR, D), b16),
            pltpu.VMEM((2, HALF, D), b16),
            pltpu.VMEM((PAIRS, HALF, WIDE), b16),
            pltpu.VMEM((PAIRS, NEAR, WIDE), b16),
            pltpu.VMEM((FLOWS, PAIRS, NEAR, WIDE), b16),
            pltpu.VMEM((FLOWS, PAIRS, KEEP, WIDE), b16),
            pltpu.VMEM((2, PAIRS, NEAR, WIDE), b16),
            pltpu.VMEM((2, HALF, WIDE), b16),
            pltpu.VMEM((2, HALF, WIDE), b16),
            pltpu.VMEM((FLOWS, PAIRS, KEEP, WIDE), b16),
            pltpu.VMEM((FLOWS, PAIRS, NEAR, WIDE), b16),
            pltpu.VMEM((FLOWS, 2 * CAP, KEEP, D), b16),
            pltpu.VMEM((FLOWS, 2 * CAP, KEEP, D), b16),
            pltpu.VMEM((FLOWS, CAP, NEAR, D), b16),
            pltpu.VMEM((FLOWS, CAP, NEAR, D), b16),
            pltpu.VMEM((FLOWS, CAP, KEEP, D), b16),
            pltpu.VMEM((5, 16, D), f32),
            dma((REST, 7)),
            dma((REST, 7)),
            dma((PAIRS, 11)),
            dma((PAIRS, 11)),
            dma((FLOWS, 2)),
            dma((FLOWS, 2)),
            dma((FLOWS, 3)),
            dma((REST,)),
            dma((REST,)),
            dma((PAIRS,)),
            dma((PAIRS,)),
            dma((3,)),
            dma((PAIRS, 3)),
            dma((3,)),
            dma((3,)),
            dma((3,)),
            dma((5,)),
            dma((5,)),
        ],
        compiler_params=pltpu.CompilerParams(
            collective_id=1, has_side_effects=True, vmem_limit_bytes=62 * MIB
        ),
        name="back",
    )(table, *attention, weights, normed, x, residual, vectors, tiles, sums, y)


def update_kernel(tile_at, one, two, w_ref, m_ref, s_ref, y_in, i_in, w_out, m_out, s_out, y_out, i_out):
    step = pl.program_id(0)
    tile = tile_at[step // 2]
    grad = jnp.where(tile < 3, one[0], two[0]).astype(f32)
    parts = adam_step(w_ref[0], grad, m_ref[0], s_ref[0], RATE)
    for target, part in zip((w_out, m_out, s_out), parts):
        target[0] = jnp.where(tile >= 0, part, jnp.zeros_like(part))

    @pl.when(step < 4)
    def widen():
        y_out[...] = y_in[...].astype(f32)
        i_out[...] = i_in[...].astype(f32)


def update(tile_at, one, two, master, first, second, y, grad):
    tokens = y.shape[0]
    size = HALF // 2
    state = pl.BlockSpec((1, size, D), lambda s, tile_at: (s // 2, lax.rem(s, 2), 0))
    wide = pl.BlockSpec((tokens // 4, D), lambda s, tile_at: (jnp.minimum(s, 3), 0))
    return pl.pallas_call(
        update_kernel,
        grid_spec=pltpu.PrefetchScalarGridSpec(
            num_scalar_prefetch=1,
            grid=(CAP * 2,),
            in_specs=[
                pl.BlockSpec(
                    (1, size, D),
                    lambda s, tile_at: (jnp.clip(tile_at[s // 2], 0, 2), lax.rem(s, 2), 0),
                ),
                state,
                state,
                state,
                state,
                wide,
                wide,
            ],
            out_specs=[state] * 3 + [wide] * 2,
        ),
        out_shape=[jax.ShapeDtypeStruct(master.shape, f32)] * 3
        + [jax.ShapeDtypeStruct((tokens, D), f32)] * 2,
        compiler_params=pltpu.CompilerParams(vmem_limit_bytes=60 * MIB),
        name="update",
    )(tile_at, one, two, master, first, second, y, grad)


def shards_paired(
    inputs,
    cotangent,
    doc_lengths,
    owner_list,
    master,
    first_moment,
    second_moment,
    vectors,
    vector_first,
    vector_second,
):
    rows_here, span, width = inputs.shape
    place = lax.axis_index("blk")
    member = lax.axis_index("dp")
    rows_mine = rows_here // 2
    order = jnp.arange(PIECES)
    same_owner = owner_list[:, None] == owner_list[None, :]
    ranks = jnp.sum(same_owner & (order[None, :] < order[:, None]), axis=1).astype(jnp.int32)
    slot_of = owner_list * CAP + ranks
    front_outs = front(owner_list, doc_lengths, master, vectors, inputs, cotangent)
    x, cot, normed, weights_one, weights_two, queries, keys, values = front_outs[:8]
    weights, recips, context_turned, context = front_outs[8:]
    x = x.reshape(-1, width)
    cot = cot.reshape(-1, width)
    block_out, residual, grad_context, sums, tiles_two = feed(
        context, context_turned, x, cot, weights_two, vectors
    )
    hits = jnp.arange(16 * CAP)[:, None] == slot_of[None, :]
    tile_at = jnp.sum(jnp.where(hits, order[None, :] + 1, 0), axis=1).astype(jnp.int32) - 1
    table = jnp.maximum(tile_at - 3, 0)
    block_out, input_grad, total_one, total_two, vector_total = back(
        table,
        (weights, recips, values, queries, keys, context_turned, grad_context),
        weights_one,
        normed,
        x,
        residual,
        vectors,
        tiles_two,
        sums,
        block_out.reshape(rows_mine, LEN, width),
    )
    mine = lax.dynamic_slice_in_dim(tile_at, member * CAP, CAP, 0)
    *updated, block_out, input_grad = update(
        mine,
        total_one,
        total_two,
        master,
        first_moment,
        second_moment,
        block_out.reshape(-1, width),
        input_grad.reshape(-1, width),
    )
    columns = vector_first.shape[1]
    vector_cols = lax.dynamic_slice_in_dim(vectors, place * columns, columns, 1)
    vector_total = lax.dynamic_slice(vector_total, (0, place * columns), (PIECES, columns))
    updated_vectors = adam_step(vector_cols, vector_total, vector_first, vector_second, VEC_RATE)
    return (
        block_out.reshape(inputs.shape),
        input_grad.reshape(inputs.shape),
        *updated,
        *updated_vectors,
    )


def solution(mesh):
    in_specs = (
        P("dp", "blk", None),
        P("dp", "blk", None),
        P("dp", None),
        P(),
        P("dp", "blk", None),
        P("dp", "blk", None),
        P("dp", "blk", None),
        P(),
        P(None, "blk"),
        P(None, "blk"),
    )
    out_specs = (
        P("dp", "blk", None),
        P("dp", "blk", None),
        P("dp", "blk", None),
        P("dp", "blk", None),
        P("dp", "blk", None),
        P(None, "blk"),
        P(None, "blk"),
        P(None, "blk"),
    )
    paired = mesh.shape["blk"] == 2 and mesh.shape["dp"] == 16
    shards = shards_paired if paired else shards_any
    return jax.shard_map(shards, mesh=mesh, in_specs=in_specs, out_specs=out_specs, check_vma=False)
```

```python
from functools import partial

import jax
import jax.numpy as jnp
from jax import lax
from jax.experimental import pallas as pl
from jax.experimental.pallas import tpu as pltpu
from jax.sharding import PartitionSpec as P

D = 768
FF = 3072
HEADS = 12
HEAD_DIM = 64
LEN = 1024
CAP = 3
STEP = 10
PIECES = 12


EPS_NORM = 1e-05
BETA_ONE = 0.9
BETA_TWO = 0.999
RATE = 0.04
VEC_RATE = 0.25
DECAY = 0.01
ADAM_EPS = 1e-08


def normalize(values_in, gain, shift):
    center = jnp.mean(values_in, axis=-1, keepdims=True)
    offset = values_in - center
    spread = jnp.mean(offset * offset, axis=-1, keepdims=True)
    return offset * lax.rsqrt(spread + EPS_NORM) * gain + shift


def adam_step(weight, grad, first, second, rate):
    first_new = BETA_ONE * first + (1.0 - BETA_ONE) * grad
    second_new = BETA_TWO * second + (1.0 - BETA_TWO) * grad * grad
    corrected = (
        first_new
        / (1.0 - BETA_ONE**STEP)
        / (jnp.sqrt(second_new / (1.0 - BETA_TWO**STEP)) + ADAM_EPS)
    )
    return (weight - rate * (corrected + DECAY * weight), first_new, second_new)


def shards_any(
    inputs,
    cotangent,
    doc_lengths,
    owner_list,
    master,
    first_moment,
    second_moment,
    vectors,
    vector_first,
    vector_second,
):
    rows_here, span, width = inputs.shape
    tokens_here = rows_here * span
    fold = FF // D
    scale = HEAD_DIM ** (-0.5)
    place = lax.axis_index("blk")
    f32 = jnp.float32
    b16 = jnp.bfloat16
    order = jnp.arange(PIECES)
    same_owner = owner_list[:, None] == owner_list[None, :]
    ranks = jnp.sum(same_owner & (order[None, :] < order[:, None]), axis=1)
    slot_of = owner_list * CAP + ranks

    mine = (owner_list == lax.axis_index("dp"))[:, None, None]
    tile_rows = lax.psum(jnp.where(mine, master[ranks], 0.0).astype(b16), "dp")
    tiles = lax.all_gather(tile_rows, "blk", axis=1, tiled=True)
    query_weight = tiles[0]
    key_weight = tiles[1]
    value_weight = tiles[2]
    out_weight = tiles[3]
    up_weight = jnp.transpose(tiles[4 : 4 + fold], (1, 0, 2)).reshape(width, FF)
    down_weight = tiles[4 + fold :].reshape(FF, width)
    flat_in = inputs.reshape(tokens_here, width).astype(f32)
    normed_one = normalize(flat_in, vectors[0], vectors[1]).astype(b16)
    queries = (jnp.dot(normed_one, query_weight, preferred_element_type=f32) + vectors[4]).astype(
        b16
    )
    keys_here = jnp.dot(normed_one, key_weight, preferred_element_type=f32).astype(b16)
    values_here = (
        jnp.dot(normed_one, value_weight, preferred_element_type=f32) + vectors[5]
    ).astype(b16)
    query_heads = queries.reshape(rows_here, span, HEADS, HEAD_DIM)
    first_len = doc_lengths[:, 0]
    query_seg = (place * span + jnp.arange(span))[None, :] >= first_len[:, None]

    def block_scores(key_block, start):
        count = key_block.shape[1]
        key_heads = key_block.reshape(rows_here, count, HEADS, HEAD_DIM)
        raw = (
            jnp.einsum("rqhd,rkhd->rhqk", query_heads, key_heads, preferred_element_type=f32)
            * scale
        )
        key_seg = (start + jnp.arange(count))[None, :] >= first_len[:, None]
        allowed = query_seg[:, None, :, None] == key_seg[:, None, None, :]
        return (raw, allowed)

    key_rows = keys_here.reshape(rows_here, span, width)
    value_rows = values_here.reshape(rows_here, span, width)
    top = jnp.full((rows_here, HEADS, span), -1e30, f32)
    key_block = lax.all_gather(key_rows, "blk", axis=1, tiled=True)
    value_block = lax.all_gather(value_rows, "blk", axis=1, tiled=True)
    count = key_block.shape[1]
    raw, allowed = block_scores(key_block, jnp.int32(0))
    new_top = jnp.maximum(top, jnp.max(jnp.where(allowed, raw, -1e30), axis=-1))
    weights = jnp.where(allowed, jnp.exp(raw - new_top[..., None]), 0.0)
    value_heads = value_block.reshape(rows_here, count, HEADS, HEAD_DIM)
    update = jnp.einsum(
        "rhqk,rkhd->rhqd", weights.astype(b16), value_heads, preferred_element_type=f32
    )
    total = jnp.sum(weights, axis=-1)
    log_total = new_top + jnp.log(total)
    context_raw = update / total[..., None]
    context_low = jnp.transpose(context_raw, (0, 2, 1, 3)).reshape(tokens_here, width).astype(b16)
    residual = flat_in + (jnp.dot(context_low, out_weight, preferred_element_type=f32) + vectors[6])
    normed_two = normalize(residual, vectors[2], vectors[3]).astype(b16)
    hidden = jnp.dot(normed_two, up_weight, preferred_element_type=f32) + vectors[8:].reshape(FF)
    gelu_exact = partial(jax.nn.gelu, approximate=False)
    active, gelu_pull = jax.vjp(gelu_exact, hidden)
    active_low = active.astype(b16)
    block_out = (
        residual + (jnp.dot(active_low, down_weight, preferred_element_type=f32) + vectors[7])
    ).reshape(rows_here, span, width)
    grad_out = cotangent.reshape(tokens_here, width)
    down_grad = jnp.einsum("tf,td->fd", active_low, grad_out, preferred_element_type=f32)
    down_sum = jnp.sum(grad_out, axis=0, dtype=f32)
    grad_active = jnp.einsum("td,fd->tf", grad_out, down_weight, preferred_element_type=f32)
    grad_hidden = gelu_pull(grad_active)[0].astype(b16)
    up_grad = jnp.einsum("td,tf->df", normed_two, grad_hidden, preferred_element_type=f32)
    up_sum = jnp.sum(grad_hidden, axis=0, dtype=f32)
    ffn_tiles = jnp.concatenate(
        [
            jnp.transpose(up_grad.reshape(width, fold, width), (1, 0, 2)),
            down_grad.reshape(fold, width, width),
        ],
        axis=0,
    )
    grad_normed_two = jnp.einsum("tf,df->td", grad_hidden, up_weight, preferred_element_type=f32)
    unused, second_pull = jax.vjp(normalize, residual, vectors[2], vectors[3])
    residual_part, gain_two_grad, shift_two_grad = second_pull(grad_normed_two)
    grad_residual = grad_out.astype(f32) + residual_part
    grad_attended = grad_residual.astype(b16)
    out_grad = jnp.einsum("tm,td->md", context_low, grad_attended, preferred_element_type=f32)
    out_sum = jnp.sum(grad_attended, axis=0, dtype=f32)
    grad_context = jnp.einsum(
        "td,md->tm", grad_attended, out_weight, preferred_element_type=f32
    ).astype(b16)
    grad_heads = grad_context.reshape(rows_here, span, HEADS, HEAD_DIM)
    delta = jnp.einsum("rqhd,rhqd->rhq", grad_heads.astype(f32), context_raw)
    key_all, value_all = (
        lax.all_gather(key_rows, "blk", axis=1, tiled=True),
        lax.all_gather(value_rows, "blk", axis=1, tiled=True),
    )
    key_size = min(512, LEN)

    def back_block(index, carry):
        grad_query, key_total, value_total = carry
        start = index * key_size
        key_block = lax.dynamic_slice_in_dim(key_all, start, key_size, 1)
        value_block = lax.dynamic_slice_in_dim(value_all, start, key_size, 1)
        raw, allowed = block_scores(key_block, start)
        weights_back = jnp.where(allowed, jnp.exp(raw - log_total[..., None]), 0.0)
        key_heads = key_block.reshape(rows_here, key_size, HEADS, HEAD_DIM)
        value_heads = value_block.reshape(rows_here, key_size, HEADS, HEAD_DIM)
        value_grad = jnp.einsum(
            "rhqk,rqhd->rkhd", weights_back.astype(b16), grad_heads, preferred_element_type=f32
        )
        weight_grad = jnp.einsum(
            "rqhd,rkhd->rhqk", grad_heads, value_heads, preferred_element_type=f32
        )
        score_grad = (weights_back * (weight_grad - delta[..., None])).astype(b16)
        grad_query = (
            grad_query
            + jnp.einsum("rhqk,rkhd->rqhd", score_grad, key_heads, preferred_element_type=f32)
            * scale
        )
        key_grad = (
            jnp.einsum("rhqk,rqhd->rkhd", score_grad, query_heads, preferred_element_type=f32)
            * scale
        )
        key_total = lax.dynamic_update_slice_in_dim(
            key_total, key_grad.reshape(rows_here, key_size, width), start, 1
        )
        value_total = lax.dynamic_update_slice_in_dim(
            value_total, value_grad.reshape(rows_here, key_size, width), start, 1
        )
        return (grad_query, key_total, value_total)

    zero_rows = jnp.zeros((rows_here, LEN, width), f32)
    grad_query, key_total, value_total = lax.fori_loop(
        0,
        LEN // key_size,
        back_block,
        (jnp.zeros((rows_here, span, HEADS, HEAD_DIM), f32), zero_rows, zero_rows),
    )
    key_grad_here, value_grad_here = (
        lax.psum_scatter(
            key_total.astype(jnp.bfloat16), "blk", scatter_dimension=1, tiled=True
        ).astype(jnp.float32),
        lax.psum_scatter(
            value_total.astype(jnp.bfloat16), "blk", scatter_dimension=1, tiled=True
        ).astype(jnp.float32),
    )
    query_low = grad_query.reshape(tokens_here, width).astype(b16)
    key_low = key_grad_here.reshape(tokens_here, width).astype(b16)
    value_low = value_grad_here.reshape(tokens_here, width).astype(b16)
    query_tile = jnp.einsum("td,te->de", normed_one, query_low, preferred_element_type=f32)
    key_tile = jnp.einsum("td,te->de", normed_one, key_low, preferred_element_type=f32)
    value_tile = jnp.einsum("td,te->de", normed_one, value_low, preferred_element_type=f32)
    grad_normed_one = (
        jnp.einsum("te,de->td", query_low, query_weight, preferred_element_type=f32)
        + jnp.einsum("te,de->td", key_low, key_weight, preferred_element_type=f32)
        + jnp.einsum("te,de->td", value_low, value_weight, preferred_element_type=f32)
    )
    unused, first_pull = jax.vjp(normalize, flat_in, vectors[0], vectors[1])
    input_part, gain_one_grad, shift_one_grad = first_pull(grad_normed_one)
    input_grad = (grad_residual + input_part).reshape(rows_here, span, width)
    vector_grads = jnp.concatenate(
        [
            jnp.stack(
                [
                    gain_one_grad,
                    shift_one_grad,
                    gain_two_grad,
                    shift_two_grad,
                    jnp.sum(query_low, axis=0, dtype=f32),
                    jnp.sum(value_low, axis=0, dtype=f32),
                    out_sum,
                    down_sum,
                ]
            ),
            up_sum.reshape(fold, width),
        ],
        axis=0,
    )
    attn_tiles = jnp.stack([query_tile, key_tile, value_tile, out_grad])
    piece_share, vector_share = (
        lax.psum_scatter(
            jnp.concatenate([attn_tiles, ffn_tiles], axis=0).astype(jnp.bfloat16),
            "blk",
            scatter_dimension=1,
            tiled=True,
        ).astype(jnp.float32),
        lax.psum_scatter(
            vector_grads.astype(jnp.bfloat16), "blk", scatter_dimension=1, tiled=True
        ).astype(jnp.float32),
    )
    own_slots = lax.axis_index("dp") * CAP + jnp.arange(CAP)
    pick = (own_slots[:, None] == slot_of[None, :]).astype(f32)
    occupied = jnp.sum(pick, axis=1)[:, None, None]
    total_share, vector_total = (
        lax.psum(piece_share.astype(jnp.bfloat16), "dp").astype(jnp.float32),
        lax.psum(vector_share.astype(jnp.bfloat16), "dp").astype(jnp.float32),
    )
    slot_grads = jnp.einsum("cp,prd->crd", pick, total_share, precision=lax.Precision.HIGHEST)
    new_master, new_first, new_second = adam_step(
        master, slot_grads, first_moment, second_moment, RATE
    )
    columns = vector_first.shape[1]
    vector_cols = lax.dynamic_slice_in_dim(vectors, place * columns, columns, 1)
    new_vectors, new_vector_first, new_vector_second = adam_step(
        vector_cols, vector_total, vector_first, vector_second, VEC_RATE
    )
    return (
        block_out,
        input_grad,
        new_master * occupied,
        new_first * occupied,
        new_second * occupied,
        new_vectors,
        new_vector_first,
        new_vector_second,
    )


f32 = jnp.float32
b16 = jnp.bfloat16
LOG2E = 1.4426950408889634
MIB = 1024 * 1024
PAIRS = HEADS // 2
PAIR = 2 * HEAD_DIM


def dot_nn(left, right):
    return lax.dot_general(left, right, (((1,), (0,)), ((), ())), preferred_element_type=f32)


def dot_nt(left, right):
    return lax.dot_general(left, right, (((1,), (1,)), ((), ())), preferred_element_type=f32)


def dot_tn(left, right):
    return lax.dot_general(left, right, (((0,), (0,)), ((), ())), preferred_element_type=f32)


def norm_parts(values_in):
    center = jnp.mean(values_in, axis=-1, keepdims=True)
    offset = values_in - center
    spread = jnp.mean(offset * offset, axis=-1, keepdims=True)
    rstd = lax.rsqrt(spread + EPS_NORM)
    return offset * rstd, rstd


def norm_back(grad, unit, rstd, gain):
    scaled = grad * gain
    first = jnp.mean(scaled, axis=-1, keepdims=True)
    second = jnp.mean(scaled * unit, axis=-1, keepdims=True)
    return rstd * (scaled - first - unit * second)


def gelu_parts(value):
    bell = jnp.exp2(value * value * (-0.5 * LOG2E))
    ratio = pl.reciprocal(1.0 + (0.3275911 * 0.7071067811865476) * jnp.abs(value))
    poly = 0.5 * 1.061405429
    poly = poly * ratio + 0.5 * -1.453152027
    poly = poly * ratio + 0.5 * 1.421413741
    poly = poly * ratio + 0.5 * -0.284496736
    poly = poly * ratio + 0.5 * 0.254829592
    tail = poly * ratio * bell
    cdf = jnp.where(value >= 0.0, 1.0 - tail, tail)
    return value * cdf, cdf + value * (bell * 0.3989422804014327)


def head_only(block, head):
    lane = lax.broadcasted_iota(jnp.int32, block.shape, 1)
    keep = (lane >= head * HEAD_DIM) & (lane < (head + 1) * HEAD_DIM)
    return jnp.where(keep, block, jnp.zeros_like(block))


FEED_SIZE = 256
FEED_WIDE = FF // 2


def feed_kernel(
    c_ref, o_ref, x_ref, g_ref, mix_ref, up_ref, down_ref, vec_ref,
    y_ref, r_ref, d_ref, sums_ref, up_sums_ref, tiles_ref,
    mix_acc, up_acc, down_acc, stage_ref, sem_ref,
):
    fold = FF // D
    step = pl.program_id(0)

    @pl.when(step == 0)
    def clear():
        mix_acc[...] = jnp.zeros_like(mix_acc)
        up_acc[...] = jnp.zeros_like(up_acc)
        down_acc[...] = jnp.zeros_like(down_acc)
        sums_ref[...] = jnp.zeros_like(sums_ref)
        up_sums_ref[...] = jnp.zeros_like(up_sums_ref)

    residual = x_ref[...].astype(f32) + (dot_nn(c_ref[...], mix_ref[...]) + vec_ref[6:7, :])
    unit, rstd = norm_parts(residual)
    gain = vec_ref[2:3, :]
    normed = (unit * gain + vec_ref[3:4, :]).astype(b16)
    turned = normed.T
    cot = g_ref[...]
    out = residual + vec_ref[7:8, :]
    grad = jnp.zeros_like(out)
    for start in range(0, FF, FEED_WIDE):
        part = slice(start, start + FEED_WIDE)
        rows = range(8 + start // D, 8 + (start + FEED_WIDE) // D)
        bias = jnp.concatenate([vec_ref[row : row + 1, :] for row in rows], axis=1)
        hidden = dot_nn(normed, up_ref[:, part]) + bias
        pulled = dot_nt(cot, down_ref[part, :])
        active, slope = gelu_parts(hidden)
        active = active.astype(b16)
        pulled = (pulled * slope).astype(b16)
        out = out + dot_nn(active, down_ref[part, :])
        grad = grad + dot_nt(pulled, up_ref[:, part])
        up_acc[:, part] += dot_nn(turned, pulled)
        down_acc[part, :] += dot_tn(active, cot)
        up_sums_ref[:, part] += jnp.sum(pulled.astype(f32), 0, keepdims=True)
    y_ref[...] = out.astype(b16)
    wide = cot.astype(f32)
    sums_ref[2:3, :] += jnp.sum(grad * unit, 0, keepdims=True)
    sums_ref[3:4, :] += jnp.sum(grad, 0, keepdims=True)
    sums_ref[7:8, :] += jnp.sum(wide, 0, keepdims=True)
    back = wide + norm_back(grad, unit, rstd, gain)
    low = back.astype(b16)
    r_ref[...] = low
    sums_ref[6:7, :] += jnp.sum(low.astype(f32), 0, keepdims=True)
    d_ref[...] = dot_nt(mix_ref[...], low).astype(b16)
    mix_acc[...] += dot_nn(o_ref[...], low)

    @pl.when(step == pl.num_programs(0) - 1)
    def send():
        for part in range(fold):
            sums_ref[8 + part : 9 + part, :] = up_sums_ref[:, part * D : (part + 1) * D]
        tiles = [mix_acc.at[...]]
        tiles += [up_acc.at[:, pl.ds(part * D, D)] for part in range(fold)]
        tiles += [down_acc.at[pl.ds(part * D, D)] for part in range(fold)]
        copies = []
        for part, tile in enumerate(tiles):
            if part >= 2:
                copies[part - 2].wait()
            stage_ref[part % 2] = tile[...].astype(b16)
            copy = pltpu.make_async_copy(
                stage_ref.at[part % 2], tiles_ref.at[part], sem_ref.at[part % 2]
            )
            copy.start()
            copies.append(copy)
        copies[-2].wait()
        copies[-1].wait()


def feed(context, turned, x, cot, mix, up, down, vectors):
    tokens = x.shape[0]
    size = FEED_SIZE
    count = 1 + 2 * (FF // D)
    token_block = pl.BlockSpec((size, D), lambda i: (i, 0))
    turned_block = pl.BlockSpec((D, size), lambda i: (0, i))

    def once(array):
        return pl.BlockSpec(array.shape, lambda i: (0, 0), pipeline_mode=pl.Buffered(1))

    return pl.pallas_call(
        feed_kernel,
        grid=(tokens // size,),
        in_specs=[
            token_block,
            turned_block,
            token_block,
            token_block,
            once(mix),
            once(up),
            once(down),
            pl.BlockSpec((PIECES, D), lambda i: (0, 0)),
        ],
        out_specs=[
            token_block,
            token_block,
            turned_block,
            pl.BlockSpec((16, D), lambda i: (0, 0)),
            pl.BlockSpec((1, FF), lambda i: (0, 0)),
            pl.BlockSpec(memory_space=pl.ANY),
        ],
        out_shape=[
            jax.ShapeDtypeStruct((tokens, D), b16),
            jax.ShapeDtypeStruct((tokens, D), b16),
            jax.ShapeDtypeStruct((D, tokens), b16),
            jax.ShapeDtypeStruct((16, D), f32),
            jax.ShapeDtypeStruct((1, FF), f32),
            jax.ShapeDtypeStruct((count, D, D), b16),
        ],
        scratch_shapes=[
            pltpu.VMEM((D, D), f32),
            pltpu.VMEM((D, FF), f32),
            pltpu.VMEM((FF, D), f32),
            pltpu.VMEM((2, D, D), b16),
            pltpu.SemaphoreType.DMA((2,)),
        ],
        compiler_params=pltpu.CompilerParams(vmem_limit_bytes=60 * MIB),
        cost_estimate=pl.CostEstimate(
            flops=6 * count * tokens * D * D,
            bytes_accessed=18 * tokens * D + 4 * count * D * D,
            transcendentals=2 * tokens * FF,
        ),
        name="feed",
    )(context, turned, x, cot, mix, up, down, vectors)


MESH = pl.DeviceIdType.MESH
HALF = D // 2
FLOWS = 2
FLOW = HALF // FLOWS
NEAR = FLOW // 2
KEEP = NEAR // 2
WIDE = 3 * PAIR
REST = PIECES - 3
GROUPS = ((0, 1), (1, 2), (3, 3))
CHUNKS = len(GROUPS)


class Place:
    def __init__(self):
        self.me = lax.axis_index("dp")
        self.core = lax.axis_index("blk")
        self.bits = [lax.rem(self.me // weight, 2) for weight in (1, 2, 4, 8)]
        self.chips = [
            self.me + weight - 2 * weight * bit for weight, bit in zip((1, 2, 4, 8), self.bits)
        ]
        self.partners = [{"dp": chip} for chip in self.chips]
        low, high = self.bits[2:]
        self.inner = low != high
        self.across = {"dp": self.me + 4 - 8 * low + 8 - 16 * high}
        self.other = 1 - self.core
        self.twin = {"blk": self.other}

    def greet(self):
        barrier = pltpu.get_barrier_semaphore()
        for device in self.partners + [self.across, self.twin]:
            pl.semaphore_signal(barrier, 1, device_id=device, device_id_type=MESH)
        pl.semaphore_wait(barrier, 6)

    def flow(self, index):
        first, second = (0, 1) if index == 0 else (1, 0)
        base = index * FLOW
        near = base + self.bits[first] * NEAR
        far = base + NEAR - self.bits[first] * NEAR
        keep = near + self.bits[second] * KEEP
        give = near + KEEP - self.bits[second] * KEEP
        return first, second, near, far, keep, give


def remote(source, target, send, receive, device):
    return pltpu.make_async_remote_copy(
        src_ref=source,
        dst_ref=target,
        send_sem=send,
        recv_sem=receive,
        device_id=device,
        device_id_type=MESH,
    )


def rows_at(start, count):
    return pl.ds(pl.multiple_of(start, 16), count)


class Spread:
    def __init__(self, place, owner, rank, slots, land, gift, sems):
        self.place, self.owner, self.rank = place, owner, rank
        self.slots, self.land, self.gift, self.sems = slots, land, gift, sems

    def cols(self, chunk):
        return pl.ds(GROUPS[chunk][0] * PAIR, GROUPS[chunk][1] * PAIR)

    def first_copy(self, chunk, index):
        first, second, near, far, keep, give = self.place.flow(index)
        return remote(
            self.slots.at[:, rows_at(far, NEAR), self.cols(chunk)],
            self.land[chunk].at[index],
            self.sems[0].at[chunk, index, 0],
            self.sems[1].at[chunk, index, 0],
            self.place.partners[first],
        )

    def second_copy(self, chunk, index, which):
        first, second, near, far, keep, give = self.place.flow(index)
        if which == 0:
            source = self.slots.at[:, rows_at(give, KEEP), self.cols(chunk)]
        else:
            source = self.land[chunk].at[index, :, rows_at(give - near, KEEP)]
        return remote(
            source,
            self.gift[chunk].at[index, pl.ds(which * CAP, CAP)],
            self.sems[0].at[chunk, index, 1 + which],
            self.sems[1].at[chunk, index, 1 + which],
            self.place.partners[second],
        )

    def step(self, chunk, index):
        for flow in range(FLOWS):
            if index == 0:
                self.first_copy(chunk, flow).start()
                self.second_copy(chunk, flow, 0).start()
            if index == 1:
                self.first_copy(chunk, flow).wait()
                self.second_copy(chunk, flow, 1).start()
            if index == 2:
                self.second_copy(chunk, flow, 0).wait()
                self.second_copy(chunk, flow, 1).wait()

    def piece(self, tile, index, chunk, start, count):
        first, second, near, far, keep, give = self.place.flow(index)
        owner, rank = self.owner[tile], self.rank[tile]
        bits = [lax.rem(owner, 2), lax.rem(owner // 2, 2)]
        apart = [bit != mine for bit, mine in zip(bits, self.place.bits)]
        cols = pl.ds(start, count)
        mine = self.slots[rank, rows_at(keep, KEEP), pl.ds(GROUPS[chunk][0] * PAIR + start, count)]
        firsts = self.land[chunk][index, rank, rows_at(keep - near, KEEP), cols]
        gifts = self.gift[chunk][index, jnp.where(apart[first], CAP, 0) + rank, :, cols]
        value = jnp.where(apart[second], gifts, jnp.where(apart[first], firsts, mine))
        layer = owner // 4 == self.place.me // 4
        return jnp.where(layer, value, jnp.zeros_like(value))


class Column:
    steps = 4

    def __init__(self, place, kept, land, sems):
        self.place, self.kept, self.land, self.sems = place, kept, land, sems

    def copy(self, index):
        device = self.place.across if index == 1 else self.place.partners[2]
        return remote(
            self.kept, self.land.at[index % 2], self.sems[0].at[index], self.sems[1].at[index], device
        )

    def add(self, index):
        self.kept[...] = (self.kept[...].astype(f32) + self.land[index].astype(f32)).astype(b16)


def both_flows(flow):
    return pl.ds(flow * KEEP, KEEP)


def column_step(place, column, index):
    @pl.when(place.inner)
    def inner():
        if index == 1:
            column.copy(0).wait_recv()
            column.add(0)
            column.copy(1).start()
        if index == 2:
            column.copy(1).wait()
            column.add(1)
            column.copy(2).start()
        if index == 3:
            column.copy(2).wait_send()

    @pl.when(jnp.logical_not(place.inner))
    def outer():
        if index == 0:
            column.copy(0).start()
        if index == 1:
            column.copy(0).wait_send()
        if index == 3:
            column.copy(2).wait_recv()
            column.kept[...] = column.land[0]


class Item:
    steps = 7

    def __init__(self, place, work, kept, land, sems, load, store=None):
        self.place, self.work, self.kept, self.land, self.sems = place, work, kept, land, sems
        self.load, self.store = load, store
        self.base = place.core * HALF

    def copy(self, flow, index):
        first, second, near, far, keep, give = self.place.flow(flow)
        kept = self.work.at[:, rows_at(self.base + keep, KEEP)]
        half = self.work.at[:, rows_at(self.base + near, NEAR)]
        source, device = [
            (kept, self.place.partners[second]),
            (half, self.place.partners[first]),
        ][index]
        number = 3 + 2 * flow + index
        return remote(source, source, self.sems[0].at[number], self.sems[1].at[number], device)

    def pair(self):
        rows = self.work.at[:, rows_at(self.base, HALF)]
        return remote(rows, rows, self.sems[0].at[7], self.sems[1].at[7], self.place.twin)

    def step(self, index):
        if index == 0:
            for flow in range(FLOWS):
                self.load(self.kept, both_flows(flow), flow)
        if index <= 3:
            column_step(self.place, Column(self.place, self.kept, self.land, self.sems), index)
        for flow in range(FLOWS):
            if index == 3:
                rows = rows_at(self.base + self.place.flow(flow)[4], KEEP)
                self.work[:, rows] = self.kept[:, both_flows(flow)]
            if 4 <= index <= 5:
                self.copy(flow, index - 4).wait()
            if 3 <= index <= 4:
                self.copy(flow, index - 3).start()
        if index == 5:
            self.pair().start()
        if index == 6:
            self.pair().wait()
            self.store().start()


REST_GROUPS = tuple((index, 1) for index in range(REST))
PAIR_CHUNK = (0, 1, 1, 2, 2, 2)
FRONT_PAIRS = (2, 4, 5, 6, 7, 8)
FRONT_REST = (6, 7, 8, 9, 10, 11, 12, 13, 14)
FRONT_LEAD = 9


def front_kernel(
    owner, lengths, master, vec_ref, x_in, c_in,
    x_out, c_out, n_out, one_out, mix_out, up_out, down_out, q_ref, k_ref, v_ref, p_ref, r_ref, o_ref, ctx_ref,
    rank, rows_ref, normed, keys, turned_values, scores, slots,
    land_one, land_two, land_three, gift_one, gift_two, gift_three,
    one, one_kept, one_land, two, two_kept, two_land,
    spread_send, spread_recv, one_send, one_recv, two_send, two_recv,
    swap_send, swap_recv, swap_local, store_sem,
):
    pair = pl.program_id(0)
    row = pl.program_id(1)
    grid_step = pair * 2 + row
    place = Place()
    rows, span = x_in.shape[0] // 2, x_in.shape[1]
    land = (land_one, land_two, land_three)
    gift = (gift_one, gift_two, gift_three)
    spread = Spread(place, owner, rank, slots, land, gift, (spread_send, spread_recv))

    def swaps(index):
        source, target = [(x_in, rows_ref), (c_in, c_out)][index]
        here = pl.ds(place.core * span, span)
        near = pltpu.make_async_copy(
            source.at[pl.ds(place.core * rows, rows)], target.at[:, here], swap_local.at[index]
        )
        far = remote(
            source.at[pl.ds(place.other * rows, rows)],
            target.at[:, here],
            swap_send.at[index],
            swap_recv.at[index],
            place.twin,
        )
        return near, far

    def row_store():
        return pltpu.make_async_copy(rows_ref, x_out, store_sem.at[PAIRS + REST])

    def normed_store():
        return pltpu.make_async_copy(normed, n_out, store_sem.at[PAIRS + REST + 1])

    def pair_item(group):
        span_of = pl.ds(group, 1)

        def load(work, where, flow):
            chunk = PAIR_CHUNK[group]
            for tile in range(3):
                part = spread.piece(tile, flow, chunk, (group - GROUPS[chunk][0]) * PAIR, PAIR)
                work[0, where, pl.ds(tile * PAIR, PAIR)] = part

        def store():
            return pltpu.make_async_copy(one.at[span_of], one_out.at[span_of], store_sem.at[group])

        sems = (one_send.at[group], one_recv.at[group])
        return Item(place, one.at[span_of], one_kept.at[span_of], one_land.at[:, span_of], sems, load, store)

    def rest_item(group):
        first, count = REST_GROUPS[group]
        span_of = pl.ds(first, count)

        def load(work, where, flow):
            for index in range(count):
                for chunk, (start, wide) in enumerate(GROUPS):
                    part = spread.piece(3 + first + index, flow, chunk, 0, wide * PAIR)
                    work[index, where, pl.ds(start * PAIR, wide * PAIR)] = part

        def store():
            if first == 0:
                target = mix_out
            elif first <= FF // D:
                target = up_out.at[:, pl.ds((first - 1) * D, D)]
            else:
                target = down_out.at[pl.ds((first - 1 - FF // D) * D, D)]
            return pltpu.make_async_copy(two.at[first], target, store_sem.at[PAIRS + group])

        sems = (two_send.at[group], two_recv.at[group])
        return Item(place, two.at[span_of], two_kept.at[span_of], two_land.at[:, span_of], sems, load, store)

    def tick(number, odd):
        for chunk in range(CHUNKS):
            if odd == 0 and 0 <= number - 2 * chunk <= 2:
                spread.step(chunk, number - 2 * chunk)
        starts = [(pair_item, group, start) for group, start in enumerate(FRONT_PAIRS)]
        starts += [(rest_item, group, start) for group, start in enumerate(FRONT_REST)]
        for make, group, start in starts:
            if group % 2 == odd and 0 <= number - start < Item.steps:
                make(group).step(number - start)

    def both(number):
        tick(number, 0)
        tick(number, 1)

    @pl.when(grid_step == 0)
    def lead():
        slots[...] = master[...].astype(b16)
        for tile in range(PIECES):
            count = jnp.int32(0)
            for before in range(tile):
                count = count + (owner[before] == owner[tile]).astype(jnp.int32)
            rank[tile] = jnp.minimum(count, CAP - 1)
        place.greet()
        for copy in swaps(0):
            copy.start()
        both(0)
        for copy in swaps(1):
            copy.start()
        for copy in swaps(0):
            copy.wait()
        row_store().start()

        def norm_rows(index, carry):
            for part in range(rows):
                for block in range(4):
                    where = pl.ds(pl.multiple_of(index * 128 + block * 32, 32), 32)
                    unit, unused = norm_parts(rows_ref[part, where].astype(f32))
                    low = (unit * vec_ref[0:1, :] + vec_ref[1:2, :]).astype(b16)
                    normed[pl.ds(pl.multiple_of(part * LEN + index * 128 + block * 32, 32), 32)] = low
            return carry

        both(1)
        lax.fori_loop(0, LEN // 128, norm_rows, 0)
        normed_store().start()
        for number in range(2, FRONT_LEAD):
            both(number)

    for number in range(2 * PAIRS):
        pl.when(grid_step == number)(partial(tick, FRONT_LEAD + number, 0))

    @pl.when(row == 0)
    def project():
        lanes = pl.ds(pl.multiple_of(pair * PAIR, PAIR), PAIR)
        weight = one[pair]

        def part(index, carry):
            where = pl.ds(pl.multiple_of(index * 512, 512), 512)
            both = dot_nn(normed[where], weight)
            queries = both[:, :PAIR] + vec_ref[4:5, lanes]
            queries = (queries * (HEAD_DIM**-0.5 * LOG2E)).astype(b16)
            q_ref[:, where] = queries.T
            low = both[:, PAIR : 2 * PAIR].astype(b16)
            keys[where] = low
            k_ref[:, where] = low.T
            values = (both[:, 2 * PAIR :] + vec_ref[5:6, lanes]).astype(b16)
            v_ref[where] = values
            turned_values[:, where] = values.T
            return carry

        lax.fori_loop(0, normed.shape[0] // 512, part, 0)

    half = LEN // 2
    start = pl.multiple_of(row * LEN, LEN)
    split = lengths[place.core * rows + row, 0] < LEN
    shift = jnp.where(split, jnp.float32(-1e30), jnp.float32(0.0))

    quarter = LEN // 4
    units = [(head, step) for head in range(2) for step in range(2)]

    def score_block(unit, block, peak):
        head, step = units[unit]
        rows_here = pl.ds(pl.multiple_of(start + block * quarter, quarter), quarter)
        queries = q_ref[:, pl.ds(pl.multiple_of(start + step * half, half), half)]
        raw = dot_nn(head_only(keys[rows_here], head), queries)
        if block // 2 != step:
            raw = raw + shift
        scores[unit % 2, block * quarter : (block + 1) * quarter] = raw
        best = jnp.max(raw.reshape(-1, 8, half), axis=0)
        return best if peak is None else jnp.maximum(peak, best)

    def context_block(unit, block, total):
        head, step = units[unit]
        part = slice(head * HEAD_DIM, (head + 1) * HEAD_DIM)
        cols = pl.ds(pl.multiple_of(start + block * quarter, quarter), quarter)
        here = slice(step * half, (step + 1) * half)
        term = dot_nn(
            turned_values[part, cols], p_ref[head, block * quarter : (block + 1) * quarter, here]
        )
        return term if total is None else total + term

    def context_store(unit, total, recip):
        head, step = units[unit]
        part = slice(head * HEAD_DIM, (head + 1) * HEAD_DIM)
        o_ref[part, step * half : (step + 1) * half] = (total * recip).astype(b16)

    peak = None
    for block in range(4):
        peak = score_block(0, block, peak)
    before = None
    for unit, (head, step) in enumerate(units):
        if unit == 2:
            for number in range(2 * PAIRS):
                pl.when(grid_step == number)(partial(tick, FRONT_LEAD + number, 1))
        here = slice(step * half, (step + 1) * half)
        top = jnp.max(peak, 0, keepdims=True)
        total = jnp.zeros((8, half), f32)
        peak, context = None, None
        for block in range(4):
            if unit + 1 < len(units):
                peak = score_block(unit + 1, block, peak)
            for small in range(4 * block, 4 * block + 4):
                rows_here = slice(small * 64, (small + 1) * 64)
                value = jnp.exp2(scores[unit % 2, rows_here] - top)
                total = total + jnp.sum(value.reshape(-1, 8, half), axis=0)
                p_ref[head, rows_here, here] = value.astype(b16)
            if unit > 0:
                context = context_block(unit - 1, block, context)
        if unit > 0:
            context_store(unit - 1, context, before)
        before = 1.0 / jnp.sum(total, 0, keepdims=True)
        r_ref[0, head : head + 1, here] = before
    context = None
    for block in range(4):
        context = context_block(3, block, context)
    context_store(3, context, before)
    ctx_ref[...] = o_ref[...].T

    @pl.when(grid_step == 2 * PAIRS - 1)
    def finish_copies():
        for copy in swaps(1):
            copy.wait()
        row_store().wait()
        normed_store().wait()
        for group in range(PAIRS):
            pair_item(group).store().wait()
        for group in range(REST):
            rest_item(group).store().wait()


def front(owner, lengths, master, vectors, inputs, cotangent):
    rows, span = inputs.shape[0] // 2, inputs.shape[1]
    tokens = rows * LEN
    any_spec = pl.BlockSpec(memory_space=pl.ANY)
    smem = pl.BlockSpec(memory_space=pltpu.SMEM)
    whole = jax.ShapeDtypeStruct((rows, LEN, D), b16)
    dma = pltpu.SemaphoreType.DMA
    return pl.pallas_call(
        front_kernel,
        grid=(PAIRS, rows),
        in_specs=[
            smem,
            smem,
            pl.BlockSpec((CAP, HALF, D), lambda h, r: (0, 0, 0), pipeline_mode=pl.Buffered(1)),
            pl.BlockSpec((PIECES, D), lambda h, r: (0, 0)),
            any_spec,
            any_spec,
        ],
        out_specs=[any_spec] * 7
        + [
            pl.BlockSpec((PAIR, tokens), lambda h, r: (h, 0)),
            pl.BlockSpec((PAIR, tokens), lambda h, r: (h, 0)),
            pl.BlockSpec((tokens, PAIR), lambda h, r: (0, h)),
            pl.BlockSpec((2, LEN, LEN), lambda h, r: (h * 2 + r, 0, 0)),
            pl.BlockSpec((1, 2, LEN), lambda h, r: (h * 2 + r, 0, 0)),
            pl.BlockSpec((PAIR, LEN), lambda h, r: (h, r)),
            pl.BlockSpec((LEN, PAIR), lambda h, r: (r, h)),
        ],
        out_shape=[
            whole,
            whole,
            jax.ShapeDtypeStruct((tokens, D), b16),
            jax.ShapeDtypeStruct((PAIRS, D, WIDE), b16),
            jax.ShapeDtypeStruct((D, D), b16),
            jax.ShapeDtypeStruct((D, FF), b16),
            jax.ShapeDtypeStruct((FF, D), b16),
            jax.ShapeDtypeStruct((D, tokens), b16),
            jax.ShapeDtypeStruct((D, tokens), b16),
            jax.ShapeDtypeStruct((tokens, D), b16),
            jax.ShapeDtypeStruct((rows * HEADS, LEN, LEN), b16),
            jax.ShapeDtypeStruct((rows * PAIRS, 2, LEN), f32),
            jax.ShapeDtypeStruct((D, tokens), b16),
            jax.ShapeDtypeStruct((tokens, D), b16),
        ],
        scratch_shapes=[
            pltpu.SMEM((PIECES,), jnp.int32),
            pltpu.VMEM((rows, LEN, D), b16),
            pltpu.VMEM((tokens, D), b16),
            pltpu.VMEM((tokens, PAIR), b16),
            pltpu.VMEM((PAIR, tokens), b16),
            pltpu.VMEM((2, LEN, LEN // 2), f32),
            pltpu.VMEM((CAP, HALF, D), b16),
        ]
        + [pltpu.VMEM((FLOWS, CAP, NEAR, wide * PAIR), b16) for unused, wide in GROUPS]
        + [pltpu.VMEM((FLOWS, 2 * CAP, KEEP, wide * PAIR), b16) for unused, wide in GROUPS]
        + [
            pltpu.VMEM((PAIRS, D, WIDE), b16),
            pltpu.VMEM((PAIRS, NEAR, WIDE), b16),
            pltpu.VMEM((2, PAIRS, NEAR, WIDE), b16),
            pltpu.VMEM((REST, D, D), b16),
            pltpu.VMEM((REST, NEAR, D), b16),
            pltpu.VMEM((2, REST, NEAR, D), b16),
            dma((CHUNKS, FLOWS, 3)),
            dma((CHUNKS, FLOWS, 3)),
            dma((PAIRS, 8)),
            dma((PAIRS, 8)),
            dma((REST, 8)),
            dma((REST, 8)),
            dma((2,)),
            dma((2,)),
            dma((2,)),
            dma((PAIRS + REST + 2,)),
        ],
        compiler_params=pltpu.CompilerParams(
            collective_id=0, has_side_effects=True, vmem_limit_bytes=60 * MIB
        ),
        name="front",
    )(owner, lengths, master, vectors, inputs, cotangent)


class Sum:
    steps = 7

    def __init__(self, place, work, kept, wide, narrow, land, sems, send_pair, add_own):
        self.place, self.work, self.kept, self.sems = place, work, kept, sems
        self.wide, self.narrow, self.land = wide, narrow, land
        self.send_pair, self.add_own = send_pair, add_own

    def copy(self, flow, index):
        first, second, near, far, keep, give = self.place.flow(flow)
        source, target, device = [
            (self.work.at[:, rows_at(far, NEAR)], self.wide.at[flow], first),
            (self.work.at[:, rows_at(give, KEEP)], self.narrow.at[flow], second),
        ][index]
        number = 3 + 2 * flow + index
        return remote(
            source,
            target,
            self.sems[0].at[number],
            self.sems[1].at[number],
            self.place.partners[device],
        )

    def step(self, index):
        if index == 0:
            self.send_pair().start()
        if index == 1:
            self.send_pair().wait()
            self.add_own()
        for flow in range(FLOWS):
            first, second, near, far, keep, give = self.place.flow(flow)
            if index == 1:
                self.copy(flow, 0).start()
            if index == 2:
                self.copy(flow, 0).wait()
                rows = rows_at(near, NEAR)
                total = self.work[:, rows].astype(f32) + self.wide[flow].astype(f32)
                self.work[:, rows] = total.astype(b16)
                self.copy(flow, 1).start()
            if index == 3:
                self.copy(flow, 1).wait()
                total = self.work[:, rows_at(keep, KEEP)].astype(f32) + self.narrow[flow].astype(f32)
                self.kept[:, both_flows(flow)] = total.astype(b16)
        if index >= 3:
            column_step(self.place, Column(self.place, self.kept, self.land, self.sems), index - 3)


class Gather:
    steps = 3

    def __init__(self, place, work, kept, narrow, wide, sems):
        self.place, self.work, self.kept = place, work, kept
        self.narrow, self.wide, self.sems = narrow, wide, sems

    def copy(self, flow, index):
        first, second, near, far, keep, give = self.place.flow(flow)
        source, target, device = [
            (self.kept.at[:, both_flows(flow)], self.narrow, second),
            (self.work.at[:, rows_at(near, NEAR)], self.wide, first),
        ][index]
        number = 7 + 2 * flow + index
        return remote(
            source,
            target.at[flow],
            self.sems[0].at[number],
            self.sems[1].at[number],
            self.place.partners[device],
        )

    def step(self, index):
        for flow in range(FLOWS):
            first, second, near, far, keep, give = self.place.flow(flow)
            if index == 0:
                self.work[:, rows_at(keep, KEEP)] = self.kept[:, both_flows(flow)]
            if index > 0:
                self.copy(flow, index - 1).wait()
            if index == 1:
                self.work[:, rows_at(give, KEEP)] = self.narrow[flow]
            if index == 2:
                self.work[:, rows_at(far, NEAR)] = self.wide[flow]
            if index < 2:
                self.copy(flow, index).start()


class Hand:
    steps = 3

    def __init__(self, place, table, kept, bag, gift, pack, last, own, out, sems, store_sems):
        self.place, self.table, self.kept = place, table, kept
        self.bag, self.gift, self.pack, self.last, self.own = bag, gift, pack, last, own
        self.out, self.sems, self.store_sems = out, sems, store_sems

    def tile(self, chip, rank, flow):
        return self.kept[self.table[chip * CAP + rank], both_flows(flow)]

    def copy(self, flow, index):
        first, second = self.place.flow(flow)[:2]
        source, target, device = [
            (self.bag.at[flow], self.gift.at[flow], second),
            (self.pack.at[flow], self.last.at[flow], first),
        ][index]
        return remote(
            source,
            target,
            self.sems[0].at[flow, index],
            self.sems[1].at[flow, index],
            self.place.partners[device],
        )

    def stores(self, flow):
        first, second, near, far, keep, give = self.place.flow(flow)
        parts = [
            (self.own.at[flow], rows_at(keep, KEEP)),
            (self.gift.at[flow, pl.ds(0, CAP)], rows_at(give, KEEP)),
            (self.last.at[flow], rows_at(far, NEAR)),
        ]
        return [
            pltpu.make_async_copy(source, self.out.at[:, rows], self.store_sems.at[flow, index])
            for index, (source, rows) in enumerate(parts)
        ]

    def step(self, index):
        for flow in range(FLOWS):
            first, second, near, far, keep, give = self.place.flow(flow)
            if index == 0:
                beside = self.place.chips[second]
                across = beside + self.place.chips[first] - self.place.me
                for rank in range(CAP):
                    self.bag[flow, rank] = self.tile(beside, rank, flow)
                    self.bag[flow, CAP + rank] = self.tile(across, rank, flow)
                    self.own[flow, rank] = self.tile(self.place.me, rank, flow)
                self.copy(flow, 0).start()
            if index == 1:
                self.copy(flow, 0).wait()
                for rank in range(CAP):
                    mine = self.tile(self.place.chips[first], rank, flow)
                    self.pack[flow, rank, rows_at(keep - near, KEEP)] = mine
                    self.pack[flow, rank, rows_at(give - near, KEEP)] = self.gift[flow, CAP + rank]
                self.copy(flow, 1).start()
            if index == 2:
                self.copy(flow, 1).wait()
                for copy in self.stores(flow):
                    copy.start()


BACK_STEPS = 2 * PAIRS
BACK_TAIL = 4
BACK_PAIRS = tuple((index, 1) for index in range(PAIRS))
BACK_REST = (0, 1, 2, 3, 4, 5, 6, 7, 8)
BACK_HAND = 15


def back_kernel(
    table, p_ref, r_ref, v_ref, q_ref, k_ref, o_ref, g_ref, w_ref, n_ref, x_ref, z_ref, vec_ref,
    tiles_in, sums_in, y_in,
    y_out, i_out, pairs_out, slots_out, sums_ref,
    grad_sum, wide_sum, turned, slopes, block_out,
    two, two_kept, two_wide, two_narrow, two_land, two_stage,
    one, one_kept, one_wide, one_narrow, one_land, one_send_stage, one_stage,
    gather_narrow, gather_wide,
    bag, gift, pack, last, own, vec_land,
    two_send, two_recv, one_send, one_recv, hand_send, hand_recv, hand_store,
    pair_two_send, pair_two_recv, pair_one_send, pair_one_recv, load_sem, store_sem,
    swap_send, swap_recv, swap_local, vec_send, vec_recv,
):
    step = pl.program_id(0)
    place = Place()
    rows, span = y_in.shape[0], y_in.shape[1] // 2
    near_half = rows_at(place.core * HALF, HALF)
    far_half = rows_at(place.other * HALF, HALF)

    def load_two(group):
        first, count = REST_GROUPS[group]
        return pltpu.make_async_copy(
            tiles_in.at[pl.ds(first, count), near_half],
            two_stage.at[pl.ds(group % 2, 1)],
            load_sem.at[group % 2],
        )

    def rest_sum(group):
        first, count = REST_GROUPS[group]
        span_of = pl.ds(first, count)
        work = two.at[span_of]

        def send_pair():
            return remote(
                tiles_in.at[span_of, far_half],
                work,
                pair_two_send.at[group],
                pair_two_recv.at[group],
                place.twin,
            )

        def add_own():
            load_two(group).wait()
            work[...] = (work[...].astype(f32) + two_stage[group % 2].astype(f32)).astype(b16)

        sems = (two_send.at[group], two_recv.at[group])
        parts = (two_kept.at[span_of], two_wide.at[:, span_of], two_narrow.at[:, span_of])
        return Sum(place, work, *parts, two_land.at[:, span_of], sems, send_pair, add_own)

    def pair_sum(group):
        first, count = BACK_PAIRS[group]
        span_of = pl.ds(first, count)
        work = one.at[span_of]

        def send_pair():
            return remote(
                one_send_stage.at[pl.ds(group % 2, 1)],
                work,
                pair_one_send.at[group],
                pair_one_recv.at[group],
                place.twin,
            )

        def add_own():
            own = one_stage[group % 2].astype(f32)
            work[...] = (work[...].astype(f32) + own).astype(b16)

        sems = (one_send.at[group], one_recv.at[group])
        parts = (one_kept.at[span_of], one_wide.at[:, span_of], one_narrow.at[:, span_of])
        return Sum(place, work, *parts, one_land.at[:, span_of], sems, send_pair, add_own)

    def pair_gather(group):
        first, count = BACK_PAIRS[group]
        span_of = pl.ds(first, count)
        sems = (one_send.at[group], one_recv.at[group])
        narrow, wide = gather_narrow.at[:, span_of], gather_wide.at[:, span_of]
        return Gather(place, one.at[span_of], one_kept.at[span_of], narrow, wide, sems)

    hand = Hand(
        place, table, two_kept, bag, gift, pack, last, own, slots_out, (hand_send, hand_recv), hand_store
    )

    def pair_store(index, tile):
        return pltpu.make_async_copy(
            one.at[index, :, pl.ds(tile * PAIR, PAIR)],
            pairs_out.at[tile, :, pl.ds(index * PAIR, PAIR)],
            store_sem.at[index, tile],
        )

    def tick(number, odd):
        for group, start in enumerate(BACK_REST):
            if group % 2 == odd and 0 <= number - start < Sum.steps:
                rest_sum(group).step(number - start)
        for group, (first, count) in enumerate(BACK_PAIRS):
            if group % 2 != odd:
                continue
            start = 2 * (first + count)
            if 0 <= number - start < Sum.steps:
                pair_sum(group).step(number - start)
            if 0 <= number - start - Sum.steps + 1 < Gather.steps:
                pair_gather(group).step(number - start - Sum.steps + 1)
            if number == start + Sum.steps + 1:
                for index in range(first, first + count):
                    for tile in range(3):
                        pair_store(index, tile).start()
        if odd == 0 and 0 <= number - BACK_HAND < Hand.steps:
            hand.step(number - BACK_HAND)
        for group, start in enumerate(BACK_REST):
            if odd == 1 and number == max(start - 1, 0):
                load_two(group).start()

    def both(number):
        tick(number, 0)
        tick(number, 1)

    def swap_y(index):
        there = pl.ds(place.core * rows, rows)
        if index == 0:
            return pltpu.make_async_copy(
                y_in.at[:, pl.ds(place.core * span, span)], y_out.at[there], swap_local.at[0]
            )
        return remote(
            y_in.at[:, pl.ds(place.other * span, span)],
            y_out.at[there],
            swap_send.at[0],
            swap_recv.at[0],
            place.twin,
        )

    @pl.when(step == 0)
    def lead():
        place.greet()
        for index in range(2):
            swap_y(index).start()
        sums_ref[...] = sums_in[...]

    for number in range(BACK_STEPS + BACK_TAIL):
        early = partial(tick, number, 0) if number < BACK_STEPS else partial(both, number)
        pl.when(step == number)(early)

    half = LEN // 2
    pair, row = step // 2, lax.rem(step, 2)

    quarter = LEN // 4

    def attention_inputs(head):
        part = slice(head * HEAD_DIM, (head + 1) * HEAD_DIM)
        values = head_only(v_ref[...], head)
        recip = r_ref[0, head : head + 1, :]
        grad = g_ref[part, :].astype(f32) * recip
        delta = jnp.sum(grad * o_ref[part, :].astype(f32), 0, keepdims=True)
        grad = grad.astype(b16)
        return values, grad, delta, jnp.concatenate([grad, grad], axis=0)

    def attention(head):
        part = slice(head * HEAD_DIM, (head + 1) * HEAD_DIM)
        values, grad, delta, doubled = attention_inputs(head)
        units = [(which, block) for which in range(2) for block in range(4)]
        value_grad, key_grad, query_grad = {}, {}, {}

        def raw_block(unit):
            which, block = units[unit]
            cols = slice(which * half, (which + 1) * half)
            return dot_nn(values[block * quarter : (block + 1) * quarter], doubled[:, cols])

        def slope_block(unit, raw):
            which, block = units[unit]
            cols = slice(which * half, (which + 1) * half)
            for small in range(4):
                rows_here = slice(small * 64, (small + 1) * 64)
                rows_all = slice(block * quarter + small * 64, block * quarter + (small + 1) * 64)
                slope = p_ref[head, rows_all, cols].astype(f32) * (raw[rows_here] - delta[:, cols])
                slopes[unit % 2, rows_here] = slope.astype(b16)

        def add(totals, key, term):
            totals[key] = totals[key] + term if key in totals else term

        def grad_block(unit):
            which, block = units[unit]
            cols = slice(which * half, (which + 1) * half)
            rows_all = slice(block * quarter, (block + 1) * quarter)
            slope = slopes[unit % 2]
            add(value_grad, block, dot_nt(grad[:, cols], p_ref[head, rows_all, cols]))
            add(key_grad, block, dot_nt(q_ref[part, cols], slope))
            add(query_grad, which, dot_nn(k_ref[part, rows_all], slope))

        raw = raw_block(0)
        for unit in range(len(units)):
            after = raw_block(unit + 1) if unit + 1 < len(units) else None
            slope_block(unit, raw)
            if unit > 0:
                grad_block(unit - 1)
            raw = after
        grad_block(len(units) - 1)
        for which in range(2):
            total = query_grad[which] * (HEAD_DIM**-0.5)
            turned[part, which * half : (which + 1) * half] = total.astype(b16)
        for block in range(4):
            rows_all = slice(block * quarter, (block + 1) * quarter)
            lower = slice(PAIR + head * HEAD_DIM, PAIR + (head + 1) * HEAD_DIM)
            turned[lower, rows_all] = (key_grad[block] * (1.0 / LOG2E)).astype(b16)
            lower = slice(2 * PAIR + head * HEAD_DIM, 2 * PAIR + (head + 1) * HEAD_DIM)
            turned[lower, rows_all] = value_grad[block].astype(b16)

    @pl.when(step < BACK_STEPS)
    def first_head():
        attention(0)

    for number in range(BACK_STEPS):
        pl.when(step == number)(partial(tick, number, 1))

    @pl.when(step < BACK_STEPS)
    def second_head():
        attention(1)
        where = pl.ds(pl.multiple_of(row * LEN, LEN), LEN)
        block = dot_nn(turned[...], n_ref[where])
        back = turned[...].T
        lanes = pl.ds(pl.multiple_of(pair * PAIR, PAIR), PAIR)
        ones = jnp.sum(back.astype(f32), 0, keepdims=True)
        sums_ref[4:5, lanes] += ones[:, :PAIR]
        sums_ref[5:6, lanes] += ones[:, 2 * PAIR :]
        term = dot_nt(back, w_ref[0])

        @pl.when(pair == 0)
        def begin():
            grad_sum[where] = term

        @pl.when(pair > 0)
        def add():
            grad_sum[where] += term

        @pl.when(row == 0)
        def keep():
            wide_sum[...] = block

        @pl.when(row == 1)
        def hand_on():
            whole = (wide_sum[...] + block).T
            low = whole.astype(b16)
            for core in range(2):

                @pl.when(place.core == core)
                def split():
                    slot = lax.rem(pair, 2)
                    one_stage[slot] = low[core * HALF : (core + 1) * HALF]
                    one_send_stage[slot] = low[(1 - core) * HALF : (2 - core) * HALF]

    def store_block(index):
        row, half = index // 2, index % 2
        target = i_out.at[place.core * rows + row]
        local = pltpu.make_async_copy(block_out.at[half], target, swap_local.at[1 + row])
        far = remote(
            block_out.at[half], target, swap_send.at[1 + row], swap_recv.at[1 + row], place.twin
        )
        return local, far, half

    def wait_block(index):
        local, far, half = store_block(index)

        @pl.when(place.core == half)
        def keep():
            local.wait()

        @pl.when(place.core != half)
        def give():
            far.wait()

    for index in range(BACK_TAIL):

        @pl.when(step == BACK_STEPS + index)
        def close():
            size = LEN // 2
            if index >= 2:
                wait_block(index - 2)
            gain_sum = jnp.zeros((8, D), f32)
            shift_sum = jnp.zeros((8, D), f32)
            for block in range(size // 16):
                rows_here = slice(block * 16, (block + 1) * 16)
                grad = grad_sum[index * size + block * 16 : index * size + (block + 1) * 16]
                unit, rstd = norm_parts(x_ref[rows_here].astype(f32))
                gain_sum = gain_sum + jnp.sum((grad * unit).reshape(-1, 8, D), axis=0)
                shift_sum = shift_sum + jnp.sum(grad.reshape(-1, 8, D), axis=0)
                total = norm_back(grad, unit, rstd, vec_ref[0:1, :])
                block_out[index % 2, rows_here] = (z_ref[rows_here].astype(f32) + total).astype(b16)
            sums_ref[0:1, :] += jnp.sum(gain_sum, 0, keepdims=True)
            sums_ref[1:2, :] += jnp.sum(shift_sum, 0, keepdims=True)
            local, far, half = store_block(index)

            @pl.when(place.core == half)
            def keep():
                local.start()

            @pl.when(place.core != half)
            def give():
                far.start()

    @pl.when(step == BACK_STEPS + BACK_TAIL - 1)
    def drain():
        devices = [place.twin] + place.partners

        def vector(index):
            return remote(
                sums_ref, vec_land.at[index], vec_send.at[index], vec_recv.at[index], devices[index]
            )

        vector(0).start()
        for number in range(BACK_STEPS + BACK_TAIL, BACK_STEPS + Sum.steps + Gather.steps):
            both(number)
            index = number - BACK_STEPS - BACK_TAIL
            if index < 5:
                vector(index).wait()
                sums_ref[...] += vec_land[index]
                if index < 4:
                    vector(index + 1).start()
        for index in range(2):
            swap_y(index).wait()
        for index in range(2, BACK_TAIL):
            wait_block(index)
        for index in range(PAIRS):
            for tile in range(3):
                pair_store(index, tile).wait()
        for flow in range(FLOWS):
            for copy in hand.stores(flow):
                copy.wait()


def back(table, attention, weights, normed, x, residual, vectors, tiles, sums, y):
    rows, length = y.shape[:2]
    tokens = rows * length
    any_spec = pl.BlockSpec(memory_space=pl.ANY)
    smem = pl.BlockSpec(memory_space=pltpu.SMEM)
    dma = pltpu.SemaphoreType.DMA

    def now(step):
        return jnp.minimum(step, BACK_STEPS - 1)

    def tail(step):
        return jnp.maximum(step - BACK_STEPS, 0)

    head_block = pl.BlockSpec((PAIR, LEN), lambda s: (now(s) // 2, lax.rem(now(s), 2)))
    tail_block = pl.BlockSpec((LEN // 2, D), lambda s: (tail(s), 0))
    whole = pl.BlockSpec((PIECES, D), lambda s: (0, 0))
    sums_block = pl.BlockSpec((16, D), lambda s: (0, 0))
    return pl.pallas_call(
        back_kernel,
        grid=(BACK_STEPS + BACK_TAIL,),
        in_specs=[
            smem,
            pl.BlockSpec((2, LEN, LEN), lambda s: (now(s), 0, 0)),
            pl.BlockSpec((1, 2, LEN), lambda s: (now(s), 0, 0)),
            pl.BlockSpec((LEN, PAIR), lambda s: (lax.rem(now(s), 2), now(s) // 2)),
            head_block,
            head_block,
            head_block,
            head_block,
            pl.BlockSpec((1, D, WIDE), lambda s: (now(s) // 2, 0, 0)),
            pl.BlockSpec((tokens, D), lambda s: (0, 0), pipeline_mode=pl.Buffered(1)),
            tail_block,
            tail_block,
            whole,
            any_spec,
            sums_block,
            any_spec,
        ],
        out_specs=[any_spec] * 4 + [sums_block],
        out_shape=[
            jax.ShapeDtypeStruct((2 * rows, length // 2, D), b16),
            jax.ShapeDtypeStruct((2 * rows, length // 2, D), b16),
            jax.ShapeDtypeStruct((3, HALF, D), b16),
            jax.ShapeDtypeStruct((CAP, HALF, D), b16),
            jax.ShapeDtypeStruct((16, D), f32),
        ],
        scratch_shapes=[
            pltpu.VMEM((tokens, D), f32),
            pltpu.VMEM((WIDE, D), f32),
            pltpu.VMEM((WIDE, LEN), b16),
            pltpu.VMEM((2, LEN // 4, LEN // 2), b16),
            pltpu.VMEM((2, LEN // 2, D), b16),
            pltpu.VMEM((REST, HALF, D), b16),
            pltpu.VMEM((REST, NEAR, D), b16),
            pltpu.VMEM((FLOWS, REST, NEAR, D), b16),
            pltpu.VMEM((FLOWS, REST, KEEP, D), b16),
            pltpu.VMEM((2, REST, NEAR, D), b16),
            pltpu.VMEM((2, HALF, D), b16),
            pltpu.VMEM((PAIRS, HALF, WIDE), b16),
            pltpu.VMEM((PAIRS, NEAR, WIDE), b16),
            pltpu.VMEM((FLOWS, PAIRS, NEAR, WIDE), b16),
            pltpu.VMEM((FLOWS, PAIRS, KEEP, WIDE), b16),
            pltpu.VMEM((2, PAIRS, NEAR, WIDE), b16),
            pltpu.VMEM((2, HALF, WIDE), b16),
            pltpu.VMEM((2, HALF, WIDE), b16),
            pltpu.VMEM((FLOWS, PAIRS, KEEP, WIDE), b16),
            pltpu.VMEM((FLOWS, PAIRS, NEAR, WIDE), b16),
            pltpu.VMEM((FLOWS, 2 * CAP, KEEP, D), b16),
            pltpu.VMEM((FLOWS, 2 * CAP, KEEP, D), b16),
            pltpu.VMEM((FLOWS, CAP, NEAR, D), b16),
            pltpu.VMEM((FLOWS, CAP, NEAR, D), b16),
            pltpu.VMEM((FLOWS, CAP, KEEP, D), b16),
            pltpu.VMEM((5, 16, D), f32),
            dma((REST, 7)),
            dma((REST, 7)),
            dma((PAIRS, 11)),
            dma((PAIRS, 11)),
            dma((FLOWS, 2)),
            dma((FLOWS, 2)),
            dma((FLOWS, 3)),
            dma((REST,)),
            dma((REST,)),
            dma((PAIRS,)),
            dma((PAIRS,)),
            dma((3,)),
            dma((PAIRS, 3)),
            dma((3,)),
            dma((3,)),
            dma((3,)),
            dma((5,)),
            dma((5,)),
        ],
        compiler_params=pltpu.CompilerParams(
            collective_id=1, has_side_effects=True, vmem_limit_bytes=62 * MIB
        ),
        name="back",
    )(table, *attention, weights, normed, x, residual, vectors, tiles, sums, y)


def update_kernel(tile_at, one, two, w_ref, m_ref, s_ref, y_in, i_in, w_out, m_out, s_out, y_out, i_out):
    step = pl.program_id(0)
    tile = tile_at[step // 2]
    grad = jnp.where(tile < 3, one[0], two[0]).astype(f32)
    parts = adam_step(w_ref[0], grad, m_ref[0], s_ref[0], RATE)
    for target, part in zip((w_out, m_out, s_out), parts):
        target[0] = jnp.where(tile >= 0, part, jnp.zeros_like(part))

    @pl.when(step < 4)
    def widen():
        y_out[...] = y_in[...].astype(f32)
        i_out[...] = i_in[...].astype(f32)


def update(tile_at, one, two, master, first, second, y, grad):
    tokens = y.shape[0]
    size = HALF // 2
    state = pl.BlockSpec((1, size, D), lambda s, tile_at: (s // 2, lax.rem(s, 2), 0))
    wide = pl.BlockSpec((tokens // 4, D), lambda s, tile_at: (jnp.minimum(s, 3), 0))
    return pl.pallas_call(
        update_kernel,
        grid_spec=pltpu.PrefetchScalarGridSpec(
            num_scalar_prefetch=1,
            grid=(CAP * 2,),
            in_specs=[
                pl.BlockSpec(
                    (1, size, D),
                    lambda s, tile_at: (jnp.clip(tile_at[s // 2], 0, 2), lax.rem(s, 2), 0),
                ),
                state,
                state,
                state,
                state,
                wide,
                wide,
            ],
            out_specs=[state] * 3 + [wide] * 2,
        ),
        out_shape=[jax.ShapeDtypeStruct(master.shape, f32)] * 3
        + [jax.ShapeDtypeStruct((tokens, D), f32)] * 2,
        compiler_params=pltpu.CompilerParams(vmem_limit_bytes=60 * MIB),
        name="update",
    )(tile_at, one, two, master, first, second, y, grad)


def shards_paired(
    inputs,
    cotangent,
    doc_lengths,
    owner_list,
    master,
    first_moment,
    second_moment,
    vectors,
    vector_first,
    vector_second,
):
    rows_here, span, width = inputs.shape
    place = lax.axis_index("blk")
    member = lax.axis_index("dp")
    rows_mine = rows_here // 2
    order = jnp.arange(PIECES)
    same_owner = owner_list[:, None] == owner_list[None, :]
    ranks = jnp.sum(same_owner & (order[None, :] < order[:, None]), axis=1).astype(jnp.int32)
    slot_of = owner_list * CAP + ranks
    front_outs = front(owner_list, doc_lengths, master, vectors, inputs, cotangent)
    x, cot, normed, weights_one, mix, up, down, queries, keys, values = front_outs[:10]
    weights, recips, context_turned, context = front_outs[10:]
    x = x.reshape(-1, width)
    cot = cot.reshape(-1, width)
    block_out, residual, grad_context, sums, up_sums, tiles_two = feed(
        context, context_turned, x, cot, mix, up, down, vectors
    )
    hits = jnp.arange(16 * CAP)[:, None] == slot_of[None, :]
    tile_at = jnp.sum(jnp.where(hits, order[None, :] + 1, 0), axis=1).astype(jnp.int32) - 1
    table = jnp.maximum(tile_at - 3, 0)
    block_out, input_grad, total_one, total_two, vector_total = back(
        table,
        (weights, recips, values, queries, keys, context_turned, grad_context),
        weights_one,
        normed,
        x,
        residual,
        vectors,
        tiles_two,
        sums,
        block_out.reshape(rows_mine, LEN, width),
    )
    mine = lax.dynamic_slice_in_dim(tile_at, member * CAP, CAP, 0)
    *updated, block_out, input_grad = update(
        mine,
        total_one,
        total_two,
        master,
        first_moment,
        second_moment,
        block_out.reshape(-1, width),
        input_grad.reshape(-1, width),
    )
    columns = vector_first.shape[1]
    vector_cols = lax.dynamic_slice_in_dim(vectors, place * columns, columns, 1)
    vector_total = lax.dynamic_slice(vector_total, (0, place * columns), (PIECES, columns))
    updated_vectors = adam_step(vector_cols, vector_total, vector_first, vector_second, VEC_RATE)
    return (
        block_out.reshape(inputs.shape),
        input_grad.reshape(inputs.shape),
        *updated,
        *updated_vectors,
    )


def solution(mesh):
    in_specs = (
        P("dp", "blk", None),
        P("dp", "blk", None),
        P("dp", None),
        P(),
        P("dp", "blk", None),
        P("dp", "blk", None),
        P("dp", "blk", None),
        P(),
        P(None, "blk"),
        P(None, "blk"),
    )
    out_specs = (
        P("dp", "blk", None),
        P("dp", "blk", None),
        P("dp", "blk", None),
        P("dp", "blk", None),
        P("dp", "blk", None),
        P(None, "blk"),
        P(None, "blk"),
        P(None, "blk"),
    )
    paired = mesh.shape["blk"] == 2 and mesh.shape["dp"] == 16
    shards = shards_paired if paired else shards_any
    return jax.shard_map(shards, mesh=mesh, in_specs=in_specs, out_specs=out_specs, check_vma=False)
```

```python
from functools import partial

import jax
import jax.numpy as jnp
from jax import lax
from jax.experimental import pallas as pl
from jax.experimental.pallas import tpu as pltpu
from jax.sharding import PartitionSpec as P

D = 768
FF = 3072
HEADS = 12
HEAD_DIM = 64
LEN = 1024
CAP = 3
STEP = 10
PIECES = 12


EPS_NORM = 1e-05
BETA_ONE = 0.9
BETA_TWO = 0.999
RATE = 0.04
VEC_RATE = 0.25
DECAY = 0.01
ADAM_EPS = 1e-08


def normalize(values_in, gain, shift):
    center = jnp.mean(values_in, axis=-1, keepdims=True)
    offset = values_in - center
    spread = jnp.mean(offset * offset, axis=-1, keepdims=True)
    return offset * lax.rsqrt(spread + EPS_NORM) * gain + shift


def adam_step(weight, grad, first, second, rate):
    first_new = BETA_ONE * first + (1.0 - BETA_ONE) * grad
    second_new = BETA_TWO * second + (1.0 - BETA_TWO) * grad * grad
    corrected = (
        first_new
        / (1.0 - BETA_ONE**STEP)
        / (jnp.sqrt(second_new / (1.0 - BETA_TWO**STEP)) + ADAM_EPS)
    )
    return (weight - rate * (corrected + DECAY * weight), first_new, second_new)


def shards_any(
    inputs,
    cotangent,
    doc_lengths,
    owner_list,
    master,
    first_moment,
    second_moment,
    vectors,
    vector_first,
    vector_second,
):
    rows_here, span, width = inputs.shape
    tokens_here = rows_here * span
    fold = FF // D
    scale = HEAD_DIM ** (-0.5)
    place = lax.axis_index("blk")
    f32 = jnp.float32
    b16 = jnp.bfloat16
    order = jnp.arange(PIECES)
    same_owner = owner_list[:, None] == owner_list[None, :]
    ranks = jnp.sum(same_owner & (order[None, :] < order[:, None]), axis=1)
    slot_of = owner_list * CAP + ranks

    mine = (owner_list == lax.axis_index("dp"))[:, None, None]
    tile_rows = lax.psum(jnp.where(mine, master[ranks], 0.0).astype(b16), "dp")
    tiles = lax.all_gather(tile_rows, "blk", axis=1, tiled=True)
    query_weight = tiles[0]
    key_weight = tiles[1]
    value_weight = tiles[2]
    out_weight = tiles[3]
    up_weight = jnp.transpose(tiles[4 : 4 + fold], (1, 0, 2)).reshape(width, FF)
    down_weight = tiles[4 + fold :].reshape(FF, width)
    flat_in = inputs.reshape(tokens_here, width).astype(f32)
    normed_one = normalize(flat_in, vectors[0], vectors[1]).astype(b16)
    queries = (jnp.dot(normed_one, query_weight, preferred_element_type=f32) + vectors[4]).astype(
        b16
    )
    keys_here = jnp.dot(normed_one, key_weight, preferred_element_type=f32).astype(b16)
    values_here = (
        jnp.dot(normed_one, value_weight, preferred_element_type=f32) + vectors[5]
    ).astype(b16)
    query_heads = queries.reshape(rows_here, span, HEADS, HEAD_DIM)
    first_len = doc_lengths[:, 0]
    query_seg = (place * span + jnp.arange(span))[None, :] >= first_len[:, None]

    def block_scores(key_block, start):
        count = key_block.shape[1]
        key_heads = key_block.reshape(rows_here, count, HEADS, HEAD_DIM)
        raw = (
            jnp.einsum("rqhd,rkhd->rhqk", query_heads, key_heads, preferred_element_type=f32)
            * scale
        )
        key_seg = (start + jnp.arange(count))[None, :] >= first_len[:, None]
        allowed = query_seg[:, None, :, None] == key_seg[:, None, None, :]
        return (raw, allowed)

    key_rows = keys_here.reshape(rows_here, span, width)
    value_rows = values_here.reshape(rows_here, span, width)
    top = jnp.full((rows_here, HEADS, span), -1e30, f32)
    key_block = lax.all_gather(key_rows, "blk", axis=1, tiled=True)
    value_block = lax.all_gather(value_rows, "blk", axis=1, tiled=True)
    count = key_block.shape[1]
    raw, allowed = block_scores(key_block, jnp.int32(0))
    new_top = jnp.maximum(top, jnp.max(jnp.where(allowed, raw, -1e30), axis=-1))
    weights = jnp.where(allowed, jnp.exp(raw - new_top[..., None]), 0.0)
    value_heads = value_block.reshape(rows_here, count, HEADS, HEAD_DIM)
    update = jnp.einsum(
        "rhqk,rkhd->rhqd", weights.astype(b16), value_heads, preferred_element_type=f32
    )
    total = jnp.sum(weights, axis=-1)
    log_total = new_top + jnp.log(total)
    context_raw = update / total[..., None]
    context_low = jnp.transpose(context_raw, (0, 2, 1, 3)).reshape(tokens_here, width).astype(b16)
    residual = flat_in + (jnp.dot(context_low, out_weight, preferred_element_type=f32) + vectors[6])
    normed_two = normalize(residual, vectors[2], vectors[3]).astype(b16)
    hidden = jnp.dot(normed_two, up_weight, preferred_element_type=f32) + vectors[8:].reshape(FF)
    gelu_exact = partial(jax.nn.gelu, approximate=False)
    active, gelu_pull = jax.vjp(gelu_exact, hidden)
    active_low = active.astype(b16)
    block_out = (
        residual + (jnp.dot(active_low, down_weight, preferred_element_type=f32) + vectors[7])
    ).reshape(rows_here, span, width)
    grad_out = cotangent.reshape(tokens_here, width)
    down_grad = jnp.einsum("tf,td->fd", active_low, grad_out, preferred_element_type=f32)
    down_sum = jnp.sum(grad_out, axis=0, dtype=f32)
    grad_active = jnp.einsum("td,fd->tf", grad_out, down_weight, preferred_element_type=f32)
    grad_hidden = gelu_pull(grad_active)[0].astype(b16)
    up_grad = jnp.einsum("td,tf->df", normed_two, grad_hidden, preferred_element_type=f32)
    up_sum = jnp.sum(grad_hidden, axis=0, dtype=f32)
    ffn_tiles = jnp.concatenate(
        [
            jnp.transpose(up_grad.reshape(width, fold, width), (1, 0, 2)),
            down_grad.reshape(fold, width, width),
        ],
        axis=0,
    )
    grad_normed_two = jnp.einsum("tf,df->td", grad_hidden, up_weight, preferred_element_type=f32)
    unused, second_pull = jax.vjp(normalize, residual, vectors[2], vectors[3])
    residual_part, gain_two_grad, shift_two_grad = second_pull(grad_normed_two)
    grad_residual = grad_out.astype(f32) + residual_part
    grad_attended = grad_residual.astype(b16)
    out_grad = jnp.einsum("tm,td->md", context_low, grad_attended, preferred_element_type=f32)
    out_sum = jnp.sum(grad_attended, axis=0, dtype=f32)
    grad_context = jnp.einsum(
        "td,md->tm", grad_attended, out_weight, preferred_element_type=f32
    ).astype(b16)
    grad_heads = grad_context.reshape(rows_here, span, HEADS, HEAD_DIM)
    delta = jnp.einsum("rqhd,rhqd->rhq", grad_heads.astype(f32), context_raw)
    key_all, value_all = (
        lax.all_gather(key_rows, "blk", axis=1, tiled=True),
        lax.all_gather(value_rows, "blk", axis=1, tiled=True),
    )
    key_size = min(512, LEN)

    def back_block(index, carry):
        grad_query, key_total, value_total = carry
        start = index * key_size
        key_block = lax.dynamic_slice_in_dim(key_all, start, key_size, 1)
        value_block = lax.dynamic_slice_in_dim(value_all, start, key_size, 1)
        raw, allowed = block_scores(key_block, start)
        weights_back = jnp.where(allowed, jnp.exp(raw - log_total[..., None]), 0.0)
        key_heads = key_block.reshape(rows_here, key_size, HEADS, HEAD_DIM)
        value_heads = value_block.reshape(rows_here, key_size, HEADS, HEAD_DIM)
        value_grad = jnp.einsum(
            "rhqk,rqhd->rkhd", weights_back.astype(b16), grad_heads, preferred_element_type=f32
        )
        weight_grad = jnp.einsum(
            "rqhd,rkhd->rhqk", grad_heads, value_heads, preferred_element_type=f32
        )
        score_grad = (weights_back * (weight_grad - delta[..., None])).astype(b16)
        grad_query = (
            grad_query
            + jnp.einsum("rhqk,rkhd->rqhd", score_grad, key_heads, preferred_element_type=f32)
            * scale
        )
        key_grad = (
            jnp.einsum("rhqk,rqhd->rkhd", score_grad, query_heads, preferred_element_type=f32)
            * scale
        )
        key_total = lax.dynamic_update_slice_in_dim(
            key_total, key_grad.reshape(rows_here, key_size, width), start, 1
        )
        value_total = lax.dynamic_update_slice_in_dim(
            value_total, value_grad.reshape(rows_here, key_size, width), start, 1
        )
        return (grad_query, key_total, value_total)

    zero_rows = jnp.zeros((rows_here, LEN, width), f32)
    grad_query, key_total, value_total = lax.fori_loop(
        0,
        LEN // key_size,
        back_block,
        (jnp.zeros((rows_here, span, HEADS, HEAD_DIM), f32), zero_rows, zero_rows),
    )
    key_grad_here, value_grad_here = (
        lax.psum_scatter(
            key_total.astype(jnp.bfloat16), "blk", scatter_dimension=1, tiled=True
        ).astype(jnp.float32),
        lax.psum_scatter(
            value_total.astype(jnp.bfloat16), "blk", scatter_dimension=1, tiled=True
        ).astype(jnp.float32),
    )
    query_low = grad_query.reshape(tokens_here, width).astype(b16)
    key_low = key_grad_here.reshape(tokens_here, width).astype(b16)
    value_low = value_grad_here.reshape(tokens_here, width).astype(b16)
    query_tile = jnp.einsum("td,te->de", normed_one, query_low, preferred_element_type=f32)
    key_tile = jnp.einsum("td,te->de", normed_one, key_low, preferred_element_type=f32)
    value_tile = jnp.einsum("td,te->de", normed_one, value_low, preferred_element_type=f32)
    grad_normed_one = (
        jnp.einsum("te,de->td", query_low, query_weight, preferred_element_type=f32)
        + jnp.einsum("te,de->td", key_low, key_weight, preferred_element_type=f32)
        + jnp.einsum("te,de->td", value_low, value_weight, preferred_element_type=f32)
    )
    unused, first_pull = jax.vjp(normalize, flat_in, vectors[0], vectors[1])
    input_part, gain_one_grad, shift_one_grad = first_pull(grad_normed_one)
    input_grad = (grad_residual + input_part).reshape(rows_here, span, width)
    vector_grads = jnp.concatenate(
        [
            jnp.stack(
                [
                    gain_one_grad,
                    shift_one_grad,
                    gain_two_grad,
                    shift_two_grad,
                    jnp.sum(query_low, axis=0, dtype=f32),
                    jnp.sum(value_low, axis=0, dtype=f32),
                    out_sum,
                    down_sum,
                ]
            ),
            up_sum.reshape(fold, width),
        ],
        axis=0,
    )
    attn_tiles = jnp.stack([query_tile, key_tile, value_tile, out_grad])
    piece_share, vector_share = (
        lax.psum_scatter(
            jnp.concatenate([attn_tiles, ffn_tiles], axis=0).astype(jnp.bfloat16),
            "blk",
            scatter_dimension=1,
            tiled=True,
        ).astype(jnp.float32),
        lax.psum_scatter(
            vector_grads.astype(jnp.bfloat16), "blk", scatter_dimension=1, tiled=True
        ).astype(jnp.float32),
    )
    own_slots = lax.axis_index("dp") * CAP + jnp.arange(CAP)
    pick = (own_slots[:, None] == slot_of[None, :]).astype(f32)
    occupied = jnp.sum(pick, axis=1)[:, None, None]
    total_share, vector_total = (
        lax.psum(piece_share.astype(jnp.bfloat16), "dp").astype(jnp.float32),
        lax.psum(vector_share.astype(jnp.bfloat16), "dp").astype(jnp.float32),
    )
    slot_grads = jnp.einsum("cp,prd->crd", pick, total_share, precision=lax.Precision.HIGHEST)
    new_master, new_first, new_second = adam_step(
        master, slot_grads, first_moment, second_moment, RATE
    )
    columns = vector_first.shape[1]
    vector_cols = lax.dynamic_slice_in_dim(vectors, place * columns, columns, 1)
    new_vectors, new_vector_first, new_vector_second = adam_step(
        vector_cols, vector_total, vector_first, vector_second, VEC_RATE
    )
    return (
        block_out,
        input_grad,
        new_master * occupied,
        new_first * occupied,
        new_second * occupied,
        new_vectors,
        new_vector_first,
        new_vector_second,
    )


f32 = jnp.float32
b16 = jnp.bfloat16
LOG2E = 1.4426950408889634
MIB = 1024 * 1024
PAIRS = HEADS // 2
PAIR = 2 * HEAD_DIM


def dot_nn(left, right):
    return lax.dot_general(left, right, (((1,), (0,)), ((), ())), preferred_element_type=f32)


def dot_nt(left, right):
    return lax.dot_general(left, right, (((1,), (1,)), ((), ())), preferred_element_type=f32)


def dot_tn(left, right):
    return lax.dot_general(left, right, (((0,), (0,)), ((), ())), preferred_element_type=f32)


def norm_parts(values_in):
    center = jnp.mean(values_in, axis=-1, keepdims=True)
    offset = values_in - center
    spread = jnp.mean(offset * offset, axis=-1, keepdims=True)
    rstd = lax.rsqrt(spread + EPS_NORM)
    return offset * rstd, rstd


def norm_back(grad, unit, rstd, gain):
    scaled = grad * gain
    first = jnp.mean(scaled, axis=-1, keepdims=True)
    second = jnp.mean(scaled * unit, axis=-1, keepdims=True)
    return rstd * (scaled - first - unit * second)


def gelu_parts(value):
    bell = jnp.exp2(value * value * (-0.5 * LOG2E))
    ratio = pl.reciprocal(1.0 + (0.3275911 * 0.7071067811865476) * jnp.abs(value))
    poly = 0.5 * 1.061405429
    poly = poly * ratio + 0.5 * -1.453152027
    poly = poly * ratio + 0.5 * 1.421413741
    poly = poly * ratio + 0.5 * -0.284496736
    poly = poly * ratio + 0.5 * 0.254829592
    tail = poly * ratio * bell
    cdf = jnp.where(value >= 0.0, 1.0 - tail, tail)
    return value * cdf, cdf + value * (bell * 0.3989422804014327)


def head_only(block, head):
    lane = lax.broadcasted_iota(jnp.int32, block.shape, 1)
    keep = (lane >= head * HEAD_DIM) & (lane < (head + 1) * HEAD_DIM)
    return jnp.where(keep, block, jnp.zeros_like(block))


def feed_kernel(
    c_ref, o_ref, x_ref, g_ref, w_ref, vec_ref,
    y_ref, r_ref, d_ref, sums_ref, tiles_ref,
    acc_ref, stage_ref, sem_ref,
):
    fold = FF // D
    step = pl.program_id(0)

    @pl.when(step == 0)
    def clear():
        acc_ref[...] = jnp.zeros_like(acc_ref)
        sums_ref[...] = jnp.zeros_like(sums_ref)

    residual = x_ref[...].astype(f32) + (dot_nn(c_ref[...], w_ref[0]) + vec_ref[6:7, :])
    unit, rstd = norm_parts(residual)
    gain = vec_ref[2:3, :]
    normed = (unit * gain + vec_ref[3:4, :]).astype(b16)
    turned = normed.T
    cot = g_ref[...]
    out = residual + vec_ref[7:8, :]
    grad = jnp.zeros_like(out)

    for part in range(fold):
        hidden = dot_nn(normed, w_ref[1 + part]) + vec_ref[8 + part : 9 + part, :]
        pulled = dot_nt(cot, w_ref[1 + fold + part])
        active, slope = gelu_parts(hidden)
        active = active.astype(b16)
        pulled = (pulled * slope).astype(b16)
        out = out + dot_nn(active, w_ref[1 + fold + part])
        grad = grad + dot_nt(pulled, w_ref[1 + part])
        acc_ref[1 + part] += dot_nn(turned, pulled)
        acc_ref[1 + fold + part] += dot_tn(active, cot)
        sums_ref[8 + part : 9 + part, :] += jnp.sum(pulled.astype(f32), 0, keepdims=True)
    y_ref[...] = out.astype(b16)
    wide = cot.astype(f32)
    sums_ref[2:3, :] += jnp.sum(grad * unit, 0, keepdims=True)
    sums_ref[3:4, :] += jnp.sum(grad, 0, keepdims=True)
    sums_ref[7:8, :] += jnp.sum(wide, 0, keepdims=True)
    back = wide + norm_back(grad, unit, rstd, gain)
    r_ref[...] = back.astype(b16)
    low = back.astype(b16)
    sums_ref[6:7, :] += jnp.sum(low.astype(f32), 0, keepdims=True)
    d_ref[...] = dot_nt(w_ref[0], low).astype(b16)
    acc_ref[0] += dot_nn(o_ref[...], low)

    @pl.when(step == pl.num_programs(0) - 1)
    def send():
        count = 1 + 2 * fold
        copies = []
        for part in range(count):
            if part >= 2:
                copies[part - 2].wait()
            stage_ref[part % 2] = acc_ref[part].astype(b16)
            copy = pltpu.make_async_copy(stage_ref.at[part % 2], tiles_ref.at[part], sem_ref.at[part % 2])
            copy.start()
            copies.append(copy)
        copies[count - 2].wait()
        copies[count - 1].wait()


def feed(context, turned, x, cot, weights, vectors):
    tokens = x.shape[0]
    size = 256
    count = 1 + 2 * (FF // D)
    token_block = pl.BlockSpec((size, D), lambda i: (i, 0))
    turned_block = pl.BlockSpec((D, size), lambda i: (0, i))
    return pl.pallas_call(
        feed_kernel,
        grid=(tokens // size,),
        in_specs=[
            token_block,
            turned_block,
            token_block,
            token_block,
            pl.BlockSpec((count, D, D), lambda i: (0, 0, 0), pipeline_mode=pl.Buffered(1)),
            pl.BlockSpec((PIECES, D), lambda i: (0, 0)),
        ],
        out_specs=[
            token_block,
            token_block,
            turned_block,
            pl.BlockSpec((16, D), lambda i: (0, 0)),
            pl.BlockSpec(memory_space=pl.ANY),
        ],
        out_shape=[
            jax.ShapeDtypeStruct((tokens, D), b16),
            jax.ShapeDtypeStruct((tokens, D), b16),
            jax.ShapeDtypeStruct((D, tokens), b16),
            jax.ShapeDtypeStruct((16, D), f32),
            jax.ShapeDtypeStruct((count, D, D), b16),
        ],
        scratch_shapes=[
            pltpu.VMEM((count, D, D), f32),
            pltpu.VMEM((2, D, D), b16),
            pltpu.SemaphoreType.DMA((2,)),
        ],
        compiler_params=pltpu.CompilerParams(vmem_limit_bytes=60 * MIB),
        cost_estimate=pl.CostEstimate(
            flops=6 * count * tokens * D * D,
            bytes_accessed=18 * tokens * D + 4 * count * D * D,
            transcendentals=2 * tokens * FF,
        ),
        name="feed",
    )(context, turned, x, cot, weights, vectors)


MESH = pl.DeviceIdType.MESH
HALF = D // 2
FLOWS = 2
FLOW = HALF // FLOWS
NEAR = FLOW // 2
KEEP = NEAR // 2
WIDE = 3 * PAIR
REST = PIECES - 3
GROUPS = ((0, 1), (1, 2), (3, 3))
CHUNKS = len(GROUPS)


class Place:
    def __init__(self):
        self.me = lax.axis_index("dp")
        self.core = lax.axis_index("blk")
        self.bits = [lax.rem(self.me // weight, 2) for weight in (1, 2, 4, 8)]
        self.chips = [
            self.me + weight - 2 * weight * bit for weight, bit in zip((1, 2, 4, 8), self.bits)
        ]
        self.partners = [{"dp": chip} for chip in self.chips]
        low, high = self.bits[2:]
        self.inner = low != high
        self.across = {"dp": self.me + 4 - 8 * low + 8 - 16 * high}
        self.other = 1 - self.core
        self.twin = {"blk": self.other}

    def greet(self):
        barrier = pltpu.get_barrier_semaphore()
        for device in self.partners + [self.across, self.twin]:
            pl.semaphore_signal(barrier, 1, device_id=device, device_id_type=MESH)
        pl.semaphore_wait(barrier, 6)

    def flow(self, index):
        first, second = (0, 1) if index == 0 else (1, 0)
        base = index * FLOW
        near = base + self.bits[first] * NEAR
        far = base + NEAR - self.bits[first] * NEAR
        keep = near + self.bits[second] * KEEP
        give = near + KEEP - self.bits[second] * KEEP
        return first, second, near, far, keep, give


def remote(source, target, send, receive, device):
    return pltpu.make_async_remote_copy(
        src_ref=source,
        dst_ref=target,
        send_sem=send,
        recv_sem=receive,
        device_id=device,
        device_id_type=MESH,
    )


def rows_at(start, count):
    return pl.ds(pl.multiple_of(start, 16), count)


class Spread:
    def __init__(self, place, owner, rank, slots, land, gift, sems):
        self.place, self.owner, self.rank = place, owner, rank
        self.slots, self.land, self.gift, self.sems = slots, land, gift, sems

    def cols(self, chunk):
        return pl.ds(GROUPS[chunk][0] * PAIR, GROUPS[chunk][1] * PAIR)

    def first_copy(self, chunk, index):
        first, second, near, far, keep, give = self.place.flow(index)
        return remote(
            self.slots.at[:, rows_at(far, NEAR), self.cols(chunk)],
            self.land[chunk].at[index],
            self.sems[0].at[chunk, index, 0],
            self.sems[1].at[chunk, index, 0],
            self.place.partners[first],
        )

    def second_copy(self, chunk, index, which):
        first, second, near, far, keep, give = self.place.flow(index)
        if which == 0:
            source = self.slots.at[:, rows_at(give, KEEP), self.cols(chunk)]
        else:
            source = self.land[chunk].at[index, :, rows_at(give - near, KEEP)]
        return remote(
            source,
            self.gift[chunk].at[index, pl.ds(which * CAP, CAP)],
            self.sems[0].at[chunk, index, 1 + which],
            self.sems[1].at[chunk, index, 1 + which],
            self.place.partners[second],
        )

    def step(self, chunk, index):
        for flow in range(FLOWS):
            if index == 0:
                self.first_copy(chunk, flow).start()
                self.second_copy(chunk, flow, 0).start()
            if index == 1:
                self.first_copy(chunk, flow).wait()
                self.second_copy(chunk, flow, 1).start()
            if index == 2:
                self.second_copy(chunk, flow, 0).wait()
                self.second_copy(chunk, flow, 1).wait()

    def piece(self, tile, index, chunk, start, count):
        first, second, near, far, keep, give = self.place.flow(index)
        owner, rank = self.owner[tile], self.rank[tile]
        bits = [lax.rem(owner, 2), lax.rem(owner // 2, 2)]
        apart = [bit != mine for bit, mine in zip(bits, self.place.bits)]
        cols = pl.ds(start, count)
        mine = self.slots[rank, rows_at(keep, KEEP), pl.ds(GROUPS[chunk][0] * PAIR + start, count)]
        firsts = self.land[chunk][index, rank, rows_at(keep - near, KEEP), cols]
        gifts = self.gift[chunk][index, jnp.where(apart[first], CAP, 0) + rank, :, cols]
        value = jnp.where(apart[second], gifts, jnp.where(apart[first], firsts, mine))
        layer = owner // 4 == self.place.me // 4
        return jnp.where(layer, value, jnp.zeros_like(value))


class Column:
    steps = 4

    def __init__(self, place, kept, land, sems):
        self.place, self.kept, self.land, self.sems = place, kept, land, sems

    def copy(self, index):
        device = self.place.across if index == 1 else self.place.partners[2]
        return remote(
            self.kept, self.land.at[index % 2], self.sems[0].at[index], self.sems[1].at[index], device
        )

    def add(self, index):
        self.kept[...] = (self.kept[...].astype(f32) + self.land[index].astype(f32)).astype(b16)


def both_flows(flow):
    return pl.ds(flow * KEEP, KEEP)


def column_step(place, column, index):
    @pl.when(place.inner)
    def inner():
        if index == 1:
            column.copy(0).wait_recv()
            column.add(0)
            column.copy(1).start()
        if index == 2:
            column.copy(1).wait()
            column.add(1)
            column.copy(2).start()
        if index == 3:
            column.copy(2).wait_send()

    @pl.when(jnp.logical_not(place.inner))
    def outer():
        if index == 0:
            column.copy(0).start()
        if index == 1:
            column.copy(0).wait_send()
        if index == 3:
            column.copy(2).wait_recv()
            column.kept[...] = column.land[0]


class Item:
    steps = 7

    def __init__(self, place, work, kept, land, sems, load, store=None):
        self.place, self.work, self.kept, self.land, self.sems = place, work, kept, land, sems
        self.load, self.store = load, store
        self.base = place.core * HALF

    def copy(self, flow, index):
        first, second, near, far, keep, give = self.place.flow(flow)
        kept = self.work.at[:, rows_at(self.base + keep, KEEP)]
        half = self.work.at[:, rows_at(self.base + near, NEAR)]
        source, device = [
            (kept, self.place.partners[second]),
            (half, self.place.partners[first]),
        ][index]
        number = 3 + 2 * flow + index
        return remote(source, source, self.sems[0].at[number], self.sems[1].at[number], device)

    def pair(self):
        rows = self.work.at[:, rows_at(self.base, HALF)]
        return remote(rows, rows, self.sems[0].at[7], self.sems[1].at[7], self.place.twin)

    def step(self, index):
        if index == 0:
            for flow in range(FLOWS):
                self.load(self.kept, both_flows(flow), flow)
        if index <= 3:
            column_step(self.place, Column(self.place, self.kept, self.land, self.sems), index)
        for flow in range(FLOWS):
            if index == 3:
                rows = rows_at(self.base + self.place.flow(flow)[4], KEEP)
                self.work[:, rows] = self.kept[:, both_flows(flow)]
            if 4 <= index <= 5:
                self.copy(flow, index - 4).wait()
            if 3 <= index <= 4:
                self.copy(flow, index - 3).start()
        if index == 5:
            self.pair().start()
        if index == 6:
            self.pair().wait()
            self.store().start()


REST_GROUPS = tuple((index, 1) for index in range(REST))
PAIR_CHUNK = (0, 1, 1, 2, 2, 2)
FRONT_PAIRS = (2, 4, 5, 6, 7, 8)
FRONT_REST = (6, 7, 8, 9, 10, 11, 12, 13, 14)
FRONT_LEAD = 9
FRONT_PHASES = 4


def front_kernel(
    owner, lengths, master, vec_ref, x_in, c_in,
    x_out, c_out, n_out, one_out, two_out, q_ref, k_ref, v_ref, p_ref, r_ref, o_ref, ctx_ref,
    rank, rows_ref, normed, keys, turned_values, scores, slots,
    land_one, land_two, land_three, gift_one, gift_two, gift_three,
    one, one_kept, one_land, two, two_kept, two_land,
    spread_send, spread_recv, one_send, one_recv, two_send, two_recv,
    swap_send, swap_recv, swap_local, store_sem,
):
    pair = pl.program_id(0)
    row = pl.program_id(1)
    grid_step = pair * 2 + row
    place = Place()
    rows, span = x_in.shape[0] // 2, x_in.shape[1]
    land = (land_one, land_two, land_three)
    gift = (gift_one, gift_two, gift_three)
    spread = Spread(place, owner, rank, slots, land, gift, (spread_send, spread_recv))

    def swaps(index):
        source, target = [(x_in, rows_ref), (c_in, c_out)][index]
        here = pl.ds(place.core * span, span)
        near = pltpu.make_async_copy(
            source.at[pl.ds(place.core * rows, rows)], target.at[:, here], swap_local.at[index]
        )
        far = remote(
            source.at[pl.ds(place.other * rows, rows)],
            target.at[:, here],
            swap_send.at[index],
            swap_recv.at[index],
            place.twin,
        )
        return near, far

    def row_store():
        return pltpu.make_async_copy(rows_ref, x_out, store_sem.at[PAIRS + REST])

    def normed_store():
        return pltpu.make_async_copy(normed, n_out, store_sem.at[PAIRS + REST + 1])

    def pair_item(group):
        span_of = pl.ds(group, 1)

        def load(work, where, flow):
            chunk = PAIR_CHUNK[group]
            for tile in range(3):
                part = spread.piece(tile, flow, chunk, (group - GROUPS[chunk][0]) * PAIR, PAIR)
                work[0, where, pl.ds(tile * PAIR, PAIR)] = part

        def store():
            return pltpu.make_async_copy(one.at[span_of], one_out.at[span_of], store_sem.at[group])

        sems = (one_send.at[group], one_recv.at[group])
        return Item(place, one.at[span_of], one_kept.at[span_of], one_land.at[:, span_of], sems, load, store)

    def rest_item(group):
        first, count = REST_GROUPS[group]
        span_of = pl.ds(first, count)

        def load(work, where, flow):
            for index in range(count):
                for chunk, (start, wide) in enumerate(GROUPS):
                    part = spread.piece(3 + first + index, flow, chunk, 0, wide * PAIR)
                    work[index, where, pl.ds(start * PAIR, wide * PAIR)] = part

        def store():
            return pltpu.make_async_copy(
                two.at[span_of], two_out.at[span_of], store_sem.at[PAIRS + group]
            )

        sems = (two_send.at[group], two_recv.at[group])
        return Item(place, two.at[span_of], two_kept.at[span_of], two_land.at[:, span_of], sems, load, store)

    def tick(number, phase):
        for chunk in range(CHUNKS):
            if phase == 0 and 0 <= number - 2 * chunk <= 2:
                spread.step(chunk, number - 2 * chunk)
        for index, start in enumerate(FRONT_PAIRS):
            if index % 2 * 2 == phase and 0 <= number - start < Item.steps:
                pair_item(index).step(number - start)
        for index, start in enumerate(FRONT_REST):
            if (index + 1) % FRONT_PHASES == phase and 0 <= number - start < Item.steps:
                rest_item(index).step(number - start)

    def both(number):
        for phase in range(FRONT_PHASES):
            tick(number, phase)

    @pl.when(grid_step == 0)
    def lead():
        slots[...] = master[...].astype(b16)
        for tile in range(PIECES):
            count = jnp.int32(0)
            for before in range(tile):
                count = count + (owner[before] == owner[tile]).astype(jnp.int32)
            rank[tile] = jnp.minimum(count, CAP - 1)
        place.greet()
        for copy in swaps(0):
            copy.start()
        both(0)
        for copy in swaps(1):
            copy.start()
        for copy in swaps(0):
            copy.wait()
        row_store().start()

        def norm_rows(index, carry):
            for part in range(rows):
                for block in range(4):
                    where = pl.ds(pl.multiple_of(index * 128 + block * 32, 32), 32)
                    unit, unused = norm_parts(rows_ref[part, where].astype(f32))
                    low = (unit * vec_ref[0:1, :] + vec_ref[1:2, :]).astype(b16)
                    normed[pl.ds(pl.multiple_of(part * LEN + index * 128 + block * 32, 32), 32)] = low
            return carry

        both(1)
        lax.fori_loop(0, LEN // 128, norm_rows, 0)
        normed_store().start()
        for number in range(2, FRONT_LEAD):
            both(number)

    for number in range(2 * PAIRS):
        pl.when(grid_step == number)(partial(tick, FRONT_LEAD + number, 0))

    @pl.when(row == 0)
    def project():
        lanes = pl.ds(pl.multiple_of(pair * PAIR, PAIR), PAIR)
        weight = one[pair]

        def part(index, carry):
            where = pl.ds(pl.multiple_of(index * 512, 512), 512)
            both = dot_nn(normed[where], weight)
            queries = both[:, :PAIR] + vec_ref[4:5, lanes]
            queries = (queries * (HEAD_DIM**-0.5 * LOG2E)).astype(b16)
            q_ref[:, where] = queries.T
            low = both[:, PAIR : 2 * PAIR].astype(b16)
            keys[where] = low
            k_ref[:, where] = low.T
            values = (both[:, 2 * PAIR :] + vec_ref[5:6, lanes]).astype(b16)
            v_ref[where] = values
            turned_values[:, where] = values.T
            return carry

        lax.fori_loop(0, normed.shape[0] // 512, part, 0)

    half = LEN // 2
    start = pl.multiple_of(row * LEN, LEN)
    split = lengths[place.core * rows + row, 0] < LEN
    shift = jnp.where(split, jnp.float32(-1e30), jnp.float32(0.0))

    quarter = LEN // 4
    units = [(head, step) for head in range(2) for step in range(2)]

    def score_block(unit, block, peak):
        head, step = units[unit]
        rows_here = pl.ds(pl.multiple_of(start + block * quarter, quarter), quarter)
        queries = q_ref[:, pl.ds(pl.multiple_of(start + step * half, half), half)]
        raw = dot_nn(head_only(keys[rows_here], head), queries)
        if block // 2 != step:
            raw = raw + shift
        scores[unit % 2, block * quarter : (block + 1) * quarter] = raw
        best = jnp.max(raw.reshape(-1, 8, half), axis=0)
        return best if peak is None else jnp.maximum(peak, best)

    def context_block(unit, block, total):
        head, step = units[unit]
        part = slice(head * HEAD_DIM, (head + 1) * HEAD_DIM)
        cols = pl.ds(pl.multiple_of(start + block * quarter, quarter), quarter)
        here = slice(step * half, (step + 1) * half)
        term = dot_nn(
            turned_values[part, cols], p_ref[head, block * quarter : (block + 1) * quarter, here]
        )
        return term if total is None else total + term

    def context_store(unit, total, recip):
        head, step = units[unit]
        part = slice(head * HEAD_DIM, (head + 1) * HEAD_DIM)
        o_ref[part, step * half : (step + 1) * half] = (total * recip).astype(b16)

    peak = None
    for block in range(4):
        peak = score_block(0, block, peak)
    before = None
    for unit, (head, step) in enumerate(units):
        if unit > 0:
            for number in range(2 * PAIRS):
                pl.when(grid_step == number)(partial(tick, FRONT_LEAD + number, unit))
        here = slice(step * half, (step + 1) * half)
        top = jnp.max(peak, 0, keepdims=True)
        total = jnp.zeros((8, half), f32)
        peak, context = None, None
        for block in range(4):
            if unit + 1 < len(units):
                peak = score_block(unit + 1, block, peak)
            for small in range(4 * block, 4 * block + 4):
                rows_here = slice(small * 64, (small + 1) * 64)
                value = jnp.exp2(scores[unit % 2, rows_here] - top)
                total = total + jnp.sum(value.reshape(-1, 8, half), axis=0)
                p_ref[head, rows_here, here] = value.astype(b16)
            if unit > 0:
                context = context_block(unit - 1, block, context)
        if unit > 0:
            context_store(unit - 1, context, before)
        before = 1.0 / jnp.sum(total, 0, keepdims=True)
        r_ref[0, head : head + 1, here] = before
    context = None
    for block in range(4):
        context = context_block(3, block, context)
    context_store(3, context, before)
    ctx_ref[...] = o_ref[...].T

    @pl.when(grid_step == 2 * PAIRS - 1)
    def finish_copies():
        for copy in swaps(1):
            copy.wait()
        row_store().wait()
        normed_store().wait()
        for group in range(PAIRS):
            pair_item(group).store().wait()
        for group in range(REST):
            rest_item(group).store().wait()


def front(owner, lengths, master, vectors, inputs, cotangent):
    rows, span = inputs.shape[0] // 2, inputs.shape[1]
    tokens = rows * LEN
    any_spec = pl.BlockSpec(memory_space=pl.ANY)
    smem = pl.BlockSpec(memory_space=pltpu.SMEM)
    whole = jax.ShapeDtypeStruct((rows, LEN, D), b16)
    dma = pltpu.SemaphoreType.DMA
    return pl.pallas_call(
        front_kernel,
        grid=(PAIRS, rows),
        in_specs=[
            smem,
            smem,
            pl.BlockSpec((CAP, HALF, D), lambda h, r: (0, 0, 0), pipeline_mode=pl.Buffered(1)),
            pl.BlockSpec((PIECES, D), lambda h, r: (0, 0)),
            any_spec,
            any_spec,
        ],
        out_specs=[any_spec] * 5
        + [
            pl.BlockSpec((PAIR, tokens), lambda h, r: (h, 0)),
            pl.BlockSpec((PAIR, tokens), lambda h, r: (h, 0)),
            pl.BlockSpec((tokens, PAIR), lambda h, r: (0, h)),
            pl.BlockSpec((2, LEN, LEN), lambda h, r: (h * 2 + r, 0, 0)),
            pl.BlockSpec((1, 2, LEN), lambda h, r: (h * 2 + r, 0, 0)),
            pl.BlockSpec((PAIR, LEN), lambda h, r: (h, r)),
            pl.BlockSpec((LEN, PAIR), lambda h, r: (r, h)),
        ],
        out_shape=[
            whole,
            whole,
            jax.ShapeDtypeStruct((tokens, D), b16),
            jax.ShapeDtypeStruct((PAIRS, D, WIDE), b16),
            jax.ShapeDtypeStruct((REST, D, D), b16),
            jax.ShapeDtypeStruct((D, tokens), b16),
            jax.ShapeDtypeStruct((D, tokens), b16),
            jax.ShapeDtypeStruct((tokens, D), b16),
            jax.ShapeDtypeStruct((rows * HEADS, LEN, LEN), b16),
            jax.ShapeDtypeStruct((rows * PAIRS, 2, LEN), f32),
            jax.ShapeDtypeStruct((D, tokens), b16),
            jax.ShapeDtypeStruct((tokens, D), b16),
        ],
        scratch_shapes=[
            pltpu.SMEM((PIECES,), jnp.int32),
            pltpu.VMEM((rows, LEN, D), b16),
            pltpu.VMEM((tokens, D), b16),
            pltpu.VMEM((tokens, PAIR), b16),
            pltpu.VMEM((PAIR, tokens), b16),
            pltpu.VMEM((2, LEN, LEN // 2), f32),
            pltpu.VMEM((CAP, HALF, D), b16),
        ]
        + [pltpu.VMEM((FLOWS, CAP, NEAR, wide * PAIR), b16) for unused, wide in GROUPS]
        + [pltpu.VMEM((FLOWS, 2 * CAP, KEEP, wide * PAIR), b16) for unused, wide in GROUPS]
        + [
            pltpu.VMEM((PAIRS, D, WIDE), b16),
            pltpu.VMEM((PAIRS, NEAR, WIDE), b16),
            pltpu.VMEM((2, PAIRS, NEAR, WIDE), b16),
            pltpu.VMEM((REST, D, D), b16),
            pltpu.VMEM((REST, NEAR, D), b16),
            pltpu.VMEM((2, REST, NEAR, D), b16),
            dma((CHUNKS, FLOWS, 3)),
            dma((CHUNKS, FLOWS, 3)),
            dma((PAIRS, 8)),
            dma((PAIRS, 8)),
            dma((REST, 8)),
            dma((REST, 8)),
            dma((2,)),
            dma((2,)),
            dma((2,)),
            dma((PAIRS + REST + 2,)),
        ],
        compiler_params=pltpu.CompilerParams(
            collective_id=0, has_side_effects=True, vmem_limit_bytes=60 * MIB
        ),
        name="front",
    )(owner, lengths, master, vectors, inputs, cotangent)


class Sum:
    steps = 7

    def __init__(self, place, work, kept, wide, narrow, land, sems, send_pair, add_own):
        self.place, self.work, self.kept, self.sems = place, work, kept, sems
        self.wide, self.narrow, self.land = wide, narrow, land
        self.send_pair, self.add_own = send_pair, add_own

    def copy(self, flow, index):
        first, second, near, far, keep, give = self.place.flow(flow)
        source, target, device = [
            (self.work.at[:, rows_at(far, NEAR)], self.wide.at[flow], first),
            (self.work.at[:, rows_at(give, KEEP)], self.narrow.at[flow], second),
        ][index]
        number = 3 + 2 * flow + index
        return remote(
            source,
            target,
            self.sems[0].at[number],
            self.sems[1].at[number],
            self.place.partners[device],
        )

    def step(self, index):
        if index == 0:
            self.send_pair().start()
        if index == 1:
            self.send_pair().wait()
            self.add_own()
        for flow in range(FLOWS):
            first, second, near, far, keep, give = self.place.flow(flow)
            if index == 1:
                self.copy(flow, 0).start()
            if index == 2:
                self.copy(flow, 0).wait()
                rows = rows_at(near, NEAR)
                total = self.work[:, rows].astype(f32) + self.wide[flow].astype(f32)
                self.work[:, rows] = total.astype(b16)
                self.copy(flow, 1).start()
            if index == 3:
                self.copy(flow, 1).wait()
                total = self.work[:, rows_at(keep, KEEP)].astype(f32) + self.narrow[flow].astype(f32)
                self.kept[:, both_flows(flow)] = total.astype(b16)
        if index >= 3:
            column_step(self.place, Column(self.place, self.kept, self.land, self.sems), index - 3)


class Gather:
    steps = 3

    def __init__(self, place, work, kept, narrow, wide, sems):
        self.place, self.work, self.kept = place, work, kept
        self.narrow, self.wide, self.sems = narrow, wide, sems

    def copy(self, flow, index):
        first, second, near, far, keep, give = self.place.flow(flow)
        source, target, device = [
            (self.kept.at[:, both_flows(flow)], self.narrow, second),
            (self.work.at[:, rows_at(near, NEAR)], self.wide, first),
        ][index]
        number = 7 + 2 * flow + index
        return remote(
            source,
            target.at[flow],
            self.sems[0].at[number],
            self.sems[1].at[number],
            self.place.partners[device],
        )

    def step(self, index):
        for flow in range(FLOWS):
            first, second, near, far, keep, give = self.place.flow(flow)
            if index == 0:
                self.work[:, rows_at(keep, KEEP)] = self.kept[:, both_flows(flow)]
            if index > 0:
                self.copy(flow, index - 1).wait()
            if index == 1:
                self.work[:, rows_at(give, KEEP)] = self.narrow[flow]
            if index == 2:
                self.work[:, rows_at(far, NEAR)] = self.wide[flow]
            if index < 2:
                self.copy(flow, index).start()


class Hand:
    steps = 3

    def __init__(self, place, table, kept, bag, gift, pack, last, own, out, sems, store_sems):
        self.place, self.table, self.kept = place, table, kept
        self.bag, self.gift, self.pack, self.last, self.own = bag, gift, pack, last, own
        self.out, self.sems, self.store_sems = out, sems, store_sems

    def tile(self, chip, rank, flow):
        return self.kept[self.table[chip * CAP + rank], both_flows(flow)]

    def copy(self, flow, index):
        first, second = self.place.flow(flow)[:2]
        source, target, device = [
            (self.bag.at[flow], self.gift.at[flow], second),
            (self.pack.at[flow], self.last.at[flow], first),
        ][index]
        return remote(
            source,
            target,
            self.sems[0].at[flow, index],
            self.sems[1].at[flow, index],
            self.place.partners[device],
        )

    def stores(self, flow):
        first, second, near, far, keep, give = self.place.flow(flow)
        parts = [
            (self.own.at[flow], rows_at(keep, KEEP)),
            (self.gift.at[flow, pl.ds(0, CAP)], rows_at(give, KEEP)),
            (self.last.at[flow], rows_at(far, NEAR)),
        ]
        return [
            pltpu.make_async_copy(source, self.out.at[:, rows], self.store_sems.at[flow, index])
            for index, (source, rows) in enumerate(parts)
        ]

    def step(self, index):
        for flow in range(FLOWS):
            first, second, near, far, keep, give = self.place.flow(flow)
            if index == 0:
                beside = self.place.chips[second]
                across = beside + self.place.chips[first] - self.place.me
                for rank in range(CAP):
                    self.bag[flow, rank] = self.tile(beside, rank, flow)
                    self.bag[flow, CAP + rank] = self.tile(across, rank, flow)
                    self.own[flow, rank] = self.tile(self.place.me, rank, flow)
                self.copy(flow, 0).start()
            if index == 1:
                self.copy(flow, 0).wait()
                for rank in range(CAP):
                    mine = self.tile(self.place.chips[first], rank, flow)
                    self.pack[flow, rank, rows_at(keep - near, KEEP)] = mine
                    self.pack[flow, rank, rows_at(give - near, KEEP)] = self.gift[flow, CAP + rank]
                self.copy(flow, 1).start()
            if index == 2:
                self.copy(flow, 1).wait()
                for copy in self.stores(flow):
                    copy.start()


BACK_STEPS = 2 * PAIRS
BACK_TAIL = 4
BACK_PAIRS = tuple((index, 1) for index in range(PAIRS))
BACK_REST = (0, 1, 2, 3, 4, 5, 6, 7, 8)
BACK_HAND = 15
BACK_PHASES = 3


def back_kernel(
    table, p_ref, r_ref, v_ref, q_ref, k_ref, o_ref, g_ref, w_ref, n_ref, x_ref, z_ref, vec_ref,
    tiles_in, sums_in, y_in,
    y_out, i_out, pairs_out, slots_out, sums_ref,
    grad_sum, wide_sum, turned, slopes, block_out,
    two, two_kept, two_wide, two_narrow, two_land, two_stage,
    one, one_kept, one_wide, one_narrow, one_land, one_send_stage, one_stage,
    gather_narrow, gather_wide,
    bag, gift, pack, last, own, vec_land,
    two_send, two_recv, one_send, one_recv, hand_send, hand_recv, hand_store,
    pair_two_send, pair_two_recv, pair_one_send, pair_one_recv, load_sem, store_sem,
    swap_send, swap_recv, swap_local, vec_send, vec_recv,
):
    step = pl.program_id(0)
    place = Place()
    rows, span = y_in.shape[0], y_in.shape[1] // 2
    near_half = rows_at(place.core * HALF, HALF)
    far_half = rows_at(place.other * HALF, HALF)

    def load_two(group):
        first, count = REST_GROUPS[group]
        return pltpu.make_async_copy(
            tiles_in.at[pl.ds(first, count), near_half],
            two_stage.at[pl.ds(group % 2, 1)],
            load_sem.at[group % 2],
        )

    def rest_sum(group):
        first, count = REST_GROUPS[group]
        span_of = pl.ds(first, count)
        work = two.at[span_of]

        def send_pair():
            return remote(
                tiles_in.at[span_of, far_half],
                work,
                pair_two_send.at[group],
                pair_two_recv.at[group],
                place.twin,
            )

        def add_own():
            load_two(group).wait()
            work[...] = (work[...].astype(f32) + two_stage[group % 2].astype(f32)).astype(b16)

        sems = (two_send.at[group], two_recv.at[group])
        parts = (two_kept.at[span_of], two_wide.at[:, span_of], two_narrow.at[:, span_of])
        return Sum(place, work, *parts, two_land.at[:, span_of], sems, send_pair, add_own)

    def pair_sum(group):
        first, count = BACK_PAIRS[group]
        span_of = pl.ds(first, count)
        work = one.at[span_of]

        def send_pair():
            return remote(
                one_send_stage.at[pl.ds(group % 2, 1)],
                work,
                pair_one_send.at[group],
                pair_one_recv.at[group],
                place.twin,
            )

        def add_own():
            own = one_stage[group % 2].astype(f32)
            work[...] = (work[...].astype(f32) + own).astype(b16)

        sems = (one_send.at[group], one_recv.at[group])
        parts = (one_kept.at[span_of], one_wide.at[:, span_of], one_narrow.at[:, span_of])
        return Sum(place, work, *parts, one_land.at[:, span_of], sems, send_pair, add_own)

    def pair_gather(group):
        first, count = BACK_PAIRS[group]
        span_of = pl.ds(first, count)
        sems = (one_send.at[group], one_recv.at[group])
        narrow, wide = gather_narrow.at[:, span_of], gather_wide.at[:, span_of]
        return Gather(place, one.at[span_of], one_kept.at[span_of], narrow, wide, sems)

    hand = Hand(
        place, table, two_kept, bag, gift, pack, last, own, slots_out, (hand_send, hand_recv), hand_store
    )

    def pair_store(index, tile):
        return pltpu.make_async_copy(
            one.at[index, :, pl.ds(tile * PAIR, PAIR)],
            pairs_out.at[tile, :, pl.ds(index * PAIR, PAIR)],
            store_sem.at[index, tile],
        )

    def tick(number, phase):
        for index, start in enumerate(BACK_REST):
            if (index + 1) % BACK_PHASES == phase and 0 <= number - start < Sum.steps:
                rest_sum(index).step(number - start)
        for index in range(PAIRS):
            start = 2 * index + 2
            if index % 2 != phase:
                continue
            if 0 <= number - start < Sum.steps:
                pair_sum(index).step(number - start)
            if 0 <= number - start - Sum.steps + 1 < Gather.steps:
                pair_gather(index).step(number - start - Sum.steps + 1)
            if number == start + Sum.steps + 1:
                for tile in range(3):
                    pair_store(index, tile).start()
        if phase == 0 and 0 <= number - BACK_HAND < Hand.steps:
            hand.step(number - BACK_HAND)
        for index, start in enumerate(BACK_REST):
            if phase == BACK_PHASES - 1 and number == max(start - 1, 0):
                load_two(index).start()

    def both(number):
        for phase in range(BACK_PHASES):
            tick(number, phase)

    def swap_y(index):
        there = pl.ds(place.core * rows, rows)
        if index == 0:
            return pltpu.make_async_copy(
                y_in.at[:, pl.ds(place.core * span, span)], y_out.at[there], swap_local.at[0]
            )
        return remote(
            y_in.at[:, pl.ds(place.other * span, span)],
            y_out.at[there],
            swap_send.at[0],
            swap_recv.at[0],
            place.twin,
        )

    @pl.when(step == 0)
    def lead():
        place.greet()
        for index in range(2):
            swap_y(index).start()
        sums_ref[...] = sums_in[...]

    for number in range(BACK_STEPS + BACK_TAIL):
        early = partial(tick, number, 0) if number < BACK_STEPS else partial(both, number)
        pl.when(step == number)(early)

    half = LEN // 2
    pair, row = step // 2, lax.rem(step, 2)

    quarter = LEN // 4

    def attention_inputs(head):
        part = slice(head * HEAD_DIM, (head + 1) * HEAD_DIM)
        values = head_only(v_ref[...], head)
        recip = r_ref[0, head : head + 1, :]
        grad = g_ref[part, :].astype(f32) * recip
        delta = jnp.sum(grad * o_ref[part, :].astype(f32), 0, keepdims=True)
        grad = grad.astype(b16)
        return values, grad, delta, jnp.concatenate([grad, grad], axis=0)

    def attention(head):
        part = slice(head * HEAD_DIM, (head + 1) * HEAD_DIM)
        values, grad, delta, doubled = attention_inputs(head)
        units = [(which, block) for which in range(2) for block in range(4)]
        value_grad, key_grad, query_grad = {}, {}, {}

        def raw_block(unit):
            which, block = units[unit]
            cols = slice(which * half, (which + 1) * half)
            return dot_nn(values[block * quarter : (block + 1) * quarter], doubled[:, cols])

        def slope_block(unit, raw):
            which, block = units[unit]
            cols = slice(which * half, (which + 1) * half)
            for small in range(4):
                rows_here = slice(small * 64, (small + 1) * 64)
                rows_all = slice(block * quarter + small * 64, block * quarter + (small + 1) * 64)
                slope = p_ref[head, rows_all, cols].astype(f32) * (raw[rows_here] - delta[:, cols])
                slopes[unit % 2, rows_here] = slope.astype(b16)

        def add(totals, key, term):
            totals[key] = totals[key] + term if key in totals else term

        def grad_block(unit):
            which, block = units[unit]
            cols = slice(which * half, (which + 1) * half)
            rows_all = slice(block * quarter, (block + 1) * quarter)
            slope = slopes[unit % 2]
            add(value_grad, block, dot_nt(grad[:, cols], p_ref[head, rows_all, cols]))
            add(key_grad, block, dot_nt(q_ref[part, cols], slope))
            add(query_grad, which, dot_nn(k_ref[part, rows_all], slope))

        raw = raw_block(0)
        for unit in range(len(units)):
            after = raw_block(unit + 1) if unit + 1 < len(units) else None
            slope_block(unit, raw)
            if unit > 0:
                grad_block(unit - 1)
            raw = after
        grad_block(len(units) - 1)
        for which in range(2):
            total = query_grad[which] * (HEAD_DIM**-0.5)
            turned[part, which * half : (which + 1) * half] = total.astype(b16)
        for block in range(4):
            rows_all = slice(block * quarter, (block + 1) * quarter)
            lower = slice(PAIR + head * HEAD_DIM, PAIR + (head + 1) * HEAD_DIM)
            turned[lower, rows_all] = (key_grad[block] * (1.0 / LOG2E)).astype(b16)
            lower = slice(2 * PAIR + head * HEAD_DIM, 2 * PAIR + (head + 1) * HEAD_DIM)
            turned[lower, rows_all] = value_grad[block].astype(b16)

    @pl.when(step < BACK_STEPS)
    def first_head():
        attention(0)

    for number in range(BACK_STEPS):
        pl.when(step == number)(partial(tick, number, 1))

    @pl.when(step < BACK_STEPS)
    def second_head():
        attention(1)

    for number in range(BACK_STEPS):
        pl.when(step == number)(partial(tick, number, 2))

    @pl.when(step < BACK_STEPS)
    def weight_grads():
        where = pl.ds(pl.multiple_of(row * LEN, LEN), LEN)
        block = dot_nn(turned[...], n_ref[where])
        back = turned[...].T
        lanes = pl.ds(pl.multiple_of(pair * PAIR, PAIR), PAIR)
        ones = jnp.sum(back.astype(f32), 0, keepdims=True)
        sums_ref[4:5, lanes] += ones[:, :PAIR]
        sums_ref[5:6, lanes] += ones[:, 2 * PAIR :]
        term = dot_nt(back, w_ref[0])

        @pl.when(pair == 0)
        def begin():
            grad_sum[where] = term

        @pl.when(pair > 0)
        def add():
            grad_sum[where] += term

        @pl.when(row == 0)
        def keep():
            wide_sum[...] = block

        @pl.when(row == 1)
        def hand_on():
            whole = (wide_sum[...] + block).T
            low = whole.astype(b16)
            for core in range(2):

                @pl.when(place.core == core)
                def split():
                    slot = lax.rem(pair, 2)
                    one_stage[slot] = low[core * HALF : (core + 1) * HALF]
                    one_send_stage[slot] = low[(1 - core) * HALF : (2 - core) * HALF]

    def store_block(index):
        row, half = index // 2, index % 2
        target = i_out.at[place.core * rows + row]
        local = pltpu.make_async_copy(block_out.at[half], target, swap_local.at[1 + row])
        far = remote(
            block_out.at[half], target, swap_send.at[1 + row], swap_recv.at[1 + row], place.twin
        )
        return local, far, half

    def wait_block(index):
        local, far, half = store_block(index)

        @pl.when(place.core == half)
        def keep():
            local.wait()

        @pl.when(place.core != half)
        def give():
            far.wait()

    for index in range(BACK_TAIL):

        @pl.when(step == BACK_STEPS + index)
        def close():
            size = LEN // 2
            if index >= 2:
                wait_block(index - 2)
            gain_sum = jnp.zeros((8, D), f32)
            shift_sum = jnp.zeros((8, D), f32)
            for block in range(size // 16):
                rows_here = slice(block * 16, (block + 1) * 16)
                grad = grad_sum[index * size + block * 16 : index * size + (block + 1) * 16]
                unit, rstd = norm_parts(x_ref[rows_here].astype(f32))
                gain_sum = gain_sum + jnp.sum((grad * unit).reshape(-1, 8, D), axis=0)
                shift_sum = shift_sum + jnp.sum(grad.reshape(-1, 8, D), axis=0)
                total = norm_back(grad, unit, rstd, vec_ref[0:1, :])
                block_out[index % 2, rows_here] = (z_ref[rows_here].astype(f32) + total).astype(b16)
            sums_ref[0:1, :] += jnp.sum(gain_sum, 0, keepdims=True)
            sums_ref[1:2, :] += jnp.sum(shift_sum, 0, keepdims=True)
            local, far, half = store_block(index)

            @pl.when(place.core == half)
            def keep():
                local.start()

            @pl.when(place.core != half)
            def give():
                far.start()

    @pl.when(step == BACK_STEPS + BACK_TAIL - 1)
    def drain():
        devices = [place.twin] + place.partners

        def vector(index):
            return remote(
                sums_ref, vec_land.at[index], vec_send.at[index], vec_recv.at[index], devices[index]
            )

        vector(0).start()
        for number in range(BACK_STEPS + BACK_TAIL, BACK_STEPS + Sum.steps + Gather.steps):
            both(number)
            index = number - BACK_STEPS - BACK_TAIL
            if index < 5:
                vector(index).wait()
                sums_ref[...] += vec_land[index]
                if index < 4:
                    vector(index + 1).start()
        for index in range(2):
            swap_y(index).wait()
        for index in range(2, BACK_TAIL):
            wait_block(index)
        for index in range(PAIRS):
            for tile in range(3):
                pair_store(index, tile).wait()
        for flow in range(FLOWS):
            for copy in hand.stores(flow):
                copy.wait()


def back(table, attention, weights, normed, x, residual, vectors, tiles, sums, y):
    rows, length = y.shape[:2]
    tokens = rows * length
    any_spec = pl.BlockSpec(memory_space=pl.ANY)
    smem = pl.BlockSpec(memory_space=pltpu.SMEM)
    dma = pltpu.SemaphoreType.DMA

    def now(step):
        return jnp.minimum(step, BACK_STEPS - 1)

    def tail(step):
        return jnp.maximum(step - BACK_STEPS, 0)

    head_block = pl.BlockSpec((PAIR, LEN), lambda s: (now(s) // 2, lax.rem(now(s), 2)))
    tail_block = pl.BlockSpec((LEN // 2, D), lambda s: (tail(s), 0))
    whole = pl.BlockSpec((PIECES, D), lambda s: (0, 0))
    sums_block = pl.BlockSpec((16, D), lambda s: (0, 0))
    return pl.pallas_call(
        back_kernel,
        grid=(BACK_STEPS + BACK_TAIL,),
        in_specs=[
            smem,
            pl.BlockSpec((2, LEN, LEN), lambda s: (now(s), 0, 0)),
            pl.BlockSpec((1, 2, LEN), lambda s: (now(s), 0, 0)),
            pl.BlockSpec((LEN, PAIR), lambda s: (lax.rem(now(s), 2), now(s) // 2)),
            head_block,
            head_block,
            head_block,
            head_block,
            pl.BlockSpec((1, D, WIDE), lambda s: (now(s) // 2, 0, 0)),
            pl.BlockSpec((tokens, D), lambda s: (0, 0), pipeline_mode=pl.Buffered(1)),
            tail_block,
            tail_block,
            whole,
            any_spec,
            sums_block,
            any_spec,
        ],
        out_specs=[any_spec] * 4 + [sums_block],
        out_shape=[
            jax.ShapeDtypeStruct((2 * rows, length // 2, D), b16),
            jax.ShapeDtypeStruct((2 * rows, length // 2, D), b16),
            jax.ShapeDtypeStruct((3, HALF, D), b16),
            jax.ShapeDtypeStruct((CAP, HALF, D), b16),
            jax.ShapeDtypeStruct((16, D), f32),
        ],
        scratch_shapes=[
            pltpu.VMEM((tokens, D), f32),
            pltpu.VMEM((WIDE, D), f32),
            pltpu.VMEM((WIDE, LEN), b16),
            pltpu.VMEM((2, LEN // 4, LEN // 2), b16),
            pltpu.VMEM((2, LEN // 2, D), b16),
            pltpu.VMEM((REST, HALF, D), b16),
            pltpu.VMEM((REST, NEAR, D), b16),
            pltpu.VMEM((FLOWS, REST, NEAR, D), b16),
            pltpu.VMEM((FLOWS, REST, KEEP, D), b16),
            pltpu.VMEM((2, REST, NEAR, D), b16),
            pltpu.VMEM((2, HALF, D), b16),
            pltpu.VMEM((PAIRS, HALF, WIDE), b16),
            pltpu.VMEM((PAIRS, NEAR, WIDE), b16),
            pltpu.VMEM((FLOWS, PAIRS, NEAR, WIDE), b16),
            pltpu.VMEM((FLOWS, PAIRS, KEEP, WIDE), b16),
            pltpu.VMEM((2, PAIRS, NEAR, WIDE), b16),
            pltpu.VMEM((2, HALF, WIDE), b16),
            pltpu.VMEM((2, HALF, WIDE), b16),
            pltpu.VMEM((FLOWS, PAIRS, KEEP, WIDE), b16),
            pltpu.VMEM((FLOWS, PAIRS, NEAR, WIDE), b16),
            pltpu.VMEM((FLOWS, 2 * CAP, KEEP, D), b16),
            pltpu.VMEM((FLOWS, 2 * CAP, KEEP, D), b16),
            pltpu.VMEM((FLOWS, CAP, NEAR, D), b16),
            pltpu.VMEM((FLOWS, CAP, NEAR, D), b16),
            pltpu.VMEM((FLOWS, CAP, KEEP, D), b16),
            pltpu.VMEM((5, 16, D), f32),
            dma((REST, 7)),
            dma((REST, 7)),
            dma((PAIRS, 11)),
            dma((PAIRS, 11)),
            dma((FLOWS, 2)),
            dma((FLOWS, 2)),
            dma((FLOWS, 3)),
            dma((REST,)),
            dma((REST,)),
            dma((PAIRS,)),
            dma((PAIRS,)),
            dma((3,)),
            dma((PAIRS, 3)),
            dma((3,)),
            dma((3,)),
            dma((3,)),
            dma((5,)),
            dma((5,)),
        ],
        compiler_params=pltpu.CompilerParams(
            collective_id=1, has_side_effects=True, vmem_limit_bytes=62 * MIB
        ),
        name="back",
    )(table, *attention, weights, normed, x, residual, vectors, tiles, sums, y)


def update_kernel(tile_at, one, two, w_ref, m_ref, s_ref, y_in, i_in, w_out, m_out, s_out, y_out, i_out):
    step = pl.program_id(0)
    tile = tile_at[step // 2]
    grad = jnp.where(tile < 3, one[0], two[0]).astype(f32)
    parts = adam_step(w_ref[0], grad, m_ref[0], s_ref[0], RATE)
    for target, part in zip((w_out, m_out, s_out), parts):
        target[0] = jnp.where(tile >= 0, part, jnp.zeros_like(part))

    @pl.when(step < 4)
    def widen():
        y_out[...] = y_in[...].astype(f32)
        i_out[...] = i_in[...].astype(f32)


def update(tile_at, one, two, master, first, second, y, grad):
    tokens = y.shape[0]
    size = HALF // 2
    state = pl.BlockSpec((1, size, D), lambda s, tile_at: (s // 2, lax.rem(s, 2), 0))
    wide = pl.BlockSpec((tokens // 4, D), lambda s, tile_at: (jnp.minimum(s, 3), 0))
    return pl.pallas_call(
        update_kernel,
        grid_spec=pltpu.PrefetchScalarGridSpec(
            num_scalar_prefetch=1,
            grid=(CAP * 2,),
            in_specs=[
                pl.BlockSpec(
                    (1, size, D),
                    lambda s, tile_at: (jnp.clip(tile_at[s // 2], 0, 2), lax.rem(s, 2), 0),
                ),
                state,
                state,
                state,
                state,
                wide,
                wide,
            ],
            out_specs=[state] * 3 + [wide] * 2,
        ),
        out_shape=[jax.ShapeDtypeStruct(master.shape, f32)] * 3
        + [jax.ShapeDtypeStruct((tokens, D), f32)] * 2,
        compiler_params=pltpu.CompilerParams(vmem_limit_bytes=60 * MIB),
        name="update",
    )(tile_at, one, two, master, first, second, y, grad)


def shards_paired(
    inputs,
    cotangent,
    doc_lengths,
    owner_list,
    master,
    first_moment,
    second_moment,
    vectors,
    vector_first,
    vector_second,
):
    rows_here, span, width = inputs.shape
    place = lax.axis_index("blk")
    member = lax.axis_index("dp")
    rows_mine = rows_here // 2
    order = jnp.arange(PIECES)
    same_owner = owner_list[:, None] == owner_list[None, :]
    ranks = jnp.sum(same_owner & (order[None, :] < order[:, None]), axis=1).astype(jnp.int32)
    slot_of = owner_list * CAP + ranks
    front_outs = front(owner_list, doc_lengths, master, vectors, inputs, cotangent)
    x, cot, normed, weights_one, weights_two, queries, keys, values = front_outs[:8]
    weights, recips, context_turned, context = front_outs[8:]
    x = x.reshape(-1, width)
    cot = cot.reshape(-1, width)
    block_out, residual, grad_context, sums, tiles_two = feed(
        context, context_turned, x, cot, weights_two, vectors
    )
    hits = jnp.arange(16 * CAP)[:, None] == slot_of[None, :]
    tile_at = jnp.sum(jnp.where(hits, order[None, :] + 1, 0), axis=1).astype(jnp.int32) - 1
    table = jnp.maximum(tile_at - 3, 0)
    block_out, input_grad, total_one, total_two, vector_total = back(
        table,
        (weights, recips, values, queries, keys, context_turned, grad_context),
        weights_one,
        normed,
        x,
        residual,
        vectors,
        tiles_two,
        sums,
        block_out.reshape(rows_mine, LEN, width),
    )
    mine = lax.dynamic_slice_in_dim(tile_at, member * CAP, CAP, 0)
    *updated, block_out, input_grad = update(
        mine,
        total_one,
        total_two,
        master,
        first_moment,
        second_moment,
        block_out.reshape(-1, width),
        input_grad.reshape(-1, width),
    )
    columns = vector_first.shape[1]
    vector_cols = lax.dynamic_slice_in_dim(vectors, place * columns, columns, 1)
    vector_total = lax.dynamic_slice(vector_total, (0, place * columns), (PIECES, columns))
    updated_vectors = adam_step(vector_cols, vector_total, vector_first, vector_second, VEC_RATE)
    return (
        block_out.reshape(inputs.shape),
        input_grad.reshape(inputs.shape),
        *updated,
        *updated_vectors,
    )


def solution(mesh):
    in_specs = (
        P("dp", "blk", None),
        P("dp", "blk", None),
        P("dp", None),
        P(),
        P("dp", "blk", None),
        P("dp", "blk", None),
        P("dp", "blk", None),
        P(),
        P(None, "blk"),
        P(None, "blk"),
    )
    out_specs = (
        P("dp", "blk", None),
        P("dp", "blk", None),
        P("dp", "blk", None),
        P("dp", "blk", None),
        P("dp", "blk", None),
        P(None, "blk"),
        P(None, "blk"),
        P(None, "blk"),
    )
    paired = mesh.shape["blk"] == 2 and mesh.shape["dp"] == 16
    shards = shards_paired if paired else shards_any
    return jax.shard_map(shards, mesh=mesh, in_specs=in_specs, out_specs=out_specs, check_vma=False)
```

```python
from functools import partial

import jax
import jax.numpy as jnp
from jax import lax
from jax.experimental import pallas as pl
from jax.experimental.pallas import tpu as pltpu
from jax.sharding import PartitionSpec as P

D = 768
FF = 3072
HEADS = 12
HEAD_DIM = 64
LEN = 1024
CAP = 3
STEP = 10
PIECES = 12


EPS_NORM = 1e-05
BETA_ONE = 0.9
BETA_TWO = 0.999
RATE = 0.04
VEC_RATE = 0.25
DECAY = 0.01
ADAM_EPS = 1e-08


def normalize(values_in, gain, shift):
    center = jnp.mean(values_in, axis=-1, keepdims=True)
    offset = values_in - center
    spread = jnp.mean(offset * offset, axis=-1, keepdims=True)
    return offset * lax.rsqrt(spread + EPS_NORM) * gain + shift


def adam_step(weight, grad, first, second, rate):
    first_new = BETA_ONE * first + (1.0 - BETA_ONE) * grad
    second_new = BETA_TWO * second + (1.0 - BETA_TWO) * grad * grad
    corrected = (
        first_new
        / (1.0 - BETA_ONE**STEP)
        / (jnp.sqrt(second_new / (1.0 - BETA_TWO**STEP)) + ADAM_EPS)
    )
    return (weight - rate * (corrected + DECAY * weight), first_new, second_new)


def shards_any(
    inputs,
    cotangent,
    doc_lengths,
    owner_list,
    master,
    first_moment,
    second_moment,
    vectors,
    vector_first,
    vector_second,
):
    rows_here, span, width = inputs.shape
    tokens_here = rows_here * span
    fold = FF // D
    scale = HEAD_DIM ** (-0.5)
    place = lax.axis_index("blk")
    f32 = jnp.float32
    b16 = jnp.bfloat16
    order = jnp.arange(PIECES)
    same_owner = owner_list[:, None] == owner_list[None, :]
    ranks = jnp.sum(same_owner & (order[None, :] < order[:, None]), axis=1)
    slot_of = owner_list * CAP + ranks

    mine = (owner_list == lax.axis_index("dp"))[:, None, None]
    tile_rows = lax.psum(jnp.where(mine, master[ranks], 0.0).astype(b16), "dp")
    tiles = lax.all_gather(tile_rows, "blk", axis=1, tiled=True)
    query_weight = tiles[0]
    key_weight = tiles[1]
    value_weight = tiles[2]
    out_weight = tiles[3]
    up_weight = jnp.transpose(tiles[4 : 4 + fold], (1, 0, 2)).reshape(width, FF)
    down_weight = tiles[4 + fold :].reshape(FF, width)
    flat_in = inputs.reshape(tokens_here, width).astype(f32)
    normed_one = normalize(flat_in, vectors[0], vectors[1]).astype(b16)
    queries = (jnp.dot(normed_one, query_weight, preferred_element_type=f32) + vectors[4]).astype(
        b16
    )
    keys_here = jnp.dot(normed_one, key_weight, preferred_element_type=f32).astype(b16)
    values_here = (
        jnp.dot(normed_one, value_weight, preferred_element_type=f32) + vectors[5]
    ).astype(b16)
    query_heads = queries.reshape(rows_here, span, HEADS, HEAD_DIM)
    first_len = doc_lengths[:, 0]
    query_seg = (place * span + jnp.arange(span))[None, :] >= first_len[:, None]

    def block_scores(key_block, start):
        count = key_block.shape[1]
        key_heads = key_block.reshape(rows_here, count, HEADS, HEAD_DIM)
        raw = (
            jnp.einsum("rqhd,rkhd->rhqk", query_heads, key_heads, preferred_element_type=f32)
            * scale
        )
        key_seg = (start + jnp.arange(count))[None, :] >= first_len[:, None]
        allowed = query_seg[:, None, :, None] == key_seg[:, None, None, :]
        return (raw, allowed)

    key_rows = keys_here.reshape(rows_here, span, width)
    value_rows = values_here.reshape(rows_here, span, width)
    top = jnp.full((rows_here, HEADS, span), -1e30, f32)
    key_block = lax.all_gather(key_rows, "blk", axis=1, tiled=True)
    value_block = lax.all_gather(value_rows, "blk", axis=1, tiled=True)
    count = key_block.shape[1]
    raw, allowed = block_scores(key_block, jnp.int32(0))
    new_top = jnp.maximum(top, jnp.max(jnp.where(allowed, raw, -1e30), axis=-1))
    weights = jnp.where(allowed, jnp.exp(raw - new_top[..., None]), 0.0)
    value_heads = value_block.reshape(rows_here, count, HEADS, HEAD_DIM)
    update = jnp.einsum(
        "rhqk,rkhd->rhqd", weights.astype(b16), value_heads, preferred_element_type=f32
    )
    total = jnp.sum(weights, axis=-1)
    log_total = new_top + jnp.log(total)
    context_raw = update / total[..., None]
    context_low = jnp.transpose(context_raw, (0, 2, 1, 3)).reshape(tokens_here, width).astype(b16)
    residual = flat_in + (jnp.dot(context_low, out_weight, preferred_element_type=f32) + vectors[6])
    normed_two = normalize(residual, vectors[2], vectors[3]).astype(b16)
    hidden = jnp.dot(normed_two, up_weight, preferred_element_type=f32) + vectors[8:].reshape(FF)
    gelu_exact = partial(jax.nn.gelu, approximate=False)
    active, gelu_pull = jax.vjp(gelu_exact, hidden)
    active_low = active.astype(b16)
    block_out = (
        residual + (jnp.dot(active_low, down_weight, preferred_element_type=f32) + vectors[7])
    ).reshape(rows_here, span, width)
    grad_out = cotangent.reshape(tokens_here, width)
    down_grad = jnp.einsum("tf,td->fd", active_low, grad_out, preferred_element_type=f32)
    down_sum = jnp.sum(grad_out, axis=0, dtype=f32)
    grad_active = jnp.einsum("td,fd->tf", grad_out, down_weight, preferred_element_type=f32)
    grad_hidden = gelu_pull(grad_active)[0].astype(b16)
    up_grad = jnp.einsum("td,tf->df", normed_two, grad_hidden, preferred_element_type=f32)
    up_sum = jnp.sum(grad_hidden, axis=0, dtype=f32)
    ffn_tiles = jnp.concatenate(
        [
            jnp.transpose(up_grad.reshape(width, fold, width), (1, 0, 2)),
            down_grad.reshape(fold, width, width),
        ],
        axis=0,
    )
    grad_normed_two = jnp.einsum("tf,df->td", grad_hidden, up_weight, preferred_element_type=f32)
    unused, second_pull = jax.vjp(normalize, residual, vectors[2], vectors[3])
    residual_part, gain_two_grad, shift_two_grad = second_pull(grad_normed_two)
    grad_residual = grad_out.astype(f32) + residual_part
    grad_attended = grad_residual.astype(b16)
    out_grad = jnp.einsum("tm,td->md", context_low, grad_attended, preferred_element_type=f32)
    out_sum = jnp.sum(grad_attended, axis=0, dtype=f32)
    grad_context = jnp.einsum(
        "td,md->tm", grad_attended, out_weight, preferred_element_type=f32
    ).astype(b16)
    grad_heads = grad_context.reshape(rows_here, span, HEADS, HEAD_DIM)
    delta = jnp.einsum("rqhd,rhqd->rhq", grad_heads.astype(f32), context_raw)
    key_all, value_all = (
        lax.all_gather(key_rows, "blk", axis=1, tiled=True),
        lax.all_gather(value_rows, "blk", axis=1, tiled=True),
    )
    key_size = min(512, LEN)

    def back_block(index, carry):
        grad_query, key_total, value_total = carry
        start = index * key_size
        key_block = lax.dynamic_slice_in_dim(key_all, start, key_size, 1)
        value_block = lax.dynamic_slice_in_dim(value_all, start, key_size, 1)
        raw, allowed = block_scores(key_block, start)
        weights_back = jnp.where(allowed, jnp.exp(raw - log_total[..., None]), 0.0)
        key_heads = key_block.reshape(rows_here, key_size, HEADS, HEAD_DIM)
        value_heads = value_block.reshape(rows_here, key_size, HEADS, HEAD_DIM)
        value_grad = jnp.einsum(
            "rhqk,rqhd->rkhd", weights_back.astype(b16), grad_heads, preferred_element_type=f32
        )
        weight_grad = jnp.einsum(
            "rqhd,rkhd->rhqk", grad_heads, value_heads, preferred_element_type=f32
        )
        score_grad = (weights_back * (weight_grad - delta[..., None])).astype(b16)
        grad_query = (
            grad_query
            + jnp.einsum("rhqk,rkhd->rqhd", score_grad, key_heads, preferred_element_type=f32)
            * scale
        )
        key_grad = (
            jnp.einsum("rhqk,rqhd->rkhd", score_grad, query_heads, preferred_element_type=f32)
            * scale
        )
        key_total = lax.dynamic_update_slice_in_dim(
            key_total, key_grad.reshape(rows_here, key_size, width), start, 1
        )
        value_total = lax.dynamic_update_slice_in_dim(
            value_total, value_grad.reshape(rows_here, key_size, width), start, 1
        )
        return (grad_query, key_total, value_total)

    zero_rows = jnp.zeros((rows_here, LEN, width), f32)
    grad_query, key_total, value_total = lax.fori_loop(
        0,
        LEN // key_size,
        back_block,
        (jnp.zeros((rows_here, span, HEADS, HEAD_DIM), f32), zero_rows, zero_rows),
    )
    key_grad_here, value_grad_here = (
        lax.psum_scatter(
            key_total.astype(jnp.bfloat16), "blk", scatter_dimension=1, tiled=True
        ).astype(jnp.float32),
        lax.psum_scatter(
            value_total.astype(jnp.bfloat16), "blk", scatter_dimension=1, tiled=True
        ).astype(jnp.float32),
    )
    query_low = grad_query.reshape(tokens_here, width).astype(b16)
    key_low = key_grad_here.reshape(tokens_here, width).astype(b16)
    value_low = value_grad_here.reshape(tokens_here, width).astype(b16)
    query_tile = jnp.einsum("td,te->de", normed_one, query_low, preferred_element_type=f32)
    key_tile = jnp.einsum("td,te->de", normed_one, key_low, preferred_element_type=f32)
    value_tile = jnp.einsum("td,te->de", normed_one, value_low, preferred_element_type=f32)
    grad_normed_one = (
        jnp.einsum("te,de->td", query_low, query_weight, preferred_element_type=f32)
        + jnp.einsum("te,de->td", key_low, key_weight, preferred_element_type=f32)
        + jnp.einsum("te,de->td", value_low, value_weight, preferred_element_type=f32)
    )
    unused, first_pull = jax.vjp(normalize, flat_in, vectors[0], vectors[1])
    input_part, gain_one_grad, shift_one_grad = first_pull(grad_normed_one)
    input_grad = (grad_residual + input_part).reshape(rows_here, span, width)
    vector_grads = jnp.concatenate(
        [
            jnp.stack(
                [
                    gain_one_grad,
                    shift_one_grad,
                    gain_two_grad,
                    shift_two_grad,
                    jnp.sum(query_low, axis=0, dtype=f32),
                    jnp.sum(value_low, axis=0, dtype=f32),
                    out_sum,
                    down_sum,
                ]
            ),
            up_sum.reshape(fold, width),
        ],
        axis=0,
    )
    attn_tiles = jnp.stack([query_tile, key_tile, value_tile, out_grad])
    piece_share, vector_share = (
        lax.psum_scatter(
            jnp.concatenate([attn_tiles, ffn_tiles], axis=0).astype(jnp.bfloat16),
            "blk",
            scatter_dimension=1,
            tiled=True,
        ).astype(jnp.float32),
        lax.psum_scatter(
            vector_grads.astype(jnp.bfloat16), "blk", scatter_dimension=1, tiled=True
        ).astype(jnp.float32),
    )
    own_slots = lax.axis_index("dp") * CAP + jnp.arange(CAP)
    pick = (own_slots[:, None] == slot_of[None, :]).astype(f32)
    occupied = jnp.sum(pick, axis=1)[:, None, None]
    total_share, vector_total = (
        lax.psum(piece_share.astype(jnp.bfloat16), "dp").astype(jnp.float32),
        lax.psum(vector_share.astype(jnp.bfloat16), "dp").astype(jnp.float32),
    )
    slot_grads = jnp.einsum("cp,prd->crd", pick, total_share, precision=lax.Precision.HIGHEST)
    new_master, new_first, new_second = adam_step(
        master, slot_grads, first_moment, second_moment, RATE
    )
    columns = vector_first.shape[1]
    vector_cols = lax.dynamic_slice_in_dim(vectors, place * columns, columns, 1)
    new_vectors, new_vector_first, new_vector_second = adam_step(
        vector_cols, vector_total, vector_first, vector_second, VEC_RATE
    )
    return (
        block_out,
        input_grad,
        new_master * occupied,
        new_first * occupied,
        new_second * occupied,
        new_vectors,
        new_vector_first,
        new_vector_second,
    )


f32 = jnp.float32
b16 = jnp.bfloat16
LOG2E = 1.4426950408889634
MIB = 1024 * 1024
PAIRS = HEADS // 2
PAIR = 2 * HEAD_DIM


def dot_nn(left, right):
    return lax.dot_general(left, right, (((1,), (0,)), ((), ())), preferred_element_type=f32)


def dot_nt(left, right):
    return lax.dot_general(left, right, (((1,), (1,)), ((), ())), preferred_element_type=f32)


def dot_tn(left, right):
    return lax.dot_general(left, right, (((0,), (0,)), ((), ())), preferred_element_type=f32)


def norm_parts(values_in):
    center = jnp.mean(values_in, axis=-1, keepdims=True)
    offset = values_in - center
    spread = jnp.mean(offset * offset, axis=-1, keepdims=True)
    rstd = lax.rsqrt(spread + EPS_NORM)
    return offset * rstd, rstd


def norm_back(grad, unit, rstd, gain):
    scaled = grad * gain
    first = jnp.mean(scaled, axis=-1, keepdims=True)
    second = jnp.mean(scaled * unit, axis=-1, keepdims=True)
    return rstd * (scaled - first - unit * second)


def gelu_parts(value):
    bell = jnp.exp2(value * value * (-0.5 * LOG2E))
    ratio = pl.reciprocal(1.0 + (0.3275911 * 0.7071067811865476) * jnp.abs(value))
    poly = 0.5 * 1.061405429
    poly = poly * ratio + 0.5 * -1.453152027
    poly = poly * ratio + 0.5 * 1.421413741
    poly = poly * ratio + 0.5 * -0.284496736
    poly = poly * ratio + 0.5 * 0.254829592
    tail = poly * ratio * bell
    cdf = jnp.where(value >= 0.0, 1.0 - tail, tail)
    return value * cdf, cdf + value * (bell * 0.3989422804014327)


def head_only(block, head):
    lane = lax.broadcasted_iota(jnp.int32, block.shape, 1)
    keep = (lane >= head * HEAD_DIM) & (lane < (head + 1) * HEAD_DIM)
    return jnp.where(keep, block, jnp.zeros_like(block))


def feed_kernel(
    c_ref, o_ref, x_ref, g_ref, w_ref, vec_ref,
    y_ref, r_ref, d_ref, sums_ref, tiles_ref,
    acc_ref, stage_ref, sem_ref,
):
    fold = FF // D
    step = pl.program_id(0)

    @pl.when(step == 0)
    def clear():
        acc_ref[...] = jnp.zeros_like(acc_ref)
        sums_ref[...] = jnp.zeros_like(sums_ref)

    residual = x_ref[...].astype(f32) + (dot_nn(c_ref[...], w_ref[0]) + vec_ref[6:7, :])
    unit, rstd = norm_parts(residual)
    gain = vec_ref[2:3, :]
    normed = (unit * gain + vec_ref[3:4, :]).astype(b16)
    turned = normed.T
    cot = g_ref[...]
    out = residual + vec_ref[7:8, :]
    grad = jnp.zeros_like(out)

    for part in range(fold):
        hidden = dot_nn(normed, w_ref[1 + part]) + vec_ref[8 + part : 9 + part, :]
        pulled = dot_nt(cot, w_ref[1 + fold + part])
        active, slope = gelu_parts(hidden)
        active = active.astype(b16)
        pulled = (pulled * slope).astype(b16)
        out = out + dot_nn(active, w_ref[1 + fold + part])
        grad = grad + dot_nt(pulled, w_ref[1 + part])
        acc_ref[1 + part] += dot_nn(turned, pulled)
        acc_ref[1 + fold + part] += dot_tn(active, cot)
        sums_ref[8 + part : 9 + part, :] += jnp.sum(pulled.astype(f32), 0, keepdims=True)
    y_ref[...] = out.astype(b16)
    wide = cot.astype(f32)
    sums_ref[2:3, :] += jnp.sum(grad * unit, 0, keepdims=True)
    sums_ref[3:4, :] += jnp.sum(grad, 0, keepdims=True)
    sums_ref[7:8, :] += jnp.sum(wide, 0, keepdims=True)
    back = wide + norm_back(grad, unit, rstd, gain)
    r_ref[...] = back.astype(b16)
    low = back.astype(b16)
    sums_ref[6:7, :] += jnp.sum(low.astype(f32), 0, keepdims=True)
    d_ref[...] = dot_nt(w_ref[0], low).astype(b16)
    acc_ref[0] += dot_nn(o_ref[...], low)

    @pl.when(step == pl.num_programs(0) - 1)
    def send():
        count = 1 + 2 * fold
        copies = []
        for part in range(count):
            if part >= 2:
                copies[part - 2].wait()
            stage_ref[part % 2] = acc_ref[part].astype(b16)
            copy = pltpu.make_async_copy(stage_ref.at[part % 2], tiles_ref.at[part], sem_ref.at[part % 2])
            copy.start()
            copies.append(copy)
        copies[count - 2].wait()
        copies[count - 1].wait()


def feed(context, turned, x, cot, weights, vectors):
    tokens = x.shape[0]
    size = 256
    count = 1 + 2 * (FF // D)
    token_block = pl.BlockSpec((size, D), lambda i: (i, 0))
    turned_block = pl.BlockSpec((D, size), lambda i: (0, i))
    return pl.pallas_call(
        feed_kernel,
        grid=(tokens // size,),
        in_specs=[
            token_block,
            turned_block,
            token_block,
            token_block,
            pl.BlockSpec((count, D, D), lambda i: (0, 0, 0), pipeline_mode=pl.Buffered(1)),
            pl.BlockSpec((PIECES, D), lambda i: (0, 0)),
        ],
        out_specs=[
            token_block,
            token_block,
            turned_block,
            pl.BlockSpec((16, D), lambda i: (0, 0)),
            pl.BlockSpec(memory_space=pl.ANY),
        ],
        out_shape=[
            jax.ShapeDtypeStruct((tokens, D), b16),
            jax.ShapeDtypeStruct((tokens, D), b16),
            jax.ShapeDtypeStruct((D, tokens), b16),
            jax.ShapeDtypeStruct((16, D), f32),
            jax.ShapeDtypeStruct((count, D, D), b16),
        ],
        scratch_shapes=[
            pltpu.VMEM((count, D, D), f32),
            pltpu.VMEM((2, D, D), b16),
            pltpu.SemaphoreType.DMA((2,)),
        ],
        compiler_params=pltpu.CompilerParams(vmem_limit_bytes=60 * MIB),
        cost_estimate=pl.CostEstimate(
            flops=6 * count * tokens * D * D,
            bytes_accessed=18 * tokens * D + 4 * count * D * D,
            transcendentals=2 * tokens * FF,
        ),
        name="feed",
    )(context, turned, x, cot, weights, vectors)


MESH = pl.DeviceIdType.MESH
HALF = D // 2
FLOWS = 2
FLOW = HALF // FLOWS
NEAR = FLOW // 2
KEEP = NEAR // 2
WIDE = 3 * PAIR
REST = PIECES - 3
GROUPS = ((0, 1), (1, 2), (3, 3))
CHUNKS = len(GROUPS)


class Place:
    def __init__(self):
        self.me = lax.axis_index("dp")
        self.core = lax.axis_index("blk")
        self.bits = [lax.rem(self.me // weight, 2) for weight in (1, 2, 4, 8)]
        self.chips = [
            self.me + weight - 2 * weight * bit for weight, bit in zip((1, 2, 4, 8), self.bits)
        ]
        self.partners = [{"dp": chip} for chip in self.chips]
        low, high = self.bits[2:]
        self.inner = low != high
        self.across = {"dp": self.me + 4 - 8 * low + 8 - 16 * high}
        self.other = 1 - self.core
        self.twin = {"blk": self.other}

    def greet(self):
        barrier = pltpu.get_barrier_semaphore()
        for device in self.partners + [self.across, self.twin]:
            pl.semaphore_signal(barrier, 1, device_id=device, device_id_type=MESH)
        pl.semaphore_wait(barrier, 6)

    def flow(self, index):
        first, second = (0, 1) if index == 0 else (1, 0)
        base = index * FLOW
        near = base + self.bits[first] * NEAR
        far = base + NEAR - self.bits[first] * NEAR
        keep = near + self.bits[second] * KEEP
        give = near + KEEP - self.bits[second] * KEEP
        return first, second, near, far, keep, give


def remote(source, target, send, receive, device):
    return pltpu.make_async_remote_copy(
        src_ref=source,
        dst_ref=target,
        send_sem=send,
        recv_sem=receive,
        device_id=device,
        device_id_type=MESH,
    )


def rows_at(start, count):
    return pl.ds(pl.multiple_of(start, 16), count)


class Spread:
    def __init__(self, place, owner, rank, slots, land, gift, sems):
        self.place, self.owner, self.rank = place, owner, rank
        self.slots, self.land, self.gift, self.sems = slots, land, gift, sems

    def cols(self, chunk):
        return pl.ds(GROUPS[chunk][0] * PAIR, GROUPS[chunk][1] * PAIR)

    def first_copy(self, chunk, index):
        first, second, near, far, keep, give = self.place.flow(index)
        return remote(
            self.slots.at[:, rows_at(far, NEAR), self.cols(chunk)],
            self.land[chunk].at[index],
            self.sems[0].at[chunk, index, 0],
            self.sems[1].at[chunk, index, 0],
            self.place.partners[first],
        )

    def second_copy(self, chunk, index, which):
        first, second, near, far, keep, give = self.place.flow(index)
        if which == 0:
            source = self.slots.at[:, rows_at(give, KEEP), self.cols(chunk)]
        else:
            source = self.land[chunk].at[index, :, rows_at(give - near, KEEP)]
        return remote(
            source,
            self.gift[chunk].at[index, pl.ds(which * CAP, CAP)],
            self.sems[0].at[chunk, index, 1 + which],
            self.sems[1].at[chunk, index, 1 + which],
            self.place.partners[second],
        )

    def step(self, chunk, index):
        for flow in range(FLOWS):
            if index == 0:
                self.first_copy(chunk, flow).start()
                self.second_copy(chunk, flow, 0).start()
            if index == 1:
                self.first_copy(chunk, flow).wait()
                self.second_copy(chunk, flow, 1).start()
            if index == 2:
                self.second_copy(chunk, flow, 0).wait()
                self.second_copy(chunk, flow, 1).wait()

    def piece(self, tile, index, chunk, start, count):
        first, second, near, far, keep, give = self.place.flow(index)
        owner, rank = self.owner[tile], self.rank[tile]
        bits = [lax.rem(owner, 2), lax.rem(owner // 2, 2)]
        apart = [bit != mine for bit, mine in zip(bits, self.place.bits)]
        cols = pl.ds(start, count)
        mine = self.slots[rank, rows_at(keep, KEEP), pl.ds(GROUPS[chunk][0] * PAIR + start, count)]
        firsts = self.land[chunk][index, rank, rows_at(keep - near, KEEP), cols]
        gifts = self.gift[chunk][index, jnp.where(apart[first], CAP, 0) + rank, :, cols]
        value = jnp.where(apart[second], gifts, jnp.where(apart[first], firsts, mine))
        layer = owner // 4 == self.place.me // 4
        return jnp.where(layer, value, jnp.zeros_like(value))


class Column:
    steps = 4

    def __init__(self, place, kept, land, sems):
        self.place, self.kept, self.land, self.sems = place, kept, land, sems

    def copy(self, index):
        device = self.place.across if index == 1 else self.place.partners[2]
        return remote(
            self.kept, self.land.at[index % 2], self.sems[0].at[index], self.sems[1].at[index], device
        )

    def add(self, index):
        self.kept[...] = (self.kept[...].astype(f32) + self.land[index].astype(f32)).astype(b16)


def both_flows(flow):
    return pl.ds(flow * KEEP, KEEP)


def column_step(place, column, index):
    @pl.when(place.inner)
    def inner():
        if index == 1:
            column.copy(0).wait_recv()
            column.add(0)
            column.copy(1).start()
        if index == 2:
            column.copy(1).wait()
            column.add(1)
            column.copy(2).start()
        if index == 3:
            column.copy(2).wait_send()

    @pl.when(jnp.logical_not(place.inner))
    def outer():
        if index == 0:
            column.copy(0).start()
        if index == 1:
            column.copy(0).wait_send()
        if index == 3:
            column.copy(2).wait_recv()
            column.kept[...] = column.land[0]


class Item:
    steps = 7

    def __init__(self, place, work, kept, land, sems, load, store=None):
        self.place, self.work, self.kept, self.land, self.sems = place, work, kept, land, sems
        self.load, self.store = load, store
        self.base = place.core * HALF

    def copy(self, flow, index):
        first, second, near, far, keep, give = self.place.flow(flow)
        kept = self.work.at[:, rows_at(self.base + keep, KEEP)]
        half = self.work.at[:, rows_at(self.base + near, NEAR)]
        source, device = [
            (kept, self.place.partners[second]),
            (half, self.place.partners[first]),
        ][index]
        number = 3 + 2 * flow + index
        return remote(source, source, self.sems[0].at[number], self.sems[1].at[number], device)

    def pair(self):
        rows = self.work.at[:, rows_at(self.base, HALF)]
        return remote(rows, rows, self.sems[0].at[7], self.sems[1].at[7], self.place.twin)

    def step(self, index):
        if index == 0:
            for flow in range(FLOWS):
                self.load(self.kept, both_flows(flow), flow)
        if index <= 3:
            column_step(self.place, Column(self.place, self.kept, self.land, self.sems), index)
        for flow in range(FLOWS):
            if index == 3:
                rows = rows_at(self.base + self.place.flow(flow)[4], KEEP)
                self.work[:, rows] = self.kept[:, both_flows(flow)]
            if 4 <= index <= 5:
                self.copy(flow, index - 4).wait()
            if 3 <= index <= 4:
                self.copy(flow, index - 3).start()
        if index == 5:
            self.pair().start()
        if index == 6:
            self.pair().wait()
            self.store().start()


REST_GROUPS = tuple((index, 1) for index in range(REST))
PAIR_CHUNK = (0, 1, 1, 2, 2, 2)
FRONT_PAIRS = (2, 4, 5, 6, 7, 8)
FRONT_REST = (6, 7, 8, 9, 10, 11, 12, 13, 14)
FRONT_LEAD = 9
FRONT_PHASES = 4


def front_kernel(
    owner, lengths, master, vec_ref, x_in, c_in,
    x_out, c_out, n_out, one_out, two_out, q_ref, k_ref, v_ref, p_ref, r_ref, o_ref, ctx_ref,
    rank, rows_ref, normed, keys, turned_values, scores, slots,
    land_one, land_two, land_three, gift_one, gift_two, gift_three,
    one, one_kept, one_land, two, two_kept, two_land,
    spread_send, spread_recv, one_send, one_recv, two_send, two_recv,
    swap_send, swap_recv, swap_local, store_sem,
):
    pair = pl.program_id(0)
    row = pl.program_id(1)
    grid_step = pair * 2 + row
    place = Place()
    rows, span = x_in.shape[0] // 2, x_in.shape[1]
    land = (land_one, land_two, land_three)
    gift = (gift_one, gift_two, gift_three)
    spread = Spread(place, owner, rank, slots, land, gift, (spread_send, spread_recv))

    def swaps(index):
        source, target = [(x_in, rows_ref), (c_in, c_out)][index]
        here = pl.ds(place.core * span, span)
        near = pltpu.make_async_copy(
            source.at[pl.ds(place.core * rows, rows)], target.at[:, here], swap_local.at[index]
        )
        far = remote(
            source.at[pl.ds(place.other * rows, rows)],
            target.at[:, here],
            swap_send.at[index],
            swap_recv.at[index],
            place.twin,
        )
        return near, far

    def row_store():
        return pltpu.make_async_copy(rows_ref, x_out, store_sem.at[PAIRS + REST])

    def normed_store():
        return pltpu.make_async_copy(normed, n_out, store_sem.at[PAIRS + REST + 1])

    def pair_item(group):
        span_of = pl.ds(group, 1)

        def load(work, where, flow):
            chunk = PAIR_CHUNK[group]
            for tile in range(3):
                part = spread.piece(tile, flow, chunk, (group - GROUPS[chunk][0]) * PAIR, PAIR)
                work[0, where, pl.ds(tile * PAIR, PAIR)] = part

        def store():
            return pltpu.make_async_copy(one.at[span_of], one_out.at[span_of], store_sem.at[group])

        sems = (one_send.at[group], one_recv.at[group])
        return Item(place, one.at[span_of], one_kept.at[span_of], one_land.at[:, span_of], sems, load, store)

    def rest_item(group):
        first, count = REST_GROUPS[group]
        span_of = pl.ds(first, count)

        def load(work, where, flow):
            for index in range(count):
                for chunk, (start, wide) in enumerate(GROUPS):
                    part = spread.piece(3 + first + index, flow, chunk, 0, wide * PAIR)
                    work[index, where, pl.ds(start * PAIR, wide * PAIR)] = part

        def store():
            return pltpu.make_async_copy(
                two.at[span_of], two_out.at[span_of], store_sem.at[PAIRS + group]
            )

        sems = (two_send.at[group], two_recv.at[group])
        return Item(place, two.at[span_of], two_kept.at[span_of], two_land.at[:, span_of], sems, load, store)

    def tick(number, phase):
        for chunk in range(CHUNKS):
            if phase == 0 and 0 <= number - 2 * chunk <= 2:
                spread.step(chunk, number - 2 * chunk)
        for index, start in enumerate(FRONT_PAIRS):
            if index % 2 * 2 == phase and 0 <= number - start < Item.steps:
                pair_item(index).step(number - start)
        for index, start in enumerate(FRONT_REST):
            if (index + 1) % FRONT_PHASES == phase and 0 <= number - start < Item.steps:
                rest_item(index).step(number - start)

    def both(number):
        for phase in range(FRONT_PHASES):
            tick(number, phase)

    @pl.when(grid_step == 0)
    def lead():
        slots[...] = master[...].astype(b16)
        for tile in range(PIECES):
            count = jnp.int32(0)
            for before in range(tile):
                count = count + (owner[before] == owner[tile]).astype(jnp.int32)
            rank[tile] = jnp.minimum(count, CAP - 1)
        place.greet()
        for copy in swaps(0):
            copy.start()
        both(0)
        for copy in swaps(1):
            copy.start()
        for copy in swaps(0):
            copy.wait()
        row_store().start()

        def norm_rows(index, carry):
            for part in range(rows):
                for block in range(4):
                    where = pl.ds(pl.multiple_of(index * 128 + block * 32, 32), 32)
                    unit, unused = norm_parts(rows_ref[part, where].astype(f32))
                    low = (unit * vec_ref[0:1, :] + vec_ref[1:2, :]).astype(b16)
                    normed[pl.ds(pl.multiple_of(part * LEN + index * 128 + block * 32, 32), 32)] = low
            return carry

        both(1)
        lax.fori_loop(0, LEN // 128, norm_rows, 0)
        normed_store().start()
        for number in range(2, FRONT_LEAD):
            both(number)

    for number in range(2 * PAIRS):
        pl.when(grid_step == number)(partial(tick, FRONT_LEAD + number, 0))

    @pl.when(row == 0)
    def project():
        lanes = pl.ds(pl.multiple_of(pair * PAIR, PAIR), PAIR)
        weight = one[pair]

        def part(index, carry):
            where = pl.ds(pl.multiple_of(index * 512, 512), 512)
            both = dot_nn(normed[where], weight)
            queries = both[:, :PAIR] + vec_ref[4:5, lanes]
            queries = (queries * (HEAD_DIM**-0.5 * LOG2E)).astype(b16)
            q_ref[:, where] = queries.T
            low = both[:, PAIR : 2 * PAIR].astype(b16)
            keys[where] = low
            k_ref[:, where] = low.T
            values = (both[:, 2 * PAIR :] + vec_ref[5:6, lanes]).astype(b16)
            v_ref[where] = values
            turned_values[:, where] = values.T
            return carry

        lax.fori_loop(0, normed.shape[0] // 512, part, 0)

    half = LEN // 2
    start = pl.multiple_of(row * LEN, LEN)
    split = lengths[place.core * rows + row, 0] < LEN
    shift = jnp.where(split, jnp.float32(-1e30), jnp.float32(0.0))

    quarter = LEN // 4
    units = [(head, step) for head in range(2) for step in range(2)]

    def score_block(unit, block, peak):
        head, step = units[unit]
        rows_here = pl.ds(pl.multiple_of(start + block * quarter, quarter), quarter)
        queries = q_ref[:, pl.ds(pl.multiple_of(start + step * half, half), half)]
        raw = dot_nn(head_only(keys[rows_here], head), queries)
        if block // 2 != step:
            raw = raw + shift
        scores[unit % 2, block * quarter : (block + 1) * quarter] = raw
        best = jnp.max(raw.reshape(-1, 8, half), axis=0)
        return best if peak is None else jnp.maximum(peak, best)

    def context_block(unit, block, total):
        head, step = units[unit]
        part = slice(head * HEAD_DIM, (head + 1) * HEAD_DIM)
        cols = pl.ds(pl.multiple_of(start + block * quarter, quarter), quarter)
        here = slice(step * half, (step + 1) * half)
        term = dot_nn(
            turned_values[part, cols], p_ref[head, block * quarter : (block + 1) * quarter, here]
        )
        return term if total is None else total + term

    def context_store(unit, total, recip):
        head, step = units[unit]
        part = slice(head * HEAD_DIM, (head + 1) * HEAD_DIM)
        o_ref[part, step * half : (step + 1) * half] = (total * recip).astype(b16)

    peak = None
    for block in range(4):
        peak = score_block(0, block, peak)
    before = None
    for unit, (head, step) in enumerate(units):
        if unit > 0:
            for number in range(2 * PAIRS):
                pl.when(grid_step == number)(partial(tick, FRONT_LEAD + number, unit))
        here = slice(step * half, (step + 1) * half)
        top = jnp.max(peak, 0, keepdims=True)
        total = jnp.zeros((8, half), f32)
        peak, context = None, None
        for block in range(4):
            if unit + 1 < len(units):
                peak = score_block(unit + 1, block, peak)
            for small in range(4 * block, 4 * block + 4):
                rows_here = slice(small * 64, (small + 1) * 64)
                value = jnp.exp2(scores[unit % 2, rows_here] - top)
                total = total + jnp.sum(value.reshape(-1, 8, half), axis=0)
                p_ref[head, rows_here, here] = value.astype(b16)
            if unit > 0:
                context = context_block(unit - 1, block, context)
        if unit > 0:
            context_store(unit - 1, context, before)
        before = 1.0 / jnp.sum(total, 0, keepdims=True)
        r_ref[0, head : head + 1, here] = before
    context = None
    for block in range(4):
        context = context_block(3, block, context)
    context_store(3, context, before)
    ctx_ref[...] = o_ref[...].T

    @pl.when(grid_step == 2 * PAIRS - 1)
    def finish_copies():
        for copy in swaps(1):
            copy.wait()
        row_store().wait()
        normed_store().wait()
        for group in range(PAIRS):
            pair_item(group).store().wait()
        for group in range(REST):
            rest_item(group).store().wait()


def front(owner, lengths, master, vectors, inputs, cotangent):
    rows, span = inputs.shape[0] // 2, inputs.shape[1]
    tokens = rows * LEN
    any_spec = pl.BlockSpec(memory_space=pl.ANY)
    smem = pl.BlockSpec(memory_space=pltpu.SMEM)
    whole = jax.ShapeDtypeStruct((rows, LEN, D), b16)
    dma = pltpu.SemaphoreType.DMA
    return pl.pallas_call(
        front_kernel,
        grid=(PAIRS, rows),
        in_specs=[
            smem,
            smem,
            pl.BlockSpec((CAP, HALF, D), lambda h, r: (0, 0, 0), pipeline_mode=pl.Buffered(1)),
            pl.BlockSpec((PIECES, D), lambda h, r: (0, 0)),
            any_spec,
            any_spec,
        ],
        out_specs=[any_spec] * 5
        + [
            pl.BlockSpec((PAIR, tokens), lambda h, r: (h, 0)),
            pl.BlockSpec((PAIR, tokens), lambda h, r: (h, 0)),
            pl.BlockSpec((tokens, PAIR), lambda h, r: (0, h)),
            pl.BlockSpec((2, LEN, LEN), lambda h, r: (h * 2 + r, 0, 0)),
            pl.BlockSpec((1, 2, LEN), lambda h, r: (h * 2 + r, 0, 0)),
            pl.BlockSpec((PAIR, LEN), lambda h, r: (h, r)),
            pl.BlockSpec((LEN, PAIR), lambda h, r: (r, h)),
        ],
        out_shape=[
            whole,
            whole,
            jax.ShapeDtypeStruct((tokens, D), b16),
            jax.ShapeDtypeStruct((PAIRS, D, WIDE), b16),
            jax.ShapeDtypeStruct((REST, D, D), b16),
            jax.ShapeDtypeStruct((D, tokens), b16),
            jax.ShapeDtypeStruct((D, tokens), b16),
            jax.ShapeDtypeStruct((tokens, D), b16),
            jax.ShapeDtypeStruct((rows * HEADS, LEN, LEN), b16),
            jax.ShapeDtypeStruct((rows * PAIRS, 2, LEN), f32),
            jax.ShapeDtypeStruct((D, tokens), b16),
            jax.ShapeDtypeStruct((tokens, D), b16),
        ],
        scratch_shapes=[
            pltpu.SMEM((PIECES,), jnp.int32),
            pltpu.VMEM((rows, LEN, D), b16),
            pltpu.VMEM((tokens, D), b16),
            pltpu.VMEM((tokens, PAIR), b16),
            pltpu.VMEM((PAIR, tokens), b16),
            pltpu.VMEM((2, LEN, LEN // 2), f32),
            pltpu.VMEM((CAP, HALF, D), b16),
        ]
        + [pltpu.VMEM((FLOWS, CAP, NEAR, wide * PAIR), b16) for unused, wide in GROUPS]
        + [pltpu.VMEM((FLOWS, 2 * CAP, KEEP, wide * PAIR), b16) for unused, wide in GROUPS]
        + [
            pltpu.VMEM((PAIRS, D, WIDE), b16),
            pltpu.VMEM((PAIRS, NEAR, WIDE), b16),
            pltpu.VMEM((2, PAIRS, NEAR, WIDE), b16),
            pltpu.VMEM((REST, D, D), b16),
            pltpu.VMEM((REST, NEAR, D), b16),
            pltpu.VMEM((2, REST, NEAR, D), b16),
            dma((CHUNKS, FLOWS, 3)),
            dma((CHUNKS, FLOWS, 3)),
            dma((PAIRS, 8)),
            dma((PAIRS, 8)),
            dma((REST, 8)),
            dma((REST, 8)),
            dma((2,)),
            dma((2,)),
            dma((2,)),
            dma((PAIRS + REST + 2,)),
        ],
        compiler_params=pltpu.CompilerParams(
            collective_id=0, has_side_effects=True, vmem_limit_bytes=60 * MIB
        ),
        name="front",
    )(owner, lengths, master, vectors, inputs, cotangent)


class Sum:
    steps = 7

    def __init__(self, place, work, kept, wide, narrow, land, sems, send_pair, add_own):
        self.place, self.work, self.kept, self.sems = place, work, kept, sems
        self.wide, self.narrow, self.land = wide, narrow, land
        self.send_pair, self.add_own = send_pair, add_own

    def copy(self, flow, index):
        first, second, near, far, keep, give = self.place.flow(flow)
        source, target, device = [
            (self.work.at[:, rows_at(far, NEAR)], self.wide.at[flow], first),
            (self.work.at[:, rows_at(give, KEEP)], self.narrow.at[flow], second),
        ][index]
        number = 3 + 2 * flow + index
        return remote(
            source,
            target,
            self.sems[0].at[number],
            self.sems[1].at[number],
            self.place.partners[device],
        )

    def step(self, index):
        if index == 0:
            self.send_pair().start()
        if index == 1:
            self.send_pair().wait()
            self.add_own()
        for flow in range(FLOWS):
            first, second, near, far, keep, give = self.place.flow(flow)
            if index == 1:
                self.copy(flow, 0).start()
            if index == 2:
                self.copy(flow, 0).wait()
                rows = rows_at(near, NEAR)
                total = self.work[:, rows].astype(f32) + self.wide[flow].astype(f32)
                self.work[:, rows] = total.astype(b16)
                self.copy(flow, 1).start()
            if index == 3:
                self.copy(flow, 1).wait()
                total = self.work[:, rows_at(keep, KEEP)].astype(f32) + self.narrow[flow].astype(f32)
                self.kept[:, both_flows(flow)] = total.astype(b16)
        if index >= 3:
            column_step(self.place, Column(self.place, self.kept, self.land, self.sems), index - 3)


class Gather:
    steps = 3

    def __init__(self, place, work, kept, narrow, wide, sems):
        self.place, self.work, self.kept = place, work, kept
        self.narrow, self.wide, self.sems = narrow, wide, sems

    def copy(self, flow, index):
        first, second, near, far, keep, give = self.place.flow(flow)
        source, target, device = [
            (self.kept.at[:, both_flows(flow)], self.narrow, second),
            (self.work.at[:, rows_at(near, NEAR)], self.wide, first),
        ][index]
        number = 7 + 2 * flow + index
        return remote(
            source,
            target.at[flow],
            self.sems[0].at[number],
            self.sems[1].at[number],
            self.place.partners[device],
        )

    def step(self, index):
        for flow in range(FLOWS):
            first, second, near, far, keep, give = self.place.flow(flow)
            if index == 0:
                self.work[:, rows_at(keep, KEEP)] = self.kept[:, both_flows(flow)]
            if index > 0:
                self.copy(flow, index - 1).wait()
            if index == 1:
                self.work[:, rows_at(give, KEEP)] = self.narrow[flow]
            if index == 2:
                self.work[:, rows_at(far, NEAR)] = self.wide[flow]
            if index < 2:
                self.copy(flow, index).start()


class Hand:
    steps = 3

    def __init__(self, place, table, kept, bag, gift, pack, last, own, out, sems, store_sems):
        self.place, self.table, self.kept = place, table, kept
        self.bag, self.gift, self.pack, self.last, self.own = bag, gift, pack, last, own
        self.out, self.sems, self.store_sems = out, sems, store_sems

    def tile(self, chip, rank, flow):
        return self.kept[self.table[chip * CAP + rank], both_flows(flow)]

    def copy(self, flow, index):
        first, second = self.place.flow(flow)[:2]
        source, target, device = [
            (self.bag.at[flow], self.gift.at[flow], second),
            (self.pack.at[flow], self.last.at[flow], first),
        ][index]
        return remote(
            source,
            target,
            self.sems[0].at[flow, index],
            self.sems[1].at[flow, index],
            self.place.partners[device],
        )

    def stores(self, flow):
        first, second, near, far, keep, give = self.place.flow(flow)
        parts = [
            (self.own.at[flow], rows_at(keep, KEEP)),
            (self.gift.at[flow, pl.ds(0, CAP)], rows_at(give, KEEP)),
            (self.last.at[flow], rows_at(far, NEAR)),
        ]
        return [
            pltpu.make_async_copy(source, self.out.at[:, rows], self.store_sems.at[flow, index])
            for index, (source, rows) in enumerate(parts)
        ]

    def step(self, index):
        for flow in range(FLOWS):
            first, second, near, far, keep, give = self.place.flow(flow)
            if index == 0:
                beside = self.place.chips[second]
                across = beside + self.place.chips[first] - self.place.me
                for rank in range(CAP):
                    self.bag[flow, rank] = self.tile(beside, rank, flow)
                    self.bag[flow, CAP + rank] = self.tile(across, rank, flow)
                    self.own[flow, rank] = self.tile(self.place.me, rank, flow)
                self.copy(flow, 0).start()
            if index == 1:
                self.copy(flow, 0).wait()
                for rank in range(CAP):
                    mine = self.tile(self.place.chips[first], rank, flow)
                    self.pack[flow, rank, rows_at(keep - near, KEEP)] = mine
                    self.pack[flow, rank, rows_at(give - near, KEEP)] = self.gift[flow, CAP + rank]
                self.copy(flow, 1).start()
            if index == 2:
                self.copy(flow, 1).wait()
                for copy in self.stores(flow):
                    copy.start()


BACK_STEPS = 2 * PAIRS
BACK_TAIL = 4
BACK_PAIRS = tuple((index, 1) for index in range(PAIRS))
BACK_REST = (0, 1, 2, 3, 4, 5, 6, 7, 8)
BACK_HANDS = (14, 17, 20)


def back_kernel(
    table, p_ref, r_ref, v_ref, q_ref, k_ref, o_ref, g_ref, w_ref, n_ref, x_ref, z_ref, vec_ref,
    tiles_in, sums_in, y_in,
    y_out, i_out, pairs_out, slots_out, sums_ref,
    grad_sum, wide_sum, turned, slopes, block_out,
    two, two_kept, two_wide, two_narrow, two_land, two_stage,
    one, one_kept, one_wide, one_narrow, one_land, one_send_stage, one_stage,
    gather_narrow, gather_wide,
    bag, gift, pack, last, own, vec_land,
    two_send, two_recv, one_send, one_recv, hand_send, hand_recv, hand_store,
    pair_two_send, pair_two_recv, pair_one_send, pair_one_recv, load_sem, store_sem,
    swap_send, swap_recv, swap_local, vec_send, vec_recv,
):
    step = pl.program_id(0)
    place = Place()
    rows, span = y_in.shape[0], y_in.shape[1] // 2
    near_half = rows_at(place.core * HALF, HALF)
    far_half = rows_at(place.other * HALF, HALF)

    def load_two(group):
        first, count = REST_GROUPS[group]
        return pltpu.make_async_copy(
            tiles_in.at[pl.ds(first, count), near_half],
            two_stage.at[pl.ds(group % 2, 1)],
            load_sem.at[group % 2],
        )

    def rest_sum(group):
        first, count = REST_GROUPS[group]
        span_of = pl.ds(first, count)
        work = two.at[span_of]

        def send_pair():
            return remote(
                tiles_in.at[span_of, far_half],
                work,
                pair_two_send.at[group],
                pair_two_recv.at[group],
                place.twin,
            )

        def add_own():
            load_two(group).wait()
            work[...] = (work[...].astype(f32) + two_stage[group % 2].astype(f32)).astype(b16)

        sems = (two_send.at[group], two_recv.at[group])
        parts = (two_kept.at[span_of], two_wide.at[:, span_of], two_narrow.at[:, span_of])
        return Sum(place, work, *parts, two_land.at[:, span_of], sems, send_pair, add_own)

    def pair_sum(group):
        first, count = BACK_PAIRS[group]
        span_of = pl.ds(first, count)
        work = one.at[span_of]

        def send_pair():
            return remote(
                one_send_stage.at[pl.ds(group % 2, 1)],
                work,
                pair_one_send.at[group],
                pair_one_recv.at[group],
                place.twin,
            )

        def add_own():
            own = one_stage[group % 2].astype(f32)
            work[...] = (work[...].astype(f32) + own).astype(b16)

        sems = (one_send.at[group], one_recv.at[group])
        parts = (one_kept.at[span_of], one_wide.at[:, span_of], one_narrow.at[:, span_of])
        return Sum(place, work, *parts, one_land.at[:, span_of], sems, send_pair, add_own)

    def pair_gather(group):
        first, count = BACK_PAIRS[group]
        span_of = pl.ds(first, count)
        sems = (one_send.at[group], one_recv.at[group])
        narrow, wide = gather_narrow.at[:, span_of], gather_wide.at[:, span_of]
        return Gather(place, one.at[span_of], one_kept.at[span_of], narrow, wide, sems)

    hand = Hand(
        place, table, two_kept, bag, gift, pack, last, own, slots_out, (hand_send, hand_recv), hand_store
    )

    def pair_store(index, tile):
        return pltpu.make_async_copy(
            one.at[index, :, pl.ds(tile * PAIR, PAIR)],
            pairs_out.at[tile, :, pl.ds(index * PAIR, PAIR)],
            store_sem.at[index, tile],
        )

    def tick(number, odd):
        for group, start in enumerate(BACK_REST):
            if group % 2 == odd and 0 <= number - start < Sum.steps:
                rest_sum(group).step(number - start)
        for group, (first, count) in enumerate(BACK_PAIRS):
            if group % 2 != odd:
                continue
            start = 2 * (first + count)
            if 0 <= number - start < Sum.steps:
                pair_sum(group).step(number - start)
            if 0 <= number - start - Sum.steps + 1 < Gather.steps:
                pair_gather(group).step(number - start - Sum.steps + 1)
            if number == start + Sum.steps + 1:
                for index in range(first, first + count):
                    for tile in range(3):
                        pair_store(index, tile).start()
        if odd == 0 and number in BACK_HANDS:
            hand.step(BACK_HANDS.index(number))
        for group, start in enumerate(BACK_REST):
            if odd == 1 and number == max(start - 1, 0):
                load_two(group).start()

    def both(number):
        tick(number, 0)
        tick(number, 1)

    def swap_y(index):
        there = pl.ds(place.core * rows, rows)
        if index == 0:
            return pltpu.make_async_copy(
                y_in.at[:, pl.ds(place.core * span, span)], y_out.at[there], swap_local.at[0]
            )
        return remote(
            y_in.at[:, pl.ds(place.other * span, span)],
            y_out.at[there],
            swap_send.at[0],
            swap_recv.at[0],
            place.twin,
        )

    @pl.when(step == 0)
    def lead():
        place.greet()
        for index in range(2):
            swap_y(index).start()
        sums_ref[...] = sums_in[...]

    for number in range(BACK_STEPS + BACK_TAIL):
        early = partial(tick, number, 0) if number < BACK_STEPS else partial(both, number)
        pl.when(step == number)(early)

    half = LEN // 2
    pair, row = step // 2, lax.rem(step, 2)

    quarter = LEN // 4

    def attention_inputs(head):
        part = slice(head * HEAD_DIM, (head + 1) * HEAD_DIM)
        values = head_only(v_ref[...], head)
        recip = r_ref[0, head : head + 1, :]
        grad = g_ref[part, :].astype(f32) * recip
        delta = jnp.sum(grad * o_ref[part, :].astype(f32), 0, keepdims=True)
        grad = grad.astype(b16)
        return values, grad, delta, jnp.concatenate([grad, grad], axis=0)

    def attention(head):
        part = slice(head * HEAD_DIM, (head + 1) * HEAD_DIM)
        values, grad, delta, doubled = attention_inputs(head)
        units = [(which, block) for which in range(2) for block in range(4)]
        value_grad, key_grad, query_grad = {}, {}, {}

        def raw_block(unit):
            which, block = units[unit]
            cols = slice(which * half, (which + 1) * half)
            return dot_nn(values[block * quarter : (block + 1) * quarter], doubled[:, cols])

        def slope_block(unit, raw):
            which, block = units[unit]
            cols = slice(which * half, (which + 1) * half)
            for small in range(4):
                rows_here = slice(small * 64, (small + 1) * 64)
                rows_all = slice(block * quarter + small * 64, block * quarter + (small + 1) * 64)
                slope = p_ref[head, rows_all, cols].astype(f32) * (raw[rows_here] - delta[:, cols])
                slopes[unit % 2, rows_here] = slope.astype(b16)

        def add(totals, key, term):
            totals[key] = totals[key] + term if key in totals else term

        def grad_block(unit):
            which, block = units[unit]
            cols = slice(which * half, (which + 1) * half)
            rows_all = slice(block * quarter, (block + 1) * quarter)
            slope = slopes[unit % 2]
            add(value_grad, block, dot_nt(grad[:, cols], p_ref[head, rows_all, cols]))
            add(key_grad, block, dot_nt(q_ref[part, cols], slope))
            add(query_grad, which, dot_nn(k_ref[part, rows_all], slope))

        raw = raw_block(0)
        for unit in range(len(units)):
            after = raw_block(unit + 1) if unit + 1 < len(units) else None
            slope_block(unit, raw)
            if unit > 0:
                grad_block(unit - 1)
            raw = after
        grad_block(len(units) - 1)
        for which in range(2):
            total = query_grad[which] * (HEAD_DIM**-0.5)
            turned[part, which * half : (which + 1) * half] = total.astype(b16)
        for block in range(4):
            rows_all = slice(block * quarter, (block + 1) * quarter)
            lower = slice(PAIR + head * HEAD_DIM, PAIR + (head + 1) * HEAD_DIM)
            turned[lower, rows_all] = (key_grad[block] * (1.0 / LOG2E)).astype(b16)
            lower = slice(2 * PAIR + head * HEAD_DIM, 2 * PAIR + (head + 1) * HEAD_DIM)
            turned[lower, rows_all] = value_grad[block].astype(b16)

    @pl.when(step < BACK_STEPS)
    def first_head():
        attention(0)

    for number in range(BACK_STEPS):
        pl.when(step == number)(partial(tick, number, 1))

    @pl.when(step < BACK_STEPS)
    def second_head():
        attention(1)
        where = pl.ds(pl.multiple_of(row * LEN, LEN), LEN)
        block = dot_nn(turned[...], n_ref[where])
        back = turned[...].T
        lanes = pl.ds(pl.multiple_of(pair * PAIR, PAIR), PAIR)
        ones = jnp.sum(back.astype(f32), 0, keepdims=True)
        sums_ref[4:5, lanes] += ones[:, :PAIR]
        sums_ref[5:6, lanes] += ones[:, 2 * PAIR :]
        term = dot_nt(back, w_ref[0])

        @pl.when(pair == 0)
        def begin():
            grad_sum[where] = term

        @pl.when(pair > 0)
        def add():
            grad_sum[where] += term

        @pl.when(row == 0)
        def keep():
            wide_sum[...] = block

        @pl.when(row == 1)
        def hand_on():
            whole = (wide_sum[...] + block).T
            low = whole.astype(b16)
            for core in range(2):

                @pl.when(place.core == core)
                def split():
                    slot = lax.rem(pair, 2)
                    one_stage[slot] = low[core * HALF : (core + 1) * HALF]
                    one_send_stage[slot] = low[(1 - core) * HALF : (2 - core) * HALF]

    def store_block(index):
        row, half = index // 2, index % 2
        target = i_out.at[place.core * rows + row]
        local = pltpu.make_async_copy(block_out.at[half], target, swap_local.at[1 + row])
        far = remote(
            block_out.at[half], target, swap_send.at[1 + row], swap_recv.at[1 + row], place.twin
        )
        return local, far, half

    def wait_block(index):
        local, far, half = store_block(index)

        @pl.when(place.core == half)
        def keep():
            local.wait()

        @pl.when(place.core != half)
        def give():
            far.wait()

    for index in range(BACK_TAIL):

        @pl.when(step == BACK_STEPS + index)
        def close():
            size = LEN // 2
            if index >= 2:
                wait_block(index - 2)
            gain_sum = jnp.zeros((8, D), f32)
            shift_sum = jnp.zeros((8, D), f32)
            for block in range(size // 16):
                rows_here = slice(block * 16, (block + 1) * 16)
                grad = grad_sum[index * size + block * 16 : index * size + (block + 1) * 16]
                unit, rstd = norm_parts(x_ref[rows_here].astype(f32))
                gain_sum = gain_sum + jnp.sum((grad * unit).reshape(-1, 8, D), axis=0)
                shift_sum = shift_sum + jnp.sum(grad.reshape(-1, 8, D), axis=0)
                total = norm_back(grad, unit, rstd, vec_ref[0:1, :])
                block_out[index % 2, rows_here] = (z_ref[rows_here].astype(f32) + total).astype(b16)
            sums_ref[0:1, :] += jnp.sum(gain_sum, 0, keepdims=True)
            sums_ref[1:2, :] += jnp.sum(shift_sum, 0, keepdims=True)
            local, far, half = store_block(index)

            @pl.when(place.core == half)
            def keep():
                local.start()

            @pl.when(place.core != half)
            def give():
                far.start()

    @pl.when(step == BACK_STEPS + BACK_TAIL - 1)
    def drain():
        devices = [place.twin] + place.partners

        def vector(index):
            return remote(
                sums_ref, vec_land.at[index], vec_send.at[index], vec_recv.at[index], devices[index]
            )

        vector(0).start()
        for number in range(BACK_STEPS + BACK_TAIL, BACK_STEPS + Sum.steps + Gather.steps):
            both(number)
            index = number - BACK_STEPS - BACK_TAIL
            if index < 5:
                vector(index).wait()
                sums_ref[...] += vec_land[index]
                if index < 4:
                    vector(index + 1).start()
        for index in range(2):
            swap_y(index).wait()
        for index in range(2, BACK_TAIL):
            wait_block(index)
        for index in range(PAIRS):
            for tile in range(3):
                pair_store(index, tile).wait()
        for flow in range(FLOWS):
            for copy in hand.stores(flow):
                copy.wait()


def back(table, attention, weights, normed, x, residual, vectors, tiles, sums, y):
    rows, length = y.shape[:2]
    tokens = rows * length
    any_spec = pl.BlockSpec(memory_space=pl.ANY)
    smem = pl.BlockSpec(memory_space=pltpu.SMEM)
    dma = pltpu.SemaphoreType.DMA

    def now(step):
        return jnp.minimum(step, BACK_STEPS - 1)

    def tail(step):
        return jnp.maximum(step - BACK_STEPS, 0)

    head_block = pl.BlockSpec((PAIR, LEN), lambda s: (now(s) // 2, lax.rem(now(s), 2)))
    tail_block = pl.BlockSpec((LEN // 2, D), lambda s: (tail(s), 0))
    whole = pl.BlockSpec((PIECES, D), lambda s: (0, 0))
    sums_block = pl.BlockSpec((16, D), lambda s: (0, 0))
    return pl.pallas_call(
        back_kernel,
        grid=(BACK_STEPS + BACK_TAIL,),
        in_specs=[
            smem,
            pl.BlockSpec((2, LEN, LEN), lambda s: (now(s), 0, 0)),
            pl.BlockSpec((1, 2, LEN), lambda s: (now(s), 0, 0)),
            pl.BlockSpec((LEN, PAIR), lambda s: (lax.rem(now(s), 2), now(s) // 2)),
            head_block,
            head_block,
            head_block,
            head_block,
            pl.BlockSpec((1, D, WIDE), lambda s: (now(s) // 2, 0, 0)),
            pl.BlockSpec((tokens, D), lambda s: (0, 0), pipeline_mode=pl.Buffered(1)),
            tail_block,
            tail_block,
            whole,
            any_spec,
            sums_block,
            any_spec,
        ],
        out_specs=[any_spec] * 4 + [sums_block],
        out_shape=[
            jax.ShapeDtypeStruct((2 * rows, length // 2, D), b16),
            jax.ShapeDtypeStruct((2 * rows, length // 2, D), b16),
            jax.ShapeDtypeStruct((3, HALF, D), b16),
            jax.ShapeDtypeStruct((CAP, HALF, D), b16),
            jax.ShapeDtypeStruct((16, D), f32),
        ],
        scratch_shapes=[
            pltpu.VMEM((tokens, D), f32),
            pltpu.VMEM((WIDE, D), f32),
            pltpu.VMEM((WIDE, LEN), b16),
            pltpu.VMEM((2, LEN // 4, LEN // 2), b16),
            pltpu.VMEM((2, LEN // 2, D), b16),
            pltpu.VMEM((REST, HALF, D), b16),
            pltpu.VMEM((REST, NEAR, D), b16),
            pltpu.VMEM((FLOWS, REST, NEAR, D), b16),
            pltpu.VMEM((FLOWS, REST, KEEP, D), b16),
            pltpu.VMEM((2, REST, NEAR, D), b16),
            pltpu.VMEM((2, HALF, D), b16),
            pltpu.VMEM((PAIRS, HALF, WIDE), b16),
            pltpu.VMEM((PAIRS, NEAR, WIDE), b16),
            pltpu.VMEM((FLOWS, PAIRS, NEAR, WIDE), b16),
            pltpu.VMEM((FLOWS, PAIRS, KEEP, WIDE), b16),
            pltpu.VMEM((2, PAIRS, NEAR, WIDE), b16),
            pltpu.VMEM((2, HALF, WIDE), b16),
            pltpu.VMEM((2, HALF, WIDE), b16),
            pltpu.VMEM((FLOWS, PAIRS, KEEP, WIDE), b16),
            pltpu.VMEM((FLOWS, PAIRS, NEAR, WIDE), b16),
            pltpu.VMEM((FLOWS, 2 * CAP, KEEP, D), b16),
            pltpu.VMEM((FLOWS, 2 * CAP, KEEP, D), b16),
            pltpu.VMEM((FLOWS, CAP, NEAR, D), b16),
            pltpu.VMEM((FLOWS, CAP, NEAR, D), b16),
            pltpu.VMEM((FLOWS, CAP, KEEP, D), b16),
            pltpu.VMEM((5, 16, D), f32),
            dma((REST, 7)),
            dma((REST, 7)),
            dma((PAIRS, 11)),
            dma((PAIRS, 11)),
            dma((FLOWS, 2)),
            dma((FLOWS, 2)),
            dma((FLOWS, 3)),
            dma((REST,)),
            dma((REST,)),
            dma((PAIRS,)),
            dma((PAIRS,)),
            dma((3,)),
            dma((PAIRS, 3)),
            dma((3,)),
            dma((3,)),
            dma((3,)),
            dma((5,)),
            dma((5,)),
        ],
        compiler_params=pltpu.CompilerParams(
            collective_id=1, has_side_effects=True, vmem_limit_bytes=62 * MIB
        ),
        name="back",
    )(table, *attention, weights, normed, x, residual, vectors, tiles, sums, y)


def update_kernel(tile_at, one, two, w_ref, m_ref, s_ref, y_in, i_in, w_out, m_out, s_out, y_out, i_out):
    step = pl.program_id(0)
    tile = tile_at[step // 2]
    grad = jnp.where(tile < 3, one[0], two[0]).astype(f32)
    parts = adam_step(w_ref[0], grad, m_ref[0], s_ref[0], RATE)
    for target, part in zip((w_out, m_out, s_out), parts):
        target[0] = jnp.where(tile >= 0, part, jnp.zeros_like(part))

    @pl.when(step < 4)
    def widen():
        y_out[...] = y_in[...].astype(f32)
        i_out[...] = i_in[...].astype(f32)


def update(tile_at, one, two, master, first, second, y, grad):
    tokens = y.shape[0]
    size = HALF // 2
    state = pl.BlockSpec((1, size, D), lambda s, tile_at: (s // 2, lax.rem(s, 2), 0))
    wide = pl.BlockSpec((tokens // 4, D), lambda s, tile_at: (jnp.minimum(s, 3), 0))
    return pl.pallas_call(
        update_kernel,
        grid_spec=pltpu.PrefetchScalarGridSpec(
            num_scalar_prefetch=1,
            grid=(CAP * 2,),
            in_specs=[
                pl.BlockSpec(
                    (1, size, D),
                    lambda s, tile_at: (jnp.clip(tile_at[s // 2], 0, 2), lax.rem(s, 2), 0),
                ),
                state,
                state,
                state,
                state,
                wide,
                wide,
            ],
            out_specs=[state] * 3 + [wide] * 2,
        ),
        out_shape=[jax.ShapeDtypeStruct(master.shape, f32)] * 3
        + [jax.ShapeDtypeStruct((tokens, D), f32)] * 2,
        compiler_params=pltpu.CompilerParams(vmem_limit_bytes=60 * MIB),
        name="update",
    )(tile_at, one, two, master, first, second, y, grad)


def shards_paired(
    inputs,
    cotangent,
    doc_lengths,
    owner_list,
    master,
    first_moment,
    second_moment,
    vectors,
    vector_first,
    vector_second,
):
    rows_here, span, width = inputs.shape
    place = lax.axis_index("blk")
    member = lax.axis_index("dp")
    rows_mine = rows_here // 2
    order = jnp.arange(PIECES)
    same_owner = owner_list[:, None] == owner_list[None, :]
    ranks = jnp.sum(same_owner & (order[None, :] < order[:, None]), axis=1).astype(jnp.int32)
    slot_of = owner_list * CAP + ranks
    front_outs = front(owner_list, doc_lengths, master, vectors, inputs, cotangent)
    x, cot, normed, weights_one, weights_two, queries, keys, values = front_outs[:8]
    weights, recips, context_turned, context = front_outs[8:]
    x = x.reshape(-1, width)
    cot = cot.reshape(-1, width)
    block_out, residual, grad_context, sums, tiles_two = feed(
        context, context_turned, x, cot, weights_two, vectors
    )
    hits = jnp.arange(16 * CAP)[:, None] == slot_of[None, :]
    tile_at = jnp.sum(jnp.where(hits, order[None, :] + 1, 0), axis=1).astype(jnp.int32) - 1
    table = jnp.maximum(tile_at - 3, 0)
    block_out, input_grad, total_one, total_two, vector_total = back(
        table,
        (weights, recips, values, queries, keys, context_turned, grad_context),
        weights_one,
        normed,
        x,
        residual,
        vectors,
        tiles_two,
        sums,
        block_out.reshape(rows_mine, LEN, width),
    )
    mine = lax.dynamic_slice_in_dim(tile_at, member * CAP, CAP, 0)
    *updated, block_out, input_grad = update(
        mine,
        total_one,
        total_two,
        master,
        first_moment,
        second_moment,
        block_out.reshape(-1, width),
        input_grad.reshape(-1, width),
    )
    columns = vector_first.shape[1]
    vector_cols = lax.dynamic_slice_in_dim(vectors, place * columns, columns, 1)
    vector_total = lax.dynamic_slice(vector_total, (0, place * columns), (PIECES, columns))
    updated_vectors = adam_step(vector_cols, vector_total, vector_first, vector_second, VEC_RATE)
    return (
        block_out.reshape(inputs.shape),
        input_grad.reshape(inputs.shape),
        *updated,
        *updated_vectors,
    )


def solution(mesh):
    in_specs = (
        P("dp", "blk", None),
        P("dp", "blk", None),
        P("dp", None),
        P(),
        P("dp", "blk", None),
        P("dp", "blk", None),
        P("dp", "blk", None),
        P(),
        P(None, "blk"),
        P(None, "blk"),
    )
    out_specs = (
        P("dp", "blk", None),
        P("dp", "blk", None),
        P("dp", "blk", None),
        P("dp", "blk", None),
        P("dp", "blk", None),
        P(None, "blk"),
        P(None, "blk"),
        P(None, "blk"),
    )
    paired = mesh.shape["blk"] == 2 and mesh.shape["dp"] == 16
    shards = shards_paired if paired else shards_any
    return jax.shard_map(shards, mesh=mesh, in_specs=in_specs, out_specs=out_specs, check_vma=False)
```

```python
from functools import partial

import jax
import jax.numpy as jnp
from jax import lax
from jax.experimental import pallas as pl
from jax.experimental.pallas import tpu as pltpu
from jax.sharding import PartitionSpec as P

D = 768
FF = 3072
HEADS = 12
HEAD_DIM = 64
LEN = 1024
CAP = 3
STEP = 10
PIECES = 12


EPS_NORM = 1e-05
BETA_ONE = 0.9
BETA_TWO = 0.999
RATE = 0.04
VEC_RATE = 0.25
DECAY = 0.01
ADAM_EPS = 1e-08


def normalize(values_in, gain, shift):
    center = jnp.mean(values_in, axis=-1, keepdims=True)
    offset = values_in - center
    spread = jnp.mean(offset * offset, axis=-1, keepdims=True)
    return offset * lax.rsqrt(spread + EPS_NORM) * gain + shift


def adam_step(weight, grad, first, second, rate):
    first_new = BETA_ONE * first + (1.0 - BETA_ONE) * grad
    second_new = BETA_TWO * second + (1.0 - BETA_TWO) * grad * grad
    corrected = (
        first_new
        / (1.0 - BETA_ONE**STEP)
        / (jnp.sqrt(second_new / (1.0 - BETA_TWO**STEP)) + ADAM_EPS)
    )
    return (weight - rate * (corrected + DECAY * weight), first_new, second_new)


def shards_any(
    inputs,
    cotangent,
    doc_lengths,
    owner_list,
    master,
    first_moment,
    second_moment,
    vectors,
    vector_first,
    vector_second,
):
    rows_here, span, width = inputs.shape
    tokens_here = rows_here * span
    fold = FF // D
    scale = HEAD_DIM ** (-0.5)
    place = lax.axis_index("blk")
    f32 = jnp.float32
    b16 = jnp.bfloat16
    order = jnp.arange(PIECES)
    same_owner = owner_list[:, None] == owner_list[None, :]
    ranks = jnp.sum(same_owner & (order[None, :] < order[:, None]), axis=1)
    slot_of = owner_list * CAP + ranks

    mine = (owner_list == lax.axis_index("dp"))[:, None, None]
    tile_rows = lax.psum(jnp.where(mine, master[ranks], 0.0).astype(b16), "dp")
    tiles = lax.all_gather(tile_rows, "blk", axis=1, tiled=True)
    query_weight = tiles[0]
    key_weight = tiles[1]
    value_weight = tiles[2]
    out_weight = tiles[3]
    up_weight = jnp.transpose(tiles[4 : 4 + fold], (1, 0, 2)).reshape(width, FF)
    down_weight = tiles[4 + fold :].reshape(FF, width)
    flat_in = inputs.reshape(tokens_here, width).astype(f32)
    normed_one = normalize(flat_in, vectors[0], vectors[1]).astype(b16)
    queries = (jnp.dot(normed_one, query_weight, preferred_element_type=f32) + vectors[4]).astype(
        b16
    )
    keys_here = jnp.dot(normed_one, key_weight, preferred_element_type=f32).astype(b16)
    values_here = (
        jnp.dot(normed_one, value_weight, preferred_element_type=f32) + vectors[5]
    ).astype(b16)
    query_heads = queries.reshape(rows_here, span, HEADS, HEAD_DIM)
    first_len = doc_lengths[:, 0]
    query_seg = (place * span + jnp.arange(span))[None, :] >= first_len[:, None]

    def block_scores(key_block, start):
        count = key_block.shape[1]
        key_heads = key_block.reshape(rows_here, count, HEADS, HEAD_DIM)
        raw = (
            jnp.einsum("rqhd,rkhd->rhqk", query_heads, key_heads, preferred_element_type=f32)
            * scale
        )
        key_seg = (start + jnp.arange(count))[None, :] >= first_len[:, None]
        allowed = query_seg[:, None, :, None] == key_seg[:, None, None, :]
        return (raw, allowed)

    key_rows = keys_here.reshape(rows_here, span, width)
    value_rows = values_here.reshape(rows_here, span, width)
    top = jnp.full((rows_here, HEADS, span), -1e30, f32)
    key_block = lax.all_gather(key_rows, "blk", axis=1, tiled=True)
    value_block = lax.all_gather(value_rows, "blk", axis=1, tiled=True)
    count = key_block.shape[1]
    raw, allowed = block_scores(key_block, jnp.int32(0))
    new_top = jnp.maximum(top, jnp.max(jnp.where(allowed, raw, -1e30), axis=-1))
    weights = jnp.where(allowed, jnp.exp(raw - new_top[..., None]), 0.0)
    value_heads = value_block.reshape(rows_here, count, HEADS, HEAD_DIM)
    update = jnp.einsum(
        "rhqk,rkhd->rhqd", weights.astype(b16), value_heads, preferred_element_type=f32
    )
    total = jnp.sum(weights, axis=-1)
    log_total = new_top + jnp.log(total)
    context_raw = update / total[..., None]
    context_low = jnp.transpose(context_raw, (0, 2, 1, 3)).reshape(tokens_here, width).astype(b16)
    residual = flat_in + (jnp.dot(context_low, out_weight, preferred_element_type=f32) + vectors[6])
    normed_two = normalize(residual, vectors[2], vectors[3]).astype(b16)
    hidden = jnp.dot(normed_two, up_weight, preferred_element_type=f32) + vectors[8:].reshape(FF)
    gelu_exact = partial(jax.nn.gelu, approximate=False)
    active, gelu_pull = jax.vjp(gelu_exact, hidden)
    active_low = active.astype(b16)
    block_out = (
        residual + (jnp.dot(active_low, down_weight, preferred_element_type=f32) + vectors[7])
    ).reshape(rows_here, span, width)
    grad_out = cotangent.reshape(tokens_here, width)
    down_grad = jnp.einsum("tf,td->fd", active_low, grad_out, preferred_element_type=f32)
    down_sum = jnp.sum(grad_out, axis=0, dtype=f32)
    grad_active = jnp.einsum("td,fd->tf", grad_out, down_weight, preferred_element_type=f32)
    grad_hidden = gelu_pull(grad_active)[0].astype(b16)
    up_grad = jnp.einsum("td,tf->df", normed_two, grad_hidden, preferred_element_type=f32)
    up_sum = jnp.sum(grad_hidden, axis=0, dtype=f32)
    ffn_tiles = jnp.concatenate(
        [
            jnp.transpose(up_grad.reshape(width, fold, width), (1, 0, 2)),
            down_grad.reshape(fold, width, width),
        ],
        axis=0,
    )
    grad_normed_two = jnp.einsum("tf,df->td", grad_hidden, up_weight, preferred_element_type=f32)
    unused, second_pull = jax.vjp(normalize, residual, vectors[2], vectors[3])
    residual_part, gain_two_grad, shift_two_grad = second_pull(grad_normed_two)
    grad_residual = grad_out.astype(f32) + residual_part
    grad_attended = grad_residual.astype(b16)
    out_grad = jnp.einsum("tm,td->md", context_low, grad_attended, preferred_element_type=f32)
    out_sum = jnp.sum(grad_attended, axis=0, dtype=f32)
    grad_context = jnp.einsum(
        "td,md->tm", grad_attended, out_weight, preferred_element_type=f32
    ).astype(b16)
    grad_heads = grad_context.reshape(rows_here, span, HEADS, HEAD_DIM)
    delta = jnp.einsum("rqhd,rhqd->rhq", grad_heads.astype(f32), context_raw)
    key_all, value_all = (
        lax.all_gather(key_rows, "blk", axis=1, tiled=True),
        lax.all_gather(value_rows, "blk", axis=1, tiled=True),
    )
    key_size = min(512, LEN)

    def back_block(index, carry):
        grad_query, key_total, value_total = carry
        start = index * key_size
        key_block = lax.dynamic_slice_in_dim(key_all, start, key_size, 1)
        value_block = lax.dynamic_slice_in_dim(value_all, start, key_size, 1)
        raw, allowed = block_scores(key_block, start)
        weights_back = jnp.where(allowed, jnp.exp(raw - log_total[..., None]), 0.0)
        key_heads = key_block.reshape(rows_here, key_size, HEADS, HEAD_DIM)
        value_heads = value_block.reshape(rows_here, key_size, HEADS, HEAD_DIM)
        value_grad = jnp.einsum(
            "rhqk,rqhd->rkhd", weights_back.astype(b16), grad_heads, preferred_element_type=f32
        )
        weight_grad = jnp.einsum(
            "rqhd,rkhd->rhqk", grad_heads, value_heads, preferred_element_type=f32
        )
        score_grad = (weights_back * (weight_grad - delta[..., None])).astype(b16)
        grad_query = (
            grad_query
            + jnp.einsum("rhqk,rkhd->rqhd", score_grad, key_heads, preferred_element_type=f32)
            * scale
        )
        key_grad = (
            jnp.einsum("rhqk,rqhd->rkhd", score_grad, query_heads, preferred_element_type=f32)
            * scale
        )
        key_total = lax.dynamic_update_slice_in_dim(
            key_total, key_grad.reshape(rows_here, key_size, width), start, 1
        )
        value_total = lax.dynamic_update_slice_in_dim(
            value_total, value_grad.reshape(rows_here, key_size, width), start, 1
        )
        return (grad_query, key_total, value_total)

    zero_rows = jnp.zeros((rows_here, LEN, width), f32)
    grad_query, key_total, value_total = lax.fori_loop(
        0,
        LEN // key_size,
        back_block,
        (jnp.zeros((rows_here, span, HEADS, HEAD_DIM), f32), zero_rows, zero_rows),
    )
    key_grad_here, value_grad_here = (
        lax.psum_scatter(
            key_total.astype(jnp.bfloat16), "blk", scatter_dimension=1, tiled=True
        ).astype(jnp.float32),
        lax.psum_scatter(
            value_total.astype(jnp.bfloat16), "blk", scatter_dimension=1, tiled=True
        ).astype(jnp.float32),
    )
    query_low = grad_query.reshape(tokens_here, width).astype(b16)
    key_low = key_grad_here.reshape(tokens_here, width).astype(b16)
    value_low = value_grad_here.reshape(tokens_here, width).astype(b16)
    query_tile = jnp.einsum("td,te->de", normed_one, query_low, preferred_element_type=f32)
    key_tile = jnp.einsum("td,te->de", normed_one, key_low, preferred_element_type=f32)
    value_tile = jnp.einsum("td,te->de", normed_one, value_low, preferred_element_type=f32)
    grad_normed_one = (
        jnp.einsum("te,de->td", query_low, query_weight, preferred_element_type=f32)
        + jnp.einsum("te,de->td", key_low, key_weight, preferred_element_type=f32)
        + jnp.einsum("te,de->td", value_low, value_weight, preferred_element_type=f32)
    )
    unused, first_pull = jax.vjp(normalize, flat_in, vectors[0], vectors[1])
    input_part, gain_one_grad, shift_one_grad = first_pull(grad_normed_one)
    input_grad = (grad_residual + input_part).reshape(rows_here, span, width)
    vector_grads = jnp.concatenate(
        [
            jnp.stack(
                [
                    gain_one_grad,
                    shift_one_grad,
                    gain_two_grad,
                    shift_two_grad,
                    jnp.sum(query_low, axis=0, dtype=f32),
                    jnp.sum(value_low, axis=0, dtype=f32),
                    out_sum,
                    down_sum,
                ]
            ),
            up_sum.reshape(fold, width),
        ],
        axis=0,
    )
    attn_tiles = jnp.stack([query_tile, key_tile, value_tile, out_grad])
    piece_share, vector_share = (
        lax.psum_scatter(
            jnp.concatenate([attn_tiles, ffn_tiles], axis=0).astype(jnp.bfloat16),
            "blk",
            scatter_dimension=1,
            tiled=True,
        ).astype(jnp.float32),
        lax.psum_scatter(
            vector_grads.astype(jnp.bfloat16), "blk", scatter_dimension=1, tiled=True
        ).astype(jnp.float32),
    )
    own_slots = lax.axis_index("dp") * CAP + jnp.arange(CAP)
    pick = (own_slots[:, None] == slot_of[None, :]).astype(f32)
    occupied = jnp.sum(pick, axis=1)[:, None, None]
    total_share, vector_total = (
        lax.psum(piece_share.astype(jnp.bfloat16), "dp").astype(jnp.float32),
        lax.psum(vector_share.astype(jnp.bfloat16), "dp").astype(jnp.float32),
    )
    slot_grads = jnp.einsum("cp,prd->crd", pick, total_share, precision=lax.Precision.HIGHEST)
    new_master, new_first, new_second = adam_step(
        master, slot_grads, first_moment, second_moment, RATE
    )
    columns = vector_first.shape[1]
    vector_cols = lax.dynamic_slice_in_dim(vectors, place * columns, columns, 1)
    new_vectors, new_vector_first, new_vector_second = adam_step(
        vector_cols, vector_total, vector_first, vector_second, VEC_RATE
    )
    return (
        block_out,
        input_grad,
        new_master * occupied,
        new_first * occupied,
        new_second * occupied,
        new_vectors,
        new_vector_first,
        new_vector_second,
    )


f32 = jnp.float32
b16 = jnp.bfloat16
LOG2E = 1.4426950408889634
MIB = 1024 * 1024
PAIRS = HEADS // 2
PAIR = 2 * HEAD_DIM


def dot_nn(left, right):
    return lax.dot_general(left, right, (((1,), (0,)), ((), ())), preferred_element_type=f32)


def dot_nt(left, right):
    return lax.dot_general(left, right, (((1,), (1,)), ((), ())), preferred_element_type=f32)


def dot_tn(left, right):
    return lax.dot_general(left, right, (((0,), (0,)), ((), ())), preferred_element_type=f32)


def norm_parts(values_in):
    center = jnp.mean(values_in, axis=-1, keepdims=True)
    offset = values_in - center
    spread = jnp.mean(offset * offset, axis=-1, keepdims=True)
    rstd = lax.rsqrt(spread + EPS_NORM)
    return offset * rstd, rstd


def norm_back(grad, unit, rstd, gain):
    scaled = grad * gain
    first = jnp.mean(scaled, axis=-1, keepdims=True)
    second = jnp.mean(scaled * unit, axis=-1, keepdims=True)
    return rstd * (scaled - first - unit * second)


def gelu_parts(value):
    bell = jnp.exp2(value * value * (-0.5 * LOG2E))
    ratio = pl.reciprocal(1.0 + (0.3275911 * 0.7071067811865476) * jnp.abs(value))
    poly = 0.5 * 1.061405429
    poly = poly * ratio + 0.5 * -1.453152027
    poly = poly * ratio + 0.5 * 1.421413741
    poly = poly * ratio + 0.5 * -0.284496736
    poly = poly * ratio + 0.5 * 0.254829592
    tail = poly * ratio * bell
    cdf = jnp.where(value >= 0.0, 1.0 - tail, tail)
    return value * cdf, cdf + value * (bell * 0.3989422804014327)


def head_only(block, head):
    lane = lax.broadcasted_iota(jnp.int32, block.shape, 1)
    keep = (lane >= head * HEAD_DIM) & (lane < (head + 1) * HEAD_DIM)
    return jnp.where(keep, block, jnp.zeros_like(block))


def feed_kernel(
    c_ref, o_ref, x_ref, g_ref, w_ref, vec_ref,
    y_ref, r_ref, d_ref, sums_ref, tiles_ref,
    acc_ref, stage_ref, sem_ref,
):
    fold = FF // D
    step = pl.program_id(0)

    @pl.when(step == 0)
    def clear():
        acc_ref[...] = jnp.zeros_like(acc_ref)
        sums_ref[...] = jnp.zeros_like(sums_ref)

    residual = x_ref[...].astype(f32) + (dot_nn(c_ref[...], w_ref[0]) + vec_ref[6:7, :])
    unit, rstd = norm_parts(residual)
    gain = vec_ref[2:3, :]
    normed = (unit * gain + vec_ref[3:4, :]).astype(b16)
    turned = normed.T
    cot = g_ref[...]
    out = residual + vec_ref[7:8, :]
    grad = jnp.zeros_like(out)

    for part in range(fold):
        hidden = dot_nn(normed, w_ref[1 + part]) + vec_ref[8 + part : 9 + part, :]
        pulled = dot_nt(cot, w_ref[1 + fold + part])
        active, slope = gelu_parts(hidden)
        active = active.astype(b16)
        pulled = (pulled * slope).astype(b16)
        out = out + dot_nn(active, w_ref[1 + fold + part])
        grad = grad + dot_nt(pulled, w_ref[1 + part])
        acc_ref[1 + part] += dot_nn(turned, pulled)
        acc_ref[1 + fold + part] += dot_tn(active, cot)
        sums_ref[8 + part : 9 + part, :] += jnp.sum(pulled.astype(f32), 0, keepdims=True)
    y_ref[...] = out.astype(b16)
    wide = cot.astype(f32)
    sums_ref[2:3, :] += jnp.sum(grad * unit, 0, keepdims=True)
    sums_ref[3:4, :] += jnp.sum(grad, 0, keepdims=True)
    sums_ref[7:8, :] += jnp.sum(wide, 0, keepdims=True)
    back = wide + norm_back(grad, unit, rstd, gain)
    r_ref[...] = back.astype(b16)
    low = back.astype(b16)
    sums_ref[6:7, :] += jnp.sum(low.astype(f32), 0, keepdims=True)
    d_ref[...] = dot_nt(w_ref[0], low).astype(b16)
    acc_ref[0] += dot_nn(o_ref[...], low)

    @pl.when(step == pl.num_programs(0) - 1)
    def send():
        count = 1 + 2 * fold
        copies = []
        for part in range(count):
            if part >= 2:
                copies[part - 2].wait()
            stage_ref[part % 2] = acc_ref[part].astype(b16)
            copy = pltpu.make_async_copy(stage_ref.at[part % 2], tiles_ref.at[part], sem_ref.at[part % 2])
            copy.start()
            copies.append(copy)
        copies[count - 2].wait()
        copies[count - 1].wait()


def feed(context, turned, x, cot, weights, vectors):
    tokens = x.shape[0]
    size = 256
    count = 1 + 2 * (FF // D)
    token_block = pl.BlockSpec((size, D), lambda i: (i, 0))
    turned_block = pl.BlockSpec((D, size), lambda i: (0, i))
    return pl.pallas_call(
        feed_kernel,
        grid=(tokens // size,),
        in_specs=[
            token_block,
            turned_block,
            token_block,
            token_block,
            pl.BlockSpec((count, D, D), lambda i: (0, 0, 0), pipeline_mode=pl.Buffered(1)),
            pl.BlockSpec((PIECES, D), lambda i: (0, 0)),
        ],
        out_specs=[
            token_block,
            token_block,
            turned_block,
            pl.BlockSpec((16, D), lambda i: (0, 0)),
            pl.BlockSpec(memory_space=pl.ANY),
        ],
        out_shape=[
            jax.ShapeDtypeStruct((tokens, D), b16),
            jax.ShapeDtypeStruct((tokens, D), b16),
            jax.ShapeDtypeStruct((D, tokens), b16),
            jax.ShapeDtypeStruct((16, D), f32),
            jax.ShapeDtypeStruct((count, D, D), b16),
        ],
        scratch_shapes=[
            pltpu.VMEM((count, D, D), f32),
            pltpu.VMEM((2, D, D), b16),
            pltpu.SemaphoreType.DMA((2,)),
        ],
        compiler_params=pltpu.CompilerParams(vmem_limit_bytes=60 * MIB),
        cost_estimate=pl.CostEstimate(
            flops=6 * count * tokens * D * D,
            bytes_accessed=18 * tokens * D + 4 * count * D * D,
            transcendentals=2 * tokens * FF,
        ),
        name="feed",
    )(context, turned, x, cot, weights, vectors)


MESH = pl.DeviceIdType.MESH
HALF = D // 2
FLOWS = 2
FLOW = HALF // FLOWS
NEAR = FLOW // 2
KEEP = NEAR // 2
WIDE = 3 * PAIR
REST = PIECES - 3
GROUPS = ((0, 1), (1, 2), (3, 3))
CHUNKS = len(GROUPS)


class Place:
    def __init__(self):
        self.me = lax.axis_index("dp")
        self.core = lax.axis_index("blk")
        self.bits = [lax.rem(self.me // weight, 2) for weight in (1, 2, 4, 8)]
        self.chips = [
            self.me + weight - 2 * weight * bit for weight, bit in zip((1, 2, 4, 8), self.bits)
        ]
        self.partners = [{"dp": chip} for chip in self.chips]
        low, high = self.bits[2:]
        self.inner = low != high
        self.across = {"dp": self.me + 4 - 8 * low + 8 - 16 * high}
        self.other = 1 - self.core
        self.twin = {"blk": self.other}

    def greet(self):
        barrier = pltpu.get_barrier_semaphore()
        for device in self.partners + [self.across, self.twin]:
            pl.semaphore_signal(barrier, 1, device_id=device, device_id_type=MESH)
        pl.semaphore_wait(barrier, 6)

    def flow(self, index):
        first, second = (0, 1) if index == 0 else (1, 0)
        base = index * FLOW
        near = base + self.bits[first] * NEAR
        far = base + NEAR - self.bits[first] * NEAR
        keep = near + self.bits[second] * KEEP
        give = near + KEEP - self.bits[second] * KEEP
        return first, second, near, far, keep, give


def remote(source, target, send, receive, device):
    return pltpu.make_async_remote_copy(
        src_ref=source,
        dst_ref=target,
        send_sem=send,
        recv_sem=receive,
        device_id=device,
        device_id_type=MESH,
    )


def rows_at(start, count):
    return pl.ds(pl.multiple_of(start, 16), count)


class Spread:
    def __init__(self, place, owner, rank, slots, land, gift, sems):
        self.place, self.owner, self.rank = place, owner, rank
        self.slots, self.land, self.gift, self.sems = slots, land, gift, sems

    def cols(self, chunk):
        return pl.ds(GROUPS[chunk][0] * PAIR, GROUPS[chunk][1] * PAIR)

    def first_copy(self, chunk, index):
        first, second, near, far, keep, give = self.place.flow(index)
        return remote(
            self.slots.at[:, rows_at(far, NEAR), self.cols(chunk)],
            self.land[chunk].at[index],
            self.sems[0].at[chunk, index, 0],
            self.sems[1].at[chunk, index, 0],
            self.place.partners[first],
        )

    def second_copy(self, chunk, index, which):
        first, second, near, far, keep, give = self.place.flow(index)
        if which == 0:
            source = self.slots.at[:, rows_at(give, KEEP), self.cols(chunk)]
        else:
            source = self.land[chunk].at[index, :, rows_at(give - near, KEEP)]
        return remote(
            source,
            self.gift[chunk].at[index, pl.ds(which * CAP, CAP)],
            self.sems[0].at[chunk, index, 1 + which],
            self.sems[1].at[chunk, index, 1 + which],
            self.place.partners[second],
        )

    def step(self, chunk, index):
        for flow in range(FLOWS):
            if index == 0:
                self.first_copy(chunk, flow).start()
                self.second_copy(chunk, flow, 0).start()
            if index == 1:
                self.first_copy(chunk, flow).wait()
                self.second_copy(chunk, flow, 1).start()
            if index == 2:
                self.second_copy(chunk, flow, 0).wait()
                self.second_copy(chunk, flow, 1).wait()

    def piece(self, tile, index, chunk, start, count):
        first, second, near, far, keep, give = self.place.flow(index)
        owner, rank = self.owner[tile], self.rank[tile]
        bits = [lax.rem(owner, 2), lax.rem(owner // 2, 2)]
        apart = [bit != mine for bit, mine in zip(bits, self.place.bits)]
        cols = pl.ds(start, count)
        mine = self.slots[rank, rows_at(keep, KEEP), pl.ds(GROUPS[chunk][0] * PAIR + start, count)]
        firsts = self.land[chunk][index, rank, rows_at(keep - near, KEEP), cols]
        gifts = self.gift[chunk][index, jnp.where(apart[first], CAP, 0) + rank, :, cols]
        value = jnp.where(apart[second], gifts, jnp.where(apart[first], firsts, mine))
        layer = owner // 4 == self.place.me // 4
        return jnp.where(layer, value, jnp.zeros_like(value))


class Column:
    steps = 4

    def __init__(self, place, kept, land, sems):
        self.place, self.kept, self.land, self.sems = place, kept, land, sems

    def copy(self, index):
        device = self.place.across if index == 1 else self.place.partners[2]
        return remote(
            self.kept, self.land.at[index % 2], self.sems[0].at[index], self.sems[1].at[index], device
        )

    def add(self, index):
        self.kept[...] = (self.kept[...].astype(f32) + self.land[index].astype(f32)).astype(b16)


def both_flows(flow):
    return pl.ds(flow * KEEP, KEEP)


def column_step(place, column, index):
    @pl.when(place.inner)
    def inner():
        if index == 1:
            column.copy(0).wait_recv()
            column.add(0)
            column.copy(1).start()
        if index == 2:
            column.copy(1).wait()
            column.add(1)
            column.copy(2).start()
        if index == 3:
            column.copy(2).wait_send()

    @pl.when(jnp.logical_not(place.inner))
    def outer():
        if index == 0:
            column.copy(0).start()
        if index == 1:
            column.copy(0).wait_send()
        if index == 3:
            column.copy(2).wait_recv()
            column.kept[...] = column.land[0]


class Item:
    steps = 7

    def __init__(self, place, work, kept, land, sems, load, store=None):
        self.place, self.work, self.kept, self.land, self.sems = place, work, kept, land, sems
        self.load, self.store = load, store
        self.base = place.core * HALF

    def copy(self, flow, index):
        first, second, near, far, keep, give = self.place.flow(flow)
        kept = self.work.at[:, rows_at(self.base + keep, KEEP)]
        half = self.work.at[:, rows_at(self.base + near, NEAR)]
        source, device = [
            (kept, self.place.partners[second]),
            (half, self.place.partners[first]),
        ][index]
        number = 3 + 2 * flow + index
        return remote(source, source, self.sems[0].at[number], self.sems[1].at[number], device)

    def pair(self):
        rows = self.work.at[:, rows_at(self.base, HALF)]
        return remote(rows, rows, self.sems[0].at[7], self.sems[1].at[7], self.place.twin)

    def step(self, index):
        if index == 0:
            for flow in range(FLOWS):
                self.load(self.kept, both_flows(flow), flow)
        if index <= 3:
            column_step(self.place, Column(self.place, self.kept, self.land, self.sems), index)
        for flow in range(FLOWS):
            if index == 3:
                rows = rows_at(self.base + self.place.flow(flow)[4], KEEP)
                self.work[:, rows] = self.kept[:, both_flows(flow)]
            if 4 <= index <= 5:
                self.copy(flow, index - 4).wait()
            if 3 <= index <= 4:
                self.copy(flow, index - 3).start()
        if index == 5:
            self.pair().start()
        if index == 6:
            self.pair().wait()
            self.store().start()


REST_GROUPS = tuple((index, 1) for index in range(REST))
PAIR_CHUNK = (0, 1, 1, 2, 2, 2)
FRONT_PAIRS = (2, 4, 5, 6, 7, 8)
FRONT_REST = (6, 7, 8, 9, 10, 11, 12, 13, 14)
FRONT_LEAD = 9
FRONT_CHUNKS = ((0, 1, 2), (1, 3, 4), (3, 5, 6))
FRONT_PHASES = 4


def front_kernel(
    owner, lengths, master, vec_ref, x_in, c_in,
    x_out, c_out, n_out, one_out, two_out, q_ref, k_ref, v_ref, p_ref, r_ref, o_ref, ctx_ref,
    rank, rows_ref, normed, keys, turned_values, scores, slots,
    land_one, land_two, land_three, gift_one, gift_two, gift_three,
    one, one_kept, one_land, two, two_kept, two_land,
    spread_send, spread_recv, one_send, one_recv, two_send, two_recv,
    swap_send, swap_recv, swap_local, store_sem,
):
    pair = pl.program_id(0)
    row = pl.program_id(1)
    grid_step = pair * 2 + row
    place = Place()
    rows, span = x_in.shape[0] // 2, x_in.shape[1]
    land = (land_one, land_two, land_three)
    gift = (gift_one, gift_two, gift_three)
    spread = Spread(place, owner, rank, slots, land, gift, (spread_send, spread_recv))

    def swaps(index):
        source, target = [(x_in, rows_ref), (c_in, c_out)][index]
        here = pl.ds(place.core * span, span)
        near = pltpu.make_async_copy(
            source.at[pl.ds(place.core * rows, rows)], target.at[:, here], swap_local.at[index]
        )
        far = remote(
            source.at[pl.ds(place.other * rows, rows)],
            target.at[:, here],
            swap_send.at[index],
            swap_recv.at[index],
            place.twin,
        )
        return near, far

    def row_store():
        return pltpu.make_async_copy(rows_ref, x_out, store_sem.at[PAIRS + REST])

    def normed_store():
        return pltpu.make_async_copy(normed, n_out, store_sem.at[PAIRS + REST + 1])

    def pair_item(group):
        span_of = pl.ds(group, 1)

        def load(work, where, flow):
            chunk = PAIR_CHUNK[group]
            for tile in range(3):
                part = spread.piece(tile, flow, chunk, (group - GROUPS[chunk][0]) * PAIR, PAIR)
                work[0, where, pl.ds(tile * PAIR, PAIR)] = part

        def store():
            return pltpu.make_async_copy(one.at[span_of], one_out.at[span_of], store_sem.at[group])

        sems = (one_send.at[group], one_recv.at[group])
        return Item(place, one.at[span_of], one_kept.at[span_of], one_land.at[:, span_of], sems, load, store)

    def rest_item(group):
        first, count = REST_GROUPS[group]
        span_of = pl.ds(first, count)

        def load(work, where, flow):
            for index in range(count):
                for chunk, (start, wide) in enumerate(GROUPS):
                    part = spread.piece(3 + first + index, flow, chunk, 0, wide * PAIR)
                    work[index, where, pl.ds(start * PAIR, wide * PAIR)] = part

        def store():
            return pltpu.make_async_copy(
                two.at[span_of], two_out.at[span_of], store_sem.at[PAIRS + group]
            )

        sems = (two_send.at[group], two_recv.at[group])
        return Item(place, two.at[span_of], two_kept.at[span_of], two_land.at[:, span_of], sems, load, store)

    def tick(number, phase):
        for chunk, ticks in enumerate(FRONT_CHUNKS):
            if phase == 0 and number in ticks:
                spread.step(chunk, ticks.index(number))
        for index, start in enumerate(FRONT_PAIRS):
            if index % 2 * 2 == phase and 0 <= number - start < Item.steps:
                pair_item(index).step(number - start)
        for index, start in enumerate(FRONT_REST):
            if (index + 1) % FRONT_PHASES == phase and 0 <= number - start < Item.steps:
                rest_item(index).step(number - start)

    def both(number):
        for phase in range(FRONT_PHASES):
            tick(number, phase)

    @pl.when(grid_step == 0)
    def lead():
        slots[...] = master[...].astype(b16)
        for tile in range(PIECES):
            count = jnp.int32(0)
            for before in range(tile):
                count = count + (owner[before] == owner[tile]).astype(jnp.int32)
            rank[tile] = jnp.minimum(count, CAP - 1)
        place.greet()
        for copy in swaps(0):
            copy.start()
        both(0)
        for copy in swaps(1):
            copy.start()
        for copy in swaps(0):
            copy.wait()
        row_store().start()

        def norm_rows(index, carry):
            for part in range(rows):
                for block in range(4):
                    where = pl.ds(pl.multiple_of(index * 128 + block * 32, 32), 32)
                    unit, unused = norm_parts(rows_ref[part, where].astype(f32))
                    low = (unit * vec_ref[0:1, :] + vec_ref[1:2, :]).astype(b16)
                    normed[pl.ds(pl.multiple_of(part * LEN + index * 128 + block * 32, 32), 32)] = low
            return carry

        both(1)
        lax.fori_loop(0, LEN // 128, norm_rows, 0)
        normed_store().start()
        for number in range(2, FRONT_LEAD):
            both(number)

    for number in range(2 * PAIRS):
        pl.when(grid_step == number)(partial(tick, FRONT_LEAD + number, 0))

    @pl.when(row == 0)
    def project():
        lanes = pl.ds(pl.multiple_of(pair * PAIR, PAIR), PAIR)
        weight = one[pair]

        def part(index, carry):
            where = pl.ds(pl.multiple_of(index * 512, 512), 512)
            both = dot_nn(normed[where], weight)
            queries = both[:, :PAIR] + vec_ref[4:5, lanes]
            queries = (queries * (HEAD_DIM**-0.5 * LOG2E)).astype(b16)
            q_ref[:, where] = queries.T
            low = both[:, PAIR : 2 * PAIR].astype(b16)
            keys[where] = low
            k_ref[:, where] = low.T
            values = (both[:, 2 * PAIR :] + vec_ref[5:6, lanes]).astype(b16)
            v_ref[where] = values
            turned_values[:, where] = values.T
            return carry

        lax.fori_loop(0, normed.shape[0] // 512, part, 0)

    half = LEN // 2
    start = pl.multiple_of(row * LEN, LEN)
    split = lengths[place.core * rows + row, 0] < LEN
    shift = jnp.where(split, jnp.float32(-1e30), jnp.float32(0.0))

    quarter = LEN // 4
    units = [(head, step) for head in range(2) for step in range(2)]

    def score_block(unit, block, peak):
        head, step = units[unit]
        rows_here = pl.ds(pl.multiple_of(start + block * quarter, quarter), quarter)
        queries = q_ref[:, pl.ds(pl.multiple_of(start + step * half, half), half)]
        raw = dot_nn(head_only(keys[rows_here], head), queries)
        if block // 2 != step:
            raw = raw + shift
        scores[unit % 2, block * quarter : (block + 1) * quarter] = raw
        best = jnp.max(raw.reshape(-1, 8, half), axis=0)
        return best if peak is None else jnp.maximum(peak, best)

    def context_block(unit, block, total):
        head, step = units[unit]
        part = slice(head * HEAD_DIM, (head + 1) * HEAD_DIM)
        cols = pl.ds(pl.multiple_of(start + block * quarter, quarter), quarter)
        here = slice(step * half, (step + 1) * half)
        term = dot_nn(
            turned_values[part, cols], p_ref[head, block * quarter : (block + 1) * quarter, here]
        )
        return term if total is None else total + term

    def context_store(unit, total, recip):
        head, step = units[unit]
        part = slice(head * HEAD_DIM, (head + 1) * HEAD_DIM)
        o_ref[part, step * half : (step + 1) * half] = (total * recip).astype(b16)

    peak = None
    for block in range(4):
        peak = score_block(0, block, peak)
    before = None
    for unit, (head, step) in enumerate(units):
        if unit > 0:
            for number in range(2 * PAIRS):
                pl.when(grid_step == number)(partial(tick, FRONT_LEAD + number, unit))
        here = slice(step * half, (step + 1) * half)
        top = jnp.max(peak, 0, keepdims=True)
        total = jnp.zeros((8, half), f32)
        peak, context = None, None
        for block in range(4):
            if unit + 1 < len(units):
                peak = score_block(unit + 1, block, peak)
            for small in range(4 * block, 4 * block + 4):
                rows_here = slice(small * 64, (small + 1) * 64)
                value = jnp.exp2(scores[unit % 2, rows_here] - top)
                total = total + jnp.sum(value.reshape(-1, 8, half), axis=0)
                p_ref[head, rows_here, here] = value.astype(b16)
            if unit > 0:
                context = context_block(unit - 1, block, context)
        if unit > 0:
            context_store(unit - 1, context, before)
        before = 1.0 / jnp.sum(total, 0, keepdims=True)
        r_ref[0, head : head + 1, here] = before
    context = None
    for block in range(4):
        context = context_block(3, block, context)
    context_store(3, context, before)
    ctx_ref[...] = o_ref[...].T

    @pl.when(grid_step == 2 * PAIRS - 1)
    def finish_copies():
        for copy in swaps(1):
            copy.wait()
        row_store().wait()
        normed_store().wait()
        for group in range(PAIRS):
            pair_item(group).store().wait()
        for group in range(REST):
            rest_item(group).store().wait()


def front(owner, lengths, master, vectors, inputs, cotangent):
    rows, span = inputs.shape[0] // 2, inputs.shape[1]
    tokens = rows * LEN
    any_spec = pl.BlockSpec(memory_space=pl.ANY)
    smem = pl.BlockSpec(memory_space=pltpu.SMEM)
    whole = jax.ShapeDtypeStruct((rows, LEN, D), b16)
    dma = pltpu.SemaphoreType.DMA
    return pl.pallas_call(
        front_kernel,
        grid=(PAIRS, rows),
        in_specs=[
            smem,
            smem,
            pl.BlockSpec((CAP, HALF, D), lambda h, r: (0, 0, 0), pipeline_mode=pl.Buffered(1)),
            pl.BlockSpec((PIECES, D), lambda h, r: (0, 0)),
            any_spec,
            any_spec,
        ],
        out_specs=[any_spec] * 5
        + [
            pl.BlockSpec((PAIR, tokens), lambda h, r: (h, 0)),
            pl.BlockSpec((PAIR, tokens), lambda h, r: (h, 0)),
            pl.BlockSpec((tokens, PAIR), lambda h, r: (0, h)),
            pl.BlockSpec((2, LEN, LEN), lambda h, r: (h * 2 + r, 0, 0)),
            pl.BlockSpec((1, 2, LEN), lambda h, r: (h * 2 + r, 0, 0)),
            pl.BlockSpec((PAIR, LEN), lambda h, r: (h, r)),
            pl.BlockSpec((LEN, PAIR), lambda h, r: (r, h)),
        ],
        out_shape=[
            whole,
            whole,
            jax.ShapeDtypeStruct((tokens, D), b16),
            jax.ShapeDtypeStruct((PAIRS, D, WIDE), b16),
            jax.ShapeDtypeStruct((REST, D, D), b16),
            jax.ShapeDtypeStruct((D, tokens), b16),
            jax.ShapeDtypeStruct((D, tokens), b16),
            jax.ShapeDtypeStruct((tokens, D), b16),
            jax.ShapeDtypeStruct((rows * HEADS, LEN, LEN), b16),
            jax.ShapeDtypeStruct((rows * PAIRS, 2, LEN), f32),
            jax.ShapeDtypeStruct((D, tokens), b16),
            jax.ShapeDtypeStruct((tokens, D), b16),
        ],
        scratch_shapes=[
            pltpu.SMEM((PIECES,), jnp.int32),
            pltpu.VMEM((rows, LEN, D), b16),
            pltpu.VMEM((tokens, D), b16),
            pltpu.VMEM((tokens, PAIR), b16),
            pltpu.VMEM((PAIR, tokens), b16),
            pltpu.VMEM((2, LEN, LEN // 2), f32),
            pltpu.VMEM((CAP, HALF, D), b16),
        ]
        + [pltpu.VMEM((FLOWS, CAP, NEAR, wide * PAIR), b16) for unused, wide in GROUPS]
        + [pltpu.VMEM((FLOWS, 2 * CAP, KEEP, wide * PAIR), b16) for unused, wide in GROUPS]
        + [
            pltpu.VMEM((PAIRS, D, WIDE), b16),
            pltpu.VMEM((PAIRS, NEAR, WIDE), b16),
            pltpu.VMEM((2, PAIRS, NEAR, WIDE), b16),
            pltpu.VMEM((REST, D, D), b16),
            pltpu.VMEM((REST, NEAR, D), b16),
            pltpu.VMEM((2, REST, NEAR, D), b16),
            dma((CHUNKS, FLOWS, 3)),
            dma((CHUNKS, FLOWS, 3)),
            dma((PAIRS, 8)),
            dma((PAIRS, 8)),
            dma((REST, 8)),
            dma((REST, 8)),
            dma((2,)),
            dma((2,)),
            dma((2,)),
            dma((PAIRS + REST + 2,)),
        ],
        compiler_params=pltpu.CompilerParams(
            collective_id=0, has_side_effects=True, vmem_limit_bytes=60 * MIB
        ),
        name="front",
    )(owner, lengths, master, vectors, inputs, cotangent)


class Sum:
    steps = 7

    def __init__(self, place, work, kept, wide, narrow, land, sems, send_pair, add_own):
        self.place, self.work, self.kept, self.sems = place, work, kept, sems
        self.wide, self.narrow, self.land = wide, narrow, land
        self.send_pair, self.add_own = send_pair, add_own

    def copy(self, flow, index):
        first, second, near, far, keep, give = self.place.flow(flow)
        source, target, device = [
            (self.work.at[:, rows_at(far, NEAR)], self.wide.at[flow], first),
            (self.work.at[:, rows_at(give, KEEP)], self.narrow.at[flow], second),
        ][index]
        number = 3 + 2 * flow + index
        return remote(
            source,
            target,
            self.sems[0].at[number],
            self.sems[1].at[number],
            self.place.partners[device],
        )

    def step(self, index):
        if index == 0:
            self.send_pair().start()
        if index == 1:
            self.send_pair().wait()
            self.add_own()
        for flow in range(FLOWS):
            first, second, near, far, keep, give = self.place.flow(flow)
            if index == 1:
                self.copy(flow, 0).start()
            if index == 2:
                self.copy(flow, 0).wait()
                rows = rows_at(near, NEAR)
                total = self.work[:, rows].astype(f32) + self.wide[flow].astype(f32)
                self.work[:, rows] = total.astype(b16)
                self.copy(flow, 1).start()
            if index == 3:
                self.copy(flow, 1).wait()
                total = self.work[:, rows_at(keep, KEEP)].astype(f32) + self.narrow[flow].astype(f32)
                self.kept[:, both_flows(flow)] = total.astype(b16)
        if index >= 3:
            column_step(self.place, Column(self.place, self.kept, self.land, self.sems), index - 3)


class Gather:
    steps = 3

    def __init__(self, place, work, kept, narrow, wide, sems):
        self.place, self.work, self.kept = place, work, kept
        self.narrow, self.wide, self.sems = narrow, wide, sems

    def copy(self, flow, index):
        first, second, near, far, keep, give = self.place.flow(flow)
        source, target, device = [
            (self.kept.at[:, both_flows(flow)], self.narrow, second),
            (self.work.at[:, rows_at(near, NEAR)], self.wide, first),
        ][index]
        number = 7 + 2 * flow + index
        return remote(
            source,
            target.at[flow],
            self.sems[0].at[number],
            self.sems[1].at[number],
            self.place.partners[device],
        )

    def step(self, index):
        for flow in range(FLOWS):
            first, second, near, far, keep, give = self.place.flow(flow)
            if index == 0:
                self.work[:, rows_at(keep, KEEP)] = self.kept[:, both_flows(flow)]
            if index > 0:
                self.copy(flow, index - 1).wait()
            if index == 1:
                self.work[:, rows_at(give, KEEP)] = self.narrow[flow]
            if index == 2:
                self.work[:, rows_at(far, NEAR)] = self.wide[flow]
            if index < 2:
                self.copy(flow, index).start()


class Hand:
    steps = 3

    def __init__(self, place, table, kept, bag, gift, pack, last, own, out, sems, store_sems):
        self.place, self.table, self.kept = place, table, kept
        self.bag, self.gift, self.pack, self.last, self.own = bag, gift, pack, last, own
        self.out, self.sems, self.store_sems = out, sems, store_sems

    def tile(self, chip, rank, flow):
        return self.kept[self.table[chip * CAP + rank], both_flows(flow)]

    def copy(self, flow, index):
        first, second = self.place.flow(flow)[:2]
        source, target, device = [
            (self.bag.at[flow], self.gift.at[flow], second),
            (self.pack.at[flow], self.last.at[flow], first),
        ][index]
        return remote(
            source,
            target,
            self.sems[0].at[flow, index],
            self.sems[1].at[flow, index],
            self.place.partners[device],
        )

    def stores(self, flow):
        first, second, near, far, keep, give = self.place.flow(flow)
        parts = [
            (self.own.at[flow], rows_at(keep, KEEP)),
            (self.gift.at[flow, pl.ds(0, CAP)], rows_at(give, KEEP)),
            (self.last.at[flow], rows_at(far, NEAR)),
        ]
        return [
            pltpu.make_async_copy(source, self.out.at[:, rows], self.store_sems.at[flow, index])
            for index, (source, rows) in enumerate(parts)
        ]

    def step(self, index):
        for flow in range(FLOWS):
            first, second, near, far, keep, give = self.place.flow(flow)
            if index == 0:
                beside = self.place.chips[second]
                across = beside + self.place.chips[first] - self.place.me
                for rank in range(CAP):
                    self.bag[flow, rank] = self.tile(beside, rank, flow)
                    self.bag[flow, CAP + rank] = self.tile(across, rank, flow)
                    self.own[flow, rank] = self.tile(self.place.me, rank, flow)
                self.copy(flow, 0).start()
            if index == 1:
                self.copy(flow, 0).wait()
                for rank in range(CAP):
                    mine = self.tile(self.place.chips[first], rank, flow)
                    self.pack[flow, rank, rows_at(keep - near, KEEP)] = mine
                    self.pack[flow, rank, rows_at(give - near, KEEP)] = self.gift[flow, CAP + rank]
                self.copy(flow, 1).start()
            if index == 2:
                self.copy(flow, 1).wait()
                for copy in self.stores(flow):
                    copy.start()


BACK_STEPS = 2 * PAIRS
BACK_TAIL = 4
BACK_PAIRS = tuple((index, 1) for index in range(PAIRS))
BACK_REST = (0, 1, 2, 3, 4, 5, 6, 7, 8)
BACK_HANDS = (14, 17, 20)


def back_kernel(
    table, p_ref, r_ref, v_ref, q_ref, k_ref, o_ref, g_ref, w_ref, n_ref, x_ref, z_ref, vec_ref,
    tiles_in, sums_in, y_in,
    y_out, i_out, pairs_out, slots_out, sums_ref,
    grad_sum, wide_sum, turned, slopes, block_out,
    two, two_kept, two_wide, two_narrow, two_land, two_stage,
    one, one_kept, one_wide, one_narrow, one_land, one_send_stage, one_stage,
    gather_narrow, gather_wide,
    bag, gift, pack, last, own, vec_land,
    two_send, two_recv, one_send, one_recv, hand_send, hand_recv, hand_store,
    pair_two_send, pair_two_recv, pair_one_send, pair_one_recv, load_sem, store_sem,
    swap_send, swap_recv, swap_local, vec_send, vec_recv,
):
    step = pl.program_id(0)
    place = Place()
    rows, span = y_in.shape[0], y_in.shape[1] // 2
    near_half = rows_at(place.core * HALF, HALF)
    far_half = rows_at(place.other * HALF, HALF)

    def load_two(group):
        first, count = REST_GROUPS[group]
        return pltpu.make_async_copy(
            tiles_in.at[pl.ds(first, count), near_half],
            two_stage.at[pl.ds(group % 2, 1)],
            load_sem.at[group % 2],
        )

    def rest_sum(group):
        first, count = REST_GROUPS[group]
        span_of = pl.ds(first, count)
        work = two.at[span_of]

        def send_pair():
            return remote(
                tiles_in.at[span_of, far_half],
                work,
                pair_two_send.at[group],
                pair_two_recv.at[group],
                place.twin,
            )

        def add_own():
            load_two(group).wait()
            work[...] = (work[...].astype(f32) + two_stage[group % 2].astype(f32)).astype(b16)

        sems = (two_send.at[group], two_recv.at[group])
        parts = (two_kept.at[span_of], two_wide.at[:, span_of], two_narrow.at[:, span_of])
        return Sum(place, work, *parts, two_land.at[:, span_of], sems, send_pair, add_own)

    def pair_sum(group):
        first, count = BACK_PAIRS[group]
        span_of = pl.ds(first, count)
        work = one.at[span_of]

        def send_pair():
            return remote(
                one_send_stage.at[pl.ds(group % 2, 1)],
                work,
                pair_one_send.at[group],
                pair_one_recv.at[group],
                place.twin,
            )

        def add_own():
            own = one_stage[group % 2].astype(f32)
            work[...] = (work[...].astype(f32) + own).astype(b16)

        sems = (one_send.at[group], one_recv.at[group])
        parts = (one_kept.at[span_of], one_wide.at[:, span_of], one_narrow.at[:, span_of])
        return Sum(place, work, *parts, one_land.at[:, span_of], sems, send_pair, add_own)

    def pair_gather(group):
        first, count = BACK_PAIRS[group]
        span_of = pl.ds(first, count)
        sems = (one_send.at[group], one_recv.at[group])
        narrow, wide = gather_narrow.at[:, span_of], gather_wide.at[:, span_of]
        return Gather(place, one.at[span_of], one_kept.at[span_of], narrow, wide, sems)

    hand = Hand(
        place, table, two_kept, bag, gift, pack, last, own, slots_out, (hand_send, hand_recv), hand_store
    )

    def pair_store(index, tile):
        return pltpu.make_async_copy(
            one.at[index, :, pl.ds(tile * PAIR, PAIR)],
            pairs_out.at[tile, :, pl.ds(index * PAIR, PAIR)],
            store_sem.at[index, tile],
        )

    def tick(number, odd):
        for group, start in enumerate(BACK_REST):
            if group % 2 == odd and 0 <= number - start < Sum.steps:
                rest_sum(group).step(number - start)
        for group, (first, count) in enumerate(BACK_PAIRS):
            if group % 2 != odd:
                continue
            start = 2 * (first + count)
            if 0 <= number - start < Sum.steps:
                pair_sum(group).step(number - start)
            if 0 <= number - start - Sum.steps + 1 < Gather.steps:
                pair_gather(group).step(number - start - Sum.steps + 1)
            if number == start + Sum.steps + 1:
                for index in range(first, first + count):
                    for tile in range(3):
                        pair_store(index, tile).start()
        if odd == 0 and number in BACK_HANDS:
            hand.step(BACK_HANDS.index(number))
        for group, start in enumerate(BACK_REST):
            if odd == 1 and number == max(start - 1, 0):
                load_two(group).start()

    def both(number):
        tick(number, 0)
        tick(number, 1)

    def swap_y(index):
        there = pl.ds(place.core * rows, rows)
        if index == 0:
            return pltpu.make_async_copy(
                y_in.at[:, pl.ds(place.core * span, span)], y_out.at[there], swap_local.at[0]
            )
        return remote(
            y_in.at[:, pl.ds(place.other * span, span)],
            y_out.at[there],
            swap_send.at[0],
            swap_recv.at[0],
            place.twin,
        )

    @pl.when(step == 0)
    def lead():
        place.greet()
        for index in range(2):
            swap_y(index).start()
        sums_ref[...] = sums_in[...]

    for number in range(BACK_STEPS + BACK_TAIL):
        early = partial(tick, number, 0) if number < BACK_STEPS else partial(both, number)
        pl.when(step == number)(early)

    half = LEN // 2
    pair, row = step // 2, lax.rem(step, 2)

    quarter = LEN // 4

    def attention_inputs(head):
        part = slice(head * HEAD_DIM, (head + 1) * HEAD_DIM)
        values = head_only(v_ref[...], head)
        recip = r_ref[0, head : head + 1, :]
        grad = g_ref[part, :].astype(f32) * recip
        delta = jnp.sum(grad * o_ref[part, :].astype(f32), 0, keepdims=True)
        grad = grad.astype(b16)
        return values, grad, delta, jnp.concatenate([grad, grad], axis=0)

    def attention(head):
        part = slice(head * HEAD_DIM, (head + 1) * HEAD_DIM)
        values, grad, delta, doubled = attention_inputs(head)
        units = [(which, block) for which in range(2) for block in range(4)]
        value_grad, key_grad, query_grad = {}, {}, {}

        def raw_block(unit):
            which, block = units[unit]
            cols = slice(which * half, (which + 1) * half)
            return dot_nn(values[block * quarter : (block + 1) * quarter], doubled[:, cols])

        def slope_block(unit, raw):
            which, block = units[unit]
            cols = slice(which * half, (which + 1) * half)
            for small in range(4):
                rows_here = slice(small * 64, (small + 1) * 64)
                rows_all = slice(block * quarter + small * 64, block * quarter + (small + 1) * 64)
                slope = p_ref[head, rows_all, cols].astype(f32) * (raw[rows_here] - delta[:, cols])
                slopes[unit % 2, rows_here] = slope.astype(b16)

        def add(totals, key, term):
            totals[key] = totals[key] + term if key in totals else term

        def grad_block(unit):
            which, block = units[unit]
            cols = slice(which * half, (which + 1) * half)
            rows_all = slice(block * quarter, (block + 1) * quarter)
            slope = slopes[unit % 2]
            add(value_grad, block, dot_nt(grad[:, cols], p_ref[head, rows_all, cols]))
            add(key_grad, block, dot_nt(q_ref[part, cols], slope))
            add(query_grad, which, dot_nn(k_ref[part, rows_all], slope))

        raw = raw_block(0)
        for unit in range(len(units)):
            after = raw_block(unit + 1) if unit + 1 < len(units) else None
            slope_block(unit, raw)
            if unit > 0:
                grad_block(unit - 1)
            raw = after
        grad_block(len(units) - 1)
        for which in range(2):
            total = query_grad[which] * (HEAD_DIM**-0.5)
            turned[part, which * half : (which + 1) * half] = total.astype(b16)
        for block in range(4):
            rows_all = slice(block * quarter, (block + 1) * quarter)
            lower = slice(PAIR + head * HEAD_DIM, PAIR + (head + 1) * HEAD_DIM)
            turned[lower, rows_all] = (key_grad[block] * (1.0 / LOG2E)).astype(b16)
            lower = slice(2 * PAIR + head * HEAD_DIM, 2 * PAIR + (head + 1) * HEAD_DIM)
            turned[lower, rows_all] = value_grad[block].astype(b16)

    @pl.when(step < BACK_STEPS)
    def first_head():
        attention(0)

    for number in range(BACK_STEPS):
        pl.when(step == number)(partial(tick, number, 1))

    @pl.when(step < BACK_STEPS)
    def second_head():
        attention(1)
        where = pl.ds(pl.multiple_of(row * LEN, LEN), LEN)
        block = dot_nn(turned[...], n_ref[where])
        back = turned[...].T
        lanes = pl.ds(pl.multiple_of(pair * PAIR, PAIR), PAIR)
        ones = jnp.sum(back.astype(f32), 0, keepdims=True)
        sums_ref[4:5, lanes] += ones[:, :PAIR]
        sums_ref[5:6, lanes] += ones[:, 2 * PAIR :]
        term = dot_nt(back, w_ref[0])

        @pl.when(pair == 0)
        def begin():
            grad_sum[where] = term

        @pl.when(pair > 0)
        def add():
            grad_sum[where] += term

        @pl.when(row == 0)
        def keep():
            wide_sum[...] = block

        @pl.when(row == 1)
        def hand_on():
            whole = (wide_sum[...] + block).T
            low = whole.astype(b16)
            for core in range(2):

                @pl.when(place.core == core)
                def split():
                    slot = lax.rem(pair, 2)
                    one_stage[slot] = low[core * HALF : (core + 1) * HALF]
                    one_send_stage[slot] = low[(1 - core) * HALF : (2 - core) * HALF]

    def store_block(index):
        row, half = index // 2, index % 2
        target = i_out.at[place.core * rows + row]
        local = pltpu.make_async_copy(block_out.at[half], target, swap_local.at[1 + row])
        far = remote(
            block_out.at[half], target, swap_send.at[1 + row], swap_recv.at[1 + row], place.twin
        )
        return local, far, half

    def wait_block(index):
        local, far, half = store_block(index)

        @pl.when(place.core == half)
        def keep():
            local.wait()

        @pl.when(place.core != half)
        def give():
            far.wait()

    for index in range(BACK_TAIL):

        @pl.when(step == BACK_STEPS + index)
        def close():
            size = LEN // 2
            if index >= 2:
                wait_block(index - 2)
            gain_sum = jnp.zeros((8, D), f32)
            shift_sum = jnp.zeros((8, D), f32)
            for block in range(size // 16):
                rows_here = slice(block * 16, (block + 1) * 16)
                grad = grad_sum[index * size + block * 16 : index * size + (block + 1) * 16]
                unit, rstd = norm_parts(x_ref[rows_here].astype(f32))
                gain_sum = gain_sum + jnp.sum((grad * unit).reshape(-1, 8, D), axis=0)
                shift_sum = shift_sum + jnp.sum(grad.reshape(-1, 8, D), axis=0)
                total = norm_back(grad, unit, rstd, vec_ref[0:1, :])
                block_out[index % 2, rows_here] = (z_ref[rows_here].astype(f32) + total).astype(b16)
            sums_ref[0:1, :] += jnp.sum(gain_sum, 0, keepdims=True)
            sums_ref[1:2, :] += jnp.sum(shift_sum, 0, keepdims=True)
            local, far, half = store_block(index)

            @pl.when(place.core == half)
            def keep():
                local.start()

            @pl.when(place.core != half)
            def give():
                far.start()

    @pl.when(step == BACK_STEPS + BACK_TAIL - 1)
    def drain():
        devices = [place.twin] + place.partners

        def vector(index):
            return remote(
                sums_ref, vec_land.at[index], vec_send.at[index], vec_recv.at[index], devices[index]
            )

        vector(0).start()
        for number in range(BACK_STEPS + BACK_TAIL, BACK_STEPS + Sum.steps + Gather.steps):
            both(number)
            index = number - BACK_STEPS - BACK_TAIL
            if index < 5:
                vector(index).wait()
                sums_ref[...] += vec_land[index]
                if index < 4:
                    vector(index + 1).start()
        for index in range(2):
            swap_y(index).wait()
        for index in range(2, BACK_TAIL):
            wait_block(index)
        for index in range(PAIRS):
            for tile in range(3):
                pair_store(index, tile).wait()
        for flow in range(FLOWS):
            for copy in hand.stores(flow):
                copy.wait()


def back(table, attention, weights, normed, x, residual, vectors, tiles, sums, y):
    rows, length = y.shape[:2]
    tokens = rows * length
    any_spec = pl.BlockSpec(memory_space=pl.ANY)
    smem = pl.BlockSpec(memory_space=pltpu.SMEM)
    dma = pltpu.SemaphoreType.DMA

    def now(step):
        return jnp.minimum(step, BACK_STEPS - 1)

    def tail(step):
        return jnp.maximum(step - BACK_STEPS, 0)

    head_block = pl.BlockSpec((PAIR, LEN), lambda s: (now(s) // 2, lax.rem(now(s), 2)))
    tail_block = pl.BlockSpec((LEN // 2, D), lambda s: (tail(s), 0))
    whole = pl.BlockSpec((PIECES, D), lambda s: (0, 0))
    sums_block = pl.BlockSpec((16, D), lambda s: (0, 0))
    return pl.pallas_call(
        back_kernel,
        grid=(BACK_STEPS + BACK_TAIL,),
        in_specs=[
            smem,
            pl.BlockSpec((2, LEN, LEN), lambda s: (now(s), 0, 0)),
            pl.BlockSpec((1, 2, LEN), lambda s: (now(s), 0, 0)),
            pl.BlockSpec((LEN, PAIR), lambda s: (lax.rem(now(s), 2), now(s) // 2)),
            head_block,
            head_block,
            head_block,
            head_block,
            pl.BlockSpec((1, D, WIDE), lambda s: (now(s) // 2, 0, 0)),
            pl.BlockSpec((tokens, D), lambda s: (0, 0), pipeline_mode=pl.Buffered(1)),
            tail_block,
            tail_block,
            whole,
            any_spec,
            sums_block,
            any_spec,
        ],
        out_specs=[any_spec] * 4 + [sums_block],
        out_shape=[
            jax.ShapeDtypeStruct((2 * rows, length // 2, D), b16),
            jax.ShapeDtypeStruct((2 * rows, length // 2, D), b16),
            jax.ShapeDtypeStruct((3, HALF, D), b16),
            jax.ShapeDtypeStruct((CAP, HALF, D), b16),
            jax.ShapeDtypeStruct((16, D), f32),
        ],
        scratch_shapes=[
            pltpu.VMEM((tokens, D), f32),
            pltpu.VMEM((WIDE, D), f32),
            pltpu.VMEM((WIDE, LEN), b16),
            pltpu.VMEM((2, LEN // 4, LEN // 2), b16),
            pltpu.VMEM((2, LEN // 2, D), b16),
            pltpu.VMEM((REST, HALF, D), b16),
            pltpu.VMEM((REST, NEAR, D), b16),
            pltpu.VMEM((FLOWS, REST, NEAR, D), b16),
            pltpu.VMEM((FLOWS, REST, KEEP, D), b16),
            pltpu.VMEM((2, REST, NEAR, D), b16),
            pltpu.VMEM((2, HALF, D), b16),
            pltpu.VMEM((PAIRS, HALF, WIDE), b16),
            pltpu.VMEM((PAIRS, NEAR, WIDE), b16),
            pltpu.VMEM((FLOWS, PAIRS, NEAR, WIDE), b16),
            pltpu.VMEM((FLOWS, PAIRS, KEEP, WIDE), b16),
            pltpu.VMEM((2, PAIRS, NEAR, WIDE), b16),
            pltpu.VMEM((2, HALF, WIDE), b16),
            pltpu.VMEM((2, HALF, WIDE), b16),
            pltpu.VMEM((FLOWS, PAIRS, KEEP, WIDE), b16),
            pltpu.VMEM((FLOWS, PAIRS, NEAR, WIDE), b16),
            pltpu.VMEM((FLOWS, 2 * CAP, KEEP, D), b16),
            pltpu.VMEM((FLOWS, 2 * CAP, KEEP, D), b16),
            pltpu.VMEM((FLOWS, CAP, NEAR, D), b16),
            pltpu.VMEM((FLOWS, CAP, NEAR, D), b16),
            pltpu.VMEM((FLOWS, CAP, KEEP, D), b16),
            pltpu.VMEM((5, 16, D), f32),
            dma((REST, 7)),
            dma((REST, 7)),
            dma((PAIRS, 11)),
            dma((PAIRS, 11)),
            dma((FLOWS, 2)),
            dma((FLOWS, 2)),
            dma((FLOWS, 3)),
            dma((REST,)),
            dma((REST,)),
            dma((PAIRS,)),
            dma((PAIRS,)),
            dma((3,)),
            dma((PAIRS, 3)),
            dma((3,)),
            dma((3,)),
            dma((3,)),
            dma((5,)),
            dma((5,)),
        ],
        compiler_params=pltpu.CompilerParams(
            collective_id=1, has_side_effects=True, vmem_limit_bytes=62 * MIB
        ),
        name="back",
    )(table, *attention, weights, normed, x, residual, vectors, tiles, sums, y)


def update_kernel(tile_at, one, two, w_ref, m_ref, s_ref, y_in, i_in, w_out, m_out, s_out, y_out, i_out):
    step = pl.program_id(0)
    tile = tile_at[step // 2]
    grad = jnp.where(tile < 3, one[0], two[0]).astype(f32)
    parts = adam_step(w_ref[0], grad, m_ref[0], s_ref[0], RATE)
    for target, part in zip((w_out, m_out, s_out), parts):
        target[0] = jnp.where(tile >= 0, part, jnp.zeros_like(part))

    @pl.when(step < 4)
    def widen():
        y_out[...] = y_in[...].astype(f32)
        i_out[...] = i_in[...].astype(f32)


def update(tile_at, one, two, master, first, second, y, grad):
    tokens = y.shape[0]
    size = HALF // 2
    state = pl.BlockSpec((1, size, D), lambda s, tile_at: (s // 2, lax.rem(s, 2), 0))
    wide = pl.BlockSpec((tokens // 4, D), lambda s, tile_at: (jnp.minimum(s, 3), 0))
    return pl.pallas_call(
        update_kernel,
        grid_spec=pltpu.PrefetchScalarGridSpec(
            num_scalar_prefetch=1,
            grid=(CAP * 2,),
            in_specs=[
                pl.BlockSpec(
                    (1, size, D),
                    lambda s, tile_at: (jnp.clip(tile_at[s // 2], 0, 2), lax.rem(s, 2), 0),
                ),
                state,
                state,
                state,
                state,
                wide,
                wide,
            ],
            out_specs=[state] * 3 + [wide] * 2,
        ),
        out_shape=[jax.ShapeDtypeStruct(master.shape, f32)] * 3
        + [jax.ShapeDtypeStruct((tokens, D), f32)] * 2,
        compiler_params=pltpu.CompilerParams(vmem_limit_bytes=60 * MIB),
        name="update",
    )(tile_at, one, two, master, first, second, y, grad)


def shards_paired(
    inputs,
    cotangent,
    doc_lengths,
    owner_list,
    master,
    first_moment,
    second_moment,
    vectors,
    vector_first,
    vector_second,
):
    rows_here, span, width = inputs.shape
    place = lax.axis_index("blk")
    member = lax.axis_index("dp")
    rows_mine = rows_here // 2
    order = jnp.arange(PIECES)
    same_owner = owner_list[:, None] == owner_list[None, :]
    ranks = jnp.sum(same_owner & (order[None, :] < order[:, None]), axis=1).astype(jnp.int32)
    slot_of = owner_list * CAP + ranks
    front_outs = front(owner_list, doc_lengths, master, vectors, inputs, cotangent)
    x, cot, normed, weights_one, weights_two, queries, keys, values = front_outs[:8]
    weights, recips, context_turned, context = front_outs[8:]
    x = x.reshape(-1, width)
    cot = cot.reshape(-1, width)
    block_out, residual, grad_context, sums, tiles_two = feed(
        context, context_turned, x, cot, weights_two, vectors
    )
    hits = jnp.arange(16 * CAP)[:, None] == slot_of[None, :]
    tile_at = jnp.sum(jnp.where(hits, order[None, :] + 1, 0), axis=1).astype(jnp.int32) - 1
    table = jnp.maximum(tile_at - 3, 0)
    block_out, input_grad, total_one, total_two, vector_total = back(
        table,
        (weights, recips, values, queries, keys, context_turned, grad_context),
        weights_one,
        normed,
        x,
        residual,
        vectors,
        tiles_two,
        sums,
        block_out.reshape(rows_mine, LEN, width),
    )
    mine = lax.dynamic_slice_in_dim(tile_at, member * CAP, CAP, 0)
    *updated, block_out, input_grad = update(
        mine,
        total_one,
        total_two,
        master,
        first_moment,
        second_moment,
        block_out.reshape(-1, width),
        input_grad.reshape(-1, width),
    )
    columns = vector_first.shape[1]
    vector_cols = lax.dynamic_slice_in_dim(vectors, place * columns, columns, 1)
    vector_total = lax.dynamic_slice(vector_total, (0, place * columns), (PIECES, columns))
    updated_vectors = adam_step(vector_cols, vector_total, vector_first, vector_second, VEC_RATE)
    return (
        block_out.reshape(inputs.shape),
        input_grad.reshape(inputs.shape),
        *updated,
        *updated_vectors,
    )


def solution(mesh):
    in_specs = (
        P("dp", "blk", None),
        P("dp", "blk", None),
        P("dp", None),
        P(),
        P("dp", "blk", None),
        P("dp", "blk", None),
        P("dp", "blk", None),
        P(),
        P(None, "blk"),
        P(None, "blk"),
    )
    out_specs = (
        P("dp", "blk", None),
        P("dp", "blk", None),
        P("dp", "blk", None),
        P("dp", "blk", None),
        P("dp", "blk", None),
        P(None, "blk"),
        P(None, "blk"),
        P(None, "blk"),
    )
    paired = mesh.shape["blk"] == 2 and mesh.shape["dp"] == 16
    shards = shards_paired if paired else shards_any
    return jax.shard_map(shards, mesh=mesh, in_specs=in_specs, out_specs=out_specs, check_vma=False)
```
